32 devices in a mesh: section: 2 (over y), dp: 16 (over z, x, core).
Axes of the slice: x: 2, y: 2, z: 4, core: 2. Of those that a mesh axis runs over, the one named last changes fastest.
Arguments:
- patch_rows: bfloat16 [2, 64, 196, 768], P('section', 'dp'), may hold values from -6 to 6
- cotangent: bfloat16 [2, 64, 196, 768], P('section', 'dp'), may hold values from -6 to 6
- patch_order: int32 [64, 196], P('dp'), may hold values from 0 to 195, each once within a row
- visible: int32 [64], P('dp'), may hold values from 78 to 137, as said below
- qkv_weight: bfloat16 [2, 768, 2304], P('section'), may hold values from -0.21875 to 0.21875
- out_weight: bfloat16 [2, 768, 768], P('section'), may hold values from -1.25 to 1.25
- up_weight: bfloat16 [2, 768, 3072], P('section'), may hold values from -0.21875 to 0.21875
- down_weight: bfloat16 [2, 3072, 768], P('section'), may hold values from -0.109375 to 0.109375
- norm_gains: bfloat16 [2, 2, 768], P('section'), may hold values from 0.5 to 1.5
- biases: bfloat16 [2, 4, 768], P('section'), may hold values from -1.796875 to 1.796875
- qv_bias: bfloat16 [2, 1536], P('section'), may hold values from -1.796875 to 1.796875
- up_bias: bfloat16 [2, 3072], P('section'), may hold values from -1.796875 to 1.796875
- target_qkv: bfloat16 [768, 2304], replicated, may hold values from -0.21875 to 0.21875
- target_out: bfloat16 [768, 768], replicated, may hold values from -1.25 to 1.25
- target_up: bfloat16 [768, 3072], replicated, may hold values from -0.21875 to 0.21875
- target_down: bfloat16 [3072, 768], replicated, may hold values from -0.109375 to 0.109375
- target_gains: bfloat16 [2, 768], replicated, may hold values from 0.5 to 1.5
- target_biases: bfloat16 [4, 768], replicated, may hold values from -1.796875 to 1.796875
- target_qv_bias: bfloat16 [1536], replicated, may hold values from -1.796875 to 1.796875
- target_up_bias: bfloat16 [3072], replicated, may hold values from -1.796875 to 1.796875
Outputs:
- block_out: bfloat16 [2, 64, 196, 768], P('section', 'dp')
- grad_rows: float32 [2, 64, 196, 768], P('section', 'dp')
- grad_qkv: float32 [2, 768, 2304], P('section', 'dp')
- grad_out: float32 [2, 768, 768], P('section', 'dp')
- grad_up: float32 [2, 768, 3072], P('section', 'dp')
- grad_down: float32 [2, 3072, 768], P('section', 'dp')
- grad_gains: float32 [2, 2, 768], P('section', None, 'dp')
- grad_biases: float32 [2, 4, 768], P('section', None, 'dp')
- grad_qv_bias: float32 [2, 1536], P('section', 'dp')
- grad_up_bias: float32 [2, 3072], P('section', 'dp')
The draws below stay inside these ranges and needn't reach their ends.
Inputs may be any that keep to these rules, and one draw needn't show every extreme that they name: `patch_order`: row i lists the 196 patch positions of image i once each; its first visible[i] entries are the visible patches, the rest the masked ones. In every draw some image has exactly 137 visible patches and some exactly 78.
All inputs are finite; a program needn't handle non-finite values.
Results may differ from the reference program's by a relative error of at most 0.012.
Values may be sent and summed in bfloat16 or wider, within the bound.
No kernel may reach another device: no remote copies, remote signals or barrier semaphores. Data moves between devices by JAX's collectives and lax.ppermute only.
A program may use at most 256 MiB of HBM per device.

```python
import math
import jax
import jax.numpy as jnp
from jax import lax

D = 768
HEADS = 12
FF = 3072
PATCH = 196
SLOTS = 137
VIS_LEAST = 78
IMG_DEV = 4
IMAGES = 64


def draw_visible(key, part):
    key = jax.random.fold_in(key, 11)
    key_counts, key_pick = jax.random.split(key)
    counts = jax.random.randint(key_counts, (IMAGES,), VIS_LEAST, SLOTS + 1)
    chosen = jax.random.permutation(key_pick, IMAGES)
    counts = counts.at[chosen[0]].set(SLOTS).at[chosen[1]].set(VIS_LEAST)
    return counts.astype(jnp.int32)


def strengthened(values, stream_key, source, target, blocks, factor):
    owner, partner = [(jnp.arange(values.shape[position]) // (values.shape[position] // blocks)).reshape([-1 if axis == position else 1 for axis in range(values.ndim)]) for position in (source, target)]
    chosen = jax.random.permutation(stream_key, blocks)[partner]
    strong = (owner == chosen) | (owner == (partner + blocks // 2) % blocks)
    return jnp.where(strong, factor * values, values)


def shard_levels(rng, shape, cuts, least, largest):
    def one(position, blocks):
        heights = jax.random.uniform(jax.random.fold_in(jax.random.fold_in(rng, 6), position), (blocks,), jnp.float32, least / len(cuts), largest / len(cuts))
        return jnp.repeat(jnp.exp(heights), shape[position] // blocks).reshape((-1,) + (1,) * (len(shape) - position - 1))

    loudness = one(*cuts[0])
    for cut in cuts[1:]:
        loudness = loudness * one(*cut)
    return loudness


def scatter_about(own_key, dims, width, reach, cuts=(), kind=jnp.bfloat16):
    array = jax.random.normal(own_key, dims, jnp.float32) * width
    if len(cuts) > 0:
        array = shard_levels(own_key, dims, cuts, -0.22, 0.18) * array
    return jnp.clip(array, min=-reach, max=reach).astype(kind)


def noise_with(key, extent, spread, most, cuts, heavy, kind=jnp.bfloat16):
    values = spread * jax.random.normal(key, extent, jnp.float32)
    if cuts:
        values = values * shard_levels(key, extent, cuts, -0.22, 0.18)
    return jnp.clip(strengthened(values, jax.random.fold_in(key, 3), *heavy), -most, most).astype(kind)


def setup_inputs(seed: int = 0) -> dict:
    key_of = jax.random.split(jax.random.key(seed), 21)
    patch_rows = scatter_about(key_of[0], (2, IMAGES, PATCH, D), 1.0, 6.0, ((0, 2), (1, 16)))
    cotangent = noise_with(key_of[1], (2, IMAGES, PATCH, D), 1.0, 6.0, ((0, 2), (1, 16)), (1, 3, 16, 2.0))
    patch_order = jax.vmap(lambda own: jax.random.permutation(own, PATCH))(jax.random.split(key_of[2], IMAGES)).reshape((IMAGES, PATCH)).astype(jnp.int32)
    visible = draw_visible(jax.random.fold_in(key_of[20], 71), 0)
    qkv_weight = scatter_about(key_of[4], (2, D, 3 * D), D ** -0.5, 0.21875, ((0, 2),))
    out_weight = scatter_about(key_of[5], (2, D, D), (D // 32) ** -0.5, 1.25, ((0, 2),))
    up_weight = scatter_about(key_of[6], (2, D, FF), D ** -0.5, 0.21875, ((0, 2),))
    down_weight = scatter_about(key_of[7], (2, FF, D), FF ** -0.5, 0.109375, ((0, 2),))
    norm_gains = jnp.clip(1.0 + 0.1 * jax.random.normal(key_of[8], (2, 2, D), jnp.float32), 0.5, 1.5).astype(jnp.bfloat16)
    biases = scatter_about(key_of[9], (2, 4, D), 0.3, 1.796875, ((0, 2),))
    qv_bias = scatter_about(key_of[10], (2, 2 * D), 0.3, 1.796875, ((0, 2),))
    up_bias = scatter_about(key_of[11], (2, FF), 0.3, 1.796875, ((0, 2),))
    target_qkv = scatter_about(key_of[12], (D, 3 * D), D ** -0.5, 0.21875)
    target_out = scatter_about(key_of[13], (D, D), (D // 32) ** -0.5, 1.25)
    target_up = scatter_about(key_of[14], (D, FF), D ** -0.5, 0.21875)
    target_down = scatter_about(key_of[15], (FF, D), FF ** -0.5, 0.109375)
    target_gains = jnp.clip(1.0 + 0.1 * jax.random.normal(key_of[16], (2, D), jnp.float32), 0.5, 1.5).astype(jnp.bfloat16)
    target_biases = scatter_about(key_of[17], (4, D), 0.3, 1.796875)
    target_qv_bias = scatter_about(key_of[18], (2 * D,), 0.3, 1.796875)
    target_up_bias = scatter_about(key_of[19], (FF,), 0.3, 1.796875)
    return dict(patch_rows=patch_rows, cotangent=cotangent, patch_order=patch_order, visible=visible, qkv_weight=qkv_weight, out_weight=out_weight, up_weight=up_weight, down_weight=down_weight, norm_gains=norm_gains, biases=biases, qv_bias=qv_bias, up_bias=up_bias, target_qkv=target_qkv, target_out=target_out, target_up=target_up, target_down=target_down, target_gains=target_gains, target_biases=target_biases, target_qv_bias=target_qv_bias, target_up_bias=target_up_bias)


EPS = 1e-06

@jax.custom_vjp
def low(v):
    return lax.optimization_barrier(v.astype(jnp.bfloat16)).astype(jnp.float32)

@jax.custom_vjp
def low_back(v):
    return v

def low_keep(v):
    return (low(v), None)

def low_pass(kept, grad):
    return (grad,)

def back_keep(v):
    return (v, None)

def back_low(kept, grad):
    return (low(grad),)
low.defvjp(low_keep, low_pass)
low_back.defvjp(back_keep, back_low)

def layer_norm(inputs, scale_vec, offset):
    mean_row = lax.optimization_barrier(jnp.mean(inputs, axis=-1, keepdims=True))
    centered = inputs - mean_row
    var_row = lax.optimization_barrier(jnp.mean(centered * centered, axis=-1, keepdims=True))
    return centered * lax.rsqrt(var_row + EPS) * scale_vec + offset

def matmul_hi(a, b):
    return jnp.einsum('bsd,df->bsf', a, b, precision=lax.Precision.HIGHEST)

def split_heads(a):
    return a.reshape(a.shape[0], a.shape[1], HEADS, a.shape[2] // HEADS)

def pick_rows(source, index):
    return jnp.take_along_axis(source, index[:, :, None], axis=1)

def vit_block(xq, xk, key_mask, weights, same):
    qkv_w, out_w, up_w, down_w, gain_rows, bias_rows, qv_b, up_b = weights
    model_width = xq.shape[-1]
    head_size = model_width // HEADS
    normed = low(layer_norm(xq, gain_rows[0], bias_rows[0]))
    if same:
        source = normed
    else:
        source = low(layer_norm(xk, gain_rows[0], bias_rows[0]))
    query_rows = low(low_back(matmul_hi(normed, qkv_w[:, :model_width]) + qv_b[:model_width]))
    key_rows = low(low_back(matmul_hi(source, qkv_w[:, model_width:2 * model_width])))
    value_rows = low(low_back(matmul_hi(source, qkv_w[:, 2 * model_width:]) + qv_b[model_width:]))
    raw_scores = jnp.einsum('bqhd,bkhd->bhqk', split_heads(query_rows), split_heads(key_rows), precision=lax.Precision.HIGHEST)
    scores = low_back(raw_scores * (1.0 / math.sqrt(head_size)))
    scores = jnp.where(key_mask[:, None, None, :], scores, -1000000000.0)
    row_top = lax.optimization_barrier(jnp.max(scores, axis=-1, keepdims=True))
    exp_scores = jnp.exp(scores - row_top)
    attn_probs = low(exp_scores / lax.optimization_barrier(jnp.sum(exp_scores, axis=-1, keepdims=True)))
    mixed_heads = jnp.einsum('bhqk,bkhd->bqhd', attn_probs, split_heads(value_rows), precision=lax.Precision.HIGHEST)
    mixed_heads = low(low_back(mixed_heads.reshape(xq.shape)))
    residual = xq + low_back(matmul_hi(mixed_heads, out_w) + bias_rows[1])
    hidden_in = low(layer_norm(residual, gain_rows[1], bias_rows[2]))
    pre_act = low_back(matmul_hi(hidden_in, up_w) + up_b)
    active = low(jax.nn.gelu(pre_act, approximate=False))
    return residual + low_back(matmul_hi(active, down_w) + bias_rows[3])

def reference(patch_rows, cotangent, patch_order, visible, qkv_weight, out_weight, up_weight, down_weight, norm_gains, biases, qv_bias, up_bias, target_qkv, target_out, target_up, target_down, target_gains, target_biases, target_qv_bias, target_up_bias):
    first_slot = PATCH - SLOTS
    group_count = IMAGES // IMG_DEV
    stacked = tuple((a.astype(jnp.float32) for a in (qkv_weight, out_weight, up_weight, down_weight, norm_gains, biases, qv_bias, up_bias)))
    frozen = tuple((a.astype(jnp.float32) for a in (target_qkv, target_out, target_up, target_down, target_gains, target_biases, target_qv_bias, target_up_bias)))
    rows_full = patch_rows.astype(jnp.float32)
    places = jnp.arange(SLOTS, dtype=jnp.int32)
    vis_idx = patch_order[:, :SLOTS]
    msk_idx = patch_order[:, first_slot:]
    key_mask = places[None, :] < visible[:, None]
    target_mask = (first_slot + places)[None, :] >= visible[:, None]

    def grouped(a):
        return a.reshape((group_count, IMG_DEV) + a.shape[1:])

    def forward_all(enc_rows, reg_rows, weights):

        def group_pass(pieces):
            enc_g, reg_g, vis_g, msk_g, mask_g = pieces
            enc_w = tuple((a[0] for a in weights))
            reg_w = tuple((a[1] for a in weights))
            xq = pick_rows(enc_g, vis_g)
            latent = low(low_back(vit_block(xq, xq, mask_g, enc_w, True)))
            regressed = vit_block(pick_rows(reg_g, msk_g), latent, mask_g, reg_w, False)
            return (latent, regressed)
        latent, regressed = lax.map(jax.checkpoint(group_pass), (grouped(enc_rows), grouped(reg_rows), grouped(vis_idx), grouped(msk_idx), grouped(key_mask)))
        return (latent.reshape((IMAGES,) + latent.shape[2:]), regressed.reshape((IMAGES,) + regressed.shape[2:]))
    (latent, regressed), pullback = jax.vjp(forward_all, rows_full[0], rows_full[1], stacked)
    cot_full = cotangent.astype(jnp.float32)
    cot_enc = jnp.where(key_mask[:, :, None], pick_rows(cot_full[0], vis_idx), 0.0)
    cot_reg = jnp.where(target_mask[:, :, None], pick_rows(cot_full[1], msk_idx), 0.0)
    d_enc, d_reg, d_weights = pullback((cot_enc, cot_reg))

    def target_group(pieces):
        enc_g, msk_g, mask_g = pieces
        xm = pick_rows(enc_g, msk_g)
        return vit_block(xm, xm, mask_g, frozen, True)
    target_out = lax.map(target_group, (grouped(rows_full[0]), grouped(msk_idx), grouped(target_mask)))
    target_out = target_out.reshape((IMAGES,) + target_out.shape[2:])
    position_rank = jnp.zeros((IMAGES, PATCH), jnp.int32).at[jnp.arange(IMAGES, dtype=jnp.int32)[:, None], patch_order].set(jnp.broadcast_to(jnp.arange(PATCH, dtype=jnp.int32), (IMAGES, PATCH)))
    vis_pos = position_rank < visible[:, None]
    enc_slot = jnp.clip(position_rank, 0, SLOTS - 1)
    msk_slot = jnp.clip(position_rank - first_slot, 0, SLOTS - 1)
    out_enc = jnp.where(vis_pos[:, :, None], pick_rows(latent, enc_slot), pick_rows(target_out, msk_slot))
    out_reg = jnp.where(vis_pos[:, :, None], 0.0, pick_rows(regressed, msk_slot))
    block_out = jnp.stack([out_enc, out_reg]).astype(jnp.bfloat16)
    grad_rows = jnp.stack([d_enc, d_reg])
    return (block_out, grad_rows, d_weights[0], d_weights[1], d_weights[2], d_weights[3], d_weights[4], d_weights[5], d_weights[6], d_weights[7])
```

```python
from functools import partial
import math

import jax
import jax.numpy as jnp
from jax import lax
from jax.sharding import PartitionSpec as P

HEADS = 12
PATCH = 196
SLOTS = 137


EPS = 1e-06


def shifted(value, axis, steps):
    count = lax.axis_size(axis)
    initial, last = (max(0, -steps), min(count, count - steps))
    return lax.ppermute(value, axis, [(source, source + steps) for source in range(initial, last)])


def layer_norm(inputs, scale_vec, offset):
    mean_row = jnp.mean(inputs, axis=-1, keepdims=True)
    centered = inputs - mean_row
    var_row = jnp.mean(centered * centered, axis=-1, keepdims=True)
    return centered * lax.rsqrt(var_row + EPS) * scale_vec + offset


def project(a, b):
    return jnp.einsum("bsd,df->bsf", a, b, preferred_element_type=jnp.float32)


def back_project(g, b):
    return jnp.einsum("bsf,df->bsd", g, b, preferred_element_type=jnp.float32)


def weight_sum(a, g):
    return jnp.einsum("bsd,bsf->df", a, g, preferred_element_type=jnp.float32)


def split_heads(a):
    return a.reshape(a.shape[0], a.shape[1], HEADS, a.shape[2] // HEADS)


def pick_rows(source, index):
    return jnp.take_along_axis(source, index[:, :, None], axis=1)


def attention_scores(query_rows, key_rows, key_mask):
    head_size = query_rows.shape[-1] // HEADS
    scores = jnp.einsum(
        "bqhd,bkhd->bhqk",
        split_heads(query_rows),
        split_heads(key_rows),
        preferred_element_type=jnp.float32,
    ) * (1.0 / math.sqrt(head_size))
    return jnp.where(key_mask[:, None, None, :], scores, -1000000000.0)


def forward(xq, xk, key_mask, weights, same):
    qkv_w, out_w, up_w, down_w, gain_rows, bias_rows, qv_b, up_b = weights
    model_width = xq.shape[-1]
    normed = layer_norm(xq, gain_rows[0], bias_rows[0]).astype(jnp.bfloat16)
    if same:
        united_qkv = project(normed, qkv_w)
        source = normed
        query_raw = united_qkv[..., :model_width]
        key_value = united_qkv[..., model_width:]
    else:
        source = layer_norm(xk, gain_rows[0], bias_rows[0]).astype(jnp.bfloat16)
        query_raw = project(normed, qkv_w[:, :model_width])
        key_value = project(source, qkv_w[:, model_width:])
    query_rows = (query_raw + qv_b[:model_width]).astype(jnp.bfloat16)
    key_rows = key_value[..., :model_width].astype(jnp.bfloat16)
    value_rows = (key_value[..., model_width:] + qv_b[model_width:]).astype(jnp.bfloat16)
    scores = attention_scores(query_rows, key_rows, key_mask)
    row_top = jnp.max(scores, axis=-1, keepdims=True)
    exp_scores = jnp.exp(scores - row_top)
    row_total = jnp.sum(exp_scores, axis=-1, keepdims=True)
    attn_probs = (exp_scores / row_total).astype(jnp.bfloat16)
    log_total = row_top + jnp.log(row_total)
    mixed_heads = jnp.einsum(
        "bhqk,bkhd->bqhd", attn_probs, split_heads(value_rows), preferred_element_type=jnp.float32
    )
    mixed_heads = mixed_heads.reshape(xq.shape).astype(jnp.bfloat16)
    residual = xq + project(mixed_heads, out_w) + bias_rows[1]
    hidden_in = layer_norm(residual, gain_rows[1], bias_rows[2]).astype(jnp.bfloat16)
    pre_act = project(hidden_in, up_w) + up_b
    active = jax.nn.gelu(pre_act, approximate=False).astype(jnp.bfloat16)
    result = residual + project(active, down_w) + bias_rows[3]
    return (
        result,
        (
            xq,
            xk,
            normed,
            source,
            query_rows,
            key_rows,
            value_rows,
            log_total,
            mixed_heads,
            residual,
            hidden_in,
            pre_act,
            active,
        ),
    )


def mlp_back(cache, grad_y, weights):
    residual, hidden_in, pre_act, active = cache[9:]
    qkv_w, out_w, up_w, down_w, gain_rows, bias_rows, qv_b, up_b = weights
    grad_low = grad_y.astype(jnp.bfloat16)
    grad_full = grad_low.astype(jnp.float32)
    d_down = weight_sum(active, grad_low)
    d_last = jnp.sum(grad_full, axis=(0, 1))
    d_active = back_project(grad_low, down_w)
    _, gelu_back = jax.vjp(partial(jax.nn.gelu, approximate=False), pre_act)
    d_pre = gelu_back(d_active)[0].astype(jnp.bfloat16)
    d_up = weight_sum(hidden_in, d_pre)
    d_up_bias = jnp.sum(d_pre.astype(jnp.float32), axis=(0, 1))
    d_hidden = back_project(d_pre, up_w)
    _, norm_back = jax.vjp(layer_norm, residual, gain_rows[1], bias_rows[2])
    d_resid, d_gain, d_offset = norm_back(d_hidden)
    return ((d_up, d_down, d_up_bias, d_gain, d_offset, d_last), grad_full + d_resid)


def attn_back(cache, d_resid, key_mask, weights, same):
    xq, xk, normed, source, query_rows, key_rows, value_rows, log_total, mixed_heads = cache[:9]
    qkv_w, out_w, up_w, down_w, gain_rows, bias_rows, qv_b, up_b = weights
    model_width = xq.shape[-1]
    head_size = model_width // HEADS
    d_low = d_resid.astype(jnp.bfloat16)
    d_out = weight_sum(mixed_heads, d_low)
    d_out_bias = jnp.sum(d_low.astype(jnp.float32), axis=(0, 1))
    d_mixed = split_heads(back_project(d_low, out_w).astype(jnp.bfloat16))
    attn_probs = jnp.exp(attention_scores(query_rows, key_rows, key_mask) - log_total)
    d_values = jnp.einsum(
        "bhqk,bqhd->bkhd",
        attn_probs.astype(jnp.bfloat16),
        d_mixed,
        preferred_element_type=jnp.float32,
    )
    d_probs = jnp.einsum(
        "bqhd,bkhd->bhqk", d_mixed, split_heads(value_rows), preferred_element_type=jnp.float32
    )
    d_scores = (
        attn_probs * (d_probs - jnp.sum(d_probs * attn_probs, axis=-1, keepdims=True))
    ).astype(jnp.bfloat16)
    score_scale = 1.0 / math.sqrt(head_size)
    d_query = (
        (
            jnp.einsum(
                "bhqk,bkhd->bqhd",
                d_scores,
                split_heads(key_rows),
                preferred_element_type=jnp.float32,
            )
            * score_scale
        )
        .reshape(xq.shape)
        .astype(jnp.bfloat16)
    )
    d_keys = (
        (
            jnp.einsum(
                "bhqk,bqhd->bkhd",
                d_scores,
                split_heads(query_rows),
                preferred_element_type=jnp.float32,
            )
            * score_scale
        )
        .reshape(xq.shape)
        .astype(jnp.bfloat16)
    )
    d_values = d_values.reshape(xq.shape).astype(jnp.bfloat16)
    d_qv_bias = jnp.concatenate(
        [
            jnp.sum(d_query.astype(jnp.float32), axis=(0, 1)),
            jnp.sum(d_values.astype(jnp.float32), axis=(0, 1)),
        ]
    )
    d_pair = jnp.concatenate([d_keys, d_values], axis=-1)
    if same:
        d_united = jnp.concatenate([d_query, d_pair], axis=-1)
        d_qkv = weight_sum(normed, d_united)
        d_normed = back_project(d_united, qkv_w)
    else:
        d_qkv = jnp.concatenate([weight_sum(normed, d_query), weight_sum(source, d_pair)], axis=1)
        d_normed = back_project(d_query, qkv_w[:, :model_width])
        d_source = back_project(d_pair, qkv_w[:, model_width:])
    _, norm_back = jax.vjp(layer_norm, xq, gain_rows[0], bias_rows[0])
    d_input, d_gain, d_offset = norm_back(d_normed)
    d_input = d_resid + d_input
    if same:
        return ((d_qkv, d_out, d_qv_bias, d_gain, d_offset, d_out_bias), d_input, None)
    _, side_back = jax.vjp(layer_norm, xk, gain_rows[0], bias_rows[0])
    d_side, side_gain, side_offset = side_back(d_source)
    return (
        (d_qkv, d_out, d_qv_bias, d_gain + side_gain, d_offset + side_offset, d_out_bias),
        d_input,
        d_side,
    )


def assemble(attn_grads, mlp_grads):
    gain_grads = jnp.stack([attn_grads[3], mlp_grads[3]])
    bias_grads = jnp.stack([attn_grads[4], attn_grads[5], mlp_grads[4], mlp_grads[5]])
    return (
        attn_grads[0],
        attn_grads[1],
        mlp_grads[0],
        mlp_grads[1],
        gain_grads,
        bias_grads,
        attn_grads[2],
        mlp_grads[2],
    )


def combined_sum(grads, count):
    d_qkv, d_out, d_up, d_down, d_gains, d_biases, d_qv, d_upb = grads
    width = d_out.shape[1]
    own = width // count

    def blocks(a):
        return [
            a[:, i * width : (i + 1) * width].astype(jnp.bfloat16).reshape(count, own, width)
            for i in range(a.shape[1] // width)
        ]

    small = jnp.concatenate(
        [
            jnp.moveaxis(d_gains.reshape(2, count, own), 1, 0).reshape(count, -1),
            jnp.moveaxis(d_biases.reshape(4, count, own), 1, 0).reshape(count, -1),
            d_qv.reshape(count, -1),
            d_upb.reshape(count, -1),
        ],
        axis=1,
    )
    spare = width - small.shape[1]
    small = jnp.pad(small, ((0, 0), (0, spare))).astype(jnp.bfloat16)[:, None, :]
    down = d_down.astype(jnp.bfloat16).reshape(count, 4 * own, width)
    parts = blocks(d_qkv) + blocks(d_out) + blocks(d_up) + [down, small]
    packed = jnp.concatenate(parts, axis=1)
    got = lax.psum_scatter(packed, "dp", scatter_dimension=0, tiled=True)[0].astype(jnp.float32)

    def take(start, cols):
        return jnp.concatenate(
            [got[start + i * own : start + (i + 1) * own] for i in range(cols)], axis=1
        )

    tail = got[12 * own]
    return (
        take(0, 3),
        take(3 * own, 1),
        take(4 * own, 4),
        got[8 * own : 12 * own],
        tail[: 2 * own].reshape(2, own),
        tail[2 * own : 6 * own].reshape(4, own),
        tail[6 * own : 8 * own],
        tail[8 * own : 12 * own],
    )


def local(
    patch_rows,
    cotangent,
    patch_order,
    visible,
    qkv_weight,
    out_weight,
    up_weight,
    down_weight,
    norm_gains,
    biases,
    qv_bias,
    up_bias,
    target_qkv,
    target_out,
    target_up,
    target_down,
    target_gains,
    target_biases,
    target_qv_bias,
    target_up_bias,
):
    encoder = lax.axis_index("section") == 0
    first_slot = PATCH - SLOTS
    images = patch_order.shape[0]
    model_width = patch_rows.shape[-1]
    places = jnp.arange(SLOTS, dtype=jnp.int32)
    slot_start = jnp.where(encoder, 0, first_slot).astype(jnp.int32)
    own_slots = lax.dynamic_slice_in_dim(patch_order, slot_start, SLOTS, 1)
    own_ranks = (slot_start + places)[None, :]
    visible_col = visible[:, None]
    query_ok = jnp.where(encoder, own_ranks < visible_col, own_ranks >= visible_col)
    key_mask = places[None, :] < visible_col
    target_mask = (first_slot + places)[None, :] >= visible_col
    own_rows = patch_rows[0]
    queries = pick_rows(own_rows, own_slots).astype(jnp.float32)
    grad_in = jnp.where(
        query_ok[:, :, None], pick_rows(cotangent[0], own_slots).astype(jnp.float32), 0.0
    )
    masked_rows = pick_rows(own_rows, patch_order[:, first_slot:]).astype(jnp.float32)
    weights = (
        qkv_weight[0],
        out_weight[0],
        up_weight[0],
        down_weight[0],
        norm_gains[0].astype(jnp.float32),
        biases[0].astype(jnp.float32),
        qv_bias[0].astype(jnp.float32),
        up_bias[0].astype(jnp.float32),
    )
    frozen = (
        target_qkv,
        target_out,
        target_up,
        target_down,
        target_gains.astype(jnp.float32),
        target_biases.astype(jnp.float32),
        target_qv_bias.astype(jnp.float32),
        target_up_bias.astype(jnp.float32),
    )
    shape_main = (images, SLOTS, model_width)
    blank_grads = tuple((jnp.zeros(w.shape, jnp.float32) for w in weights))

    def encode():
        return forward(queries, queries, key_mask, weights, True)[0].astype(jnp.bfloat16)

    latents, early_side = lax.cond(
        encoder,
        lambda: (encode(), forward(masked_rows, masked_rows, target_mask, frozen, True)[0]),
        lambda: (jnp.zeros(shape_main, jnp.bfloat16), jnp.zeros(shape_main, jnp.float32)),
    )
    received = shifted(latents, "section", 1)

    def regress():
        result, cache = forward(queries, received.astype(jnp.float32), key_mask, weights, False)
        mlp_grads, d_resid = mlp_back(cache, grad_in, weights)
        attn_grads, d_input, d_side = attn_back(cache, d_resid, key_mask, weights, False)
        return (result, assemble(attn_grads, mlp_grads), d_input, d_side)

    def wait_side():
        return (
            early_side,
            blank_grads,
            jnp.zeros(shape_main, jnp.float32),
            jnp.zeros(shape_main, jnp.float32),
        )

    produced, late_grads, late_input, side_grads = lax.cond(encoder, wait_side, regress)
    returned = shifted(side_grads.astype(jnp.bfloat16), "section", -1).astype(side_grads.dtype)
    total_grad = grad_in + returned

    def encode_back():
        result, cache = forward(queries, queries, key_mask, weights, True)
        mlp_grads, d_resid = mlp_back(cache, total_grad, weights)
        attn_grads, d_input, unused_side = attn_back(cache, d_resid, key_mask, weights, True)
        return (assemble(attn_grads, mlp_grads), d_input)

    all_grads, d_rows = lax.cond(encoder, encode_back, lambda: (late_grads, late_input))
    summed = combined_sum(all_grads, lax.axis_size("dp"))
    slot_of = patch_order[:, :, None] == jnp.arange(PATCH, dtype=jnp.int32)[None, None, :]
    position_rank = jnp.sum(
        jnp.where(slot_of, jnp.arange(PATCH, dtype=jnp.int32)[None, :, None], 0), axis=1
    )
    main_rows = jnp.where(encoder, latents.astype(jnp.float32), produced)
    main_ok = jnp.where(encoder, position_rank < visible_col, position_rank >= visible_col)
    main_slot = jnp.clip(position_rank - slot_start, 0, SLOTS - 1)
    side_slot = jnp.clip(position_rank - first_slot, 0, SLOTS - 1)
    side_rows = jnp.where(encoder, pick_rows(produced, side_slot), 0.0)
    block_out = jnp.where(main_ok[:, :, None], pick_rows(main_rows, main_slot), side_rows)
    grad_rows = jnp.where(main_ok[:, :, None], pick_rows(d_rows, main_slot), 0.0)
    return (
        block_out.astype(jnp.bfloat16)[None],
        grad_rows[None],
        summed[0][None],
        summed[1][None],
        summed[2][None],
        summed[3][None],
        summed[4][None],
        summed[5][None],
        summed[6][None],
        summed[7][None],
    )


def solution(mesh):
    return jax.shard_map(
        local,
        mesh=mesh,
        in_specs=(
            P("section", "dp", None, None),
            P("section", "dp", None, None),
            P("dp", None),
            P("dp"),
            P("section", None, None),
            P("section", None, None),
            P("section", None, None),
            P("section", None, None),
            P("section", None, None),
            P("section", None, None),
            P("section", None),
            P("section", None),
            P(),
            P(),
            P(),
            P(),
            P(),
            P(),
            P(),
            P(),
        ),
        out_specs=(
            P("section", "dp", None, None),
            P("section", "dp", None, None),
            P("section", "dp", None),
            P("section", "dp", None),
            P("section", "dp", None),
            P("section", "dp", None),
            P("section", None, "dp"),
            P("section", None, "dp"),
            P("section", "dp"),
            P("section", "dp"),
        ),
        check_vma=False,
    )
```

```python
from functools import partial

import jax
import jax.numpy as jnp
from jax import lax
from jax.experimental import pallas as pl
from jax.experimental.pallas import tpu as pltpu
from jax.sharding import PartitionSpec as P

HEADS = 12
PATCH = 196
D = 768
FF = 3072
EPS = 1e-06
NV = 144
NM = 128
FIRST = PATCH - NM
GROUP = 2
CHUNK = 32

BF = jnp.bfloat16
F32 = jnp.float32
MIB = 1024 * 1024

HBM = pl.BlockSpec(memory_space=pl.ANY)
VMEM = pl.BlockSpec(memory_space=pltpu.VMEM)
SMEM = pl.BlockSpec(memory_space=pltpu.SMEM)


def nn(a, b):
    return jnp.dot(a, b, preferred_element_type=F32)


def nt(a, b):
    return lax.dot_general(a, b, (((1,), (1,)), ((), ())), preferred_element_type=F32)


def tn(a, b):
    return lax.dot_general(a, b, (((0,), (0,)), ((), ())), preferred_element_type=F32)


def loop(count, body):
    def step(i, carry):
        body(i)
        return carry

    lax.fori_loop(0, count, step, 0)


def rows_of(i, size):
    return pl.ds(pl.multiple_of(i * size, size), size)


def f32_row(ref, row, col=0, width=D):
    return ref[pl.ds(row, 1), pl.ds(col, width)].astype(F32)


class Copies:
    def __init__(self, sems):
        self.sems = sems
        self.used = 0
        self.open = []

    def start(self, src, dst):
        copy = pltpu.make_async_copy(src, dst, self.sems.at[self.used])
        self.used += 1
        copy.start()
        self.open.append(copy)
        return copy

    def wait(self, *copies):
        for copy in copies:
            copy.wait()
            self.open.remove(copy)

    def finish(self):
        self.wait(*list(self.open))


def gelu_pair(u):
    size = jnp.abs(u)
    base = 1.0 + (0.3275911 * 0.7071067811865476) * size
    guess = pl.reciprocal(base, approx=True)
    t = guess * (2.0 - base * guess)
    ex = jnp.exp(-0.5 * (u * u))
    poly = 0.5306027145 * t - 0.7265760135
    poly = poly * t + 0.7107068705
    poly = poly * t - 0.142248368
    poly = poly * t + 0.127414796
    tail = poly * t * ex
    phi = jnp.where(u >= 0.0, 1.0 - tail, tail)
    return u * phi, phi + u * (0.3989422804014327 * ex)


def norm_rows(src, dst, rows, gain, shift):
    def body(i):
        sel = rows_of(i, CHUNK)
        x = src[sel, :].astype(F32)
        centered = x - jnp.mean(x, axis=-1, keepdims=True)
        var = jnp.mean(centered * centered, axis=-1, keepdims=True)
        dst[sel, :] = (centered * lax.rsqrt(var + EPS) * gain + shift).astype(BF)

    loop(rows // CHUNK, body)


def norm_back(src, grad, base, write, rows, gain):
    def step(i, carry):
        d_gain, d_shift = carry
        sel = rows_of(i, CHUNK)
        x = src[sel, :].astype(F32)
        dh = grad[sel, :]
        centered = x - jnp.mean(x, axis=-1, keepdims=True)
        var = jnp.mean(centered * centered, axis=-1, keepdims=True)
        rstd = lax.rsqrt(var + EPS)
        hat = centered * rstd
        g = dh * gain
        part = dh * hat
        dx = rstd * (
            g
            - jnp.mean(g, axis=-1, keepdims=True)
            - hat * jnp.mean(g * hat, axis=-1, keepdims=True)
        )
        if base is not None:
            dx = dx + base[sel, :].astype(F32)
        write(sel, dx)
        d_gain = d_gain + jnp.sum(part.reshape(CHUNK // 8, 8, D), axis=0)
        d_shift = d_shift + jnp.sum(dh.reshape(CHUNK // 8, 8, D), axis=0)
        return d_gain, d_shift

    zero = jnp.zeros((8, D), F32)
    d_gain, d_shift = lax.fori_loop(0, rows // CHUNK, step, (zero, zero))
    return jnp.sum(d_gain, axis=0, keepdims=True), jnp.sum(d_shift, axis=0, keepdims=True)


def column_sum(ref, rows, col=0, width=D):
    def step(i, carry):
        x = ref[rows_of(i, CHUNK), pl.ds(col, width)].astype(F32)
        return carry + jnp.sum(x.reshape(CHUNK // 8, 8, width), axis=0)

    total = lax.fori_loop(0, rows // CHUNK, step, jnp.zeros((8, width), F32))
    return jnp.sum(total, axis=0, keepdims=True)


def as_bf16(flags):
    return jnp.where(flags, 1.0, 0.0).astype(BF)


def pick_matrix(order_col, image, start, count, low, high):
    col = order_col[pl.ds(start, count), pl.ds(image, 1)]
    rank = start + lax.broadcasted_iota(jnp.int32, (count, 1), 0)
    col = jnp.where((rank >= low) & (rank < high), col, -1)
    return as_bf16(col == lax.broadcasted_iota(jnp.int32, (count, PATCH), 1))


def place_matrix(order_row, image, start, count, low, high):
    row = order_row[pl.ds(image, 1), pl.ds(start, count)]
    rank = start + lax.broadcasted_iota(jnp.int32, (1, count), 1)
    row = jnp.where((rank >= low) & (rank < high), row, -1)
    return as_bf16(row == lax.broadcasted_iota(jnp.int32, (PATCH, count), 0))


def head_masks(rows):
    lane = lax.broadcasted_iota(jnp.int32, (rows, 128), 1)
    return lane < 64, lane >= 64


def attention_forward(images, nq, nk, q, k, v, p, o, key_ok):
    def body(i):
        image = i // 2
        qs, ks = rows_of(image, nq), rows_of(image, nk)
        ok = key_ok(image)
        for step in range(3):
            pair = (i % 2) * 3 + step
            lanes = pl.ds(pl.multiple_of(pair * 128, 128), 128)
            q2, k2, v2 = q[qs, lanes], k[ks, lanes], v[ks, lanes]
            mixed = None
            for part in range(2):
                mine = head_masks(nq)[part]
                scores = nt(k2, jnp.where(mine, q2, jnp.zeros_like(q2)))
                scores = jnp.where(ok, scores, -1000000000.0)
                ex = jnp.exp(scores - jnp.max(scores, axis=0, keepdims=True))
                probs = (ex * (1.0 / jnp.sum(ex, axis=0, keepdims=True))).astype(BF)
                if p is not None:
                    p[image * HEADS + pair * 2 + part] = probs
                term = tn(probs, jnp.where(head_masks(nk)[part], v2, jnp.zeros_like(v2)))
                mixed = term if mixed is None else mixed + term
            o[qs, lanes] = mixed.astype(BF)

    loop(images * 2, body)


def attention_back(images, nq, nk, q, k, v, p, do, dq, dk, dv):
    def body(i):
        image = i // 2
        qs, ks = rows_of(image, nq), rows_of(image, nk)
        for step in range(3):
            pair = (i % 2) * 3 + step
            lanes = pl.ds(pl.multiple_of(pair * 128, 128), 128)
            q2, k2, v2, do2 = q[qs, lanes], k[ks, lanes], v[ks, lanes], do[qs, lanes]
            dq2 = dk2 = dv2 = None
            for part in range(2):
                mine_q, mine_k = head_masks(nq)[part], head_masks(nk)[part]
                qm = jnp.where(mine_q, q2, jnp.zeros_like(q2))
                dom = jnp.where(mine_q, do2, jnp.zeros_like(do2))
                km = jnp.where(mine_k, k2, jnp.zeros_like(k2))
                probs = p[image * HEADS + pair * 2 + part]
                wide = probs.astype(F32)
                d_probs = nt(v2, dom)
                delta = jnp.sum(d_probs * wide, axis=0, keepdims=True)
                d_scores = (wide * (d_probs - delta)).astype(BF)
                terms = (tn(d_scores, km), nn(d_scores, qm), nn(probs, dom))
                if part == 0:
                    dq2, dk2, dv2 = terms
                else:
                    dq2, dk2, dv2 = dq2 + terms[0], dk2 + terms[1], dv2 + terms[2]
            dq[qs, lanes] = (dq2 * 0.125).astype(BF)
            dk[ks, lanes] = dk2.astype(BF)
            dv[ks, lanes] = dv2.astype(BF)

    loop(images * 2, body)


def mlp_forward(rows, h2, w1, w2, up_b, u, a, gp, acc):
    def body(j):
        for n in range(3):
            cols = pl.ds(pl.multiple_of(j * D + n * 256, 256), 256)
            half = u.at[n % 2]
            half[pl.ds(0, rows), :] = nn(h2[...], w1[:, cols]) + up_b[pl.ds(0, 1), cols].astype(F32)
            for r in range(0, rows, CHUNK):
                value, slope = gelu_pair(half[pl.ds(r, CHUNK), :])
                a[pl.ds(r, CHUNK), cols] = value.astype(BF)
                if gp is not None:
                    gp[pl.ds(r, CHUNK), cols] = slope.astype(BF)
        wide = pl.ds(pl.multiple_of(j * D, D), D)
        acc[...] += nn(a[:, wide], w2[wide, :])

    loop(FF // D, body)


def mlp_back(rows, dyb, gp, w1, w2, du, acc):
    def body(j):
        for n in range(3):
            cols = pl.ds(pl.multiple_of(j * D + n * 256, 256), 256)
            d_active = nt(dyb[...], w2[cols, :])
            du[:, cols] = (gp[:, cols].astype(F32) * d_active).astype(BF)
        wide = pl.ds(pl.multiple_of(j * D, D), D)
        acc[...] += nt(du[:, wide], w1[:, wide])

    acc[...] = jnp.zeros_like(acc)
    loop(FF // D, body)


def cost(flops, nbytes):
    return pl.CostEstimate(flops=int(flops), bytes_accessed=int(nbytes), transcendentals=0)


def params(mib):
    return pltpu.CompilerParams(vmem_limit_bytes=mib * MIB)


def struct(shape, dtype=BF):
    return jax.ShapeDtypeStruct(shape, dtype)


def start_weights(copies, sources, scratch):
    return [copies.start(src, dst) for src, dst in zip(sources, scratch)]


def encode_kernel(group, role, visible, order_col, gains, biases, qvb, upb, rows, wqkv, wo, w1, w2,
                  lat_out, x_out, hq_out, q_out, k_out, v_out, p_out, o_out, y1_out, h2_out, gp_out, a_out,
                  rows_v, sqkv, so, s1, s2, x, hq, q, k, v, p, o, y1, h2, gp, a, u, acc, lat, sems):
    n = GROUP * NV

    @pl.when(role[0] == 0)
    def _():
        copies = Copies(sems)
        got_rows = copies.start(rows.at[0, pl.ds(group * GROUP, GROUP)], rows_v)
        got_qkv, got_o, got_1, got_2 = start_weights(
            copies, (wqkv.at[0], wo.at[0], w1.at[0], w2.at[0]), (sqkv, so, s1, s2)
        )
        gain, bias = gains.at[0], biases.at[0]
        copies.wait(got_rows)
        for i in range(GROUP):
            image = group * GROUP + i
            pick = pick_matrix(order_col, image, 0, NV, 0, visible[image])
            x[pl.ds(i * NV, NV), :] = nn(pick, rows_v[i]).astype(BF)
        copies.start(x, x_out)
        norm_rows(x, hq, n, f32_row(gain, 0), f32_row(bias, 0))
        copies.start(hq, hq_out)
        copies.wait(got_qkv)
        q[...] = ((nn(hq[...], sqkv[:, 0:D]) + f32_row(qvb, 0)).astype(BF) * 0.125).astype(BF)
        k[...] = nn(hq[...], sqkv[:, D : 2 * D]).astype(BF)
        v[...] = (nn(hq[...], sqkv[:, 2 * D :]) + f32_row(qvb, 0, D)).astype(BF)
        copies.start(q, q_out)
        copies.start(k, k_out)
        copies.start(v, v_out)

        def key_ok(i):
            place = lax.broadcasted_iota(jnp.int32, (NV, 1), 0)
            return place < visible[group * GROUP + i]

        attention_forward(GROUP, NV, NV, q, k, v, p, o, key_ok)
        copies.start(p, p_out)
        copies.start(o, o_out)
        copies.wait(got_o)
        y1[...] = nn(o[...], so[...]) + f32_row(bias, 1) + x[...].astype(F32)
        copies.start(y1, y1_out)
        norm_rows(y1, h2, n, f32_row(gain, 1), f32_row(bias, 2))
        copies.start(h2, h2_out)
        acc[...] = y1[...] + f32_row(bias, 3)
        copies.wait(got_1, got_2)
        mlp_forward(n, h2, s1, s2, upb, u, a, gp, acc)
        copies.start(gp, gp_out)
        copies.start(a, a_out)
        lat[...] = acc[...].astype(BF)
        copies.start(lat, lat_out)
        copies.finish()


def encode(group, role, visible, order_col, gains, biases, qvb, upb, rows, weights):
    n = GROUP * NV
    row, wide = struct((n, D)), struct((n, FF))
    heads = struct((GROUP * HEADS, NV, NV))
    outs = [row] * 6 + [heads, row, struct((n, D), F32), row, wide, wide]
    vm = lambda s: pltpu.VMEM(s.shape, s.dtype)
    scratch = [
        pltpu.VMEM((GROUP, PATCH, D), BF),
        pltpu.VMEM((D, 3 * D), BF), pltpu.VMEM((D, D), BF), pltpu.VMEM((D, FF), BF), pltpu.VMEM((FF, D), BF),
        vm(row), vm(row), vm(row), vm(row), vm(row), vm(heads), vm(row), pltpu.VMEM((n, D), F32), vm(row),
        vm(wide), vm(wide), pltpu.VMEM((2, n, 256), F32), pltpu.VMEM((n, D), F32), vm(row),
        pltpu.SemaphoreType.DMA((20,)),
    ]
    return pl.pallas_call(
        partial(encode_kernel, group),
        in_specs=[SMEM, SMEM] + [VMEM] * 5 + [HBM] * 5,
        out_specs=[HBM] * len(outs),
        out_shape=outs,
        scratch_shapes=scratch,
        compiler_params=params(56),
        cost_estimate=cost(2 * n * 12 * D * D, 25e6),
        name="encode",
    )(role, visible, order_col, gains, biases, qvb, upb, rows, *weights)


def middle_kernel(group, role, visible, order_col, gains, biases, qvb, upb, tgains, tbiases, tqvb, tupb,
                  rows, cot, lat_in, wqkv, wo, w1, w2, tqkv, to, t1, t2,
                  dlat_out, res_out, hq_out, hk_out, dq_out, dk_out, dv_out, o_out, dy1b_out, h2_out, du_out, a_out,
                  dyb_out, dx_out, sums_out,
                  rows_v, cot_v, sqkv, so, s1, s2, x, lat, hq, hk, q, k, v, p, o, y1, h2, gp, a, u, acc,
                  res, dyb, du, dy1, dy1b, do, dq, dk, dv, dh, dlat, sums, sems):
    n, m = GROUP * NM, GROUP * NV

    def shared(copies, sources, gain, bias, qv, ub, target):
        got_rows = copies.start(rows.at[0, pl.ds(group * GROUP, GROUP)], rows_v)
        got_qkv = copies.start(sources[0], sqkv)
        if not target:
            got_lat = copies.start(lat_in, lat)
        got_o, got_1, got_2 = start_weights(copies, sources[1:], (so, s1, s2))
        if not target:
            got_cot = copies.start(cot.at[0, pl.ds(group * GROUP, GROUP)], cot_v)
        copies.wait(got_rows)
        for i in range(GROUP):
            image = group * GROUP + i
            pick = pick_matrix(order_col, image, FIRST, NM, visible[image], PATCH)
            x[pl.ds(i * NM, NM), :] = nn(pick, rows_v[i]).astype(BF)
        norm_rows(x, hq, n, f32_row(gain, 0), f32_row(bias, 0))
        copies.wait(got_qkv)
        q[...] = ((nn(hq[...], sqkv[:, 0:D]) + f32_row(qv, 0)).astype(BF) * 0.125).astype(BF)
        if target:
            k[pl.ds(0, n), :] = nn(hq[...], sqkv[:, D : 2 * D]).astype(BF)
            v[pl.ds(0, n), :] = (nn(hq[...], sqkv[:, 2 * D :]) + f32_row(qv, 0, D)).astype(BF)
        else:
            copies.start(hq, hq_out)
            copies.wait(got_lat)
            norm_rows(lat, hk, m, f32_row(gain, 0), f32_row(bias, 0))
            copies.start(hk, hk_out)
            k[...] = nn(hk[...], sqkv[:, D : 2 * D]).astype(BF)
            v[...] = (nn(hk[...], sqkv[:, 2 * D :]) + f32_row(qv, 0, D)).astype(BF)
        nk = NM if target else NV

        def key_ok(i):
            place = lax.broadcasted_iota(jnp.int32, (nk, 1), 0)
            count = visible[group * GROUP + i]
            return place + FIRST >= count if target else place < count

        attention_forward(GROUP, NM, nk, q, k, v, None if target else p, o, key_ok)
        copies.wait(got_o)
        y1[...] = nn(o[...], so[...]) + f32_row(bias, 1) + x[...].astype(F32)
        norm_rows(y1, h2, n, f32_row(gain, 1), f32_row(bias, 2))
        acc[...] = y1[...] + f32_row(bias, 3)
        copies.wait(got_1, got_2)
        mlp_forward(n, h2, s1, s2, ub, u, a, None if target else gp, acc)
        res[...] = acc[...].astype(BF)
        copies.start(res, res_out)
        return None if target else got_cot

    @pl.when(role[0] == 0)
    def _():
        copies = Copies(sems)
        shared(copies, (tqkv, to, t1, t2), tgains, tbiases, tqvb, tupb, True)
        copies.finish()

    @pl.when(role[0] == 1)
    def _():
        copies = Copies(sems)
        gain = gains.at[0]
        got_cot = shared(
            copies, (wqkv.at[0], wo.at[0], w1.at[0], w2.at[0]), gain, biases.at[0], qvb, upb.at[0:1], False
        )
        copies.start(o, o_out)
        copies.start(h2, h2_out)
        copies.start(a, a_out)
        copies.wait(got_cot)
        for i in range(GROUP):
            image = group * GROUP + i
            pick = pick_matrix(order_col, image, FIRST, NM, visible[image], PATCH)
            dyb[pl.ds(i * NM, NM), :] = nn(pick, cot_v[i]).astype(BF)
        copies.start(dyb, dyb_out)
        mlp_back(n, dyb, gp, s1, s2, du, acc)
        copies.start(du, du_out)

        def keep(sel, dx):
            dy1[sel, :] = dx
            dy1b[sel, :] = dx.astype(BF)

        g2, b2 = norm_back(y1, acc, dyb, keep, n, f32_row(gain, 1))
        copies.start(dy1b, dy1b_out)
        do[...] = nt(dy1b[...], so[...]).astype(BF)
        attention_back(GROUP, NM, NV, q, k, v, p, do, dq, dk, dv)
        copies.start(dq, dq_out)
        copies.start(dk, dk_out)
        copies.start(dv, dv_out)
        dh[...] = nt(dk[...], sqkv[:, D : 2 * D]) + nt(dv[...], sqkv[:, 2 * D :])

        def keep_side(sel, dx):
            dlat[sel, :] = dx.astype(BF)

        gk, bk = norm_back(lat, dh, None, keep_side, m, f32_row(gain, 0))
        copies.start(dlat, dlat_out)
        acc[...] = nt(dq[...], sqkv[:, 0:D])

        def keep_input(sel, dx):
            dy1[sel, :] = dx

        gq, bq = norm_back(x, acc, dy1, keep_input, n, f32_row(gain, 0))
        copies.start(dy1, dx_out)
        for row, value in enumerate((gq + gk, g2, bq + bk, b2)):
            sums[pl.ds(row, 1), :] = value
        copies.start(sums, sums_out)
        copies.finish()


def middle(group, role, visible, order_col, own_vecs, target_vecs, rows, cot, lat, weights, targets):
    n, m = GROUP * NM, GROUP * NV
    row, side, wide = struct((n, D)), struct((m, D)), struct((n, FF))
    outs = [side, row, row, side, row, side, side, row, row, row, wide, wide, row, struct((n, D), F32), struct((8, D), F32)]
    vm = lambda s: pltpu.VMEM(s.shape, s.dtype)
    full, fside = pltpu.VMEM((n, D), F32), pltpu.VMEM((m, D), F32)
    scratch = [
        pltpu.VMEM((GROUP, PATCH, D), BF), pltpu.VMEM((GROUP, PATCH, D), BF),
        pltpu.VMEM((D, 3 * D), BF), pltpu.VMEM((D, D), BF), pltpu.VMEM((D, FF), BF), pltpu.VMEM((FF, D), BF),
        vm(row), vm(side), vm(row), vm(side), vm(row), vm(side), vm(side),
        pltpu.VMEM((GROUP * HEADS, NV, NM), BF), vm(row), full, vm(row), vm(wide), vm(wide),
        pltpu.VMEM((2, n, 256), F32), full,
        vm(row), vm(row), vm(wide), full, vm(row), vm(row), vm(row), vm(side), vm(side), fside, vm(side),
        pltpu.VMEM((8, D), F32),
        pltpu.SemaphoreType.DMA((24,)),
    ]
    return pl.pallas_call(
        partial(middle_kernel, group),
        in_specs=[SMEM, SMEM] + [VMEM] * 9 + [HBM] * 11,
        out_specs=[HBM] * len(outs),
        out_shape=outs,
        scratch_shapes=scratch,
        compiler_params=params(56),
        cost_estimate=cost(4 * n * 12 * D * D, 25e6),
        name="middle",
    )(role, visible, order_col, *own_vecs, *target_vecs, rows, cot, lat, *weights, *targets)


def stack_rows(copies, pieces, ref, size):
    return [copies.start(piece, ref.at[pl.ds(i * size, size)]) for i, piece in enumerate(pieces)]


def clear_tail(ref, used):
    ref[pl.ds(used, ref.shape[0] - used), :] = jnp.zeros((ref.shape[0] - used, ref.shape[1]), ref.dtype)


def down_kernel(groups, role, visible, order_col, cot, *refs):
    lat = refs[:groups]
    a_enc, a_reg, dyb_reg = (refs[i * groups : (i + 1) * groups] for i in (1, 2, 3))
    dw2, dyb_out, sums_out, cot_v, dyb, a, dlat, out, sums, sems = refs[4 * groups :]
    images = groups * GROUP
    nv, nm = GROUP * NV, GROUP * NM

    @pl.when(role[0] == 0)
    def _():
        copies = Copies(sems)
        got = [copies.start(cot.at[0], cot_v)] + stack_rows(copies, lat, dlat, nv)
        got_a = stack_rows(copies, a_enc, a, nv)
        copies.wait(*got)
        for i in range(images):
            pick = pick_matrix(order_col, i, 0, NV, 0, visible[i])
            sel = pl.ds(i * NV, NV)
            dyb[sel, :] = (nn(pick, cot_v[i]) + dlat[sel, :].astype(F32)).astype(BF)
        copies.start(dyb, dyb_out)
        copies.finish()

    @pl.when(role[0] == 1)
    def _():
        copies = Copies(sems)
        stack_rows(copies, a_reg, a, nm)
        stack_rows(copies, dyb_reg, dyb, nm)
        clear_tail(a, images * NM)
        clear_tail(dyb, images * NM)
        copies.finish()

    copies = Copies(sems)
    for j in range(4):
        def body(t, j=j):
            cols = pl.ds(pl.multiple_of(j * D + t * 256, 256), 256)
            out[pl.ds(pl.multiple_of(j * D + t * 256, 256), 256), :] = tn(a[:, cols], dyb[...]).astype(BF)

        loop(3, body)
        copies.start(out.at[pl.ds(j * D, D)], dw2.at[pl.ds(j * D, D)])
    sums[...] = jnp.broadcast_to(column_sum(dyb, images * NV), (8, D))
    copies.start(sums, sums_out)
    copies.finish()


def down_grad(groups, role, visible, order_col, cot, dlat, a_enc, a_reg, dyb_reg):
    n = groups * GROUP * NV
    outs = [struct((FF, D)), struct((n, D)), struct((8, D), F32)]
    scratch = [
        pltpu.VMEM((groups * GROUP, PATCH, D), BF), pltpu.VMEM((n, D), BF), pltpu.VMEM((n, FF), BF),
        pltpu.VMEM((n, D), BF), pltpu.VMEM((FF, D), BF), pltpu.VMEM((8, D), F32), pltpu.SemaphoreType.DMA((12,)),
    ]
    return pl.pallas_call(
        partial(down_kernel, groups),
        in_specs=[SMEM, SMEM, VMEM] + [HBM] * (1 + 4 * groups),
        out_specs=[HBM] * len(outs),
        out_shape=outs,
        scratch_shapes=scratch,
        compiler_params=params(56),
        cost_estimate=cost(2 * n * 4 * D * D, 15e6),
        name="down_grad",
    )(role, visible, order_col, cot, *dlat, *a_enc, *a_reg, *dyb_reg)


def up_kernel(groups, role, gains, dyb_in, w1, w2, *refs):
    y1_enc, gp_enc, h2_enc, du_reg, h2_reg = (refs[i * groups : (i + 1) * groups] for i in range(5))
    dw1, dy1_out, sums_out, s1, s2, dyb, gp, y1, h2, du, acc, dy1, out, sums, sems = refs[5 * groups :]
    images = groups * GROUP
    nv, nm = GROUP * NV, GROUP * NM

    @pl.when(role[0] == 0)
    def _():
        copies = Copies(sems)
        got = [copies.start(dyb_in, dyb), copies.start(w2.at[0], s2)]
        got += stack_rows(copies, gp_enc, gp, nv)
        got.append(copies.start(w1.at[0], s1))
        got_y = stack_rows(copies, y1_enc, y1, nv)
        stack_rows(copies, h2_enc, h2, nv)
        copies.wait(*got)
        mlp_back(images * NV, dyb, gp, s1, s2, du, acc)
        copies.wait(*got_y)

        def keep(sel, dx):
            dy1[sel, :] = dx

        g2, b2 = norm_back(y1, acc, dyb, keep, images * NV, f32_row(gains.at[0], 1))
        copies.start(dy1, dy1_out)
        sums[pl.ds(0, 1), :] = g2
        sums[pl.ds(1, 1), :] = b2
        copies.finish()

    @pl.when(role[0] == 1)
    def _():
        copies = Copies(sems)
        stack_rows(copies, du_reg, du, nm)
        stack_rows(copies, h2_reg, h2, nm)
        clear_tail(du, images * NM)
        clear_tail(h2, images * NM)
        sums[pl.ds(0, 2), :] = jnp.zeros((2, D), F32)
        copies.finish()

    copies = Copies(sems)
    for j in range(4):
        def body(t, j=j):
            cols = pl.ds(pl.multiple_of(j * D + t * 256, 256), 256)
            out[j, :, pl.ds(pl.multiple_of(t * 256, 256), 256)] = tn(h2[...], du[:, cols]).astype(BF)

        loop(3, body)
        copies.start(out.at[j], dw1.at[j])
        sums[pl.ds(4 + j, 1), :] = column_sum(du, images * NV, j * D)
    copies.start(sums, sums_out)
    copies.finish()


def up_grad(groups, role, gains, dyb, w1, w2, y1_enc, gp_enc, h2_enc, du_reg, h2_reg):
    n = groups * GROUP * NV
    outs = [struct((4, D, D)), struct((n, D), F32), struct((8, D), F32)]
    scratch = [
        pltpu.VMEM((D, FF), BF), pltpu.VMEM((FF, D), BF), pltpu.VMEM((n, D), BF), pltpu.VMEM((n, FF), BF),
        pltpu.VMEM((n, D), F32), pltpu.VMEM((n, D), BF), pltpu.VMEM((n, FF), BF), pltpu.VMEM((n, D), F32),
        pltpu.VMEM((n, D), F32), pltpu.VMEM((4, D, D), BF), pltpu.VMEM((8, D), F32), pltpu.SemaphoreType.DMA((16,)),
    ]
    return pl.pallas_call(
        partial(up_kernel, groups),
        in_specs=[SMEM, VMEM] + [HBM] * (3 + 5 * groups),
        out_specs=[HBM] * len(outs),
        out_shape=outs,
        scratch_shapes=scratch,
        compiler_params=params(56),
        cost_estimate=cost(6 * n * 4 * D * D, 25e6),
        name="up_grad",
    )(role, gains, dyb, w1, w2, *y1_enc, *gp_enc, *h2_enc, *du_reg, *h2_reg)


def attn_kernel(groups, role, dy1_in, wqkv, wo, *refs):
    parts = [refs[i * groups : (i + 1) * groups] for i in range(13)]
    q_enc, k_enc, v_enc, p_enc, o_enc, hq_enc = parts[:6]
    hq_reg, hk_reg, dq_reg, dk_reg, dv_reg, o_reg, dy1b_reg = parts[6:]
    (dwa, dh_out, sums_out,
     sqkv, so, dy1, dy1b, q, k, v, p, o, hq, hk, do, dq, dk, dv, dh, out, sums, sems) = refs[13 * groups :]
    images = groups * GROUP
    nv, nm = GROUP * NV, GROUP * NM

    @pl.when(role[0] == 0)
    def _():
        copies = Copies(sems)
        got = [copies.start(dy1_in, dy1), copies.start(wo.at[0], so)]
        for pieces, ref in ((q_enc, q), (k_enc, k), (v_enc, v)):
            got += stack_rows(copies, pieces, ref, nv)
        got += stack_rows(copies, p_enc, p, GROUP * HEADS)
        stack_rows(copies, o_enc, o, nv)
        stack_rows(copies, hq_enc, hq, nv)
        stack_rows(copies, hq_enc, hk, nv)
        copies.wait(*got)
        dy1b[...] = dy1[...].astype(BF)
        do[...] = nt(dy1b[...], so[...]).astype(BF)
        attention_back(images, NV, NV, q, k, v, p, do, dq, dk, dv)
        copies.finish()

    @pl.when(role[0] == 1)
    def _():
        copies = Copies(sems)
        for pieces, ref in ((hq_reg, hq), (dq_reg, dq), (o_reg, o), (dy1b_reg, dy1b)):
            stack_rows(copies, pieces, ref, nm)
            clear_tail(ref, images * NM)
        for pieces, ref in ((hk_reg, hk), (dk_reg, dk), (dv_reg, dv)):
            stack_rows(copies, pieces, ref, nv)
        copies.finish()

    copies = Copies(sems)
    for j, (left, right) in enumerate(((o, dy1b), (hq, dq), (hk, dk), (hk, dv))):
        out[j] = tn(left[...], right[...]).astype(BF)
        copies.start(out.at[j], dwa.at[j])
    for row, ref in ((0, dy1b), (1, dq), (2, dv)):
        sums[pl.ds(row, 1), :] = column_sum(ref, images * NV)
    copies.start(sums, sums_out)

    @pl.when(role[0] == 0)
    def _():
        copies = Copies(sems.at[pl.ds(8, 2)])
        copies.wait(copies.start(wqkv.at[0], sqkv))
        dh[...] = nt(dq[...], sqkv[:, 0:D]) + nt(dk[...], sqkv[:, D : 2 * D]) + nt(dv[...], sqkv[:, 2 * D :])
        copies.wait(copies.start(dh, dh_out))

    copies.finish()


def attn_grad(groups, role, dy1, wqkv, wo, *parts):
    n = groups * GROUP * NV
    row = pltpu.VMEM((n, D), BF)
    outs = [struct((4, D, D)), struct((n, D), F32), struct((8, D), F32)]
    scratch = [
        pltpu.VMEM((D, 3 * D), BF), pltpu.VMEM((D, D), BF), pltpu.VMEM((n, D), F32), row, row, row, row,
        pltpu.VMEM((groups * GROUP * HEADS, NV, NV), BF), row, row, row, row, row, row, row,
        pltpu.VMEM((n, D), F32), pltpu.VMEM((4, D, D), BF), pltpu.VMEM((8, D), F32), pltpu.SemaphoreType.DMA((20,)),
    ]
    return pl.pallas_call(
        partial(attn_kernel, groups),
        in_specs=[SMEM] + [HBM] * (3 + 13 * groups),
        out_specs=[HBM] * len(outs),
        out_shape=outs,
        scratch_shapes=scratch,
        compiler_params=params(56),
        cost_estimate=cost(6 * n * 4 * D * D, 25e6),
        name="attn_grad",
    )(role, dy1, wqkv, wo, *[ref for part in parts for ref in part])


def place_kernel(groups, role, visible, order_row, gains, dh_in, dy1_in, *refs):
    x_enc, lat_enc, res, dx_reg = (refs[i * groups : (i + 1) * groups] for i in range(4))
    block_out, grad_out, sums_out, x, dh, dy1, lat, out, sems = refs[4 * groups :]
    images = groups * GROUP
    nv, nm = GROUP * NV, GROUP * NM

    def put_grad(i, put, value):
        high = value.astype(BF)
        low = (value - high.astype(F32)).astype(BF)
        grad_out[0, i] = nn(put, high) + nn(put, low)

    @pl.when(role[0] == 0)
    def _():
        copies = Copies(sems)
        got = [copies.start(dh_in, dh), copies.start(dy1_in, dy1)] + stack_rows(copies, x_enc, x, nv)
        got_out = stack_rows(copies, lat_enc, lat, nv) + stack_rows(copies, res, out, nm)
        copies.wait(*got)

        def keep(sel, dx):
            dy1[sel, :] = dx

        gq, bq = norm_back(x, dh, dy1, keep, images * NV, f32_row(gains.at[0], 0))
        sums_out[pl.ds(0, 1), :] = gq
        sums_out[pl.ds(1, 1), :] = bq
        copies.wait(*got_out)
        for i in range(images):
            put = place_matrix(order_row, i, 0, NV, 0, visible[i])
            put_side = place_matrix(order_row, i, FIRST, NM, visible[i], PATCH)
            put_grad(i, put, dy1[pl.ds(i * NV, NV), :])
            block_out[0, i] = (nn(put, lat[pl.ds(i * NV, NV), :]) + nn(put_side, out[pl.ds(i * NM, NM), :])).astype(BF)

    @pl.when(role[0] == 1)
    def _():
        copies = Copies(sems)
        stack_rows(copies, res, out, nm)
        stack_rows(copies, dx_reg, dy1, nm)
        copies.finish()
        sums_out[...] = jnp.zeros_like(sums_out)
        for i in range(images):
            put = place_matrix(order_row, i, FIRST, NM, visible[i], PATCH)
            put_grad(i, put, dy1[pl.ds(i * NM, NM), :])
            block_out[0, i] = nn(put, out[pl.ds(i * NM, NM), :]).astype(BF)


def place(groups, role, visible, order_row, gains, dh, dy1, x_enc, lat_enc, res, dx_reg):
    images = groups * GROUP
    n = images * NV
    outs = [struct((1, images, PATCH, D)), struct((1, images, PATCH, D), F32), struct((8, D), F32)]
    scratch = [
        pltpu.VMEM((n, D), BF), pltpu.VMEM((n, D), F32), pltpu.VMEM((n, D), F32), pltpu.VMEM((n, D), BF),
        pltpu.VMEM((images * NM, D), BF), pltpu.SemaphoreType.DMA((12,)),
    ]
    return pl.pallas_call(
        partial(place_kernel, groups),
        in_specs=[SMEM, SMEM, VMEM, VMEM] + [HBM] * (2 + 4 * groups),
        out_specs=[VMEM] * len(outs),
        out_shape=outs,
        scratch_shapes=scratch,
        compiler_params=params(40),
        cost_estimate=cost(1e9, 15e6),
        name="place",
    )(role, visible, order_row, gains, dh, dy1, *x_enc, *lat_enc, *res, *dx_reg)


def half_pick(a, axis, index):
    return lax.dynamic_index_in_dim(a, index, axis, keepdims=False)


def tree_scatter(value, axis):
    me = lax.axis_index("dp")
    shape = value.shape
    value = value.reshape(shape[:axis] + (2, 2, 2, 2) + shape[axis + 1 :])
    kind = value.dtype
    for bit, place_axis in ((1, axis + 3), (2, axis + 2), (4, axis + 1), (8, axis)):
        mine = (me // bit) % 2
        sent = half_pick(value, place_axis, 1 - mine).astype(kind)
        kept = half_pick(value, place_axis, mine)
        got = lax.ppermute(sent, "dp", [(i, i ^ bit) for i in range(16)])
        value = kept.astype(F32) + got.astype(F32)
    return value


def scatter_blocks(blocks, count):
    own = D // count
    shards = blocks.reshape(blocks.shape[0], count, own, D)
    if count == 16:
        return tree_scatter(shards, 1)
    return lax.psum_scatter(shards, "dp", scatter_dimension=1, tiled=True)[:, 0].astype(F32)


def scatter_small(rows, count):
    own = D // count
    flat = jnp.concatenate(
        [
            jnp.moveaxis(rows[:6].reshape(6, count, own), 1, 0).reshape(count, 6 * own),
            rows[6:8].reshape(count, 2 * own),
            rows[8:12].reshape(count, 4 * own),
        ],
        axis=1,
    )
    if count == 16:
        got = tree_scatter(flat, 0)
    else:
        got = lax.psum_scatter(flat, "dp", scatter_dimension=0, tiled=True)[0]
    return (
        got[: 2 * own].reshape(2, own),
        got[2 * own : 6 * own].reshape(4, own),
        got[6 * own : 8 * own],
        got[8 * own :],
    )


def side_by_side(blocks):
    return jnp.concatenate([blocks[i] for i in range(blocks.shape[0])], axis=1)


def local(
    patch_rows, cotangent, patch_order, visible, qkv_weight, out_weight, up_weight, down_weight, norm_gains, biases,
    qv_bias, up_bias, target_qkv, target_out, target_up, target_down, target_gains, target_biases, target_qv_bias,
    target_up_bias,
):
    section = lax.axis_index("section").astype(jnp.int32)
    role = section.reshape(1)
    images = patch_order.shape[0]
    groups = images // GROUP
    count = lax.axis_size("dp")
    order_col = patch_order.T
    weights = (qkv_weight, out_weight, up_weight, down_weight)
    targets = (target_qkv, target_out, target_up, target_down)
    vecs = (norm_gains, biases, qv_bias, up_bias)
    target_vecs = (target_gains, target_biases, target_qv_bias[None], target_up_bias[None])

    encoded = [encode(g, role, visible, order_col, *vecs, patch_rows, weights) for g in range(groups)]
    lat, x_e, hq_e, q_e, k_e, v_e, p_e, o_e, y1_e, h2_e, gp_e, a_e = zip(*encoded)
    sent = [lax.ppermute(piece, "section", [(0, 1)]) for piece in lat]
    middles = [
        middle(g, role, visible, order_col, vecs, target_vecs, patch_rows, cotangent, sent[g], weights, targets)
        for g in range(groups)
    ]
    (dlat, res, hq_r, hk_r, dq_r, dk_r, dv_r, o_r, dy1b_r, h2_r, du_r, a_r, dyb_r, dx_r, sums_r) = zip(*middles)
    back = [lax.ppermute(piece, "section", [(1, 0)]) for piece in dlat]
    dw2, dyb, sums_down = down_grad(groups, role, visible, order_col, cotangent, back, a_e, a_r, dyb_r)
    dw1, dy1, sums_up = up_grad(
        groups, role, norm_gains, dyb, up_weight, down_weight, y1_e, gp_e, h2_e, du_r, h2_r
    )
    dwa, dh, sums_attn = attn_grad(
        groups, role, dy1, qkv_weight, out_weight, q_e, k_e, v_e, p_e, o_e, hq_e,
        hq_r, hk_r, dq_r, dk_r, dv_r, o_r, dy1b_r,
    )
    block_out, grad_rows, sums_in = place(
        groups, role, visible, patch_order, norm_gains, dh, dy1, x_e, lat, res, dx_r
    )
    sums_reg = sums_r[0]
    for more in sums_r[1:]:
        sums_reg = sums_reg + more
    norms = jnp.where(
        section == 0, jnp.stack([sums_in[0], sums_up[0], sums_in[1], sums_up[1]]), sums_reg[:4]
    )
    small = jnp.concatenate(
        [
            norms[0:3],
            sums_attn[0:1],
            norms[3:4],
            sums_down[0:1],
            sums_attn[1:3],
            sums_up[4:8],
        ],
        axis=0,
    )
    own_down = D * 4 // count
    if count == 16:
        grad_down = tree_scatter(dw2.reshape(16, own_down, D), 0)
    else:
        grad_down = lax.psum_scatter(dw2, "dp", scatter_dimension=0, tiled=True).astype(F32)
    up = scatter_blocks(dw1, count)
    attn = scatter_blocks(dwa, count)
    gains, bias_rows, qv_rows, up_rows = scatter_small(small, count)
    return (
        block_out,
        grad_rows,
        side_by_side(attn[1:4])[None],
        attn[0][None],
        side_by_side(up)[None],
        grad_down[None],
        gains[None],
        bias_rows[None],
        qv_rows[None],
        up_rows[None],
    )


def solution(mesh):
    three, four = P("section", None, None), P("section", "dp", None, None)
    grad = P("section", "dp", None)
    return jax.shard_map(
        local,
        mesh=mesh,
        in_specs=(four, four, P("dp", None), P("dp"), three, three, three, three, three, three,
                  P("section", None), P("section", None), P(), P(), P(), P(), P(), P(), P(), P()),
        out_specs=(four, four, grad, grad, grad, grad, P("section", None, "dp"), P("section", None, "dp"),
                   P("section", "dp"), P("section", "dp")),
        check_vma=False,
    )
```

```python
from functools import partial

import jax
import jax.numpy as jnp
from jax import lax
from jax.experimental import pallas as pl
from jax.experimental.pallas import tpu as pltpu
from jax.sharding import PartitionSpec as P

HEADS = 12
PATCH = 196
D = 768
FF = 3072
EPS = 1e-06
NV = 144
NM = 128
FIRST = PATCH - NM
GROUP = 2
CHUNK = 32

BF = jnp.bfloat16
F32 = jnp.float32
MIB = 1024 * 1024

HBM = pl.BlockSpec(memory_space=pl.ANY)
VMEM = pl.BlockSpec(memory_space=pltpu.VMEM)
SMEM = pl.BlockSpec(memory_space=pltpu.SMEM)


def nn(a, b):
    return jnp.dot(a, b, preferred_element_type=F32)


def nt(a, b):
    return lax.dot_general(a, b, (((1,), (1,)), ((), ())), preferred_element_type=F32)


def tn(a, b):
    return lax.dot_general(a, b, (((0,), (0,)), ((), ())), preferred_element_type=F32)


def loop(count, body, unroll=1):
    def step(i, carry):
        for u in range(unroll):
            body(i * unroll + u)
        return carry

    if count == unroll:
        step(0, 0)
    else:
        lax.fori_loop(0, count // unroll, step, 0)


def unroll_of(count):
    return next(u for u in (4, 3, 2, 1) if count % u == 0)


def rows_of(i, size):
    return pl.ds(pl.multiple_of(i * size, size), size)


def f32_row(ref, row, col=0, width=D):
    return ref[pl.ds(row, 1), pl.ds(col, width)].astype(F32)


class Copies:
    def __init__(self, sems):
        self.sems = sems
        self.used = 0
        self.open = []

    def start(self, src, dst):
        copy = pltpu.make_async_copy(src, dst, self.sems.at[self.used])
        self.used += 1
        copy.start()
        self.open.append(copy)
        return copy

    def wait(self, *copies):
        for copy in copies:
            copy.wait()
            self.open.remove(copy)

    def finish(self):
        self.wait(*list(self.open))


def gelu_pair(u):
    size = jnp.abs(u)
    base = 1.0 + (0.3275911 * 0.7071067811865476) * size
    guess = pl.reciprocal(base, approx=True)
    t = guess * (2.0 - base * guess)
    ex = jnp.exp(-0.5 * (u * u))
    poly = 0.5306027145 * t - 0.7265760135
    poly = poly * t + 0.7107068705
    poly = poly * t - 0.142248368
    poly = poly * t + 0.127414796
    tail = poly * t * ex
    phi = jnp.where(u >= 0.0, 1.0 - tail, tail)
    return u * phi, phi + u * (0.3989422804014327 * ex)


def norm_rows(src, dst, rows, gain, shift):
    def body(i):
        sel = rows_of(i, CHUNK)
        x = src[sel, :].astype(F32)
        centered = x - jnp.mean(x, axis=-1, keepdims=True)
        var = jnp.mean(centered * centered, axis=-1, keepdims=True)
        dst[sel, :] = (centered * lax.rsqrt(var + EPS) * gain + shift).astype(BF)

    loop(rows // CHUNK, body, unroll_of(rows // CHUNK))


def norm_back(src, grad, base, write, rows, gain):
    count = rows // CHUNK
    unroll = 3 if count % 3 == 0 else 2

    def step(i, carry):
        for u in range(unroll):
            carry = one(i * unroll + u, carry)
        return carry

    def one(i, carry):
        d_gain, d_shift = carry
        sel = rows_of(i, CHUNK)
        x = src[sel, :].astype(F32)
        dh = grad[sel, :]
        centered = x - jnp.mean(x, axis=-1, keepdims=True)
        var = jnp.mean(centered * centered, axis=-1, keepdims=True)
        rstd = lax.rsqrt(var + EPS)
        hat = centered * rstd
        g = dh * gain
        part = dh * hat
        dx = rstd * (
            g
            - jnp.mean(g, axis=-1, keepdims=True)
            - hat * jnp.mean(g * hat, axis=-1, keepdims=True)
        )
        if base is not None:
            dx = dx + base[sel, :].astype(F32)
        write(sel, dx)
        d_gain = d_gain + jnp.sum(part.reshape(CHUNK // 8, 8, D), axis=0)
        d_shift = d_shift + jnp.sum(dh.reshape(CHUNK // 8, 8, D), axis=0)
        return d_gain, d_shift

    zero = jnp.zeros((8, D), F32)
    d_gain, d_shift = lax.fori_loop(0, count // unroll, step, (zero, zero))
    return jnp.sum(d_gain, axis=0, keepdims=True), jnp.sum(d_shift, axis=0, keepdims=True)


def column_sum(ref, rows, col=0, width=D):
    def step(i, carry):
        x = ref[rows_of(i, CHUNK), pl.ds(col, width)].astype(F32)
        return carry + jnp.sum(x.reshape(CHUNK // 8, 8, width), axis=0)

    total = lax.fori_loop(0, rows // CHUNK, step, jnp.zeros((8, width), F32))
    return jnp.sum(total, axis=0, keepdims=True)


def as_bf16(flags):
    return jnp.where(flags, 1.0, 0.0).astype(BF)


def place_matrix(order, image, start, count, low, high):
    row = order[pl.ds(image, 1), pl.ds(start, count)]
    rank = start + lax.broadcasted_iota(jnp.int32, (1, count), 1)
    row = jnp.where((rank >= low) & (rank < high), row, -1)
    return as_bf16(row == lax.broadcasted_iota(jnp.int32, (PATCH, count), 0))


def split_pair(pair):
    lane = lax.broadcasted_iota(jnp.int32, pair.shape, 1)
    zero = jnp.zeros_like(pair)
    return jnp.concatenate([jnp.where(lane < 64, pair, zero), jnp.where(lane < 64, zero, pair)], axis=0)


def join_rows(both):
    rows = both.shape[0] // 2
    lane = lax.broadcasted_iota(jnp.int32, (rows, 128), 1)
    return jnp.where(lane < 64, both[:rows], both[rows:])


def join_columns(both):
    rows = both.shape[1] // 2
    return jnp.concatenate([both[:64, :rows], both[64:, rows:]], axis=0).T


PAIRS = HEADS // 2
STEP = 3


def each_pair_group(images, body):
    def group(i):
        image = i // (PAIRS // STEP)
        first = (i % (PAIRS // STEP)) * STEP
        pairs = [first + step for step in range(STEP)]
        body(image, [image * PAIRS + pair for pair in pairs], [pl.ds(pl.multiple_of(pair * 128, 128), 128) for pair in pairs])

    loop(images * (PAIRS // STEP), group)


def softmax(scores, axis):
    ex = jnp.exp(scores - jnp.max(scores, axis=axis, keepdims=True))
    return (ex * (1.0 / jnp.sum(ex, axis=axis, keepdims=True))).astype(BF)


def score_back(probs, d_probs, axis):
    wide = probs.astype(F32)
    return (wide * (d_probs - jnp.sum(d_probs * wide, axis=axis, keepdims=True))).astype(BF)


def attention_by_rows(images, n, q, k, v, p, o, count_of):
    def body(image, slots, lanes):
        sel = rows_of(image, n)
        ok = lax.broadcasted_iota(jnp.int32, (1, n), 1) < count_of(image)
        scores = [nt(split_pair(q[sel, at]), k[sel, at]) for at in lanes]
        probs = [softmax(jnp.where(ok, one, -1000000000.0), 1) for one in scores]
        for slot, one in zip(slots, probs):
            p[slot] = one
        mixed = [nn(one, v[sel, at]) for one, at in zip(probs, lanes)]
        for at, one in zip(lanes, mixed):
            o[sel, at] = join_rows(one).astype(BF)

    each_pair_group(images, body)


def attention_by_columns(images, nk, q, k, v, p, o, key_ok):
    def body(image, slots, lanes):
        qs, ks = rows_of(image, NM), rows_of(image, nk)
        ok = key_ok(image)
        scores = [nt(k[ks, at], split_pair(q[qs, at])) for at in lanes]
        probs = [softmax(jnp.where(ok, one, -1000000000.0), 0) for one in scores]
        if p is not None:
            for slot, one in zip(slots, probs):
                p[slot] = one
        mixed = [tn(v[ks, at], one) for one, at in zip(probs, lanes)]
        for at, one in zip(lanes, mixed):
            o[qs, at] = join_columns(one).astype(BF)

    each_pair_group(images, body)


def attention_back_rows(images, n, q, k, v, p, do, dq, dkv):
    def body(image, slots, lanes):
        sel = rows_of(image, n)
        d_mixed = [split_pair(do[sel, at]) for at in lanes]
        d_probs = [nt(one, v[sel, at]) for one, at in zip(d_mixed, lanes)]
        d_scores = [score_back(p[slot], one, 1) for slot, one in zip(slots, d_probs)]
        d_values = [tn(p[slot], one) for slot, one in zip(slots, d_mixed)]
        d_query = [nn(one, k[sel, at]) for one, at in zip(d_scores, lanes)]
        d_keys = [tn(one, split_pair(q[sel, at])) for one, at in zip(d_scores, lanes)]
        for at, value, query, key in zip(lanes, d_values, d_query, d_keys):
            dq[sel, at] = (join_rows(query) * 0.125).astype(BF)
            dkv[sel, at] = key.astype(BF)
            dkv[sel, pl.ds(pl.multiple_of(D + at.start, 128), 128)] = value.astype(BF)

    each_pair_group(images, body)


def attention_back_columns(images, nk, q, k, v, p, do, dq, dkv):
    def body(image, slots, lanes):
        qs, ks = rows_of(image, NM), rows_of(image, nk)
        d_mixed = [split_pair(do[qs, at]) for at in lanes]
        d_probs = [nt(v[ks, at], one) for one, at in zip(d_mixed, lanes)]
        d_scores = [score_back(p[slot], one, 0) for slot, one in zip(slots, d_probs)]
        d_values = [nn(p[slot], one) for slot, one in zip(slots, d_mixed)]
        d_query = [tn(k[ks, at], one) for one, at in zip(d_scores, lanes)]
        d_keys = [nn(one, split_pair(q[qs, at])) for one, at in zip(d_scores, lanes)]
        for at, value, query, key in zip(lanes, d_values, d_query, d_keys):
            dq[qs, at] = (join_columns(query) * 0.125).astype(BF)
            dkv[ks, at] = key.astype(BF)
            dkv[ks, pl.ds(pl.multiple_of(D + at.start, 128), 128)] = value.astype(BF)

    each_pair_group(images, body)


TILE = 1024


def mlp_forward(rows, h2, w1, w2, up_b, u, a, gp, base):
    def multiply(j):
        u[j % 2] = nn(h2[...], w1[:, j * TILE : (j + 1) * TILE])

    multiply(0)
    for j in range(FF // TILE):
        if j + 1 < FF // TILE:
            multiply(j + 1)
        for c in range(0, TILE, 256):
            cols = slice(j * TILE + c, j * TILE + c + 256)
            shift = up_b[0:1, cols].astype(F32)
            for r in range(0, rows, CHUNK):
                value, slope = gelu_pair(u[j % 2, r : r + CHUNK, c : c + 256] + shift)
                a[r : r + CHUNK, cols] = value.astype(BF)
                if gp is not None:
                    gp[r : r + CHUNK, cols] = slope.astype(BF)
    return nn(a[...], w2[...]) + base()


def mlp_back(rows, dyb, gp, w1, w2, du, u, acc):
    for j in range(FF // TILE):
        cols = slice(j * TILE, (j + 1) * TILE)
        u[j % 2] = nt(dyb[...], w2[cols, :])
        for c in range(0, TILE, 256):
            at = slice(j * TILE + c, j * TILE + c + 256)
            for r in range(0, rows, CHUNK):
                sel = slice(r, r + CHUNK)
                du[sel, at] = (gp[sel, at].astype(F32) * u[j % 2, sel, c : c + 256]).astype(BF)
    acc[...] = nt(du[...], w1[...])


def cost(flops, nbytes):
    return pl.CostEstimate(flops=int(flops), bytes_accessed=int(nbytes), transcendentals=0)


def params(mib):
    return pltpu.CompilerParams(vmem_limit_bytes=mib * MIB)


def struct(shape, dtype=BF):
    return jax.ShapeDtypeStruct(shape, dtype)


def start_weights(copies, sources, scratch):
    return [copies.start(src, dst) for src, dst in zip(sources, scratch)]


def encode_kernel(group, ids, visible, order, gains, biases, qvb, upb, rows, wqkv, wo, w1, w2,
                  lat_out, x_out, hq_out, q_out, k_out, v_out, p_out, o_out, y1_out, h2_out, gp_out, a_out,
                  rows_v, sqkv, so, s1, s2, x, hq, q, k, v, p, o, y1, h2, gp, a, u, lat, sems):
    n = GROUP * NV

    @pl.when(ids[0] == 0)
    def _():
        copies = Copies(sems)
        got_rows = copies.start(rows.at[0, pl.ds(group * GROUP, GROUP)], rows_v)
        got_qkv, got_o, got_1, got_2 = start_weights(
            copies, (wqkv.at[0], wo.at[0], w1.at[0], w2.at[0]), (sqkv, so, s1, s2)
        )
        gain, bias = gains.at[0], biases.at[0]
        copies.wait(got_rows)
        for i in range(GROUP):
            image = group * GROUP + i
            pick = place_matrix(order, image, 0, NV, 0, visible[image])
            x[pl.ds(i * NV, NV), :] = tn(pick, rows_v[i]).astype(BF)
        copies.start(x, x_out)
        norm_rows(x, hq, n, f32_row(gain, 0), f32_row(bias, 0))
        copies.start(hq, hq_out)
        copies.wait(got_qkv)
        united = nn(hq[...], sqkv[...])
        q[...] = ((united[:, 0:D] + f32_row(qvb, 0)).astype(BF) * 0.125).astype(BF)
        k[...] = united[:, D : 2 * D].astype(BF)
        v[...] = (united[:, 2 * D :] + f32_row(qvb, 0, D)).astype(BF)
        copies.start(q, q_out)
        copies.start(k, k_out)
        copies.start(v, v_out)

        attention_by_rows(GROUP, NV, q, k, v, p, o, lambda i: visible[group * GROUP + i])
        copies.start(p, p_out)
        copies.start(o, o_out)
        copies.wait(got_o)
        y1[...] = nn(o[...], so[...]) + f32_row(bias, 1) + x[...].astype(F32)
        copies.start(y1, y1_out)
        norm_rows(y1, h2, n, f32_row(gain, 1), f32_row(bias, 2))
        copies.start(h2, h2_out)
        copies.wait(got_1, got_2)
        lat[...] = mlp_forward(n, h2, s1, s2, upb, u, a, gp, lambda: y1[...] + f32_row(bias, 3)).astype(BF)
        copies.start(gp, gp_out)
        copies.start(a, a_out)
        copies.start(lat, lat_out)
        copies.finish()


def encode(group, ids, visible, order, gains, biases, qvb, upb, rows, weights):
    n = GROUP * NV
    row, wide = struct((n, D)), struct((n, FF))
    heads = struct((GROUP * PAIRS, 2 * NV, NV))
    outs = [row] * 6 + [heads, row, struct((n, D), F32), row, wide, wide]
    vm = lambda s: pltpu.VMEM(s.shape, s.dtype)
    scratch = [
        pltpu.VMEM((GROUP, PATCH, D), BF),
        pltpu.VMEM((D, 3 * D), BF), pltpu.VMEM((D, D), BF), pltpu.VMEM((D, FF), BF), pltpu.VMEM((FF, D), BF),
        vm(row), vm(row), vm(row), vm(row), vm(row), vm(heads), vm(row), pltpu.VMEM((n, D), F32), vm(row),
        vm(wide), vm(wide), pltpu.VMEM((2, n, TILE), F32), vm(row),
        pltpu.SemaphoreType.DMA((20,)),
    ]
    return pl.pallas_call(
        partial(encode_kernel, group),
        in_specs=[SMEM, SMEM] + [VMEM] * 5 + [HBM] * 5,
        out_specs=[HBM] * len(outs),
        out_shape=outs,
        scratch_shapes=scratch,
        compiler_params=params(56),
        cost_estimate=cost(2 * n * 12 * D * D, 25e6),
        name="encode",
    )(ids, visible, order, gains, biases, qvb, upb, rows, *weights)


def middle_kernel(group, ids, visible, order, gains, biases, qvb, upb, tgains, tbiases, tqvb, tupb,
                  rows, cot, lat_in, wqkv, wo, w1, w2, tqkv, to, t1, t2,
                  dlat_out, res_out, hq_out, hk_out, dq_out, dkv_out, o_out, dy1b_out, h2_out, du_out, a_out,
                  dyb_out, dx_out, sums_out, cot_out,
                  rows_v, cot_v, sqkv, so, s1, s2, x, lat, hq, hk, q, k, v, p, o, y1, h2, gp, a, u, acc,
                  res, dyb, du, dy1, dy1b, do, dq, dkv, dh, dlat, sums, sems):
    n, m = GROUP * NM, GROUP * NV

    def shared(copies, sources, gain, bias, qv, ub, target):
        got_rows = copies.start(rows.at[0, pl.ds(group * GROUP, GROUP)], rows_v)
        got_qkv = copies.start(sources[0], sqkv)
        if not target:
            got_lat = copies.start(lat_in, lat)
        got_o, got_1, got_2 = start_weights(copies, sources[1:], (so, s1, s2))
        got_cot = copies.start(cot.at[0, pl.ds(group * GROUP, GROUP)], cot_v)
        copies.wait(got_rows)
        for i in range(GROUP):
            image = group * GROUP + i
            pick = place_matrix(order, image, FIRST, NM, visible[image], PATCH)
            x[pl.ds(i * NM, NM), :] = tn(pick, rows_v[i]).astype(BF)
        norm_rows(x, hq, n, f32_row(gain, 0), f32_row(bias, 0))
        copies.wait(got_qkv)
        q[...] = ((nn(hq[...], sqkv[:, 0:D]) + f32_row(qv, 0)).astype(BF) * 0.125).astype(BF)
        if target:
            united = nn(hq[...], sqkv[:, D:])
            k[pl.ds(0, n), :] = united[:, :D].astype(BF)
            v[pl.ds(0, n), :] = (united[:, D:] + f32_row(qv, 0, D)).astype(BF)
        else:
            copies.start(hq, hq_out)
            copies.wait(got_lat)
            norm_rows(lat, hk, m, f32_row(gain, 0), f32_row(bias, 0))
            copies.start(hk, hk_out)
            united = nn(hk[...], sqkv[:, D:])
            k[...] = united[:, :D].astype(BF)
            v[...] = (united[:, D:] + f32_row(qv, 0, D)).astype(BF)
        nk = NM if target else NV

        def key_ok(i):
            place = lax.broadcasted_iota(jnp.int32, (nk, 1), 0)
            count = visible[group * GROUP + i]
            return place + FIRST >= count if target else place < count

        attention_by_columns(GROUP, nk, q, k, v, None if target else p, o, key_ok)
        copies.wait(got_o)
        y1[...] = nn(o[...], so[...]) + f32_row(bias, 1) + x[...].astype(F32)
        norm_rows(y1, h2, n, f32_row(gain, 1), f32_row(bias, 2))
        copies.wait(got_1, got_2)
        keep_slope = None if target else gp
        res[...] = mlp_forward(n, h2, s1, s2, ub, u, a, keep_slope, lambda: y1[...] + f32_row(bias, 3)).astype(BF)
        copies.start(res, res_out)
        return got_cot

    @pl.when(ids[0] == 0)
    def _():
        copies = Copies(sems)
        copies.wait(shared(copies, (tqkv, to, t1, t2), tgains, tbiases, tqvb, tupb, True))
        for i in range(GROUP):
            image = group * GROUP + i
            pick = place_matrix(order, image, 0, NV, 0, visible[image])
            lat[pl.ds(i * NV, NV), :] = tn(pick, cot_v[i]).astype(BF)
        copies.start(lat, cot_out)
        copies.finish()

    @pl.when(ids[0] == 1)
    def _():
        copies = Copies(sems)
        gain = gains.at[0]
        got_cot = shared(
            copies, (wqkv.at[0], wo.at[0], w1.at[0], w2.at[0]), gain, biases.at[0], qvb, upb.at[0:1], False
        )
        copies.start(o, o_out)
        copies.start(h2, h2_out)
        copies.start(a, a_out)
        copies.wait(got_cot)
        for i in range(GROUP):
            image = group * GROUP + i
            pick = place_matrix(order, image, FIRST, NM, visible[image], PATCH)
            dyb[pl.ds(i * NM, NM), :] = tn(pick, cot_v[i]).astype(BF)
        copies.start(dyb, dyb_out)
        mlp_back(n, dyb, gp, s1, s2, du, u, acc)
        copies.start(du, du_out)

        def keep(sel, dx):
            dy1[sel, :] = dx
            dy1b[sel, :] = dx.astype(BF)

        g2, b2 = norm_back(y1, acc, dyb, keep, n, f32_row(gain, 1))
        copies.start(dy1b, dy1b_out)
        do[...] = nt(dy1b[...], so[...]).astype(BF)
        attention_back_columns(GROUP, NV, q, k, v, p, do, dq, dkv)
        copies.start(dq, dq_out)
        copies.start(dkv, dkv_out)
        dh[...] = nt(dkv[...], sqkv[:, D:])

        def keep_side(sel, dx):
            dlat[sel, :] = dx.astype(BF)

        gk, bk = norm_back(lat, dh, None, keep_side, m, f32_row(gain, 0))
        copies.start(dlat, dlat_out)
        acc[...] = nt(dq[...], sqkv[:, 0:D])

        def keep_input(sel, dx):
            dy1[sel, :] = dx

        gq, bq = norm_back(x, acc, dy1, keep_input, n, f32_row(gain, 0))
        copies.start(dy1, dx_out)
        for row, value in enumerate((gq + gk, g2, bq + bk, b2)):
            sums[pl.ds(row, 1), :] = value
        copies.start(sums, sums_out)
        copies.finish()


def middle(group, ids, visible, order, own_vecs, target_vecs, rows, cot, lat, weights, targets):
    n, m = GROUP * NM, GROUP * NV
    row, side, wide = struct((n, D)), struct((m, D)), struct((n, FF))
    pair = struct((m, 2 * D))
    outs = [side, row, row, side, row, pair, row, row, row, wide, wide, row, struct((n, D), F32), struct((8, D), F32), side]
    vm = lambda s: pltpu.VMEM(s.shape, s.dtype)
    full, fside = pltpu.VMEM((n, D), F32), pltpu.VMEM((m, D), F32)
    scratch = [
        pltpu.VMEM((GROUP, PATCH, D), BF), pltpu.VMEM((GROUP, PATCH, D), BF),
        pltpu.VMEM((D, 3 * D), BF), pltpu.VMEM((D, D), BF), pltpu.VMEM((D, FF), BF), pltpu.VMEM((FF, D), BF),
        vm(row), vm(side), vm(row), vm(side), vm(row), vm(side), vm(side),
        pltpu.VMEM((GROUP * PAIRS, NV, 2 * NM), BF), vm(row), full, vm(row), vm(wide), vm(wide),
        pltpu.VMEM((2, n, TILE), F32), full,
        vm(row), vm(row), vm(wide), full, vm(row), vm(row), vm(row), vm(pair), fside, vm(side),
        pltpu.VMEM((8, D), F32),
        pltpu.SemaphoreType.DMA((24,)),
    ]
    return pl.pallas_call(
        partial(middle_kernel, group),
        in_specs=[SMEM, SMEM] + [VMEM] * 9 + [HBM] * 11,
        out_specs=[HBM] * len(outs),
        out_shape=outs,
        scratch_shapes=scratch,
        compiler_params=params(56),
        cost_estimate=cost(4 * n * 12 * D * D, 25e6),
        name="middle",
    )(ids, visible, order, *own_vecs, *target_vecs, rows, cot, lat, *weights, *targets)


def stack_rows(copies, pieces, ref, size):
    return [copies.start(piece, ref.at[pl.ds(i * size, size)]) for i, piece in enumerate(pieces)]


def clear_tail(ref, used):
    ref[pl.ds(used, ref.shape[0] - used), :] = jnp.zeros((ref.shape[0] - used, ref.shape[1]), ref.dtype)


def halves(count, blocks, rows):
    if count == 16:
        return [struct((2, 2, 2, blocks, rows // 16, D))] * 2
    return [struct((blocks, rows, D))]


def give_block(copies, core, value, out, dest, j):
    out[j] = value
    if len(dest) == 1:
        copies.start(out.at[j], dest[0].at[j])
        return
    view = out.at[j].reshape(2, 2, 2, 2, D // 16, D)
    for x in range(2):
        for low in range(2):
            copies.start(view.at[:, low, x, core], dest[0].at[x, low, :, j])
            copies.start(view.at[:, low, x, 1 - core], dest[1].at[x, low, :, j])


def give_rows(copies, core, value, out, dest, j):
    out[j] = value
    if len(dest) == 1:
        copies.start(out.at[j], dest[0].at[0, pl.ds(j * D, D)])
        return
    view = out.at[j].reshape(2, 2, D // 4, D)
    for x in range(2):
        copies.start(view.at[x, core], dest[0].at[x, j % 2, j // 2, 0])
        copies.start(view.at[x, 1 - core], dest[1].at[x, j % 2, j // 2, 0])


def down_kernel(groups, parts, ids, *refs):
    cot, lat, a_enc, a_reg, dyb_reg = (refs[i * groups : (i + 1) * groups] for i in range(5))
    refs = refs[5 * groups :]
    dest, refs = refs[:parts], refs[parts:]
    dyb_out, sums_out, cot_v, dyb, a, dlat, out, sums, sems = refs
    images = groups * GROUP
    nv, nm = GROUP * NV, GROUP * NM

    @pl.when(ids[0] == 0)
    def _():
        copies = Copies(sems)
        got = stack_rows(copies, cot, cot_v, nv) + stack_rows(copies, lat, dlat, nv)
        stack_rows(copies, a_enc, a, nv)
        copies.wait(*got)
        dyb[...] = (cot_v[...].astype(F32) + dlat[...].astype(F32)).astype(BF)
        copies.start(dyb, dyb_out)
        copies.finish()

    @pl.when(ids[0] == 1)
    def _():
        copies = Copies(sems)
        stack_rows(copies, a_reg, a, nm)
        stack_rows(copies, dyb_reg, dyb, nm)
        clear_tail(a, images * NM)
        clear_tail(dyb, images * NM)
        copies.finish()

    copies = Copies(sems)
    for j in range(4):
        give_rows(copies, ids[1], tn(a[:, j * D : (j + 1) * D], dyb[...]).astype(BF), out, dest, j)
    sums[...] = jnp.broadcast_to(column_sum(dyb, images * NV), (8, D))
    copies.start(sums, sums_out)
    copies.finish()


def down_grad(groups, count, ids, cot, dlat, a_enc, a_reg, dyb_reg):
    n = groups * GROUP * NV
    main = [struct((2, 2, 2, 1, D // 4, D))] * 2 if count == 16 else [struct((1, FF, D))]
    outs = main + [struct((n, D)), struct((8, D), F32)]
    row = pltpu.VMEM((n, D), BF)
    scratch = [
        row, row, pltpu.VMEM((n, FF), BF), row, pltpu.VMEM((4, D, D), BF), pltpu.VMEM((8, D), F32),
        pltpu.SemaphoreType.DMA((24,)),
    ]
    got = pl.pallas_call(
        partial(down_kernel, groups, len(main)),
        in_specs=[SMEM] + [HBM] * (5 * groups),
        out_specs=[HBM] * len(outs),
        out_shape=outs,
        scratch_shapes=scratch,
        compiler_params=params(56),
        cost_estimate=cost(2 * n * 4 * D * D, 15e6),
        name="down_grad",
    )(ids, *cot, *dlat, *a_enc, *a_reg, *dyb_reg)
    return got[: len(main)], got[-2], got[-1]


def up_kernel(groups, parts, ids, gains, dyb_in, w1, w2, *refs):
    y1_enc, gp_enc, h2_enc, du_reg, h2_reg = (refs[i * groups : (i + 1) * groups] for i in range(5))
    refs = refs[5 * groups :]
    dest, refs = refs[:parts], refs[parts:]
    dy1_out, sums_out, s1, s2, dyb, gp, y1, h2, du, u, acc, dy1, out, sums, sems = refs
    images = groups * GROUP
    nv, nm = GROUP * NV, GROUP * NM

    @pl.when(ids[0] == 0)
    def _():
        copies = Copies(sems)
        got = [copies.start(dyb_in, dyb), copies.start(w2.at[0], s2)]
        got += stack_rows(copies, gp_enc, gp, nv)
        got.append(copies.start(w1.at[0], s1))
        got_y = stack_rows(copies, y1_enc, y1, nv)
        stack_rows(copies, h2_enc, h2, nv)
        copies.wait(*got)
        mlp_back(images * NV, dyb, gp, s1, s2, du, u, acc)
        copies.wait(*got_y)

        def keep(sel, dx):
            dy1[sel, :] = dx

        g2, b2 = norm_back(y1, acc, dyb, keep, images * NV, f32_row(gains.at[0], 1))
        copies.start(dy1, dy1_out)
        sums[pl.ds(0, 1), :] = g2
        sums[pl.ds(1, 1), :] = b2
        copies.finish()

    @pl.when(ids[0] == 1)
    def _():
        copies = Copies(sems)
        stack_rows(copies, du_reg, du, nm)
        stack_rows(copies, h2_reg, h2, nm)
        clear_tail(du, images * NM)
        clear_tail(h2, images * NM)
        sums[pl.ds(0, 2), :] = jnp.zeros((2, D), F32)
        copies.finish()

    copies = Copies(sems)
    for j in range(4):
        value = tn(h2[...], du[:, j * D : (j + 1) * D]).astype(BF)
        give_block(copies, ids[1], value, out, dest, j)
        sums[pl.ds(4 + j, 1), :] = column_sum(du, images * NV, j * D)
    copies.start(sums, sums_out)
    copies.finish()


def up_grad(groups, count, ids, gains, dyb, w1, w2, y1_enc, gp_enc, h2_enc, du_reg, h2_reg):
    n = groups * GROUP * NV
    main = halves(count, 4, D)
    outs = main + [struct((n, D), F32), struct((8, D), F32)]
    scratch = [
        pltpu.VMEM((D, FF), BF), pltpu.VMEM((FF, D), BF), pltpu.VMEM((n, D), BF), pltpu.VMEM((n, FF), BF),
        pltpu.VMEM((n, D), F32), pltpu.VMEM((n, D), BF), pltpu.VMEM((n, FF), BF), pltpu.VMEM((2, n, TILE), F32),
        pltpu.VMEM((n, D), F32), pltpu.VMEM((n, D), F32), pltpu.VMEM((4, D, D), BF), pltpu.VMEM((8, D), F32),
        pltpu.SemaphoreType.DMA((36,)),
    ]
    got = pl.pallas_call(
        partial(up_kernel, groups, len(main)),
        in_specs=[SMEM, VMEM] + [HBM] * (3 + 5 * groups),
        out_specs=[HBM] * len(outs),
        out_shape=outs,
        scratch_shapes=scratch,
        compiler_params=params(56),
        cost_estimate=cost(6 * n * 4 * D * D, 25e6),
        name="up_grad",
    )(ids, gains, dyb, w1, w2, *y1_enc, *gp_enc, *h2_enc, *du_reg, *h2_reg)
    return got[: len(main)], got[-2], got[-1]


def attn_kernel(groups, parts, ids, dy1_in, wqkv, wo, *refs):
    pieces = [refs[i * groups : (i + 1) * groups] for i in range(12)]
    q_enc, k_enc, v_enc, p_enc, o_enc, hq_enc = pieces[:6]
    hq_reg, hk_reg, dq_reg, dkv_reg, o_reg, dy1b_reg = pieces[6:]
    refs = refs[12 * groups :]
    dest, refs = refs[:parts], refs[parts:]
    (dh_out, sums_out, sqkv, so, dy1, dy1b, q, k, v, p, o, hq, hk, do, dq, dkv, dh, out, sums, sems) = refs
    images = groups * GROUP
    nv, nm = GROUP * NV, GROUP * NM

    @pl.when(ids[0] == 0)
    def _():
        copies = Copies(sems)
        got = [copies.start(dy1_in, dy1), copies.start(wo.at[0], so)]
        for piece, ref in ((v_enc, v), (k_enc, k), (q_enc, q)):
            got += stack_rows(copies, piece, ref, nv)
        got += stack_rows(copies, p_enc, p, GROUP * PAIRS)
        stack_rows(copies, o_enc, o, nv)
        stack_rows(copies, hq_enc, hq, nv)
        stack_rows(copies, hq_enc, hk, nv)
        copies.start(wqkv.at[0], sqkv)
        copies.wait(*got[:2])
        dy1b[...] = dy1[...].astype(BF)
        do[...] = nt(dy1b[...], so[...]).astype(BF)
        copies.wait(*got[2:])
        attention_back_rows(images, NV, q, k, v, p, do, dq, dkv)
        copies.finish()

    @pl.when(ids[0] == 1)
    def _():
        copies = Copies(sems)
        for piece, ref in ((hq_reg, hq), (dq_reg, dq), (o_reg, o), (dy1b_reg, dy1b)):
            stack_rows(copies, piece, ref, nm)
            clear_tail(ref, images * NM)
        for piece, ref in ((hk_reg, hk), (dkv_reg, dkv)):
            stack_rows(copies, piece, ref, nv)
        copies.finish()

    copies = Copies(sems)
    for j, (left, right) in enumerate(((hk, dkv.at[:, pl.ds(0, D)]), (hk, dkv.at[:, pl.ds(D, D)]), (hq, dq), (o, dy1b))):
        give_block(copies, ids[1], tn(left[...], right[...]).astype(BF), out, dest, j)
    for row, value in enumerate((
        column_sum(dy1b, images * NV), column_sum(dq, images * NV), column_sum(dkv, images * NV, D)
    )):
        sums[pl.ds(row, 1), :] = value
    copies.start(sums, sums_out)

    @pl.when(ids[0] == 0)
    def _():
        late = Copies(sems.at[pl.ds(40, 1)])
        dh[...] = nt(dq[...], sqkv[:, 0:D]) + nt(dkv[...], sqkv[:, D:])
        late.start(dh, dh_out)
        late.finish()

    copies.finish()


def attn_grad(groups, count, ids, dy1, wqkv, wo, *pieces):
    n = groups * GROUP * NV
    row = pltpu.VMEM((n, D), BF)
    main = halves(count, 4, D)
    outs = main + [struct((n, D), F32), struct((8, D), F32)]
    scratch = [
        pltpu.VMEM((D, 3 * D), BF), pltpu.VMEM((D, D), BF), pltpu.VMEM((n, D), F32), row, row, row, row,
        pltpu.VMEM((groups * GROUP * PAIRS, 2 * NV, NV), BF), row, row, row, row, row, pltpu.VMEM((n, 2 * D), BF),
        pltpu.VMEM((n, D), F32), pltpu.VMEM((4, D, D), BF), pltpu.VMEM((8, D), F32), pltpu.SemaphoreType.DMA((44,)),
    ]
    got = pl.pallas_call(
        partial(attn_kernel, groups, len(main)),
        in_specs=[SMEM] + [HBM] * (3 + 12 * groups),
        out_specs=[HBM] * len(outs),
        out_shape=outs,
        scratch_shapes=scratch,
        compiler_params=params(56),
        cost_estimate=cost(6 * n * 4 * D * D, 25e6),
        name="attn_grad",
    )(ids, dy1, wqkv, wo, *[ref for piece in pieces for ref in piece])
    return got[: len(main)], got[-2], got[-1]


def place_kernel(groups, ids, visible, order, gains, down_sums, up_sums, attn_sums, *refs):
    sums_reg, (dh_in, dy1_in), refs = refs[:groups], refs[groups : groups + 2], refs[groups + 2 :]
    x_enc, lat_enc, res, dx_reg = (refs[i * groups : (i + 1) * groups] for i in range(4))
    block_out, grad_out, small, x, dh, dy1, lat, out, sems = refs[4 * groups :]
    images = groups * GROUP
    nv, nm = GROUP * NV, GROUP * NM

    def put_grad(i, put, value):
        high = value.astype(BF)
        low = (value - high.astype(F32)).astype(BF)
        grad_out[0, i] = nn(put, high) + nn(put, low)

    def set_norms(g1, g2, b1, b2):
        for row, value in ((0, g1), (1, g2), (2, b1), (4, b2)):
            small[pl.ds(row, 1), :] = value

    small[pl.ds(3, 1), :] = attn_sums[0:1, :]
    small[pl.ds(5, 1), :] = down_sums[0:1, :]
    small[pl.ds(6, 2), :] = attn_sums[1:3, :]
    small[pl.ds(8, 4), :] = up_sums[4:8, :]
    small[pl.ds(12, 4), :] = jnp.zeros((4, D), F32)

    @pl.when(ids[0] == 0)
    def _():
        copies = Copies(sems)
        got = [copies.start(dh_in, dh), copies.start(dy1_in, dy1)] + stack_rows(copies, x_enc, x, nv)
        got_out = stack_rows(copies, lat_enc, lat, nv) + stack_rows(copies, res, out, nm)
        copies.wait(*got)

        def keep(sel, dx):
            dy1[sel, :] = dx

        g1, b1 = norm_back(x, dh, dy1, keep, images * NV, f32_row(gains.at[0], 0))
        set_norms(g1, up_sums[0:1, :], b1, up_sums[1:2, :])
        copies.wait(*got_out)
        for i in range(images):
            put = place_matrix(order, i, 0, NV, 0, visible[i])
            put_side = place_matrix(order, i, FIRST, NM, visible[i], PATCH)
            put_grad(i, put, dy1[pl.ds(i * NV, NV), :])
            block_out[0, i] = (nn(put, lat[pl.ds(i * NV, NV), :]) + nn(put_side, out[pl.ds(i * NM, NM), :])).astype(BF)

    @pl.when(ids[0] == 1)
    def _():
        copies = Copies(sems)
        stack_rows(copies, res, out, nm)
        stack_rows(copies, dx_reg, dy1, nm)
        copies.finish()
        total = sums_reg[0][...]
        for more in sums_reg[1:]:
            total = total + more[...]
        set_norms(total[0:1], total[1:2], total[2:3], total[3:4])
        for i in range(images):
            put = place_matrix(order, i, FIRST, NM, visible[i], PATCH)
            put_grad(i, put, dy1[pl.ds(i * NM, NM), :])
            block_out[0, i] = nn(put, out[pl.ds(i * NM, NM), :]).astype(BF)


def place(groups, ids, visible, order, gains, sums, sums_reg, dh, dy1, x_enc, lat_enc, res, dx_reg):
    images = groups * GROUP
    n = images * NV
    outs = [struct((1, images, PATCH, D)), struct((1, images, PATCH, D), F32), struct((16, D), F32)]
    scratch = [
        pltpu.VMEM((n, D), BF), pltpu.VMEM((n, D), F32), pltpu.VMEM((n, D), F32), pltpu.VMEM((n, D), BF),
        pltpu.VMEM((images * NM, D), BF), pltpu.SemaphoreType.DMA((12,)),
    ]
    return pl.pallas_call(
        partial(place_kernel, groups),
        in_specs=[SMEM, SMEM, VMEM, VMEM] + [VMEM] * (3 + groups) + [HBM] * (2 + 4 * groups),
        out_specs=[VMEM] * len(outs),
        out_shape=outs,
        scratch_shapes=scratch,
        compiler_params=params(40),
        cost_estimate=cost(1e9, 15e6),
        name="place",
    )(ids, visible, order, gains, *sums, *sums_reg, dh, dy1, *x_enc, *lat_enc, *res, *dx_reg)


def hop(value, bit):
    return lax.ppermute(value, "dp", [(i, i ^ bit) for i in range(16)])


def halve(terms, bit):
    mine = (lax.axis_index("dp") // bit) % 2

    def half(which):
        return [lax.dynamic_index_in_dim(term, which, 0, keepdims=False) for term in terms]

    theirs = half(1 - mine)
    total = theirs[0].astype(F32)
    for term in theirs[1:]:
        total = total + term.astype(F32)
    return total.astype(terms[0].dtype), half(mine)


def total_of(terms):
    total = terms[0].astype(F32)
    for term in terms[1:]:
        total = total + term.astype(F32)
    return total


def in_order(first, then):
    return lax.optimization_barrier((first, then))


def scatter_small(rows, count):
    own = D // count
    flat = jnp.concatenate(
        [
            jnp.moveaxis(rows[:6].reshape(6, count, own), 1, 0).reshape(count, 6 * own),
            rows[6:8].reshape(count, 2 * own),
            rows[8:12].reshape(count, 4 * own),
        ],
        axis=1,
    )
    if count == 16:
        terms = [flat.reshape(2, 2, 2, 2, 12 * own).transpose(3, 2, 1, 0, 4)]
        for bit in (1, 2, 4, 8):
            sent, terms = halve(terms, bit)
            terms = terms + [hop(sent, bit)]
        got = total_of(terms)
    else:
        got = lax.psum_scatter(flat, "dp", scatter_dimension=0, tiled=True)[0]
    return (
        got[: 2 * own].reshape(2, own),
        got[2 * own : 6 * own].reshape(4, own),
        got[6 * own : 8 * own],
        got[8 * own :],
    )


def scatter_natural(blocks, count):
    return lax.psum_scatter(blocks, "dp", scatter_dimension=1, tiled=True).astype(F32)


def side_by_side(blocks):
    return jnp.concatenate([blocks[i] for i in range(blocks.shape[0])], axis=1)


def local(
    patch_rows, cotangent, patch_order, visible, qkv_weight, out_weight, up_weight, down_weight, norm_gains, biases,
    qv_bias, up_bias, target_qkv, target_out, target_up, target_down, target_gains, target_biases, target_qv_bias,
    target_up_bias,
):
    count = lax.axis_size("dp")
    tree = count == 16
    ids = jnp.stack([lax.axis_index("section"), lax.axis_index("dp") % 2]).astype(jnp.int32)
    groups = patch_order.shape[0] // GROUP
    weights = (qkv_weight, out_weight, up_weight, down_weight)
    targets = (target_qkv, target_out, target_up, target_down)
    vecs = (norm_gains, biases, qv_bias, up_bias)
    target_vecs = (target_gains, target_biases, target_qv_bias[None], target_up_bias[None])

    encoded = [encode(g, ids, visible, patch_order, *vecs, patch_rows, weights) for g in range(groups)]
    lat, x_e, hq_e, q_e, k_e, v_e, p_e, o_e, y1_e, h2_e, gp_e, a_e = zip(*encoded)
    sent = [lax.ppermute(piece, "section", [(0, 1)]) for piece in lat]
    middles = [
        middle(g, ids, visible, patch_order, vecs, target_vecs, patch_rows, cotangent, sent[g], weights, targets)
        for g in range(groups)
    ]
    (dlat, res, hq_r, hk_r, dq_r, dkv_r, o_r, dy1b_r, h2_r, du_r, a_r, dyb_r, dx_r, sums_r, cot_e) = zip(*middles)
    back = [lax.ppermute(piece, "section", [(1, 0)]) for piece in dlat]

    down, dyb, sums_down = down_grad(groups, count, ids, cot_e, back, a_e, a_r, dyb_r)
    if tree:
        down_x, down_own = halve([down[0], hop(down[1], 1)], 2)
        down_x, dyb = in_order(down_x, dyb)
        down_own = down_own + [hop(down_x, 2)]
    up, dy1, sums_up = up_grad(
        groups, count, ids, norm_gains, dyb, up_weight, down_weight, y1_e, gp_e, h2_e, du_r, h2_r
    )
    if tree:
        up_x, up_own = halve([up[0], hop(up[1], 1)], 2)
        down_z, down_own = halve(down_own, 4)
        (up_x, down_z), dy1 = in_order((up_x, down_z), dy1)
        up_own = up_own + [hop(up_x, 2)]
        down_own = down_own + [hop(down_z, 4)]
    attn, dh, sums_attn = attn_grad(
        groups, count, ids, dy1, qkv_weight, out_weight, q_e, k_e, v_e, p_e, o_e, hq_e,
        hq_r, hk_r, dq_r, dkv_r, o_r, dy1b_r,
    )
    if tree:
        attn_x, attn_own = halve([attn[0], hop(attn[1], 1)], 2)
        up_z, up_own = halve(up_own, 4)
        down_z, down_own = halve(down_own, 8)
        (attn_x, up_z, down_z), dh = in_order((attn_x, up_z, down_z), dh)
        attn_own = attn_own + [hop(attn_x, 2)]
        up_own = up_own + [hop(up_z, 4)]
        down_own = down_own + [hop(down_z, 8)]
    block_out, grad_rows, small = place(
        groups, ids, visible, patch_order, norm_gains, (sums_down, sums_up, sums_attn), sums_r, dh, dy1, x_e, lat,
        res, dx_r,
    )
    if tree:
        up_z, up_own = halve(up_own, 8)
        up_own = up_own + [hop(up_z, 8)]
        for bit in (4, 8):
            attn_z, attn_own = halve(attn_own, bit)
            attn_own = attn_own + [hop(attn_z, bit)]
        down_sum, up_sum, attn_sum = total_of(down_own), total_of(up_own), total_of(attn_own)
    else:
        down_sum, up_sum, attn_sum = (scatter_natural(one[0], count) for one in (down, up, attn))
    gains, bias_rows, qv_rows, up_rows = scatter_small(small, count)
    return (
        block_out,
        grad_rows,
        jnp.concatenate([attn_sum[2], attn_sum[0], attn_sum[1]], axis=1)[None],
        attn_sum[3][None],
        side_by_side(up_sum)[None],
        down_sum,
        gains[None],
        bias_rows[None],
        qv_rows[None],
        up_rows[None],
    )


def solution(mesh):
    three, four = P("section", None, None), P("section", "dp", None, None)
    grad = P("section", "dp", None)
    return jax.shard_map(
        local,
        mesh=mesh,
        in_specs=(four, four, P("dp", None), P("dp"), three, three, three, three, three, three,
                  P("section", None), P("section", None), P(), P(), P(), P(), P(), P(), P(), P()),
        out_specs=(four, four, grad, grad, grad, grad, P("section", None, "dp"), P("section", None, "dp"),
                   P("section", "dp"), P("section", "dp")),
        check_vma=False,
    )
```

```python
from functools import partial

import jax
import jax.numpy as jnp
from jax import lax
from jax.experimental import pallas as pl
from jax.experimental.pallas import tpu as pltpu
from jax.sharding import PartitionSpec as P

HEADS = 12
PATCH = 196
D = 768
FF = 3072
EPS = 1e-06
NV = 144
NM = 128
FIRST = PATCH - NM
GROUP = 2
CHUNK = 32

BF = jnp.bfloat16
F32 = jnp.float32
MIB = 1024 * 1024

HBM = pl.BlockSpec(memory_space=pl.ANY)
VMEM = pl.BlockSpec(memory_space=pltpu.VMEM)
SMEM = pl.BlockSpec(memory_space=pltpu.SMEM)


def nn(a, b):
    return jnp.dot(a, b, preferred_element_type=F32)


def nt(a, b):
    return lax.dot_general(a, b, (((1,), (1,)), ((), ())), preferred_element_type=F32)


def tn(a, b):
    return lax.dot_general(a, b, (((0,), (0,)), ((), ())), preferred_element_type=F32)


def loop(count, body, unroll=1):
    def step(i, carry):
        for u in range(unroll):
            body(i * unroll + u)
        return carry

    if count == unroll:
        step(0, 0)
    else:
        lax.fori_loop(0, count // unroll, step, 0)


def unroll_of(count):
    return next(u for u in (4, 3, 2, 1) if count % u == 0)


def rows_of(i, size):
    return pl.ds(pl.multiple_of(i * size, size), size)


def f32_row(ref, row, col=0, width=D):
    return ref[pl.ds(row, 1), pl.ds(col, width)].astype(F32)


class Copies:
    def __init__(self, sems):
        self.sems = sems
        self.used = 0
        self.open = []

    def start(self, src, dst):
        copy = pltpu.make_async_copy(src, dst, self.sems.at[self.used])
        self.used += 1
        copy.start()
        self.open.append(copy)
        return copy

    def wait(self, *copies):
        for copy in copies:
            copy.wait()
            self.open.remove(copy)

    def finish(self):
        self.wait(*list(self.open))


def gelu_pair(u):
    size = jnp.abs(u)
    base = 1.0 + (0.3275911 * 0.7071067811865476) * size
    guess = pl.reciprocal(base, approx=True)
    t = guess * (2.0 - base * guess)
    ex = jnp.exp(-0.5 * (u * u))
    poly = 0.5306027145 * t - 0.7265760135
    poly = poly * t + 0.7107068705
    poly = poly * t - 0.142248368
    poly = poly * t + 0.127414796
    tail = poly * t * ex
    phi = jnp.where(u >= 0.0, 1.0 - tail, tail)
    return u * phi, phi + u * (0.3989422804014327 * ex)


def norm_rows(src, dst, rows, gain, shift):
    def body(i):
        sel = rows_of(i, CHUNK)
        x = src[sel, :].astype(F32)
        centered = x - jnp.mean(x, axis=-1, keepdims=True)
        var = jnp.mean(centered * centered, axis=-1, keepdims=True)
        dst[sel, :] = (centered * lax.rsqrt(var + EPS) * gain + shift).astype(BF)

    loop(rows // CHUNK, body, unroll_of(rows // CHUNK))


def norm_back(src, grad, base, write, rows, gain):
    count = rows // CHUNK
    unroll = 3 if count % 3 == 0 else 2

    def step(i, carry):
        for u in range(unroll):
            carry = one(i * unroll + u, carry)
        return carry

    def one(i, carry):
        d_gain, d_shift = carry
        sel = rows_of(i, CHUNK)
        x = src[sel, :].astype(F32)
        dh = grad[sel, :]
        centered = x - jnp.mean(x, axis=-1, keepdims=True)
        var = jnp.mean(centered * centered, axis=-1, keepdims=True)
        rstd = lax.rsqrt(var + EPS)
        hat = centered * rstd
        g = dh * gain
        part = dh * hat
        dx = rstd * (
            g
            - jnp.mean(g, axis=-1, keepdims=True)
            - hat * jnp.mean(g * hat, axis=-1, keepdims=True)
        )
        if base is not None:
            dx = dx + base[sel, :].astype(F32)
        write(sel, dx)
        d_gain = d_gain + jnp.sum(part.reshape(CHUNK // 8, 8, D), axis=0)
        d_shift = d_shift + jnp.sum(dh.reshape(CHUNK // 8, 8, D), axis=0)
        return d_gain, d_shift

    zero = jnp.zeros((8, D), F32)
    d_gain, d_shift = lax.fori_loop(0, count // unroll, step, (zero, zero))
    return jnp.sum(d_gain, axis=0, keepdims=True), jnp.sum(d_shift, axis=0, keepdims=True)


def column_sum(ref, rows, col=0, width=D):
    def step(i, carry):
        x = ref[rows_of(i, CHUNK), pl.ds(col, width)].astype(F32)
        return carry + jnp.sum(x.reshape(CHUNK // 8, 8, width), axis=0)

    total = lax.fori_loop(0, rows // CHUNK, step, jnp.zeros((8, width), F32))
    return jnp.sum(total, axis=0, keepdims=True)


def as_bf16(flags):
    return jnp.where(flags, 1.0, 0.0).astype(BF)


def place_matrix(order, image, start, count, low, high):
    row = order[pl.ds(image, 1), pl.ds(start, count)]
    rank = start + lax.broadcasted_iota(jnp.int32, (1, count), 1)
    row = jnp.where((rank >= low) & (rank < high), row, -1)
    return as_bf16(row == lax.broadcasted_iota(jnp.int32, (PATCH, count), 0))


def split_pair(pair):
    lane = lax.broadcasted_iota(jnp.int32, pair.shape, 1)
    zero = jnp.zeros_like(pair)
    return jnp.concatenate([jnp.where(lane < 64, pair, zero), jnp.where(lane < 64, zero, pair)], axis=0)


def join_rows(both):
    rows = both.shape[0] // 2
    lane = lax.broadcasted_iota(jnp.int32, (rows, 128), 1)
    return jnp.where(lane < 64, both[:rows], both[rows:])


def join_columns(both):
    rows = both.shape[1] // 2
    return jnp.concatenate([both[:64, :rows], both[64:, rows:]], axis=0).T


PAIRS = HEADS // 2
STEP = 3


def each_pair_group(images, body):
    def group(i):
        image = i // (PAIRS // STEP)
        first = (i % (PAIRS // STEP)) * STEP
        pairs = [first + step for step in range(STEP)]
        body(image, [image * PAIRS + pair for pair in pairs], [pl.ds(pl.multiple_of(pair * 128, 128), 128) for pair in pairs])

    loop(images * (PAIRS // STEP), group)


def softmax(scores, axis):
    ex = jnp.exp(scores - jnp.max(scores, axis=axis, keepdims=True))
    return (ex * (1.0 / jnp.sum(ex, axis=axis, keepdims=True))).astype(BF)


def score_back(probs, d_probs, axis):
    wide = probs.astype(F32)
    return (wide * (d_probs - jnp.sum(d_probs * wide, axis=axis, keepdims=True))).astype(BF)


def attention_by_rows(images, n, q, k, v, p, o, count_of):
    def body(image, slots, lanes):
        sel = rows_of(image, n)
        ok = lax.broadcasted_iota(jnp.int32, (1, n), 1) < count_of(image)
        scores = [nt(split_pair(q[sel, at]), k[sel, at]) for at in lanes]
        probs = [softmax(jnp.where(ok, one, -1000000000.0), 1) for one in scores]
        for slot, one in zip(slots, probs):
            p[slot] = one
        mixed = [nn(one, v[sel, at]) for one, at in zip(probs, lanes)]
        for at, one in zip(lanes, mixed):
            o[sel, at] = join_rows(one).astype(BF)

    each_pair_group(images, body)


def attention_by_columns(images, nk, q, k, v, p, o, key_ok):
    def body(image, slots, lanes):
        qs, ks = rows_of(image, NM), rows_of(image, nk)
        ok = key_ok(image)
        scores = [nt(k[ks, at], split_pair(q[qs, at])) for at in lanes]
        probs = [softmax(jnp.where(ok, one, -1000000000.0), 0) for one in scores]
        if p is not None:
            for slot, one in zip(slots, probs):
                p[slot] = one
        mixed = [tn(v[ks, at], one) for one, at in zip(probs, lanes)]
        for at, one in zip(lanes, mixed):
            o[qs, at] = join_columns(one).astype(BF)

    each_pair_group(images, body)


def attention_back_rows(images, n, q, k, v, p, do, dq, dkv):
    def body(image, slots, lanes):
        sel = rows_of(image, n)
        d_mixed = [split_pair(do[sel, at]) for at in lanes]
        d_probs = [nt(one, v[sel, at]) for one, at in zip(d_mixed, lanes)]
        d_scores = [score_back(p[slot], one, 1) for slot, one in zip(slots, d_probs)]
        d_values = [tn(p[slot], one) for slot, one in zip(slots, d_mixed)]
        d_query = [nn(one, k[sel, at]) for one, at in zip(d_scores, lanes)]
        d_keys = [tn(one, split_pair(q[sel, at])) for one, at in zip(d_scores, lanes)]
        for at, value, query, key in zip(lanes, d_values, d_query, d_keys):
            dq[sel, at] = (join_rows(query) * 0.125).astype(BF)
            dkv[sel, at] = key.astype(BF)
            dkv[sel, pl.ds(pl.multiple_of(D + at.start, 128), 128)] = value.astype(BF)

    each_pair_group(images, body)


def attention_back_columns(images, nk, q, k, v, p, do, dq, dkv):
    def body(image, slots, lanes):
        qs, ks = rows_of(image, NM), rows_of(image, nk)
        d_mixed = [split_pair(do[qs, at]) for at in lanes]
        d_probs = [nt(v[ks, at], one) for one, at in zip(d_mixed, lanes)]
        d_scores = [score_back(p[slot], one, 0) for slot, one in zip(slots, d_probs)]
        d_values = [nn(p[slot], one) for slot, one in zip(slots, d_mixed)]
        d_query = [tn(k[ks, at], one) for one, at in zip(d_scores, lanes)]
        d_keys = [nn(one, split_pair(q[qs, at])) for one, at in zip(d_scores, lanes)]
        for at, value, query, key in zip(lanes, d_values, d_query, d_keys):
            dq[qs, at] = (join_columns(query) * 0.125).astype(BF)
            dkv[ks, at] = key.astype(BF)
            dkv[ks, pl.ds(pl.multiple_of(D + at.start, 128), 128)] = value.astype(BF)

    each_pair_group(images, body)


TILE = 1024


def mlp_forward(rows, h2, w1, w2, up_b, u, a, gp, base):
    def multiply(j):
        u[j % 2] = nn(h2[...], w1[:, j * TILE : (j + 1) * TILE])

    multiply(0)
    for j in range(FF // TILE):
        if j + 1 < FF // TILE:
            multiply(j + 1)
        for c in range(0, TILE, 256):
            cols = slice(j * TILE + c, j * TILE + c + 256)
            shift = up_b[0:1, cols].astype(F32)
            for r in range(0, rows, CHUNK):
                value, slope = gelu_pair(u[j % 2, r : r + CHUNK, c : c + 256] + shift)
                a[r : r + CHUNK, cols] = value.astype(BF)
                if gp is not None:
                    gp[r : r + CHUNK, cols] = slope.astype(BF)
    return nn(a[...], w2[...]) + base()


def mlp_back(rows, dyb, gp, w1, w2, du, u, acc):
    for j in range(FF // TILE):
        cols = slice(j * TILE, (j + 1) * TILE)
        u[j % 2] = nt(dyb[...], w2[cols, :])
        for c in range(0, TILE, 256):
            at = slice(j * TILE + c, j * TILE + c + 256)
            for r in range(0, rows, CHUNK):
                sel = slice(r, r + CHUNK)
                du[sel, at] = (gp[sel, at].astype(F32) * u[j % 2, sel, c : c + 256]).astype(BF)
    acc[...] = nt(du[...], w1[...])


def cost(flops, nbytes):
    return pl.CostEstimate(flops=int(flops), bytes_accessed=int(nbytes), transcendentals=0)


def params(mib):
    return pltpu.CompilerParams(vmem_limit_bytes=mib * MIB)


def struct(shape, dtype=BF):
    return jax.ShapeDtypeStruct(shape, dtype)


def start_weights(copies, sources, scratch):
    return [copies.start(src, dst) for src, dst in zip(sources, scratch)]


def encode_kernel(group, ids, visible, order, gains, biases, qvb, upb, rows, cot, wqkv, wo, w1, w2,
                  lat_out, x_out, hq_out, q_out, k_out, v_out, p_out, o_out, y1_out, h2_out, gp_out, a_out,
                  rows_v, cot_v, sqkv, so, s1, s2, x, hq, q, k, v, p, o, y1, h2, gp, a, u, lat, sems):
    n = GROUP * NV

    @pl.when(ids[0] == 0)
    def _():
        copies = Copies(sems)
        got_rows = copies.start(rows.at[0, pl.ds(group * GROUP, GROUP)], rows_v)
        got_qkv, got_o, got_1, got_2 = start_weights(
            copies, (wqkv.at[0], wo.at[0], w1.at[0], w2.at[0]), (sqkv, so, s1, s2)
        )
        gain, bias = gains.at[0], biases.at[0]
        copies.wait(got_rows)
        for i in range(GROUP):
            image = group * GROUP + i
            pick = place_matrix(order, image, 0, NV, 0, visible[image])
            x[pl.ds(i * NV, NV), :] = tn(pick, rows_v[i]).astype(BF)
        copies.start(x, x_out)
        norm_rows(x, hq, n, f32_row(gain, 0), f32_row(bias, 0))
        copies.start(hq, hq_out)
        copies.wait(got_qkv)
        united = nn(hq[...], sqkv[...])
        q[...] = ((united[:, 0:D] + f32_row(qvb, 0)).astype(BF) * 0.125).astype(BF)
        k[...] = united[:, D : 2 * D].astype(BF)
        v[...] = (united[:, 2 * D :] + f32_row(qvb, 0, D)).astype(BF)
        copies.start(q, q_out)
        copies.start(k, k_out)
        copies.start(v, v_out)

        attention_by_rows(GROUP, NV, q, k, v, p, o, lambda i: visible[group * GROUP + i])
        copies.start(p, p_out)
        copies.start(o, o_out)
        copies.wait(got_o)
        y1[...] = nn(o[...], so[...]) + f32_row(bias, 1) + x[...].astype(F32)
        copies.start(y1, y1_out)
        norm_rows(y1, h2, n, f32_row(gain, 1), f32_row(bias, 2))
        copies.start(h2, h2_out)
        copies.wait(got_1, got_2)
        lat[...] = mlp_forward(n, h2, s1, s2, upb, u, a, gp, lambda: y1[...] + f32_row(bias, 3)).astype(BF)
        copies.start(gp, gp_out)
        copies.start(a, a_out)
        copies.start(lat, lat_out)
        copies.finish()

    @pl.when(ids[0] == 1)
    def _():
        m = GROUP * NM
        top = pl.ds(0, m)
        copies = Copies(sems)
        got_rows = copies.start(rows.at[0, pl.ds(group * GROUP, GROUP)], rows_v)
        got_cot = copies.start(cot.at[0, pl.ds(group * GROUP, GROUP)], cot_v)
        got_q = copies.start(wqkv.at[0, :, pl.ds(0, D)], so)
        gain, bias = gains.at[0], biases.at[0]
        copies.wait(got_rows, got_cot)
        for i in range(GROUP):
            image = group * GROUP + i
            pick = place_matrix(order, image, FIRST, NM, visible[image], PATCH)
            x[pl.ds(i * NM, NM), :] = tn(pick, rows_v[i]).astype(BF)
            k[pl.ds(i * NM, NM), :] = tn(pick, cot_v[i]).astype(BF)
        copies.start(x.at[top], x_out.at[top])
        copies.start(k.at[top], k_out.at[top])
        norm_rows(x, hq, m, f32_row(gain, 0), f32_row(bias, 0))
        copies.start(hq.at[top], hq_out.at[top])
        copies.wait(got_q)
        q[top, :] = ((nn(hq[top, :], so[...]) + f32_row(qvb, 0)).astype(BF) * 0.125).astype(BF)
        copies.start(q.at[top], q_out.at[top])
        copies.finish()


def encode(group, ids, visible, order, gains, biases, qvb, upb, rows, cot, weights):
    n = GROUP * NV
    row, wide = struct((n, D)), struct((n, FF))
    heads = struct((GROUP * PAIRS, 2 * NV, NV))
    outs = [row] * 6 + [heads, row, struct((n, D), F32), row, wide, wide]
    vm = lambda s: pltpu.VMEM(s.shape, s.dtype)
    scratch = [
        pltpu.VMEM((GROUP, PATCH, D), BF), pltpu.VMEM((GROUP, PATCH, D), BF),
        pltpu.VMEM((D, 3 * D), BF), pltpu.VMEM((D, D), BF), pltpu.VMEM((D, FF), BF), pltpu.VMEM((FF, D), BF),
        vm(row), vm(row), vm(row), vm(row), vm(row), vm(heads), vm(row), pltpu.VMEM((n, D), F32), vm(row),
        vm(wide), vm(wide), pltpu.VMEM((2, n, TILE), F32), vm(row),
        pltpu.SemaphoreType.DMA((20,)),
    ]
    return pl.pallas_call(
        partial(encode_kernel, group),
        in_specs=[SMEM, SMEM] + [VMEM] * 5 + [HBM] * 6,
        out_specs=[HBM] * len(outs),
        out_shape=outs,
        scratch_shapes=scratch,
        compiler_params=params(56),
        cost_estimate=cost(2 * n * 12 * D * D, 25e6),
        name="encode",
    )(ids, visible, order, gains, biases, qvb, upb, rows, cot, *weights)


def middle_kernel(group, ids, visible, order, gains, biases, qvb, upb, tgains, tbiases, tqvb, tupb,
                  rows, cot, lat_in, x_in, q_in, dyb_in, wqkv, wo, w1, w2, tqkv, to, t1, t2,
                  dlat_out, res_out, hk_out, dq_out, dkv_out, o_out, dy1b_out, h2_out, du_out, a_out,
                  dy1_out, sums_out, cot_out,
                  rows_v, cot_v, sqkv, so, s1, s2, x, lat, hq, hk, q, k, v, p, o, y1, h2, gp, a, u, acc,
                  res, dyb, du, dy1, dy1b, do, dq, dkv, dh, dlat, sums, sems):
    n, m = GROUP * NM, GROUP * NV
    top = pl.ds(0, n)

    def forward(copies, got_weights, gain, bias, ub, nk, key_ok, keep_p, keep_slope):
        got_o, got_1, got_2 = got_weights
        attention_by_columns(GROUP, nk, q, k, v, keep_p, o, key_ok)
        copies.wait(got_o)
        y1[...] = nn(o[...], so[...]) + f32_row(bias, 1) + x[...].astype(F32)
        norm_rows(y1, h2, n, f32_row(gain, 1), f32_row(bias, 2))
        copies.wait(got_1, got_2)
        res[...] = mlp_forward(n, h2, s1, s2, ub, u, a, keep_slope, lambda: y1[...] + f32_row(bias, 3)).astype(BF)
        copies.start(res, res_out)

    @pl.when(ids[0] == 0)
    def _():
        copies = Copies(sems)
        gain, bias = tgains, tbiases
        got_rows = copies.start(rows.at[0, pl.ds(group * GROUP, GROUP)], rows_v)
        got_qkv = copies.start(tqkv, sqkv)
        got_weights = start_weights(copies, (to, t1, t2), (so, s1, s2))
        got_cot = copies.start(cot.at[0, pl.ds(group * GROUP, GROUP)], cot_v)
        copies.wait(got_rows)
        for i in range(GROUP):
            image = group * GROUP + i
            pick = place_matrix(order, image, FIRST, NM, visible[image], PATCH)
            x[pl.ds(i * NM, NM), :] = tn(pick, rows_v[i]).astype(BF)
        norm_rows(x, hq, n, f32_row(gain, 0), f32_row(bias, 0))
        copies.wait(got_qkv)
        united = nn(hq[...], sqkv[...])
        q[...] = ((united[:, :D] + f32_row(tqvb, 0)).astype(BF) * 0.125).astype(BF)
        k[top, :] = united[:, D : 2 * D].astype(BF)
        v[top, :] = (united[:, 2 * D :] + f32_row(tqvb, 0, D)).astype(BF)

        def key_ok(i):
            return lax.broadcasted_iota(jnp.int32, (NM, 1), 0) + FIRST >= visible[group * GROUP + i]

        forward(copies, got_weights, gain, bias, tupb, NM, key_ok, None, None)
        copies.wait(got_cot)
        for i in range(GROUP):
            image = group * GROUP + i
            pick = place_matrix(order, image, 0, NV, 0, visible[image])
            lat[pl.ds(i * NV, NV), :] = tn(pick, cot_v[i]).astype(BF)
        copies.start(lat, cot_out)
        copies.finish()

    @pl.when(ids[0] == 1)
    def _():
        copies = Copies(sems)
        gain, bias = gains.at[0], biases.at[0]
        got_lat = copies.start(lat_in, lat)
        got_kv = copies.start(wqkv.at[0, :, pl.ds(D, 2 * D)], sqkv.at[:, pl.ds(D, 2 * D)])
        got_q = copies.start(q_in.at[top], q)
        got_x = copies.start(x_in.at[top], x)
        got_weights = start_weights(copies, (wo.at[0], w1.at[0], w2.at[0]), (so, s1, s2))
        got_dyb = copies.start(dyb_in.at[top], dyb)
        copies.wait(got_lat)
        norm_rows(lat, hk, m, f32_row(gain, 0), f32_row(bias, 0))
        copies.start(hk, hk_out)
        copies.wait(got_kv)
        united = nn(hk[...], sqkv[:, D:])
        k[...] = united[:, :D].astype(BF)
        v[...] = (united[:, D:] + f32_row(qvb, 0, D)).astype(BF)
        copies.wait(got_q, got_x)

        def key_ok(i):
            return lax.broadcasted_iota(jnp.int32, (NV, 1), 0) < visible[group * GROUP + i]

        forward(copies, got_weights, gain, bias, upb.at[0:1], NV, key_ok, p, gp)
        copies.start(o, o_out)
        copies.start(h2, h2_out)
        copies.start(a, a_out)
        copies.wait(got_dyb)
        mlp_back(n, dyb, gp, s1, s2, du, u, acc)
        copies.start(du, du_out)

        def keep(sel, dx):
            dy1[sel, :] = dx
            dy1b[sel, :] = dx.astype(BF)

        g2, b2 = norm_back(y1, acc, dyb, keep, n, f32_row(gain, 1))
        copies.start(dy1, dy1_out)
        copies.start(dy1b, dy1b_out)
        do[...] = nt(dy1b[...], so[...]).astype(BF)
        attention_back_columns(GROUP, NV, q, k, v, p, do, dq, dkv)
        copies.start(dq, dq_out)
        copies.start(dkv, dkv_out)
        dh[...] = nt(dkv[...], sqkv[:, D:])

        def keep_side(sel, dx):
            dlat[sel, :] = dx.astype(BF)

        gk, bk = norm_back(lat, dh, None, keep_side, m, f32_row(gain, 0))
        copies.start(dlat, dlat_out)
        for row, value in enumerate((gk, g2, bk, b2)):
            sums[pl.ds(row, 1), :] = value
        copies.start(sums, sums_out)
        copies.finish()


def middle(group, ids, visible, order, own_vecs, target_vecs, rows, cot, lat, x, q, dyb, weights, targets):
    n, m = GROUP * NM, GROUP * NV
    row, side, wide = struct((n, D)), struct((m, D)), struct((n, FF))
    pair = struct((m, 2 * D))
    outs = [side, row, side, row, pair, row, row, row, wide, wide, struct((n, D), F32), struct((8, D), F32), side]
    vm = lambda s: pltpu.VMEM(s.shape, s.dtype)
    full, fside = pltpu.VMEM((n, D), F32), pltpu.VMEM((m, D), F32)
    scratch = [
        pltpu.VMEM((GROUP, PATCH, D), BF), pltpu.VMEM((GROUP, PATCH, D), BF),
        pltpu.VMEM((D, 3 * D), BF), pltpu.VMEM((D, D), BF), pltpu.VMEM((D, FF), BF), pltpu.VMEM((FF, D), BF),
        vm(row), vm(side), vm(row), vm(side), vm(row), vm(side), vm(side),
        pltpu.VMEM((GROUP * PAIRS, NV, 2 * NM), BF), vm(row), full, vm(row), vm(wide), vm(wide),
        pltpu.VMEM((2, n, TILE), F32), full,
        vm(row), vm(row), vm(wide), full, vm(row), vm(row), vm(row), vm(pair), fside, vm(side),
        pltpu.VMEM((8, D), F32),
        pltpu.SemaphoreType.DMA((24,)),
    ]
    return pl.pallas_call(
        partial(middle_kernel, group),
        in_specs=[SMEM, SMEM] + [VMEM] * 9 + [HBM] * 14,
        out_specs=[HBM] * len(outs),
        out_shape=outs,
        scratch_shapes=scratch,
        compiler_params=params(56),
        cost_estimate=cost(4 * n * 12 * D * D, 25e6),
        name="middle",
    )(ids, visible, order, *own_vecs, *target_vecs, rows, cot, lat, x, q, dyb, *weights, *targets)


def stack_rows(copies, pieces, ref, size):
    return [copies.start(piece, ref.at[pl.ds(i * size, size)]) for i, piece in enumerate(pieces)]


def clear_tail(ref, used):
    ref[pl.ds(used, ref.shape[0] - used), :] = jnp.zeros((ref.shape[0] - used, ref.shape[1]), ref.dtype)


def halves(count):
    return [struct((2, 2, 2, D // 16, D))] * 2 if count == 16 else [struct((D, D))]


def give_block(copies, core, value, out, dest, j):
    out[j] = value
    if len(dest) == 4:
        copies.start(out.at[j], dest[j])
        return
    view = out.at[j].reshape(2, 2, 2, 2, D // 16, D)
    for x in range(2):
        for low in range(2):
            copies.start(view.at[:, low, x, core], dest[2 * j].at[x, low])
            copies.start(view.at[:, low, x, 1 - core], dest[2 * j + 1].at[x, low])


def give_rows(copies, core, value, out, dest, j):
    out[j] = value
    if len(dest) == 1:
        copies.start(out.at[j], dest[0].at[pl.ds(j * D, D)])
        return
    view = out.at[j].reshape(2, 2, D // 4, D)
    for x in range(2):
        copies.start(view.at[x, core], dest[0].at[x, j % 2, j // 2])
        copies.start(view.at[x, 1 - core], dest[1].at[x, j % 2, j // 2])


def down_kernel(groups, parts, ids, *refs):
    cot, lat, a_enc, a_reg, dyb_reg = (refs[i * groups : (i + 1) * groups] for i in range(5))
    refs = refs[5 * groups :]
    dest, refs = refs[:parts], refs[parts:]
    dyb_out, sums_out, cot_v, dyb, a, dlat, out, sums, sems = refs
    images = groups * GROUP
    nv, nm = GROUP * NV, GROUP * NM

    @pl.when(ids[0] == 0)
    def _():
        copies = Copies(sems)
        got = stack_rows(copies, cot, cot_v, nv) + stack_rows(copies, lat, dlat, nv)
        stack_rows(copies, a_enc, a, nv)
        copies.wait(*got)
        dyb[...] = (cot_v[...].astype(F32) + dlat[...].astype(F32)).astype(BF)
        copies.start(dyb, dyb_out)
        copies.finish()

    @pl.when(ids[0] == 1)
    def _():
        copies = Copies(sems)
        stack_rows(copies, a_reg, a, nm)
        stack_rows(copies, [piece.at[pl.ds(0, nm)] for piece in dyb_reg], dyb, nm)
        clear_tail(a, images * NM)
        clear_tail(dyb, images * NM)
        copies.finish()

    copies = Copies(sems)
    for j in range(4):
        give_rows(copies, ids[1], tn(a[:, j * D : (j + 1) * D], dyb[...]).astype(BF), out, dest, j)
    sums[...] = jnp.broadcast_to(column_sum(dyb, images * NV), (8, D))
    copies.start(sums, sums_out)
    copies.finish()


def down_grad(groups, count, ids, cot, dlat, a_enc, a_reg, dyb_reg):
    n = groups * GROUP * NV
    main = [struct((2, 2, 2, D // 4, D))] * 2 if count == 16 else [struct((FF, D))]
    outs = main + [struct((n, D)), struct((8, D), F32)]
    row = pltpu.VMEM((n, D), BF)
    scratch = [
        row, row, pltpu.VMEM((n, FF), BF), row, pltpu.VMEM((4, D, D), BF), pltpu.VMEM((8, D), F32),
        pltpu.SemaphoreType.DMA((24,)),
    ]
    got = pl.pallas_call(
        partial(down_kernel, groups, len(main)),
        in_specs=[SMEM] + [HBM] * (5 * groups),
        out_specs=[HBM] * len(outs),
        out_shape=outs,
        scratch_shapes=scratch,
        compiler_params=params(56),
        cost_estimate=cost(1e6, 1e5),
        name="down_grad",
    )(ids, *cot, *dlat, *a_enc, *a_reg, *dyb_reg)
    return got[: len(main)], got[-2], got[-1]


def up_kernel(groups, parts, ids, gains, dyb_in, w1, w2, *refs):
    y1_enc, gp_enc, h2_enc, du_reg, h2_reg = (refs[i * groups : (i + 1) * groups] for i in range(5))
    refs = refs[5 * groups :]
    dest, refs = refs[:parts], refs[parts:]
    dy1_out, sums_out, s1, s2, dyb, gp, y1, h2, du, u, acc, dy1, out, sums, sems = refs
    images = groups * GROUP
    nv, nm = GROUP * NV, GROUP * NM

    @pl.when(ids[0] == 0)
    def _():
        copies = Copies(sems)
        got = [copies.start(dyb_in, dyb), copies.start(w2.at[0], s2)]
        got += stack_rows(copies, gp_enc, gp, nv)
        got.append(copies.start(w1.at[0], s1))
        got_y = stack_rows(copies, y1_enc, y1, nv)
        stack_rows(copies, h2_enc, h2, nv)
        copies.wait(*got)
        mlp_back(images * NV, dyb, gp, s1, s2, du, u, acc)
        copies.wait(*got_y)

        def keep(sel, dx):
            dy1[sel, :] = dx

        g2, b2 = norm_back(y1, acc, dyb, keep, images * NV, f32_row(gains.at[0], 1))
        copies.start(dy1, dy1_out)
        sums[pl.ds(0, 1), :] = g2
        sums[pl.ds(1, 1), :] = b2
        copies.finish()

    @pl.when(ids[0] == 1)
    def _():
        copies = Copies(sems)
        stack_rows(copies, du_reg, du, nm)
        stack_rows(copies, h2_reg, h2, nm)
        clear_tail(du, images * NM)
        clear_tail(h2, images * NM)
        sums[pl.ds(0, 2), :] = jnp.zeros((2, D), F32)
        copies.finish()

    copies = Copies(sems)
    for j in range(4):
        value = tn(h2[...], du[:, j * D : (j + 1) * D]).astype(BF)
        give_block(copies, ids[1], value, out, dest, j)
        sums[pl.ds(4 + j, 1), :] = column_sum(du, images * NV, j * D)
    copies.start(sums, sums_out)
    copies.finish()


def up_grad(groups, count, ids, gains, dyb, w1, w2, y1_enc, gp_enc, h2_enc, du_reg, h2_reg):
    n = groups * GROUP * NV
    main = halves(count) * 4
    outs = main + [struct((n, D), F32), struct((8, D), F32)]
    scratch = [
        pltpu.VMEM((D, FF), BF), pltpu.VMEM((FF, D), BF), pltpu.VMEM((n, D), BF), pltpu.VMEM((n, FF), BF),
        pltpu.VMEM((n, D), F32), pltpu.VMEM((n, D), BF), pltpu.VMEM((n, FF), BF), pltpu.VMEM((2, n, TILE), F32),
        pltpu.VMEM((n, D), F32), pltpu.VMEM((n, D), F32), pltpu.VMEM((4, D, D), BF), pltpu.VMEM((8, D), F32),
        pltpu.SemaphoreType.DMA((36,)),
    ]
    got = pl.pallas_call(
        partial(up_kernel, groups, len(main)),
        in_specs=[SMEM, VMEM] + [HBM] * (3 + 5 * groups),
        out_specs=[HBM] * len(outs),
        out_shape=outs,
        scratch_shapes=scratch,
        compiler_params=params(56),
        cost_estimate=cost(1e6, 1e5),
        name="up_grad",
    )(ids, gains, dyb, w1, w2, *y1_enc, *gp_enc, *h2_enc, *du_reg, *h2_reg)
    return got[: len(main)], got[-2], got[-1]


def attn_kernel(groups, ids, dy1_in, wo, *refs):
    q_enc, k_enc, v_enc, p_enc = (refs[i * groups : (i + 1) * groups] for i in range(4))
    dq_out, dkv_out, dy1b_out, so, dy1, dy1b, q, k, v, p, do, dq, dkv, sems = refs[4 * groups :]
    images = groups * GROUP
    nv = GROUP * NV

    @pl.when(ids[0] == 0)
    def _():
        copies = Copies(sems)
        got = [copies.start(dy1_in, dy1), copies.start(wo.at[0], so)]
        for piece, ref in ((v_enc, v), (k_enc, k), (q_enc, q)):
            got += stack_rows(copies, piece, ref, nv)
        got += stack_rows(copies, p_enc, p, GROUP * PAIRS)
        copies.wait(*got[:2])
        dy1b[...] = dy1[...].astype(BF)
        copies.start(dy1b, dy1b_out)
        do[...] = nt(dy1b[...], so[...]).astype(BF)
        copies.wait(*got[2:])
        attention_back_rows(images, NV, q, k, v, p, do, dq, dkv)
        copies.start(dq, dq_out)
        copies.start(dkv, dkv_out)
        copies.finish()


def attn_back(groups, ids, dy1, wo, *pieces):
    n = groups * GROUP * NV
    row = pltpu.VMEM((n, D), BF)
    outs = [struct((n, D)), struct((n, 2 * D)), struct((n, D))]
    scratch = [
        pltpu.VMEM((D, D), BF), pltpu.VMEM((n, D), F32), row, row, row, row,
        pltpu.VMEM((groups * GROUP * PAIRS, 2 * NV, NV), BF), row, row, pltpu.VMEM((n, 2 * D), BF),
        pltpu.SemaphoreType.DMA((16,)),
    ]
    return pl.pallas_call(
        partial(attn_kernel, groups),
        in_specs=[SMEM] + [HBM] * (2 + 4 * groups),
        out_specs=[HBM] * len(outs),
        out_shape=outs,
        scratch_shapes=scratch,
        compiler_params=params(56),
        cost_estimate=cost(1e6, 1e5),
        name="attn_back",
    )(ids, dy1, wo, *[ref for piece in pieces for ref in piece])


def qkv_kernel(groups, parts, ids, dq_enc, dkv_enc, dy1b_enc, *refs):
    pieces = [refs[i * groups : (i + 1) * groups] for i in range(7)]
    o_enc, hq_in, hk_reg, dq_reg, dkv_reg, o_reg, dy1b_reg = pieces
    refs = refs[7 * groups :]
    dest, refs = refs[:parts], refs[parts:]
    sums_out, dy1b, o, hq, hk, dq, dkv, out, sums, sems = refs
    images = groups * GROUP
    nv, nm = GROUP * NV, GROUP * NM

    @pl.when(ids[0] == 0)
    def _():
        copies = Copies(sems)
        copies.start(dq_enc, dq)
        stack_rows(copies, hq_in, hq, nv)
        stack_rows(copies, hq_in, hk, nv)
        copies.start(dkv_enc, dkv)
        copies.start(dy1b_enc, dy1b)
        stack_rows(copies, o_enc, o, nv)
        copies.finish()

    @pl.when(ids[0] == 1)
    def _():
        copies = Copies(sems)
        for piece, ref in ((hq_in, hq), (dq_reg, dq), (o_reg, o), (dy1b_reg, dy1b)):
            stack_rows(copies, [one.at[pl.ds(0, nm)] for one in piece], ref, nm)
            clear_tail(ref, images * NM)
        for piece, ref in ((hk_reg, hk), (dkv_reg, dkv)):
            stack_rows(copies, piece, ref, nv)
        copies.finish()

    copies = Copies(sems)
    pairs = ((hq, dq), (hk, dkv.at[:, pl.ds(0, D)]), (hk, dkv.at[:, pl.ds(D, D)]), (o, dy1b))
    for j, (left, right) in enumerate(pairs):
        give_block(copies, ids[1], tn(left[...], right[...]).astype(BF), out, dest, j)
    for row, value in enumerate((
        column_sum(dy1b, images * NV), column_sum(dq, images * NV), column_sum(dkv, images * NV, D)
    )):
        sums[pl.ds(row, 1), :] = value
    copies.start(sums, sums_out)
    copies.finish()


def qkv_grad(groups, count, ids, dq, dkv, dy1b, *pieces):
    n = groups * GROUP * NV
    row = pltpu.VMEM((n, D), BF)
    main = halves(count) * 4
    outs = main + [struct((8, D), F32)]
    scratch = [
        row, row, row, row, row, pltpu.VMEM((n, 2 * D), BF), pltpu.VMEM((4, D, D), BF), pltpu.VMEM((8, D), F32),
        pltpu.SemaphoreType.DMA((40,)),
    ]
    got = pl.pallas_call(
        partial(qkv_kernel, groups, len(main)),
        in_specs=[SMEM] + [HBM] * (3 + 7 * groups),
        out_specs=[HBM] * len(outs),
        out_shape=outs,
        scratch_shapes=scratch,
        compiler_params=params(56),
        cost_estimate=cost(1e6, 1e5),
        name="qkv_grad",
    )(ids, dq, dkv, dy1b, *[ref for piece in pieces for ref in piece])
    return got[: len(main)], got[-1]


def place_kernel(groups, ids, visible, order, gains, down_sums, up_sums, attn_sums, *refs):
    sums_reg, (wqkv, dq_in, dkv_in, dy1_in), refs = refs[:groups], refs[groups : groups + 4], refs[groups + 4 :]
    x_in, lat_enc, res, dq_reg, dy1_reg = (refs[i * groups : (i + 1) * groups] for i in range(5))
    block_out, grad_out, small, sqkv, x, dq, dkv, dh, dy1, lat, out, sems = refs[5 * groups :]
    images = groups * GROUP
    nv, nm = GROUP * NV, GROUP * NM

    def put_grad(i, put, value):
        high = value.astype(BF)
        low = (value - high.astype(F32)).astype(BF)
        grad_out[0, i] = nn(put, high) + nn(put, low)

    def set_norms(g1, g2, b1, b2):
        for row, value in ((0, g1), (1, g2), (2, b1), (4, b2)):
            small[pl.ds(row, 1), :] = value

    small[pl.ds(3, 1), :] = attn_sums[0:1, :]
    small[pl.ds(5, 1), :] = down_sums[0:1, :]
    small[pl.ds(6, 2), :] = attn_sums[1:3, :]
    small[pl.ds(8, 4), :] = up_sums[4:8, :]
    small[pl.ds(12, 4), :] = jnp.zeros((4, D), F32)

    @pl.when(ids[0] == 0)
    def _():
        copies = Copies(sems)
        got = [copies.start(dkv_in, dkv), copies.start(wqkv.at[0], sqkv), copies.start(dq_in, dq)]
        got += [copies.start(dy1_in, dy1)] + stack_rows(copies, x_in, x, nv)
        got_out = stack_rows(copies, lat_enc, lat, nv) + stack_rows(copies, res, out, nm)
        copies.wait(*got)
        dh[...] = nt(dq[...], sqkv[:, 0:D]) + nt(dkv[...], sqkv[:, D:])

        def keep(sel, dx):
            dy1[sel, :] = dx

        g1, b1 = norm_back(x, dh, dy1, keep, images * NV, f32_row(gains.at[0], 0))
        set_norms(g1, up_sums[0:1, :], b1, up_sums[1:2, :])
        copies.wait(*got_out)
        for i in range(images):
            put = place_matrix(order, i, 0, NV, 0, visible[i])
            put_side = place_matrix(order, i, FIRST, NM, visible[i], PATCH)
            put_grad(i, put, dy1[pl.ds(i * NV, NV), :])
            block_out[0, i] = (nn(put, lat[pl.ds(i * NV, NV), :]) + nn(put_side, out[pl.ds(i * NM, NM), :])).astype(BF)

    @pl.when(ids[0] == 1)
    def _():
        copies = Copies(sems)
        copies.start(wqkv.at[0, :, pl.ds(0, D)], sqkv.at[:, pl.ds(0, D)])
        stack_rows(copies, [piece.at[pl.ds(0, nm)] for piece in x_in], x, nm)
        stack_rows(copies, dq_reg, dq, nm)
        stack_rows(copies, dy1_reg, dy1, nm)
        stack_rows(copies, res, out, nm)
        copies.finish()
        rows = images * NM
        dh[pl.ds(0, rows), :] = nt(dq[pl.ds(0, rows), :], sqkv[:, 0:D])

        def keep(sel, dx):
            dy1[sel, :] = dx

        g1, b1 = norm_back(x, dh, dy1, keep, rows, f32_row(gains.at[0], 0))
        total = sums_reg[0][...]
        for more in sums_reg[1:]:
            total = total + more[...]
        set_norms(total[0:1] + g1, total[1:2], total[2:3] + b1, total[3:4])
        for i in range(images):
            put = place_matrix(order, i, FIRST, NM, visible[i], PATCH)
            put_grad(i, put, dy1[pl.ds(i * NM, NM), :])
            block_out[0, i] = nn(put, out[pl.ds(i * NM, NM), :]).astype(BF)


def place(groups, ids, visible, order, gains, sums, sums_reg, wqkv, dq, dkv, dy1, x, lat_enc, res, dq_reg, dy1_reg):
    images = groups * GROUP
    n = images * NV
    outs = [struct((1, images, PATCH, D)), struct((1, images, PATCH, D), F32), struct((16, D), F32)]
    scratch = [
        pltpu.VMEM((D, 3 * D), BF), pltpu.VMEM((n, D), BF), pltpu.VMEM((n, D), BF), pltpu.VMEM((n, 2 * D), BF),
        pltpu.VMEM((n, D), F32), pltpu.VMEM((n, D), F32), pltpu.VMEM((n, D), BF),
        pltpu.VMEM((images * NM, D), BF), pltpu.SemaphoreType.DMA((16,)),
    ]
    return pl.pallas_call(
        partial(place_kernel, groups),
        in_specs=[SMEM, SMEM, VMEM, VMEM] + [VMEM] * (3 + groups) + [HBM] * (4 + 5 * groups),
        out_specs=[VMEM] * len(outs),
        out_shape=outs,
        scratch_shapes=scratch,
        compiler_params=params(56),
        cost_estimate=cost(1e6, 1e5),
        name="place",
    )(ids, visible, order, gains, *sums, *sums_reg, wqkv, dq, dkv, dy1, *x, *lat_enc, *res, *dq_reg, *dy1_reg)


BITS = (2, 4, 8)


def hop(value, bit):
    return lax.ppermute(value, "dp", [(i, i ^ bit) for i in range(16)])


def combine_kernel(shape, ids, *refs):
    counts, stacked, stage, rows = shape
    rest = (2,) * max(0, 2 - stage)
    total = sum(counts)
    terms, refs = refs[:total], refs[total:]
    parts, (out, *scratch) = refs[:stacked], refs[stacked:]
    sems = scratch[-1]
    copies = Copies(sems)

    def at(first):
        path = [ids[2 + bit] for bit in range(first, min(stage, 3))]
        return tuple(path + [1 - ids[2 + stage]]) if stage < 3 else tuple(path)

    for ref, own in zip(terms, scratch):
        copies.start(ref.at[at(0)], own)
    for part, (ref, own) in enumerate(zip(parts, scratch[total:])):
        path = at(part + 1)
        copies.start(ref.at[path] if path else ref, own)
    copies.finish()
    spots = [()] if not rest else ([(i,) for i in range(2)] if len(rest) == 1 else [(i, j) for i in range(2) for j in range(2)])
    for spot in spots:
        start = 0
        for j, count in enumerate(counts):
            value = scratch[start][spot].astype(F32) if spot else scratch[start][...].astype(F32)
            for own in scratch[start + 1 : start + count]:
                value = value + (own[spot] if spot else own[...]).astype(F32)
            for own in scratch[total : total + stacked]:
                value = value + own[spot + (j,)].astype(F32)
            start += count
            if stage < 3:
                out[spot + (j,)] = value.astype(BF)
            else:
                out[:, j * D : (j + 1) * D] = value


def combine(ids, pieces, stacked, stage):
    rows = pieces[0][0].shape[-2]
    rest = (2,) * max(0, 2 - stage)
    counts = tuple(len(terms) for terms in pieces)
    if stage < 3:
        out = struct(rest + (len(pieces), rows, D))
    else:
        out = struct((rows, len(pieces) * D), F32)
    scratch = [pltpu.VMEM(rest + (rows, D), BF) for _ in range(sum(counts))]
    scratch += [pltpu.VMEM(rest + (len(pieces), rows, D), BF) for _ in stacked]
    scratch.append(pltpu.SemaphoreType.DMA((len(scratch),)))
    return pl.pallas_call(
        partial(combine_kernel, (counts, len(stacked), stage, rows)),
        in_specs=[SMEM] + [HBM] * (sum(counts) + len(stacked)),
        out_specs=VMEM,
        out_shape=out,
        scratch_shapes=scratch,
        compiler_params=params(32),
        cost_estimate=cost(1e5, 1e4),
        name="combine",
    )(ids, *[term for terms in pieces for term in terms], *stacked)


def halve(terms, bit):
    mine = (lax.axis_index("dp") // bit) % 2

    def half(which):
        return [lax.dynamic_index_in_dim(term, which, 0, keepdims=False) for term in terms]

    return total_of(half(1 - mine)), half(mine)


def total_of(terms):
    total = terms[0].astype(F32)
    for term in terms[1:]:
        total = total + term.astype(F32)
    return total


def in_order(first, then):
    return lax.optimization_barrier((first, then))


def scatter_small(rows, count):
    own = D // count
    flat = jnp.concatenate(
        [
            jnp.moveaxis(rows[:6].reshape(6, count, own), 1, 0).reshape(count, 6 * own),
            rows[6:8].reshape(count, 2 * own),
            rows[8:12].reshape(count, 4 * own),
        ],
        axis=1,
    )
    if count == 16:
        terms = [flat.reshape(2, 2, 2, 2, 12 * own).transpose(3, 2, 1, 0, 4)]
        for bit in (1, 2, 4, 8):
            sent, terms = halve(terms, bit)
            terms = terms + [hop(sent, bit)]
        got = total_of(terms)
    else:
        got = lax.psum_scatter(flat, "dp", scatter_dimension=0, tiled=True)[0]
    return (
        got[: 2 * own].reshape(2, own),
        got[2 * own : 6 * own].reshape(4, own),
        got[6 * own : 8 * own],
        got[8 * own :],
    )


def scatter_natural(block):
    shards = block.reshape(lax.axis_size("dp"), -1, D)
    return lax.psum_scatter(shards, "dp", scatter_dimension=0, tiled=True)[0].astype(F32)


def local(
    patch_rows, cotangent, patch_order, visible, qkv_weight, out_weight, up_weight, down_weight, norm_gains, biases,
    qv_bias, up_bias, target_qkv, target_out, target_up, target_down, target_gains, target_biases, target_qv_bias,
    target_up_bias,
):
    count = lax.axis_size("dp")
    tree = count == 16
    place_dp = lax.axis_index("dp")
    bits = [(place_dp // bit) % 2 for bit in (1,) + BITS]
    ids = jnp.stack([lax.axis_index("section")] + bits).astype(jnp.int32)
    groups = patch_order.shape[0] // GROUP
    weights = (qkv_weight, out_weight, up_weight, down_weight)
    targets = (target_qkv, target_out, target_up, target_down)
    vecs = (norm_gains, biases, qv_bias, up_bias)
    target_vecs = (target_gains, target_biases, target_qv_bias[None], target_up_bias[None])

    encoded = [encode(g, ids, visible, patch_order, *vecs, patch_rows, cotangent, weights) for g in range(groups)]
    lat, x, hq, q, k, v_e, p_e, o_e, y1_e, h2_e, gp_e, a_e = zip(*encoded)
    sent = [lax.ppermute(piece, "section", [(0, 1)]) for piece in lat]
    middles = [
        middle(
            g, ids, visible, patch_order, vecs, target_vecs, patch_rows, cotangent, sent[g], x[g], q[g], k[g],
            weights, targets,
        )
        for g in range(groups)
    ]
    dlat, res, hk_r, dq_r, dkv_r, o_r, dy1b_r, h2_r, du_r, a_r, dy1_r, sums_r, cot_e = zip(*middles)
    back = [lax.ppermute(piece, "section", [(1, 0)]) for piece in dlat]

    send = partial(combine, ids)
    down, dyb, sums_down = down_grad(groups, count, ids, cot_e, back, a_e, a_r, k)
    if tree:
        downs = [[down[0], hop(down[1], 1)]]
        down_x, dyb = in_order(send(downs, [], 0), dyb)
        down_got = [hop(down_x, 2)]
    up, dy1, sums_up = up_grad(
        groups, count, ids, norm_gains, dyb, up_weight, down_weight, y1_e, gp_e, h2_e, du_r, h2_r
    )
    if tree:
        ups = [[up[2 * j], hop(up[2 * j + 1], 1)] for j in range(4)]
        (up_x, down_z), dy1 = in_order((send(ups, [], 0), send(downs, down_got, 1)), dy1)
        up_got = [hop(up_x, 2)]
        down_got = down_got + [hop(down_z, 4)]
    dq, dkv, dy1b = attn_back(groups, ids, dy1, out_weight, q, k, v_e, p_e)
    if tree:
        down_z, dq = in_order(send(downs, down_got, 2), dq)
        down_got = down_got + [hop(down_z, 8)]
    attn, sums_attn = qkv_grad(groups, count, ids, dq, dkv, dy1b, o_e, hq, hk_r, dq_r, dkv_r, o_r, dy1b_r)
    if tree:
        attns = [[attn[2 * j], hop(attn[2 * j + 1], 1)] for j in range(4)]
        qkvs, outs = attns[:3], attns[3:]
        (qkv_x, out_x, up_z, down_sum), dq = in_order(
            (send(qkvs, [], 0), send(outs, [], 0), send(ups, up_got, 1), send(downs, down_got, 3)), dq
        )
        qkv_got, out_got = [hop(qkv_x, 2)], [hop(out_x, 2)]
        up_got = up_got + [hop(up_z, 4)]
    block_out, grad_rows, small = place(
        groups, ids, visible, patch_order, norm_gains, (sums_down, sums_up, sums_attn), sums_r, qkv_weight, dq, dkv,
        dy1, x, lat, res, dq_r, dy1_r,
    )
    if tree:
        up_z, small = in_order(send(ups, up_got, 2), small)
        up_got = up_got + [hop(up_z, 8)]
        qkv_got = qkv_got + [hop(send(qkvs, qkv_got, 1), 4)]
        out_got = out_got + [hop(send(outs, out_got, 1), 4)]
        qkv_got = qkv_got + [hop(send(qkvs, qkv_got, 2), 8)]
        out_got = out_got + [hop(send(outs, out_got, 2), 8)]
        up_sum, qkv_sum, out_sum = send(ups, up_got, 3), send(qkvs, qkv_got, 3), send(outs, out_got, 3)
    else:
        down_sum = scatter_natural(down[0])
        up_sum = jnp.concatenate([scatter_natural(one) for one in up], axis=1)
        qkv_sum = jnp.concatenate([scatter_natural(one) for one in attn[:3]], axis=1)
        out_sum = scatter_natural(attn[3])
    gains, bias_rows, qv_rows, up_rows = scatter_small(small, count)
    return (
        block_out,
        grad_rows,
        qkv_sum[None],
        out_sum[None],
        up_sum[None],
        down_sum[None],
        gains[None],
        bias_rows[None],
        qv_rows[None],
        up_rows[None],
    )


def solution(mesh):
    three, four = P("section", None, None), P("section", "dp", None, None)
    grad = P("section", "dp", None)
    return jax.shard_map(
        local,
        mesh=mesh,
        in_specs=(four, four, P("dp", None), P("dp"), three, three, three, three, three, three,
                  P("section", None), P("section", None), P(), P(), P(), P(), P(), P(), P(), P()),
        out_specs=(four, four, grad, grad, grad, grad, P("section", None, "dp"), P("section", None, "dp"),
                   P("section", "dp"), P("section", "dp")),
        check_vma=False,
    )
```

```python
from functools import partial

import jax
import jax.numpy as jnp
from jax import lax
from jax.experimental import pallas as pl
from jax.experimental.pallas import tpu as pltpu
from jax.sharding import PartitionSpec as P

HEADS = 12
PATCH = 196
D = 768
FF = 3072
EPS = 1e-06
NV = 144
NM = 128
FIRST = PATCH - NM
GROUP = 2
CHUNK = 32

BF = jnp.bfloat16
F32 = jnp.float32
MIB = 1024 * 1024
LIMIT = 62

HBM = pl.BlockSpec(memory_space=pl.ANY)
VMEM = pl.BlockSpec(memory_space=pltpu.VMEM)
SMEM = pl.BlockSpec(memory_space=pltpu.SMEM)


def nn(a, b):
    return jnp.dot(a, b, preferred_element_type=F32)


def nt(a, b):
    return lax.dot_general(a, b, (((1,), (1,)), ((), ())), preferred_element_type=F32)


def tn(a, b):
    return lax.dot_general(a, b, (((0,), (0,)), ((), ())), preferred_element_type=F32)


def loop(count, body, unroll=1):
    def step(i, carry):
        for u in range(unroll):
            body(i * unroll + u)
        return carry

    if count == unroll:
        step(0, 0)
    else:
        lax.fori_loop(0, count // unroll, step, 0)


def unroll_of(count):
    return next(u for u in (4, 3, 2, 1) if count % u == 0)


def rows_of(i, size):
    return pl.ds(pl.multiple_of(i * size, size), size)


def f32_row(ref, row, col=0, width=D):
    return ref[pl.ds(row, 1), pl.ds(col, width)].astype(F32)


class Copies:
    def __init__(self, sems):
        self.sems = sems
        self.used = 0
        self.open = []

    def start(self, src, dst):
        copy = pltpu.make_async_copy(src, dst, self.sems.at[self.used])
        self.used += 1
        copy.start()
        self.open.append(copy)
        return copy

    def wait(self, *copies):
        for copy in copies:
            copy.wait()
            self.open.remove(copy)

    def finish(self):
        self.wait(*list(self.open))

    def take(self, count):
        self.used += count
        return self.used - count

    def begin(self, src, dst, at):
        pltpu.make_async_copy(src, dst, self.sems.at[at]).start()

    def wait_at(self, src, dst, at):
        pltpu.make_async_copy(src, dst, self.sems.at[at]).wait()


def gelu_pair(u):
    size = jnp.abs(u)
    base = 1.0 + (0.3275911 * 0.7071067811865476) * size
    guess = pl.reciprocal(base, approx=True)
    t = guess * (2.0 - base * guess)
    ex = jnp.exp(-0.5 * (u * u))
    poly = 0.5306027145 * t - 0.7265760135
    poly = poly * t + 0.7107068705
    poly = poly * t - 0.142248368
    poly = poly * t + 0.127414796
    tail = poly * t * ex
    phi = jnp.where(u >= 0.0, 1.0 - tail, tail)
    return u * phi, phi + u * (0.3989422804014327 * ex)


def norm_rows(src, dst, rows, gain, shift):
    def body(i):
        sel = rows_of(i, CHUNK)
        x = src[sel, :].astype(F32)
        centered = x - jnp.mean(x, axis=-1, keepdims=True)
        var = jnp.mean(centered * centered, axis=-1, keepdims=True)
        dst[sel, :] = (centered * lax.rsqrt(var + EPS) * gain + shift).astype(BF)

    loop(rows // CHUNK, body, unroll_of(rows // CHUNK))


def norm_back(src, grad, base, write, rows, gain):
    count = rows // CHUNK
    unroll = 3 if count % 3 == 0 else 2

    def step(i, carry):
        for u in range(unroll):
            carry = one(i * unroll + u, carry)
        return carry

    def one(i, carry):
        d_gain, d_shift = carry
        sel = rows_of(i, CHUNK)
        x = src[sel, :].astype(F32)
        dh = grad[sel, :]
        centered = x - jnp.mean(x, axis=-1, keepdims=True)
        var = jnp.mean(centered * centered, axis=-1, keepdims=True)
        rstd = lax.rsqrt(var + EPS)
        hat = centered * rstd
        g = dh * gain
        part = dh * hat
        dx = rstd * (
            g
            - jnp.mean(g, axis=-1, keepdims=True)
            - hat * jnp.mean(g * hat, axis=-1, keepdims=True)
        )
        if base is not None:
            dx = dx + base[sel, :].astype(F32)
        write(sel, dx)
        d_gain = d_gain + jnp.sum(part.reshape(CHUNK // 8, 8, D), axis=0)
        d_shift = d_shift + jnp.sum(dh.reshape(CHUNK // 8, 8, D), axis=0)
        return d_gain, d_shift

    zero = jnp.zeros((8, D), F32)
    d_gain, d_shift = lax.fori_loop(0, count // unroll, step, (zero, zero))
    return jnp.sum(d_gain, axis=0, keepdims=True), jnp.sum(d_shift, axis=0, keepdims=True)


def column_sum(ref, rows, col=0, width=D):
    def step(i, carry):
        x = ref[rows_of(i, CHUNK), pl.ds(col, width)].astype(F32)
        return carry + jnp.sum(x.reshape(CHUNK // 8, 8, width), axis=0)

    total = lax.fori_loop(0, rows // CHUNK, step, jnp.zeros((8, width), F32))
    return jnp.sum(total, axis=0, keepdims=True)


def as_bf16(flags):
    return jnp.where(flags, 1.0, 0.0).astype(BF)


def place_matrix(order, image, start, count, low, high):
    row = order[image, :, pl.ds(start, count)]
    rank = start + lax.broadcasted_iota(jnp.int32, (1, count), 1)
    row = jnp.where((rank >= low) & (rank < high), row, -1)
    return as_bf16(row == lax.broadcasted_iota(jnp.int32, (PATCH, count), 0))


def split_orders(order, split):
    for image in range(split.shape[0]):
        split[image] = order[image : image + 1, :]


def split_pair(pair):
    lane = lax.broadcasted_iota(jnp.int32, pair.shape, 1)
    zero = jnp.zeros_like(pair)
    return jnp.concatenate([jnp.where(lane < 64, pair, zero), jnp.where(lane < 64, zero, pair)], axis=0)


def join_rows(both):
    rows = both.shape[0] // 2
    lane = lax.broadcasted_iota(jnp.int32, (rows, 128), 1)
    return jnp.where(lane < 64, both[:rows], both[rows:])


def join_columns(both):
    rows = both.shape[1] // 2
    return jnp.concatenate([both[:64, :rows], both[64:, rows:]], axis=0).T


PAIRS = HEADS // 2
STEP = 3


def each_pair_group(images, body):
    def group(i):
        image = i // (PAIRS // STEP)
        first = (i % (PAIRS // STEP)) * STEP
        pairs = [first + step for step in range(STEP)]
        body(image, [image * PAIRS + pair for pair in pairs], [pl.ds(pl.multiple_of(pair * 128, 128), 128) for pair in pairs])

    loop(images * (PAIRS // STEP), group)


def softmax(scores, axis):
    ex = jnp.exp(scores - jnp.max(scores, axis=axis, keepdims=True))
    return (ex * (1.0 / jnp.sum(ex, axis=axis, keepdims=True))).astype(BF)


def score_back(probs, d_probs, axis):
    wide = probs.astype(F32)
    return (wide * (d_probs - jnp.sum(d_probs * wide, axis=axis, keepdims=True))).astype(BF)


def attention_by_rows(images, n, q, k, v, p, o, count_of):
    def body(image, slots, lanes):
        sel = rows_of(image, n)
        ok = lax.broadcasted_iota(jnp.int32, (1, n), 1) < count_of(image)
        scores = [nt(split_pair(q[sel, at]), k[sel, at]) for at in lanes]
        probs = [softmax(jnp.where(ok, one, -1000000000.0), 1) for one in scores]
        for slot, one in zip(slots, probs):
            p[slot] = one
        mixed = [nn(one, v[sel, at]) for one, at in zip(probs, lanes)]
        for at, one in zip(lanes, mixed):
            o[sel, at] = join_rows(one).astype(BF)

    each_pair_group(images, body)


def attention_by_columns(images, nk, q, k, v, p, o, key_ok):
    def body(image, slots, lanes):
        qs, ks = rows_of(image, NM), rows_of(image, nk)
        ok = key_ok(image)
        scores = [nt(k[ks, at], split_pair(q[qs, at])) for at in lanes]
        probs = [softmax(jnp.where(ok, one, -1000000000.0), 0) for one in scores]
        if p is not None:
            for slot, one in zip(slots, probs):
                p[slot] = one
        mixed = [tn(v[ks, at], one) for one, at in zip(probs, lanes)]
        for at, one in zip(lanes, mixed):
            o[qs, at] = join_columns(one).astype(BF)

    each_pair_group(images, body)


def attention_back_rows(images, n, q, k, v, p, do, dq, dkv):
    def body(image, slots, lanes):
        sel = rows_of(image, n)
        d_mixed = [split_pair(do[sel, at]) for at in lanes]
        d_probs = [nt(one, v[sel, at]) for one, at in zip(d_mixed, lanes)]
        d_scores = [score_back(p[slot], one, 1) for slot, one in zip(slots, d_probs)]
        d_values = [tn(p[slot], one) for slot, one in zip(slots, d_mixed)]
        d_query = [nn(one, k[sel, at]) for one, at in zip(d_scores, lanes)]
        d_keys = [tn(one, split_pair(q[sel, at])) for one, at in zip(d_scores, lanes)]
        for at, value, query, key in zip(lanes, d_values, d_query, d_keys):
            dq[sel, at] = (join_rows(query) * 0.125).astype(BF)
            dkv[sel, at] = key.astype(BF)
            dkv[sel, pl.ds(pl.multiple_of(D + at.start, 128), 128)] = value.astype(BF)

    each_pair_group(images, body)


def attention_back_columns(images, nk, q, k, v, p, do, dq, dkv):
    def body(image, slots, lanes):
        qs, ks = rows_of(image, NM), rows_of(image, nk)
        d_mixed = [split_pair(do[qs, at]) for at in lanes]
        d_probs = [nt(v[ks, at], one) for one, at in zip(d_mixed, lanes)]
        d_scores = [score_back(p[slot], one, 0) for slot, one in zip(slots, d_probs)]
        d_values = [nn(p[slot], one) for slot, one in zip(slots, d_mixed)]
        d_query = [tn(k[ks, at], one) for one, at in zip(d_scores, lanes)]
        d_keys = [nn(one, split_pair(q[qs, at])) for one, at in zip(d_scores, lanes)]
        for at, value, query, key in zip(lanes, d_values, d_query, d_keys):
            dq[qs, at] = (join_columns(query) * 0.125).astype(BF)
            dkv[ks, at] = key.astype(BF)
            dkv[ks, pl.ds(pl.multiple_of(D + at.start, 128), 128)] = value.astype(BF)

    each_pair_group(images, body)


HALF = 512


def mlp_forward(rows, h2, w1, w2, up_b, u, a, gp, acc, out, base):
    acc[...] = base()

    def body(i):
        cols = [pl.ds(pl.multiple_of((2 * i + part) * HALF, HALF), HALF) for part in range(2)]
        for part in range(2):
            u[part] = nn(h2[...], w1[:, cols[part]])
        for part in range(2):
            for c in range(0, HALF, 256):
                at = pl.ds(pl.multiple_of((2 * i + part) * HALF + c, 256), 256)
                shift = up_b[0:1, at].astype(F32)
                for r in range(0, rows, CHUNK):
                    value, slope = gelu_pair(u[part, r : r + CHUNK, c : c + 256] + shift)
                    a[r : r + CHUNK, at] = value.astype(BF)
                    if gp is not None:
                        gp[r : r + CHUNK, at] = slope.astype(BF)
            acc[...] += nn(a[:, cols[part]], w2[cols[part], :])

    loop(FF // (2 * HALF), body)
    out[...] = acc[...].astype(BF)


def mlp_back(rows, dyb, gp, w1, w2, du, u, acc):
    acc[...] = jnp.zeros_like(acc)

    def body(i):
        cols = [pl.ds(pl.multiple_of((2 * i + part) * HALF, HALF), HALF) for part in range(2)]
        for part in range(2):
            u[part] = nt(dyb[...], w2[cols[part], :])
        for part in range(2):
            for r in range(0, rows, CHUNK):
                sel = slice(r, r + CHUNK)
                du[sel, cols[part]] = (gp[sel, cols[part]].astype(F32) * u[part, sel, :]).astype(BF)
            acc[...] += nt(du[:, cols[part]], w1[:, cols[part]])

    loop(FF // (2 * HALF), body)


def project(count, rows, left, weight, first, write):
    def body(j):
        write(j, nn(left[...], weight[:, pl.ds(pl.multiple_of((first + j) * D, D), D)]))

    loop(count, body)


def set_biases(ref, bias):
    ref[0] = f32_row(bias, 0)
    ref[1] = jnp.zeros((1, D), F32)
    ref[2] = f32_row(bias, 0, D)


def cost(flops, nbytes):
    return pl.CostEstimate(flops=int(flops), bytes_accessed=int(nbytes), transcendentals=0)


def params(mib):
    return pltpu.CompilerParams(vmem_limit_bytes=mib * MIB)


def struct(shape, dtype=BF):
    return jax.ShapeDtypeStruct(shape, dtype)


def start_weights(copies, sources, scratch):
    return [copies.start(src, dst) for src, dst in zip(sources, scratch)]


def encode_kernel(group, ids, visible, order_in, gains, biases, qvb, upb, rows, cot, wqkv, wo, w1, w2,
                  lat_out, x_out, hq_out, q_out, k_out, v_out, p_out, o_out, y1_out, h2_out, gp_out, a_out,
                  order, rows_v, cot_v, sqkv, so, s1, s2, x, hq, qkv, p, o, y1, h2, gp, a, u, acc, shifts, lat, sems):
    n = GROUP * NV
    split_orders(order_in, order)

    @pl.when(ids[0] == 0)
    def _():
        copies = Copies(sems)
        got_rows = copies.start(rows.at[0, pl.ds(group * GROUP, GROUP)], rows_v)
        got_qkv, got_o, got_1, got_2 = start_weights(
            copies, (wqkv.at[0], wo.at[0], w1.at[0], w2.at[0]), (sqkv, so, s1, s2)
        )
        gain, bias = gains.at[0], biases.at[0]
        copies.wait(got_rows)

        def pick_rows(i):
            image = group * GROUP + i
            pick = place_matrix(order, image, 0, NV, 0, visible[image])
            x[rows_of(i, NV), :] = tn(pick, rows_v[i]).astype(BF)

        loop(GROUP, pick_rows)
        copies.start(x, x_out)
        norm_rows(x, hq, n, f32_row(gain, 0), f32_row(bias, 0))
        copies.start(hq, hq_out)
        copies.wait(got_qkv)
        set_biases(shifts, qvb)

        def keep(j, value):
            scale = jnp.where(j == 0, 0.125, 1.0)
            qkv[j] = ((value + shifts[j]).astype(BF).astype(F32) * scale).astype(BF)

        project(3, n, hq, sqkv, 0, keep)
        q, k, v = qkv.at[0], qkv.at[1], qkv.at[2]
        copies.start(q, q_out)
        copies.start(k, k_out)
        copies.start(v, v_out)

        attention_by_rows(GROUP, NV, q, k, v, p, o, lambda i: visible[group * GROUP + i])
        copies.start(p, p_out)
        copies.start(o, o_out)
        copies.wait(got_o)
        y1[...] = nn(o[...], so[...]) + f32_row(bias, 1) + x[...].astype(F32)
        copies.start(y1, y1_out)
        norm_rows(y1, h2, n, f32_row(gain, 1), f32_row(bias, 2))
        copies.start(h2, h2_out)
        copies.wait(got_1, got_2)
        mlp_forward(n, h2, s1, s2, upb, u, a, gp, acc, lat, lambda: y1[...] + f32_row(bias, 3))
        copies.start(gp, gp_out)
        copies.start(a, a_out)
        copies.start(lat, lat_out)
        copies.finish()

    @pl.when(ids[0] == 1)
    def _():
        m = GROUP * NM
        top = pl.ds(0, m)
        q, k = qkv.at[0], qkv.at[1]
        copies = Copies(sems)
        got_rows = copies.start(rows.at[0, pl.ds(group * GROUP, GROUP)], rows_v)
        got_cot = copies.start(cot.at[0, pl.ds(group * GROUP, GROUP)], cot_v)
        got_q = copies.start(wqkv.at[0, :, pl.ds(0, D)], so)
        gain, bias = gains.at[0], biases.at[0]
        copies.wait(got_rows, got_cot)

        def pick_rows(i):
            image = group * GROUP + i
            pick = place_matrix(order, image, FIRST, NM, visible[image], PATCH)
            x[rows_of(i, NM), :] = tn(pick, rows_v[i]).astype(BF)
            k[rows_of(i, NM), :] = tn(pick, cot_v[i]).astype(BF)

        loop(GROUP, pick_rows)
        copies.start(x.at[top], x_out.at[top])
        copies.start(k.at[top], k_out.at[top])
        norm_rows(x, hq, m, f32_row(gain, 0), f32_row(bias, 0))
        copies.start(hq.at[top], hq_out.at[top])
        copies.wait(got_q)
        q[top, :] = ((nn(hq[top, :], so[...]) + f32_row(qvb, 0)).astype(BF) * 0.125).astype(BF)
        copies.start(q.at[top], q_out.at[top])
        copies.finish()


def encode(group, ids, visible, order, gains, biases, qvb, upb, rows, cot, weights):
    n = GROUP * NV
    row, wide = struct((n, D)), struct((n, FF))
    heads = struct((GROUP * PAIRS, 2 * NV, NV))
    outs = [row] * 6 + [heads, row, struct((n, D), F32), row, wide, wide]
    vm = lambda s: pltpu.VMEM(s.shape, s.dtype)
    scratch = [
        pltpu.VMEM((order.shape[0], 1, PATCH), jnp.int32),
        pltpu.VMEM((GROUP, PATCH, D), BF), pltpu.VMEM((GROUP, PATCH, D), BF),
        pltpu.VMEM((D, 3 * D), BF), pltpu.VMEM((D, D), BF), pltpu.VMEM((D, FF), BF), pltpu.VMEM((FF, D), BF),
        vm(row), vm(row), pltpu.VMEM((3, n, D), BF), vm(heads), vm(row), pltpu.VMEM((n, D), F32), vm(row),
        vm(wide), vm(wide), pltpu.VMEM((2, n, HALF), F32), pltpu.VMEM((n, D), F32), pltpu.VMEM((3, 1, D), F32), vm(row),
        pltpu.SemaphoreType.DMA((20,)),
    ]
    return pl.pallas_call(
        partial(encode_kernel, group),
        in_specs=[SMEM, SMEM] + [VMEM] * 5 + [HBM] * 6,
        out_specs=[HBM] * len(outs),
        out_shape=outs,
        scratch_shapes=scratch,
        compiler_params=params(LIMIT),
        cost_estimate=cost(2 * n * 12 * D * D, 25e6),
        name="encode",
    )(ids, visible, order, gains, biases, qvb, upb, rows, cot, *weights)


def middle_kernel(group, ids, visible, order_in, gains, biases, qvb, upb, tgains, tbiases, tqvb, tupb,
                  rows, cot, lat_in, x_in, q_in, dyb_in, wqkv, wo, w1, w2, tqkv, to, t1, t2,
                  dlat_out, res_out, hk_out, dq_out, dkv_out, o_out, dy1b_out, h2_out, du_out, a_out,
                  dy1_out, sums_out, cot_out,
                  order, rows_v, cot_v, sqkv, so, s1, s2, x, lat, hq, hk, q, kv, p, o, y1, h2, gp, a, u, acc, shifts,
                  res, dyb, du, dy1, dy1b, do, dq, dkv, dh, dlat, sums, sems):
    n, m = GROUP * NM, GROUP * NV
    top = pl.ds(0, n)
    k, v = kv.at[0], kv.at[1]
    split_orders(order_in, order)

    def forward(copies, got_weights, gain, bias, ub, nk, key_ok, keep_p, keep_slope):
        got_o, got_1, got_2 = got_weights
        attention_by_columns(GROUP, nk, q, k, v, keep_p, o, key_ok)
        copies.wait(got_o)
        y1[...] = nn(o[...], so[...]) + f32_row(bias, 1) + x[...].astype(F32)
        norm_rows(y1, h2, n, f32_row(gain, 1), f32_row(bias, 2))
        copies.wait(got_1, got_2)
        mlp_forward(n, h2, s1, s2, ub, u, a, keep_slope, acc, res, lambda: y1[...] + f32_row(bias, 3))
        copies.start(res, res_out)

    @pl.when(ids[0] == 0)
    def _():
        copies = Copies(sems)
        gain, bias = tgains, tbiases
        got_rows = copies.start(rows.at[0, pl.ds(group * GROUP, GROUP)], rows_v)
        got_qkv = copies.start(tqkv, sqkv)
        got_weights = start_weights(copies, (to, t1, t2), (so, s1, s2))
        got_cot = copies.start(cot.at[0, pl.ds(group * GROUP, GROUP)], cot_v)
        copies.wait(got_rows)

        def pick_rows(i):
            image = group * GROUP + i
            pick = place_matrix(order, image, FIRST, NM, visible[image], PATCH)
            x[rows_of(i, NM), :] = tn(pick, rows_v[i]).astype(BF)

        loop(GROUP, pick_rows)
        norm_rows(x, hq, n, f32_row(gain, 0), f32_row(bias, 0))
        copies.wait(got_qkv)
        set_biases(shifts, tqvb)
        q[...] = ((nn(hq[...], sqkv[:, :D]) + f32_row(tqvb, 0)).astype(BF) * 0.125).astype(BF)

        def keep_kv(j, value):
            kv[j, top, :] = (value + shifts[j + 1]).astype(BF)

        project(2, n, hq, sqkv, 1, keep_kv)

        def key_ok(i):
            return lax.broadcasted_iota(jnp.int32, (NM, 1), 0) + FIRST >= visible[group * GROUP + i]

        forward(copies, got_weights, gain, bias, tupb, NM, key_ok, None, None)
        copies.wait(got_cot)

        def pick_cot(i):
            image = group * GROUP + i
            pick = place_matrix(order, image, 0, NV, 0, visible[image])
            lat[rows_of(i, NV), :] = tn(pick, cot_v[i]).astype(BF)

        loop(GROUP, pick_cot)
        copies.start(lat, cot_out)
        copies.finish()

    @pl.when(ids[0] == 1)
    def _():
        copies = Copies(sems)
        gain, bias = gains.at[0], biases.at[0]
        got_lat = copies.start(lat_in, lat)
        got_kv = copies.start(wqkv.at[0, :, pl.ds(D, 2 * D)], sqkv.at[:, pl.ds(D, 2 * D)])
        got_q = copies.start(q_in.at[top], q)
        got_x = copies.start(x_in.at[top], x)
        got_weights = start_weights(copies, (wo.at[0], w1.at[0], w2.at[0]), (so, s1, s2))
        got_dyb = copies.start(dyb_in.at[top], dyb)
        copies.wait(got_lat)
        norm_rows(lat, hk, m, f32_row(gain, 0), f32_row(bias, 0))
        copies.start(hk, hk_out)
        copies.wait(got_kv)
        set_biases(shifts, qvb)

        def keep_kv(j, value):
            kv[j] = (value + shifts[j + 1]).astype(BF)

        project(2, m, hk, sqkv, 1, keep_kv)
        copies.wait(got_q, got_x)

        def key_ok(i):
            return lax.broadcasted_iota(jnp.int32, (NV, 1), 0) < visible[group * GROUP + i]

        forward(copies, got_weights, gain, bias, upb.at[0:1], NV, key_ok, p, gp)
        copies.start(o, o_out)
        copies.start(h2, h2_out)
        copies.start(a, a_out)
        copies.wait(got_dyb)
        mlp_back(n, dyb, gp, s1, s2, du, u, acc)
        copies.start(du, du_out)

        def keep(sel, dx):
            dy1[sel, :] = dx
            dy1b[sel, :] = dx.astype(BF)

        g2, b2 = norm_back(y1, acc, dyb, keep, n, f32_row(gain, 1))
        copies.start(dy1, dy1_out)
        copies.start(dy1b, dy1b_out)
        do[...] = nt(dy1b[...], so[...]).astype(BF)
        attention_back_columns(GROUP, NV, q, k, v, p, do, dq, dkv)
        copies.start(dq, dq_out)
        copies.start(dkv, dkv_out)
        dh[...] = nt(dkv[:, :D], sqkv[:, D : 2 * D])
        dh[...] += nt(dkv[:, D:], sqkv[:, 2 * D :])

        def keep_side(sel, dx):
            dlat[sel, :] = dx.astype(BF)

        gk, bk = norm_back(lat, dh, None, keep_side, m, f32_row(gain, 0))
        copies.start(dlat, dlat_out)
        for row, value in enumerate((gk, g2, bk, b2)):
            sums[pl.ds(row, 1), :] = value
        copies.start(sums, sums_out)
        copies.finish()


def middle(group, ids, visible, order, own_vecs, target_vecs, rows, cot, lat, x, q, dyb, weights, targets):
    n, m = GROUP * NM, GROUP * NV
    row, side, wide = struct((n, D)), struct((m, D)), struct((n, FF))
    pair = struct((m, 2 * D))
    outs = [side, row, side, row, pair, row, row, row, wide, wide, struct((n, D), F32), struct((8, D), F32), side]
    vm = lambda s: pltpu.VMEM(s.shape, s.dtype)
    full, fside = pltpu.VMEM((n, D), F32), pltpu.VMEM((m, D), F32)
    scratch = [
        pltpu.VMEM((order.shape[0], 1, PATCH), jnp.int32),
        pltpu.VMEM((GROUP, PATCH, D), BF), pltpu.VMEM((GROUP, PATCH, D), BF),
        pltpu.VMEM((D, 3 * D), BF), pltpu.VMEM((D, D), BF), pltpu.VMEM((D, FF), BF), pltpu.VMEM((FF, D), BF),
        vm(row), vm(side), vm(row), vm(side), vm(row), pltpu.VMEM((2, m, D), BF),
        pltpu.VMEM((GROUP * PAIRS, NV, 2 * NM), BF), vm(row), full, vm(row), vm(wide), vm(wide),
        pltpu.VMEM((2, n, HALF), F32), full, pltpu.VMEM((3, 1, D), F32),
        vm(row), vm(row), vm(wide), full, vm(row), vm(row), vm(row), vm(pair), fside, vm(side),
        pltpu.VMEM((8, D), F32),
        pltpu.SemaphoreType.DMA((24,)),
    ]
    return pl.pallas_call(
        partial(middle_kernel, group),
        in_specs=[SMEM, SMEM] + [VMEM] * 9 + [HBM] * 14,
        out_specs=[HBM] * len(outs),
        out_shape=outs,
        scratch_shapes=scratch,
        compiler_params=params(LIMIT),
        cost_estimate=cost(4 * n * 12 * D * D, 25e6),
        name="middle",
    )(ids, visible, order, *own_vecs, *target_vecs, rows, cot, lat, x, q, dyb, *weights, *targets)


def stack_rows(copies, pieces, ref, size):
    return [copies.start(piece, ref.at[pl.ds(i * size, size)]) for i, piece in enumerate(pieces)]


def clear_tail(ref, used):
    ref[pl.ds(used, ref.shape[0] - used), :] = jnp.zeros((ref.shape[0] - used, ref.shape[1]), ref.dtype)


def halves(count):
    return [struct((2, 2, 2, D // 16, D))] * 2 if count == 16 else [struct((D, D))]


def give_blocks(copies, core, tree, left_right, out, dest):
    size = 8 if tree else 1
    first = copies.take(4 * size)

    def send(j, act):
        view = out.at[j].reshape(2, 2, 2, 2, D // 16, D)
        if not tree:
            act(out.at[j], dest[j], first + j)
            return
        for x in range(2):
            for low in range(2):
                at = first + j * size + 4 * x + 2 * low
                act(view.at[:, low, x, core], dest[2 * j].at[x, low], at)
                act(view.at[:, low, x, 1 - core], dest[2 * j + 1].at[x, low], at + 1)

    left_right(send, copies.begin)
    for j in range(4):
        send(j, copies.wait_at)


def give_rows(copies, core, tree, multiply, out, dest):
    size = 4 if tree else 1
    first = copies.take(4 * size)

    def send(j, act):
        if not tree:
            act(out.at[j], dest[0].at[pl.ds(pl.multiple_of(j * D, D), D)], first + j)
            return
        view = out.at[j].reshape(2, 2, D // 4, D)
        low, high = lax.rem(j, 2), lax.div(j, 2)
        for x in range(2):
            at = first + j * size + 2 * x
            act(view.at[x, core], dest[0].at[x, low, high], at)
            act(view.at[x, 1 - core], dest[1].at[x, low, high], at + 1)

    def body(j):
        out[j] = multiply(j)
        send(j, copies.begin)

    loop(4, body)
    loop(4, lambda j: send(j, copies.wait_at))


def down_kernel(groups, parts, ids, *refs):
    cot, lat, a_enc, a_reg, dyb_reg = (refs[i * groups : (i + 1) * groups] for i in range(5))
    refs = refs[5 * groups :]
    dest, refs = refs[:parts], refs[parts:]
    dyb_out, sums_out, cot_v, dyb, a, dlat, out, sums, sems = refs
    images = groups * GROUP
    nv, nm = GROUP * NV, GROUP * NM

    @pl.when(ids[0] == 0)
    def _():
        copies = Copies(sems)
        got = stack_rows(copies, cot, cot_v, nv) + stack_rows(copies, lat, dlat, nv)
        stack_rows(copies, a_enc, a, nv)
        copies.wait(*got)
        dyb[...] = (cot_v[...].astype(F32) + dlat[...].astype(F32)).astype(BF)
        copies.start(dyb, dyb_out)
        copies.finish()

    @pl.when(ids[0] == 1)
    def _():
        copies = Copies(sems)
        stack_rows(copies, a_reg, a, nm)
        stack_rows(copies, [piece.at[pl.ds(0, nm)] for piece in dyb_reg], dyb, nm)
        clear_tail(a, images * NM)
        clear_tail(dyb, images * NM)
        copies.finish()

    copies = Copies(sems)

    def multiply(j):
        return tn(a[:, pl.ds(pl.multiple_of(j * D, D), D)], dyb[...]).astype(BF)

    give_rows(copies, ids[1], parts == 2, multiply, out, dest)
    sums[...] = jnp.broadcast_to(column_sum(dyb, images * NV), (8, D))
    copies.start(sums, sums_out)
    copies.finish()


def down_grad(groups, count, ids, cot, dlat, a_enc, a_reg, dyb_reg):
    n = groups * GROUP * NV
    main = [struct((2, 2, 2, D // 4, D))] * 2 if count == 16 else [struct((FF, D))]
    outs = main + [struct((n, D)), struct((8, D), F32)]
    row = pltpu.VMEM((n, D), BF)
    scratch = [
        row, row, pltpu.VMEM((n, FF), BF), row, pltpu.VMEM((4, D, D), BF), pltpu.VMEM((8, D), F32),
        pltpu.SemaphoreType.DMA((24,)),
    ]
    got = pl.pallas_call(
        partial(down_kernel, groups, len(main)),
        in_specs=[SMEM] + [HBM] * (5 * groups),
        out_specs=[HBM] * len(outs),
        out_shape=outs,
        scratch_shapes=scratch,
        compiler_params=params(LIMIT),
        cost_estimate=cost(1e6, 1e5),
        name="down_grad",
    )(ids, *cot, *dlat, *a_enc, *a_reg, *dyb_reg)
    return got[: len(main)], got[-2], got[-1]


def up_kernel(groups, parts, ids, gains, dyb_in, w1, w2, *refs):
    y1_enc, gp_enc, h2_enc, du_reg, h2_reg = (refs[i * groups : (i + 1) * groups] for i in range(5))
    refs = refs[5 * groups :]
    dest, refs = refs[:parts], refs[parts:]
    dy1_out, sums_out, s1, s2, dyb, gp, y1, h2, du, u, acc, dy1, out, sums, sems = refs
    images = groups * GROUP
    nv, nm = GROUP * NV, GROUP * NM

    @pl.when(ids[0] == 0)
    def _():
        copies = Copies(sems)
        got = [copies.start(dyb_in, dyb), copies.start(w2.at[0], s2)]
        got += stack_rows(copies, gp_enc, gp, nv)
        got.append(copies.start(w1.at[0], s1))
        got_y = stack_rows(copies, y1_enc, y1, nv)
        stack_rows(copies, h2_enc, h2, nv)
        copies.wait(*got)
        mlp_back(images * NV, dyb, gp, s1, s2, du, u, acc)
        copies.wait(*got_y)

        def keep(sel, dx):
            dy1[sel, :] = dx

        g2, b2 = norm_back(y1, acc, dyb, keep, images * NV, f32_row(gains.at[0], 1))
        copies.start(dy1, dy1_out)
        sums[pl.ds(0, 1), :] = g2
        sums[pl.ds(1, 1), :] = b2
        copies.finish()

    @pl.when(ids[0] == 1)
    def _():
        copies = Copies(sems)
        stack_rows(copies, du_reg, du, nm)
        stack_rows(copies, h2_reg, h2, nm)
        clear_tail(du, images * NM)
        clear_tail(h2, images * NM)
        sums[pl.ds(0, 2), :] = jnp.zeros((2, D), F32)
        copies.finish()

    copies = Copies(sems)

    def multiply(send, act):
        def body(j):
            cols = pl.ds(pl.multiple_of(j * D, D), D)
            out[j] = tn(h2[...], du[:, cols]).astype(BF)
            for block in range(4):
                pl.when(j == block)(lambda block=block: send(block, act))
            sums[pl.ds(4 + j, 1), :] = column_sum(du, images * NV, pl.multiple_of(j * D, D))

        loop(4, body)

    give_blocks(copies, ids[1], parts == 8, multiply, out, dest)
    copies.start(sums, sums_out)
    copies.finish()


def up_grad(groups, count, ids, gains, dyb, w1, w2, y1_enc, gp_enc, h2_enc, du_reg, h2_reg):
    n = groups * GROUP * NV
    main = halves(count) * 4
    outs = main + [struct((n, D), F32), struct((8, D), F32)]
    scratch = [
        pltpu.VMEM((D, FF), BF), pltpu.VMEM((FF, D), BF), pltpu.VMEM((n, D), BF), pltpu.VMEM((n, FF), BF),
        pltpu.VMEM((n, D), F32), pltpu.VMEM((n, D), BF), pltpu.VMEM((n, FF), BF), pltpu.VMEM((2, n, HALF), F32),
        pltpu.VMEM((n, D), F32), pltpu.VMEM((n, D), F32), pltpu.VMEM((4, D, D), BF), pltpu.VMEM((8, D), F32),
        pltpu.SemaphoreType.DMA((36,)),
    ]
    got = pl.pallas_call(
        partial(up_kernel, groups, len(main)),
        in_specs=[SMEM, VMEM] + [HBM] * (3 + 5 * groups),
        out_specs=[HBM] * len(outs),
        out_shape=outs,
        scratch_shapes=scratch,
        compiler_params=params(LIMIT),
        cost_estimate=cost(1e6, 1e5),
        name="up_grad",
    )(ids, gains, dyb, w1, w2, *y1_enc, *gp_enc, *h2_enc, *du_reg, *h2_reg)
    return got[: len(main)], got[-2], got[-1]


def attn_kernel(groups, ids, dy1_in, wo, *refs):
    q_enc, k_enc, v_enc, p_enc = (refs[i * groups : (i + 1) * groups] for i in range(4))
    dq_out, dkv_out, dy1b_out, so, dy1, dy1b, q, k, v, p, do, dq, dkv, sems = refs[4 * groups :]
    images = groups * GROUP
    nv = GROUP * NV

    @pl.when(ids[0] == 0)
    def _():
        copies = Copies(sems)
        got = [copies.start(dy1_in, dy1), copies.start(wo.at[0], so)]
        for piece, ref in ((v_enc, v), (k_enc, k), (q_enc, q)):
            got += stack_rows(copies, piece, ref, nv)
        got += stack_rows(copies, p_enc, p, GROUP * PAIRS)
        copies.wait(*got[:2])
        dy1b[...] = dy1[...].astype(BF)
        copies.start(dy1b, dy1b_out)
        do[...] = nt(dy1b[...], so[...]).astype(BF)
        copies.wait(*got[2:])
        attention_back_rows(images, NV, q, k, v, p, do, dq, dkv)
        copies.start(dq, dq_out)
        copies.start(dkv, dkv_out)
        copies.finish()


def attn_back(groups, ids, dy1, wo, *pieces):
    n = groups * GROUP * NV
    row = pltpu.VMEM((n, D), BF)
    outs = [struct((n, D)), struct((n, 2 * D)), struct((n, D))]
    scratch = [
        pltpu.VMEM((D, D), BF), pltpu.VMEM((n, D), F32), row, row, row, row,
        pltpu.VMEM((groups * GROUP * PAIRS, 2 * NV, NV), BF), row, row, pltpu.VMEM((n, 2 * D), BF),
        pltpu.SemaphoreType.DMA((16,)),
    ]
    return pl.pallas_call(
        partial(attn_kernel, groups),
        in_specs=[SMEM] + [HBM] * (2 + 4 * groups),
        out_specs=[HBM] * len(outs),
        out_shape=outs,
        scratch_shapes=scratch,
        compiler_params=params(LIMIT),
        cost_estimate=cost(1e6, 1e5),
        name="attn_back",
    )(ids, dy1, wo, *[ref for piece in pieces for ref in piece])


def qkv_kernel(groups, parts, ids, dq_enc, dkv_enc, dy1b_enc, *refs):
    pieces = [refs[i * groups : (i + 1) * groups] for i in range(7)]
    o_enc, hq_in, hk_reg, dq_reg, dkv_reg, o_reg, dy1b_reg = pieces
    refs = refs[7 * groups :]
    dest, refs = refs[:parts], refs[parts:]
    sums_out, left, right, out, sums, sems = refs
    images = groups * GROUP
    nv, nm = GROUP * NV, GROUP * NM
    hk, hq, o = (left.at[i] for i in range(3))
    dk, dv, dq, dy1b = (right.at[i] for i in range(4))

    @pl.when(ids[0] == 0)
    def _():
        copies = Copies(sems)
        copies.start(dq_enc, dq)
        stack_rows(copies, hq_in, hq, nv)
        stack_rows(copies, hq_in, hk, nv)
        copies.start(dkv_enc.at[:, pl.ds(0, D)], dk)
        copies.start(dkv_enc.at[:, pl.ds(D, D)], dv)
        copies.start(dy1b_enc, dy1b)
        stack_rows(copies, o_enc, o, nv)
        copies.finish()

    @pl.when(ids[0] == 1)
    def _():
        copies = Copies(sems)
        for piece, ref in ((hq_in, hq), (dq_reg, dq), (o_reg, o), (dy1b_reg, dy1b)):
            stack_rows(copies, [one.at[pl.ds(0, nm)] for one in piece], ref, nm)
            clear_tail(ref, images * NM)
        stack_rows(copies, hk_reg, hk, nv)
        stack_rows(copies, [one.at[:, pl.ds(0, D)] for one in dkv_reg], dk, nv)
        stack_rows(copies, [one.at[:, pl.ds(D, D)] for one in dkv_reg], dv, nv)
        copies.finish()

    copies = Copies(sems)

    def multiply(send, act):
        def body(j):
            out[j] = tn(left[jnp.maximum(j - 1, 0)], right[j]).astype(BF)
            for block in range(4):
                pl.when(j == block)(lambda block=block: send(block, act))

        loop(4, body)

    give_blocks(copies, ids[1], parts == 8, multiply, out, dest)
    for row, value in enumerate((
        column_sum(right.at[3], images * NV), column_sum(right.at[2], images * NV), column_sum(right.at[1], images * NV)
    )):
        sums[pl.ds(row, 1), :] = value
    copies.start(sums, sums_out)
    copies.finish()


def qkv_grad(groups, count, ids, dq, dkv, dy1b, *pieces):
    n = groups * GROUP * NV
    row = pltpu.VMEM((n, D), BF)
    main = halves(count) * 4
    outs = main + [struct((8, D), F32)]
    scratch = [
        pltpu.VMEM((3, n, D), BF), pltpu.VMEM((4, n, D), BF), pltpu.VMEM((4, D, D), BF), pltpu.VMEM((8, D), F32),
        pltpu.SemaphoreType.DMA((40,)),
    ]
    got = pl.pallas_call(
        partial(qkv_kernel, groups, len(main)),
        in_specs=[SMEM] + [HBM] * (3 + 7 * groups),
        out_specs=[HBM] * len(outs),
        out_shape=outs,
        scratch_shapes=scratch,
        compiler_params=params(LIMIT),
        cost_estimate=cost(1e6, 1e5),
        name="qkv_grad",
    )(ids, dq, dkv, dy1b, *[ref for piece in pieces for ref in piece])
    return got[: len(main)], got[-1]


def place_kernel(groups, ids, visible, order_in, gains, down_sums, up_sums, attn_sums, *refs):
    sums_reg, (wqkv, dq_in, dkv_in, dy1_in), refs = refs[:groups], refs[groups : groups + 4], refs[groups + 4 :]
    x_in, lat_enc, res, dq_reg, dy1_reg = (refs[i * groups : (i + 1) * groups] for i in range(5))
    block_out, grad_out, small, order, sqkv, x, dq, dkv, dh, dy1, lat, out, sems = refs[5 * groups :]
    images = groups * GROUP
    nv, nm = GROUP * NV, GROUP * NM

    split_orders(order_in, order)

    def put_grad(i, put, value):
        high = value.astype(BF)
        low = (value - high.astype(F32)).astype(BF)
        grad_out[0, i] = nn(put, high) + nn(put, low)

    def set_norms(g1, g2, b1, b2):
        for row, value in ((0, g1), (1, g2), (2, b1), (4, b2)):
            small[pl.ds(row, 1), :] = value

    small[pl.ds(3, 1), :] = attn_sums[0:1, :]
    small[pl.ds(5, 1), :] = down_sums[0:1, :]
    small[pl.ds(6, 2), :] = attn_sums[1:3, :]
    small[pl.ds(8, 4), :] = up_sums[4:8, :]
    small[pl.ds(12, 4), :] = jnp.zeros((4, D), F32)

    @pl.when(ids[0] == 0)
    def _():
        copies = Copies(sems)
        got = [copies.start(dkv_in, dkv), copies.start(wqkv.at[0], sqkv), copies.start(dq_in, dq)]
        got += [copies.start(dy1_in, dy1)] + stack_rows(copies, x_in, x, nv)
        got_out = stack_rows(copies, lat_enc, lat, nv) + stack_rows(copies, res, out, nm)
        copies.wait(*got)
        dh[...] = nt(dq[...], sqkv[:, 0:D])
        for j in range(2):
            dh[...] += nt(dkv[:, j * D : (j + 1) * D], sqkv[:, (j + 1) * D : (j + 2) * D])

        def keep(sel, dx):
            dy1[sel, :] = dx

        g1, b1 = norm_back(x, dh, dy1, keep, images * NV, f32_row(gains.at[0], 0))
        set_norms(g1, up_sums[0:1, :], b1, up_sums[1:2, :])
        copies.wait(*got_out)

        def put_image(i):
            put = place_matrix(order, i, 0, NV, 0, visible[i])
            put_side = place_matrix(order, i, FIRST, NM, visible[i], PATCH)
            put_grad(i, put, dy1[rows_of(i, NV), :])
            block_out[0, i] = (nn(put, lat[rows_of(i, NV), :]) + nn(put_side, out[rows_of(i, NM), :])).astype(BF)

        loop(images, put_image)

    @pl.when(ids[0] == 1)
    def _():
        copies = Copies(sems)
        copies.start(wqkv.at[0, :, pl.ds(0, D)], sqkv.at[:, pl.ds(0, D)])
        stack_rows(copies, [piece.at[pl.ds(0, nm)] for piece in x_in], x, nm)
        stack_rows(copies, dq_reg, dq, nm)
        stack_rows(copies, dy1_reg, dy1, nm)
        stack_rows(copies, res, out, nm)
        copies.finish()
        rows = images * NM
        dh[pl.ds(0, rows), :] = nt(dq[pl.ds(0, rows), :], sqkv[:, 0:D])

        def keep(sel, dx):
            dy1[sel, :] = dx

        g1, b1 = norm_back(x, dh, dy1, keep, rows, f32_row(gains.at[0], 0))
        total = sums_reg[0][...]
        for more in sums_reg[1:]:
            total = total + more[...]
        set_norms(total[0:1] + g1, total[1:2], total[2:3] + b1, total[3:4])

        def put_image(i):
            put = place_matrix(order, i, FIRST, NM, visible[i], PATCH)
            put_grad(i, put, dy1[rows_of(i, NM), :])
            block_out[0, i] = nn(put, out[rows_of(i, NM), :]).astype(BF)

        loop(images, put_image)


def place(groups, ids, visible, order, gains, sums, sums_reg, wqkv, dq, dkv, dy1, x, lat_enc, res, dq_reg, dy1_reg):
    images = groups * GROUP
    n = images * NV
    outs = [struct((1, images, PATCH, D)), struct((1, images, PATCH, D), F32), struct((16, D), F32)]
    scratch = [
        pltpu.VMEM((images, 1, PATCH), jnp.int32),
        pltpu.VMEM((D, 3 * D), BF), pltpu.VMEM((n, D), BF), pltpu.VMEM((n, D), BF), pltpu.VMEM((n, 2 * D), BF),
        pltpu.VMEM((n, D), F32), pltpu.VMEM((n, D), F32), pltpu.VMEM((n, D), BF),
        pltpu.VMEM((images * NM, D), BF), pltpu.SemaphoreType.DMA((16,)),
    ]
    return pl.pallas_call(
        partial(place_kernel, groups),
        in_specs=[SMEM, SMEM, VMEM, VMEM] + [VMEM] * (3 + groups) + [HBM] * (4 + 5 * groups),
        out_specs=[VMEM] * len(outs),
        out_shape=outs,
        scratch_shapes=scratch,
        compiler_params=params(LIMIT),
        cost_estimate=cost(1e6, 1e5),
        name="place",
    )(ids, visible, order, gains, *sums, *sums_reg, wqkv, dq, dkv, dy1, *x, *lat_enc, *res, *dq_reg, *dy1_reg)


BITS = (2, 4, 8)


def hop(value, bit):
    return lax.ppermute(value, "dp", [(i, i ^ bit) for i in range(16)])


def combine_kernel(shape, ids, *refs):
    counts, arrivals, first, last, targets, kinds, given = shape
    total = sum(counts)
    terms, refs = refs[:total], refs[total:]
    parts, refs = refs[: len(arrivals)], refs[len(arrivals) :]
    outs, scratch = refs[:given], refs[given:]
    sems = scratch[-1]
    copies = Copies(sems)
    width = total + len(arrivals)

    def path(gone, target):
        bits = []
        for bit in range(gone, last):
            own = ids[2 + bit]
            flip = bit >= first and (target >> (bit - first)) & 1
            bits.append(1 - own if flip else own)
        return tuple(bits)

    def take(ref, at, own):
        copies.start(ref.at[at] if at else ref, own)

    for t, target in enumerate(targets):
        for ref, own in zip(terms, scratch[t * width :]):
            take(ref, path(0, target), own)
        for gone, ref, own in zip(arrivals, parts, scratch[t * width + total :]):
            take(ref, path(gone, target), own)
    copies.finish()
    rest = (2,) * (3 - last)
    spots = [()]
    for _ in rest:
        spots = [spot + (i,) for spot in spots for i in range(2)]
    for t in range(len(targets)):
        own_terms = scratch[t * width : t * width + total]
        own_parts = scratch[t * width + total : (t + 1) * width]
        for spot in spots:
            start = column = 0
            for j, count in enumerate(counts):
                values = [own[spot] if spot else own[...] for own in own_terms[start : start + count]]
                values += [own[spot + (j,)] for own in own_parts]
                value = values[0].astype(F32)
                for more in values[1:]:
                    value = value + more.astype(F32)
                start += count
                if kinds[0] is None:
                    outs[t][spot + (j,)] = value.astype(BF)
                else:
                    which = kinds[j]
                    at = sum(1 for other in kinds[:j] if other == which) * D
                    outs[which][:, at : at + D] = value


def combine(ids, pieces, arrivals, first, last, targets=(1,), finals=None):
    rows = pieces[0][0].shape[-2]
    rest = (2,) * (3 - last)
    counts = tuple(len(terms) for terms in pieces)
    gone = tuple(3 - (part.ndim - 3) for part in arrivals)
    if finals is None:
        outs = [struct(rest + (len(pieces), rows, D)) for _ in targets]
        kinds = (None,) * len(targets)
    else:
        outs = [struct((rows, finals.count(i) * D), F32) for i in range(max(finals) + 1)]
        kinds, targets = finals, (0,)
    scratch = []
    for _ in targets:
        scratch += [pltpu.VMEM(rest + (rows, D), BF) for _ in range(sum(counts))]
        scratch += [pltpu.VMEM(rest + (len(pieces), rows, D), BF) for _ in arrivals]
    scratch.append(pltpu.SemaphoreType.DMA((len(scratch),)))
    return pl.pallas_call(
        partial(combine_kernel, (counts, gone, first, last, targets, kinds, len(outs))),
        in_specs=[SMEM] + [HBM] * (sum(counts) + len(arrivals)),
        out_specs=[VMEM] * len(outs),
        out_shape=outs,
        scratch_shapes=scratch,
        compiler_params=params(LIMIT),
        cost_estimate=cost(1e5, 1e4),
        name="combine",
    )(ids, *[term for terms in pieces for term in terms], *arrivals)


def in_order(first, then):
    return lax.optimization_barrier((first, then))


def own_columns(rows, count):
    own = D // count
    me = lax.axis_index("dp")

    def part(block, wide):
        return lax.dynamic_slice_in_dim(block, me * wide, wide, block.ndim - 1)

    return (
        part(rows[:2], own),
        part(rows[2:6], own),
        part(rows[6:8].reshape(-1), 2 * own),
        part(rows[8:12].reshape(-1), 4 * own),
    )


def scatter_natural(block):
    shards = block.reshape(lax.axis_size("dp"), -1, D)
    return lax.psum_scatter(shards, "dp", scatter_dimension=0, tiled=True)[0].astype(F32)


def local(
    patch_rows, cotangent, patch_order, visible, qkv_weight, out_weight, up_weight, down_weight, norm_gains, biases,
    qv_bias, up_bias, target_qkv, target_out, target_up, target_down, target_gains, target_biases, target_qv_bias,
    target_up_bias,
):
    count = lax.axis_size("dp")
    tree = count == 16
    place_dp = lax.axis_index("dp")
    bits = [(place_dp // bit) % 2 for bit in (1,) + BITS]
    ids = jnp.stack([lax.axis_index("section")] + bits).astype(jnp.int32)
    groups = patch_order.shape[0] // GROUP
    weights = (qkv_weight, out_weight, up_weight, down_weight)
    targets = (target_qkv, target_out, target_up, target_down)
    vecs = (norm_gains, biases, qv_bias, up_bias)
    target_vecs = (target_gains, target_biases, target_qv_bias[None], target_up_bias[None])

    encoded = [encode(g, ids, visible, patch_order, *vecs, patch_rows, cotangent, weights) for g in range(groups)]
    lat, x, hq, q, k, v_e, p_e, o_e, y1_e, h2_e, gp_e, a_e = zip(*encoded)
    sent = [lax.ppermute(piece, "section", [(0, 1)]) for piece in lat]
    middles = [
        middle(
            g, ids, visible, patch_order, vecs, target_vecs, patch_rows, cotangent, sent[g], x[g], q[g], k[g],
            weights, targets,
        )
        for g in range(groups)
    ]
    dlat, res, hk_r, dq_r, dkv_r, o_r, dy1b_r, h2_r, du_r, a_r, dy1_r, sums_r, cot_e = zip(*middles)
    back = [lax.ppermute(piece, "section", [(1, 0)]) for piece in dlat]

    send = partial(combine, ids)
    down, dyb, sums_down = down_grad(groups, count, ids, cot_e, back, a_e, a_r, k)
    if tree:
        downs = [[down[0], hop(down[1], 1)]]
        down_x, dyb = in_order(send(downs, [], 0, 1)[0], dyb)
        down_got = [hop(down_x, 2)]
    up, dy1, sums_up = up_grad(
        groups, count, ids, norm_gains, dyb, up_weight, down_weight, y1_e, gp_e, h2_e, du_r, h2_r
    )
    if tree:
        ups = [[up[2 * j], hop(up[2 * j + 1], 1)] for j in range(4)]
        (up_x, down_z), dy1 = in_order((send(ups, [], 0, 1)[0], send(downs, down_got, 1, 2)[0]), dy1)
        up_got = [hop(up_x, 2)]
        down_got = down_got + [hop(down_z, 4)]
    dq, dkv, dy1b = attn_back(groups, ids, dy1, out_weight, q, k, v_e, p_e)
    if tree:
        down_z, dq = in_order(send(downs, down_got, 2, 3)[0], dq)
        down_got = down_got + [hop(down_z, 8)]
    attn, sums_attn = qkv_grad(groups, count, ids, dq, dkv, dy1b, o_e, hq, hk_r, dq_r, dkv_r, o_r, dy1b_r)
    if tree:
        attns = [[attn[2 * j], hop(attn[2 * j + 1], 1)] for j in range(4)]
        early, late = attns[:2], attns[2:]
        (early_x, up_z), dq = in_order((send(early, [], 0, 1)[0], send(ups, up_got, 1, 2)[0]), dq)
        early_got = [hop(early_x, 2)]
        up_got = up_got + [hop(up_z, 4)]
    block_out, grad_rows, small = place(
        groups, ids, visible, patch_order, norm_gains, (sums_down, sums_up, sums_attn), sums_r, qkv_weight, dq, dkv,
        dy1, x, lat, res, dq_r, dy1_r,
    )
    if tree:
        up_z = send(ups, up_got, 2, 3)[0]
        early_z = send(early, early_got, 1, 3, (1, 2, 3))
        (late_x, up_z, early_z), small = in_order((send(late, [], 0, 1)[0], up_z, early_z), small)
        late_got = [hop(late_x, 2)]
        up_got = up_got + [hop(up_z, 8)]
        early_got = early_got + [hop(one, bit) for one, bit in zip(early_z, (4, 8, 12))]
        down_sum = send(downs, down_got, 0, 3, finals=(0,))[0]
        for bit in (1, 2):
            small = small + hop(small, bit)
        late_z, (block_out, grad_rows, small) = in_order(
            send(late, late_got, 1, 3, (1, 2, 3)), (block_out, grad_rows, small)
        )
        for bit in (4, 8):
            small = small + hop(small, bit)
        late_got = late_got + [hop(one, bit) for one, bit in zip(late_z, (4, 8, 12))]
        up_sum = send(ups, up_got, 0, 3, finals=(0, 0, 0, 0))[0]
        key_value = send(early, early_got, 0, 3, finals=(0, 0))[0]
        query, out_sum = send(late, late_got, 0, 3, finals=(0, 1))
        qkv_sum = jnp.concatenate([query, key_value], axis=1)
    else:
        down_sum = scatter_natural(down[0])
        up_sum = jnp.concatenate([scatter_natural(one) for one in up], axis=1)
        qkv_sum = jnp.concatenate([scatter_natural(attn[i]) for i in (2, 0, 1)], axis=1)
        small = lax.psum(small, "dp")
        out_sum = scatter_natural(attn[3])
    gains, bias_rows, qv_rows, up_rows = own_columns(small, count)
    return (
        block_out,
        grad_rows,
        qkv_sum[None],
        out_sum[None],
        up_sum[None],
        down_sum[None],
        gains[None],
        bias_rows[None],
        qv_rows[None],
        up_rows[None],
    )


def solution(mesh):
    three, four = P("section", None, None), P("section", "dp", None, None)
    grad = P("section", "dp", None)
    return jax.shard_map(
        local,
        mesh=mesh,
        in_specs=(four, four, P("dp", None), P("dp"), three, three, three, three, three, three,
                  P("section", None), P("section", None), P(), P(), P(), P(), P(), P(), P(), P()),
        out_specs=(four, four, grad, grad, grad, grad, P("section", None, "dp"), P("section", None, "dp"),
                   P("section", "dp"), P("section", "dp")),
        check_vma=False,
    )
```

```python
from functools import partial

import jax
import jax.numpy as jnp
from jax import lax
from jax.experimental import pallas as pl
from jax.experimental.pallas import tpu as pltpu
from jax.sharding import PartitionSpec as P

HEADS = 12
PATCH = 196
D = 768
FF = 3072
EPS = 1e-06
NV = 144
NM = 128
FIRST = PATCH - NM
GROUP = 2
CHUNK = 32

BF = jnp.bfloat16
F32 = jnp.float32
MIB = 1024 * 1024
LIMIT = 62

HBM = pl.BlockSpec(memory_space=pl.ANY)
VMEM = pl.BlockSpec(memory_space=pltpu.VMEM)
SMEM = pl.BlockSpec(memory_space=pltpu.SMEM)


def nn(a, b):
    return jnp.dot(a, b, preferred_element_type=F32)


def nt(a, b):
    return lax.dot_general(a, b, (((1,), (1,)), ((), ())), preferred_element_type=F32)


def tn(a, b):
    return lax.dot_general(a, b, (((0,), (0,)), ((), ())), preferred_element_type=F32)


def loop(count, body, unroll=1):
    def step(i, carry):
        for u in range(unroll):
            body(i * unroll + u)
        return carry

    if count == unroll:
        step(0, 0)
    else:
        lax.fori_loop(0, count // unroll, step, 0)


def unroll_of(count):
    return next(u for u in (4, 3, 2, 1) if count % u == 0)


def rows_of(i, size):
    return pl.ds(pl.multiple_of(i * size, size), size)


def f32_row(ref, row, col=0, width=D):
    return ref[pl.ds(row, 1), pl.ds(col, width)].astype(F32)


class Copies:
    def __init__(self, sems):
        self.sems = sems
        self.used = 0
        self.open = []

    def start(self, src, dst):
        copy = pltpu.make_async_copy(src, dst, self.sems.at[self.used])
        self.used += 1
        copy.start()
        self.open.append(copy)
        return copy

    def wait(self, *copies):
        for copy in copies:
            copy.wait()
            self.open.remove(copy)

    def finish(self):
        self.wait(*list(self.open))

    def take(self, count):
        self.used += count
        return self.used - count

    def begin(self, src, dst, at):
        pltpu.make_async_copy(src, dst, self.sems.at[at]).start()

    def wait_at(self, src, dst, at):
        pltpu.make_async_copy(src, dst, self.sems.at[at]).wait()


def gelu_pair(u):
    size = jnp.abs(u)
    base = 1.0 + (0.3275911 * 0.7071067811865476) * size
    guess = pl.reciprocal(base, approx=True)
    t = guess * (2.0 - base * guess)
    ex = jnp.exp2((u * u) * (-0.5 * 1.4426950408889634))
    poly = 0.5306027145 * t - 0.7265760135
    poly = poly * t + 0.7107068705
    poly = poly * t - 0.142248368
    poly = poly * t + 0.127414796
    tail = poly * t * ex
    phi = jnp.where(u >= 0.0, 1.0 - tail, tail)
    return u * phi, phi + u * (0.3989422804014327 * ex)


def norm_rows(src, dst, rows, gain, shift):
    def body(i):
        sel = rows_of(i, CHUNK)
        x = src[sel, :].astype(F32)
        centered = x - jnp.mean(x, axis=-1, keepdims=True)
        var = jnp.mean(centered * centered, axis=-1, keepdims=True)
        dst[sel, :] = (centered * lax.rsqrt(var + EPS) * gain + shift).astype(BF)

    loop(rows // CHUNK, body, unroll_of(rows // CHUNK))


def norm_back(src, grad, base, write, rows, gain):
    count = rows // CHUNK
    unroll = 3 if count % 3 == 0 else 2

    def step(i, carry):
        for u in range(unroll):
            carry = one(i * unroll + u, carry)
        return carry

    def one(i, carry):
        d_gain, d_shift = carry
        sel = rows_of(i, CHUNK)
        x = src[sel, :].astype(F32)
        dh = grad[sel, :]
        centered = x - jnp.mean(x, axis=-1, keepdims=True)
        var = jnp.mean(centered * centered, axis=-1, keepdims=True)
        rstd = lax.rsqrt(var + EPS)
        hat = centered * rstd
        g = dh * gain
        part = dh * hat
        dx = rstd * (
            g
            - jnp.mean(g, axis=-1, keepdims=True)
            - hat * jnp.mean(g * hat, axis=-1, keepdims=True)
        )
        if base is not None:
            dx = dx + base[sel, :].astype(F32)
        write(sel, dx)
        d_gain = d_gain + jnp.sum(part.reshape(CHUNK // 8, 8, D), axis=0)
        d_shift = d_shift + jnp.sum(dh.reshape(CHUNK // 8, 8, D), axis=0)
        return d_gain, d_shift

    zero = jnp.zeros((8, D), F32)
    d_gain, d_shift = lax.fori_loop(0, count // unroll, step, (zero, zero))
    return jnp.sum(d_gain, axis=0, keepdims=True), jnp.sum(d_shift, axis=0, keepdims=True)


def column_sum(ref, rows, col=0, width=D):
    def step(i, carry):
        x = ref[rows_of(i, CHUNK), pl.ds(col, width)].astype(F32)
        return carry + jnp.sum(x.reshape(CHUNK // 8, 8, width), axis=0)

    total = lax.fori_loop(0, rows // CHUNK, step, jnp.zeros((8, width), F32))
    return jnp.sum(total, axis=0, keepdims=True)


def as_bf16(flags):
    return jnp.where(flags, 1.0, 0.0).astype(BF)


def place_matrix(order, image, start, count, low, high):
    row = order[image, :, pl.ds(start, count)]
    rank = start + lax.broadcasted_iota(jnp.int32, (1, count), 1)
    row = jnp.where((rank >= low) & (rank < high), row, -1)
    return as_bf16(row == lax.broadcasted_iota(jnp.int32, (PATCH, count), 0))


def split_orders(order, split):
    for image in range(split.shape[0]):
        split[image] = order[image : image + 1, :]


def split_pair(pair):
    lane = lax.broadcasted_iota(jnp.int32, pair.shape, 1)
    zero = jnp.zeros_like(pair)
    return jnp.concatenate([jnp.where(lane < 64, pair, zero), jnp.where(lane < 64, zero, pair)], axis=0)


def join_rows(both):
    rows = both.shape[0] // 2
    lane = lax.broadcasted_iota(jnp.int32, (rows, 128), 1)
    return jnp.where(lane < 64, both[:rows], both[rows:])


def join_columns(both):
    rows = both.shape[1] // 2
    return jnp.concatenate([both[:64, :rows], both[64:, rows:]], axis=0).T


PAIRS = HEADS // 2
STEP = 6


def each_pair_group(images, body):
    def group(i):
        image = i // (PAIRS // STEP)
        first = (i % (PAIRS // STEP)) * STEP
        pairs = [first + step for step in range(STEP)]
        body(image, [image * PAIRS + pair for pair in pairs], [pl.ds(pl.multiple_of(pair * 128, 128), 128) for pair in pairs])

    loop(images * (PAIRS // STEP), group)


def softmax(scores, axis):
    ex = jnp.exp(scores - jnp.max(scores, axis=axis, keepdims=True))
    return (ex * (1.0 / jnp.sum(ex, axis=axis, keepdims=True))).astype(BF)


def score_back(probs, d_probs, axis):
    wide = probs.astype(F32)
    return (wide * (d_probs - jnp.sum(d_probs * wide, axis=axis, keepdims=True))).astype(BF)


def attention_by_rows(images, n, q, k, v, p, o, count_of):
    def body(image, slots, lanes):
        sel = rows_of(image, n)
        ok = lax.broadcasted_iota(jnp.int32, (1, n), 1) < count_of(image)
        scores = [nt(split_pair(q[sel, at]), k[sel, at]) for at in lanes]
        probs = [softmax(jnp.where(ok, one, -1000000000.0), 1) for one in scores]
        for slot, one in zip(slots, probs):
            p[slot] = one
        mixed = [nn(one, v[sel, at]) for one, at in zip(probs, lanes)]
        for at, one in zip(lanes, mixed):
            o[sel, at] = join_rows(one).astype(BF)

    each_pair_group(images, body)


def attention_by_columns(images, nk, q, k, v, p, o, key_ok):
    def body(image, slots, lanes):
        qs, ks = rows_of(image, NM), rows_of(image, nk)
        ok = key_ok(image)
        scores = [nt(k[ks, at], split_pair(q[qs, at])) for at in lanes]
        probs = [softmax(jnp.where(ok, one, -1000000000.0), 0) for one in scores]
        if p is not None:
            for slot, one in zip(slots, probs):
                p[slot] = one
        mixed = [tn(v[ks, at], one) for one, at in zip(probs, lanes)]
        for at, one in zip(lanes, mixed):
            o[qs, at] = join_columns(one).astype(BF)

    each_pair_group(images, body)


def attention_back_rows(images, n, q, k, v, p, do, dq, dkv):
    def body(image, slots, lanes):
        sel = rows_of(image, n)
        d_mixed = [split_pair(do[sel, at]) for at in lanes]
        d_probs = [nt(one, v[sel, at]) for one, at in zip(d_mixed, lanes)]
        d_scores = [score_back(p[slot], one, 1) for slot, one in zip(slots, d_probs)]
        d_values = [tn(p[slot], one) for slot, one in zip(slots, d_mixed)]
        d_query = [nn(one, k[sel, at]) for one, at in zip(d_scores, lanes)]
        d_keys = [tn(one, split_pair(q[sel, at])) for one, at in zip(d_scores, lanes)]
        for at, value, query, key in zip(lanes, d_values, d_query, d_keys):
            dq[sel, at] = (join_rows(query) * 0.125).astype(BF)
            dkv[sel, at] = key.astype(BF)
            dkv[sel, pl.ds(pl.multiple_of(D + at.start, 128), 128)] = value.astype(BF)

    each_pair_group(images, body)


def attention_back_columns(images, nk, q, k, v, p, do, dq, dkv):
    def body(image, slots, lanes):
        qs, ks = rows_of(image, NM), rows_of(image, nk)
        d_mixed = [split_pair(do[qs, at]) for at in lanes]
        d_probs = [nt(v[ks, at], one) for one, at in zip(d_mixed, lanes)]
        d_scores = [score_back(p[slot], one, 0) for slot, one in zip(slots, d_probs)]
        d_values = [nn(p[slot], one) for slot, one in zip(slots, d_mixed)]
        d_query = [tn(k[ks, at], one) for one, at in zip(d_scores, lanes)]
        d_keys = [nn(one, split_pair(q[qs, at])) for one, at in zip(d_scores, lanes)]
        for at, value, query, key in zip(lanes, d_values, d_query, d_keys):
            dq[qs, at] = (join_columns(query) * 0.125).astype(BF)
            dkv[ks, at] = key.astype(BF)
            dkv[ks, pl.ds(pl.multiple_of(D + at.start, 128), 128)] = value.astype(BF)

    each_pair_group(images, body)


HALF = 512


def mlp_forward(rows, h2, w1, w2, up_b, u, a, gp, acc, out, base):
    acc[...] = base()

    def body(i):
        cols = [pl.ds(pl.multiple_of((2 * i + part) * HALF, HALF), HALF) for part in range(2)]
        for part in range(2):
            u[part] = nn(h2[...], w1[:, cols[part]])
        for part in range(2):
            for c in range(0, HALF, 256):
                at = pl.ds(pl.multiple_of((2 * i + part) * HALF + c, 256), 256)
                shift = up_b[0:1, at].astype(F32)
                for r in range(0, rows, CHUNK):
                    value, slope = gelu_pair(u[part, r : r + CHUNK, c : c + 256] + shift)
                    a[r : r + CHUNK, at] = value.astype(BF)
                    if gp is not None:
                        gp[r : r + CHUNK, at] = slope.astype(BF)
            acc[...] += nn(a[:, cols[part]], w2[cols[part], :])

    loop(FF // (2 * HALF), body)
    out[...] = acc[...].astype(BF)


def mlp_back(rows, dyb, gp, w1, w2, du, u, acc):
    acc[...] = jnp.zeros_like(acc)

    def body(i):
        cols = [pl.ds(pl.multiple_of((2 * i + part) * HALF, HALF), HALF) for part in range(2)]
        for part in range(2):
            u[part] = nt(dyb[...], w2[cols[part], :])
        for part in range(2):
            for r in range(0, rows, CHUNK):
                sel = slice(r, r + CHUNK)
                du[sel, cols[part]] = (gp[sel, cols[part]].astype(F32) * u[part, sel, :]).astype(BF)
            acc[...] += nt(du[:, cols[part]], w1[:, cols[part]])

    loop(FF // (2 * HALF), body)


def project(count, rows, left, weight, first, write):
    def body(j):
        write(j, nn(left[...], weight[:, pl.ds(pl.multiple_of((first + j) * D, D), D)]))

    loop(count, body)


def set_biases(ref, bias):
    ref[0] = f32_row(bias, 0)
    ref[1] = jnp.zeros((1, D), F32)
    ref[2] = f32_row(bias, 0, D)


def cost(flops, nbytes):
    return pl.CostEstimate(flops=int(flops), bytes_accessed=int(nbytes), transcendentals=0)


def params(mib):
    return pltpu.CompilerParams(vmem_limit_bytes=mib * MIB)


def struct(shape, dtype=BF):
    return jax.ShapeDtypeStruct(shape, dtype)


def start_weights(copies, sources, scratch):
    return [copies.start(src, dst) for src, dst in zip(sources, scratch)]


def encode_kernel(group, ids, visible, order_in, gains, biases, qvb, upb, rows, wqkv, wo, w1, w2,
                  lat_out, x_out, hq_out, q_out, k_out, v_out, p_out, o_out, y1_out, h2_out, gp_out, a_out,
                  order, rows_v, sqkv, so, s1, s2, x, hq, qkv, p, o, y1, h2, gp, a, u, acc, shifts, lat, sems):
    n = GROUP * NV
    split_orders(order_in, order)

    @pl.when(ids[0] == 0)
    def _():
        copies = Copies(sems)
        got_rows = copies.start(rows.at[0], rows_v)
        got_qkv, got_o, got_1, got_2 = start_weights(
            copies, (wqkv.at[0], wo.at[0], w1.at[0], w2.at[0]), (sqkv, so, s1, s2)
        )
        gain, bias = gains.at[0], biases.at[0]
        copies.wait(got_rows)

        def pick_rows(i):
            image = group * GROUP + i
            pick = place_matrix(order, image, 0, NV, 0, visible[image])
            x[rows_of(i, NV), :] = tn(pick, rows_v[i]).astype(BF)

        loop(GROUP, pick_rows)
        copies.start(x, x_out)
        norm_rows(x, hq, n, f32_row(gain, 0), f32_row(bias, 0))
        copies.start(hq, hq_out)
        copies.wait(got_qkv)
        set_biases(shifts, qvb)

        def keep(j, value):
            scale = jnp.where(j == 0, 0.125, 1.0)
            qkv[j] = ((value + shifts[j]).astype(BF).astype(F32) * scale).astype(BF)

        project(3, n, hq, sqkv, 0, keep)
        q, k, v = qkv.at[0], qkv.at[1], qkv.at[2]
        copies.start(q, q_out)
        copies.start(k, k_out)
        copies.start(v, v_out)

        attention_by_rows(GROUP, NV, q, k, v, p, o, lambda i: visible[group * GROUP + i])
        copies.start(p, p_out)
        copies.start(o, o_out)
        copies.wait(got_o)
        y1[...] = nn(o[...], so[...]) + f32_row(bias, 1) + x[...].astype(F32)
        copies.start(y1, y1_out)
        norm_rows(y1, h2, n, f32_row(gain, 1), f32_row(bias, 2))
        copies.start(h2, h2_out)
        copies.wait(got_1, got_2)
        mlp_forward(n, h2, s1, s2, upb, u, a, gp, acc, lat, lambda: y1[...] + f32_row(bias, 3))
        copies.start(gp, gp_out)
        copies.start(a, a_out)
        copies.start(lat, lat_out)
        copies.finish()


def encode(group, ids, visible, order, gains, biases, qvb, upb, rows, weights):
    n = GROUP * NV
    row, wide = struct((n, D)), struct((n, FF))
    heads = struct((GROUP * PAIRS, 2 * NV, NV))
    outs = [row] * 6 + [heads, row, struct((n, D), F32), row, wide, wide]
    vm = lambda s: pltpu.VMEM(s.shape, s.dtype)
    scratch = [
        pltpu.VMEM((order.shape[0], 1, PATCH), jnp.int32),
        pltpu.VMEM((GROUP, PATCH, D), BF),
        pltpu.VMEM((D, 3 * D), BF), pltpu.VMEM((D, D), BF), pltpu.VMEM((D, FF), BF), pltpu.VMEM((FF, D), BF),
        vm(row), vm(row), pltpu.VMEM((3, n, D), BF), vm(heads), vm(row), pltpu.VMEM((n, D), F32), vm(row),
        vm(wide), vm(wide), pltpu.VMEM((2, n, HALF), F32), pltpu.VMEM((n, D), F32), pltpu.VMEM((3, 1, D), F32), vm(row),
        pltpu.SemaphoreType.DMA((20,)),
    ]
    return pl.pallas_call(
        partial(encode_kernel, group),
        in_specs=[SMEM, SMEM] + [VMEM] * 5 + [HBM] * 5,
        out_specs=[HBM] * len(outs),
        out_shape=outs,
        scratch_shapes=scratch,
        compiler_params=params(LIMIT),
        cost_estimate=cost(2 * n * 12 * D * D, 25e6),
        name="encode",
    )(ids, visible, order, gains, biases, qvb, upb, rows, *weights)


def prepare_kernel(groups, ids, visible, order_in, gains, biases, qvb, *refs):
    rows, (cot, wqkv), refs = refs[:groups], refs[groups : groups + 2], refs[groups + 2 :]
    x_out, hq_out, q_out, dyb_out = (refs[i * groups : (i + 1) * groups] for i in range(4))
    order, rows_v, cot_v, wq, x, hq, q, dyb, sems = refs[4 * groups :]
    images = groups * GROUP
    m = GROUP * NM

    @pl.when(ids[0] == 1)
    def _():
        copies = Copies(sems)
        split_orders(order_in, order)
        got = [copies.start(piece.at[0], rows_v.at[pl.ds(g * GROUP, GROUP)]) for g, piece in enumerate(rows)]
        got.append(copies.start(cot.at[0], cot_v))
        got_q = copies.start(wqkv.at[0, :, pl.ds(0, D)], wq)
        gain, bias = gains.at[0], biases.at[0]
        copies.wait(*got)

        def pick_rows(image):
            pick = place_matrix(order, image, FIRST, NM, visible[image], PATCH)
            x[rows_of(image, NM), :] = tn(pick, rows_v[image]).astype(BF)
            dyb[rows_of(image, NM), :] = tn(pick, cot_v[image]).astype(BF)

        loop(images, pick_rows)
        norm_rows(x, hq, images * NM, f32_row(gain, 0), f32_row(bias, 0))
        copies.wait(got_q)
        q[...] = ((nn(hq[...], wq[...]) + f32_row(qvb, 0)).astype(BF) * 0.125).astype(BF)
        for g in range(groups):
            for ref, dest in ((x, x_out), (hq, hq_out), (q, q_out), (dyb, dyb_out)):
                copies.start(ref.at[pl.ds(g * m, m)], dest[g])
        copies.finish()


def prepare(groups, ids, visible, order, gains, biases, qvb, rows, cot, wqkv):
    images = groups * GROUP
    row = struct((GROUP * NM, D))
    whole = pltpu.VMEM((images * NM, D), BF)
    picture = pltpu.VMEM((images, PATCH, D), BF)
    outs = [row] * (4 * groups)
    got = pl.pallas_call(
        partial(prepare_kernel, groups),
        in_specs=[SMEM, SMEM] + [VMEM] * 4 + [HBM] * (2 + groups),
        out_specs=[HBM] * len(outs),
        out_shape=outs,
        scratch_shapes=[
            pltpu.VMEM((images, 1, PATCH), jnp.int32), picture, picture, pltpu.VMEM((D, D), BF),
            whole, whole, whole, whole, pltpu.SemaphoreType.DMA((16,)),
        ],
        compiler_params=params(LIMIT),
        cost_estimate=cost(1e6, 1e5),
        name="prepare",
    )(ids, visible, order, gains, biases, qvb, *rows, cot, wqkv)
    return [got[i * groups : (i + 1) * groups] for i in range(4)]


def middle_kernel(group, ids, visible, order_in, gains, biases, qvb, upb, tgains, tbiases, tqvb, tupb,
                  rows, cot, lat_in, x_in, q_in, dyb_in, wqkv, wo, w1, w2, tqkv, to, t1, t2,
                  dlat_out, res_out, hk_out, dq_out, dkv_out, o_out, dy1b_out, h2_out, du_out, a_out,
                  dy1_out, sums_out, cot_out,
                  order, rows_v, cot_v, sqkv, so, s1, s2, x, lat, hq, hk, q, kv, p, o, y1, h2, gp, a, u, acc, shifts,
                  res, dyb, du, dy1, dy1b, do, dq, dkv, dh, dlat, sums, sems):
    n, m = GROUP * NM, GROUP * NV
    top = pl.ds(0, n)
    k, v = kv.at[0], kv.at[1]
    split_orders(order_in, order)

    def forward(copies, got_weights, gain, bias, ub, nk, key_ok, keep_p, keep_slope):
        got_o, got_1, got_2 = got_weights
        attention_by_columns(GROUP, nk, q, k, v, keep_p, o, key_ok)
        copies.wait(got_o)
        y1[...] = nn(o[...], so[...]) + f32_row(bias, 1) + x[...].astype(F32)
        norm_rows(y1, h2, n, f32_row(gain, 1), f32_row(bias, 2))
        copies.wait(got_1, got_2)
        mlp_forward(n, h2, s1, s2, ub, u, a, keep_slope, acc, res, lambda: y1[...] + f32_row(bias, 3))
        copies.start(res, res_out)

    @pl.when(ids[0] == 0)
    def _():
        copies = Copies(sems)
        gain, bias = tgains, tbiases
        got_rows = copies.start(rows.at[0], rows_v)
        got_qkv = copies.start(tqkv, sqkv)
        got_weights = start_weights(copies, (to, t1, t2), (so, s1, s2))
        got_cot = copies.start(cot.at[0, pl.ds(group * GROUP, GROUP)], cot_v)
        copies.wait(got_rows)

        def pick_rows(i):
            image = group * GROUP + i
            pick = place_matrix(order, image, FIRST, NM, visible[image], PATCH)
            x[rows_of(i, NM), :] = tn(pick, rows_v[i]).astype(BF)

        loop(GROUP, pick_rows)
        norm_rows(x, hq, n, f32_row(gain, 0), f32_row(bias, 0))
        copies.wait(got_qkv)
        set_biases(shifts, tqvb)
        q[...] = ((nn(hq[...], sqkv[:, :D]) + f32_row(tqvb, 0)).astype(BF) * 0.125).astype(BF)

        def keep_kv(j, value):
            kv[j, top, :] = (value + shifts[j + 1]).astype(BF)

        project(2, n, hq, sqkv, 1, keep_kv)

        def key_ok(i):
            return lax.broadcasted_iota(jnp.int32, (NM, 1), 0) + FIRST >= visible[group * GROUP + i]

        forward(copies, got_weights, gain, bias, tupb, NM, key_ok, None, None)
        copies.wait(got_cot)

        def pick_cot(i):
            image = group * GROUP + i
            pick = place_matrix(order, image, 0, NV, 0, visible[image])
            lat[rows_of(i, NV), :] = tn(pick, cot_v[i]).astype(BF)

        loop(GROUP, pick_cot)
        copies.start(lat, cot_out)
        copies.finish()

    @pl.when(ids[0] == 1)
    def _():
        copies = Copies(sems)
        gain, bias = gains.at[0], biases.at[0]
        got_lat = copies.start(lat_in, lat)
        got_kv = copies.start(wqkv.at[0, :, pl.ds(D, 2 * D)], sqkv.at[:, pl.ds(D, 2 * D)])
        got_q = copies.start(q_in, q)
        got_x = copies.start(x_in, x)
        got_weights = start_weights(copies, (wo.at[0], w1.at[0], w2.at[0]), (so, s1, s2))
        got_dyb = copies.start(dyb_in, dyb)
        copies.wait(got_lat)
        norm_rows(lat, hk, m, f32_row(gain, 0), f32_row(bias, 0))
        copies.start(hk, hk_out)
        copies.wait(got_kv)
        set_biases(shifts, qvb)

        def keep_kv(j, value):
            kv[j] = (value + shifts[j + 1]).astype(BF)

        project(2, m, hk, sqkv, 1, keep_kv)
        copies.wait(got_q, got_x)

        def key_ok(i):
            return lax.broadcasted_iota(jnp.int32, (NV, 1), 0) < visible[group * GROUP + i]

        forward(copies, got_weights, gain, bias, upb.at[0:1], NV, key_ok, p, gp)
        copies.start(o, o_out)
        copies.start(h2, h2_out)
        copies.start(a, a_out)
        copies.wait(got_dyb)
        mlp_back(n, dyb, gp, s1, s2, du, u, acc)
        copies.start(du, du_out)

        def keep(sel, dx):
            dy1[sel, :] = dx
            dy1b[sel, :] = dx.astype(BF)

        g2, b2 = norm_back(y1, acc, dyb, keep, n, f32_row(gain, 1))
        copies.start(dy1, dy1_out)
        copies.start(dy1b, dy1b_out)
        do[...] = nt(dy1b[...], so[...]).astype(BF)
        attention_back_columns(GROUP, NV, q, k, v, p, do, dq, dkv)
        copies.start(dq, dq_out)
        copies.start(dkv, dkv_out)
        dh[...] = nt(dkv[:, :D], sqkv[:, D : 2 * D])
        dh[...] += nt(dkv[:, D:], sqkv[:, 2 * D :])

        def keep_side(sel, dx):
            dlat[sel, :] = dx.astype(BF)

        gk, bk = norm_back(lat, dh, None, keep_side, m, f32_row(gain, 0))
        copies.start(dlat, dlat_out)
        for row, value in enumerate((gk, g2, bk, b2)):
            sums[pl.ds(row, 1), :] = value
        copies.start(sums, sums_out)
        copies.finish()


def middle(group, ids, visible, order, own_vecs, target_vecs, rows, cot, lat, x, q, dyb, weights, targets):
    n, m = GROUP * NM, GROUP * NV
    row, side, wide = struct((n, D)), struct((m, D)), struct((n, FF))
    pair = struct((m, 2 * D))
    outs = [side, row, side, row, pair, row, row, row, wide, wide, struct((n, D), F32), struct((8, D), F32), side]
    vm = lambda s: pltpu.VMEM(s.shape, s.dtype)
    full, fside = pltpu.VMEM((n, D), F32), pltpu.VMEM((m, D), F32)
    scratch = [
        pltpu.VMEM((order.shape[0], 1, PATCH), jnp.int32),
        pltpu.VMEM((GROUP, PATCH, D), BF), pltpu.VMEM((GROUP, PATCH, D), BF),
        pltpu.VMEM((D, 3 * D), BF), pltpu.VMEM((D, D), BF), pltpu.VMEM((D, FF), BF), pltpu.VMEM((FF, D), BF),
        vm(row), vm(side), vm(row), vm(side), vm(row), pltpu.VMEM((2, m, D), BF),
        pltpu.VMEM((GROUP * PAIRS, NV, 2 * NM), BF), vm(row), full, vm(row), vm(wide), vm(wide),
        pltpu.VMEM((2, n, HALF), F32), full, pltpu.VMEM((3, 1, D), F32),
        vm(row), vm(row), vm(wide), full, vm(row), vm(row), vm(row), vm(pair), fside, vm(side),
        pltpu.VMEM((8, D), F32),
        pltpu.SemaphoreType.DMA((24,)),
    ]
    return pl.pallas_call(
        partial(middle_kernel, group),
        in_specs=[SMEM, SMEM] + [VMEM] * 9 + [HBM] * 14,
        out_specs=[HBM] * len(outs),
        out_shape=outs,
        scratch_shapes=scratch,
        compiler_params=params(LIMIT),
        cost_estimate=cost(4 * n * 12 * D * D, 25e6),
        name="middle",
    )(ids, visible, order, *own_vecs, *target_vecs, rows, cot, lat, x, q, dyb, *weights, *targets)


def stack_rows(copies, pieces, ref, size):
    return [copies.start(piece, ref.at[pl.ds(i * size, size)]) for i, piece in enumerate(pieces)]


def clear_tail(ref, used):
    ref[pl.ds(used, ref.shape[0] - used), :] = jnp.zeros((ref.shape[0] - used, ref.shape[1]), ref.dtype)


def halves(count):
    return [struct((2, 2, 2, D // 16, D))] * 2 if count == 16 else [struct((D, D))]


def give_blocks(copies, core, tree, left_right, out, dest):
    size = 8 if tree else 1
    first = copies.take(4 * size)

    def send(j, act):
        view = out.at[j].reshape(2, 2, 2, 2, D // 16, D)
        if not tree:
            act(out.at[j], dest[j], first + j)
            return
        for x in range(2):
            for low in range(2):
                at = first + j * size + 4 * x + 2 * low
                act(view.at[:, low, x, core], dest[2 * j].at[x, low], at)
                act(view.at[:, low, x, 1 - core], dest[2 * j + 1].at[x, low], at + 1)

    left_right(send, copies.begin)
    for j in range(4):
        send(j, copies.wait_at)


def give_rows(copies, core, tree, multiply, out, dest):
    size = 4 if tree else 1
    first = copies.take(4 * size)

    def send(j, act):
        if not tree:
            act(out.at[j], dest[0].at[pl.ds(pl.multiple_of(j * D, D), D)], first + j)
            return
        view = out.at[j].reshape(2, 2, D // 4, D)
        low, high = lax.rem(j, 2), lax.div(j, 2)
        for x in range(2):
            at = first + j * size + 2 * x
            act(view.at[x, core], dest[0].at[x, low, high], at)
            act(view.at[x, 1 - core], dest[1].at[x, low, high], at + 1)

    def body(j):
        out[j] = multiply(j)
        send(j, copies.begin)

    loop(4, body)
    loop(4, lambda j: send(j, copies.wait_at))


def down_kernel(groups, parts, ids, *refs):
    cot, lat, a_enc, a_reg, dyb_reg = (refs[i * groups : (i + 1) * groups] for i in range(5))
    refs = refs[5 * groups :]
    dest, refs = refs[:parts], refs[parts:]
    sums_out, cot_v, dyb, a, dlat, out, sums, sems = refs
    images = groups * GROUP
    nv, nm = GROUP * NV, GROUP * NM

    @pl.when(ids[0] == 0)
    def _():
        copies = Copies(sems)
        got = stack_rows(copies, cot, cot_v, nv) + stack_rows(copies, lat, dlat, nv)
        stack_rows(copies, a_enc, a, nv)
        copies.wait(*got)
        dyb[...] = (cot_v[...].astype(F32) + dlat[...].astype(F32)).astype(BF)
        copies.finish()

    @pl.when(ids[0] == 1)
    def _():
        copies = Copies(sems)
        stack_rows(copies, a_reg, a, nm)
        stack_rows(copies, dyb_reg, dyb, nm)
        clear_tail(a, images * NM)
        clear_tail(dyb, images * NM)
        copies.finish()

    copies = Copies(sems)

    def multiply(j):
        return tn(a[:, pl.ds(pl.multiple_of(j * D, D), D)], dyb[...]).astype(BF)

    give_rows(copies, ids[1], parts == 2, multiply, out, dest)
    sums[...] = jnp.broadcast_to(column_sum(dyb, images * NV), (8, D))
    copies.start(sums, sums_out)
    copies.finish()


def down_grad(groups, count, ids, cot, dlat, a_enc, a_reg, dyb_reg):
    n = groups * GROUP * NV
    main = [struct((2, 2, 2, D // 4, D))] * 2 if count == 16 else [struct((FF, D))]
    outs = main + [struct((8, D), F32)]
    row = pltpu.VMEM((n, D), BF)
    scratch = [
        row, row, pltpu.VMEM((n, FF), BF), row, pltpu.VMEM((4, D, D), BF), pltpu.VMEM((8, D), F32),
        pltpu.SemaphoreType.DMA((24,)),
    ]
    got = pl.pallas_call(
        partial(down_kernel, groups, len(main)),
        in_specs=[SMEM] + [HBM] * (5 * groups),
        out_specs=[HBM] * len(outs),
        out_shape=outs,
        scratch_shapes=scratch,
        compiler_params=params(LIMIT),
        cost_estimate=cost(1e6, 1e5),
        name="down_grad",
    )(ids, *cot, *dlat, *a_enc, *a_reg, *dyb_reg)
    return got[: len(main)], got[-1]


def mlp_kernel(ids, gains, cot, dlat_in, w1, w2, y1_in, gp_in, dyb_out, du_out, dy1_out, sums_out,
               s1, s2, cot_v, dlat, dyb, gp, y1, du, u, acc, dy1, sums, sems):
    n = GROUP * NV

    @pl.when(ids[0] == 0)
    def _():
        copies = Copies(sems)
        got = [copies.start(cot, cot_v), copies.start(dlat_in, dlat)]
        got_w = [copies.start(w2.at[0], s2), copies.start(gp_in, gp), copies.start(w1.at[0], s1)]
        got_y = copies.start(y1_in, y1)
        copies.wait(*got)
        dyb[...] = (cot_v[...].astype(F32) + dlat[...].astype(F32)).astype(BF)
        copies.start(dyb, dyb_out)
        copies.wait(*got_w)
        mlp_back(n, dyb, gp, s1, s2, du, u, acc)
        copies.start(du, du_out)
        copies.wait(got_y)

        def keep(sel, dx):
            dy1[sel, :] = dx

        g2, b2 = norm_back(y1, acc, dyb, keep, n, f32_row(gains.at[0], 1))
        copies.start(dy1, dy1_out)
        sums[pl.ds(0, 1), :] = g2
        sums[pl.ds(1, 1), :] = b2
        copies.start(sums, sums_out)
        copies.finish()


def mlp_grad(ids, gains, cot, dlat, w1, w2, y1, gp):
    n = GROUP * NV
    row, wide, full = pltpu.VMEM((n, D), BF), pltpu.VMEM((n, FF), BF), pltpu.VMEM((n, D), F32)
    outs = [struct((n, D)), struct((n, FF)), struct((n, D), F32), struct((8, D), F32)]
    return pl.pallas_call(
        mlp_kernel,
        in_specs=[SMEM, VMEM] + [HBM] * 6,
        out_specs=[HBM] * len(outs),
        out_shape=outs,
        scratch_shapes=[
            pltpu.VMEM((D, FF), BF), pltpu.VMEM((FF, D), BF), row, row, row, wide, full, wide,
            pltpu.VMEM((2, n, HALF), F32), full, full, pltpu.VMEM((8, D), F32), pltpu.SemaphoreType.DMA((12,)),
        ],
        compiler_params=params(LIMIT),
        cost_estimate=cost(1e6, 1e5),
        name="mlp_grad",
    )(ids, gains, cot, dlat, w1, w2, y1, gp)


def up_kernel(groups, parts, ids, *refs):
    du_enc, h2_enc, du_reg, h2_reg = (refs[i * groups : (i + 1) * groups] for i in range(4))
    refs = refs[4 * groups :]
    dest, refs = refs[:parts], refs[parts:]
    sums_out, h2, du, out, sums, sems = refs
    images = groups * GROUP
    nv, nm = GROUP * NV, GROUP * NM

    @pl.when(ids[0] == 0)
    def _():
        copies = Copies(sems)
        stack_rows(copies, h2_enc, h2, nv)
        stack_rows(copies, du_enc, du, nv)
        copies.finish()

    @pl.when(ids[0] == 1)
    def _():
        copies = Copies(sems)
        stack_rows(copies, h2_reg, h2, nm)
        stack_rows(copies, du_reg, du, nm)
        clear_tail(du, images * NM)
        clear_tail(h2, images * NM)
        copies.finish()

    copies = Copies(sems)

    def multiply(send, act):
        def body(j):
            cols = pl.ds(pl.multiple_of(j * D, D), D)
            out[j] = tn(h2[...], du[:, cols]).astype(BF)
            for block in range(4):
                pl.when(j == block)(lambda block=block: send(block, act))
            sums[pl.ds(4 + j, 1), :] = column_sum(du, images * NV, pl.multiple_of(j * D, D))

        loop(4, body)

    give_blocks(copies, ids[1], parts == 8, multiply, out, dest)
    copies.start(sums, sums_out)
    copies.finish()


def up_grad(groups, count, ids, du_enc, h2_enc, du_reg, h2_reg):
    n = groups * GROUP * NV
    main = halves(count) * 4
    outs = main + [struct((8, D), F32)]
    got = pl.pallas_call(
        partial(up_kernel, groups, len(main)),
        in_specs=[SMEM] + [HBM] * (4 * groups),
        out_specs=[HBM] * len(outs),
        out_shape=outs,
        scratch_shapes=[
            pltpu.VMEM((n, D), BF), pltpu.VMEM((n, FF), BF), pltpu.VMEM((4, D, D), BF), pltpu.VMEM((8, D), F32),
            pltpu.SemaphoreType.DMA((36,)),
        ],
        compiler_params=params(LIMIT),
        cost_estimate=cost(1e6, 1e5),
        name="up_grad",
    )(ids, *du_enc, *h2_enc, *du_reg, *h2_reg)
    return got[: len(main)], got[-1]


def attn_kernel(ids, gains, wqkv, wo, dy1_enc, q_in, k_in, v_in, p_in, x_enc, dq_reg, dy1_reg, x_reg,
                dq_out, dkv_out, dy1b_out, dx_out, sums_out,
                sqkv, so, dy1, dy1b, q, k, v, p, x, do, dq, dkv, dh, sums, sems):
    m = GROUP * NM
    top = pl.ds(0, m)
    gain = f32_row(gains.at[0], 0)

    def finish(copies, rows):
        def keep(sel, dx):
            dy1[sel, :] = dx

        g1, b1 = norm_back(x, dh, dy1, keep, rows, gain)
        copies.start(dy1, dx_out)
        sums[0:1, :] = g1
        sums[1:2, :] = b1
        copies.start(sums, sums_out)
        copies.finish()

    @pl.when(ids[0] == 0)
    def _():
        copies = Copies(sems)
        got = [copies.start(dy1_enc, dy1), copies.start(wo.at[0], so)]
        later = [copies.start(src, dst) for src, dst in ((v_in, v), (p_in, p), (k_in, k), (q_in, q))]
        last = [copies.start(wqkv.at[0], sqkv), copies.start(x_enc, x)]
        copies.wait(*got)
        dy1b[...] = dy1[...].astype(BF)
        copies.start(dy1b, dy1b_out)
        do[...] = nt(dy1b[...], so[...]).astype(BF)
        copies.wait(*later)
        attention_back_rows(GROUP, NV, q, k, v, p, do, dq, dkv)
        copies.start(dq, dq_out)
        copies.start(dkv, dkv_out)
        copies.wait(*last)
        dh[...] = nt(dq[...], sqkv[:, 0:D])
        for j in range(2):
            dh[...] += nt(dkv[:, j * D : (j + 1) * D], sqkv[:, (j + 1) * D : (j + 2) * D])
        finish(copies, GROUP * NV)

    @pl.when(ids[0] == 1)
    def _():
        copies = Copies(sems)
        for src, dst in ((dq_reg, dq), (dy1_reg, dy1), (x_reg, x)):
            copies.start(src, dst.at[top])
        copies.start(wqkv.at[0, :, pl.ds(0, D)], sqkv.at[:, pl.ds(0, D)])
        copies.finish()
        dh[top, :] = nt(dq[top, :], sqkv[:, 0:D])
        finish(copies, m)


def attn_back(ids, gains, wqkv, wo, *pieces):
    n = GROUP * NV
    row, full = pltpu.VMEM((n, D), BF), pltpu.VMEM((n, D), F32)
    outs = [struct((n, D)), struct((n, 2 * D)), struct((n, D)), struct((n, D), F32), struct((8, D), F32)]
    return pl.pallas_call(
        attn_kernel,
        in_specs=[SMEM, VMEM] + [HBM] * (2 + len(pieces)),
        out_specs=[HBM] * len(outs),
        out_shape=outs,
        scratch_shapes=[
            pltpu.VMEM((D, 3 * D), BF), pltpu.VMEM((D, D), BF), full, row, row, row, row,
            pltpu.VMEM((GROUP * PAIRS, 2 * NV, NV), BF), row, row, row, pltpu.VMEM((n, 2 * D), BF), full,
            pltpu.VMEM((8, D), F32), pltpu.SemaphoreType.DMA((20,)),
        ],
        compiler_params=params(LIMIT),
        cost_estimate=cost(1e6, 1e5),
        name="attn_back",
    )(ids, gains, wqkv, wo, *pieces)


def qkv_kernel(groups, parts, ids, down_sums, up_sums, *refs):
    mlp_sums, reg_sums, in_sums = (refs[i * groups : (i + 1) * groups] for i in range(3))
    refs = refs[3 * groups :]
    pieces = [refs[i * groups : (i + 1) * groups] for i in range(11)]
    dq_enc, dkv_enc, dy1b_enc, o_enc, hq_enc, hq_reg, hk_reg, dq_reg, dkv_reg, o_reg, dy1b_reg = pieces
    refs = refs[11 * groups :]
    dest, refs = refs[:parts], refs[parts:]
    small, left, right, out, sems = refs
    images = groups * GROUP
    nv, nm = GROUP * NV, GROUP * NM
    hk, hq, o = (left.at[i] for i in range(3))
    dk, dv, dq, dy1b = (right.at[i] for i in range(4))

    @pl.when(ids[0] == 0)
    def _():
        copies = Copies(sems)
        for piece, ref in ((dq_enc, dq), (hq_enc, hq), (hq_enc, hk), (dy1b_enc, dy1b), (o_enc, o)):
            stack_rows(copies, piece, ref, nv)
        stack_rows(copies, [one.at[:, pl.ds(0, D)] for one in dkv_enc], dk, nv)
        stack_rows(copies, [one.at[:, pl.ds(D, D)] for one in dkv_enc], dv, nv)
        copies.finish()

    @pl.when(ids[0] == 1)
    def _():
        copies = Copies(sems)
        for piece, ref in ((hq_reg, hq), (dq_reg, dq), (o_reg, o), (dy1b_reg, dy1b)):
            stack_rows(copies, piece, ref, nm)
            clear_tail(ref, images * NM)
        stack_rows(copies, hk_reg, hk, nv)
        stack_rows(copies, [one.at[:, pl.ds(0, D)] for one in dkv_reg], dk, nv)
        stack_rows(copies, [one.at[:, pl.ds(D, D)] for one in dkv_reg], dv, nv)
        copies.finish()

    copies = Copies(sems)

    def multiply(send, act):
        def body(j):
            out[j] = tn(left[jnp.maximum(j - 1, 0)], right[j]).astype(BF)
            for block in range(4):
                pl.when(j == block)(lambda block=block: send(block, act))

        loop(4, body)

    give_blocks(copies, ids[1], parts == 8, multiply, out, dest)

    def total_of(sums):
        total = sums[0][...]
        for more in sums[1:]:
            total = total + more[...]
        return total

    first, mlp, reg = total_of(in_sums), total_of(mlp_sums), total_of(reg_sums)
    encoder = ids[0] == 0
    small[0:1, :] = first[0:1, :] + jnp.where(encoder, 0.0, reg[0:1, :])
    small[1:2, :] = jnp.where(encoder, mlp[0:1, :], reg[1:2, :])
    small[2:3, :] = first[1:2, :] + jnp.where(encoder, 0.0, reg[2:3, :])
    small[3:4, :] = column_sum(right.at[3], images * NV)
    small[4:5, :] = jnp.where(encoder, mlp[1:2, :], reg[3:4, :])
    small[5:6, :] = down_sums[0:1, :]
    small[6:7, :] = column_sum(right.at[2], images * NV)
    small[7:8, :] = column_sum(right.at[1], images * NV)
    small[8:12, :] = up_sums[4:8, :]
    small[12:16, :] = jnp.zeros((4, D), F32)
    copies.finish()


def qkv_grad(groups, count, ids, sums, *pieces):
    n = groups * GROUP * NV
    row = pltpu.VMEM((n, D), BF)
    main = halves(count) * 4
    outs = main + [struct((16, D), F32)]
    scratch = [
        pltpu.VMEM((3, n, D), BF), pltpu.VMEM((4, n, D), BF), pltpu.VMEM((4, D, D), BF),
        pltpu.SemaphoreType.DMA((40,)),
    ]
    got = pl.pallas_call(
        partial(qkv_kernel, groups, len(main)),
        in_specs=[SMEM] + [VMEM] * (2 + 3 * groups) + [HBM] * (11 * groups),
        out_specs=[HBM] * len(main) + [VMEM],
        out_shape=outs,
        scratch_shapes=scratch,
        compiler_params=params(LIMIT),
        cost_estimate=cost(1e6, 1e5),
        name="qkv_grad",
    )(ids, *sums, *[ref for piece in pieces for ref in piece])
    return got[: len(main)], got[-1]


def place_kernel(groups, ids, visible, order_in, *refs):
    dx_in, lat_enc, res = (refs[i * groups : (i + 1) * groups] for i in range(3))
    block_out, grad_out, order, dx, lat, out, sems = refs[3 * groups :]
    images = groups * GROUP
    nv, nm = GROUP * NV, GROUP * NM
    split_orders(order_in, order)

    def put_grad(i, put, value):
        high = value.astype(BF)
        low = (value - high.astype(F32)).astype(BF)
        grad_out[0, i] = nn(put, high) + nn(put, low)

    @pl.when(ids[0] == 0)
    def _():
        copies = Copies(sems)
        for piece, ref, size in ((dx_in, dx, nv), (lat_enc, lat, nv), (res, out, nm)):
            stack_rows(copies, piece, ref, size)
        copies.finish()

        def put_image(i):
            put = place_matrix(order, i, 0, NV, 0, visible[i])
            put_side = place_matrix(order, i, FIRST, NM, visible[i], PATCH)
            put_grad(i, put, dx[rows_of(i, NV), :])
            block_out[0, i] = (nn(put, lat[rows_of(i, NV), :]) + nn(put_side, out[rows_of(i, NM), :])).astype(BF)

        loop(images, put_image)

    @pl.when(ids[0] == 1)
    def _():
        copies = Copies(sems)
        stack_rows(copies, res, out, nm)
        stack_rows(copies, [piece.at[pl.ds(0, nm)] for piece in dx_in], dx, nm)
        copies.finish()

        def put_image(i):
            put = place_matrix(order, i, FIRST, NM, visible[i], PATCH)
            put_grad(i, put, dx[rows_of(i, NM), :])
            block_out[0, i] = nn(put, out[rows_of(i, NM), :]).astype(BF)

        loop(images, put_image)


def place(groups, ids, visible, order, *pieces):
    images = groups * GROUP
    n = images * NV
    outs = [struct((1, images, PATCH, D)), struct((1, images, PATCH, D), F32)]
    return pl.pallas_call(
        partial(place_kernel, groups),
        in_specs=[SMEM, SMEM, VMEM] + [HBM] * (3 * groups),
        out_specs=[VMEM] * len(outs),
        out_shape=outs,
        scratch_shapes=[
            pltpu.VMEM((images, 1, PATCH), jnp.int32), pltpu.VMEM((n, D), F32), pltpu.VMEM((n, D), BF),
            pltpu.VMEM((images * NM, D), BF), pltpu.SemaphoreType.DMA((8,)),
        ],
        compiler_params=params(LIMIT),
        cost_estimate=cost(1e6, 1e5),
        name="place",
    )(ids, visible, order, *[ref for piece in pieces for ref in piece])


BITS = (2, 4, 8)


def hop(value, bit):
    return lax.ppermute(value, "dp", [(i, i ^ bit) for i in range(16)])


def combine_kernel(jobs, given, ids, *refs):
    used = sum(sum(counts) + len(gone) for counts, gone, *_ in jobs)
    inputs, outs, scratch = list(refs[:used]), list(refs[used : used + given]), list(refs[used + given :])
    copies = Copies(scratch.pop())
    plans = []
    for counts, gone, first, last, targets, finals in jobs:
        terms = [inputs.pop(0) for _ in range(sum(counts))]
        parts = [inputs.pop(0) for _ in gone]
        for target in targets:

            def at(start):
                bits = []
                for bit in range(start, last):
                    flip = bit >= first and (target >> (bit - first)) & 1
                    bits.append(1 - ids[2 + bit] if flip else ids[2 + bit])
                return tuple(bits)

            started, own_terms, own_parts = [], [], []
            for ref, start, kept in [(ref, 0, own_terms) for ref in terms] + [
                (ref, start, own_parts) for ref, start in zip(parts, gone)
            ]:
                kept.append(scratch.pop(0))
                path = at(start)
                started.append(copies.start(ref.at[path] if path else ref, kept[-1]))
            plans.append((started, own_terms, own_parts, counts, last, finals, None if finals else outs.pop(0)))
    for started, own_terms, own_parts, counts, last, finals, out in plans:
        copies.wait(*started)
        spots = [()]
        for _ in range(3 - last):
            spots = [spot + (i,) for spot in spots for i in range(2)]
        for spot in spots:
            start = 0
            for j, count in enumerate(counts):
                values = [own[spot] if spot else own[...] for own in own_terms[start : start + count]]
                values += [own[spot + (j,)] for own in own_parts]
                value = values[0].astype(F32)
                for more in values[1:]:
                    value = value + more.astype(F32)
                start += count
                if finals:
                    which, column = finals[j]
                    outs[which][:, column * D : (column + 1) * D] = value
                else:
                    out[spot + (j,)] = value.astype(BF)


def send_job(pieces, arrivals, first, last, targets=(1,)):
    return pieces, arrivals, first, last, targets, None


def final_job(pieces, arrivals, finals):
    return pieces, arrivals, 0, 3, (0,), finals


def combine(ids, *jobs, outs=()):
    shapes = [struct(shape, F32) for shape in outs]
    plans, inputs, scratch = [], [], []
    for pieces, arrivals, first, last, targets, finals in jobs:
        rows = pieces[0][0].shape[-2]
        rest = (2,) * (3 - last)
        counts = tuple(len(terms) for terms in pieces)
        gone = tuple(3 - (part.ndim - 3) for part in arrivals)
        inputs += [term for terms in pieces for term in terms] + list(arrivals)
        plans.append((counts, gone, first, last, targets, finals))
        for _ in targets:
            scratch += [pltpu.VMEM(rest + (rows, D), BF) for _ in range(sum(counts))]
            scratch += [pltpu.VMEM(rest + (len(pieces), rows, D), BF) for _ in arrivals]
            if finals is None:
                shapes.append(struct(rest + (len(pieces), rows, D)))
    scratch.append(pltpu.SemaphoreType.DMA((len(scratch),)))
    return pl.pallas_call(
        partial(combine_kernel, tuple(plans), len(shapes)),
        in_specs=[SMEM] + [HBM] * len(inputs),
        out_specs=[VMEM] * len(shapes),
        out_shape=shapes,
        scratch_shapes=scratch,
        compiler_params=params(LIMIT),
        cost_estimate=cost(1e5, 1e4),
        name="combine",
    )(ids, *inputs)


def in_order(first, then):
    return lax.optimization_barrier((first, then))


def own_columns(rows, count):
    own = D // count
    me = lax.axis_index("dp")

    def part(block, wide):
        return lax.dynamic_slice_in_dim(block, me * wide, wide, block.ndim - 1)

    return (
        part(rows[:2], own),
        part(rows[2:6], own),
        part(rows[6:8].reshape(-1), 2 * own),
        part(rows[8:12].reshape(-1), 4 * own),
    )


def scatter_natural(block):
    shards = block.reshape(lax.axis_size("dp"), -1, D)
    return lax.psum_scatter(shards, "dp", scatter_dimension=0, tiled=True)[0].astype(F32)


def local(
    patch_rows, cotangent, patch_order, visible, qkv_weight, out_weight, up_weight, down_weight, norm_gains, biases,
    qv_bias, up_bias, target_qkv, target_out, target_up, target_down, target_gains, target_biases, target_qv_bias,
    target_up_bias,
):
    count = lax.axis_size("dp")
    tree = count == 16
    place_dp = lax.axis_index("dp")
    bits = [(place_dp // bit) % 2 for bit in (1,) + BITS]
    ids = jnp.stack([lax.axis_index("section")] + bits).astype(jnp.int32)
    groups = patch_order.shape[0] // GROUP
    weights = (qkv_weight, out_weight, up_weight, down_weight)
    targets = (target_qkv, target_out, target_up, target_down)
    vecs = (norm_gains, biases, qv_bias, up_bias)
    target_vecs = (target_gains, target_biases, target_qv_bias[None], target_up_bias[None])

    rows = [patch_rows[:, g * GROUP : (g + 1) * GROUP] for g in range(groups)]
    encoded = [encode(g, ids, visible, patch_order, *vecs, rows[g], weights) for g in range(groups)]
    lat, x_e, hq_e, q_e, k_e, v_e, p_e, o_e, y1_e, h2_e, gp_e, a_e = zip(*encoded)
    sent = [lax.ppermute(piece, "section", [(0, 1)]) for piece in lat]
    x_r, hq_r, q_r, dyb_r = prepare(
        groups, ids, visible, patch_order, norm_gains, biases, qv_bias, rows, cotangent, qkv_weight
    )
    middles = [
        middle(
            g, ids, visible, patch_order, vecs, target_vecs, rows[g], cotangent, sent[g], x_r[g], q_r[g], dyb_r[g],
            weights, targets,
        )
        for g in range(groups)
    ]
    dlat, res, hk_r, dq_r, dkv_r, o_r, dy1b_r, h2_r, du_r, a_r, dy1_r, sums_r, cot_e = zip(*middles)
    back = [lax.ppermute(piece, "section", [(1, 0)]) for piece in dlat]

    def mlp(g):
        return mlp_grad(ids, norm_gains, cot_e[g], back[g], up_weight, down_weight, y1_e[g], gp_e[g])

    def attention(g, dy1):
        return attn_back(
            ids, norm_gains, qkv_weight, out_weight, dy1, q_e[g], k_e[g], v_e[g], p_e[g], x_e[g],
            dq_r[g], dy1_r[g], x_r[g],
        )

    mlps = [mlp(g) for g in range(groups - 1)]
    attns = [attention(g, mlps[g][2]) for g in range(groups - 1)]
    last = groups - 1
    send = partial(combine, ids)
    attns, back[last] = in_order(attns, back[last])
    down, sums_down = down_grad(groups, count, ids, cot_e, back, a_e, a_r, dyb_r)
    cot_last = cot_e[last]
    if tree:
        downs = [[down[0], hop(down[1], 1)]]
        (down_x,), cot_last = in_order(send(send_job(downs, [], 0, 1)), cot_last)
        down_got = [hop(down_x, 2)]
    mlps.append(mlp_grad(ids, norm_gains, cot_last, back[last], up_weight, down_weight, y1_e[last], gp_e[last]))
    _, du_e, dy1_e, sums_e = zip(*mlps)
    up, sums_up = up_grad(groups, count, ids, du_e, h2_e, du_r, h2_r)
    dy1_last = dy1_e[last]
    if tree:
        ups = [[up[2 * j], hop(up[2 * j + 1], 1)] for j in range(4)]
        (up_x, down_z), dy1_last = in_order(
            send(send_job(ups, [], 0, 1), send_job(downs, down_got, 1, 2)), dy1_last
        )
        up_got = [hop(up_x, 2)]
        down_got = down_got + [hop(down_z, 4)]
    attns.append(attention(last, dy1_last))
    dq_e, dkv_e, dy1b_e, dx, sums_in = (list(piece) for piece in zip(*attns))
    if tree:
        (down_z,), dq_e[last] = in_order(send(send_job(downs, down_got, 2, 3)), dq_e[last])
        down_got = down_got + [hop(down_z, 8)]
    attn, small = qkv_grad(
        groups, count, ids, (sums_down, sums_up, *sums_e, *sums_r, *sums_in),
        dq_e, dkv_e, dy1b_e, o_e, hq_e, hq_r, hk_r, dq_r, dkv_r, o_r, dy1b_r,
    )
    if tree:
        grads = [[attn[2 * j], hop(attn[2 * j + 1], 1)] for j in range(4)]
        early, late = grads[:2], grads[2:]
        (early_x, late_x, up_z), (dx, small) = in_order(
            send(send_job(early, [], 0, 1), send_job(late, [], 0, 1), send_job(ups, up_got, 1, 2)), (dx, small)
        )
        early_got = [hop(early_x, 2)]
        up_got = up_got + [hop(up_z, 4)]
    block_out, grad_rows = place(groups, ids, visible, patch_order, dx, lat, res)
    if tree:
        peers = (1, 2, 3)
        for bit in (1, 2):
            small = small + hop(small, bit)
        (*early_z, up_z), (small, late_x, block_out, grad_rows) = in_order(
            send(send_job(early, early_got, 1, 3, peers), send_job(ups, up_got, 2, 3)),
            (small, late_x, block_out, grad_rows),
        )
        late_got = [hop(late_x, 2)]
        early_got = early_got + [hop(one, 4 * peer) for one, peer in zip(early_z, peers)]
        up_got = up_got + [hop(up_z, 8)]
        for bit in (4, 8):
            small = small + hop(small, bit)
        late_z, (block_out, grad_rows, small, early_got, up_got) = in_order(
            send(send_job(late, late_got, 1, 3, peers)), (block_out, grad_rows, small, early_got, up_got)
        )
        late_got = late_got + [hop(one, 4 * peer) for one, peer in zip(late_z, peers)]
        down_sum, up_sum = send(
            final_job(downs, down_got, ((0, 0),)),
            final_job(ups, up_got, tuple((1, j) for j in range(4))),
            outs=((D // 4, D), (D // 16, 4 * D)),
        )
        late_got, (down_sum, up_sum) = in_order(late_got, (down_sum, up_sum))
        qkv_sum, out_sum = send(
            final_job(early, early_got, ((0, 1), (0, 2))),
            final_job(late, late_got, ((0, 0), (1, 0))),
            outs=((D // 16, 3 * D), (D // 16, D)),
        )
    else:
        down_sum = scatter_natural(down[0])
        up_sum = jnp.concatenate([scatter_natural(one) for one in up], axis=1)
        qkv_sum = jnp.concatenate([scatter_natural(attn[i]) for i in (2, 0, 1)], axis=1)
        out_sum = scatter_natural(attn[3])
        small = lax.psum(small, "dp")
    gains, bias_rows, qv_rows, up_rows = own_columns(small, count)
    return (
        block_out,
        grad_rows,
        qkv_sum[None],
        out_sum[None],
        up_sum[None],
        down_sum[None],
        gains[None],
        bias_rows[None],
        qv_rows[None],
        up_rows[None],
    )


def solution(mesh):
    three, four = P("section", None, None), P("section", "dp", None, None)
    grad = P("section", "dp", None)
    return jax.shard_map(
        local,
        mesh=mesh,
        in_specs=(four, four, P("dp", None), P("dp"), three, three, three, three, three, three,
                  P("section", None), P("section", None), P(), P(), P(), P(), P(), P(), P(), P()),
        out_specs=(four, four, grad, grad, grad, grad, P("section", None, "dp"), P("section", None, "dp"),
                   P("section", "dp"), P("section", "dp")),
        check_vma=False,
    )
```

```python
from functools import partial

import jax
import jax.numpy as jnp
from jax import lax
from jax.experimental import pallas as pl
from jax.experimental.pallas import tpu as pltpu
from jax.sharding import PartitionSpec as P

HEADS = 12
PATCH = 196
D = 768
FF = 3072
EPS = 1e-06
NV = 144
NM = 128
FIRST = PATCH - NM
GROUP = 2
CHUNK = 32

BF = jnp.bfloat16
F32 = jnp.float32
MIB = 1024 * 1024
LIMIT = 62

HBM = pl.BlockSpec(memory_space=pl.ANY)
VMEM = pl.BlockSpec(memory_space=pltpu.VMEM)
SMEM = pl.BlockSpec(memory_space=pltpu.SMEM)


def nn(a, b):
    return jnp.dot(a, b, preferred_element_type=F32)


def nt(a, b):
    return lax.dot_general(a, b, (((1,), (1,)), ((), ())), preferred_element_type=F32)


def tn(a, b):
    return lax.dot_general(a, b, (((0,), (0,)), ((), ())), preferred_element_type=F32)


def loop(count, body, unroll=1):
    def step(i, carry):
        for u in range(unroll):
            body(i * unroll + u)
        return carry

    if count == unroll:
        step(0, 0)
    else:
        lax.fori_loop(0, count // unroll, step, 0)


def unroll_of(count):
    return next(u for u in (4, 3, 2, 1) if count % u == 0)


def rows_of(i, size):
    return pl.ds(pl.multiple_of(i * size, size), size)


def f32_row(ref, row, col=0, width=D):
    return ref[pl.ds(row, 1), pl.ds(col, width)].astype(F32)


class Copies:
    def __init__(self, sems):
        self.sems = sems
        self.used = 0
        self.open = []

    def start(self, src, dst):
        copy = pltpu.make_async_copy(src, dst, self.sems.at[self.used])
        self.used += 1
        copy.start()
        self.open.append(copy)
        return copy

    def wait(self, *copies):
        for copy in copies:
            copy.wait()
            self.open = [one for one in self.open if one is not copy]

    def finish(self):
        self.wait(*list(self.open))

    def take(self, count):
        self.used += count
        return self.used - count

    def begin(self, src, dst, at):
        pltpu.make_async_copy(src, dst, self.sems.at[at]).start()

    def wait_at(self, src, dst, at):
        pltpu.make_async_copy(src, dst, self.sems.at[at]).wait()


def gelu_pair(u):
    size = jnp.abs(u)
    base = 1.0 + (0.3275911 * 0.7071067811865476) * size
    guess = pl.reciprocal(base, approx=True)
    t = guess * (2.0 - base * guess)
    ex = jnp.exp2((u * u) * (-0.5 * 1.4426950408889634))
    poly = 0.5306027145 * t - 0.7265760135
    poly = poly * t + 0.7107068705
    poly = poly * t - 0.142248368
    poly = poly * t + 0.127414796
    tail = poly * t * ex
    phi = jnp.where(u >= 0.0, 1.0 - tail, tail)
    return u * phi, phi + u * (0.3989422804014327 * ex)


def norm_rows(src, dst, rows, gain, shift):
    def body(i):
        sel = rows_of(i, CHUNK)
        x = src[sel, :].astype(F32)
        centered = x - jnp.mean(x, axis=-1, keepdims=True)
        var = jnp.mean(centered * centered, axis=-1, keepdims=True)
        dst[sel, :] = (centered * lax.rsqrt(var + EPS) * gain + shift).astype(BF)

    loop(rows // CHUNK, body, unroll_of(rows // CHUNK))


def norm_back(src, grad, base, write, rows, gain):
    count = rows // CHUNK
    unroll = 3 if count % 3 == 0 else 2

    def step(i, carry):
        for u in range(unroll):
            carry = one(i * unroll + u, carry)
        return carry

    def one(i, carry):
        d_gain, d_shift = carry
        sel = rows_of(i, CHUNK)
        x = src[sel, :].astype(F32)
        dh = grad[sel, :]
        centered = x - jnp.mean(x, axis=-1, keepdims=True)
        var = jnp.mean(centered * centered, axis=-1, keepdims=True)
        rstd = lax.rsqrt(var + EPS)
        hat = centered * rstd
        g = dh * gain
        part = dh * hat
        dx = rstd * (
            g
            - jnp.mean(g, axis=-1, keepdims=True)
            - hat * jnp.mean(g * hat, axis=-1, keepdims=True)
        )
        if base is not None:
            dx = dx + base[sel, :].astype(F32)
        write(sel, dx)
        d_gain = d_gain + jnp.sum(part.reshape(CHUNK // 8, 8, D), axis=0)
        d_shift = d_shift + jnp.sum(dh.reshape(CHUNK // 8, 8, D), axis=0)
        return d_gain, d_shift

    zero = jnp.zeros((8, D), F32)
    d_gain, d_shift = lax.fori_loop(0, count // unroll, step, (zero, zero))
    return jnp.sum(d_gain, axis=0, keepdims=True), jnp.sum(d_shift, axis=0, keepdims=True)


def column_sum(ref, rows, col=0, width=D):
    def step(i, carry):
        x = ref[rows_of(i, CHUNK), pl.ds(col, width)].astype(F32)
        return carry + jnp.sum(x.reshape(CHUNK // 8, 8, width), axis=0)

    total = lax.fori_loop(0, rows // CHUNK, step, jnp.zeros((8, width), F32))
    return jnp.sum(total, axis=0, keepdims=True)


def as_bf16(flags):
    return jnp.where(flags, 1.0, 0.0).astype(BF)


def pick_matrix(order, image, start, count, low, high):
    row = order[image, :, pl.ds(start, count)].astype(F32)
    images = order.shape[0]
    col = jnp.broadcast_to(row, (8, count)).T[:, 0:1].astype(jnp.int32)
    rank = start + lax.broadcasted_iota(jnp.int32, (count, 1), 0)
    col = jnp.where((rank >= low) & (rank < high), col * images + image, -1)
    return as_bf16(col == lax.broadcasted_iota(jnp.int32, (count, PATCH * images), 1))


def place_matrix(order, image, start, count, low, high):
    row = order[image, :, pl.ds(start, count)]
    rank = start + lax.broadcasted_iota(jnp.int32, (1, count), 1)
    row = jnp.where((rank >= low) & (rank < high), row, -1)
    return as_bf16(row == lax.broadcasted_iota(jnp.int32, (PATCH, count), 0))


def flatten(rows, flat):
    flat[...] = rows[...].reshape(flat.shape)


def split_orders(order, split):
    for image in range(split.shape[0]):
        split[image] = order[image : image + 1, :]


def split_pair(pair):
    lane = lax.broadcasted_iota(jnp.int32, pair.shape, 1)
    zero = jnp.zeros_like(pair)
    return jnp.concatenate([jnp.where(lane < 64, pair, zero), jnp.where(lane < 64, zero, pair)], axis=0)


def join_rows(both):
    rows = both.shape[0] // 2
    lane = lax.broadcasted_iota(jnp.int32, (rows, 128), 1)
    return jnp.where(lane < 64, both[:rows], both[rows:])


def join_columns(both):
    rows = both.shape[1] // 2
    return jnp.concatenate([both[:64, :rows], both[64:, rows:]], axis=0).T


PAIRS = HEADS // 2
STEP = 6


def each_pair_group(images, body):
    def group(i):
        image = i // (PAIRS // STEP)
        first = (i % (PAIRS // STEP)) * STEP
        pairs = [first + step for step in range(STEP)]
        body(image, [image * PAIRS + pair for pair in pairs], [pl.ds(pl.multiple_of(pair * 128, 128), 128) for pair in pairs])

    loop(images * (PAIRS // STEP), group)


def softmax(scores, axis):
    ex = jnp.exp(scores - jnp.max(scores, axis=axis, keepdims=True))
    return (ex * (1.0 / jnp.sum(ex, axis=axis, keepdims=True))).astype(BF)


def score_back(probs, d_probs, axis):
    wide = probs.astype(F32)
    return (wide * (d_probs - jnp.sum(d_probs * wide, axis=axis, keepdims=True))).astype(BF)


def attention_by_rows(images, n, q, k, v, p, o, count_of):
    def body(image, slots, lanes):
        sel = rows_of(image, n)
        ok = lax.broadcasted_iota(jnp.int32, (1, n), 1) < count_of(image)
        scores = [nt(split_pair(q[sel, at]), k[sel, at]) for at in lanes]
        probs = [softmax(jnp.where(ok, one, -1000000000.0), 1) for one in scores]
        for slot, one in zip(slots, probs):
            p[slot] = one
        mixed = [nn(one, v[sel, at]) for one, at in zip(probs, lanes)]
        for at, one in zip(lanes, mixed):
            o[sel, at] = join_rows(one).astype(BF)

    each_pair_group(images, body)


def attention_by_columns(images, nk, q, k, v, p, o, key_ok):
    def body(image, slots, lanes):
        qs, ks = rows_of(image, NM), rows_of(image, nk)
        ok = key_ok(image)
        scores = [nt(k[ks, at], split_pair(q[qs, at])) for at in lanes]
        probs = [softmax(jnp.where(ok, one, -1000000000.0), 0) for one in scores]
        if p is not None:
            for slot, one in zip(slots, probs):
                p[slot] = one
        mixed = [tn(v[ks, at], one) for one, at in zip(probs, lanes)]
        for at, one in zip(lanes, mixed):
            o[qs, at] = join_columns(one).astype(BF)

    each_pair_group(images, body)


def attention_back_rows(images, n, q, k, v, p, do, dq, dkv):
    def body(image, slots, lanes):
        sel = rows_of(image, n)
        d_mixed = [split_pair(do[sel, at]) for at in lanes]
        d_probs = [nt(one, v[sel, at]) for one, at in zip(d_mixed, lanes)]
        d_scores = [score_back(p[slot], one, 1) for slot, one in zip(slots, d_probs)]
        d_values = [tn(p[slot], one) for slot, one in zip(slots, d_mixed)]
        d_query = [nn(one, k[sel, at]) for one, at in zip(d_scores, lanes)]
        d_keys = [tn(one, split_pair(q[sel, at])) for one, at in zip(d_scores, lanes)]
        for at, value, query, key in zip(lanes, d_values, d_query, d_keys):
            dq[sel, at] = (join_rows(query) * 0.125).astype(BF)
            dkv[sel, at] = key.astype(BF)
            dkv[sel, pl.ds(pl.multiple_of(D + at.start, 128), 128)] = value.astype(BF)

    each_pair_group(images, body)


def attention_back_columns(images, nk, q, k, v, p, do, dq, dkv):
    def body(image, slots, lanes):
        qs, ks = rows_of(image, NM), rows_of(image, nk)
        d_mixed = [split_pair(do[qs, at]) for at in lanes]
        d_probs = [nt(v[ks, at], one) for one, at in zip(d_mixed, lanes)]
        d_scores = [score_back(p[slot], one, 0) for slot, one in zip(slots, d_probs)]
        d_values = [nn(p[slot], one) for slot, one in zip(slots, d_mixed)]
        d_query = [tn(k[ks, at], one) for one, at in zip(d_scores, lanes)]
        d_keys = [nn(one, split_pair(q[qs, at])) for one, at in zip(d_scores, lanes)]
        for at, value, query, key in zip(lanes, d_values, d_query, d_keys):
            dq[qs, at] = (join_columns(query) * 0.125).astype(BF)
            dkv[ks, at] = key.astype(BF)
            dkv[ks, pl.ds(pl.multiple_of(D + at.start, 128), 128)] = value.astype(BF)

    each_pair_group(images, body)


HALF = 512


def mlp_forward(rows, h2, w1, w2, up_b, u, a, gp, acc, out, base):
    acc[...] = base()

    def body(i):
        cols = [pl.ds(pl.multiple_of((2 * i + part) * HALF, HALF), HALF) for part in range(2)]
        for part in range(2):
            u[part] = nn(h2[...], w1[:, cols[part]])
        for part in range(2):
            for c in range(0, HALF, 256):
                at = pl.ds(pl.multiple_of((2 * i + part) * HALF + c, 256), 256)
                shift = up_b[0:1, at].astype(F32)
                for r in range(0, rows, CHUNK):
                    value, slope = gelu_pair(u[part, r : r + CHUNK, c : c + 256] + shift)
                    a[r : r + CHUNK, at] = value.astype(BF)
                    if gp is not None:
                        gp[r : r + CHUNK, at] = slope.astype(BF)
            acc[...] += nn(a[:, cols[part]], w2[cols[part], :])

    loop(FF // (2 * HALF), body)
    out[...] = acc[...].astype(BF)


def mlp_back(rows, dyb, gp, w1, w2, du, u, acc, ready=lambda i, which: None):
    acc[...] = jnp.zeros_like(acc)

    def body(i):
        cols = [pl.ds(pl.multiple_of((2 * i + part) * HALF, HALF), HALF) for part in range(2)]
        ready(i, 0)
        for part in range(2):
            u[part] = nt(dyb[...], w2[cols[part], :])
        ready(i, 1)
        for part in range(2):
            for r in range(0, rows, CHUNK):
                sel = slice(r, r + CHUNK)
                du[sel, cols[part]] = (gp[sel, cols[part]].astype(F32) * u[part, sel, :]).astype(BF)
            acc[...] += nt(du[:, cols[part]], w1[:, cols[part]])

    loop(FF // (2 * HALF), body)


def project(count, rows, left, weight, first, write):
    def body(j):
        write(j, nn(left[...], weight[:, pl.ds(pl.multiple_of((first + j) * D, D), D)]))

    loop(count, body)


def set_biases(ref, bias):
    ref[0] = f32_row(bias, 0)
    ref[1] = jnp.zeros((1, D), F32)
    ref[2] = f32_row(bias, 0, D)


def cost(flops, nbytes):
    return pl.CostEstimate(flops=int(flops), bytes_accessed=int(nbytes), transcendentals=0)


def params(mib):
    return pltpu.CompilerParams(vmem_limit_bytes=mib * MIB)


def struct(shape, dtype=BF):
    return jax.ShapeDtypeStruct(shape, dtype)


def start_weights(copies, sources, scratch):
    return [copies.start(src, dst) for src, dst in zip(sources, scratch)]


def encode_kernel(group, groups, ids, visible, order_in, gains, biases, qvb, upb, rows, cot, wqkv, wo, w1, w2,
                  lat_out, x_out, hq_out, q_out, k_out, v_out, p_out, o_out, y1_out, h2_out, gp_out, a_out, *refs):
    ready, refs = refs[: 4 * groups], refs[4 * groups :]
    (order, rows_v, flat, sqkv, so, s1, s2, x, hq, qkv, p, o, y1, h2, gp, a, u, acc, shifts, lat, sems) = refs
    n = GROUP * NV
    split_orders(order_in, order)

    @pl.when(ids[0] == 0)
    def _():
        copies = Copies(sems)
        got_rows = copies.start(rows.at[0], rows_v)
        got_qkv, got_o, got_1, got_2 = start_weights(
            copies, (wqkv.at[0], wo.at[0], w1.at[0], w2.at[0]), (sqkv, so, s1, s2)
        )
        gain, bias = gains.at[0], biases.at[0]
        set_biases(shifts, qvb)
        copies.wait(got_rows)
        flatten(rows_v, flat)

        def pick_rows(i):
            image = group * GROUP + i
            pick = pick_matrix(order, image, 0, NV, 0, visible[image])
            x[rows_of(i, NV), :] = nn(pick, flat[...]).astype(BF)

        loop(GROUP, pick_rows)
        copies.start(x, x_out)
        norm_rows(x, hq, n, f32_row(gain, 0), f32_row(bias, 0))
        copies.start(hq, hq_out)
        copies.wait(got_qkv)

        def keep(j, value):
            scale = jnp.where(j == 0, 0.125, 1.0)
            qkv[j] = ((value + shifts[j]).astype(BF).astype(F32) * scale).astype(BF)

        project(3, n, hq, sqkv, 0, keep)
        q, k, v = qkv.at[0], qkv.at[1], qkv.at[2]
        copies.start(q, q_out)
        copies.start(k, k_out)
        copies.start(v, v_out)
        attention_by_rows(GROUP, NV, q, k, v, p, o, lambda i: visible[group * GROUP + i])
        copies.start(p, p_out)
        copies.start(o, o_out)
        copies.wait(got_o)
        y1[...] = nn(o[...], so[...]) + f32_row(bias, 1) + x[...].astype(F32)
        copies.start(y1, y1_out)
        norm_rows(y1, h2, n, f32_row(gain, 1), f32_row(bias, 2))
        copies.start(h2, h2_out)
        copies.wait(got_1, got_2)
        mlp_forward(n, h2, s1, s2, upb, u, a, gp, acc, lat, lambda: y1[...] + f32_row(bias, 3))
        copies.start(gp, gp_out)
        copies.start(a, a_out)
        copies.start(lat, lat_out)
        copies.finish()

    if group == groups - 1:

        @pl.when(ids[0] == 1)
        def _():
            copies = Copies(sems)
            m = GROUP * NM
            x_out, hq_out, q_out, dyb_out = (ready[i * groups : (i + 1) * groups] for i in range(4))
            gain, bias = gains.at[0], biases.at[0]
            got_rows = copies.start(rows.at[0], rows_v)
            got_q = copies.start(wqkv.at[0, :, pl.ds(0, D)], so)
            copies.wait(got_rows)
            flatten(rows_v, flat)
            got_cot = copies.start(cot.at[0], rows_v)
            top = pl.ds(0, m)

            def pick_group(g):
                def pick_rows(i):
                    image = g * GROUP + i
                    pick = pick_matrix(order, image, FIRST, NM, visible[image], PATCH)
                    x[rows_of(i, NM), :] = nn(pick, flat[...]).astype(BF)

                loop(GROUP, pick_rows)

            for g in range(groups):
                pick_group(g)
                norm_rows(x, hq, m, f32_row(gain, 0), f32_row(bias, 0))
                sent = [copies.start(x.at[top], x_out[g]), copies.start(hq.at[top], hq_out[g])]
                if g == 0:
                    copies.wait(got_q)
                q = qkv.at[g]
                q[top, :] = ((nn(hq[top, :], so[...]) + f32_row(qvb, 0)).astype(BF) * 0.125).astype(BF)
                copies.start(q.at[top], q_out[g])
                copies.wait(*sent)
            copies.wait(got_cot)
            flatten(rows_v, flat)
            for g in range(groups):
                pick_group(g)
                copies.wait(copies.start(x.at[top], dyb_out[g]))
            copies.finish()


def encode(group, groups, ids, visible, order, gains, biases, qvb, upb, rows, cot, weights):
    n = GROUP * NV
    images = order.shape[0]
    row, wide = struct((n, D)), struct((n, FF))
    heads = struct((GROUP * PAIRS, 2 * NV, NV))
    outs = [row] * 6 + [heads, row, struct((n, D), F32), row, wide, wide] + [struct((GROUP * NM, D))] * (4 * groups)
    vm = lambda s: pltpu.VMEM(s.shape, s.dtype)
    scratch = [
        pltpu.VMEM((images, 1, PATCH), jnp.int32),
        pltpu.VMEM((PATCH, images, D), BF), pltpu.VMEM((PATCH * images, D), BF),
        pltpu.VMEM((D, 3 * D), BF), pltpu.VMEM((D, D), BF), pltpu.VMEM((D, FF), BF), pltpu.VMEM((FF, D), BF),
        vm(row), vm(row), pltpu.VMEM((3, n, D), BF), vm(heads), vm(row), pltpu.VMEM((n, D), F32), vm(row),
        vm(wide), vm(wide), pltpu.VMEM((2, n, HALF), F32), pltpu.VMEM((n, D), F32), pltpu.VMEM((3, 1, D), F32), vm(row),
        pltpu.SemaphoreType.DMA((24,)),
    ]
    got = pl.pallas_call(
        partial(encode_kernel, group, groups),
        in_specs=[SMEM, SMEM] + [VMEM] * 5 + [HBM] * 6,
        out_specs=[HBM] * len(outs),
        out_shape=outs,
        scratch_shapes=scratch,
        compiler_params=params(LIMIT),
        cost_estimate=cost(2 * n * 12 * D * D, 25e6),
        name="encode",
    )(ids, visible, order, gains, biases, qvb, upb, rows, cot, *weights)
    ready = got[12:]
    return got[:12], [ready[i * groups : (i + 1) * groups] for i in range(4)]


def middle_kernel(group, ids, visible, order_in, gains, biases, qvb, upb, tgains, tbiases, tqvb, tupb,
                  rows, lat_in, x_in, q_in, dyb_in, wqkv, wo, w1, w2, tqkv, to, t1, t2,
                  dlat_out, res_out, hk_out, dq_out, dkv_out, o_out, dy1b_out, h2_out, du_out, a_out,
                  dy1_out, sums_out,
                  order, rows_v, flat, sqkv, so, s1, s2, x, lat, hq, hk, q, kv, p, o, y1, h2, gp, a, u, acc, shifts,
                  res, dyb, du, dy1, dy1b, do, dq, dkv, dh, dlat, sums, sems):
    n, m = GROUP * NM, GROUP * NV
    top = pl.ds(0, n)
    k, v = kv.at[0], kv.at[1]
    split_orders(order_in, order)

    def forward(copies, got_weights, gain, bias, ub, nk, key_ok, keep_p, keep_slope):
        got_o, got_1, got_2 = got_weights
        attention_by_columns(GROUP, nk, q, k, v, keep_p, o, key_ok)
        copies.wait(got_o)
        y1[...] = nn(o[...], so[...]) + f32_row(bias, 1) + x[...].astype(F32)
        norm_rows(y1, h2, n, f32_row(gain, 1), f32_row(bias, 2))
        copies.wait(got_1, got_2)
        mlp_forward(n, h2, s1, s2, ub, u, a, keep_slope, acc, res, lambda: y1[...] + f32_row(bias, 3))
        copies.start(res, res_out)

    @pl.when(ids[0] == 0)
    def _():
        copies = Copies(sems)
        gain, bias = tgains, tbiases
        got_rows = copies.start(rows.at[0], rows_v)
        got_qkv = copies.start(tqkv, sqkv)
        got_weights = start_weights(copies, (to, t1, t2), (so, s1, s2))
        copies.wait(got_rows)
        flatten(rows_v, flat)

        def pick_rows(i):
            image = group * GROUP + i
            pick = pick_matrix(order, image, FIRST, NM, visible[image], PATCH)
            x[rows_of(i, NM), :] = nn(pick, flat[...]).astype(BF)

        loop(GROUP, pick_rows)
        norm_rows(x, hq, n, f32_row(gain, 0), f32_row(bias, 0))
        copies.wait(got_qkv)
        set_biases(shifts, tqvb)
        q[...] = ((nn(hq[...], sqkv[:, :D]) + f32_row(tqvb, 0)).astype(BF) * 0.125).astype(BF)

        def keep_kv(j, value):
            kv[j, top, :] = (value + shifts[j + 1]).astype(BF)

        project(2, n, hq, sqkv, 1, keep_kv)

        def key_ok(i):
            return lax.broadcasted_iota(jnp.int32, (NM, 1), 0) + FIRST >= visible[group * GROUP + i]

        forward(copies, got_weights, gain, bias, tupb, NM, key_ok, None, None)
        copies.finish()

    @pl.when(ids[0] == 1)
    def _():
        copies = Copies(sems)
        gain, bias = gains.at[0], biases.at[0]
        got_lat = copies.start(lat_in, lat)
        got_kv = copies.start(wqkv.at[0, :, pl.ds(D, 2 * D)], sqkv.at[:, pl.ds(D, 2 * D)])
        got_q = copies.start(q_in, q)
        got_x = copies.start(x_in, x)
        got_weights = start_weights(copies, (wo.at[0], w1.at[0], w2.at[0]), (so, s1, s2))
        got_dyb = copies.start(dyb_in, dyb)
        copies.wait(got_lat)
        norm_rows(lat, hk, m, f32_row(gain, 0), f32_row(bias, 0))
        copies.start(hk, hk_out)
        copies.wait(got_kv)
        set_biases(shifts, qvb)

        def keep_kv(j, value):
            kv[j] = (value + shifts[j + 1]).astype(BF)

        project(2, m, hk, sqkv, 1, keep_kv)
        copies.wait(got_q, got_x)

        def key_ok(i):
            return lax.broadcasted_iota(jnp.int32, (NV, 1), 0) < visible[group * GROUP + i]

        forward(copies, got_weights, gain, bias, upb.at[0:1], NV, key_ok, p, gp)
        copies.start(o, o_out)
        copies.start(h2, h2_out)
        copies.start(a, a_out)
        copies.wait(got_dyb)
        mlp_back(n, dyb, gp, s1, s2, du, u, acc)
        copies.start(du, du_out)

        def keep(sel, dx):
            dy1[sel, :] = dx
            dy1b[sel, :] = dx.astype(BF)

        g2, b2 = norm_back(y1, acc, dyb, keep, n, f32_row(gain, 1))
        copies.start(dy1, dy1_out)
        copies.start(dy1b, dy1b_out)
        do[...] = nt(dy1b[...], so[...]).astype(BF)
        attention_back_columns(GROUP, NV, q, k, v, p, do, dq, dkv)
        copies.start(dq, dq_out)
        copies.start(dkv, dkv_out)
        dh[...] = nt(dkv[:, :D], sqkv[:, D : 2 * D])
        dh[...] += nt(dkv[:, D:], sqkv[:, 2 * D :])

        def keep_side(sel, dx):
            dlat[sel, :] = dx.astype(BF)

        gk, bk = norm_back(lat, dh, None, keep_side, m, f32_row(gain, 0))
        copies.start(dlat, dlat_out)
        for row, value in enumerate((gk, g2, bk, b2)):
            sums[pl.ds(row, 1), :] = value
        copies.start(sums, sums_out)
        copies.finish()


def middle(group, ids, visible, order, own_vecs, target_vecs, rows, lat, x, q, dyb, weights, targets):
    n, m = GROUP * NM, GROUP * NV
    row, side, wide = struct((n, D)), struct((m, D)), struct((n, FF))
    pair = struct((m, 2 * D))
    outs = [side, row, side, row, pair, row, row, row, wide, wide, struct((n, D), F32), struct((8, D), F32)]
    vm = lambda s: pltpu.VMEM(s.shape, s.dtype)
    full, fside = pltpu.VMEM((n, D), F32), pltpu.VMEM((m, D), F32)
    scratch = [
        pltpu.VMEM((order.shape[0], 1, PATCH), jnp.int32),
        pltpu.VMEM((PATCH, order.shape[0], D), BF), pltpu.VMEM((PATCH * order.shape[0], D), BF),
        pltpu.VMEM((D, 3 * D), BF), pltpu.VMEM((D, D), BF), pltpu.VMEM((D, FF), BF), pltpu.VMEM((FF, D), BF),
        vm(row), vm(side), vm(row), vm(side), vm(row), pltpu.VMEM((2, m, D), BF),
        pltpu.VMEM((GROUP * PAIRS, NV, 2 * NM), BF), vm(row), full, vm(row), vm(wide), vm(wide),
        pltpu.VMEM((2, n, HALF), F32), full, pltpu.VMEM((3, 1, D), F32),
        vm(row), vm(row), vm(wide), full, vm(row), vm(row), vm(row), vm(pair), fside, vm(side),
        pltpu.VMEM((8, D), F32),
        pltpu.SemaphoreType.DMA((24,)),
    ]
    return pl.pallas_call(
        partial(middle_kernel, group),
        in_specs=[SMEM, SMEM] + [VMEM] * 9 + [HBM] * 13,
        out_specs=[HBM] * len(outs),
        out_shape=outs,
        scratch_shapes=scratch,
        compiler_params=params(LIMIT),
        cost_estimate=cost(4 * n * 12 * D * D, 25e6),
        name="middle",
    )(ids, visible, order, *own_vecs, *target_vecs, rows, lat, x, q, dyb, *weights, *targets)


def stack_rows(copies, pieces, ref, size):
    return [copies.start(piece, ref.at[pl.ds(i * size, size)]) for i, piece in enumerate(pieces)]


def clear_tail(ref, used):
    ref[pl.ds(used, ref.shape[0] - used), :] = jnp.zeros((ref.shape[0] - used, ref.shape[1]), ref.dtype)


def halves(count, blocks):
    rows = D // 16
    if count == 16:
        return [struct((2, 2, 2, blocks, rows, D))] + [struct((2, blocks, rows, D))] * 4
    return [struct((D, D))] * blocks


def give_blocks(copies, core, tree, left_right, out, dest):
    size = 8 if tree else 1
    blocks = out.shape[0]
    first = copies.take(blocks * size)

    def send(j, act):
        if not tree:
            for block in range(blocks):
                pl.when(j == block)(lambda block=block: act(out.at[block], dest[block], first + block))
            return
        view = out.at[j].reshape(2, 2, 2, 2, D // 16, D)
        for x in range(2):
            for low in range(2):
                at = first + j * size + 4 * x + 2 * low
                act(view.at[:, low, x, core], dest[0].at[x, low, :, j], at)
                act(view.at[:, low, x, 1 - core], dest[1 + 2 * x + low].at[:, j], at + 1)

    def body(j):
        out[j] = left_right(j)
        send(j, copies.begin)

    loop(blocks, body)
    loop(blocks, lambda j: send(j, copies.wait_at))


def give_rows(copies, core, tree, multiply, out, dest):
    size = 4 if tree else 1
    first = copies.take(4 * size)

    def send(j, act):
        if not tree:
            act(out.at[j], dest[0].at[pl.ds(pl.multiple_of(j * D, D), D)], first + j)
            return
        view = out.at[j].reshape(2, 2, D // 4, D)
        low, high = lax.rem(j, 2), lax.div(j, 2)
        for x in range(2):
            at = first + j * size + 2 * x
            act(view.at[x, core], dest[0].at[x, low, high, 0], at)
            act(view.at[x, 1 - core], dest[1].at[x, low, high, 0], at + 1)

    def body(j):
        out[j] = multiply(j)
        send(j, copies.begin)

    loop(4, body)
    loop(4, lambda j: send(j, copies.wait_at))


def down_kernel(groups, parts, ids, *refs):
    cot, lat, a_enc, a_reg, dyb_reg = (refs[i * groups : (i + 1) * groups] for i in range(5))
    refs = refs[5 * groups :]
    dest, refs = refs[:parts], refs[parts:]
    sums_out, cot_v, dyb, a, dlat, out, sums, sems = refs
    images = groups * GROUP
    nv, nm = GROUP * NV, GROUP * NM

    @pl.when(ids[0] == 0)
    def _():
        copies = Copies(sems)
        got = stack_rows(copies, cot, cot_v, nv) + stack_rows(copies, lat, dlat, nv)
        stack_rows(copies, a_enc, a, nv)
        copies.wait(*got)
        dyb[...] = (cot_v[...].astype(F32) + dlat[...].astype(F32)).astype(BF)
        copies.finish()

    @pl.when(ids[0] == 1)
    def _():
        copies = Copies(sems)
        stack_rows(copies, a_reg, a, nm)
        stack_rows(copies, dyb_reg, dyb, nm)
        clear_tail(a, images * NM)
        clear_tail(dyb, images * NM)
        copies.finish()

    copies = Copies(sems)

    def multiply(j):
        return tn(a[:, pl.ds(pl.multiple_of(j * D, D), D)], dyb[...]).astype(BF)

    give_rows(copies, ids[1], parts == 2, multiply, out, dest)
    sums[...] = jnp.broadcast_to(column_sum(dyb, images * NV), (8, D))
    copies.start(sums, sums_out)
    copies.finish()


def down_grad(groups, count, ids, cot, dlat, a_enc, a_reg, dyb_reg):
    n = groups * GROUP * NV
    main = [struct((2, 2, 2, 1, D // 4, D))] * 2 if count == 16 else [struct((FF, D))]
    outs = main + [struct((8, D), F32)]
    row = pltpu.VMEM((n, D), BF)
    scratch = [
        row, row, pltpu.VMEM((n, FF), BF), row, pltpu.VMEM((4, D, D), BF), pltpu.VMEM((8, D), F32),
        pltpu.SemaphoreType.DMA((24,)),
    ]
    got = pl.pallas_call(
        partial(down_kernel, groups, len(main)),
        in_specs=[SMEM] + [HBM] * (5 * groups),
        out_specs=[HBM] * len(outs),
        out_shape=outs,
        scratch_shapes=scratch,
        compiler_params=params(LIMIT),
        cost_estimate=cost(1e6, 1e5),
        name="down_grad",
    )(ids, *cot, *dlat, *a_enc, *a_reg, *dyb_reg)
    return got[: len(main)], got[-1]


def mlp_kernel(first, groups, ids, visible, order_in, gains, cot, dlat_in, w1, w2, y1_in, gp_in, *refs):
    if first:
        picked, refs = refs[:groups], refs[groups:]
    du_out, dy1_out, dy1b_out, sums_out, order, rows_v, flat, refs = *refs[:7], refs[7:]
    s1, s2, cot_v, dlat, dyb, gp, y1, du, u, acc, dy1, dy1b, sums, sems = refs
    n = GROUP * NV
    third = FF // 3

    @pl.when(ids[0] == 0)
    def _():
        copies = Copies(sems)
        got = [copies.start(dlat_in, dlat)]
        if first:
            got_rows = copies.start(cot.at[0], rows_v)
        else:
            got.append(copies.start(cot, cot_v))
        start = copies.take(9)

        def parts(i):
            cols = pl.ds(pl.multiple_of(i * third, third), third)
            return (
                (w2.at[0, cols, :], s2.at[cols, :]),
                (gp_in.at[:, cols], gp.at[:, cols]),
                (w1.at[0, :, cols], s1.at[:, cols]),
            )

        for i in range(3):
            for k, (src, dst) in enumerate(parts(i)):
                copies.begin(src, dst, start + 3 * i + k)
        got_y = copies.start(y1_in, y1)

        def ready(i, which):
            for k in ((0, 1), (2,))[which]:
                copies.wait_at(*parts(i)[k], start + 3 * i + k)

        if first:
            split_orders(order_in, order)
            copies.wait(got_rows)
            flatten(rows_v, flat)
            for g in reversed(range(groups)):

                def pick_rows(i, g=g):
                    image = g * GROUP + i
                    pick = pick_matrix(order, image, 0, NV, 0, visible[image])
                    cot_v[rows_of(i, NV), :] = nn(pick, flat[...]).astype(BF)

                loop(GROUP, pick_rows)
                copies.wait(copies.start(cot_v, picked[g]))
        copies.wait(*got)
        dyb[...] = (cot_v[...].astype(F32) + dlat[...].astype(F32)).astype(BF)
        mlp_back(n, dyb, gp, s1, s2, du, u, acc, ready)
        copies.start(du, du_out)
        copies.wait(got_y)

        def keep(sel, dx):
            dy1[sel, :] = dx
            dy1b[sel, :] = dx.astype(BF)

        g2, b2 = norm_back(y1, acc, dyb, keep, n, f32_row(gains.at[0], 1))
        copies.start(dy1, dy1_out)
        copies.start(dy1b, dy1b_out)
        sums[pl.ds(0, 1), :] = g2
        sums[pl.ds(1, 1), :] = b2
        copies.start(sums, sums_out)
        copies.finish()


def mlp_grad(first, groups, ids, visible, order, gains, cot, dlat, w1, w2, y1, gp):
    n = GROUP * NV
    images = order.shape[0]
    row, wide, full = pltpu.VMEM((n, D), BF), pltpu.VMEM((n, FF), BF), pltpu.VMEM((n, D), F32)
    outs = [struct((n, D))] * (groups if first else 0) + [struct((n, FF)), struct((n, D), F32), struct((n, D)), struct((8, D), F32)]
    got = pl.pallas_call(
        partial(mlp_kernel, first, groups),
        in_specs=[SMEM, SMEM, VMEM, VMEM] + [HBM] * 6,
        out_specs=[HBM] * len(outs),
        out_shape=outs,
        scratch_shapes=[
            pltpu.VMEM((images, 1, PATCH), jnp.int32),
            pltpu.VMEM((PATCH, images, D), BF), pltpu.VMEM((PATCH * images, D), BF),
            pltpu.VMEM((D, FF), BF), pltpu.VMEM((FF, D), BF), row, row, row, wide, full, wide,
            pltpu.VMEM((2, n, HALF), F32), full, full, row, pltpu.VMEM((8, D), F32), pltpu.SemaphoreType.DMA((24,)),
        ],
        compiler_params=params(LIMIT),
        cost_estimate=cost(1e6, 1e5),
        name="mlp_grad",
    )(ids, visible, order, gains, cot, dlat, w1, w2, y1, gp)
    return got[:-4], got[-4:]


def up_kernel(groups, parts, ids, *refs):
    pieces = [refs[i * groups : (i + 1) * groups] for i in range(8)]
    refs = refs[8 * groups :]
    dest, refs = refs[:parts], refs[parts:]
    sums_out, left, right, out, sums, sems = refs
    images = groups * GROUP

    def load(du, h2, dy1b, o, size):
        copies = Copies(sems)
        stack_rows(copies, h2, left.at[0], size)
        for j in range(4):
            stack_rows(copies, [one.at[:, pl.ds(j * D, D)] for one in du], right.at[j], size)
        stack_rows(copies, o, left.at[1], size)
        stack_rows(copies, dy1b, right.at[4], size)
        return copies

    @pl.when(ids[0] == 0)
    def _():
        load(*pieces[:4], GROUP * NV).finish()

    @pl.when(ids[0] == 1)
    def _():
        copies = load(*pieces[4:], GROUP * NM)
        for ref in (left, right):
            for i in range(ref.shape[0]):
                clear_tail(ref.at[i], images * NM)
        copies.finish()

    copies = Copies(sems)

    def multiply(j):
        value = tn(left[lax.div(j, 4)], right[j]).astype(BF)
        sums[pl.ds(j, 1), :] = column_sum(right.at[j], images * NV)
        return value

    give_blocks(copies, ids[1], dest[0].ndim == 6, multiply, out, dest)
    copies.start(sums, sums_out)
    copies.finish()


def up_grad(groups, count, ids, *pieces):
    n = groups * GROUP * NV
    main = halves(count, 5)
    outs = main + [struct((8, D), F32)]
    got = pl.pallas_call(
        partial(up_kernel, groups, len(main)),
        in_specs=[SMEM] + [HBM] * (8 * groups),
        out_specs=[HBM] * len(outs),
        out_shape=outs,
        scratch_shapes=[
            pltpu.VMEM((2, n, D), BF), pltpu.VMEM((5, n, D), BF), pltpu.VMEM((5, D, D), BF), pltpu.VMEM((8, D), F32),
            pltpu.SemaphoreType.DMA((44,)),
        ],
        compiler_params=params(LIMIT),
        cost_estimate=cost(1e6, 1e5),
        name="up_grad",
    )(ids, *[ref for piece in pieces for ref in piece])
    return got[: len(main)], got[-1]


def attn_kernel(ids, gains, wqkv, wo, dy1_enc, q_in, k_in, v_in, p_in, x_enc, dq_reg, dy1_reg, x_reg,
                dq_out, dkv_out, dx_out, sums_out,
                sqkv, so, dy1, dy1b, q, k, v, p, x, do, dq, dkv, dh, sums, sems):
    m = GROUP * NM
    top = pl.ds(0, m)
    gain = f32_row(gains.at[0], 0)

    def finish(copies, rows):
        def keep(sel, dx):
            dy1[sel, :] = dx

        g1, b1 = norm_back(x, dh, dy1, keep, rows, gain)
        copies.start(dy1, dx_out)
        sums[0:1, :] = g1
        sums[1:2, :] = b1
        copies.start(sums, sums_out)
        copies.finish()

    @pl.when(ids[0] == 0)
    def _():
        copies = Copies(sems)
        got = [copies.start(dy1_enc, dy1), copies.start(wo.at[0], so)]
        later = [copies.start(src, dst) for src, dst in ((v_in, v), (p_in, p), (k_in, k), (q_in, q))]
        last = [copies.start(wqkv.at[0], sqkv), copies.start(x_enc, x)]
        copies.wait(*got)
        dy1b[...] = dy1[...].astype(BF)
        do[...] = nt(dy1b[...], so[...]).astype(BF)
        copies.wait(*later)
        attention_back_rows(GROUP, NV, q, k, v, p, do, dq, dkv)
        copies.start(dq, dq_out)
        copies.start(dkv, dkv_out)
        copies.wait(*last)
        dh[...] = nt(dq[...], sqkv[:, 0:D])
        for j in range(2):
            dh[...] += nt(dkv[:, j * D : (j + 1) * D], sqkv[:, (j + 1) * D : (j + 2) * D])
        finish(copies, GROUP * NV)

    @pl.when(ids[0] == 1)
    def _():
        copies = Copies(sems)
        for src, dst in ((dq_reg, dq), (dy1_reg, dy1), (x_reg, x)):
            copies.start(src, dst.at[top])
        copies.start(wqkv.at[0, :, pl.ds(0, D)], sqkv.at[:, pl.ds(0, D)])
        copies.finish()
        dh[top, :] = nt(dq[top, :], sqkv[:, 0:D])
        finish(copies, m)


def attn_back(ids, gains, wqkv, wo, *pieces):
    n = GROUP * NV
    row, full = pltpu.VMEM((n, D), BF), pltpu.VMEM((n, D), F32)
    outs = [struct((n, D)), struct((n, 2 * D)), struct((n, D), F32), struct((8, D), F32)]
    return pl.pallas_call(
        attn_kernel,
        in_specs=[SMEM, VMEM] + [HBM] * (2 + len(pieces)),
        out_specs=[HBM] * len(outs),
        out_shape=outs,
        scratch_shapes=[
            pltpu.VMEM((D, 3 * D), BF), pltpu.VMEM((D, D), BF), full, row, row, row, row,
            pltpu.VMEM((GROUP * PAIRS, 2 * NV, NV), BF), row, row, row, pltpu.VMEM((n, 2 * D), BF), full,
            pltpu.VMEM((8, D), F32), pltpu.SemaphoreType.DMA((20,)),
        ],
        compiler_params=params(LIMIT),
        cost_estimate=cost(1e6, 1e5),
        name="attn_back",
    )(ids, gains, wqkv, wo, *pieces)


def qkv_kernel(groups, parts, ids, down_sums, up_sums, *refs):
    mlp_sums, reg_sums, in_sums = (refs[i * groups : (i + 1) * groups] for i in range(3))
    refs = refs[3 * groups :]
    pieces = [refs[i * groups : (i + 1) * groups] for i in range(7)]
    dq_enc, dkv_enc, hq_enc, hq_reg, hk_reg, dq_reg, dkv_reg = pieces
    refs = refs[7 * groups :]
    dest, refs = refs[:parts], refs[parts:]
    small, left, right, out, sems = refs
    images = groups * GROUP
    nv, nm = GROUP * NV, GROUP * NM
    hk, hq = left.at[0], left.at[1]
    dk, dv, dq = (right.at[i] for i in range(3))

    @pl.when(ids[0] == 0)
    def _():
        copies = Copies(sems)
        stack_rows(copies, hq_enc, hk, nv)
        stack_rows(copies, [one.at[:, pl.ds(0, D)] for one in dkv_enc], dk, nv)
        stack_rows(copies, [one.at[:, pl.ds(D, D)] for one in dkv_enc], dv, nv)
        stack_rows(copies, hq_enc, hq, nv)
        stack_rows(copies, dq_enc, dq, nv)
        copies.finish()

    @pl.when(ids[0] == 1)
    def _():
        copies = Copies(sems)
        for piece, ref in ((hq_reg, hq), (dq_reg, dq)):
            stack_rows(copies, piece, ref, nm)
            clear_tail(ref, images * NM)
        stack_rows(copies, hk_reg, hk, nv)
        stack_rows(copies, [one.at[:, pl.ds(0, D)] for one in dkv_reg], dk, nv)
        stack_rows(copies, [one.at[:, pl.ds(D, D)] for one in dkv_reg], dv, nv)
        copies.finish()

    copies = Copies(sems)

    def multiply(j):
        return tn(left[lax.div(j, 2)], right[j]).astype(BF)

    give_blocks(copies, ids[1], dest[0].ndim == 6, multiply, out, dest)

    def total_of(sums):
        total = sums[0][...]
        for more in sums[1:]:
            total = total + more[...]
        return total

    first, mlp, reg = total_of(in_sums), total_of(mlp_sums), total_of(reg_sums)
    encoder = ids[0] == 0
    small[0:1, :] = first[0:1, :] + jnp.where(encoder, 0.0, reg[0:1, :])
    small[1:2, :] = jnp.where(encoder, mlp[0:1, :], reg[1:2, :])
    small[2:3, :] = first[1:2, :] + jnp.where(encoder, 0.0, reg[2:3, :])
    small[3:4, :] = up_sums[4:5, :]
    small[4:5, :] = jnp.where(encoder, mlp[1:2, :], reg[3:4, :])
    small[5:6, :] = down_sums[0:1, :]
    small[6:7, :] = column_sum(dq, images * NV)
    small[7:8, :] = column_sum(dv, images * NV)
    small[8:12, :] = up_sums[0:4, :]
    small[12:16, :] = jnp.zeros((4, D), F32)
    copies.finish()


def qkv_grad(groups, count, ids, sums, *pieces):
    n = groups * GROUP * NV
    row = pltpu.VMEM((n, D), BF)
    main = halves(count, 3)
    outs = main + [struct((16, D), F32)]
    scratch = [
        pltpu.VMEM((2, n, D), BF), pltpu.VMEM((3, n, D), BF), pltpu.VMEM((3, D, D), BF),
        pltpu.SemaphoreType.DMA((40,)),
    ]
    got = pl.pallas_call(
        partial(qkv_kernel, groups, len(main)),
        in_specs=[SMEM] + [VMEM] * (2 + 3 * groups) + [HBM] * (7 * groups),
        out_specs=[HBM] * len(main) + [VMEM],
        out_shape=outs,
        scratch_shapes=scratch,
        compiler_params=params(LIMIT),
        cost_estimate=cost(1e6, 1e5),
        name="qkv_grad",
    )(ids, *sums, *[ref for piece in pieces for ref in piece])
    return got[: len(main)], got[-1]


def place_kernel(groups, ids, visible, order_in, *refs):
    dx_in, lat_enc, res = (refs[i * groups : (i + 1) * groups] for i in range(3))
    block_out, grad_out, order, dx, lat, out, grads, sems = refs[3 * groups :]
    images = groups * GROUP
    nv, nm = GROUP * NV, GROUP * NM
    split_orders(order_in, order)

    def put_grad(i, put, value):
        high = value.astype(BF)
        low = (value - high.astype(F32)).astype(BF)
        grads[i] = nn(put, high) + nn(put, low)

    def write_grads():
        copies = Copies(sems)
        for i in range(images):
            copies.start(grads.at[i], grad_out.at[0, :, i, :])
        copies.finish()

    @pl.when(ids[0] == 0)
    def _():
        copies = Copies(sems)
        for piece, ref, size in ((dx_in, dx, nv), (lat_enc, lat, nv), (res, out, nm)):
            stack_rows(copies, piece, ref, size)
        copies.finish()

        def put_image(i):
            put = place_matrix(order, i, 0, NV, 0, visible[i])
            put_side = place_matrix(order, i, FIRST, NM, visible[i], PATCH)
            put_grad(i, put, dx[rows_of(i, NV), :])
            block_out[0, i] = (nn(put, lat[rows_of(i, NV), :]) + nn(put_side, out[rows_of(i, NM), :])).astype(BF)

        loop(images, put_image)
        write_grads()

    @pl.when(ids[0] == 1)
    def _():
        copies = Copies(sems)
        stack_rows(copies, res, out, nm)
        stack_rows(copies, [piece.at[pl.ds(0, nm)] for piece in dx_in], dx, nm)
        copies.finish()

        def put_image(i):
            put = place_matrix(order, i, FIRST, NM, visible[i], PATCH)
            put_grad(i, put, dx[rows_of(i, NM), :])
            block_out[0, i] = nn(put, out[rows_of(i, NM), :]).astype(BF)

        loop(images, put_image)
        write_grads()


def place(groups, ids, visible, order, *pieces):
    images = groups * GROUP
    n = images * NV
    outs = [struct((1, images, PATCH, D)), struct((1, PATCH, images, D), F32)]
    return pl.pallas_call(
        partial(place_kernel, groups),
        in_specs=[SMEM, SMEM, VMEM] + [HBM] * (3 * groups),
        out_specs=[VMEM, HBM],
        out_shape=outs,
        scratch_shapes=[
            pltpu.VMEM((images, 1, PATCH), jnp.int32), pltpu.VMEM((n, D), F32), pltpu.VMEM((n, D), BF),
            pltpu.VMEM((images * NM, D), BF), pltpu.VMEM((images, PATCH, D), F32), pltpu.SemaphoreType.DMA((8,)),
        ],
        compiler_params=params(LIMIT),
        cost_estimate=cost(1e6, 1e5),
        name="place",
    )(ids, visible, order, *[ref for piece in pieces for ref in piece])


BITS = (2, 4, 8)


def hop(value, bit):
    return lax.ppermute(value, "dp", [(i, i ^ bit) for i in range(16)])


def combine_kernel(jobs, given, ids, *refs):
    used = sum(sum(4 if gone is None else 1 for gone in terms) for terms, *_ in jobs)
    inputs, outs, scratch = list(refs[:used]), list(refs[used : used + given]), list(refs[used + given :])
    copies = Copies(scratch.pop())
    plans = []

    def fetch(term, gone, bits, own):
        if gone is not None:
            path = tuple(bits[gone:])
            copy = copies.start(term.at[path] if path else term, own)
            return lambda: copies.wait(copy)
        wide = len(bits) == 1
        first = copies.take(2 if wide else 1)
        rest = tuple(bits[2:])

        def piece(x, low):
            ref = term[2 * x + low]
            return ref.at[rest] if rest else ref

        for x in range(2):
            for low in range(2):
                if wide:
                    pl.when(bits[0] == x)(
                        lambda x=x, low=low: copies.begin(piece(x, low), own.at[low], first + low)
                    )
                else:
                    pl.when((bits[0] == x) & (bits[1] == low))(
                        lambda x=x, low=low: copies.begin(piece(x, low), own, first)
                    )

        def wait():
            if wide:
                for low in range(2):
                    copies.wait_at(piece(0, low), own.at[low], first + low)
            else:
                copies.wait_at(piece(0, 0), own, first)

        return wait

    for kinds, first, last, targets, finals in jobs:
        terms = [inputs.pop(0) if gone is not None else [inputs.pop(0) for _ in range(4)] for gone in kinds]
        for target in targets:
            bits = []
            for bit in range(last):
                flip = bit >= first and (target >> (bit - first)) & 1
                bits.append(1 - ids[2 + bit] if flip else ids[2 + bit])
            owns = [scratch.pop(0) for _ in kinds]
            waits = [fetch(term, gone, bits, own) for term, gone, own in zip(terms, kinds, owns)]
            plans.append((waits, owns, last, finals, None if finals else outs.pop(0)))
    for waits, owns, last, finals, out in plans:
        for wait in waits:
            wait()
        spots = [()]
        for _ in range(3 - last):
            spots = [spot + (i,) for spot in spots for i in range(2)]
        for spot in spots:
            for j in range(owns[0].shape[-3]):
                value = owns[0][spot + (j,)].astype(F32)
                for more in owns[1:]:
                    value = value + more[spot + (j,)].astype(F32)
                if finals:
                    which, column = finals[j]
                    outs[which][:, column * D : (column + 1) * D] = value
                else:
                    out[spot + (j,)] = value.astype(BF)


def send_job(terms, first, last, targets=(1,)):
    return terms, first, last, targets, None


def final_job(terms, finals):
    return terms, 0, 3, (0,), finals


def combine(ids, *jobs, outs=()):
    shapes = [struct(shape, F32) for shape in outs]
    plans, inputs, scratch = [], [], []
    for terms, first, last, targets, finals in jobs:
        blocks, rows = terms[0].shape[-3:-1]
        kinds = tuple(None if isinstance(term, list) else 6 - term.ndim for term in terms)
        for term in terms:
            inputs += term if isinstance(term, list) else [term]
        plans.append((kinds, first, last, targets, finals))
        part = (2,) * (3 - last) + (blocks, rows, D)
        for _ in targets:
            scratch += [pltpu.VMEM(part, BF) for _ in terms]
            if finals is None:
                shapes.append(struct(part))
    scratch.append(pltpu.SemaphoreType.DMA((2 * len(scratch),)))
    return pl.pallas_call(
        partial(combine_kernel, tuple(plans), len(shapes)),
        in_specs=[SMEM] + [HBM] * len(inputs),
        out_specs=[VMEM] * len(shapes),
        out_shape=shapes,
        scratch_shapes=scratch,
        compiler_params=params(LIMIT),
        cost_estimate=cost(1e5, 1e4),
        name="combine",
    )(ids, *inputs)


def in_order(first, then):
    return lax.optimization_barrier((first, then))


def own_columns(rows, count):
    own = D // count
    me = lax.axis_index("dp")

    def part(block, wide):
        return lax.dynamic_slice_in_dim(block, me * wide, wide, block.ndim - 1)

    return (
        part(rows[:2], own),
        part(rows[2:6], own),
        part(rows[6:8].reshape(-1), 2 * own),
        part(rows[8:12].reshape(-1), 4 * own),
    )


def scatter_natural(block):
    shards = block.reshape(lax.axis_size("dp"), -1, D)
    return lax.psum_scatter(shards, "dp", scatter_dimension=0, tiled=True)[0].astype(F32)


def local(
    patch_rows, cotangent, patch_order, visible, qkv_weight, out_weight, up_weight, down_weight, norm_gains, biases,
    qv_bias, up_bias, target_qkv, target_out, target_up, target_down, target_gains, target_biases, target_qv_bias,
    target_up_bias,
):
    count = lax.axis_size("dp")
    tree = count == 16
    place_dp = lax.axis_index("dp")
    bits = [(place_dp // bit) % 2 for bit in (1,) + BITS]
    ids = jnp.stack([lax.axis_index("section")] + bits).astype(jnp.int32)
    groups = patch_order.shape[0] // GROUP
    weights = (qkv_weight, out_weight, up_weight, down_weight)
    targets = (target_qkv, target_out, target_up, target_down)
    vecs = (norm_gains, biases, qv_bias, up_bias)
    target_vecs = (target_gains, target_biases, target_qv_bias[None], target_up_bias[None])

    rows, cot = patch_rows.transpose(0, 2, 1, 3), cotangent.transpose(0, 2, 1, 3)
    calls = [
        encode(g, groups, ids, visible, patch_order, *vecs, rows, cot, weights) for g in range(groups)
    ]
    lat, x_e, hq_e, q_e, k_e, v_e, p_e, o_e, y1_e, h2_e, gp_e, a_e = zip(*[call[0] for call in calls])
    x_r, hq_r, q_r, dyb_r = calls[-1][1]
    sent = [lax.ppermute(piece, "section", [(0, 1)]) for piece in lat]
    middles = [
        middle(g, ids, visible, patch_order, vecs, target_vecs, rows, sent[g], x_r[g], q_r[g], dyb_r[g], weights, targets)
        for g in range(groups)
    ]
    dlat, res, hk_r, dq_r, dkv_r, o_r, dy1b_r, h2_r, du_r, a_r, dy1_r, sums_r = zip(*middles)
    back = [lax.ppermute(piece, "section", [(1, 0)]) for piece in dlat]

    def mlp(g, cot):
        return mlp_grad(
            g == 0, groups, ids, visible, patch_order, norm_gains, cot, back[g], up_weight, down_weight, y1_e[g], gp_e[g]
        )

    def attention(g, dy1):
        return attn_back(
            ids, norm_gains, qkv_weight, out_weight, dy1, q_e[g], k_e[g], v_e[g], p_e[g], x_e[g],
            dq_r[g], dy1_r[g], x_r[g],
        )

    cot_e, first = mlp(0, cot)
    mlps = [first] + [mlp(g, cot_e[g])[1] for g in range(1, groups - 1)]
    attns = [attention(g, mlps[g][1]) for g in range(groups - 1)]
    last = groups - 1
    send = partial(combine, ids)
    attns, back[last] = in_order(attns, back[last])
    down, sums_down = down_grad(groups, count, ids, cot_e, back, a_e, a_r, dyb_r)
    cot_last = cot_e[last]
    if tree:
        downs = [down[0], hop(down[1], 1)]
        (down_x,), cot_last = in_order(send(send_job(downs, 0, 1)), cot_last)
        downs = downs + [hop(down_x, 2)]
    mlps.append(mlp(last, cot_last)[1])
    du_e, dy1_e, dy1b_e, sums_e = zip(*mlps)
    up, sums_up = up_grad(groups, count, ids, du_e, h2_e, dy1b_e, o_e, du_r, h2_r, dy1b_r, o_r)
    dy1_last = dy1_e[last]
    if tree:
        ups = [up[0], [hop(piece, 1) for piece in up[1:]]]
        (up_x, down_z), dy1_last = in_order(send(send_job(ups, 0, 1), send_job(downs, 1, 2)), dy1_last)
        ups = ups + [hop(up_x, 2)]
        downs = downs + [hop(down_z, 4)]
    attns.append(attention(last, dy1_last))
    dq_e, dkv_e, dx, sums_in = (list(piece) for piece in zip(*attns))
    if tree:
        (down_z,), dq_e[last] = in_order(send(send_job(downs, 2, 3)), dq_e[last])
        downs = downs + [hop(down_z, 8)]
    attn, small = qkv_grad(
        groups, count, ids, (sums_down, sums_up, *sums_e, *sums_r, *sums_in),
        dq_e, dkv_e, hq_e, hq_r, hk_r, dq_r, dkv_r,
    )
    if tree:
        got = [hop(piece, 1) for piece in attn[1:]]
        got, small = in_order(got, small + hop(small, 1))
        small = small + hop(small, 2)
        qkvs = [attn[0], got]
        (qkv_x, up_z), (dx, small) = in_order(send(send_job(qkvs, 0, 1), send_job(ups, 1, 2)), (dx, small))
        qkvs = qkvs + [hop(qkv_x, 2)]
        ups = ups + [hop(up_z, 4)]
    block_out, grad_rows = place(groups, ids, visible, patch_order, dx, lat, res)
    if tree:
        (block_out, grad_rows, downs[-1]), got = in_order((block_out, grad_rows, downs[-1]), hop(small, 4))
        (up_z,), (block_out, grad_rows, small) = in_order(
            send(send_job(ups, 2, 3)), (block_out, grad_rows, small + got)
        )
        ups = ups + [hop(up_z, 8)]
        peers = (3, 2, 1)
        qkv_z, (block_out, grad_rows, small) = in_order(
            send(send_job(qkvs, 1, 3, peers)), (block_out, grad_rows, small)
        )
        qkv_got = [hop(one, 4 * peer) for one, peer in zip(qkv_z, peers)]
        small = small + hop(small, 8)
        down_sum, up_sum, out_sum = send(
            final_job(downs, ((0, 0),)),
            final_job(ups, tuple((1, j) for j in range(4)) + ((2, 0),)),
            outs=((D // 4, D), (D // 16, 4 * D), (D // 16, D)),
        )
        qkv_got, (down_sum, up_sum, out_sum) = in_order(qkv_got, (down_sum, up_sum, out_sum))
        (qkv_sum,) = send(final_job(qkvs + qkv_got, ((0, 1), (0, 2), (0, 0))), outs=((D // 16, 3 * D),))
    else:
        down_sum = scatter_natural(down[0])
        up_sum = jnp.concatenate([scatter_natural(one) for one in up[:4]], axis=1)
        out_sum = scatter_natural(up[4])
        qkv_sum = jnp.concatenate([scatter_natural(attn[i]) for i in (2, 0, 1)], axis=1)
        small = lax.psum(small, "dp")
    grad_rows = grad_rows.transpose(0, 2, 1, 3)
    gains, bias_rows, qv_rows, up_rows = own_columns(small, count)
    return (
        block_out,
        grad_rows,
        qkv_sum[None],
        out_sum[None],
        up_sum[None],
        down_sum[None],
        gains[None],
        bias_rows[None],
        qv_rows[None],
        up_rows[None],
    )


def solution(mesh):
    three, four = P("section", None, None), P("section", "dp", None, None)
    grad = P("section", "dp", None)
    return jax.shard_map(
        local,
        mesh=mesh,
        in_specs=(four, four, P("dp", None), P("dp"), three, three, three, three, three, three,
                  P("section", None), P("section", None), P(), P(), P(), P(), P(), P(), P(), P()),
        out_specs=(four, four, grad, grad, grad, grad, P("section", None, "dp"), P("section", None, "dp"),
                   P("section", "dp"), P("section", "dp")),
        check_vma=False,
    )
```

```python
from functools import partial

import jax
import jax.numpy as jnp
from jax import lax
from jax.experimental import pallas as pl
from jax.experimental.pallas import tpu as pltpu
from jax.sharding import PartitionSpec as P

HEADS = 12
PATCH = 196
D = 768
FF = 3072
EPS = 1e-06
NV = 144
NM = 128
FIRST = PATCH - NM
GROUP = 2
CHUNK = 32

BF = jnp.bfloat16
F32 = jnp.float32
MIB = 1024 * 1024
LIMIT = 62

HBM = pl.BlockSpec(memory_space=pl.ANY)
VMEM = pl.BlockSpec(memory_space=pltpu.VMEM)
SMEM = pl.BlockSpec(memory_space=pltpu.SMEM)


def nn(a, b):
    return jnp.dot(a, b, preferred_element_type=F32)


def nt(a, b):
    return lax.dot_general(a, b, (((1,), (1,)), ((), ())), preferred_element_type=F32)


def tn(a, b):
    return lax.dot_general(a, b, (((0,), (0,)), ((), ())), preferred_element_type=F32)


def loop(count, body, unroll=1):
    def step(i, carry):
        for u in range(unroll):
            body(i * unroll + u)
        return carry

    if count == unroll:
        step(0, 0)
    else:
        lax.fori_loop(0, count // unroll, step, 0)


def unroll_of(count):
    return next(u for u in (4, 3, 2, 1) if count % u == 0)


def rows_of(i, size):
    return pl.ds(pl.multiple_of(i * size, size), size)


def f32_row(ref, row, col=0, width=D):
    return ref[pl.ds(row, 1), pl.ds(col, width)].astype(F32)


class Copies:
    def __init__(self, sems):
        self.sems = sems
        self.used = 0
        self.open = []

    def start(self, src, dst):
        copy = pltpu.make_async_copy(src, dst, self.sems.at[self.used])
        self.used += 1
        copy.start()
        self.open.append(copy)
        return copy

    def wait(self, *copies):
        for copy in copies:
            copy.wait()
            self.open = [one for one in self.open if one is not copy]

    def finish(self):
        self.wait(*list(self.open))

    def take(self, count):
        self.used += count
        return self.used - count

    def begin(self, src, dst, at):
        pltpu.make_async_copy(src, dst, self.sems.at[at]).start()

    def wait_at(self, src, dst, at):
        pltpu.make_async_copy(src, dst, self.sems.at[at]).wait()


def gelu_pair(u):
    size = jnp.abs(u)
    base = 1.0 + (0.3275911 * 0.7071067811865476) * size
    guess = pl.reciprocal(base, approx=True)
    t = guess * (2.0 - base * guess)
    ex = jnp.exp2((u * u) * (-0.5 * 1.4426950408889634))
    poly = 0.5306027145 * t - 0.7265760135
    poly = poly * t + 0.7107068705
    poly = poly * t - 0.142248368
    poly = poly * t + 0.127414796
    tail = poly * t * ex
    phi = jnp.where(u >= 0.0, 1.0 - tail, tail)
    return u * phi, phi + u * (0.3989422804014327 * ex)


def norm_rows(src, dst, rows, gain, shift):
    def body(i):
        sel = rows_of(i, CHUNK)
        x = src[sel, :].astype(F32)
        centered = x - jnp.mean(x, axis=-1, keepdims=True)
        var = jnp.mean(centered * centered, axis=-1, keepdims=True)
        dst[sel, :] = (centered * lax.rsqrt(var + EPS) * gain + shift).astype(BF)

    loop(rows // CHUNK, body, unroll_of(rows // CHUNK))


def norm_back(src, grad, base, write, rows, gain):
    count = rows // CHUNK
    unroll = 3 if count % 3 == 0 else 2

    def step(i, carry):
        for u in range(unroll):
            carry = one(i * unroll + u, carry)
        return carry

    def one(i, carry):
        d_gain, d_shift = carry
        sel = rows_of(i, CHUNK)
        x = src[sel, :].astype(F32)
        dh = grad[sel, :]
        centered = x - jnp.mean(x, axis=-1, keepdims=True)
        var = jnp.mean(centered * centered, axis=-1, keepdims=True)
        rstd = lax.rsqrt(var + EPS)
        hat = centered * rstd
        g = dh * gain
        part = dh * hat
        dx = rstd * (
            g
            - jnp.mean(g, axis=-1, keepdims=True)
            - hat * jnp.mean(g * hat, axis=-1, keepdims=True)
        )
        if base is not None:
            dx = dx + base[sel, :].astype(F32)
        write(sel, dx)
        d_gain = d_gain + jnp.sum(part.reshape(CHUNK // 8, 8, D), axis=0)
        d_shift = d_shift + jnp.sum(dh.reshape(CHUNK // 8, 8, D), axis=0)
        return d_gain, d_shift

    zero = jnp.zeros((8, D), F32)
    d_gain, d_shift = lax.fori_loop(0, count // unroll, step, (zero, zero))
    return jnp.sum(d_gain, axis=0, keepdims=True), jnp.sum(d_shift, axis=0, keepdims=True)


def column_sum(ref, rows, col=0, width=D):
    def step(i, carry):
        x = ref[rows_of(i, CHUNK), pl.ds(col, width)].astype(F32)
        return carry + jnp.sum(x.reshape(CHUNK // 8, 8, width), axis=0)

    total = lax.fori_loop(0, rows // CHUNK, step, jnp.zeros((8, width), F32))
    return jnp.sum(total, axis=0, keepdims=True)


def as_bf16(flags):
    return jnp.where(flags, 1.0, 0.0).astype(BF)


def pick_matrix(order, image, start, count, low, high):
    row = order[image, :, pl.ds(start, count)].astype(F32)
    images = order.shape[0]
    col = jnp.broadcast_to(row, (8, count)).T[:, 0:1].astype(jnp.int32)
    rank = start + lax.broadcasted_iota(jnp.int32, (count, 1), 0)
    col = jnp.where((rank >= low) & (rank < high), col * images + image, -1)
    return as_bf16(col == lax.broadcasted_iota(jnp.int32, (count, PATCH * images), 1))


def place_matrix(order, image, start, count, low, high):
    row = order[image, :, pl.ds(start, count)]
    rank = start + lax.broadcasted_iota(jnp.int32, (1, count), 1)
    row = jnp.where((rank >= low) & (rank < high), row, -1)
    return as_bf16(row == lax.broadcasted_iota(jnp.int32, (PATCH, count), 0))


def flatten(rows, flat):
    flat[...] = rows[...].reshape(flat.shape)


def split_orders(order, split):
    for image in range(split.shape[0]):
        split[image] = order[image : image + 1, :]


def split_pair(pair):
    lane = lax.broadcasted_iota(jnp.int32, pair.shape, 1)
    zero = jnp.zeros_like(pair)
    return jnp.concatenate([jnp.where(lane < 64, pair, zero), jnp.where(lane < 64, zero, pair)], axis=0)


def join_rows(both):
    rows = both.shape[0] // 2
    lane = lax.broadcasted_iota(jnp.int32, (rows, 128), 1)
    return jnp.where(lane < 64, both[:rows], both[rows:])


def join_columns(both):
    rows = both.shape[1] // 2
    return jnp.concatenate([both[:64, :rows], both[64:, rows:]], axis=0).T


PAIRS = HEADS // 2
STEP = 6


def each_pair_group(images, body):
    def group(i):
        image = i // (PAIRS // STEP)
        first = (i % (PAIRS // STEP)) * STEP
        pairs = [first + step for step in range(STEP)]
        body(image, [image * PAIRS + pair for pair in pairs], [pl.ds(pl.multiple_of(pair * 128, 128), 128) for pair in pairs])

    loop(images * (PAIRS // STEP), group)


def softmax(scores, axis):
    ex = jnp.exp(scores - jnp.max(scores, axis=axis, keepdims=True))
    return (ex * (1.0 / jnp.sum(ex, axis=axis, keepdims=True))).astype(BF)


def score_back(probs, d_probs, axis):
    wide = probs.astype(F32)
    return (wide * (d_probs - jnp.sum(d_probs * wide, axis=axis, keepdims=True))).astype(BF)


def attention_by_rows(images, n, q, k, v, p, o, count_of):
    def body(image, slots, lanes):
        sel = rows_of(image, n)
        ok = lax.broadcasted_iota(jnp.int32, (1, n), 1) < count_of(image)
        scores = [nt(split_pair(q[sel, at]), k[sel, at]) for at in lanes]
        probs = [softmax(jnp.where(ok, one, -1000000000.0), 1) for one in scores]
        for slot, one in zip(slots, probs):
            p[slot] = one
        mixed = [nn(one, v[sel, at]) for one, at in zip(probs, lanes)]
        for at, one in zip(lanes, mixed):
            o[sel, at] = join_rows(one).astype(BF)

    each_pair_group(images, body)


def attention_by_columns(images, nk, q, k, v, p, o, key_ok):
    def body(image, slots, lanes):
        qs, ks = rows_of(image, NM), rows_of(image, nk)
        ok = key_ok(image)
        scores = [nt(k[ks, at], split_pair(q[qs, at])) for at in lanes]
        probs = [softmax(jnp.where(ok, one, -1000000000.0), 0) for one in scores]
        if p is not None:
            for slot, one in zip(slots, probs):
                p[slot] = one
        mixed = [tn(v[ks, at], one) for one, at in zip(probs, lanes)]
        for at, one in zip(lanes, mixed):
            o[qs, at] = join_columns(one).astype(BF)

    each_pair_group(images, body)


def attention_back_rows(images, n, q, k, v, p, do, dq, dkv):
    def body(image, slots, lanes):
        sel = rows_of(image, n)
        d_mixed = [split_pair(do[sel, at]) for at in lanes]
        d_probs = [nt(one, v[sel, at]) for one, at in zip(d_mixed, lanes)]
        d_scores = [score_back(p[slot], one, 1) for slot, one in zip(slots, d_probs)]
        d_values = [tn(p[slot], one) for slot, one in zip(slots, d_mixed)]
        d_query = [nn(one, k[sel, at]) for one, at in zip(d_scores, lanes)]
        d_keys = [tn(one, split_pair(q[sel, at])) for one, at in zip(d_scores, lanes)]
        for at, value, query, key in zip(lanes, d_values, d_query, d_keys):
            dq[sel, at] = (join_rows(query) * 0.125).astype(BF)
            dkv[sel, at] = key.astype(BF)
            dkv[sel, pl.ds(pl.multiple_of(D + at.start, 128), 128)] = value.astype(BF)

    each_pair_group(images, body)


def attention_back_columns(images, nk, q, k, v, p, do, dq, dkv):
    def body(image, slots, lanes):
        qs, ks = rows_of(image, NM), rows_of(image, nk)
        d_mixed = [split_pair(do[qs, at]) for at in lanes]
        d_probs = [nt(v[ks, at], one) for one, at in zip(d_mixed, lanes)]
        d_scores = [score_back(p[slot], one, 0) for slot, one in zip(slots, d_probs)]
        d_values = [nn(p[slot], one) for slot, one in zip(slots, d_mixed)]
        d_query = [tn(k[ks, at], one) for one, at in zip(d_scores, lanes)]
        d_keys = [nn(one, split_pair(q[qs, at])) for one, at in zip(d_scores, lanes)]
        for at, value, query, key in zip(lanes, d_values, d_query, d_keys):
            dq[qs, at] = (join_columns(query) * 0.125).astype(BF)
            dkv[ks, at] = key.astype(BF)
            dkv[ks, pl.ds(pl.multiple_of(D + at.start, 128), 128)] = value.astype(BF)

    each_pair_group(images, body)


HALF = 512


def mlp_forward(rows, h2, w1, w2, up_b, u, a, gp, acc, out, base):
    acc[...] = base()

    def body(i):
        cols = [pl.ds(pl.multiple_of((2 * i + part) * HALF, HALF), HALF) for part in range(2)]
        for part in range(2):
            u[part] = nn(h2[...], w1[:, cols[part]])
        for part in range(2):
            for c in range(0, HALF, 256):
                at = pl.ds(pl.multiple_of((2 * i + part) * HALF + c, 256), 256)
                shift = up_b[0:1, at].astype(F32)
                for r in range(0, rows, CHUNK):
                    value, slope = gelu_pair(u[part, r : r + CHUNK, c : c + 256] + shift)
                    a[r : r + CHUNK, at] = value.astype(BF)
                    if gp is not None:
                        gp[r : r + CHUNK, at] = slope.astype(BF)
            acc[...] += nn(a[:, cols[part]], w2[cols[part], :])

    loop(FF // (2 * HALF), body)
    out[...] = acc[...].astype(BF)


def mlp_back(rows, dyb, gp, w1, w2, du, u, acc, ready=lambda i, which: None, flipped=False):
    acc[...] = jnp.zeros_like(acc)

    def body(i):
        cols = [pl.ds(pl.multiple_of((2 * i + part) * HALF, HALF), HALF) for part in range(2)]
        ready(i, 0)
        for part in range(2):
            u[part] = nn(dyb[...], w2[:, cols[part]]) if flipped else nt(dyb[...], w2[cols[part], :])
        ready(i, 1)
        for part in range(2):
            for r in range(0, rows, CHUNK):
                sel = slice(r, r + CHUNK)
                du[sel, cols[part]] = (gp[sel, cols[part]].astype(F32) * u[part, sel, :]).astype(BF)
            own = du[:, cols[part]]
            acc[...] += nn(own, w1[cols[part], :]) if flipped else nt(own, w1[:, cols[part]])

    loop(FF // (2 * HALF), body)


def project(count, rows, left, weight, first, write):
    def body(j):
        write(j, nn(left[...], weight[:, pl.ds(pl.multiple_of((first + j) * D, D), D)]))

    loop(count, body)


def set_biases(ref, bias):
    ref[0] = f32_row(bias, 0)
    ref[1] = jnp.zeros((1, D), F32)
    ref[2] = f32_row(bias, 0, D)


def cost(flops, nbytes):
    return pl.CostEstimate(flops=int(flops), bytes_accessed=int(nbytes), transcendentals=0)


def params(mib):
    return pltpu.CompilerParams(vmem_limit_bytes=mib * MIB)


def struct(shape, dtype=BF):
    return jax.ShapeDtypeStruct(shape, dtype)


def start_weights(copies, sources, scratch):
    return [copies.start(src, dst) for src, dst in zip(sources, scratch)]


def encode_kernel(group, groups, ids, visible, order_in, gains, biases, qvb, upb, rows, cot, wqkv, wo, w1, w2,
                  lat_out, x_out, hq_out, q_out, k_out, v_out, p_out, o_out, y1_out, h2_out, gp_out, a_out, *refs):
    ready, refs = refs[: 4 * groups], refs[4 * groups :]
    if group == 0:
        w1t_out, w2t_out, s1t, s2t, *refs = refs
    (order, rows_v, flat, sqkv, so, s1, s2, x, hq, qkv, p, o, y1, h2, gp, a, u, acc, shifts, lat, sems) = refs
    n = GROUP * NV
    split_orders(order_in, order)

    @pl.when(ids[0] == 0)
    def _():
        copies = Copies(sems)
        got_rows = copies.start(rows.at[0], rows_v)
        got_qkv, got_o, got_1, got_2 = start_weights(
            copies, (wqkv.at[0], wo.at[0], w1.at[0], w2.at[0]), (sqkv, so, s1, s2)
        )
        gain, bias = gains.at[0], biases.at[0]
        set_biases(shifts, qvb)
        copies.wait(got_rows)
        flatten(rows_v, flat)

        def pick_rows(i):
            image = group * GROUP + i
            pick = pick_matrix(order, image, 0, NV, 0, visible[image])
            x[rows_of(i, NV), :] = nn(pick, flat[...]).astype(BF)

        loop(GROUP, pick_rows)
        copies.start(x, x_out)
        norm_rows(x, hq, n, f32_row(gain, 0), f32_row(bias, 0))
        copies.start(hq, hq_out)
        copies.wait(got_qkv)

        def keep(j, value):
            scale = jnp.where(j == 0, 0.125, 1.0)
            qkv[j] = ((value + shifts[j]).astype(BF).astype(F32) * scale).astype(BF)

        project(3, n, hq, sqkv, 0, keep)
        q, k, v = qkv.at[0], qkv.at[1], qkv.at[2]
        copies.start(q, q_out)
        copies.start(k, k_out)
        copies.start(v, v_out)
        attention_by_rows(GROUP, NV, q, k, v, p, o, lambda i: visible[group * GROUP + i])
        copies.start(p, p_out)
        copies.start(o, o_out)
        copies.wait(got_o)
        y1[...] = nn(o[...], so[...]) + f32_row(bias, 1) + x[...].astype(F32)
        copies.start(y1, y1_out)
        norm_rows(y1, h2, n, f32_row(gain, 1), f32_row(bias, 2))
        copies.start(h2, h2_out)
        copies.wait(got_1, got_2)
        mlp_forward(n, h2, s1, s2, upb, u, a, gp, acc, lat, lambda: y1[...] + f32_row(bias, 3))
        copies.start(gp, gp_out)
        copies.start(a, a_out)
        copies.start(lat, lat_out)
        copies.finish()

    if group == 0:

        @pl.when(ids[0] == 1)
        def _():
            copies = Copies(sems)
            got_2, got_1 = copies.start(w2.at[0], s2), copies.start(w1.at[0], s1)
            copies.wait(got_2)

            def turn_down(i):
                at = rows_of(i, 256)
                s2t[:, at] = s2[at, :].T

            loop(FF // 256, turn_down)
            copies.start(s2t, w2t_out)
            copies.wait(got_1)

            def turn_up(i):
                at = rows_of(i, 256)
                s1t[at, :] = s1[:, at].T

            loop(FF // 256, turn_up)
            copies.start(s1t, w1t_out)
            copies.finish()

    if group == groups - 1:

        @pl.when(ids[0] == 1)
        def _():
            copies = Copies(sems)
            m = GROUP * NM
            x_out, hq_out, q_out, dyb_out = (ready[i * groups : (i + 1) * groups] for i in range(4))
            gain, bias = gains.at[0], biases.at[0]
            got_rows = copies.start(rows.at[0], rows_v)
            got_q = copies.start(wqkv.at[0, :, pl.ds(0, D)], so)
            copies.wait(got_rows)
            flatten(rows_v, flat)
            got_cot = copies.start(cot.at[0], rows_v)
            top = pl.ds(0, m)

            def pick_group(g):
                def pick_rows(i):
                    image = g * GROUP + i
                    pick = pick_matrix(order, image, FIRST, NM, visible[image], PATCH)
                    x[rows_of(i, NM), :] = nn(pick, flat[...]).astype(BF)

                loop(GROUP, pick_rows)

            for g in range(groups):
                pick_group(g)
                norm_rows(x, hq, m, f32_row(gain, 0), f32_row(bias, 0))
                sent = [copies.start(x.at[top], x_out[g]), copies.start(hq.at[top], hq_out[g])]
                if g == 0:
                    copies.wait(got_q)
                q = qkv.at[g]
                q[top, :] = ((nn(hq[top, :], so[...]) + f32_row(qvb, 0)).astype(BF) * 0.125).astype(BF)
                copies.start(q.at[top], q_out[g])
                copies.wait(*sent)
            copies.wait(got_cot)
            flatten(rows_v, flat)
            for g in range(groups):
                pick_group(g)
                copies.wait(copies.start(x.at[top], dyb_out[g]))
            copies.finish()


def encode(group, groups, ids, visible, order, gains, biases, qvb, upb, rows, cot, weights):
    n = GROUP * NV
    images = order.shape[0]
    row, wide = struct((n, D)), struct((n, FF))
    heads = struct((GROUP * PAIRS, 2 * NV, NV))
    outs = [row] * 6 + [heads, row, struct((n, D), F32), row, wide, wide] + [struct((GROUP * NM, D))] * (4 * groups)
    vm = lambda s: pltpu.VMEM(s.shape, s.dtype)
    flipped = [struct((FF, D)), struct((D, FF))] if group == 0 else []
    outs += flipped
    scratch = [vm(one) for one in flipped] + [
        pltpu.VMEM((images, 1, PATCH), jnp.int32),
        pltpu.VMEM((PATCH, images, D), BF), pltpu.VMEM((PATCH * images, D), BF),
        pltpu.VMEM((D, 3 * D), BF), pltpu.VMEM((D, D), BF), pltpu.VMEM((D, FF), BF), pltpu.VMEM((FF, D), BF),
        vm(row), vm(row), pltpu.VMEM((3, n, D), BF), vm(heads), vm(row), pltpu.VMEM((n, D), F32), vm(row),
        vm(wide), vm(wide), pltpu.VMEM((2, n, HALF), F32), pltpu.VMEM((n, D), F32), pltpu.VMEM((3, 1, D), F32), vm(row),
        pltpu.SemaphoreType.DMA((24,)),
    ]
    got = pl.pallas_call(
        partial(encode_kernel, group, groups),
        in_specs=[SMEM, SMEM] + [VMEM] * 5 + [HBM] * 6,
        out_specs=[HBM] * len(outs),
        out_shape=outs,
        scratch_shapes=scratch,
        compiler_params=params(LIMIT),
        cost_estimate=cost(2 * n * 12 * D * D, 25e6),
        name="encode",
    )(ids, visible, order, gains, biases, qvb, upb, rows, cot, *weights)
    ready = got[12:]
    return got[:12], [ready[i * groups : (i + 1) * groups] for i in range(4)], ready[4 * groups :]


def middle_kernel(group, ids, visible, order_in, gains, biases, qvb, upb, tgains, tbiases, tqvb, tupb,
                  rows, lat_in, x_in, q_in, dyb_in, wqkv, wo, w1, w2, w1t, w2t, tqkv, to, t1, t2,
                  dlat_out, res_out, hk_out, dq_out, dkv_out, o_out, dy1b_out, h2_out, du_out, a_out,
                  dy1_out, sums_out,
                  order, rows_v, flat, sqkv, so, s1, s2, s1t, s2t, x, lat, hq, hk, q, kv, p, o, y1, h2, gp, a, u, acc, shifts,
                  res, dyb, du, dy1, dy1b, do, dq, dkv, dh, dlat, sums, sems):
    n, m = GROUP * NM, GROUP * NV
    top = pl.ds(0, n)
    k, v = kv.at[0], kv.at[1]
    split_orders(order_in, order)

    def forward(copies, got_weights, gain, bias, ub, nk, key_ok, keep_p, keep_slope):
        got_o, got_1, got_2 = got_weights
        attention_by_columns(GROUP, nk, q, k, v, keep_p, o, key_ok)
        copies.wait(got_o)
        y1[...] = nn(o[...], so[...]) + f32_row(bias, 1) + x[...].astype(F32)
        norm_rows(y1, h2, n, f32_row(gain, 1), f32_row(bias, 2))
        copies.wait(got_1, got_2)
        mlp_forward(n, h2, s1, s2, ub, u, a, keep_slope, acc, res, lambda: y1[...] + f32_row(bias, 3))
        copies.start(res, res_out)

    @pl.when(ids[0] == 0)
    def _():
        copies = Copies(sems)
        gain, bias = tgains, tbiases
        got_rows = copies.start(rows.at[0], rows_v)
        got_qkv = copies.start(tqkv, sqkv)
        got_weights = start_weights(copies, (to, t1, t2), (so, s1, s2))
        copies.wait(got_rows)
        flatten(rows_v, flat)

        def pick_rows(i):
            image = group * GROUP + i
            pick = pick_matrix(order, image, FIRST, NM, visible[image], PATCH)
            x[rows_of(i, NM), :] = nn(pick, flat[...]).astype(BF)

        loop(GROUP, pick_rows)
        norm_rows(x, hq, n, f32_row(gain, 0), f32_row(bias, 0))
        copies.wait(got_qkv)
        set_biases(shifts, tqvb)
        q[...] = ((nn(hq[...], sqkv[:, :D]) + f32_row(tqvb, 0)).astype(BF) * 0.125).astype(BF)

        def keep_kv(j, value):
            kv[j, top, :] = (value + shifts[j + 1]).astype(BF)

        project(2, n, hq, sqkv, 1, keep_kv)

        def key_ok(i):
            return lax.broadcasted_iota(jnp.int32, (NM, 1), 0) + FIRST >= visible[group * GROUP + i]

        forward(copies, got_weights, gain, bias, tupb, NM, key_ok, None, None)
        copies.finish()

    @pl.when(ids[0] == 1)
    def _():
        copies = Copies(sems)
        gain, bias = gains.at[0], biases.at[0]
        got_lat = copies.start(lat_in, lat)
        got_kv = copies.start(wqkv.at[0, :, pl.ds(D, 2 * D)], sqkv.at[:, pl.ds(D, 2 * D)])
        got_q = copies.start(q_in, q)
        got_x = copies.start(x_in, x)
        got_weights = start_weights(copies, (wo.at[0], w1.at[0], w2.at[0]), (so, s1, s2))
        got_dyb = copies.start(dyb_in, dyb)
        got_back = [copies.start(w2t, s2t), copies.start(w1t, s1t)]
        copies.wait(got_lat)
        norm_rows(lat, hk, m, f32_row(gain, 0), f32_row(bias, 0))
        copies.start(hk, hk_out)
        copies.wait(got_kv)
        set_biases(shifts, qvb)

        def keep_kv(j, value):
            kv[j] = (value + shifts[j + 1]).astype(BF)

        project(2, m, hk, sqkv, 1, keep_kv)
        copies.wait(got_q, got_x)

        def key_ok(i):
            return lax.broadcasted_iota(jnp.int32, (NV, 1), 0) < visible[group * GROUP + i]

        forward(copies, got_weights, gain, bias, upb.at[0:1], NV, key_ok, p, gp)
        copies.start(o, o_out)
        copies.start(h2, h2_out)
        copies.start(a, a_out)
        copies.wait(got_dyb, *got_back)
        mlp_back(n, dyb, gp, s1t, s2t, du, u, acc, flipped=True)
        copies.start(du, du_out)

        def keep(sel, dx):
            dy1[sel, :] = dx
            dy1b[sel, :] = dx.astype(BF)

        g2, b2 = norm_back(y1, acc, dyb, keep, n, f32_row(gain, 1))
        copies.start(dy1, dy1_out)
        copies.start(dy1b, dy1b_out)
        do[...] = nt(dy1b[...], so[...]).astype(BF)
        attention_back_columns(GROUP, NV, q, k, v, p, do, dq, dkv)
        copies.start(dq, dq_out)
        copies.start(dkv, dkv_out)
        dh[...] = nt(dkv[:, :D], sqkv[:, D : 2 * D])
        dh[...] += nt(dkv[:, D:], sqkv[:, 2 * D :])

        def keep_side(sel, dx):
            dlat[sel, :] = dx.astype(BF)

        gk, bk = norm_back(lat, dh, None, keep_side, m, f32_row(gain, 0))
        copies.start(dlat, dlat_out)
        for row, value in enumerate((gk, g2, bk, b2)):
            sums[pl.ds(row, 1), :] = value
        copies.start(sums, sums_out)
        copies.finish()


def middle(group, ids, visible, order, own_vecs, target_vecs, rows, lat, x, q, dyb, weights, flipped, targets):
    n, m = GROUP * NM, GROUP * NV
    row, side, wide = struct((n, D)), struct((m, D)), struct((n, FF))
    pair = struct((m, 2 * D))
    outs = [side, row, side, row, pair, row, row, row, wide, wide, struct((n, D), F32), struct((8, D), F32)]
    vm = lambda s: pltpu.VMEM(s.shape, s.dtype)
    full, fside = pltpu.VMEM((n, D), F32), pltpu.VMEM((m, D), F32)
    scratch = [
        pltpu.VMEM((order.shape[0], 1, PATCH), jnp.int32),
        pltpu.VMEM((PATCH, order.shape[0], D), BF), pltpu.VMEM((PATCH * order.shape[0], D), BF),
        pltpu.VMEM((D, 3 * D), BF), pltpu.VMEM((D, D), BF), pltpu.VMEM((D, FF), BF), pltpu.VMEM((FF, D), BF),
        pltpu.VMEM((FF, D), BF), pltpu.VMEM((D, FF), BF),
        vm(row), vm(side), vm(row), vm(side), vm(row), pltpu.VMEM((2, m, D), BF),
        pltpu.VMEM((GROUP * PAIRS, NV, 2 * NM), BF), vm(row), full, vm(row), vm(wide), vm(wide),
        pltpu.VMEM((2, n, HALF), F32), full, pltpu.VMEM((3, 1, D), F32),
        vm(row), vm(row), vm(wide), full, vm(row), vm(row), vm(row), vm(pair), fside, vm(side),
        pltpu.VMEM((8, D), F32),
        pltpu.SemaphoreType.DMA((24,)),
    ]
    return pl.pallas_call(
        partial(middle_kernel, group),
        in_specs=[SMEM, SMEM] + [VMEM] * 9 + [HBM] * 15,
        out_specs=[HBM] * len(outs),
        out_shape=outs,
        scratch_shapes=scratch,
        compiler_params=params(LIMIT),
        cost_estimate=cost(4 * n * 12 * D * D, 25e6),
        name="middle",
    )(ids, visible, order, *own_vecs, *target_vecs, rows, lat, x, q, dyb, *weights, *flipped, *targets)


def stack_rows(copies, pieces, ref, size):
    return [copies.start(piece, ref.at[pl.ds(i * size, size)]) for i, piece in enumerate(pieces)]


def turn_rows(ref, turned, count):
    def step(i, carry):
        turned[i] = ref[i].T
        return carry

    lax.fori_loop(0, count, step, 0)


def clear_tail(ref, used):
    ref[pl.ds(used, ref.shape[0] - used), :] = jnp.zeros((ref.shape[0] - used, ref.shape[1]), ref.dtype)


def halves(count, blocks):
    rows = D // 16
    if count == 16:
        return [struct((2, 2, 2, blocks, rows, D))] + [struct((2, blocks, rows, D))] * 4
    return [struct((D, D))] * blocks


def give_blocks(copies, core, tree, left_right, out, dest):
    size = 8 if tree else 1
    blocks = out.shape[0]
    first = copies.take(blocks * size)

    def send(j, act):
        if not tree:
            for block in range(blocks):
                pl.when(j == block)(lambda block=block: act(out.at[block], dest[block], first + block))
            return
        view = out.at[j].reshape(2, 2, 2, 2, D // 16, D)
        for x in range(2):
            for low in range(2):
                at = first + j * size + 4 * x + 2 * low
                act(view.at[:, low, x, core], dest[0].at[x, low, :, j], at)
                act(view.at[:, low, x, 1 - core], dest[1 + 2 * x + low].at[:, j], at + 1)

    def body(j):
        out[j] = left_right(j)
        send(j, copies.begin)

    loop(blocks, body)
    loop(blocks, lambda j: send(j, copies.wait_at))


def give_rows(copies, core, tree, multiply, out, dest):
    size = 4 if tree else 1
    first = copies.take(4 * size)

    def send(j, act):
        if not tree:
            act(out.at[j], dest[0].at[pl.ds(pl.multiple_of(j * D, D), D)], first + j)
            return
        view = out.at[j].reshape(2, 2, D // 4, D)
        low, high = lax.rem(j, 2), lax.div(j, 2)
        for x in range(2):
            at = first + j * size + 2 * x
            act(view.at[x, core], dest[0].at[x, low, high, 0], at)
            act(view.at[x, 1 - core], dest[1].at[x, low, high, 0], at + 1)

    def body(j):
        out[j] = multiply(j)
        send(j, copies.begin)

    loop(4, body)
    loop(4, lambda j: send(j, copies.wait_at))


def down_kernel(groups, parts, ids, *refs):
    cot, lat, a_enc, a_reg, dyb_reg = (refs[i * groups : (i + 1) * groups] for i in range(5))
    refs = refs[5 * groups :]
    dest, refs = refs[:parts], refs[parts:]
    sums_out, cot_v, dyb, a, dlat, out, sums, sems = refs
    images = groups * GROUP
    nv, nm = GROUP * NV, GROUP * NM

    @pl.when(ids[0] == 0)
    def _():
        copies = Copies(sems)
        got = stack_rows(copies, cot, cot_v, nv) + stack_rows(copies, lat, dlat, nv)
        stack_rows(copies, a_enc, a, nv)
        copies.wait(*got)
        dyb[...] = (cot_v[...].astype(F32) + dlat[...].astype(F32)).astype(BF)
        copies.finish()

    @pl.when(ids[0] == 1)
    def _():
        copies = Copies(sems)
        stack_rows(copies, a_reg, a, nm)
        stack_rows(copies, dyb_reg, dyb, nm)
        clear_tail(a, images * NM)
        clear_tail(dyb, images * NM)
        copies.finish()

    copies = Copies(sems)

    def multiply(j):
        return tn(a[:, pl.ds(pl.multiple_of(j * D, D), D)], dyb[...]).astype(BF)

    give_rows(copies, ids[1], parts == 2, multiply, out, dest)
    sums[...] = jnp.broadcast_to(column_sum(dyb, images * NV), (8, D))
    copies.start(sums, sums_out)
    copies.finish()


def down_grad(groups, count, ids, cot, dlat, a_enc, a_reg, dyb_reg):
    n = groups * GROUP * NV
    main = [struct((2, 2, 2, 1, D // 4, D))] * 2 if count == 16 else [struct((FF, D))]
    outs = main + [struct((8, D), F32)]
    row = pltpu.VMEM((n, D), BF)
    scratch = [
        row, row, pltpu.VMEM((n, FF), BF), row, pltpu.VMEM((4, D, D), BF), pltpu.VMEM((8, D), F32),
        pltpu.SemaphoreType.DMA((24,)),
    ]
    got = pl.pallas_call(
        partial(down_kernel, groups, len(main)),
        in_specs=[SMEM] + [HBM] * (5 * groups),
        out_specs=[HBM] * len(outs),
        out_shape=outs,
        scratch_shapes=scratch,
        compiler_params=params(LIMIT),
        cost_estimate=cost(1e6, 1e5),
        name="down_grad",
    )(ids, *cot, *dlat, *a_enc, *a_reg, *dyb_reg)
    return got[: len(main)], got[-1]


def mlp_kernel(first, groups, ids, visible, order_in, gains, cot, dlat_in, w1, w2, y1_in, gp_in, *refs):
    if first:
        picked, refs = refs[:groups], refs[groups:]
    du_out, dy1_out, dy1b_out, sums_out, order, rows_v, flat, refs = *refs[:7], refs[7:]
    s1, s2, cot_v, dlat, dyb, gp, y1, du, u, acc, dy1, dy1b, sums, sems = refs
    n = GROUP * NV
    third = FF // 3

    @pl.when(ids[0] == 0)
    def _():
        copies = Copies(sems)
        got = [copies.start(dlat_in, dlat)]
        if first:
            got_rows = copies.start(cot.at[0], rows_v)
        else:
            got.append(copies.start(cot, cot_v))
        start = copies.take(9)

        def parts(i):
            cols = pl.ds(pl.multiple_of(i * third, third), third)
            return (
                (w2.at[0, cols, :], s2.at[cols, :]),
                (gp_in.at[:, cols], gp.at[:, cols]),
                (w1.at[0, :, cols], s1.at[:, cols]),
            )

        for i in range(3):
            for k, (src, dst) in enumerate(parts(i)):
                copies.begin(src, dst, start + 3 * i + k)
        got_y = copies.start(y1_in, y1)

        def ready(i, which):
            for k in ((0, 1), (2,))[which]:
                copies.wait_at(*parts(i)[k], start + 3 * i + k)

        if first:
            split_orders(order_in, order)
            copies.wait(got_rows)
            flatten(rows_v, flat)
            for g in reversed(range(groups)):

                def pick_rows(i, g=g):
                    image = g * GROUP + i
                    pick = pick_matrix(order, image, 0, NV, 0, visible[image])
                    cot_v[rows_of(i, NV), :] = nn(pick, flat[...]).astype(BF)

                loop(GROUP, pick_rows)
                copies.wait(copies.start(cot_v, picked[g]))
        copies.wait(*got)
        dyb[...] = (cot_v[...].astype(F32) + dlat[...].astype(F32)).astype(BF)
        mlp_back(n, dyb, gp, s1, s2, du, u, acc, ready)
        copies.start(du, du_out)
        copies.wait(got_y)

        def keep(sel, dx):
            dy1[sel, :] = dx
            dy1b[sel, :] = dx.astype(BF)

        g2, b2 = norm_back(y1, acc, dyb, keep, n, f32_row(gains.at[0], 1))
        copies.start(dy1, dy1_out)
        copies.start(dy1b, dy1b_out)
        sums[pl.ds(0, 1), :] = g2
        sums[pl.ds(1, 1), :] = b2
        copies.start(sums, sums_out)
        copies.finish()


def mlp_grad(first, groups, ids, visible, order, gains, cot, dlat, w1, w2, y1, gp):
    n = GROUP * NV
    images = order.shape[0]
    row, wide, full = pltpu.VMEM((n, D), BF), pltpu.VMEM((n, FF), BF), pltpu.VMEM((n, D), F32)
    outs = [struct((n, D))] * (groups if first else 0) + [struct((n, FF)), struct((n, D), F32), struct((n, D)), struct((8, D), F32)]
    got = pl.pallas_call(
        partial(mlp_kernel, first, groups),
        in_specs=[SMEM, SMEM, VMEM, VMEM] + [HBM] * 6,
        out_specs=[HBM] * len(outs),
        out_shape=outs,
        scratch_shapes=[
            pltpu.VMEM((images, 1, PATCH), jnp.int32),
            pltpu.VMEM((PATCH, images, D), BF), pltpu.VMEM((PATCH * images, D), BF),
            pltpu.VMEM((D, FF), BF), pltpu.VMEM((FF, D), BF), row, row, row, wide, full, wide,
            pltpu.VMEM((2, n, HALF), F32), full, full, row, pltpu.VMEM((8, D), F32), pltpu.SemaphoreType.DMA((24,)),
        ],
        compiler_params=params(LIMIT),
        cost_estimate=cost(1e6, 1e5),
        name="mlp_grad",
    )(ids, visible, order, gains, cot, dlat, w1, w2, y1, gp)
    return got[:-4], got[-4:]


def up_kernel(groups, parts, ids, *refs):
    pieces = [refs[i * groups : (i + 1) * groups] for i in range(8)]
    refs = refs[8 * groups :]
    dest, refs = refs[:parts], refs[parts:]
    sums_out, left, right, turned, out, sums, sems = refs
    images = groups * GROUP

    def load(du, h2, dy1b, o, size):
        copies = Copies(sems)
        stack_rows(copies, h2, left.at[0], size)
        for j in range(4):
            stack_rows(copies, [one.at[:, pl.ds(j * D, D)] for one in du], right.at[j], size)
        stack_rows(copies, o, left.at[1], size)
        stack_rows(copies, dy1b, right.at[4], size)
        return copies

    @pl.when(ids[0] == 0)
    def _():
        load(*pieces[:4], GROUP * NV).finish()

    @pl.when(ids[0] == 1)
    def _():
        copies = load(*pieces[4:], GROUP * NM)
        for ref in (left, right):
            for i in range(ref.shape[0]):
                clear_tail(ref.at[i], images * NM)
        copies.finish()

    copies = Copies(sems)

    def multiply(j):
        value = nn(turned[lax.div(j, 4)], right[j]).astype(BF)
        sums[pl.ds(j, 1), :] = column_sum(right.at[j], images * NV)
        return value

    turn_rows(left, turned, 2)

    give_blocks(copies, ids[1], dest[0].ndim == 6, multiply, out, dest)
    copies.start(sums, sums_out)
    copies.finish()


def up_grad(groups, count, ids, *pieces):
    n = groups * GROUP * NV
    main = halves(count, 5)
    outs = main + [struct((8, D), F32)]
    got = pl.pallas_call(
        partial(up_kernel, groups, len(main)),
        in_specs=[SMEM] + [HBM] * (8 * groups),
        out_specs=[HBM] * len(outs),
        out_shape=outs,
        scratch_shapes=[
            pltpu.VMEM((2, n, D), BF), pltpu.VMEM((5, n, D), BF), pltpu.VMEM((2, D, n), BF), pltpu.VMEM((5, D, D), BF),
            pltpu.VMEM((8, D), F32),
            pltpu.SemaphoreType.DMA((44,)),
        ],
        compiler_params=params(LIMIT),
        cost_estimate=cost(1e6, 1e5),
        name="up_grad",
    )(ids, *[ref for piece in pieces for ref in piece])
    return got[: len(main)], got[-1]


def attn_kernel(ids, gains, wqkv, wo, dy1_enc, q_in, k_in, v_in, p_in, x_enc, dq_reg, dy1_reg, x_reg,
                dq_out, dkv_out, dx_out, sums_out,
                sqkv, so, dy1, dy1b, q, k, v, p, x, do, dq, dkv, dh, sums, sems):
    m = GROUP * NM
    top = pl.ds(0, m)
    gain = f32_row(gains.at[0], 0)

    def finish(copies, rows):
        def keep(sel, dx):
            dy1[sel, :] = dx

        g1, b1 = norm_back(x, dh, dy1, keep, rows, gain)
        copies.start(dy1, dx_out)
        sums[0:1, :] = g1
        sums[1:2, :] = b1
        copies.start(sums, sums_out)
        copies.finish()

    @pl.when(ids[0] == 0)
    def _():
        copies = Copies(sems)
        got = [copies.start(dy1_enc, dy1), copies.start(wo.at[0], so)]
        later = [copies.start(src, dst) for src, dst in ((v_in, v), (p_in, p), (k_in, k), (q_in, q))]
        last = [copies.start(wqkv.at[0], sqkv), copies.start(x_enc, x)]
        copies.wait(*got)
        dy1b[...] = dy1[...].astype(BF)
        do[...] = nt(dy1b[...], so[...]).astype(BF)
        copies.wait(*later)
        attention_back_rows(GROUP, NV, q, k, v, p, do, dq, dkv)
        copies.start(dq, dq_out)
        copies.start(dkv, dkv_out)
        copies.wait(*last)
        dh[...] = nt(dq[...], sqkv[:, 0:D])
        for j in range(2):
            dh[...] += nt(dkv[:, j * D : (j + 1) * D], sqkv[:, (j + 1) * D : (j + 2) * D])
        finish(copies, GROUP * NV)

    @pl.when(ids[0] == 1)
    def _():
        copies = Copies(sems)
        for src, dst in ((dq_reg, dq), (dy1_reg, dy1), (x_reg, x)):
            copies.start(src, dst.at[top])
        copies.start(wqkv.at[0, :, pl.ds(0, D)], sqkv.at[:, pl.ds(0, D)])
        copies.finish()
        dh[top, :] = nt(dq[top, :], sqkv[:, 0:D])
        finish(copies, m)


def attn_back(ids, gains, wqkv, wo, *pieces):
    n = GROUP * NV
    row, full = pltpu.VMEM((n, D), BF), pltpu.VMEM((n, D), F32)
    outs = [struct((n, D)), struct((n, 2 * D)), struct((n, D), F32), struct((8, D), F32)]
    return pl.pallas_call(
        attn_kernel,
        in_specs=[SMEM, VMEM] + [HBM] * (2 + len(pieces)),
        out_specs=[HBM] * len(outs),
        out_shape=outs,
        scratch_shapes=[
            pltpu.VMEM((D, 3 * D), BF), pltpu.VMEM((D, D), BF), full, row, row, row, row,
            pltpu.VMEM((GROUP * PAIRS, 2 * NV, NV), BF), row, row, row, pltpu.VMEM((n, 2 * D), BF), full,
            pltpu.VMEM((8, D), F32), pltpu.SemaphoreType.DMA((20,)),
        ],
        compiler_params=params(LIMIT),
        cost_estimate=cost(1e6, 1e5),
        name="attn_back",
    )(ids, gains, wqkv, wo, *pieces)


def qkv_kernel(groups, parts, ids, down_sums, up_sums, *refs):
    mlp_sums, reg_sums, in_sums = (refs[i * groups : (i + 1) * groups] for i in range(3))
    refs = refs[3 * groups :]
    pieces = [refs[i * groups : (i + 1) * groups] for i in range(7)]
    dq_enc, dkv_enc, hq_enc, hq_reg, hk_reg, dq_reg, dkv_reg = pieces
    refs = refs[7 * groups :]
    dest, refs = refs[:parts], refs[parts:]
    small, left, right, turned, out, sems = refs
    images = groups * GROUP
    nv, nm = GROUP * NV, GROUP * NM
    hk, hq = left.at[0], left.at[1]
    dk, dv, dq = (right.at[i] for i in range(3))

    @pl.when(ids[0] == 0)
    def _():
        copies = Copies(sems)
        stack_rows(copies, hq_enc, hk, nv)
        stack_rows(copies, [one.at[:, pl.ds(0, D)] for one in dkv_enc], dk, nv)
        stack_rows(copies, [one.at[:, pl.ds(D, D)] for one in dkv_enc], dv, nv)
        stack_rows(copies, hq_enc, hq, nv)
        stack_rows(copies, dq_enc, dq, nv)
        copies.finish()

    @pl.when(ids[0] == 1)
    def _():
        copies = Copies(sems)
        for piece, ref in ((hq_reg, hq), (dq_reg, dq)):
            stack_rows(copies, piece, ref, nm)
            clear_tail(ref, images * NM)
        stack_rows(copies, hk_reg, hk, nv)
        stack_rows(copies, [one.at[:, pl.ds(0, D)] for one in dkv_reg], dk, nv)
        stack_rows(copies, [one.at[:, pl.ds(D, D)] for one in dkv_reg], dv, nv)
        copies.finish()

    copies = Copies(sems)

    def multiply(j):
        return nn(turned[jnp.where(ids[0] == 0, 0, lax.div(j, 2))], right[j]).astype(BF)

    turn_rows(left, turned, jnp.where(ids[0] == 0, 1, 2))

    give_blocks(copies, ids[1], dest[0].ndim == 6, multiply, out, dest)

    def total_of(sums):
        total = sums[0][...]
        for more in sums[1:]:
            total = total + more[...]
        return total

    first, mlp, reg = total_of(in_sums), total_of(mlp_sums), total_of(reg_sums)
    encoder = ids[0] == 0
    small[0:1, :] = first[0:1, :] + jnp.where(encoder, 0.0, reg[0:1, :])
    small[1:2, :] = jnp.where(encoder, mlp[0:1, :], reg[1:2, :])
    small[2:3, :] = first[1:2, :] + jnp.where(encoder, 0.0, reg[2:3, :])
    small[3:4, :] = up_sums[4:5, :]
    small[4:5, :] = jnp.where(encoder, mlp[1:2, :], reg[3:4, :])
    small[5:6, :] = down_sums[0:1, :]
    small[6:7, :] = column_sum(dq, images * NV)
    small[7:8, :] = column_sum(dv, images * NV)
    small[8:12, :] = up_sums[0:4, :]
    small[12:16, :] = jnp.zeros((4, D), F32)
    copies.finish()


def qkv_grad(groups, count, ids, sums, *pieces):
    n = groups * GROUP * NV
    row = pltpu.VMEM((n, D), BF)
    main = halves(count, 3)
    outs = main + [struct((16, D), F32)]
    scratch = [
        pltpu.VMEM((2, n, D), BF), pltpu.VMEM((3, n, D), BF), pltpu.VMEM((2, D, n), BF), pltpu.VMEM((3, D, D), BF),
        pltpu.SemaphoreType.DMA((40,)),
    ]
    got = pl.pallas_call(
        partial(qkv_kernel, groups, len(main)),
        in_specs=[SMEM] + [VMEM] * (2 + 3 * groups) + [HBM] * (7 * groups),
        out_specs=[HBM] * len(main) + [VMEM],
        out_shape=outs,
        scratch_shapes=scratch,
        compiler_params=params(LIMIT),
        cost_estimate=cost(1e6, 1e5),
        name="qkv_grad",
    )(ids, *sums, *[ref for piece in pieces for ref in piece])
    return got[: len(main)], got[-1]


def place_kernel(groups, ids, visible, order_in, *refs):
    dx_in, lat_enc, res = (refs[i * groups : (i + 1) * groups] for i in range(3))
    block_out, grad_out, order, dx, lat, out, grads, sems = refs[3 * groups :]
    images = groups * GROUP
    nv, nm = GROUP * NV, GROUP * NM
    split_orders(order_in, order)

    def put_grad(i, put, value):
        high = value.astype(BF)
        low = (value - high.astype(F32)).astype(BF)
        grads[i] = nn(put, high) + nn(put, low)

    def write_grads():
        copies = Copies(sems)
        for i in range(images):
            copies.start(grads.at[i], grad_out.at[0, :, i, :])
        copies.finish()

    @pl.when(ids[0] == 0)
    def _():
        copies = Copies(sems)
        for piece, ref, size in ((dx_in, dx, nv), (lat_enc, lat, nv), (res, out, nm)):
            stack_rows(copies, piece, ref, size)
        copies.finish()

        def put_image(i):
            put = place_matrix(order, i, 0, NV, 0, visible[i])
            put_side = place_matrix(order, i, FIRST, NM, visible[i], PATCH)
            put_grad(i, put, dx[rows_of(i, NV), :])
            block_out[0, i] = (nn(put, lat[rows_of(i, NV), :]) + nn(put_side, out[rows_of(i, NM), :])).astype(BF)

        loop(images, put_image)
        write_grads()

    @pl.when(ids[0] == 1)
    def _():
        copies = Copies(sems)
        stack_rows(copies, res, out, nm)
        stack_rows(copies, [piece.at[pl.ds(0, nm)] for piece in dx_in], dx, nm)
        copies.finish()

        def put_image(i):
            put = place_matrix(order, i, FIRST, NM, visible[i], PATCH)
            put_grad(i, put, dx[rows_of(i, NM), :])
            block_out[0, i] = nn(put, out[rows_of(i, NM), :]).astype(BF)

        loop(images, put_image)
        write_grads()


def place(groups, ids, visible, order, *pieces):
    images = groups * GROUP
    n = images * NV
    outs = [struct((1, images, PATCH, D)), struct((1, PATCH, images, D), F32)]
    return pl.pallas_call(
        partial(place_kernel, groups),
        in_specs=[SMEM, SMEM, VMEM] + [HBM] * (3 * groups),
        out_specs=[VMEM, HBM],
        out_shape=outs,
        scratch_shapes=[
            pltpu.VMEM((images, 1, PATCH), jnp.int32), pltpu.VMEM((n, D), F32), pltpu.VMEM((n, D), BF),
            pltpu.VMEM((images * NM, D), BF), pltpu.VMEM((images, PATCH, D), F32), pltpu.SemaphoreType.DMA((8,)),
        ],
        compiler_params=params(LIMIT),
        cost_estimate=cost(1e6, 1e5),
        name="place",
    )(ids, visible, order, *[ref for piece in pieces for ref in piece])


BITS = (2, 4, 8)


def hop(value, bit):
    return lax.ppermute(value, "dp", [(i, i ^ bit) for i in range(16)])


def combine_kernel(jobs, given, ids, *refs):
    used = sum(sum(4 if gone is None else 1 for gone in terms) for terms, *_ in jobs)
    inputs, outs, scratch = list(refs[:used]), list(refs[used : used + given]), list(refs[used + given :])
    copies = Copies(scratch.pop())
    plans = []

    def fetch(term, gone, bits, own):
        if gone is not None:
            path = tuple(bits[gone:])
            copy = copies.start(term.at[path] if path else term, own)
            return lambda: copies.wait(copy)
        wide = len(bits) == 1
        first = copies.take(2 if wide else 1)
        rest = tuple(bits[2:])

        def piece(x, low):
            ref = term[2 * x + low]
            return ref.at[rest] if rest else ref

        for x in range(2):
            for low in range(2):
                if wide:
                    pl.when(bits[0] == x)(
                        lambda x=x, low=low: copies.begin(piece(x, low), own.at[low], first + low)
                    )
                else:
                    pl.when((bits[0] == x) & (bits[1] == low))(
                        lambda x=x, low=low: copies.begin(piece(x, low), own, first)
                    )

        def wait():
            if wide:
                for low in range(2):
                    copies.wait_at(piece(0, low), own.at[low], first + low)
            else:
                copies.wait_at(piece(0, 0), own, first)

        return wait

    for kinds, first, last, targets, finals in jobs:
        terms = [inputs.pop(0) if gone is not None else [inputs.pop(0) for _ in range(4)] for gone in kinds]
        for target in targets:
            bits = []
            for bit in range(last):
                flip = bit >= first and (target >> (bit - first)) & 1
                bits.append(1 - ids[2 + bit] if flip else ids[2 + bit])
            owns = [scratch.pop(0) for _ in kinds]
            waits = [fetch(term, gone, bits, own) for term, gone, own in zip(terms, kinds, owns)]
            plans.append((waits, owns, last, finals, None if finals else outs.pop(0)))
    for waits, owns, last, finals, out in plans:
        for wait in waits:
            wait()
        spots = [()]
        for _ in range(3 - last):
            spots = [spot + (i,) for spot in spots for i in range(2)]
        for spot in spots:
            for j in range(owns[0].shape[-3]):
                value = owns[0][spot + (j,)].astype(F32)
                for more in owns[1:]:
                    value = value + more[spot + (j,)].astype(F32)
                if finals:
                    which, column = finals[j]
                    outs[which][:, column * D : (column + 1) * D] = value
                else:
                    out[spot + (j,)] = value.astype(BF)


def send_job(terms, first, last, targets=(1,)):
    return terms, first, last, targets, None


def final_job(terms, finals):
    return terms, 0, 3, (0,), finals


def combine(ids, *jobs, outs=()):
    shapes = [struct(shape, F32) for shape in outs]
    plans, inputs, scratch = [], [], []
    for terms, first, last, targets, finals in jobs:
        blocks, rows = terms[0].shape[-3:-1]
        kinds = tuple(None if isinstance(term, list) else 6 - term.ndim for term in terms)
        for term in terms:
            inputs += term if isinstance(term, list) else [term]
        plans.append((kinds, first, last, targets, finals))
        part = (2,) * (3 - last) + (blocks, rows, D)
        for _ in targets:
            scratch += [pltpu.VMEM(part, BF) for _ in terms]
            if finals is None:
                shapes.append(struct(part))
    scratch.append(pltpu.SemaphoreType.DMA((2 * len(scratch),)))
    return pl.pallas_call(
        partial(combine_kernel, tuple(plans), len(shapes)),
        in_specs=[SMEM] + [HBM] * len(inputs),
        out_specs=[VMEM] * len(shapes),
        out_shape=shapes,
        scratch_shapes=scratch,
        compiler_params=params(LIMIT),
        cost_estimate=cost(1e5, 1e4),
        name="combine",
    )(ids, *inputs)


def in_order(first, then):
    return lax.optimization_barrier((first, then))


def own_columns(rows, count):
    own = D // count
    me = lax.axis_index("dp")

    def part(block, wide):
        return lax.dynamic_slice_in_dim(block, me * wide, wide, block.ndim - 1)

    return (
        part(rows[:2], own),
        part(rows[2:6], own),
        part(rows[6:8].reshape(-1), 2 * own),
        part(rows[8:12].reshape(-1), 4 * own),
    )


def scatter_natural(block):
    shards = block.reshape(lax.axis_size("dp"), -1, D)
    return lax.psum_scatter(shards, "dp", scatter_dimension=0, tiled=True)[0].astype(F32)


def local(
    patch_rows, cotangent, patch_order, visible, qkv_weight, out_weight, up_weight, down_weight, norm_gains, biases,
    qv_bias, up_bias, target_qkv, target_out, target_up, target_down, target_gains, target_biases, target_qv_bias,
    target_up_bias,
):
    count = lax.axis_size("dp")
    tree = count == 16
    place_dp = lax.axis_index("dp")
    bits = [(place_dp // bit) % 2 for bit in (1,) + BITS]
    ids = jnp.stack([lax.axis_index("section")] + bits).astype(jnp.int32)
    groups = patch_order.shape[0] // GROUP
    weights = (qkv_weight, out_weight, up_weight, down_weight)
    targets = (target_qkv, target_out, target_up, target_down)
    vecs = (norm_gains, biases, qv_bias, up_bias)
    target_vecs = (target_gains, target_biases, target_qv_bias[None], target_up_bias[None])

    rows, cot = patch_rows.transpose(0, 2, 1, 3), cotangent.transpose(0, 2, 1, 3)
    calls = [
        encode(g, groups, ids, visible, patch_order, *vecs, rows, cot, weights) for g in range(groups)
    ]
    lat, x_e, hq_e, q_e, k_e, v_e, p_e, o_e, y1_e, h2_e, gp_e, a_e = zip(*[call[0] for call in calls])
    x_r, hq_r, q_r, dyb_r = calls[-1][1]
    sent = [lax.ppermute(piece, "section", [(0, 1)]) for piece in lat]
    middles = [
        middle(g, ids, visible, patch_order, vecs, target_vecs, rows, sent[g], x_r[g], q_r[g], dyb_r[g], weights, calls[0][2],
               targets)
        for g in range(groups)
    ]
    dlat, res, hk_r, dq_r, dkv_r, o_r, dy1b_r, h2_r, du_r, a_r, dy1_r, sums_r = zip(*middles)
    back = [lax.ppermute(piece, "section", [(1, 0)]) for piece in dlat]

    def mlp(g, cot):
        return mlp_grad(
            g == 0, groups, ids, visible, patch_order, norm_gains, cot, back[g], up_weight, down_weight, y1_e[g], gp_e[g]
        )

    def attention(g, dy1):
        return attn_back(
            ids, norm_gains, qkv_weight, out_weight, dy1, q_e[g], k_e[g], v_e[g], p_e[g], x_e[g],
            dq_r[g], dy1_r[g], x_r[g],
        )

    cot_e, first = mlp(0, cot)
    mlps = [first] + [mlp(g, cot_e[g])[1] for g in range(1, groups - 1)]
    attns = [attention(g, mlps[g][1]) for g in range(groups - 1)]
    last = groups - 1
    send = partial(combine, ids)
    attns, back[last] = in_order(attns, back[last])
    down, sums_down = down_grad(groups, count, ids, cot_e, back, a_e, a_r, dyb_r)
    cot_last = cot_e[last]
    if tree:
        downs = [down[0], hop(down[1], 1)]
        (down_x,), cot_last = in_order(send(send_job(downs, 0, 1)), cot_last)
        downs = downs + [hop(down_x, 2)]
    mlps.append(mlp(last, cot_last)[1])
    du_e, dy1_e, dy1b_e, sums_e = zip(*mlps)
    up, sums_up = up_grad(groups, count, ids, du_e, h2_e, dy1b_e, o_e, du_r, h2_r, dy1b_r, o_r)
    dy1_last = dy1_e[last]
    if tree:
        ups = [up[0], [hop(piece, 1) for piece in up[1:]]]
        (up_x, down_z), dy1_last = in_order(send(send_job(ups, 0, 1), send_job(downs, 1, 2)), dy1_last)
        ups = ups + [hop(up_x, 2)]
        downs = downs + [hop(down_z, 4)]
    attns.append(attention(last, dy1_last))
    dq_e, dkv_e, dx, sums_in = (list(piece) for piece in zip(*attns))
    if tree:
        (down_z,), dq_e[last] = in_order(send(send_job(downs, 2, 3)), dq_e[last])
        downs = downs + [hop(down_z, 8)]
    attn, small = qkv_grad(
        groups, count, ids, (sums_down, sums_up, *sums_e, *sums_r, *sums_in),
        dq_e, dkv_e, hq_e, hq_r, hk_r, dq_r, dkv_r,
    )
    if tree:
        downs[-1], (attn, small) = in_order(downs[-1], (attn, small))
        got = [hop(piece, 1) for piece in attn[1:]]
        got, small = in_order(got, small + hop(small, 1))
        small = small + hop(small, 2)
        qkvs = [attn[0], got]
        (qkv_x, up_z), (dx, small) = in_order(send(send_job(qkvs, 0, 1), send_job(ups, 1, 2)), (dx, small))
        qkvs = qkvs + [hop(qkv_x, 2)]
        ups = ups + [hop(up_z, 4)]
    block_out, grad_rows = place(groups, ids, visible, patch_order, dx, lat, res)
    if tree:
        (block_out, grad_rows), got = in_order((block_out, grad_rows), hop(small, 4))
        (up_z,), (block_out, grad_rows, small) = in_order(
            send(send_job(ups, 2, 3)), (block_out, grad_rows, small + got)
        )
        ups = ups + [hop(up_z, 8)]
        peers = (3, 2, 1)
        qkv_z, (block_out, grad_rows, small) = in_order(
            send(send_job(qkvs, 1, 3, peers)), (block_out, grad_rows, small)
        )
        qkv_got = [hop(one, 4 * peer) for one, peer in zip(qkv_z, peers)]
        small = small + hop(small, 8)
        down_sum, up_sum, out_sum = send(
            final_job(downs, ((0, 0),)),
            final_job(ups, tuple((1, j) for j in range(4)) + ((2, 0),)),
            outs=((D // 4, D), (D // 16, 4 * D), (D // 16, D)),
        )
        qkv_got, (down_sum, up_sum, out_sum) = in_order(qkv_got, (down_sum, up_sum, out_sum))
        (qkv_sum,) = send(final_job(qkvs + qkv_got, ((0, 1), (0, 2), (0, 0))), outs=((D // 16, 3 * D),))
    else:
        down_sum = scatter_natural(down[0])
        up_sum = jnp.concatenate([scatter_natural(one) for one in up[:4]], axis=1)
        out_sum = scatter_natural(up[4])
        qkv_sum = jnp.concatenate([scatter_natural(attn[i]) for i in (2, 0, 1)], axis=1)
        small = lax.psum(small, "dp")
    grad_rows = grad_rows.transpose(0, 2, 1, 3)
    gains, bias_rows, qv_rows, up_rows = own_columns(small, count)
    return (
        block_out,
        grad_rows,
        qkv_sum[None],
        out_sum[None],
        up_sum[None],
        down_sum[None],
        gains[None],
        bias_rows[None],
        qv_rows[None],
        up_rows[None],
    )


def solution(mesh):
    three, four = P("section", None, None), P("section", "dp", None, None)
    grad = P("section", "dp", None)
    return jax.shard_map(
        local,
        mesh=mesh,
        in_specs=(four, four, P("dp", None), P("dp"), three, three, three, three, three, three,
                  P("section", None), P("section", None), P(), P(), P(), P(), P(), P(), P(), P()),
        out_specs=(four, four, grad, grad, grad, grad, P("section", None, "dp"), P("section", None, "dp"),
                   P("section", "dp"), P("section", "dp")),
        check_vma=False,
    )
```

```python
from functools import partial

import jax
import jax.numpy as jnp
from jax import lax
from jax.experimental import pallas as pl
from jax.experimental.pallas import tpu as pltpu
from jax.sharding import PartitionSpec as P

HEADS = 12
PATCH = 196
D = 768
FF = 3072
EPS = 1e-06
NV = 144
NM = 128
FIRST = PATCH - NM
GROUP = 2
CHUNK = 32

BF = jnp.bfloat16
F32 = jnp.float32
MIB = 1024 * 1024
LIMIT = 62

HBM = pl.BlockSpec(memory_space=pl.ANY)
VMEM = pl.BlockSpec(memory_space=pltpu.VMEM)
SMEM = pl.BlockSpec(memory_space=pltpu.SMEM)


def nn(a, b):
    return jnp.dot(a, b, preferred_element_type=F32)


def nt(a, b):
    return lax.dot_general(a, b, (((1,), (1,)), ((), ())), preferred_element_type=F32)


def tn(a, b):
    return lax.dot_general(a, b, (((0,), (0,)), ((), ())), preferred_element_type=F32)


def loop(count, body, unroll=1):
    def step(i, carry):
        for u in range(unroll):
            body(i * unroll + u)
        return carry

    if count == unroll:
        step(0, 0)
    else:
        lax.fori_loop(0, count // unroll, step, 0)


def unroll_of(count):
    return next(u for u in (4, 3, 2, 1) if count % u == 0)


def rows_of(i, size):
    return pl.ds(pl.multiple_of(i * size, size), size)


def f32_row(ref, row, col=0, width=D):
    return ref[pl.ds(row, 1), pl.ds(col, width)].astype(F32)


class Copies:
    def __init__(self, sems):
        self.sems = sems
        self.used = 0
        self.open = []

    def start(self, src, dst):
        copy = pltpu.make_async_copy(src, dst, self.sems.at[self.used])
        self.used += 1
        copy.start()
        self.open.append(copy)
        return copy

    def wait(self, *copies):
        for copy in copies:
            copy.wait()
            self.open = [one for one in self.open if one is not copy]

    def finish(self):
        self.wait(*list(self.open))

    def take(self, count):
        self.used += count
        return self.used - count

    def begin(self, src, dst, at):
        pltpu.make_async_copy(src, dst, self.sems.at[at]).start()

    def wait_at(self, src, dst, at):
        pltpu.make_async_copy(src, dst, self.sems.at[at]).wait()


def gelu_pair(u):
    size = jnp.abs(u)
    base = 1.0 + (0.3275911 * 0.7071067811865476) * size
    guess = pl.reciprocal(base, approx=True)
    t = guess * (2.0 - base * guess)
    ex = jnp.exp2((u * u) * (-0.5 * 1.4426950408889634))
    poly = 0.5306027145 * t - 0.7265760135
    poly = poly * t + 0.7107068705
    poly = poly * t - 0.142248368
    poly = poly * t + 0.127414796
    tail = poly * t * ex
    phi = jnp.where(u >= 0.0, 1.0 - tail, tail)
    return u * phi, phi + u * (0.3989422804014327 * ex)


def norm_rows(src, dst, rows, gain, shift):
    def body(i):
        sel = rows_of(i, CHUNK)
        x = src[sel, :].astype(F32)
        centered = x - jnp.mean(x, axis=-1, keepdims=True)
        var = jnp.mean(centered * centered, axis=-1, keepdims=True)
        dst[sel, :] = (centered * lax.rsqrt(var + EPS) * gain + shift).astype(BF)

    loop(rows // CHUNK, body, unroll_of(rows // CHUNK))


def norm_back(src, grad, base, write, rows, gain):
    count = rows // CHUNK
    unroll = 3 if count % 3 == 0 else 2

    def step(i, carry):
        for u in range(unroll):
            carry = one(i * unroll + u, carry)
        return carry

    def one(i, carry):
        d_gain, d_shift = carry
        sel = rows_of(i, CHUNK)
        x = src[sel, :].astype(F32)
        dh = grad[sel, :]
        centered = x - jnp.mean(x, axis=-1, keepdims=True)
        var = jnp.mean(centered * centered, axis=-1, keepdims=True)
        rstd = lax.rsqrt(var + EPS)
        hat = centered * rstd
        g = dh * gain
        part = dh * hat
        dx = rstd * (
            g
            - jnp.mean(g, axis=-1, keepdims=True)
            - hat * jnp.mean(g * hat, axis=-1, keepdims=True)
        )
        if base is not None:
            dx = dx + base[sel, :].astype(F32)
        write(sel, dx)
        d_gain = d_gain + jnp.sum(part.reshape(CHUNK // 8, 8, D), axis=0)
        d_shift = d_shift + jnp.sum(dh.reshape(CHUNK // 8, 8, D), axis=0)
        return d_gain, d_shift

    zero = jnp.zeros((8, D), F32)
    d_gain, d_shift = lax.fori_loop(0, count // unroll, step, (zero, zero))
    return jnp.sum(d_gain, axis=0, keepdims=True), jnp.sum(d_shift, axis=0, keepdims=True)


def column_sum(ref, rows, col=0, width=D):
    def step(i, carry):
        x = ref[rows_of(i, CHUNK), pl.ds(col, width)].astype(F32)
        return carry + jnp.sum(x.reshape(CHUNK // 8, 8, width), axis=0)

    total = lax.fori_loop(0, rows // CHUNK, step, jnp.zeros((8, width), F32))
    return jnp.sum(total, axis=0, keepdims=True)


def as_bf16(flags):
    return jnp.where(flags, 1.0, 0.0).astype(BF)


def pick_matrix(order, image, start, count, low, high):
    row = order[image, :, pl.ds(start, count)].astype(F32)
    images = order.shape[0]
    col = jnp.broadcast_to(row, (8, count)).T[:, 0:1].astype(jnp.int32)
    rank = start + lax.broadcasted_iota(jnp.int32, (count, 1), 0)
    col = jnp.where((rank >= low) & (rank < high), col * images + image, -1)
    return as_bf16(col == lax.broadcasted_iota(jnp.int32, (count, PATCH * images), 1))


def place_matrix(order, image, start, count, low, high):
    row = order[image, :, pl.ds(start, count)]
    rank = start + lax.broadcasted_iota(jnp.int32, (1, count), 1)
    row = jnp.where((rank >= low) & (rank < high), row, -1)
    return as_bf16(row == lax.broadcasted_iota(jnp.int32, (PATCH, count), 0))


def flatten(rows, flat):
    flat[...] = rows[...].reshape(flat.shape)


def split_orders(order, split):
    for image in range(split.shape[0]):
        split[image] = order[image : image + 1, :]


def split_pair(pair):
    lane = lax.broadcasted_iota(jnp.int32, pair.shape, 1)
    zero = jnp.zeros_like(pair)
    return jnp.concatenate([jnp.where(lane < 64, pair, zero), jnp.where(lane < 64, zero, pair)], axis=0)


def join_rows(both):
    rows = both.shape[0] // 2
    lane = lax.broadcasted_iota(jnp.int32, (rows, 128), 1)
    return jnp.where(lane < 64, both[:rows], both[rows:])


def join_columns(both):
    rows = both.shape[1] // 2
    return jnp.concatenate([both[:64, :rows], both[64:, rows:]], axis=0).T


PAIRS = HEADS // 2
STEP = 6


def each_pair_group(images, body):
    def group(i):
        image = i // (PAIRS // STEP)
        first = (i % (PAIRS // STEP)) * STEP
        pairs = [first + step for step in range(STEP)]
        body(image, [image * PAIRS + pair for pair in pairs], [pl.ds(pl.multiple_of(pair * 128, 128), 128) for pair in pairs])

    loop(images * (PAIRS // STEP), group)


def softmax(scores, axis):
    ex = jnp.exp(scores - jnp.max(scores, axis=axis, keepdims=True))
    return (ex * (1.0 / jnp.sum(ex, axis=axis, keepdims=True))).astype(BF)


def score_back(probs, d_probs, axis):
    wide = probs.astype(F32)
    return (wide * (d_probs - jnp.sum(d_probs * wide, axis=axis, keepdims=True))).astype(BF)


def attention_by_rows(images, n, q, k, v, p, o, count_of):
    def body(image, slots, lanes):
        sel = rows_of(image, n)
        ok = lax.broadcasted_iota(jnp.int32, (1, n), 1) < count_of(image)
        scores = [nt(split_pair(q[sel, at]), k[sel, at]) for at in lanes]
        probs = [softmax(jnp.where(ok, one, -1000000000.0), 1) for one in scores]
        for slot, one in zip(slots, probs):
            p[slot] = one
        mixed = [nn(one, v[sel, at]) for one, at in zip(probs, lanes)]
        for at, one in zip(lanes, mixed):
            o[sel, at] = join_rows(one).astype(BF)

    each_pair_group(images, body)


def attention_by_columns(images, nk, q, k, v, p, o, key_ok):
    def body(image, slots, lanes):
        qs, ks = rows_of(image, NM), rows_of(image, nk)
        ok = key_ok(image)
        scores = [nt(k[ks, at], split_pair(q[qs, at])) for at in lanes]
        probs = [softmax(jnp.where(ok, one, -1000000000.0), 0) for one in scores]
        if p is not None:
            for slot, one in zip(slots, probs):
                p[slot] = one
        mixed = [tn(v[ks, at], one) for one, at in zip(probs, lanes)]
        for at, one in zip(lanes, mixed):
            o[qs, at] = join_columns(one).astype(BF)

    each_pair_group(images, body)


def attention_back_rows(images, n, q, k, v, p, do, dq, dkv):
    def body(image, slots, lanes):
        sel = rows_of(image, n)
        d_mixed = [split_pair(do[sel, at]) for at in lanes]
        d_probs = [nt(one, v[sel, at]) for one, at in zip(d_mixed, lanes)]
        d_scores = [score_back(p[slot], one, 1) for slot, one in zip(slots, d_probs)]
        d_values = [tn(p[slot], one) for slot, one in zip(slots, d_mixed)]
        d_query = [nn(one, k[sel, at]) for one, at in zip(d_scores, lanes)]
        d_keys = [tn(one, split_pair(q[sel, at])) for one, at in zip(d_scores, lanes)]
        for at, value, query, key in zip(lanes, d_values, d_query, d_keys):
            dq[sel, at] = (join_rows(query) * 0.125).astype(BF)
            dkv[sel, at] = key.astype(BF)
            dkv[sel, pl.ds(pl.multiple_of(D + at.start, 128), 128)] = value.astype(BF)

    each_pair_group(images, body)


def attention_back_columns(images, nk, q, k, v, p, do, dq, dkv):
    def body(image, slots, lanes):
        qs, ks = rows_of(image, NM), rows_of(image, nk)
        d_mixed = [split_pair(do[qs, at]) for at in lanes]
        d_probs = [nt(v[ks, at], one) for one, at in zip(d_mixed, lanes)]
        d_scores = [score_back(p[slot], one, 0) for slot, one in zip(slots, d_probs)]
        d_values = [nn(p[slot], one) for slot, one in zip(slots, d_mixed)]
        d_query = [tn(k[ks, at], one) for one, at in zip(d_scores, lanes)]
        d_keys = [nn(one, split_pair(q[qs, at])) for one, at in zip(d_scores, lanes)]
        for at, value, query, key in zip(lanes, d_values, d_query, d_keys):
            dq[qs, at] = (join_columns(query) * 0.125).astype(BF)
            dkv[ks, at] = key.astype(BF)
            dkv[ks, pl.ds(pl.multiple_of(D + at.start, 128), 128)] = value.astype(BF)

    each_pair_group(images, body)


HALF = 512


def mlp_forward(rows, h2, w1, w2, up_b, u, a, gp, tile, acc, out, base):
    acc[...] = base()
    steps = FF // HALF

    def multiply(t):
        u[t % 2] = nn(h2[...], w1[:, t * HALF : (t + 1) * HALF])

    def add(t):
        acc[...] += nn(tile[t % 2], w2[t * HALF : (t + 1) * HALF, :])

    multiply(0)
    for t in range(steps):
        if t + 1 < steps:
            multiply(t + 1)
        if t > 0:
            add(t - 1)
        for c in range(0, HALF, 256):
            at = slice(t * HALF + c, t * HALF + c + 256)
            shift = up_b[0:1, at].astype(F32)
            for r in range(0, rows, CHUNK):
                sel = slice(r, r + CHUNK)
                value, slope = gelu_pair(u[t % 2, sel, c : c + 256] + shift)
                low = value.astype(BF)
                tile[t % 2, sel, c : c + 256] = low
                if a is not None:
                    a[sel, at] = low
                if gp is not None:
                    gp[sel, at] = slope.astype(BF)
    add(steps - 1)
    out[...] = acc[...].astype(BF)


def mlp_back(rows, dyb, gp, w1, w2, du, u, acc, ready=lambda i, which: None, flipped=False):
    acc[...] = jnp.zeros_like(acc)

    def body(i):
        cols = [pl.ds(pl.multiple_of((2 * i + part) * HALF, HALF), HALF) for part in range(2)]
        ready(i, 0)
        for part in range(2):
            u[part] = nn(dyb[...], w2[:, cols[part]]) if flipped else nt(dyb[...], w2[cols[part], :])
        ready(i, 1)
        for part in range(2):
            for r in range(0, rows, CHUNK):
                sel = slice(r, r + CHUNK)
                du[sel, cols[part]] = (gp[sel, cols[part]].astype(F32) * u[part, sel, :]).astype(BF)
            own = du[:, cols[part]]
            acc[...] += nn(own, w1[cols[part], :]) if flipped else nt(own, w1[:, cols[part]])

    loop(FF // (2 * HALF), body)


def project(count, rows, left, weight, first, write):
    def body(j):
        write(j, nn(left[...], weight[:, pl.ds(pl.multiple_of((first + j) * D, D), D)]))

    loop(count, body)


def set_biases(ref, bias):
    ref[0] = f32_row(bias, 0)
    ref[1] = jnp.zeros((1, D), F32)
    ref[2] = f32_row(bias, 0, D)


def cost(flops, nbytes):
    return pl.CostEstimate(flops=int(flops), bytes_accessed=int(nbytes), transcendentals=0)


def params(mib):
    return pltpu.CompilerParams(vmem_limit_bytes=mib * MIB)


def struct(shape, dtype=BF):
    return jax.ShapeDtypeStruct(shape, dtype)


def start_weights(copies, sources, scratch):
    return [copies.start(src, dst) for src, dst in zip(sources, scratch)]


def encode_kernel(group, groups, ids, visible, order_in, gains, biases, qvb, upb, rows, cot, wqkv, wo, w1, w2,
                  lat_out, x_out, hq_out, q_out, k_out, v_out, p_out, o_out, y1_out, h2_out, gp_out, a_out, *refs):
    ready, refs = refs[: 4 * groups], refs[4 * groups :]
    if group == 0:
        w1t_out, w2t_out, s1t, s2t, *refs = refs
    (order, rows_v, flat, sqkv, so, s1, s2, x, hq, qkv, p, o, y1, h2, gp, a, u, tile, acc, shifts, lat, sems) = refs
    n = GROUP * NV
    split_orders(order_in, order)

    @pl.when(ids[0] == 0)
    def _():
        copies = Copies(sems)
        got_rows = copies.start(rows.at[0], rows_v)
        got_qkv, got_o, got_1, got_2 = start_weights(
            copies, (wqkv.at[0], wo.at[0], w1.at[0], w2.at[0]), (sqkv, so, s1, s2)
        )
        gain, bias = gains.at[0], biases.at[0]
        set_biases(shifts, qvb)
        copies.wait(got_rows)
        flatten(rows_v, flat)

        def pick_rows(i):
            image = group * GROUP + i
            pick = pick_matrix(order, image, 0, NV, 0, visible[image])
            x[rows_of(i, NV), :] = nn(pick, flat[...]).astype(BF)

        loop(GROUP, pick_rows)
        copies.start(x, x_out)
        norm_rows(x, hq, n, f32_row(gain, 0), f32_row(bias, 0))
        copies.start(hq, hq_out)
        copies.wait(got_qkv)

        def keep(j, value):
            scale = jnp.where(j == 0, 0.125, 1.0)
            qkv[j] = ((value + shifts[j]).astype(BF).astype(F32) * scale).astype(BF)

        project(3, n, hq, sqkv, 0, keep)
        q, k, v = qkv.at[0], qkv.at[1], qkv.at[2]
        copies.start(q, q_out)
        copies.start(k, k_out)
        copies.start(v, v_out)
        attention_by_rows(GROUP, NV, q, k, v, p, o, lambda i: visible[group * GROUP + i])
        copies.start(p, p_out)
        copies.start(o, o_out)
        copies.wait(got_o)
        y1[...] = nn(o[...], so[...]) + f32_row(bias, 1) + x[...].astype(F32)
        copies.start(y1, y1_out)
        norm_rows(y1, h2, n, f32_row(gain, 1), f32_row(bias, 2))
        copies.start(h2, h2_out)
        copies.wait(got_1, got_2)
        mlp_forward(n, h2, s1, s2, upb, u, a, gp, tile, acc, lat, lambda: y1[...] + f32_row(bias, 3))
        copies.start(gp, gp_out)
        copies.start(a, a_out)
        copies.start(lat, lat_out)
        copies.finish()

    if group == 0:

        @pl.when(ids[0] == 1)
        def _():
            copies = Copies(sems)
            got_2, got_1 = copies.start(w2.at[0], s2), copies.start(w1.at[0], s1)
            copies.wait(got_2)

            def turn_down(i):
                at = rows_of(i, 256)
                s2t[:, at] = s2[at, :].T

            loop(FF // 256, turn_down)
            copies.start(s2t, w2t_out)
            copies.wait(got_1)

            def turn_up(i):
                at = rows_of(i, 256)
                s1t[at, :] = s1[:, at].T

            loop(FF // 256, turn_up)
            copies.start(s1t, w1t_out)
            copies.finish()

    if group == groups - 1:

        @pl.when(ids[0] == 1)
        def _():
            copies = Copies(sems)
            m = GROUP * NM
            x_out, hq_out, q_out, dyb_out = (ready[i * groups : (i + 1) * groups] for i in range(4))
            gain, bias = gains.at[0], biases.at[0]
            got_rows = copies.start(rows.at[0], rows_v)
            got_q = copies.start(wqkv.at[0, :, pl.ds(0, D)], so)
            copies.wait(got_rows)
            flatten(rows_v, flat)
            got_cot = copies.start(cot.at[0], rows_v)
            top = pl.ds(0, m)

            def pick_group(g):
                def pick_rows(i):
                    image = g * GROUP + i
                    pick = pick_matrix(order, image, FIRST, NM, visible[image], PATCH)
                    x[rows_of(i, NM), :] = nn(pick, flat[...]).astype(BF)

                loop(GROUP, pick_rows)

            for g in range(groups):
                pick_group(g)
                norm_rows(x, hq, m, f32_row(gain, 0), f32_row(bias, 0))
                sent = [copies.start(x.at[top], x_out[g]), copies.start(hq.at[top], hq_out[g])]
                if g == 0:
                    copies.wait(got_q)
                q = qkv.at[g]
                q[top, :] = ((nn(hq[top, :], so[...]) + f32_row(qvb, 0)).astype(BF) * 0.125).astype(BF)
                copies.start(q.at[top], q_out[g])
                copies.wait(*sent)
            copies.wait(got_cot)
            flatten(rows_v, flat)
            for g in range(groups):
                pick_group(g)
                copies.wait(copies.start(x.at[top], dyb_out[g]))
            copies.finish()


def encode(group, groups, ids, visible, order, gains, biases, qvb, upb, rows, cot, weights):
    n = GROUP * NV
    images = order.shape[0]
    row, wide = struct((n, D)), struct((n, FF))
    heads = struct((GROUP * PAIRS, 2 * NV, NV))
    outs = [row] * 6 + [heads, row, struct((n, D), F32), row, wide, wide] + [struct((GROUP * NM, D))] * (4 * groups)
    vm = lambda s: pltpu.VMEM(s.shape, s.dtype)
    flipped = [struct((FF, D)), struct((D, FF))] if group == 0 else []
    outs += flipped
    scratch = [vm(one) for one in flipped] + [
        pltpu.VMEM((images, 1, PATCH), jnp.int32),
        pltpu.VMEM((PATCH, images, D), BF), pltpu.VMEM((PATCH * images, D), BF),
        pltpu.VMEM((D, 3 * D), BF), pltpu.VMEM((D, D), BF), pltpu.VMEM((D, FF), BF), pltpu.VMEM((FF, D), BF),
        vm(row), vm(row), pltpu.VMEM((3, n, D), BF), vm(heads), vm(row), pltpu.VMEM((n, D), F32), vm(row),
        vm(wide), vm(wide), pltpu.VMEM((2, n, HALF), F32), pltpu.VMEM((2, n, HALF), BF), pltpu.VMEM((n, D), F32),
        pltpu.VMEM((3, 1, D), F32), vm(row),
        pltpu.SemaphoreType.DMA((24,)),
    ]
    got = pl.pallas_call(
        partial(encode_kernel, group, groups),
        in_specs=[SMEM, SMEM] + [VMEM] * 5 + [HBM] * 6,
        out_specs=[HBM] * len(outs),
        out_shape=outs,
        scratch_shapes=scratch,
        compiler_params=params(LIMIT),
        cost_estimate=cost(2 * n * 12 * D * D, 25e6),
        name="encode",
    )(ids, visible, order, gains, biases, qvb, upb, rows, cot, *weights)
    ready = got[12:]
    return got[:12], [ready[i * groups : (i + 1) * groups] for i in range(4)], ready[4 * groups :]


def middle_kernel(group, ids, visible, order_in, gains, biases, qvb, upb, tgains, tbiases, tqvb, tupb,
                  rows, lat_in, x_in, q_in, dyb_in, wqkv, wo, w1, w2, w1t, w2t, tqkv, to, t1, t2,
                  dlat_out, res_out, hk_out, dq_out, dkv_out, o_out, dy1b_out, h2_out, du_out, a_out,
                  dy1_out, sums_out,
                  order, rows_v, flat, sqkv, so, s1, s2, s1t, s2t, x, lat, hq, hk, q, kv, p, o, y1, h2, gp, a, u, tile, acc, shifts,
                  res, dyb, du, dy1, dy1b, do, dq, dkv, dh, dlat, sums, sems):
    n, m = GROUP * NM, GROUP * NV
    top = pl.ds(0, n)
    k, v = kv.at[0], kv.at[1]
    split_orders(order_in, order)

    def forward(copies, got_weights, gain, bias, ub, nk, key_ok, keep_p, keep_a, keep_slope):
        got_o, got_1, got_2 = got_weights
        attention_by_columns(GROUP, nk, q, k, v, keep_p, o, key_ok)
        copies.wait(got_o)
        y1[...] = nn(o[...], so[...]) + f32_row(bias, 1) + x[...].astype(F32)
        norm_rows(y1, h2, n, f32_row(gain, 1), f32_row(bias, 2))
        copies.wait(got_1, got_2)
        mlp_forward(n, h2, s1, s2, ub, u, keep_a, keep_slope, tile, acc, res, lambda: y1[...] + f32_row(bias, 3))
        copies.start(res, res_out)

    @pl.when(ids[0] == 0)
    def _():
        copies = Copies(sems)
        gain, bias = tgains, tbiases
        got_rows = copies.start(rows.at[0], rows_v)
        got_qkv = copies.start(tqkv, sqkv)
        got_weights = start_weights(copies, (to, t1, t2), (so, s1, s2))
        copies.wait(got_rows)
        flatten(rows_v, flat)

        def pick_rows(i):
            image = group * GROUP + i
            pick = pick_matrix(order, image, FIRST, NM, visible[image], PATCH)
            x[rows_of(i, NM), :] = nn(pick, flat[...]).astype(BF)

        loop(GROUP, pick_rows)
        norm_rows(x, hq, n, f32_row(gain, 0), f32_row(bias, 0))
        copies.wait(got_qkv)
        set_biases(shifts, tqvb)
        q[...] = ((nn(hq[...], sqkv[:, :D]) + f32_row(tqvb, 0)).astype(BF) * 0.125).astype(BF)

        def keep_kv(j, value):
            kv[j, top, :] = (value + shifts[j + 1]).astype(BF)

        project(2, n, hq, sqkv, 1, keep_kv)

        def key_ok(i):
            return lax.broadcasted_iota(jnp.int32, (NM, 1), 0) + FIRST >= visible[group * GROUP + i]

        forward(copies, got_weights, gain, bias, tupb, NM, key_ok, None, None, None)
        copies.finish()

    @pl.when(ids[0] == 1)
    def _():
        copies = Copies(sems)
        gain, bias = gains.at[0], biases.at[0]
        got_lat = copies.start(lat_in, lat)
        got_kv = copies.start(wqkv.at[0, :, pl.ds(D, 2 * D)], sqkv.at[:, pl.ds(D, 2 * D)])
        got_q = copies.start(q_in, q)
        got_x = copies.start(x_in, x)
        got_weights = start_weights(copies, (wo.at[0], w1.at[0], w2.at[0]), (so, s1, s2))
        got_dyb = copies.start(dyb_in, dyb)
        got_back = [copies.start(w2t, s2t), copies.start(w1t, s1t)]
        copies.wait(got_lat)
        norm_rows(lat, hk, m, f32_row(gain, 0), f32_row(bias, 0))
        copies.start(hk, hk_out)
        copies.wait(got_kv)
        set_biases(shifts, qvb)

        def keep_kv(j, value):
            kv[j] = (value + shifts[j + 1]).astype(BF)

        project(2, m, hk, sqkv, 1, keep_kv)
        copies.wait(got_q, got_x)

        def key_ok(i):
            return lax.broadcasted_iota(jnp.int32, (NV, 1), 0) < visible[group * GROUP + i]

        forward(copies, got_weights, gain, bias, upb.at[0:1], NV, key_ok, p, a, gp)
        copies.start(o, o_out)
        copies.start(h2, h2_out)
        copies.start(a, a_out)
        copies.wait(got_dyb, *got_back)
        mlp_back(n, dyb, gp, s1t, s2t, du, u, acc, flipped=True)
        copies.start(du, du_out)

        def keep(sel, dx):
            dy1[sel, :] = dx
            dy1b[sel, :] = dx.astype(BF)

        g2, b2 = norm_back(y1, acc, dyb, keep, n, f32_row(gain, 1))
        copies.start(dy1, dy1_out)
        copies.start(dy1b, dy1b_out)
        do[...] = nt(dy1b[...], so[...]).astype(BF)
        attention_back_columns(GROUP, NV, q, k, v, p, do, dq, dkv)
        copies.start(dq, dq_out)
        copies.start(dkv, dkv_out)
        dh[...] = nt(dkv[:, :D], sqkv[:, D : 2 * D])
        dh[...] += nt(dkv[:, D:], sqkv[:, 2 * D :])

        def keep_side(sel, dx):
            dlat[sel, :] = dx.astype(BF)

        gk, bk = norm_back(lat, dh, None, keep_side, m, f32_row(gain, 0))
        copies.start(dlat, dlat_out)
        for row, value in enumerate((gk, g2, bk, b2)):
            sums[pl.ds(row, 1), :] = value
        copies.start(sums, sums_out)
        copies.finish()


def middle(group, ids, visible, order, own_vecs, target_vecs, rows, lat, x, q, dyb, weights, flipped, targets):
    n, m = GROUP * NM, GROUP * NV
    row, side, wide = struct((n, D)), struct((m, D)), struct((n, FF))
    pair = struct((m, 2 * D))
    outs = [side, row, side, row, pair, row, row, row, wide, wide, struct((n, D), F32), struct((8, D), F32)]
    vm = lambda s: pltpu.VMEM(s.shape, s.dtype)
    full, fside = pltpu.VMEM((n, D), F32), pltpu.VMEM((m, D), F32)
    scratch = [
        pltpu.VMEM((order.shape[0], 1, PATCH), jnp.int32),
        pltpu.VMEM((PATCH, order.shape[0], D), BF), pltpu.VMEM((PATCH * order.shape[0], D), BF),
        pltpu.VMEM((D, 3 * D), BF), pltpu.VMEM((D, D), BF), pltpu.VMEM((D, FF), BF), pltpu.VMEM((FF, D), BF),
        pltpu.VMEM((FF, D), BF), pltpu.VMEM((D, FF), BF),
        vm(row), vm(side), vm(row), vm(side), vm(row), pltpu.VMEM((2, m, D), BF),
        pltpu.VMEM((GROUP * PAIRS, NV, 2 * NM), BF), vm(row), full, vm(row), vm(wide), vm(wide),
        pltpu.VMEM((2, n, HALF), F32), pltpu.VMEM((2, n, HALF), BF), full, pltpu.VMEM((3, 1, D), F32),
        vm(row), vm(row), vm(wide), full, vm(row), vm(row), vm(row), vm(pair), fside, vm(side),
        pltpu.VMEM((8, D), F32),
        pltpu.SemaphoreType.DMA((24,)),
    ]
    return pl.pallas_call(
        partial(middle_kernel, group),
        in_specs=[SMEM, SMEM] + [VMEM] * 9 + [HBM] * 15,
        out_specs=[HBM] * len(outs),
        out_shape=outs,
        scratch_shapes=scratch,
        compiler_params=params(LIMIT),
        cost_estimate=cost(4 * n * 12 * D * D, 25e6),
        name="middle",
    )(ids, visible, order, *own_vecs, *target_vecs, rows, lat, x, q, dyb, *weights, *flipped, *targets)


def stack_rows(copies, pieces, ref, size):
    return [copies.start(piece, ref.at[pl.ds(i * size, size)]) for i, piece in enumerate(pieces)]


def turn_rows(ref, turned, count):
    def step(i, carry):
        turned[i] = ref[i].T
        return carry

    lax.fori_loop(0, count, step, 0)


def clear_tail(ref, used):
    ref[pl.ds(used, ref.shape[0] - used), :] = jnp.zeros((ref.shape[0] - used, ref.shape[1]), ref.dtype)


def halves(count, blocks):
    rows = D // 16
    if count == 16:
        return [struct((2, 2, 2, blocks, rows, D))] + [struct((2, blocks, rows, D))] * 4
    return [struct((D, D))] * blocks


def give_blocks(copies, core, tree, left_right, out, dest):
    size = 8 if tree else 1
    blocks = out.shape[0]
    first = copies.take(blocks * size)

    def send(j, act):
        if not tree:
            for block in range(blocks):
                pl.when(j == block)(lambda block=block: act(out.at[block], dest[block], first + block))
            return
        view = out.at[j].reshape(2, 2, 2, 2, D // 16, D)
        for x in range(2):
            for low in range(2):
                at = first + j * size + 4 * x + 2 * low
                act(view.at[:, low, x, core], dest[0].at[x, low, :, j], at)
                act(view.at[:, low, x, 1 - core], dest[1 + 2 * x + low].at[:, j], at + 1)

    def body(j):
        out[j] = left_right(j)
        send(j, copies.begin)

    loop(blocks, body)
    loop(blocks, lambda j: send(j, copies.wait_at))


def down_kernel(groups, ids, *refs):
    cot, lat, a_enc, a_reg, dyb_reg = (refs[i * groups : (i + 1) * groups] for i in range(5))
    dest, sums_out, cot_v, dyb, a, dlat, out, sums, sems = refs[5 * groups :]
    images = groups * GROUP
    nv, nm = GROUP * NV, GROUP * NM

    @pl.when(ids[0] == 0)
    def _():
        copies = Copies(sems)
        got = stack_rows(copies, cot, cot_v, nv) + stack_rows(copies, lat, dlat, nv)
        stack_rows(copies, a_enc, a, nv)
        copies.wait(*got)
        dyb[...] = (cot_v[...].astype(F32) + dlat[...].astype(F32)).astype(BF)
        copies.finish()

    @pl.when(ids[0] == 1)
    def _():
        copies = Copies(sems)
        stack_rows(copies, a_reg, a, nm)
        stack_rows(copies, dyb_reg, dyb, nm)
        clear_tail(a, images * NM)
        clear_tail(dyb, images * NM)
        copies.finish()

    copies = Copies(sems)

    first = copies.take(4)

    def body(j):
        out[j] = tn(a[:, rows_of(j, D)], dyb[...]).astype(BF)
        copies.begin(out.at[j], dest.at[rows_of(j, D)], first + j)

    loop(4, body)
    loop(4, lambda j: copies.wait_at(out.at[j], dest.at[rows_of(j, D)], first + j))
    sums[...] = jnp.broadcast_to(column_sum(dyb, images * NV), (8, D))
    copies.start(sums, sums_out)
    copies.finish()


def down_grad(groups, ids, cot, dlat, a_enc, a_reg, dyb_reg):
    n = groups * GROUP * NV
    outs = [struct((FF, D)), struct((8, D), F32)]
    row = pltpu.VMEM((n, D), BF)
    scratch = [
        row, row, pltpu.VMEM((n, FF), BF), row, pltpu.VMEM((4, D, D), BF), pltpu.VMEM((8, D), F32),
        pltpu.SemaphoreType.DMA((24,)),
    ]
    return pl.pallas_call(
        partial(down_kernel, groups),
        in_specs=[SMEM] + [HBM] * (5 * groups),
        out_specs=[HBM] * len(outs),
        out_shape=outs,
        scratch_shapes=scratch,
        compiler_params=params(LIMIT),
        cost_estimate=cost(1e6, 1e5),
        name="down_grad",
    )(ids, *cot, *dlat, *a_enc, *a_reg, *dyb_reg)


def mlp_kernel(first, groups, ids, visible, order_in, gains, cot, dlat_in, w1, w2, y1_in, gp_in, *refs):
    if first:
        picked, refs = refs[:groups], refs[groups:]
    du_out, dy1_out, dy1b_out, sums_out, order, rows_v, flat, refs = *refs[:7], refs[7:]
    s1, s2, cot_v, dlat, dyb, gp, y1, du, u, acc, dy1, dy1b, sums, sems = refs
    n = GROUP * NV
    third = FF // 3

    @pl.when(ids[0] == 0)
    def _():
        copies = Copies(sems)
        got = [copies.start(dlat_in, dlat)]
        if first:
            got_rows = copies.start(cot.at[0], rows_v)
        else:
            got.append(copies.start(cot, cot_v))
        start = copies.take(9)

        def parts(i):
            cols = pl.ds(pl.multiple_of(i * third, third), third)
            return (
                (w2.at[0, cols, :], s2.at[cols, :]),
                (gp_in.at[:, cols], gp.at[:, cols]),
                (w1.at[0, :, cols], s1.at[:, cols]),
            )

        for i in range(3):
            for k, (src, dst) in enumerate(parts(i)):
                copies.begin(src, dst, start + 3 * i + k)
        got_y = copies.start(y1_in, y1)

        def ready(i, which):
            for k in ((0, 1), (2,))[which]:
                copies.wait_at(*parts(i)[k], start + 3 * i + k)

        if first:
            split_orders(order_in, order)
            copies.wait(got_rows)
            flatten(rows_v, flat)
            for g in reversed(range(groups)):

                def pick_rows(i, g=g):
                    image = g * GROUP + i
                    pick = pick_matrix(order, image, 0, NV, 0, visible[image])
                    cot_v[rows_of(i, NV), :] = nn(pick, flat[...]).astype(BF)

                loop(GROUP, pick_rows)
                copies.wait(copies.start(cot_v, picked[g]))
        copies.wait(*got)
        dyb[...] = (cot_v[...].astype(F32) + dlat[...].astype(F32)).astype(BF)
        mlp_back(n, dyb, gp, s1, s2, du, u, acc, ready)
        copies.start(du, du_out)
        copies.wait(got_y)

        def keep(sel, dx):
            dy1[sel, :] = dx
            dy1b[sel, :] = dx.astype(BF)

        g2, b2 = norm_back(y1, acc, dyb, keep, n, f32_row(gains.at[0], 1))
        copies.start(dy1, dy1_out)
        copies.start(dy1b, dy1b_out)
        sums[pl.ds(0, 1), :] = g2
        sums[pl.ds(1, 1), :] = b2
        copies.start(sums, sums_out)
        copies.finish()


def mlp_grad(first, groups, ids, visible, order, gains, cot, dlat, w1, w2, y1, gp):
    n = GROUP * NV
    images = order.shape[0]
    row, wide, full = pltpu.VMEM((n, D), BF), pltpu.VMEM((n, FF), BF), pltpu.VMEM((n, D), F32)
    outs = [struct((n, D))] * (groups if first else 0) + [struct((n, FF)), struct((n, D), F32), struct((n, D)), struct((8, D), F32)]
    got = pl.pallas_call(
        partial(mlp_kernel, first, groups),
        in_specs=[SMEM, SMEM, VMEM, VMEM] + [HBM] * 6,
        out_specs=[HBM] * len(outs),
        out_shape=outs,
        scratch_shapes=[
            pltpu.VMEM((images, 1, PATCH), jnp.int32),
            pltpu.VMEM((PATCH, images, D), BF), pltpu.VMEM((PATCH * images, D), BF),
            pltpu.VMEM((D, FF), BF), pltpu.VMEM((FF, D), BF), row, row, row, wide, full, wide,
            pltpu.VMEM((2, n, HALF), F32), full, full, row, pltpu.VMEM((8, D), F32), pltpu.SemaphoreType.DMA((24,)),
        ],
        compiler_params=params(LIMIT),
        cost_estimate=cost(1e6, 1e5),
        name="mlp_grad",
    )(ids, visible, order, gains, cot, dlat, w1, w2, y1, gp)
    return got[:-4], got[-4:]


def up_kernel(groups, parts, ids, *refs):
    pieces = [refs[i * groups : (i + 1) * groups] for i in range(8)]
    refs = refs[8 * groups :]
    dest, refs = refs[:parts], refs[parts:]
    sums_out, left, right, turned, out, sums, sems = refs
    images = groups * GROUP

    def load(du, h2, dy1b, o, size):
        copies = Copies(sems)
        stack_rows(copies, h2, left.at[0], size)
        for j in range(4):
            stack_rows(copies, [one.at[:, pl.ds(j * D, D)] for one in du], right.at[j], size)
        stack_rows(copies, o, left.at[1], size)
        stack_rows(copies, dy1b, right.at[4], size)
        return copies

    @pl.when(ids[0] == 0)
    def _():
        load(*pieces[:4], GROUP * NV).finish()

    @pl.when(ids[0] == 1)
    def _():
        copies = load(*pieces[4:], GROUP * NM)
        for ref in (left, right):
            for i in range(ref.shape[0]):
                clear_tail(ref.at[i], images * NM)
        copies.finish()

    copies = Copies(sems)

    def multiply(j):
        value = nn(turned[lax.div(j, 4)], right[j]).astype(BF)
        sums[pl.ds(j, 1), :] = column_sum(right.at[j], images * NV)
        return value

    turn_rows(left, turned, 2)

    give_blocks(copies, ids[1], dest[0].ndim == 6, multiply, out, dest)
    copies.start(sums, sums_out)
    copies.finish()


def up_grad(groups, count, ids, *pieces):
    n = groups * GROUP * NV
    main = halves(count, 5)
    outs = main + [struct((8, D), F32)]
    got = pl.pallas_call(
        partial(up_kernel, groups, len(main)),
        in_specs=[SMEM] + [HBM] * (8 * groups),
        out_specs=[HBM] * len(outs),
        out_shape=outs,
        scratch_shapes=[
            pltpu.VMEM((2, n, D), BF), pltpu.VMEM((5, n, D), BF), pltpu.VMEM((2, D, n), BF), pltpu.VMEM((5, D, D), BF),
            pltpu.VMEM((8, D), F32),
            pltpu.SemaphoreType.DMA((44,)),
        ],
        compiler_params=params(LIMIT),
        cost_estimate=cost(1e6, 1e5),
        name="up_grad",
    )(ids, *[ref for piece in pieces for ref in piece])
    return got[: len(main)], got[-1]


def attn_kernel(ids, gains, wqkv, wo, dy1_enc, q_in, k_in, v_in, p_in, x_enc, dq_reg, dy1_reg, x_reg,
                dq_out, dkv_out, dx_out, sums_out,
                sqkv, so, dy1, dy1b, q, k, v, p, x, do, dq, dkv, dh, sums, sems):
    m = GROUP * NM
    top = pl.ds(0, m)
    gain = f32_row(gains.at[0], 0)

    def finish(copies, rows):
        def keep(sel, dx):
            dy1[sel, :] = dx

        g1, b1 = norm_back(x, dh, dy1, keep, rows, gain)
        copies.start(dy1, dx_out)
        sums[0:1, :] = g1
        sums[1:2, :] = b1
        copies.start(sums, sums_out)
        copies.finish()

    @pl.when(ids[0] == 0)
    def _():
        copies = Copies(sems)
        got = [copies.start(dy1_enc, dy1), copies.start(wo.at[0], so)]
        later = [copies.start(src, dst) for src, dst in ((v_in, v), (p_in, p), (k_in, k), (q_in, q))]
        last = [copies.start(wqkv.at[0], sqkv), copies.start(x_enc, x)]
        copies.wait(*got)
        dy1b[...] = dy1[...].astype(BF)
        do[...] = nt(dy1b[...], so[...]).astype(BF)
        copies.wait(*later)
        attention_back_rows(GROUP, NV, q, k, v, p, do, dq, dkv)
        copies.start(dq, dq_out)
        copies.start(dkv, dkv_out)
        copies.wait(*last)
        dh[...] = nt(dq[...], sqkv[:, 0:D])
        for j in range(2):
            dh[...] += nt(dkv[:, j * D : (j + 1) * D], sqkv[:, (j + 1) * D : (j + 2) * D])
        finish(copies, GROUP * NV)

    @pl.when(ids[0] == 1)
    def _():
        copies = Copies(sems)
        for src, dst in ((dq_reg, dq), (dy1_reg, dy1), (x_reg, x)):
            copies.start(src, dst.at[top])
        copies.start(wqkv.at[0, :, pl.ds(0, D)], sqkv.at[:, pl.ds(0, D)])
        copies.finish()
        dh[top, :] = nt(dq[top, :], sqkv[:, 0:D])
        finish(copies, m)


def attn_back(ids, gains, wqkv, wo, *pieces):
    n = GROUP * NV
    row, full = pltpu.VMEM((n, D), BF), pltpu.VMEM((n, D), F32)
    outs = [struct((n, D)), struct((n, 2 * D)), struct((n, D), F32), struct((8, D), F32)]
    return pl.pallas_call(
        attn_kernel,
        in_specs=[SMEM, VMEM] + [HBM] * (2 + len(pieces)),
        out_specs=[HBM] * len(outs),
        out_shape=outs,
        scratch_shapes=[
            pltpu.VMEM((D, 3 * D), BF), pltpu.VMEM((D, D), BF), full, row, row, row, row,
            pltpu.VMEM((GROUP * PAIRS, 2 * NV, NV), BF), row, row, row, pltpu.VMEM((n, 2 * D), BF), full,
            pltpu.VMEM((8, D), F32), pltpu.SemaphoreType.DMA((20,)),
        ],
        compiler_params=params(LIMIT),
        cost_estimate=cost(1e6, 1e5),
        name="attn_back",
    )(ids, gains, wqkv, wo, *pieces)


def qkv_kernel(groups, parts, ids, down_sums, up_sums, *refs):
    mlp_sums, reg_sums, in_sums = (refs[i * groups : (i + 1) * groups] for i in range(3))
    refs = refs[3 * groups :]
    pieces = [refs[i * groups : (i + 1) * groups] for i in range(7)]
    dq_enc, dkv_enc, hq_enc, hq_reg, hk_reg, dq_reg, dkv_reg = pieces
    refs = refs[7 * groups :]
    dest, refs = refs[:parts], refs[parts:]
    small, left, right, turned, out, sems = refs
    images = groups * GROUP
    nv, nm = GROUP * NV, GROUP * NM
    hk, hq = left.at[0], left.at[1]
    dk, dv, dq = (right.at[i] for i in range(3))

    @pl.when(ids[0] == 0)
    def _():
        copies = Copies(sems)
        stack_rows(copies, hq_enc, hk, nv)
        stack_rows(copies, [one.at[:, pl.ds(0, D)] for one in dkv_enc], dk, nv)
        stack_rows(copies, [one.at[:, pl.ds(D, D)] for one in dkv_enc], dv, nv)
        stack_rows(copies, hq_enc, hq, nv)
        stack_rows(copies, dq_enc, dq, nv)
        copies.finish()

    @pl.when(ids[0] == 1)
    def _():
        copies = Copies(sems)
        for piece, ref in ((hq_reg, hq), (dq_reg, dq)):
            stack_rows(copies, piece, ref, nm)
            clear_tail(ref, images * NM)
        stack_rows(copies, hk_reg, hk, nv)
        stack_rows(copies, [one.at[:, pl.ds(0, D)] for one in dkv_reg], dk, nv)
        stack_rows(copies, [one.at[:, pl.ds(D, D)] for one in dkv_reg], dv, nv)
        copies.finish()

    copies = Copies(sems)

    def multiply(j):
        return nn(turned[jnp.where(ids[0] == 0, 0, lax.div(j, 2))], right[j]).astype(BF)

    turn_rows(left, turned, jnp.where(ids[0] == 0, 1, 2))

    give_blocks(copies, ids[1], dest[0].ndim == 6, multiply, out, dest)

    def total_of(sums):
        total = sums[0][...]
        for more in sums[1:]:
            total = total + more[...]
        return total

    first, mlp, reg = total_of(in_sums), total_of(mlp_sums), total_of(reg_sums)
    encoder = ids[0] == 0
    small[0:1, :] = first[0:1, :] + jnp.where(encoder, 0.0, reg[0:1, :])
    small[1:2, :] = jnp.where(encoder, mlp[0:1, :], reg[1:2, :])
    small[2:3, :] = first[1:2, :] + jnp.where(encoder, 0.0, reg[2:3, :])
    small[3:4, :] = up_sums[4:5, :]
    small[4:5, :] = jnp.where(encoder, mlp[1:2, :], reg[3:4, :])
    small[5:6, :] = down_sums[0:1, :]
    small[6:7, :] = column_sum(dq, images * NV)
    small[7:8, :] = column_sum(dv, images * NV)
    small[8:12, :] = up_sums[0:4, :]
    small[12:16, :] = jnp.zeros((4, D), F32)
    copies.finish()


def qkv_grad(groups, count, ids, sums, *pieces):
    n = groups * GROUP * NV
    row = pltpu.VMEM((n, D), BF)
    main = halves(count, 3)
    outs = main + [struct((16, D), F32)]
    scratch = [
        pltpu.VMEM((2, n, D), BF), pltpu.VMEM((3, n, D), BF), pltpu.VMEM((2, D, n), BF), pltpu.VMEM((3, D, D), BF),
        pltpu.SemaphoreType.DMA((40,)),
    ]
    got = pl.pallas_call(
        partial(qkv_kernel, groups, len(main)),
        in_specs=[SMEM] + [VMEM] * (2 + 3 * groups) + [HBM] * (7 * groups),
        out_specs=[HBM] * len(main) + [VMEM],
        out_shape=outs,
        scratch_shapes=scratch,
        compiler_params=params(LIMIT),
        cost_estimate=cost(1e6, 1e5),
        name="qkv_grad",
    )(ids, *sums, *[ref for piece in pieces for ref in piece])
    return got[: len(main)], got[-1]


def place_kernel(groups, ids, visible, order_in, *refs):
    dx_in, lat_enc, res = (refs[i * groups : (i + 1) * groups] for i in range(3))
    block_out, grad_out, order, dx, lat, out, grads, sems = refs[3 * groups :]
    images = groups * GROUP
    nv, nm = GROUP * NV, GROUP * NM
    split_orders(order_in, order)

    def put_grad(i, put, value):
        high = value.astype(BF)
        low = (value - high.astype(F32)).astype(BF)
        grads[i] = nn(put, high) + nn(put, low)

    def write_grads():
        copies = Copies(sems)
        for i in range(images):
            copies.start(grads.at[i], grad_out.at[0, :, i, :])
        copies.finish()

    @pl.when(ids[0] == 0)
    def _():
        copies = Copies(sems)
        for piece, ref, size in ((dx_in, dx, nv), (lat_enc, lat, nv), (res, out, nm)):
            stack_rows(copies, piece, ref, size)
        copies.finish()

        def put_image(i):
            put = place_matrix(order, i, 0, NV, 0, visible[i])
            put_side = place_matrix(order, i, FIRST, NM, visible[i], PATCH)
            put_grad(i, put, dx[rows_of(i, NV), :])
            block_out[0, i] = (nn(put, lat[rows_of(i, NV), :]) + nn(put_side, out[rows_of(i, NM), :])).astype(BF)

        loop(images, put_image)
        write_grads()

    @pl.when(ids[0] == 1)
    def _():
        copies = Copies(sems)
        stack_rows(copies, res, out, nm)
        stack_rows(copies, [piece.at[pl.ds(0, nm)] for piece in dx_in], dx, nm)
        copies.finish()

        def put_image(i):
            put = place_matrix(order, i, FIRST, NM, visible[i], PATCH)
            put_grad(i, put, dx[rows_of(i, NM), :])
            block_out[0, i] = nn(put, out[rows_of(i, NM), :]).astype(BF)

        loop(images, put_image)
        write_grads()


def place(groups, ids, visible, order, *pieces):
    images = groups * GROUP
    n = images * NV
    outs = [struct((1, images, PATCH, D)), struct((1, PATCH, images, D), F32)]
    return pl.pallas_call(
        partial(place_kernel, groups),
        in_specs=[SMEM, SMEM, VMEM] + [HBM] * (3 * groups),
        out_specs=[VMEM, HBM],
        out_shape=outs,
        scratch_shapes=[
            pltpu.VMEM((images, 1, PATCH), jnp.int32), pltpu.VMEM((n, D), F32), pltpu.VMEM((n, D), BF),
            pltpu.VMEM((images * NM, D), BF), pltpu.VMEM((images, PATCH, D), F32), pltpu.SemaphoreType.DMA((8,)),
        ],
        compiler_params=params(LIMIT),
        cost_estimate=cost(1e6, 1e5),
        name="place",
    )(ids, visible, order, *[ref for piece in pieces for ref in piece])


BITS = (2, 4, 8)


def hop(value, bit):
    return lax.ppermute(value, "dp", [(i, i ^ bit) for i in range(16)])


def combine_kernel(jobs, given, ids, *refs):
    used = sum(sum(4 if gone is None else 1 for gone in terms) for terms, *_ in jobs)
    inputs, outs, scratch = list(refs[:used]), list(refs[used : used + given]), list(refs[used + given :])
    copies = Copies(scratch.pop())
    plans = []

    def fetch(term, gone, bits, own):
        if gone is not None:
            path = tuple(bits[gone:])
            copy = copies.start(term.at[path] if path else term, own)
            return lambda: copies.wait(copy)
        wide = len(bits) == 1
        first = copies.take(2 if wide else 1)
        rest = tuple(bits[2:])

        def piece(x, low):
            ref = term[2 * x + low]
            return ref.at[rest] if rest else ref

        for x in range(2):
            for low in range(2):
                if wide:
                    pl.when(bits[0] == x)(
                        lambda x=x, low=low: copies.begin(piece(x, low), own.at[low], first + low)
                    )
                else:
                    pl.when((bits[0] == x) & (bits[1] == low))(
                        lambda x=x, low=low: copies.begin(piece(x, low), own, first)
                    )

        def wait():
            if wide:
                for low in range(2):
                    copies.wait_at(piece(0, low), own.at[low], first + low)
            else:
                copies.wait_at(piece(0, 0), own, first)

        return wait

    for kinds, first, last, targets, finals in jobs:
        terms = [inputs.pop(0) if gone is not None else [inputs.pop(0) for _ in range(4)] for gone in kinds]
        for target in targets:
            bits = []
            for bit in range(last):
                flip = bit >= first and (target >> (bit - first)) & 1
                bits.append(1 - ids[2 + bit] if flip else ids[2 + bit])
            owns = [scratch.pop(0) for _ in kinds]
            waits = [fetch(term, gone, bits, own) for term, gone, own in zip(terms, kinds, owns)]
            plans.append((waits, owns, last, finals, None if finals else outs.pop(0)))
    for waits, owns, last, finals, out in plans:
        for wait in waits:
            wait()
        spots = [()]
        for _ in range(3 - last):
            spots = [spot + (i,) for spot in spots for i in range(2)]
        for spot in spots:
            for j in range(owns[0].shape[-3]):
                value = owns[0][spot + (j,)].astype(F32)
                for more in owns[1:]:
                    value = value + more[spot + (j,)].astype(F32)
                if finals:
                    which, column = finals[j]
                    outs[which][:, column * D : (column + 1) * D] = value
                else:
                    out[spot + (j,)] = value.astype(BF)


def send_job(terms, first, last, targets=(1,)):
    return terms, first, last, targets, None


def final_job(terms, finals):
    return terms, 0, 3, (0,), finals


def combine(ids, *jobs, outs=()):
    shapes = [struct(shape, F32) for shape in outs]
    plans, inputs, scratch = [], [], []
    for terms, first, last, targets, finals in jobs:
        blocks, rows = terms[0].shape[-3:-1]
        kinds = tuple(None if isinstance(term, list) else 6 - term.ndim for term in terms)
        for term in terms:
            inputs += term if isinstance(term, list) else [term]
        plans.append((kinds, first, last, targets, finals))
        part = (2,) * (3 - last) + (blocks, rows, D)
        for _ in targets:
            scratch += [pltpu.VMEM(part, BF) for _ in terms]
            if finals is None:
                shapes.append(struct(part))
    scratch.append(pltpu.SemaphoreType.DMA((2 * len(scratch),)))
    return pl.pallas_call(
        partial(combine_kernel, tuple(plans), len(shapes)),
        in_specs=[SMEM] + [HBM] * len(inputs),
        out_specs=[VMEM] * len(shapes),
        out_shape=shapes,
        scratch_shapes=scratch,
        compiler_params=params(LIMIT),
        cost_estimate=cost(1e5, 1e4),
        name="combine",
    )(ids, *inputs)


def in_order(first, then):
    return lax.optimization_barrier((first, then))


def own_columns(rows, count):
    own = D // count
    me = lax.axis_index("dp")

    def part(block, wide):
        return lax.dynamic_slice_in_dim(block, me * wide, wide, block.ndim - 1)

    return (
        part(rows[:2], own),
        part(rows[2:6], own),
        part(rows[6:8].reshape(-1), 2 * own),
        part(rows[8:12].reshape(-1), 4 * own),
    )


def scatter_natural(block):
    shards = block.reshape(lax.axis_size("dp"), -1, D)
    return lax.psum_scatter(shards, "dp", scatter_dimension=0, tiled=True)[0].astype(F32)


def local(
    patch_rows, cotangent, patch_order, visible, qkv_weight, out_weight, up_weight, down_weight, norm_gains, biases,
    qv_bias, up_bias, target_qkv, target_out, target_up, target_down, target_gains, target_biases, target_qv_bias,
    target_up_bias,
):
    count = lax.axis_size("dp")
    tree = count == 16
    place_dp = lax.axis_index("dp")
    bits = [(place_dp // bit) % 2 for bit in (1,) + BITS]
    ids = jnp.stack([lax.axis_index("section")] + bits).astype(jnp.int32)
    groups = patch_order.shape[0] // GROUP
    weights = (qkv_weight, out_weight, up_weight, down_weight)
    targets = (target_qkv, target_out, target_up, target_down)
    vecs = (norm_gains, biases, qv_bias, up_bias)
    target_vecs = (target_gains, target_biases, target_qv_bias[None], target_up_bias[None])

    rows, cot = patch_rows.transpose(0, 2, 1, 3), cotangent.transpose(0, 2, 1, 3)
    calls = [
        encode(g, groups, ids, visible, patch_order, *vecs, rows, cot, weights) for g in range(groups)
    ]
    lat, x_e, hq_e, q_e, k_e, v_e, p_e, o_e, y1_e, h2_e, gp_e, a_e = zip(*[call[0] for call in calls])
    x_r, hq_r, q_r, dyb_r = calls[-1][1]
    sent = [lax.ppermute(piece, "section", [(0, 1)]) for piece in lat]
    middles = [
        middle(g, ids, visible, patch_order, vecs, target_vecs, rows, sent[g], x_r[g], q_r[g], dyb_r[g], weights, calls[0][2],
               targets)
        for g in range(groups)
    ]
    dlat, res, hk_r, dq_r, dkv_r, o_r, dy1b_r, h2_r, du_r, a_r, dy1_r, sums_r = zip(*middles)
    back = [lax.ppermute(piece, "section", [(1, 0)]) for piece in dlat]

    def mlp(g, cot):
        return mlp_grad(
            g == 0, groups, ids, visible, patch_order, norm_gains, cot, back[g], up_weight, down_weight, y1_e[g], gp_e[g]
        )

    def attention(g, dy1):
        return attn_back(
            ids, norm_gains, qkv_weight, out_weight, dy1, q_e[g], k_e[g], v_e[g], p_e[g], x_e[g],
            dq_r[g], dy1_r[g], x_r[g],
        )

    cot_e, first = mlp(0, cot)
    mlps = [first] + [mlp(g, cot_e[g])[1] for g in range(1, groups - 1)]
    attns = [attention(g, mlps[g][1]) for g in range(groups - 1)]
    last = groups - 1
    send = partial(combine, ids)
    attns, back[last] = in_order(attns, back[last])
    down, sums_down = down_grad(groups, ids, cot_e, back, a_e, a_r, dyb_r)
    cot_last = cot_e[last]
    down_sum = scatter_natural(down)
    mlps.append(mlp(last, cot_last)[1])
    du_e, dy1_e, dy1b_e, sums_e = zip(*mlps)
    up, sums_up = up_grad(groups, count, ids, du_e, h2_e, dy1b_e, o_e, du_r, h2_r, dy1b_r, o_r)
    dy1_last = dy1_e[last]
    if tree:
        ups = [up[0], [hop(piece, 1) for piece in up[1:]]]
        (up_x,), dy1_last = in_order(send(send_job(ups, 0, 1)), dy1_last)
        ups = ups + [hop(up_x, 2)]
    attns.append(attention(last, dy1_last))
    dq_e, dkv_e, dx, sums_in = (list(piece) for piece in zip(*attns))
    attn, small = qkv_grad(
        groups, count, ids, (sums_down, sums_up, *sums_e, *sums_r, *sums_in),
        dq_e, dkv_e, hq_e, hq_r, hk_r, dq_r, dkv_r,
    )
    if tree:
        got = [hop(piece, 1) for piece in attn[1:]]
        got, small = in_order(got, small + hop(small, 1))
        small = small + hop(small, 2)
        qkvs = [attn[0], got]
        peers = (3, 2, 1)
        (qkv_x, *up_z), (dx, small) = in_order(send(send_job(qkvs, 0, 1), send_job(ups, 1, 3, peers)), (dx, small))
        qkvs = qkvs + [hop(qkv_x, 2)]
        up_got = [hop(one, 4 * peer) for one, peer in zip(up_z, peers)]
    block_out, grad_rows = place(groups, ids, visible, patch_order, dx, lat, res)
    if tree:
        qkv_z, (block_out, grad_rows) = in_order(send(send_job(qkvs, 1, 3, peers)), (block_out, grad_rows))
        qkv_got = [hop(one, 4 * peer) for one, peer in zip(qkv_z, peers)]
        for bit in (4, 8):
            small = small + hop(small, bit)
        up_sum, out_sum = send(
            final_job(ups + up_got, tuple((0, j) for j in range(4)) + ((1, 0),)),
            outs=((D // 16, 4 * D), (D // 16, D)),
        )
        qkv_got, (up_sum, out_sum) = in_order(qkv_got, (up_sum, out_sum))
        (qkv_sum,) = send(final_job(qkvs + qkv_got, ((0, 1), (0, 2), (0, 0))), outs=((D // 16, 3 * D),))
    else:
        up_sum = jnp.concatenate([scatter_natural(one) for one in up[:4]], axis=1)
        out_sum = scatter_natural(up[4])
        qkv_sum = jnp.concatenate([scatter_natural(attn[i]) for i in (2, 0, 1)], axis=1)
        small = lax.psum(small, "dp")
    grad_rows = grad_rows.transpose(0, 2, 1, 3)
    gains, bias_rows, qv_rows, up_rows = own_columns(small, count)
    return (
        block_out,
        grad_rows,
        qkv_sum[None],
        out_sum[None],
        up_sum[None],
        down_sum[None],
        gains[None],
        bias_rows[None],
        qv_rows[None],
        up_rows[None],
    )


def solution(mesh):
    three, four = P("section", None, None), P("section", "dp", None, None)
    grad = P("section", "dp", None)
    return jax.shard_map(
        local,
        mesh=mesh,
        in_specs=(four, four, P("dp", None), P("dp"), three, three, three, three, three, three,
                  P("section", None), P("section", None), P(), P(), P(), P(), P(), P(), P(), P()),
        out_specs=(four, four, grad, grad, grad, grad, P("section", None, "dp"), P("section", None, "dp"),
                   P("section", "dp"), P("section", "dp")),
        check_vma=False,
    )
```

```python
from functools import partial

import jax
import jax.numpy as jnp
from jax import lax
from jax.experimental import pallas as pl
from jax.experimental.pallas import tpu as pltpu
from jax.sharding import PartitionSpec as P

HEADS = 12
PATCH = 196
D = 768
FF = 3072
EPS = 1e-06
NV = 144
NM = 128
FIRST = PATCH - NM
GROUP = 2
CHUNK = 32

BF = jnp.bfloat16
F32 = jnp.float32
MIB = 1024 * 1024
LIMIT = 62

HBM = pl.BlockSpec(memory_space=pl.ANY)
VMEM = pl.BlockSpec(memory_space=pltpu.VMEM)
SMEM = pl.BlockSpec(memory_space=pltpu.SMEM)


def nn(a, b):
    return jnp.dot(a, b, preferred_element_type=F32)


def nt(a, b):
    return lax.dot_general(a, b, (((1,), (1,)), ((), ())), preferred_element_type=F32)


def tn(a, b):
    return lax.dot_general(a, b, (((0,), (0,)), ((), ())), preferred_element_type=F32)


def loop(count, body, unroll=1):
    def step(i, carry):
        for u in range(unroll):
            body(i * unroll + u)
        return carry

    if count == unroll:
        step(0, 0)
    else:
        lax.fori_loop(0, count // unroll, step, 0)


def unroll_of(count):
    return next(u for u in (4, 3, 2, 1) if count % u == 0)


def rows_of(i, size):
    return pl.ds(pl.multiple_of(i * size, size), size)


def f32_row(ref, row, col=0, width=D):
    return ref[pl.ds(row, 1), pl.ds(col, width)].astype(F32)


class Copies:
    def __init__(self, sems):
        self.sems = sems
        self.used = 0
        self.open = []

    def start(self, src, dst):
        copy = pltpu.make_async_copy(src, dst, self.sems.at[self.used])
        self.used += 1
        copy.start()
        self.open.append(copy)
        return copy

    def wait(self, *copies):
        for copy in copies:
            copy.wait()
            self.open = [one for one in self.open if one is not copy]

    def finish(self):
        self.wait(*list(self.open))

    def take(self, count):
        self.used += count
        return self.used - count

    def begin(self, src, dst, at):
        pltpu.make_async_copy(src, dst, self.sems.at[at]).start()

    def wait_at(self, src, dst, at):
        pltpu.make_async_copy(src, dst, self.sems.at[at]).wait()


def gelu_pair(u):
    size = jnp.abs(u)
    base = 1.0 + (0.3275911 * 0.7071067811865476) * size
    guess = pl.reciprocal(base, approx=True)
    t = guess * (2.0 - base * guess)
    ex = jnp.exp2((u * u) * (-0.5 * 1.4426950408889634))
    poly = 0.5306027145 * t - 0.7265760135
    poly = poly * t + 0.7107068705
    poly = poly * t - 0.142248368
    poly = poly * t + 0.127414796
    tail = poly * t * ex
    phi = jnp.where(u >= 0.0, 1.0 - tail, tail)
    return u * phi, phi + u * (0.3989422804014327 * ex)


def norm_rows(src, dst, rows, gain, shift):
    def body(i):
        sel = rows_of(i, CHUNK)
        x = src[sel, :].astype(F32)
        centered = x - jnp.mean(x, axis=-1, keepdims=True)
        var = jnp.mean(centered * centered, axis=-1, keepdims=True)
        dst[sel, :] = (centered * lax.rsqrt(var + EPS) * gain + shift).astype(BF)

    loop(rows // CHUNK, body, unroll_of(rows // CHUNK))


def norm_back(src, grad, base, write, rows, gain):
    count = rows // CHUNK
    unroll = 3 if count % 3 == 0 else 2

    def step(i, carry):
        for u in range(unroll):
            carry = one(i * unroll + u, carry)
        return carry

    def one(i, carry):
        d_gain, d_shift = carry
        sel = rows_of(i, CHUNK)
        x = src[sel, :].astype(F32)
        dh = grad[sel, :]
        centered = x - jnp.mean(x, axis=-1, keepdims=True)
        var = jnp.mean(centered * centered, axis=-1, keepdims=True)
        rstd = lax.rsqrt(var + EPS)
        hat = centered * rstd
        g = dh * gain
        part = dh * hat
        dx = rstd * (
            g
            - jnp.mean(g, axis=-1, keepdims=True)
            - hat * jnp.mean(g * hat, axis=-1, keepdims=True)
        )
        if base is not None:
            dx = dx + base[sel, :].astype(F32)
        write(sel, dx)
        d_gain = d_gain + jnp.sum(part.reshape(CHUNK // 8, 8, D), axis=0)
        d_shift = d_shift + jnp.sum(dh.reshape(CHUNK // 8, 8, D), axis=0)
        return d_gain, d_shift

    zero = jnp.zeros((8, D), F32)
    d_gain, d_shift = lax.fori_loop(0, count // unroll, step, (zero, zero))
    return jnp.sum(d_gain, axis=0, keepdims=True), jnp.sum(d_shift, axis=0, keepdims=True)


def column_sum(ref, rows, col=0, width=D):
    def step(i, carry):
        x = ref[rows_of(i, CHUNK), pl.ds(col, width)].astype(F32)
        return carry + jnp.sum(x.reshape(CHUNK // 8, 8, width), axis=0)

    total = lax.fori_loop(0, rows // CHUNK, step, jnp.zeros((8, width), F32))
    return jnp.sum(total, axis=0, keepdims=True)


def as_bf16(flags):
    return jnp.where(flags, 1.0, 0.0).astype(BF)


def pick_matrix(order, image, start, count, low, high):
    row = order[image, :, pl.ds(start, count)].astype(F32)
    images = order.shape[0]
    col = jnp.broadcast_to(row, (8, count)).T[:, 0:1].astype(jnp.int32)
    rank = start + lax.broadcasted_iota(jnp.int32, (count, 1), 0)
    col = jnp.where((rank >= low) & (rank < high), col * images + image, -1)
    return as_bf16(col == lax.broadcasted_iota(jnp.int32, (count, PATCH * images), 1))


def place_matrix(order, image, start, count, low, high):
    row = order[image, :, pl.ds(start, count)]
    rank = start + lax.broadcasted_iota(jnp.int32, (1, count), 1)
    row = jnp.where((rank >= low) & (rank < high), row, -1)
    return as_bf16(row == lax.broadcasted_iota(jnp.int32, (PATCH, count), 0))


def flatten(rows, flat):
    flat[...] = rows[...].reshape(flat.shape)


def split_orders(order, split):
    for image in range(split.shape[0]):
        split[image] = order[image : image + 1, :]


def split_pair(pair):
    lane = lax.broadcasted_iota(jnp.int32, pair.shape, 1)
    zero = jnp.zeros_like(pair)
    return jnp.concatenate([jnp.where(lane < 64, pair, zero), jnp.where(lane < 64, zero, pair)], axis=0)


def join_rows(both):
    rows = both.shape[0] // 2
    lane = lax.broadcasted_iota(jnp.int32, (rows, 128), 1)
    return jnp.where(lane < 64, both[:rows], both[rows:])


def join_columns(both):
    rows = both.shape[1] // 2
    return jnp.concatenate([both[:64, :rows], both[64:, rows:]], axis=0).T


PAIRS = HEADS // 2
STEP = 6


def each_pair_group(images, body):
    def group(i):
        image = i // (PAIRS // STEP)
        first = (i % (PAIRS // STEP)) * STEP
        pairs = [first + step for step in range(STEP)]
        body(image, [image * PAIRS + pair for pair in pairs], [pl.ds(pl.multiple_of(pair * 128, 128), 128) for pair in pairs])

    loop(images * (PAIRS // STEP), group)


def softmax(scores, axis):
    ex = jnp.exp(scores - jnp.max(scores, axis=axis, keepdims=True))
    return (ex * (1.0 / jnp.sum(ex, axis=axis, keepdims=True))).astype(BF)


def score_back(probs, d_probs, axis):
    wide = probs.astype(F32)
    return (wide * (d_probs - jnp.sum(d_probs * wide, axis=axis, keepdims=True))).astype(BF)


def attention_by_rows(images, n, q, k, v, p, o, count_of):
    def body(image, slots, lanes):
        sel = rows_of(image, n)
        ok = lax.broadcasted_iota(jnp.int32, (1, n), 1) < count_of(image)
        scores = [nt(split_pair(q[sel, at]), k[sel, at]) for at in lanes]
        probs = [softmax(jnp.where(ok, one, -1000000000.0), 1) for one in scores]
        for slot, one in zip(slots, probs):
            p[slot] = one
        mixed = [nn(one, v[sel, at]) for one, at in zip(probs, lanes)]
        for at, one in zip(lanes, mixed):
            o[sel, at] = join_rows(one).astype(BF)

    each_pair_group(images, body)


def attention_by_columns(images, nk, q, k, v, p, o, key_ok):
    def body(image, slots, lanes):
        qs, ks = rows_of(image, NM), rows_of(image, nk)
        ok = key_ok(image)
        scores = [nt(k[ks, at], split_pair(q[qs, at])) for at in lanes]
        probs = [softmax(jnp.where(ok, one, -1000000000.0), 0) for one in scores]
        if p is not None:
            for slot, one in zip(slots, probs):
                p[slot] = one
        mixed = [tn(v[ks, at], one) for one, at in zip(probs, lanes)]
        for at, one in zip(lanes, mixed):
            o[qs, at] = join_columns(one).astype(BF)

    each_pair_group(images, body)


def attention_back_rows(images, n, q, k, v, p, do, dq, dkv):
    def body(image, slots, lanes):
        sel = rows_of(image, n)
        d_mixed = [split_pair(do[sel, at]) for at in lanes]
        d_probs = [nt(one, v[sel, at]) for one, at in zip(d_mixed, lanes)]
        d_scores = [score_back(p[slot], one, 1) for slot, one in zip(slots, d_probs)]
        d_values = [tn(p[slot], one) for slot, one in zip(slots, d_mixed)]
        d_query = [nn(one, k[sel, at]) for one, at in zip(d_scores, lanes)]
        d_keys = [tn(one, split_pair(q[sel, at])) for one, at in zip(d_scores, lanes)]
        for at, value, query, key in zip(lanes, d_values, d_query, d_keys):
            dq[sel, at] = (join_rows(query) * 0.125).astype(BF)
            dkv[sel, at] = key.astype(BF)
            dkv[sel, pl.ds(pl.multiple_of(D + at.start, 128), 128)] = value.astype(BF)

    each_pair_group(images, body)


def attention_back_columns(images, nk, q, k, v, p, do, dq, dkv):
    def body(image, slots, lanes):
        qs, ks = rows_of(image, NM), rows_of(image, nk)
        d_mixed = [split_pair(do[qs, at]) for at in lanes]
        d_probs = [nt(v[ks, at], one) for one, at in zip(d_mixed, lanes)]
        d_scores = [score_back(p[slot], one, 0) for slot, one in zip(slots, d_probs)]
        d_values = [nn(p[slot], one) for slot, one in zip(slots, d_mixed)]
        d_query = [tn(k[ks, at], one) for one, at in zip(d_scores, lanes)]
        d_keys = [nn(one, split_pair(q[qs, at])) for one, at in zip(d_scores, lanes)]
        for at, value, query, key in zip(lanes, d_values, d_query, d_keys):
            dq[qs, at] = (join_columns(query) * 0.125).astype(BF)
            dkv[ks, at] = key.astype(BF)
            dkv[ks, pl.ds(pl.multiple_of(D + at.start, 128), 128)] = value.astype(BF)

    each_pair_group(images, body)


HALF = 512


def mlp_forward(rows, h2, w1, w2, up_b, u, a, gp, tile, acc, out, base):
    acc[...] = base()
    steps = FF // HALF

    def multiply(t):
        u[t % 2] = nn(h2[...], w1[:, t * HALF : (t + 1) * HALF])

    def add(t):
        acc[...] += nn(tile[t % 2], w2[t * HALF : (t + 1) * HALF, :])

    multiply(0)
    for t in range(steps):
        if t + 1 < steps:
            multiply(t + 1)
        if t > 0:
            add(t - 1)
        for c in range(0, HALF, 256):
            at = slice(t * HALF + c, t * HALF + c + 256)
            shift = up_b[0:1, at].astype(F32)
            for r in range(0, rows, CHUNK):
                sel = slice(r, r + CHUNK)
                value, slope = gelu_pair(u[t % 2, sel, c : c + 256] + shift)
                low = value.astype(BF)
                tile[t % 2, sel, c : c + 256] = low
                if a is not None:
                    a[sel, at] = low
                if gp is not None:
                    gp[sel, at] = slope.astype(BF)
    add(steps - 1)
    out[...] = acc[...].astype(BF)


def mlp_back(rows, dyb, gp, w1, w2, du, u, acc, ready=lambda i, which: None):
    acc[...] = jnp.zeros_like(acc)

    def body(i):
        cols = [pl.ds(pl.multiple_of((2 * i + part) * HALF, HALF), HALF) for part in range(2)]
        ready(i, 0)
        for part in range(2):
            u[part] = nt(dyb[...], w2[cols[part], :])
        ready(i, 1)
        for part in range(2):
            for r in range(0, rows, CHUNK):
                sel = slice(r, r + CHUNK)
                du[sel, cols[part]] = (gp[sel, cols[part]].astype(F32) * u[part, sel, :]).astype(BF)
            acc[...] += nt(du[:, cols[part]], w1[:, cols[part]])

    loop(FF // (2 * HALF), body)


def project(count, rows, left, weight, first, write):
    def body(j):
        write(j, nn(left[...], weight[:, pl.ds(pl.multiple_of((first + j) * D, D), D)]))

    loop(count, body)


def set_biases(ref, bias):
    ref[0] = f32_row(bias, 0)
    ref[1] = jnp.zeros((1, D), F32)
    ref[2] = f32_row(bias, 0, D)


def cost(flops, nbytes):
    return pl.CostEstimate(flops=int(flops), bytes_accessed=int(nbytes), transcendentals=0)


def params(mib):
    return pltpu.CompilerParams(vmem_limit_bytes=mib * MIB)


def struct(shape, dtype=BF):
    return jax.ShapeDtypeStruct(shape, dtype)


def start_weights(copies, sources, scratch):
    return [copies.start(src, dst) for src, dst in zip(sources, scratch)]


def encode_kernel(group, groups, ids, visible, order_in, gains, biases, qvb, upb, rows, cot, wqkv, wo, w1, w2,
                  lat_out, x_out, hq_out, q_out, k_out, v_out, p_out, o_out, y1_out, h2_out, gp_out, a_out, *refs):
    ready, refs = refs[: 4 * groups], refs[4 * groups :]
    (order, rows_v, flat, sqkv, so, s1, s2, x, hq, qkv, p, o, y1, h2, gp, a, u, tile, acc, shifts, lat, sems) = refs
    n = GROUP * NV
    split_orders(order_in, order)

    @pl.when(ids[0] == 0)
    def _():
        copies = Copies(sems)
        got_rows = copies.start(rows.at[0], rows_v)
        got_qkv, got_o, got_1, got_2 = start_weights(
            copies, (wqkv.at[0], wo.at[0], w1.at[0], w2.at[0]), (sqkv, so, s1, s2)
        )
        gain, bias = gains.at[0], biases.at[0]
        set_biases(shifts, qvb)
        copies.wait(got_rows)
        flatten(rows_v, flat)

        def pick_rows(i):
            image = group * GROUP + i
            pick = pick_matrix(order, image, 0, NV, 0, visible[image])
            x[rows_of(i, NV), :] = nn(pick, flat[...]).astype(BF)

        loop(GROUP, pick_rows)
        copies.start(x, x_out)
        norm_rows(x, hq, n, f32_row(gain, 0), f32_row(bias, 0))
        copies.start(hq, hq_out)
        copies.wait(got_qkv)

        def keep(j, value):
            scale = jnp.where(j == 0, 0.125, 1.0)
            qkv[j] = ((value + shifts[j]).astype(BF).astype(F32) * scale).astype(BF)

        project(3, n, hq, sqkv, 0, keep)
        q, k, v = qkv.at[0], qkv.at[1], qkv.at[2]
        copies.start(q, q_out)
        copies.start(k, k_out)
        copies.start(v, v_out)
        attention_by_rows(GROUP, NV, q, k, v, p, o, lambda i: visible[group * GROUP + i])
        copies.start(p, p_out)
        copies.start(o, o_out)
        copies.wait(got_o)
        y1[...] = nn(o[...], so[...]) + f32_row(bias, 1) + x[...].astype(F32)
        copies.start(y1, y1_out)
        norm_rows(y1, h2, n, f32_row(gain, 1), f32_row(bias, 2))
        copies.start(h2, h2_out)
        copies.wait(got_1, got_2)
        mlp_forward(n, h2, s1, s2, upb, u, a, gp, tile, acc, lat, lambda: y1[...] + f32_row(bias, 3))
        copies.start(gp, gp_out)
        copies.start(a, a_out)
        copies.start(lat, lat_out)
        copies.finish()

    if group == groups - 1:

        @pl.when(ids[0] == 1)
        def _():
            copies = Copies(sems)
            m = GROUP * NM
            x_out, hq_out, q_out, dyb_out = (ready[i * groups : (i + 1) * groups] for i in range(4))
            gain, bias = gains.at[0], biases.at[0]
            got_rows = copies.start(rows.at[0], rows_v)
            got_q = copies.start(wqkv.at[0, :, pl.ds(0, D)], so)
            copies.wait(got_rows)
            flatten(rows_v, flat)
            got_cot = copies.start(cot.at[0], rows_v)
            top = pl.ds(0, m)

            def pick_group(g):
                def pick_rows(i):
                    image = g * GROUP + i
                    pick = pick_matrix(order, image, FIRST, NM, visible[image], PATCH)
                    x[rows_of(i, NM), :] = nn(pick, flat[...]).astype(BF)

                loop(GROUP, pick_rows)

            for g in range(groups):
                pick_group(g)
                norm_rows(x, hq, m, f32_row(gain, 0), f32_row(bias, 0))
                sent = [copies.start(x.at[top], x_out[g]), copies.start(hq.at[top], hq_out[g])]
                if g == 0:
                    copies.wait(got_q)
                q = qkv.at[g]
                q[top, :] = ((nn(hq[top, :], so[...]) + f32_row(qvb, 0)).astype(BF) * 0.125).astype(BF)
                copies.start(q.at[top], q_out[g])
                copies.wait(*sent)
            copies.wait(got_cot)
            flatten(rows_v, flat)
            for g in range(groups):
                pick_group(g)
                copies.wait(copies.start(x.at[top], dyb_out[g]))
            copies.finish()


def encode(group, groups, ids, visible, order, gains, biases, qvb, upb, rows, cot, weights):
    n = GROUP * NV
    images = order.shape[0]
    row, wide = struct((n, D)), struct((n, FF))
    heads = struct((GROUP * PAIRS, 2 * NV, NV))
    outs = [row] * 6 + [heads, row, struct((n, D), F32), row, wide, wide] + [struct((GROUP * NM, D))] * (4 * groups)
    vm = lambda s: pltpu.VMEM(s.shape, s.dtype)
    scratch = [
        pltpu.VMEM((images, 1, PATCH), jnp.int32),
        pltpu.VMEM((PATCH, images, D), BF), pltpu.VMEM((PATCH * images, D), BF),
        pltpu.VMEM((D, 3 * D), BF), pltpu.VMEM((D, D), BF), pltpu.VMEM((D, FF), BF), pltpu.VMEM((FF, D), BF),
        vm(row), vm(row), pltpu.VMEM((3, n, D), BF), vm(heads), vm(row), pltpu.VMEM((n, D), F32), vm(row),
        vm(wide), vm(wide), pltpu.VMEM((2, n, HALF), F32), pltpu.VMEM((2, n, HALF), BF), pltpu.VMEM((n, D), F32),
        pltpu.VMEM((3, 1, D), F32), vm(row),
        pltpu.SemaphoreType.DMA((24,)),
    ]
    got = pl.pallas_call(
        partial(encode_kernel, group, groups),
        in_specs=[SMEM, SMEM] + [VMEM] * 5 + [HBM] * 6,
        out_specs=[HBM] * len(outs),
        out_shape=outs,
        scratch_shapes=scratch,
        compiler_params=params(LIMIT),
        cost_estimate=cost(2 * n * 12 * D * D, 25e6),
        name="encode",
    )(ids, visible, order, gains, biases, qvb, upb, rows, cot, *weights)
    ready = got[12:]
    return got[:12], [ready[i * groups : (i + 1) * groups] for i in range(4)]


def block_end(copies, n, got_weights, so, s1, s2, bias, gain, up_b, x, o, y1, h2, a, gp, u, tile, acc, res):
    got_o, got_1, got_2 = got_weights
    copies.wait(got_o)
    y1[...] = nn(o[...], so[...]) + f32_row(bias, 1) + x[...].astype(F32)
    norm_rows(y1, h2, n, f32_row(gain, 1), f32_row(bias, 2))
    copies.wait(got_1, got_2)
    mlp_forward(n, h2, s1, s2, up_b, u, a, gp, tile, acc, res, lambda: y1[...] + f32_row(bias, 3))


def target_kernel(group, ids, visible, order_in, gain, bias, qvb, upb, rows, wqkv, wo, w1, w2, res_out,
                  order, rows_v, flat, sqkv, so, s1, s2, x, hq, qkv, o, y1, h2, u, tile, acc, shifts, res, sems):
    n = GROUP * NM
    q, k, v = qkv.at[0], qkv.at[1], qkv.at[2]

    @pl.when(ids[0] == 0)
    def _():
        copies = Copies(sems)
        split_orders(order_in, order)
        got_rows = copies.start(rows.at[0], rows_v)
        got_qkv = copies.start(wqkv, sqkv)
        got_weights = start_weights(copies, (wo, w1, w2), (so, s1, s2))
        set_biases(shifts, qvb)
        copies.wait(got_rows)
        flatten(rows_v, flat)

        def pick_rows(i):
            image = group * GROUP + i
            pick = pick_matrix(order, image, FIRST, NM, visible[image], PATCH)
            x[rows_of(i, NM), :] = nn(pick, flat[...]).astype(BF)

        loop(GROUP, pick_rows)
        norm_rows(x, hq, n, f32_row(gain, 0), f32_row(bias, 0))
        copies.wait(got_qkv)

        def keep(j, value):
            scale = jnp.where(j == 0, 0.125, 1.0)
            qkv[j] = ((value + shifts[j]).astype(BF).astype(F32) * scale).astype(BF)

        project(3, n, hq, sqkv, 0, keep)

        def key_ok(i):
            return lax.broadcasted_iota(jnp.int32, (NM, 1), 0) + FIRST >= visible[group * GROUP + i]

        attention_by_columns(GROUP, NM, q, k, v, None, o, key_ok)
        block_end(copies, n, got_weights, so, s1, s2, bias, gain, upb, x, o, y1, h2, None, None, u, tile, acc, res)
        copies.start(res, res_out)
        copies.finish()


def target(group, ids, visible, order, vecs, rows, weights):
    n = GROUP * NM
    images = order.shape[0]
    row, full = pltpu.VMEM((n, D), BF), pltpu.VMEM((n, D), F32)
    return pl.pallas_call(
        partial(target_kernel, group),
        in_specs=[SMEM, SMEM] + [VMEM] * 5 + [HBM] * 5,
        out_specs=HBM,
        out_shape=struct((n, D)),
        scratch_shapes=[
            pltpu.VMEM((images, 1, PATCH), jnp.int32),
            pltpu.VMEM((PATCH, images, D), BF), pltpu.VMEM((PATCH * images, D), BF),
            pltpu.VMEM((D, 3 * D), BF), pltpu.VMEM((D, D), BF), pltpu.VMEM((D, FF), BF), pltpu.VMEM((FF, D), BF),
            row, row, pltpu.VMEM((3, n, D), BF), row, full, row,
            pltpu.VMEM((2, n, HALF), F32), pltpu.VMEM((2, n, HALF), BF), full, pltpu.VMEM((3, 1, D), F32), row,
            pltpu.SemaphoreType.DMA((8,)),
        ],
        compiler_params=params(LIMIT),
        cost_estimate=cost(1e6, 1e5),
        name="target",
    )(ids, visible, order, *vecs, rows, *weights)


def regress_kernel(group, ids, visible, gains, biases, qvb, upb, lat_in, x_in, q_in, dyb_in, wqkv, wo, w1, w2,
                   dlat_out, res_out, hk_out, dq_out, dkv_out, o_out, dy1b_out, h2_out, du_out, a_out, dy1_out,
                   sums_out,
                   sqkv, so, s1, s2, x, lat, hk, q, kv, p, o, y1, h2, gp, a, u, tile, acc, shifts,
                   res, dyb, du, dy1, dy1b, do, dq, dkv, dh, dlat, sums, sems):
    n, m = GROUP * NM, GROUP * NV
    k, v = kv.at[0], kv.at[1]

    @pl.when(ids[0] == 1)
    def _():
        copies = Copies(sems)
        gain, bias = gains.at[0], biases.at[0]
        got_lat = copies.start(lat_in, lat)
        got_kv = copies.start(wqkv.at[0, :, pl.ds(D, 2 * D)], sqkv)
        got_q = copies.start(q_in, q)
        got_x = copies.start(x_in, x)
        got_weights = start_weights(copies, (wo.at[0], w1.at[0], w2.at[0]), (so, s1, s2))
        got_dyb = copies.start(dyb_in, dyb)
        set_biases(shifts, qvb)
        copies.wait(got_lat)
        norm_rows(lat, hk, m, f32_row(gain, 0), f32_row(bias, 0))
        copies.start(hk, hk_out)
        copies.wait(got_kv)

        def keep_kv(j, value):
            kv[j] = (value + shifts[j + 1]).astype(BF)

        project(2, m, hk, sqkv, 0, keep_kv)
        copies.wait(got_q, got_x)

        def key_ok(i):
            return lax.broadcasted_iota(jnp.int32, (NV, 1), 0) < visible[group * GROUP + i]

        attention_by_columns(GROUP, NV, q, k, v, p, o, key_ok)
        copies.start(o, o_out)
        block_end(copies, n, got_weights, so, s1, s2, bias, gain, upb, x, o, y1, h2, a, gp, u, tile, acc, res)
        copies.start(res, res_out)
        copies.start(h2, h2_out)
        copies.start(a, a_out)
        copies.wait(got_dyb)
        mlp_back(n, dyb, gp, s1, s2, du, u, acc)
        copies.start(du, du_out)

        def keep(sel, dx):
            dy1[sel, :] = dx
            dy1b[sel, :] = dx.astype(BF)

        g2, b2 = norm_back(y1, acc, dyb, keep, n, f32_row(gain, 1))
        copies.start(dy1, dy1_out)
        copies.start(dy1b, dy1b_out)
        do[...] = nt(dy1b[...], so[...]).astype(BF)
        attention_back_columns(GROUP, NV, q, k, v, p, do, dq, dkv)
        copies.start(dq, dq_out)
        copies.start(dkv, dkv_out)
        dh[...] = nt(dkv[:, :D], sqkv[:, :D])
        dh[...] += nt(dkv[:, D:], sqkv[:, D:])

        def keep_side(sel, dx):
            dlat[sel, :] = dx.astype(BF)

        gk, bk = norm_back(lat, dh, None, keep_side, m, f32_row(gain, 0))
        copies.start(dlat, dlat_out)
        for row, value in enumerate((gk, g2, bk, b2)):
            sums[pl.ds(row, 1), :] = value
        copies.start(sums, sums_out)
        copies.finish()


def regress(group, ids, visible, vecs, lat, x, q, dyb, weights):
    n, m = GROUP * NM, GROUP * NV
    row, side, wide = struct((n, D)), struct((m, D)), struct((n, FF))
    pair = struct((m, 2 * D))
    outs = [side, row, side, row, pair, row, row, row, wide, wide, struct((n, D), F32), struct((8, D), F32)]
    vm = lambda s: pltpu.VMEM(s.shape, s.dtype)
    full, fside = pltpu.VMEM((n, D), F32), pltpu.VMEM((m, D), F32)
    scratch = [
        pltpu.VMEM((D, 2 * D), BF), pltpu.VMEM((D, D), BF), pltpu.VMEM((D, FF), BF), pltpu.VMEM((FF, D), BF),
        vm(row), vm(side), vm(side), vm(row), pltpu.VMEM((2, m, D), BF),
        pltpu.VMEM((GROUP * PAIRS, NV, 2 * NM), BF), vm(row), full, vm(row), vm(wide), vm(wide),
        pltpu.VMEM((2, n, HALF), F32), pltpu.VMEM((2, n, HALF), BF), full, pltpu.VMEM((3, 1, D), F32),
        vm(row), vm(row), vm(wide), full, vm(row), vm(row), vm(row), vm(pair), fside, vm(side),
        pltpu.VMEM((8, D), F32),
        pltpu.SemaphoreType.DMA((24,)),
    ]
    return pl.pallas_call(
        partial(regress_kernel, group),
        in_specs=[SMEM, SMEM] + [VMEM] * 4 + [HBM] * 8,
        out_specs=[HBM] * len(outs),
        out_shape=outs,
        scratch_shapes=scratch,
        compiler_params=params(LIMIT),
        cost_estimate=cost(4 * n * 12 * D * D, 25e6),
        name="regress",
    )(ids, visible, *vecs, lat, x, q, dyb, *weights)


def stack_rows(copies, pieces, ref, size):
    return [copies.start(piece, ref.at[pl.ds(i * size, size)]) for i, piece in enumerate(pieces)]


def clear_tail(ref, used):
    ref[pl.ds(used, ref.shape[0] - used), :] = jnp.zeros((ref.shape[0] - used, ref.shape[1]), ref.dtype)


def halves(count, blocks):
    rows = D // 16
    if count == 16:
        return [struct((2, 2, 2, blocks, rows, D))] + [struct((2, blocks, rows, D))] * 4
    return [struct((D, D))] * blocks


def give_blocks(copies, core, tree, left_right, out, dest):
    size = 8 if tree else 1
    blocks = out.shape[0]
    first = copies.take(blocks * size)

    def send(j, act):
        if not tree:
            for block in range(blocks):
                pl.when(j == block)(lambda block=block: act(out.at[block], dest[block], first + block))
            return
        view = out.at[j].reshape(2, 2, 2, 2, D // 16, D)
        for x in range(2):
            for low in range(2):
                at = first + j * size + 4 * x + 2 * low
                act(view.at[:, low, x, core], dest[0].at[x, low, :, j], at)
                act(view.at[:, low, x, 1 - core], dest[1 + 2 * x + low].at[:, j], at + 1)

    def body(j):
        out[j] = left_right(j)
        send(j, copies.begin)

    loop(blocks, body)
    loop(blocks, lambda j: send(j, copies.wait_at))


def give_rows(copies, core, tree, multiply, out, dest):
    size = 4 if tree else 1
    first = copies.take(4 * size)

    def send(j, act):
        if not tree:
            act(out.at[j], dest[0].at[pl.ds(pl.multiple_of(j * D, D), D)], first + j)
            return
        view = out.at[j].reshape(2, 2, D // 4, D)
        low, high = lax.rem(j, 2), lax.div(j, 2)
        for x in range(2):
            at = first + j * size + 2 * x
            act(view.at[x, core], dest[0].at[x, low, high, 0], at)
            act(view.at[x, 1 - core], dest[1].at[x, low, high, 0], at + 1)

    def body(j):
        out[j] = multiply(j)
        send(j, copies.begin)

    loop(4, body)
    loop(4, lambda j: send(j, copies.wait_at))


def down_kernel(groups, parts, ids, *refs):
    cot, lat, a_enc, a_reg, dyb_reg = (refs[i * groups : (i + 1) * groups] for i in range(5))
    refs = refs[5 * groups :]
    dest, refs = refs[:parts], refs[parts:]
    sums_out, cot_v, dyb, a, dlat, out, sums, sems = refs
    images = groups * GROUP
    nv, nm = GROUP * NV, GROUP * NM

    @pl.when(ids[0] == 0)
    def _():
        copies = Copies(sems)
        got = stack_rows(copies, cot, cot_v, nv) + stack_rows(copies, lat, dlat, nv)
        stack_rows(copies, a_enc, a, nv)
        copies.wait(*got)
        dyb[...] = (cot_v[...].astype(F32) + dlat[...].astype(F32)).astype(BF)
        copies.finish()

    @pl.when(ids[0] == 1)
    def _():
        copies = Copies(sems)
        stack_rows(copies, a_reg, a, nm)
        stack_rows(copies, dyb_reg, dyb, nm)
        clear_tail(a, images * NM)
        clear_tail(dyb, images * NM)
        copies.finish()

    copies = Copies(sems)

    def multiply(j):
        return tn(a[:, pl.ds(pl.multiple_of(j * D, D), D)], dyb[...]).astype(BF)

    give_rows(copies, ids[1], parts == 2, multiply, out, dest)
    sums[...] = jnp.broadcast_to(column_sum(dyb, images * NV), (8, D))
    copies.start(sums, sums_out)
    copies.finish()


def down_grad(groups, count, ids, cot, dlat, a_enc, a_reg, dyb_reg):
    n = groups * GROUP * NV
    main = [struct((2, 2, 2, 1, D // 4, D))] * 2 if count == 16 else [struct((FF, D))]
    outs = main + [struct((8, D), F32)]
    row = pltpu.VMEM((n, D), BF)
    scratch = [
        row, row, pltpu.VMEM((n, FF), BF), row, pltpu.VMEM((4, D, D), BF), pltpu.VMEM((8, D), F32),
        pltpu.SemaphoreType.DMA((24,)),
    ]
    got = pl.pallas_call(
        partial(down_kernel, groups, len(main)),
        in_specs=[SMEM] + [HBM] * (5 * groups),
        out_specs=[HBM] * len(outs),
        out_shape=outs,
        scratch_shapes=scratch,
        compiler_params=params(LIMIT),
        cost_estimate=cost(1e6, 1e5),
        name="down_grad",
    )(ids, *cot, *dlat, *a_enc, *a_reg, *dyb_reg)
    return got[: len(main)], got[-1]


def mlp_kernel(first, groups, ids, visible, order_in, gains, cot, dlat_in, w1, w2, y1_in, gp_in, *refs):
    if first:
        picked, refs = refs[:groups], refs[groups:]
    du_out, dy1_out, dy1b_out, sums_out, order, rows_v, flat, refs = *refs[:7], refs[7:]
    s1, s2, cot_v, dlat, dyb, gp, y1, du, u, acc, dy1, dy1b, sums, sems = refs
    n = GROUP * NV
    third = FF // 3

    @pl.when(ids[0] == 0)
    def _():
        copies = Copies(sems)
        got = [copies.start(dlat_in, dlat)]
        if first:
            got_rows = copies.start(cot.at[0], rows_v)
        else:
            got.append(copies.start(cot, cot_v))
        start = copies.take(9)

        def parts(i):
            cols = pl.ds(pl.multiple_of(i * third, third), third)
            return (
                (w2.at[0, cols, :], s2.at[cols, :]),
                (gp_in.at[:, cols], gp.at[:, cols]),
                (w1.at[0, :, cols], s1.at[:, cols]),
            )

        for i in range(3):
            for k, (src, dst) in enumerate(parts(i)):
                copies.begin(src, dst, start + 3 * i + k)
        got_y = copies.start(y1_in, y1)

        def ready(i, which):
            for k in ((0, 1), (2,))[which]:
                copies.wait_at(*parts(i)[k], start + 3 * i + k)

        if first:
            split_orders(order_in, order)
            copies.wait(got_rows)
            flatten(rows_v, flat)
            for g in reversed(range(groups)):

                def pick_rows(i, g=g):
                    image = g * GROUP + i
                    pick = pick_matrix(order, image, 0, NV, 0, visible[image])
                    cot_v[rows_of(i, NV), :] = nn(pick, flat[...]).astype(BF)

                loop(GROUP, pick_rows)
                copies.wait(copies.start(cot_v, picked[g]))
        copies.wait(*got)
        dyb[...] = (cot_v[...].astype(F32) + dlat[...].astype(F32)).astype(BF)
        mlp_back(n, dyb, gp, s1, s2, du, u, acc, ready)
        copies.start(du, du_out)
        copies.wait(got_y)

        def keep(sel, dx):
            dy1[sel, :] = dx
            dy1b[sel, :] = dx.astype(BF)

        g2, b2 = norm_back(y1, acc, dyb, keep, n, f32_row(gains.at[0], 1))
        copies.start(dy1, dy1_out)
        copies.start(dy1b, dy1b_out)
        sums[pl.ds(0, 1), :] = g2
        sums[pl.ds(1, 1), :] = b2
        copies.start(sums, sums_out)
        copies.finish()


def mlp_grad(first, groups, ids, visible, order, gains, cot, dlat, w1, w2, y1, gp):
    n = GROUP * NV
    images = order.shape[0]
    row, wide, full = pltpu.VMEM((n, D), BF), pltpu.VMEM((n, FF), BF), pltpu.VMEM((n, D), F32)
    outs = [struct((n, D))] * (groups if first else 0) + [struct((n, FF)), struct((n, D), F32), struct((n, D)), struct((8, D), F32)]
    got = pl.pallas_call(
        partial(mlp_kernel, first, groups),
        in_specs=[SMEM, SMEM, VMEM, VMEM] + [HBM] * 6,
        out_specs=[HBM] * len(outs),
        out_shape=outs,
        scratch_shapes=[
            pltpu.VMEM((images, 1, PATCH), jnp.int32),
            pltpu.VMEM((PATCH, images, D), BF), pltpu.VMEM((PATCH * images, D), BF),
            pltpu.VMEM((D, FF), BF), pltpu.VMEM((FF, D), BF), row, row, row, wide, full, wide,
            pltpu.VMEM((2, n, HALF), F32), full, full, row, pltpu.VMEM((8, D), F32), pltpu.SemaphoreType.DMA((24,)),
        ],
        compiler_params=params(LIMIT),
        cost_estimate=cost(1e6, 1e5),
        name="mlp_grad",
    )(ids, visible, order, gains, cot, dlat, w1, w2, y1, gp)
    return got[:-4], got[-4:]


def up_kernel(groups, parts, ids, *refs):
    pieces = [refs[i * groups : (i + 1) * groups] for i in range(8)]
    refs = refs[8 * groups :]
    dest, refs = refs[:parts], refs[parts:]
    sums_out, left, right, out, sums, sems = refs
    images = groups * GROUP

    def load(du, h2, dy1b, o, size):
        copies = Copies(sems)
        stack_rows(copies, h2, left.at[0], size)
        for j in range(4):
            stack_rows(copies, [one.at[:, pl.ds(j * D, D)] for one in du], right.at[j], size)
        stack_rows(copies, o, left.at[1], size)
        stack_rows(copies, dy1b, right.at[4], size)
        return copies

    @pl.when(ids[0] == 0)
    def _():
        load(*pieces[:4], GROUP * NV).finish()

    @pl.when(ids[0] == 1)
    def _():
        copies = load(*pieces[4:], GROUP * NM)
        for ref in (left, right):
            for i in range(ref.shape[0]):
                clear_tail(ref.at[i], images * NM)
        copies.finish()

    copies = Copies(sems)

    def multiply(j):
        value = tn(left[lax.div(j, 4)], right[j]).astype(BF)
        sums[pl.ds(j, 1), :] = column_sum(right.at[j], images * NV)
        return value

    give_blocks(copies, ids[1], dest[0].ndim == 6, multiply, out, dest)
    copies.start(sums, sums_out)
    copies.finish()


def up_grad(groups, count, ids, *pieces):
    n = groups * GROUP * NV
    main = halves(count, 5)
    outs = main + [struct((8, D), F32)]
    got = pl.pallas_call(
        partial(up_kernel, groups, len(main)),
        in_specs=[SMEM] + [HBM] * (8 * groups),
        out_specs=[HBM] * len(outs),
        out_shape=outs,
        scratch_shapes=[
            pltpu.VMEM((2, n, D), BF), pltpu.VMEM((5, n, D), BF), pltpu.VMEM((5, D, D), BF), pltpu.VMEM((8, D), F32),
            pltpu.SemaphoreType.DMA((44,)),
        ],
        compiler_params=params(LIMIT),
        cost_estimate=cost(1e6, 1e5),
        name="up_grad",
    )(ids, *[ref for piece in pieces for ref in piece])
    return got[: len(main)], got[-1]


def attn_kernel(groups, last, ids, gains, *refs):
    if last:
        down_sums, up_sums, refs = refs[0], refs[1], refs[2:]
        mlp_sums, reg_sums = (refs[i * groups : (i + 1) * groups] for i in range(2))
        before, refs = refs[2 * groups : 3 * groups - 1], refs[3 * groups - 1 :]
    (wqkv, wo, dy1_enc, q_in, k_in, v_in, p_in, x_enc, dq_reg, dkv_reg, dy1_reg, x_reg,
     dq_out, dkv_out, dx_out, sums_out,
     sqkv, so, dy1, dy1b, q, k, v, p, x, do, dq, dkv, dh, sems) = refs
    m = GROUP * NM
    top = pl.ds(0, m)
    gain = f32_row(gains.at[0], 0)

    def finish(copies, rows):
        def keep(sel, dx):
            dy1[sel, :] = dx

        own = (*norm_back(x, dh, dy1, keep, rows, gain), column_sum(dq, rows), column_sum(dkv, GROUP * NV, D))
        copies.start(dy1, dx_out)
        if not last:
            for row, value in enumerate(own):
                sums_out[row : row + 1, :] = value
            copies.finish()
            return

        def total_of(sums):
            total = sums[0][...]
            for more in sums[1:]:
                total = total + more[...]
            return total

        done, mlp, reg = total_of(before), total_of(mlp_sums), total_of(reg_sums)
        g1, b1, queries, values = (one + done[row : row + 1, :] for row, one in enumerate(own))
        encoder = ids[0] == 0
        sums_out[0:1, :] = g1 + jnp.where(encoder, 0.0, reg[0:1, :])
        sums_out[1:2, :] = jnp.where(encoder, mlp[0:1, :], reg[1:2, :])
        sums_out[2:3, :] = b1 + jnp.where(encoder, 0.0, reg[2:3, :])
        sums_out[3:4, :] = up_sums[4:5, :]
        sums_out[4:5, :] = jnp.where(encoder, mlp[1:2, :], reg[3:4, :])
        sums_out[5:6, :] = down_sums[0:1, :]
        sums_out[6:7, :] = queries
        sums_out[7:8, :] = values
        sums_out[8:12, :] = up_sums[0:4, :]
        sums_out[12:16, :] = jnp.zeros((4, D), F32)
        copies.finish()

    @pl.when(ids[0] == 0)
    def _():
        copies = Copies(sems)
        got = [copies.start(dy1_enc, dy1), copies.start(wo.at[0], so)]
        later = [copies.start(src, dst) for src, dst in ((v_in, v), (p_in, p), (k_in, k), (q_in, q))]
        final = [copies.start(wqkv.at[0], sqkv), copies.start(x_enc, x)]
        copies.wait(*got)
        dy1b[...] = dy1[...].astype(BF)
        do[...] = nt(dy1b[...], so[...]).astype(BF)
        copies.wait(*later)
        attention_back_rows(GROUP, NV, q, k, v, p, do, dq, dkv)
        copies.start(dq, dq_out)
        copies.start(dkv, dkv_out)
        copies.wait(*final)
        dh[...] = nt(dq[...], sqkv[:, 0:D])
        for j in range(2):
            dh[...] += nt(dkv[:, j * D : (j + 1) * D], sqkv[:, (j + 1) * D : (j + 2) * D])
        finish(copies, GROUP * NV)

    @pl.when(ids[0] == 1)
    def _():
        copies = Copies(sems)
        for src, dst in ((dq_reg, dq), (dy1_reg, dy1), (x_reg, x)):
            copies.start(src, dst.at[top])
        copies.start(dkv_reg, dkv)
        copies.start(wqkv.at[0, :, pl.ds(0, D)], sqkv.at[:, pl.ds(0, D)])
        copies.finish()
        dh[top, :] = nt(dq[top, :], sqkv[:, 0:D])
        finish(copies, m)


def attn_back(groups, last, ids, gains, sums, *pieces):
    n = GROUP * NV
    row, full = pltpu.VMEM((n, D), BF), pltpu.VMEM((n, D), F32)
    outs = [struct((n, D)), struct((n, 2 * D)), struct((n, D), F32), struct((16, D), F32)]
    return pl.pallas_call(
        partial(attn_kernel, groups, last),
        in_specs=[SMEM, VMEM] + [VMEM] * len(sums) + [HBM] * len(pieces),
        out_specs=[HBM] * 3 + [VMEM],
        out_shape=outs,
        scratch_shapes=[
            pltpu.VMEM((D, 3 * D), BF), pltpu.VMEM((D, D), BF), full, row, row, row, row,
            pltpu.VMEM((GROUP * PAIRS, 2 * NV, NV), BF), row, row, row, pltpu.VMEM((n, 2 * D), BF), full,
            pltpu.SemaphoreType.DMA((20,)),
        ],
        compiler_params=params(LIMIT),
        cost_estimate=cost(1e6, 1e5),
        name="attn_back",
    )(ids, gains, *sums, *pieces)


def qkv_kernel(groups, parts, ids, *refs):
    pieces = [refs[i * groups : (i + 1) * groups] for i in range(7)]
    dq_enc, dkv_enc, hq_enc, hq_reg, hk_reg, dq_reg, dkv_reg = pieces
    refs = refs[7 * groups :]
    dest, refs = refs[:parts], refs[parts:]
    left, right, out, sems = refs
    images = groups * GROUP
    nv, nm = GROUP * NV, GROUP * NM
    hk, hq = left.at[0], left.at[1]
    dk, dv, dq = (right.at[i] for i in range(3))

    @pl.when(ids[0] == 0)
    def _():
        copies = Copies(sems)
        stack_rows(copies, hq_enc, hk, nv)
        stack_rows(copies, [one.at[:, pl.ds(0, D)] for one in dkv_enc], dk, nv)
        stack_rows(copies, [one.at[:, pl.ds(D, D)] for one in dkv_enc], dv, nv)
        stack_rows(copies, hq_enc, hq, nv)
        stack_rows(copies, dq_enc, dq, nv)
        copies.finish()

    @pl.when(ids[0] == 1)
    def _():
        copies = Copies(sems)
        for piece, ref in ((hq_reg, hq), (dq_reg, dq)):
            stack_rows(copies, piece, ref, nm)
            clear_tail(ref, images * NM)
        stack_rows(copies, hk_reg, hk, nv)
        stack_rows(copies, [one.at[:, pl.ds(0, D)] for one in dkv_reg], dk, nv)
        stack_rows(copies, [one.at[:, pl.ds(D, D)] for one in dkv_reg], dv, nv)
        copies.finish()

    copies = Copies(sems)

    def multiply(j):
        return tn(left[lax.div(j, 2)], right[j]).astype(BF)

    give_blocks(copies, ids[1], dest[0].ndim == 6, multiply, out, dest)


def qkv_grad(groups, count, ids, *pieces):
    n = groups * GROUP * NV
    row = pltpu.VMEM((n, D), BF)
    main = halves(count, 3)
    scratch = [
        pltpu.VMEM((2, n, D), BF), pltpu.VMEM((3, n, D), BF), pltpu.VMEM((3, D, D), BF),
        pltpu.SemaphoreType.DMA((40,)),
    ]
    return pl.pallas_call(
        partial(qkv_kernel, groups, len(main)),
        in_specs=[SMEM] + [HBM] * (7 * groups),
        out_specs=[HBM] * len(main),
        out_shape=main,
        scratch_shapes=scratch,
        compiler_params=params(LIMIT),
        cost_estimate=cost(1e6, 1e5),
        name="qkv_grad",
    )(ids, *[ref for piece in pieces for ref in piece])


def place_kernel(groups, ids, visible, order_in, *refs):
    dx_in, lat_enc, res_enc, res_reg = (refs[i * groups : (i + 1) * groups] for i in range(4))
    block_out, grad_out, order, dx, lat, out, grads, sems = refs[4 * groups :]
    images = groups * GROUP
    nv, nm = GROUP * NV, GROUP * NM
    split_orders(order_in, order)

    def put_grad(i, put, value):
        high = value.astype(BF)
        low = (value - high.astype(F32)).astype(BF)
        grads[i] = nn(put, high) + nn(put, low)

    def write_grads():
        copies = Copies(sems)
        for i in range(images):
            copies.start(grads.at[i], grad_out.at[0, :, i, :])
        copies.finish()

    @pl.when(ids[0] == 0)
    def _():
        copies = Copies(sems)
        for piece, ref, size in ((dx_in, dx, nv), (lat_enc, lat, nv), (res_enc, out, nm)):
            stack_rows(copies, piece, ref, size)
        copies.finish()

        def put_image(i):
            put = place_matrix(order, i, 0, NV, 0, visible[i])
            put_side = place_matrix(order, i, FIRST, NM, visible[i], PATCH)
            put_grad(i, put, dx[rows_of(i, NV), :])
            block_out[0, i] = (nn(put, lat[rows_of(i, NV), :]) + nn(put_side, out[rows_of(i, NM), :])).astype(BF)

        loop(images, put_image)
        write_grads()

    @pl.when(ids[0] == 1)
    def _():
        copies = Copies(sems)
        stack_rows(copies, res_reg, out, nm)
        stack_rows(copies, [piece.at[pl.ds(0, nm)] for piece in dx_in], dx, nm)
        copies.finish()

        def put_image(i):
            put = place_matrix(order, i, FIRST, NM, visible[i], PATCH)
            put_grad(i, put, dx[rows_of(i, NM), :])
            block_out[0, i] = nn(put, out[rows_of(i, NM), :]).astype(BF)

        loop(images, put_image)
        write_grads()


def place(groups, ids, visible, order, *pieces):
    images = groups * GROUP
    n = images * NV
    outs = [struct((1, images, PATCH, D)), struct((1, PATCH, images, D), F32)]
    return pl.pallas_call(
        partial(place_kernel, groups),
        in_specs=[SMEM, SMEM, VMEM] + [HBM] * (4 * groups),
        out_specs=[VMEM, HBM],
        out_shape=outs,
        scratch_shapes=[
            pltpu.VMEM((images, 1, PATCH), jnp.int32), pltpu.VMEM((n, D), F32), pltpu.VMEM((n, D), BF),
            pltpu.VMEM((images * NM, D), BF), pltpu.VMEM((images, PATCH, D), F32), pltpu.SemaphoreType.DMA((8,)),
        ],
        compiler_params=params(LIMIT),
        cost_estimate=cost(1e6, 1e5),
        name="place",
    )(ids, visible, order, *[ref for piece in pieces for ref in piece])


BITS = (2, 4, 8)


def hop(value, bit):
    return lax.ppermute(value, "dp", [(i, i ^ bit) for i in range(16)])


def combine_kernel(jobs, given, ids, *refs):
    used = sum(sum(4 if gone is None else 1 for gone in terms) for terms, *_ in jobs)
    inputs, outs, scratch = list(refs[:used]), list(refs[used : used + given]), list(refs[used + given :])
    copies = Copies(scratch.pop())
    plans = []

    def fetch(term, gone, bits, own):
        if gone is not None:
            path = tuple(bits[gone:])
            copy = copies.start(term.at[path] if path else term, own)
            return lambda: copies.wait(copy)
        wide = len(bits) == 1
        first = copies.take(2 if wide else 1)
        rest = tuple(bits[2:])

        def piece(x, low):
            ref = term[2 * x + low]
            return ref.at[rest] if rest else ref

        for x in range(2):
            for low in range(2):
                if wide:
                    pl.when(bits[0] == x)(
                        lambda x=x, low=low: copies.begin(piece(x, low), own.at[low], first + low)
                    )
                else:
                    pl.when((bits[0] == x) & (bits[1] == low))(
                        lambda x=x, low=low: copies.begin(piece(x, low), own, first)
                    )

        def wait():
            if wide:
                for low in range(2):
                    copies.wait_at(piece(0, low), own.at[low], first + low)
            else:
                copies.wait_at(piece(0, 0), own, first)

        return wait

    for kinds, first, last, targets, finals in jobs:
        terms = [inputs.pop(0) if gone is not None else [inputs.pop(0) for _ in range(4)] for gone in kinds]
        for target in targets:
            bits = []
            for bit in range(last):
                flip = bit >= first and (target >> (bit - first)) & 1
                bits.append(1 - ids[2 + bit] if flip else ids[2 + bit])
            owns = [scratch.pop(0) for _ in kinds]
            waits = [fetch(term, gone, bits, own) for term, gone, own in zip(terms, kinds, owns)]
            plans.append((waits, owns, last, finals, None if finals else outs.pop(0)))
    for waits, owns, last, finals, out in plans:
        for wait in waits:
            wait()
        spots = [()]
        for _ in range(3 - last):
            spots = [spot + (i,) for spot in spots for i in range(2)]
        for spot in spots:
            for j in range(owns[0].shape[-3]):
                value = owns[0][spot + (j,)].astype(F32)
                for more in owns[1:]:
                    value = value + more[spot + (j,)].astype(F32)
                if finals:
                    which, column = finals[j]
                    outs[which][:, column * D : (column + 1) * D] = value
                else:
                    out[spot + (j,)] = value.astype(BF)


def send_job(terms, first, last, targets=(1,)):
    return terms, first, last, targets, None


def final_job(terms, finals):
    return terms, 0, 3, (0,), finals


def combine(ids, *jobs, outs=()):
    shapes = [struct(shape, F32) for shape in outs]
    plans, inputs, scratch = [], [], []
    for terms, first, last, targets, finals in jobs:
        blocks, rows = terms[0].shape[-3:-1]
        kinds = tuple(None if isinstance(term, list) else 6 - term.ndim for term in terms)
        for term in terms:
            inputs += term if isinstance(term, list) else [term]
        plans.append((kinds, first, last, targets, finals))
        part = (2,) * (3 - last) + (blocks, rows, D)
        for _ in targets:
            scratch += [pltpu.VMEM(part, BF) for _ in terms]
            if finals is None:
                shapes.append(struct(part))
    scratch.append(pltpu.SemaphoreType.DMA((2 * len(scratch),)))
    return pl.pallas_call(
        partial(combine_kernel, tuple(plans), len(shapes)),
        in_specs=[SMEM] + [HBM] * len(inputs),
        out_specs=[VMEM] * len(shapes),
        out_shape=shapes,
        scratch_shapes=scratch,
        compiler_params=params(LIMIT),
        cost_estimate=cost(1e5, 1e4),
        name="combine",
    )(ids, *inputs)


def in_order(first, then):
    return lax.optimization_barrier((first, then))


def own_columns(rows, count):
    own = D // count
    me = lax.axis_index("dp")

    def part(block, wide):
        return lax.dynamic_slice_in_dim(block, me * wide, wide, block.ndim - 1)

    return (
        part(rows[:2], own),
        part(rows[2:6], own),
        part(rows[6:8].reshape(-1), 2 * own),
        part(rows[8:12].reshape(-1), 4 * own),
    )


def scatter_natural(block):
    shards = block.reshape(lax.axis_size("dp"), -1, D)
    return lax.psum_scatter(shards, "dp", scatter_dimension=0, tiled=True)[0].astype(F32)


def local(
    patch_rows, cotangent, patch_order, visible, qkv_weight, out_weight, up_weight, down_weight, norm_gains, biases,
    qv_bias, up_bias, target_qkv, target_out, target_up, target_down, target_gains, target_biases, target_qv_bias,
    target_up_bias,
):
    count = lax.axis_size("dp")
    tree = count == 16
    place_dp = lax.axis_index("dp")
    bits = [(place_dp // bit) % 2 for bit in (1,) + BITS]
    ids = jnp.stack([lax.axis_index("section")] + bits).astype(jnp.int32)
    groups = patch_order.shape[0] // GROUP
    weights = (qkv_weight, out_weight, up_weight, down_weight)
    targets = (target_qkv, target_out, target_up, target_down)
    vecs = (norm_gains, biases, qv_bias, up_bias)
    target_vecs = (target_gains, target_biases, target_qv_bias[None], target_up_bias[None])

    rows, cot = patch_rows.transpose(0, 2, 1, 3), cotangent.transpose(0, 2, 1, 3)
    calls = [
        encode(g, groups, ids, visible, patch_order, *vecs, rows, cot, weights) for g in range(groups)
    ]
    lat, x_e, hq_e, q_e, k_e, v_e, p_e, o_e, y1_e, h2_e, gp_e, a_e = zip(*[call[0] for call in calls])
    x_r, hq_r, q_r, dyb_r = calls[-1][1]
    sent = [lax.ppermute(piece, "section", [(0, 1)]) for piece in lat]
    vectors = (norm_gains, biases, qv_bias, up_bias)
    res_e = [target(0, ids, visible, patch_order, target_vecs, rows, targets)]
    res_e[0], sent[0] = in_order(res_e[0], sent[0])
    regressed = [regress(0, ids, visible, vectors, sent[0], x_r[0], q_r[0], dyb_r[0], weights)]
    back = [lax.ppermute(regressed[0][0], "section", [(1, 0)])]
    for g in range(1, groups):
        regressed.append(regress(g, ids, visible, vectors, sent[g], x_r[g], q_r[g], dyb_r[g], weights))
        back.append(lax.ppermute(regressed[g][0], "section", [(1, 0)]))
    _, res_r, hk_r, dq_r, dkv_r, o_r, dy1b_r, h2_r, du_r, a_r, dy1_r, sums_r = zip(*regressed)
    def mlp(g, cot):
        return mlp_grad(
            g == 0, groups, ids, visible, patch_order, norm_gains, cot, back[g], up_weight, down_weight, y1_e[g], gp_e[g]
        )

    def attention(g, dy1, sums=()):
        return attn_back(
            groups, len(sums) > 0, ids, norm_gains, sums, qkv_weight, out_weight, dy1, q_e[g], k_e[g], v_e[g], p_e[g],
            x_e[g], dq_r[g], dkv_r[g], dy1_r[g], x_r[g],
        )

    cot_e, first = mlp(0, cot)
    mlps = [first] + [mlp(g, cot_e[g])[1] for g in range(1, groups - 1)]
    attns = [attention(g, mlps[g][1]) for g in range(groups - 1)]
    last = groups - 1
    send = partial(combine, ids)
    attns, back[last] = in_order(attns, back[last])
    down, sums_down = down_grad(groups, count, ids, cot_e, back, a_e, a_r, dyb_r)
    cot_last = cot_e[last]
    if tree:
        downs = [down[0], hop(down[1], 1)]
        (down_x,), cot_last = in_order(send(send_job(downs, 0, 1)), cot_last)
        downs = downs + [hop(down_x, 2)]
    mlps.append(mlp(last, cot_last)[1])
    du_e, dy1_e, dy1b_e, sums_e = zip(*mlps)
    up, sums_up = up_grad(groups, count, ids, du_e, h2_e, dy1b_e, o_e, du_r, h2_r, dy1b_r, o_r)
    dy1_last = dy1_e[last]
    if tree:
        peers = (3, 2, 1)
        ups = [up[0], [hop(piece, 1) for piece in up[1:]]]
        (up_x, *down_z), dy1_last = in_order(send(send_job(ups, 0, 1), send_job(downs, 1, 3, peers)), dy1_last)
        ups = ups + [hop(up_x, 2)]
        down_got = [hop(one, 4 * peer) for one, peer in zip(down_z, peers)]
    sums_in = [piece[3] for piece in attns]
    attns.append(attention(last, dy1_last, (sums_down, sums_up, *sums_e, *sums_r, *sums_in)))
    dq_e, dkv_e, dx, small = (list(piece) for piece in zip(*attns))
    small = small[last]
    order_late = patch_order
    if tree:
        small = small + hop(small, 1)
        small, dq_e[last] = in_order(small, dq_e[last])
        got = hop(small, 2)
    attn = qkv_grad(groups, count, ids, dq_e, dkv_e, hq_e, hq_r, hk_r, dq_r, dkv_r)
    if tree:
        down_got, attn = in_order(down_got, attn)
        pieces = [hop(piece, 1) for piece in attn[1:]]
        pieces, got = in_order(pieces, got)
        small = small + got
        qkvs = [attn[0], pieces]
        (qkv_x, *up_z), got = in_order(send(send_job(qkvs, 0, 1), send_job(ups, 1, 3, peers)), hop(small, 4))
        small = small + got
        (dx, order_late), qkv_x = in_order((dx, patch_order), qkv_x)
        qkvs = qkvs + [hop(qkv_x, 2)]
        got = hop(small, 8)
        up_got = [hop(one, 4 * peer) for one, peer in zip(up_z, peers)]
    res_e += [target(g, ids, visible, order_late, target_vecs, rows, targets) for g in range(1, groups)]
    block_out, grad_rows = place(groups, ids, visible, patch_order, dx, lat, res_e, res_r)
    if tree:
        small = small + got
        qkv_z, (block_out, grad_rows) = in_order(send(send_job(qkvs, 1, 3, peers)), (block_out, grad_rows))
        qkv_got = [hop(one, 4 * peer) for one, peer in zip(qkv_z, peers)]
        down_sum, up_sum, out_sum = send(
            final_job(downs + down_got, ((0, 0),)),
            final_job(ups + up_got, tuple((1, j) for j in range(4)) + ((2, 0),)),
            outs=((D // 4, D), (D // 16, 4 * D), (D // 16, D)),
        )
        qkv_got, (down_sum, up_sum, out_sum) = in_order(qkv_got, (down_sum, up_sum, out_sum))
        (qkv_sum,) = send(final_job(qkvs + qkv_got, ((0, 1), (0, 2), (0, 0))), outs=((D // 16, 3 * D),))
    else:
        down_sum = scatter_natural(down[0])
        up_sum = jnp.concatenate([scatter_natural(one) for one in up[:4]], axis=1)
        out_sum = scatter_natural(up[4])
        qkv_sum = jnp.concatenate([scatter_natural(attn[i]) for i in (2, 0, 1)], axis=1)
        small = lax.psum(small, "dp")
    grad_rows = grad_rows.transpose(0, 2, 1, 3)
    gains, bias_rows, qv_rows, up_rows = own_columns(small, count)
    return (
        block_out,
        grad_rows,
        qkv_sum[None],
        out_sum[None],
        up_sum[None],
        down_sum[None],
        gains[None],
        bias_rows[None],
        qv_rows[None],
        up_rows[None],
    )


def solution(mesh):
    three, four = P("section", None, None), P("section", "dp", None, None)
    grad = P("section", "dp", None)
    return jax.shard_map(
        local,
        mesh=mesh,
        in_specs=(four, four, P("dp", None), P("dp"), three, three, three, three, three, three,
                  P("section", None), P("section", None), P(), P(), P(), P(), P(), P(), P(), P()),
        out_specs=(four, four, grad, grad, grad, grad, P("section", None, "dp"), P("section", None, "dp"),
                   P("section", "dp"), P("section", "dp")),
        check_vma=False,
    )
```

```python
from functools import partial

import jax
import jax.numpy as jnp
from jax import lax
from jax.experimental import pallas as pl
from jax.experimental.pallas import tpu as pltpu
from jax.sharding import PartitionSpec as P

HEADS = 12
PATCH = 196
D = 768
FF = 3072
EPS = 1e-06
NV = 144
NM = 128
FIRST = PATCH - NM
GROUP = 2
CHUNK = 32

BF = jnp.bfloat16
F32 = jnp.float32
MIB = 1024 * 1024
LIMIT = 62

HBM = pl.BlockSpec(memory_space=pl.ANY)
VMEM = pl.BlockSpec(memory_space=pltpu.VMEM)
SMEM = pl.BlockSpec(memory_space=pltpu.SMEM)


def nn(a, b):
    return jnp.dot(a, b, preferred_element_type=F32)


def nt(a, b):
    return lax.dot_general(a, b, (((1,), (1,)), ((), ())), preferred_element_type=F32)


def tn(a, b):
    return lax.dot_general(a, b, (((0,), (0,)), ((), ())), preferred_element_type=F32)


def loop(count, body, unroll=1):
    def step(i, carry):
        for u in range(unroll):
            body(i * unroll + u)
        return carry

    if count == unroll:
        step(0, 0)
    else:
        lax.fori_loop(0, count // unroll, step, 0)


def unroll_of(count):
    return next(u for u in (4, 3, 2, 1) if count % u == 0)


def rows_of(i, size):
    return pl.ds(pl.multiple_of(i * size, size), size)


def f32_row(ref, row, col=0, width=D):
    return ref[pl.ds(row, 1), pl.ds(col, width)].astype(F32)


class Copies:
    def __init__(self, sems):
        self.sems = sems
        self.used = 0
        self.open = []

    def start(self, src, dst):
        copy = pltpu.make_async_copy(src, dst, self.sems.at[self.used])
        self.used += 1
        copy.start()
        self.open.append(copy)
        return copy

    def wait(self, *copies):
        for copy in copies:
            copy.wait()
            self.open = [one for one in self.open if one is not copy]

    def finish(self):
        self.wait(*list(self.open))

    def take(self, count):
        self.used += count
        return self.used - count

    def begin(self, src, dst, at):
        pltpu.make_async_copy(src, dst, self.sems.at[at]).start()

    def wait_at(self, src, dst, at):
        pltpu.make_async_copy(src, dst, self.sems.at[at]).wait()


def gelu_pair(u):
    size = jnp.abs(u)
    base = 1.0 + (0.3275911 * 0.7071067811865476) * size
    guess = pl.reciprocal(base, approx=True)
    t = guess * (2.0 - base * guess)
    ex = jnp.exp2((u * u) * (-0.5 * 1.4426950408889634))
    poly = 0.5306027145 * t - 0.7265760135
    poly = poly * t + 0.7107068705
    poly = poly * t - 0.142248368
    poly = poly * t + 0.127414796
    tail = poly * t * ex
    phi = jnp.where(u >= 0.0, 1.0 - tail, tail)
    return u * phi, phi + u * (0.3989422804014327 * ex)


def norm_rows(src, dst, rows, gain, shift):
    def body(i):
        sel = rows_of(i, CHUNK)
        x = src[sel, :].astype(F32)
        centered = x - jnp.mean(x, axis=-1, keepdims=True)
        var = jnp.mean(centered * centered, axis=-1, keepdims=True)
        dst[sel, :] = (centered * lax.rsqrt(var + EPS) * gain + shift).astype(BF)

    loop(rows // CHUNK, body, unroll_of(rows // CHUNK))


def norm_back(src, grad, base, write, rows, gain):
    count = rows // CHUNK
    unroll = 3 if count % 3 == 0 else 2

    def step(i, carry):
        for u in range(unroll):
            carry = one(i * unroll + u, carry)
        return carry

    def one(i, carry):
        d_gain, d_shift = carry
        sel = rows_of(i, CHUNK)
        x = src[sel, :].astype(F32)
        dh = grad[sel, :]
        centered = x - jnp.mean(x, axis=-1, keepdims=True)
        var = jnp.mean(centered * centered, axis=-1, keepdims=True)
        rstd = lax.rsqrt(var + EPS)
        hat = centered * rstd
        g = dh * gain
        part = dh * hat
        dx = rstd * (
            g
            - jnp.mean(g, axis=-1, keepdims=True)
            - hat * jnp.mean(g * hat, axis=-1, keepdims=True)
        )
        if base is not None:
            dx = dx + base[sel, :].astype(F32)
        write(sel, dx)
        d_gain = d_gain + jnp.sum(part.reshape(CHUNK // 8, 8, D), axis=0)
        d_shift = d_shift + jnp.sum(dh.reshape(CHUNK // 8, 8, D), axis=0)
        return d_gain, d_shift

    zero = jnp.zeros((8, D), F32)
    d_gain, d_shift = lax.fori_loop(0, count // unroll, step, (zero, zero))
    return jnp.sum(d_gain, axis=0, keepdims=True), jnp.sum(d_shift, axis=0, keepdims=True)


def column_sum(ref, rows, col=0, width=D):
    def step(i, carry):
        x = ref[rows_of(i, CHUNK), pl.ds(col, width)].astype(F32)
        return carry + jnp.sum(x.reshape(CHUNK // 8, 8, width), axis=0)

    total = lax.fori_loop(0, rows // CHUNK, step, jnp.zeros((8, width), F32))
    return jnp.sum(total, axis=0, keepdims=True)


def as_bf16(flags):
    return jnp.where(flags, 1.0, 0.0).astype(BF)


def pick_matrix(order, image, start, count, low, high):
    row = order[image, :, pl.ds(start, count)].astype(F32)
    images = order.shape[0]
    col = jnp.broadcast_to(row, (8, count)).T[:, 0:1].astype(jnp.int32)
    rank = start + lax.broadcasted_iota(jnp.int32, (count, 1), 0)
    col = jnp.where((rank >= low) & (rank < high), col * images + image, -1)
    return as_bf16(col == lax.broadcasted_iota(jnp.int32, (count, PATCH * images), 1))


def place_matrix(order, image, start, count, low, high):
    row = order[image, :, pl.ds(start, count)]
    rank = start + lax.broadcasted_iota(jnp.int32, (1, count), 1)
    row = jnp.where((rank >= low) & (rank < high), row, -1)
    return as_bf16(row == lax.broadcasted_iota(jnp.int32, (PATCH, count), 0))


def flatten(rows, flat):
    flat[...] = rows[...].reshape(flat.shape)


def split_orders(order, split):
    for image in range(split.shape[0]):
        split[image] = order[image : image + 1, :]


def split_pair(pair):
    lane = lax.broadcasted_iota(jnp.int32, pair.shape, 1)
    zero = jnp.zeros_like(pair)
    return jnp.concatenate([jnp.where(lane < 64, pair, zero), jnp.where(lane < 64, zero, pair)], axis=0)


def join_rows(both):
    rows = both.shape[0] // 2
    lane = lax.broadcasted_iota(jnp.int32, (rows, 128), 1)
    return jnp.where(lane < 64, both[:rows], both[rows:])


def join_columns(both):
    rows = both.shape[1] // 2
    return jnp.concatenate([both[:64, :rows], both[64:, rows:]], axis=0).T


PAIRS = HEADS // 2
STEP = 6


def each_pair_group(images, body):
    def group(i):
        image = i // (PAIRS // STEP)
        first = (i % (PAIRS // STEP)) * STEP
        pairs = [first + step for step in range(STEP)]
        body(image, [image * PAIRS + pair for pair in pairs], [pl.ds(pl.multiple_of(pair * 128, 128), 128) for pair in pairs])

    loop(images * (PAIRS // STEP), group)


def softmax(scores, axis):
    ex = jnp.exp(scores - jnp.max(scores, axis=axis, keepdims=True))
    return (ex * (1.0 / jnp.sum(ex, axis=axis, keepdims=True))).astype(BF)


def score_back(probs, d_probs, axis):
    wide = probs.astype(F32)
    return (wide * (d_probs - jnp.sum(d_probs * wide, axis=axis, keepdims=True))).astype(BF)


def attention_by_rows(images, n, q, k, v, p, o, count_of):
    def body(image, slots, lanes):
        sel = rows_of(image, n)
        ok = lax.broadcasted_iota(jnp.int32, (1, n), 1) < count_of(image)
        scores = [nt(split_pair(q[sel, at]), k[sel, at]) for at in lanes]
        probs = [softmax(jnp.where(ok, one, -1000000000.0), 1) for one in scores]
        for slot, one in zip(slots, probs):
            p[slot] = one
        mixed = [nn(one, v[sel, at]) for one, at in zip(probs, lanes)]
        for at, one in zip(lanes, mixed):
            o[sel, at] = join_rows(one).astype(BF)

    each_pair_group(images, body)


def attention_by_columns(images, nk, q, k, v, p, o, key_ok):
    def body(image, slots, lanes):
        qs, ks = rows_of(image, NM), rows_of(image, nk)
        ok = key_ok(image)
        scores = [nt(k[ks, at], split_pair(q[qs, at])) for at in lanes]
        probs = [softmax(jnp.where(ok, one, -1000000000.0), 0) for one in scores]
        if p is not None:
            for slot, one in zip(slots, probs):
                p[slot] = one
        mixed = [tn(v[ks, at], one) for one, at in zip(probs, lanes)]
        for at, one in zip(lanes, mixed):
            o[qs, at] = join_columns(one).astype(BF)

    each_pair_group(images, body)


def attention_back_rows(images, n, q, k, v, p, do, dq, dkv):
    def body(image, slots, lanes):
        sel = rows_of(image, n)
        d_mixed = [split_pair(do[sel, at]) for at in lanes]
        d_probs = [nt(one, v[sel, at]) for one, at in zip(d_mixed, lanes)]
        d_scores = [score_back(p[slot], one, 1) for slot, one in zip(slots, d_probs)]
        d_values = [tn(p[slot], one) for slot, one in zip(slots, d_mixed)]
        d_query = [nn(one, k[sel, at]) for one, at in zip(d_scores, lanes)]
        d_keys = [tn(one, split_pair(q[sel, at])) for one, at in zip(d_scores, lanes)]
        for at, value, query, key in zip(lanes, d_values, d_query, d_keys):
            dq[sel, at] = (join_rows(query) * 0.125).astype(BF)
            dkv[sel, at] = key.astype(BF)
            dkv[sel, pl.ds(pl.multiple_of(D + at.start, 128), 128)] = value.astype(BF)

    each_pair_group(images, body)


def attention_back_columns(images, nk, q, k, v, p, do, dq, dkv):
    def body(image, slots, lanes):
        qs, ks = rows_of(image, NM), rows_of(image, nk)
        d_mixed = [split_pair(do[qs, at]) for at in lanes]
        d_probs = [nt(v[ks, at], one) for one, at in zip(d_mixed, lanes)]
        d_scores = [score_back(p[slot], one, 0) for slot, one in zip(slots, d_probs)]
        d_values = [nn(p[slot], one) for slot, one in zip(slots, d_mixed)]
        d_query = [tn(k[ks, at], one) for one, at in zip(d_scores, lanes)]
        d_keys = [nn(one, split_pair(q[qs, at])) for one, at in zip(d_scores, lanes)]
        for at, value, query, key in zip(lanes, d_values, d_query, d_keys):
            dq[qs, at] = (join_columns(query) * 0.125).astype(BF)
            dkv[ks, at] = key.astype(BF)
            dkv[ks, pl.ds(pl.multiple_of(D + at.start, 128), 128)] = value.astype(BF)

    each_pair_group(images, body)


HALF = 512


def mlp_forward(rows, h2, w1, w2, up_b, u, a, gp, tile, acc, out, base):
    acc[...] = base()
    steps = FF // HALF

    def multiply(t):
        u[t % 2] = nn(h2[...], w1[:, t * HALF : (t + 1) * HALF])

    def add(t):
        acc[...] += nn(tile[t % 2], w2[t * HALF : (t + 1) * HALF, :])

    multiply(0)
    for t in range(steps):
        if t + 1 < steps:
            multiply(t + 1)
        if t > 0:
            add(t - 1)
        for c in range(0, HALF, 256):
            at = slice(t * HALF + c, t * HALF + c + 256)
            shift = up_b[0:1, at].astype(F32)
            for r in range(0, rows, CHUNK):
                sel = slice(r, r + CHUNK)
                value, slope = gelu_pair(u[t % 2, sel, c : c + 256] + shift)
                low = value.astype(BF)
                tile[t % 2, sel, c : c + 256] = low
                if a is not None:
                    a[sel, at] = low
                if gp is not None:
                    gp[sel, at] = slope.astype(BF)
    add(steps - 1)
    out[...] = acc[...].astype(BF)


def mlp_back(rows, dyb, gp, w1, w2, du, u, acc, ready=lambda i, which: None):
    acc[...] = jnp.zeros_like(acc)

    def body(i):
        cols = [pl.ds(pl.multiple_of((2 * i + part) * HALF, HALF), HALF) for part in range(2)]
        ready(i, 0)
        for part in range(2):
            u[part] = nt(dyb[...], w2[cols[part], :])
        ready(i, 1)
        for part in range(2):
            for r in range(0, rows, CHUNK):
                sel = slice(r, r + CHUNK)
                du[sel, cols[part]] = (gp[sel, cols[part]].astype(F32) * u[part, sel, :]).astype(BF)
            acc[...] += nt(du[:, cols[part]], w1[:, cols[part]])

    loop(FF // (2 * HALF), body)


def project(count, rows, left, weight, first, write):
    def body(j):
        write(j, nn(left[...], weight[:, pl.ds(pl.multiple_of((first + j) * D, D), D)]))

    loop(count, body)


def set_biases(ref, bias):
    ref[0] = f32_row(bias, 0)
    ref[1] = jnp.zeros((1, D), F32)
    ref[2] = f32_row(bias, 0, D)


def cost(flops, nbytes):
    return pl.CostEstimate(flops=int(flops), bytes_accessed=int(nbytes), transcendentals=0)


def params(mib):
    return pltpu.CompilerParams(vmem_limit_bytes=mib * MIB)


def struct(shape, dtype=BF):
    return jax.ShapeDtypeStruct(shape, dtype)


def start_weights(copies, sources, scratch):
    return [copies.start(src, dst) for src, dst in zip(sources, scratch)]


def encode_kernel(group, groups, ids, visible, order_in, gains, biases, qvb, upb, rows, cot, wqkv, wo, w1, w2,
                  lat_out, x_out, hq_out, q_out, k_out, v_out, p_out, o_out, y1_out, h2_out, gp_out, a_out, *refs):
    ready, refs = refs[: 4 * groups], refs[4 * groups :]
    (order, rows_v, flat, sqkv, so, s1, s2, x, hq, qkv, p, o, y1, h2, gp, a, u, tile, acc, shifts, lat, sems) = refs
    n = GROUP * NV
    split_orders(order_in, order)

    @pl.when(ids[0] == 0)
    def _():
        copies = Copies(sems)
        got_rows = copies.start(rows.at[0], rows_v)
        got_qkv, got_o, got_1, got_2 = start_weights(
            copies, (wqkv.at[0], wo.at[0], w1.at[0], w2.at[0]), (sqkv, so, s1, s2)
        )
        gain, bias = gains.at[0], biases.at[0]
        set_biases(shifts, qvb)
        copies.wait(got_rows)
        flatten(rows_v, flat)

        def pick_rows(i):
            image = group * GROUP + i
            pick = pick_matrix(order, image, 0, NV, 0, visible[image])
            x[rows_of(i, NV), :] = nn(pick, flat[...]).astype(BF)

        loop(GROUP, pick_rows)
        copies.start(x, x_out)
        norm_rows(x, hq, n, f32_row(gain, 0), f32_row(bias, 0))
        copies.start(hq, hq_out)
        copies.wait(got_qkv)

        def keep(j, value):
            scale = jnp.where(j == 0, 0.125, 1.0)
            qkv[j] = ((value + shifts[j]).astype(BF).astype(F32) * scale).astype(BF)

        project(3, n, hq, sqkv, 0, keep)
        q, k, v = qkv.at[0], qkv.at[1], qkv.at[2]
        copies.start(q, q_out)
        copies.start(k, k_out)
        copies.start(v, v_out)
        attention_by_rows(GROUP, NV, q, k, v, p, o, lambda i: visible[group * GROUP + i])
        copies.start(p, p_out)
        copies.start(o, o_out)
        copies.wait(got_o)
        y1[...] = nn(o[...], so[...]) + f32_row(bias, 1) + x[...].astype(F32)
        copies.start(y1, y1_out)
        norm_rows(y1, h2, n, f32_row(gain, 1), f32_row(bias, 2))
        copies.start(h2, h2_out)
        copies.wait(got_1, got_2)
        mlp_forward(n, h2, s1, s2, upb, u, a, gp, tile, acc, lat, lambda: y1[...] + f32_row(bias, 3))
        copies.start(gp, gp_out)
        copies.start(a, a_out)
        copies.start(lat, lat_out)
        copies.finish()

    if group == groups - 1:

        @pl.when(ids[0] == 1)
        def _():
            copies = Copies(sems)
            m = GROUP * NM
            x_out, hq_out, q_out, dyb_out = (ready[i * groups : (i + 1) * groups] for i in range(4))
            gain, bias = gains.at[0], biases.at[0]
            got_rows = copies.start(rows.at[0], rows_v)
            got_q = copies.start(wqkv.at[0, :, pl.ds(0, D)], so)
            copies.wait(got_rows)
            flatten(rows_v, flat)
            got_cot = copies.start(cot.at[0], rows_v)
            top = pl.ds(0, m)

            def pick_group(g):
                def pick_rows(i):
                    image = g * GROUP + i
                    pick = pick_matrix(order, image, FIRST, NM, visible[image], PATCH)
                    x[rows_of(i, NM), :] = nn(pick, flat[...]).astype(BF)

                loop(GROUP, pick_rows)

            for g in range(groups):
                pick_group(g)
                norm_rows(x, hq, m, f32_row(gain, 0), f32_row(bias, 0))
                sent = [copies.start(x.at[top], x_out[g]), copies.start(hq.at[top], hq_out[g])]
                if g == 0:
                    copies.wait(got_q)
                q = qkv.at[g]
                q[top, :] = ((nn(hq[top, :], so[...]) + f32_row(qvb, 0)).astype(BF) * 0.125).astype(BF)
                copies.start(q.at[top], q_out[g])
                copies.wait(*sent)
            copies.wait(got_cot)
            flatten(rows_v, flat)
            for g in range(groups):
                pick_group(g)
                copies.wait(copies.start(x.at[top], dyb_out[g]))
            copies.finish()


def encode(group, groups, ids, visible, order, gains, biases, qvb, upb, rows, cot, weights):
    n = GROUP * NV
    images = order.shape[0]
    row, wide = struct((n, D)), struct((n, FF))
    heads = struct((GROUP * PAIRS, 2 * NV, NV))
    outs = [row] * 6 + [heads, row, struct((n, D), F32), row, wide, wide] + [struct((GROUP * NM, D))] * (4 * groups)
    vm = lambda s: pltpu.VMEM(s.shape, s.dtype)
    scratch = [
        pltpu.VMEM((images, 1, PATCH), jnp.int32),
        pltpu.VMEM((PATCH, images, D), BF), pltpu.VMEM((PATCH * images, D), BF),
        pltpu.VMEM((D, 3 * D), BF), pltpu.VMEM((D, D), BF), pltpu.VMEM((D, FF), BF), pltpu.VMEM((FF, D), BF),
        vm(row), vm(row), pltpu.VMEM((3, n, D), BF), vm(heads), vm(row), pltpu.VMEM((n, D), F32), vm(row),
        vm(wide), vm(wide), pltpu.VMEM((2, n, HALF), F32), pltpu.VMEM((2, n, HALF), BF), pltpu.VMEM((n, D), F32),
        pltpu.VMEM((3, 1, D), F32), vm(row),
        pltpu.SemaphoreType.DMA((24,)),
    ]
    got = pl.pallas_call(
        partial(encode_kernel, group, groups),
        in_specs=[SMEM, SMEM] + [VMEM] * 5 + [HBM] * 6,
        out_specs=[HBM] * len(outs),
        out_shape=outs,
        scratch_shapes=scratch,
        compiler_params=params(LIMIT),
        cost_estimate=cost(2 * n * 12 * D * D, 25e6),
        name="encode",
    )(ids, visible, order, gains, biases, qvb, upb, rows, cot, *weights)
    ready = got[12:]
    return got[:12], [ready[i * groups : (i + 1) * groups] for i in range(4)]


def block_end(copies, n, got_weights, so, s1, s2, bias, gain, up_b, x, o, y1, h2, a, gp, u, tile, acc, res):
    got_o, got_1, got_2 = got_weights
    copies.wait(got_o)
    y1[...] = nn(o[...], so[...]) + f32_row(bias, 1) + x[...].astype(F32)
    norm_rows(y1, h2, n, f32_row(gain, 1), f32_row(bias, 2))
    copies.wait(got_1, got_2)
    mlp_forward(n, h2, s1, s2, up_b, u, a, gp, tile, acc, res, lambda: y1[...] + f32_row(bias, 3))


def target_kernel(group, ids, visible, order_in, gain, bias, qvb, upb, rows, wqkv, wo, w1, w2, res_out,
                  order, rows_v, flat, sqkv, so, s1, s2, x, hq, qkv, o, y1, h2, u, tile, acc, shifts, res, sems):
    n = GROUP * NM
    q, k, v = qkv.at[0], qkv.at[1], qkv.at[2]

    @pl.when(ids[0] == 0)
    def _():
        copies = Copies(sems)
        split_orders(order_in, order)
        got_rows = copies.start(rows.at[0], rows_v)
        got_qkv = copies.start(wqkv, sqkv)
        got_weights = start_weights(copies, (wo, w1, w2), (so, s1, s2))
        set_biases(shifts, qvb)
        copies.wait(got_rows)
        flatten(rows_v, flat)

        def pick_rows(i):
            image = group * GROUP + i
            pick = pick_matrix(order, image, FIRST, NM, visible[image], PATCH)
            x[rows_of(i, NM), :] = nn(pick, flat[...]).astype(BF)

        loop(GROUP, pick_rows)
        norm_rows(x, hq, n, f32_row(gain, 0), f32_row(bias, 0))
        copies.wait(got_qkv)

        def keep(j, value):
            scale = jnp.where(j == 0, 0.125, 1.0)
            qkv[j] = ((value + shifts[j]).astype(BF).astype(F32) * scale).astype(BF)

        project(3, n, hq, sqkv, 0, keep)

        def key_ok(i):
            return lax.broadcasted_iota(jnp.int32, (NM, 1), 0) + FIRST >= visible[group * GROUP + i]

        attention_by_columns(GROUP, NM, q, k, v, None, o, key_ok)
        block_end(copies, n, got_weights, so, s1, s2, bias, gain, upb, x, o, y1, h2, None, None, u, tile, acc, res)
        copies.start(res, res_out)
        copies.finish()


def target(group, ids, visible, order, vecs, rows, weights):
    n = GROUP * NM
    images = order.shape[0]
    row, full = pltpu.VMEM((n, D), BF), pltpu.VMEM((n, D), F32)
    return pl.pallas_call(
        partial(target_kernel, group),
        in_specs=[SMEM, SMEM] + [VMEM] * 5 + [HBM] * 5,
        out_specs=HBM,
        out_shape=struct((n, D)),
        scratch_shapes=[
            pltpu.VMEM((images, 1, PATCH), jnp.int32),
            pltpu.VMEM((PATCH, images, D), BF), pltpu.VMEM((PATCH * images, D), BF),
            pltpu.VMEM((D, 3 * D), BF), pltpu.VMEM((D, D), BF), pltpu.VMEM((D, FF), BF), pltpu.VMEM((FF, D), BF),
            row, row, pltpu.VMEM((3, n, D), BF), row, full, row,
            pltpu.VMEM((2, n, HALF), F32), pltpu.VMEM((2, n, HALF), BF), full, pltpu.VMEM((3, 1, D), F32), row,
            pltpu.SemaphoreType.DMA((8,)),
        ],
        compiler_params=params(LIMIT),
        cost_estimate=cost(1e6, 1e5),
        name="target",
    )(ids, visible, order, *vecs, rows, *weights)


def regress_kernel(group, ids, visible, gains, biases, qvb, upb, lat_in, x_in, q_in, dyb_in, wqkv, wo, w1, w2,
                   dlat_out, res_out, hk_out, dq_out, dkv_out, o_out, dy1b_out, h2_out, du_out, a_out, dy1_out,
                   sums_out,
                   sqkv, so, s1, s2, x, lat, hk, q, kv, p, o, y1, h2, gp, a, u, tile, acc, shifts,
                   res, dyb, du, dy1, dy1b, do, dq, dkv, dh, dlat, sums, sems):
    n, m = GROUP * NM, GROUP * NV
    k, v = kv.at[0], kv.at[1]

    @pl.when(ids[0] == 1)
    def _():
        copies = Copies(sems)
        gain, bias = gains.at[0], biases.at[0]
        got_lat = copies.start(lat_in, lat)
        got_kv = copies.start(wqkv.at[0, :, pl.ds(D, 2 * D)], sqkv)
        got_q = copies.start(q_in, q)
        got_x = copies.start(x_in, x)
        got_weights = start_weights(copies, (wo.at[0], w1.at[0], w2.at[0]), (so, s1, s2))
        got_dyb = copies.start(dyb_in, dyb)
        set_biases(shifts, qvb)
        copies.wait(got_lat)
        norm_rows(lat, hk, m, f32_row(gain, 0), f32_row(bias, 0))
        copies.start(hk, hk_out)
        copies.wait(got_kv)

        def keep_kv(j, value):
            kv[j] = (value + shifts[j + 1]).astype(BF)

        project(2, m, hk, sqkv, 0, keep_kv)
        copies.wait(got_q, got_x)

        def key_ok(i):
            return lax.broadcasted_iota(jnp.int32, (NV, 1), 0) < visible[group * GROUP + i]

        attention_by_columns(GROUP, NV, q, k, v, p, o, key_ok)
        copies.start(o, o_out)
        block_end(copies, n, got_weights, so, s1, s2, bias, gain, upb, x, o, y1, h2, a, gp, u, tile, acc, res)
        copies.start(res, res_out)
        copies.start(h2, h2_out)
        copies.start(a, a_out)
        copies.wait(got_dyb)
        mlp_back(n, dyb, gp, s1, s2, du, u, acc)
        copies.start(du, du_out)

        def keep(sel, dx):
            dy1[sel, :] = dx
            dy1b[sel, :] = dx.astype(BF)

        g2, b2 = norm_back(y1, acc, dyb, keep, n, f32_row(gain, 1))
        copies.start(dy1, dy1_out)
        copies.start(dy1b, dy1b_out)
        do[...] = nt(dy1b[...], so[...]).astype(BF)
        attention_back_columns(GROUP, NV, q, k, v, p, do, dq, dkv)
        copies.start(dq, dq_out)
        copies.start(dkv, dkv_out)
        dh[...] = nt(dkv[:, :D], sqkv[:, :D])
        dh[...] += nt(dkv[:, D:], sqkv[:, D:])

        def keep_side(sel, dx):
            dlat[sel, :] = dx.astype(BF)

        gk, bk = norm_back(lat, dh, None, keep_side, m, f32_row(gain, 0))
        copies.start(dlat, dlat_out)
        for row, value in enumerate((gk, g2, bk, b2)):
            sums[pl.ds(row, 1), :] = value
        copies.start(sums, sums_out)
        copies.finish()


def regress(group, ids, visible, vecs, lat, x, q, dyb, weights):
    n, m = GROUP * NM, GROUP * NV
    row, side, wide = struct((n, D)), struct((m, D)), struct((n, FF))
    pair = struct((m, 2 * D))
    outs = [side, row, side, row, pair, row, row, row, wide, wide, struct((n, D), F32), struct((8, D), F32)]
    vm = lambda s: pltpu.VMEM(s.shape, s.dtype)
    full, fside = pltpu.VMEM((n, D), F32), pltpu.VMEM((m, D), F32)
    scratch = [
        pltpu.VMEM((D, 2 * D), BF), pltpu.VMEM((D, D), BF), pltpu.VMEM((D, FF), BF), pltpu.VMEM((FF, D), BF),
        vm(row), vm(side), vm(side), vm(row), pltpu.VMEM((2, m, D), BF),
        pltpu.VMEM((GROUP * PAIRS, NV, 2 * NM), BF), vm(row), full, vm(row), vm(wide), vm(wide),
        pltpu.VMEM((2, n, HALF), F32), pltpu.VMEM((2, n, HALF), BF), full, pltpu.VMEM((3, 1, D), F32),
        vm(row), vm(row), vm(wide), full, vm(row), vm(row), vm(row), vm(pair), fside, vm(side),
        pltpu.VMEM((8, D), F32),
        pltpu.SemaphoreType.DMA((24,)),
    ]
    return pl.pallas_call(
        partial(regress_kernel, group),
        in_specs=[SMEM, SMEM] + [VMEM] * 4 + [HBM] * 8,
        out_specs=[HBM] * len(outs),
        out_shape=outs,
        scratch_shapes=scratch,
        compiler_params=params(LIMIT),
        cost_estimate=cost(4 * n * 12 * D * D, 25e6),
        name="regress",
    )(ids, visible, *vecs, lat, x, q, dyb, *weights)


def stack_rows(copies, pieces, ref, size):
    return [copies.start(piece, ref.at[pl.ds(i * size, size)]) for i, piece in enumerate(pieces)]


def clear_tail(ref, used):
    ref[pl.ds(used, ref.shape[0] - used), :] = jnp.zeros((ref.shape[0] - used, ref.shape[1]), ref.dtype)


def halves(count, blocks):
    rows = D // 16
    if count == 16:
        return [struct((2, 2, 2, blocks, rows, D))] + [struct((2, blocks, rows, D))] * 4
    return [struct((D, D))] * blocks


def give_blocks(copies, core, tree, left_right, out, dest):
    size = 8 if tree else 1
    blocks = out.shape[0]
    first = copies.take(blocks * size)

    def send(j, act):
        if not tree:
            for block in range(blocks):
                pl.when(j == block)(lambda block=block: act(out.at[block], dest[block], first + block))
            return
        view = out.at[j].reshape(2, 2, 2, 2, D // 16, D)
        for x in range(2):
            for low in range(2):
                at = first + j * size + 4 * x + 2 * low
                act(view.at[:, low, x, core], dest[0].at[x, low, :, j], at)
                act(view.at[:, low, x, 1 - core], dest[1 + 2 * x + low].at[:, j], at + 1)

    def body(j):
        out[j] = left_right(j)
        send(j, copies.begin)

    loop(blocks, body)
    loop(blocks, lambda j: send(j, copies.wait_at))


def give_rows(copies, core, tree, multiply, out, dest):
    size = 4 if tree else 1
    first = copies.take(4 * size)

    def send(j, act):
        if not tree:
            act(out.at[j], dest[0].at[pl.ds(pl.multiple_of(j * D, D), D)], first + j)
            return
        view = out.at[j].reshape(2, 2, D // 4, D)
        low, high = lax.rem(j, 2), lax.div(j, 2)
        for x in range(2):
            at = first + j * size + 2 * x
            act(view.at[x, core], dest[0].at[x, low, high, 0], at)
            act(view.at[x, 1 - core], dest[1].at[x, low, high, 0], at + 1)

    def body(j):
        out[j] = multiply(j)
        send(j, copies.begin)

    loop(4, body)
    loop(4, lambda j: send(j, copies.wait_at))


def down_kernel(groups, parts, ids, *refs):
    cot, lat, a_enc, a_reg, dyb_reg = (refs[i * groups : (i + 1) * groups] for i in range(5))
    refs = refs[5 * groups :]
    dest, refs = refs[:parts], refs[parts:]
    sums_out, cot_v, dyb, a, dlat, out, sums, sems = refs
    images = groups * GROUP
    nv, nm = GROUP * NV, GROUP * NM

    @pl.when(ids[0] == 0)
    def _():
        copies = Copies(sems)
        got = stack_rows(copies, cot, cot_v, nv) + stack_rows(copies, lat, dlat, nv)
        stack_rows(copies, a_enc, a, nv)
        copies.wait(*got)
        dyb[...] = (cot_v[...].astype(F32) + dlat[...].astype(F32)).astype(BF)
        copies.finish()

    @pl.when(ids[0] == 1)
    def _():
        copies = Copies(sems)
        stack_rows(copies, a_reg, a, nm)
        stack_rows(copies, dyb_reg, dyb, nm)
        clear_tail(a, images * NM)
        clear_tail(dyb, images * NM)
        copies.finish()

    copies = Copies(sems)

    def multiply(j):
        return tn(a[:, pl.ds(pl.multiple_of(j * D, D), D)], dyb[...]).astype(BF)

    give_rows(copies, ids[1], parts == 2, multiply, out, dest)
    sums[...] = jnp.broadcast_to(column_sum(dyb, images * NV), (8, D))
    copies.start(sums, sums_out)
    copies.finish()


def down_grad(groups, count, ids, cot, dlat, a_enc, a_reg, dyb_reg):
    n = groups * GROUP * NV
    main = [struct((2, 2, 2, 1, D // 4, D))] * 2 if count == 16 else [struct((FF, D))]
    outs = main + [struct((8, D), F32)]
    row = pltpu.VMEM((n, D), BF)
    scratch = [
        row, row, pltpu.VMEM((n, FF), BF), row, pltpu.VMEM((4, D, D), BF), pltpu.VMEM((8, D), F32),
        pltpu.SemaphoreType.DMA((24,)),
    ]
    got = pl.pallas_call(
        partial(down_kernel, groups, len(main)),
        in_specs=[SMEM] + [HBM] * (5 * groups),
        out_specs=[HBM] * len(outs),
        out_shape=outs,
        scratch_shapes=scratch,
        compiler_params=params(LIMIT),
        cost_estimate=cost(1e6, 1e5),
        name="down_grad",
    )(ids, *cot, *dlat, *a_enc, *a_reg, *dyb_reg)
    return got[: len(main)], got[-1]


def mlp_kernel(first, groups, ids, visible, order_in, gains, cot, dlat_in, w1, w2, y1_in, gp_in, *refs):
    if first:
        picked, refs = refs[:groups], refs[groups:]
    du_out, dy1_out, dy1b_out, sums_out, order, rows_v, flat, refs = *refs[:7], refs[7:]
    s1, s2, cot_v, dlat, dyb, gp, y1, du, u, acc, dy1, dy1b, sums, sems = refs
    n = GROUP * NV
    third = FF // 3

    @pl.when(ids[0] == 0)
    def _():
        copies = Copies(sems)
        got = [copies.start(dlat_in, dlat)]
        if first:
            got_rows = copies.start(cot.at[0], rows_v)
        else:
            got.append(copies.start(cot, cot_v))
        start = copies.take(9)

        def parts(i):
            cols = pl.ds(pl.multiple_of(i * third, third), third)
            return (
                (w2.at[0, cols, :], s2.at[cols, :]),
                (gp_in.at[:, cols], gp.at[:, cols]),
                (w1.at[0, :, cols], s1.at[:, cols]),
            )

        for i in range(3):
            for k, (src, dst) in enumerate(parts(i)):
                copies.begin(src, dst, start + 3 * i + k)
        got_y = copies.start(y1_in, y1)

        def ready(i, which):
            for k in ((0, 1), (2,))[which]:
                copies.wait_at(*parts(i)[k], start + 3 * i + k)

        if first:
            split_orders(order_in, order)
            copies.wait(got_rows)
            flatten(rows_v, flat)
            for g in reversed(range(groups)):

                def pick_rows(i, g=g):
                    image = g * GROUP + i
                    pick = pick_matrix(order, image, 0, NV, 0, visible[image])
                    cot_v[rows_of(i, NV), :] = nn(pick, flat[...]).astype(BF)

                loop(GROUP, pick_rows)
                copies.wait(copies.start(cot_v, picked[g]))
        copies.wait(*got)
        dyb[...] = (cot_v[...].astype(F32) + dlat[...].astype(F32)).astype(BF)
        mlp_back(n, dyb, gp, s1, s2, du, u, acc, ready)
        copies.start(du, du_out)
        copies.wait(got_y)

        def keep(sel, dx):
            dy1[sel, :] = dx
            dy1b[sel, :] = dx.astype(BF)

        g2, b2 = norm_back(y1, acc, dyb, keep, n, f32_row(gains.at[0], 1))
        copies.start(dy1, dy1_out)
        copies.start(dy1b, dy1b_out)
        sums[pl.ds(0, 1), :] = g2
        sums[pl.ds(1, 1), :] = b2
        copies.start(sums, sums_out)
        copies.finish()


def mlp_grad(first, groups, ids, visible, order, gains, cot, dlat, w1, w2, y1, gp):
    n = GROUP * NV
    images = order.shape[0]
    row, wide, full = pltpu.VMEM((n, D), BF), pltpu.VMEM((n, FF), BF), pltpu.VMEM((n, D), F32)
    outs = [struct((n, D))] * (groups if first else 0) + [struct((n, FF)), struct((n, D), F32), struct((n, D)), struct((8, D), F32)]
    got = pl.pallas_call(
        partial(mlp_kernel, first, groups),
        in_specs=[SMEM, SMEM, VMEM, VMEM] + [HBM] * 6,
        out_specs=[HBM] * len(outs),
        out_shape=outs,
        scratch_shapes=[
            pltpu.VMEM((images, 1, PATCH), jnp.int32),
            pltpu.VMEM((PATCH, images, D), BF), pltpu.VMEM((PATCH * images, D), BF),
            pltpu.VMEM((D, FF), BF), pltpu.VMEM((FF, D), BF), row, row, row, wide, full, wide,
            pltpu.VMEM((2, n, HALF), F32), full, full, row, pltpu.VMEM((8, D), F32), pltpu.SemaphoreType.DMA((24,)),
        ],
        compiler_params=params(LIMIT),
        cost_estimate=cost(1e6, 1e5),
        name="mlp_grad",
    )(ids, visible, order, gains, cot, dlat, w1, w2, y1, gp)
    return got[:-4], got[-4:]


def up_kernel(groups, parts, ids, *refs):
    pieces = [refs[i * groups : (i + 1) * groups] for i in range(8)]
    refs = refs[8 * groups :]
    dest, refs = refs[:parts], refs[parts:]
    sums_out, left, right, out, sums, sems = refs
    images = groups * GROUP

    def load(du, h2, dy1b, o, size):
        copies = Copies(sems)
        stack_rows(copies, h2, left.at[0], size)
        for j in range(4):
            stack_rows(copies, [one.at[:, pl.ds(j * D, D)] for one in du], right.at[j], size)
        stack_rows(copies, o, left.at[1], size)
        stack_rows(copies, dy1b, right.at[4], size)
        return copies

    @pl.when(ids[0] == 0)
    def _():
        load(*pieces[:4], GROUP * NV).finish()

    @pl.when(ids[0] == 1)
    def _():
        copies = load(*pieces[4:], GROUP * NM)
        for ref in (left, right):
            for i in range(ref.shape[0]):
                clear_tail(ref.at[i], images * NM)
        copies.finish()

    copies = Copies(sems)

    def multiply(j):
        value = tn(left[lax.div(j, 4)], right[j]).astype(BF)
        sums[pl.ds(j, 1), :] = column_sum(right.at[j], images * NV)
        return value

    give_blocks(copies, ids[1], dest[0].ndim == 6, multiply, out, dest)
    copies.start(sums, sums_out)
    copies.finish()


def up_grad(groups, count, ids, *pieces):
    n = groups * GROUP * NV
    main = halves(count, 5)
    outs = main + [struct((8, D), F32)]
    got = pl.pallas_call(
        partial(up_kernel, groups, len(main)),
        in_specs=[SMEM] + [HBM] * (8 * groups),
        out_specs=[HBM] * len(outs),
        out_shape=outs,
        scratch_shapes=[
            pltpu.VMEM((2, n, D), BF), pltpu.VMEM((5, n, D), BF), pltpu.VMEM((5, D, D), BF), pltpu.VMEM((8, D), F32),
            pltpu.SemaphoreType.DMA((44,)),
        ],
        compiler_params=params(LIMIT),
        cost_estimate=cost(1e6, 1e5),
        name="up_grad",
    )(ids, *[ref for piece in pieces for ref in piece])
    return got[: len(main)], got[-1]


def attn_kernel(groups, last, ids, gains, *refs):
    if last:
        down_sums, up_sums, refs = refs[0], refs[1], refs[2:]
        mlp_sums, reg_sums = (refs[i * groups : (i + 1) * groups] for i in range(2))
        before, refs = refs[2 * groups : 3 * groups - 1], refs[3 * groups - 1 :]
    (wqkv, wo, dy1_enc, q_in, k_in, v_in, p_in, x_enc, dq_reg, dkv_reg, dy1_reg, x_reg,
     dq_out, dkv_out, dx_out, sums_out,
     sqkv, so, dy1, dy1b, q, k, v, p, x, do, dq, dkv, dh, sems) = refs
    m = GROUP * NM
    top = pl.ds(0, m)
    gain = f32_row(gains.at[0], 0)

    def finish(copies, rows):
        def keep(sel, dx):
            dy1[sel, :] = dx

        own = (*norm_back(x, dh, dy1, keep, rows, gain), column_sum(dq, rows), column_sum(dkv, GROUP * NV, D))
        copies.start(dy1, dx_out)
        if not last:
            for row, value in enumerate(own):
                sums_out[row : row + 1, :] = value
            copies.finish()
            return

        def total_of(sums):
            total = sums[0][...]
            for more in sums[1:]:
                total = total + more[...]
            return total

        done, mlp, reg = total_of(before), total_of(mlp_sums), total_of(reg_sums)
        g1, b1, queries, values = (one + done[row : row + 1, :] for row, one in enumerate(own))
        encoder = ids[0] == 0
        sums_out[0:1, :] = g1 + jnp.where(encoder, 0.0, reg[0:1, :])
        sums_out[1:2, :] = jnp.where(encoder, mlp[0:1, :], reg[1:2, :])
        sums_out[2:3, :] = b1 + jnp.where(encoder, 0.0, reg[2:3, :])
        sums_out[3:4, :] = up_sums[4:5, :]
        sums_out[4:5, :] = jnp.where(encoder, mlp[1:2, :], reg[3:4, :])
        sums_out[5:6, :] = down_sums[0:1, :]
        sums_out[6:7, :] = queries
        sums_out[7:8, :] = values
        sums_out[8:12, :] = up_sums[0:4, :]
        sums_out[12:16, :] = jnp.zeros((4, D), F32)
        copies.finish()

    @pl.when(ids[0] == 0)
    def _():
        copies = Copies(sems)
        got = [copies.start(dy1_enc, dy1), copies.start(wo.at[0], so)]
        later = [copies.start(src, dst) for src, dst in ((v_in, v), (p_in, p), (k_in, k), (q_in, q))]
        final = [copies.start(wqkv.at[0], sqkv), copies.start(x_enc, x)]
        copies.wait(*got)
        dy1b[...] = dy1[...].astype(BF)
        do[...] = nt(dy1b[...], so[...]).astype(BF)
        copies.wait(*later)
        attention_back_rows(GROUP, NV, q, k, v, p, do, dq, dkv)
        copies.start(dq, dq_out)
        copies.start(dkv, dkv_out)
        copies.wait(*final)
        dh[...] = nt(dq[...], sqkv[:, 0:D])
        for j in range(2):
            dh[...] += nt(dkv[:, j * D : (j + 1) * D], sqkv[:, (j + 1) * D : (j + 2) * D])
        finish(copies, GROUP * NV)

    @pl.when(ids[0] == 1)
    def _():
        copies = Copies(sems)
        for src, dst in ((dq_reg, dq), (dy1_reg, dy1), (x_reg, x)):
            copies.start(src, dst.at[top])
        copies.start(dkv_reg, dkv)
        copies.start(wqkv.at[0, :, pl.ds(0, D)], sqkv.at[:, pl.ds(0, D)])
        copies.finish()
        dh[top, :] = nt(dq[top, :], sqkv[:, 0:D])
        finish(copies, m)


def attn_back(groups, last, ids, gains, sums, *pieces):
    n = GROUP * NV
    row, full = pltpu.VMEM((n, D), BF), pltpu.VMEM((n, D), F32)
    outs = [struct((n, D)), struct((n, 2 * D)), struct((n, D), F32), struct((16, D), F32)]
    return pl.pallas_call(
        partial(attn_kernel, groups, last),
        in_specs=[SMEM, VMEM] + [VMEM] * len(sums) + [HBM] * len(pieces),
        out_specs=[HBM] * 3 + [VMEM],
        out_shape=outs,
        scratch_shapes=[
            pltpu.VMEM((D, 3 * D), BF), pltpu.VMEM((D, D), BF), full, row, row, row, row,
            pltpu.VMEM((GROUP * PAIRS, 2 * NV, NV), BF), row, row, row, pltpu.VMEM((n, 2 * D), BF), full,
            pltpu.SemaphoreType.DMA((20,)),
        ],
        compiler_params=params(LIMIT),
        cost_estimate=cost(1e6, 1e5),
        name="attn_back",
    )(ids, gains, *sums, *pieces)


def qkv_kernel(groups, parts, ids, *refs):
    pieces = [refs[i * groups : (i + 1) * groups] for i in range(7)]
    dq_enc, dkv_enc, hq_enc, hq_reg, hk_reg, dq_reg, dkv_reg = pieces
    refs = refs[7 * groups :]
    dest, refs = refs[:parts], refs[parts:]
    left, right, out, sems = refs
    images = groups * GROUP
    nv, nm = GROUP * NV, GROUP * NM
    hk, hq = left.at[0], left.at[1]
    dk, dv, dq = (right.at[i] for i in range(3))

    @pl.when(ids[0] == 0)
    def _():
        copies = Copies(sems)
        stack_rows(copies, hq_enc, hk, nv)
        stack_rows(copies, [one.at[:, pl.ds(0, D)] for one in dkv_enc], dk, nv)
        stack_rows(copies, [one.at[:, pl.ds(D, D)] for one in dkv_enc], dv, nv)
        stack_rows(copies, hq_enc, hq, nv)
        stack_rows(copies, dq_enc, dq, nv)
        copies.finish()

    @pl.when(ids[0] == 1)
    def _():
        copies = Copies(sems)
        for piece, ref in ((hq_reg, hq), (dq_reg, dq)):
            stack_rows(copies, piece, ref, nm)
            clear_tail(ref, images * NM)
        stack_rows(copies, hk_reg, hk, nv)
        stack_rows(copies, [one.at[:, pl.ds(0, D)] for one in dkv_reg], dk, nv)
        stack_rows(copies, [one.at[:, pl.ds(D, D)] for one in dkv_reg], dv, nv)
        copies.finish()

    copies = Copies(sems)

    def multiply(j):
        return tn(left[lax.div(j, 2)], right[j]).astype(BF)

    give_blocks(copies, ids[1], dest[0].ndim == 6, multiply, out, dest)


def qkv_grad(groups, count, ids, *pieces):
    n = groups * GROUP * NV
    row = pltpu.VMEM((n, D), BF)
    main = halves(count, 3)
    scratch = [
        pltpu.VMEM((2, n, D), BF), pltpu.VMEM((3, n, D), BF), pltpu.VMEM((3, D, D), BF),
        pltpu.SemaphoreType.DMA((40,)),
    ]
    return pl.pallas_call(
        partial(qkv_kernel, groups, len(main)),
        in_specs=[SMEM] + [HBM] * (7 * groups),
        out_specs=[HBM] * len(main),
        out_shape=main,
        scratch_shapes=scratch,
        compiler_params=params(LIMIT),
        cost_estimate=cost(1e6, 1e5),
        name="qkv_grad",
    )(ids, *[ref for piece in pieces for ref in piece])


def place_kernel(groups, ids, visible, order_in, *refs):
    dx_in, lat_enc, res_enc, res_reg = (refs[i * groups : (i + 1) * groups] for i in range(4))
    block_out, grad_out, order, dx, lat, out, grads, sems = refs[4 * groups :]
    images = groups * GROUP
    nv, nm = GROUP * NV, GROUP * NM
    split_orders(order_in, order)

    def put_grad(i, put, value):
        high = value.astype(BF)
        low = (value - high.astype(F32)).astype(BF)
        grads[i] = nn(put, high) + nn(put, low)

    def write_grads():
        copies = Copies(sems)
        for i in range(images):
            copies.start(grads.at[i], grad_out.at[0, :, i, :])
        copies.finish()

    @pl.when(ids[0] == 0)
    def _():
        copies = Copies(sems)
        for piece, ref, size in ((dx_in, dx, nv), (lat_enc, lat, nv), (res_enc, out, nm)):
            stack_rows(copies, piece, ref, size)
        copies.finish()

        def put_image(i):
            put = place_matrix(order, i, 0, NV, 0, visible[i])
            put_side = place_matrix(order, i, FIRST, NM, visible[i], PATCH)
            put_grad(i, put, dx[rows_of(i, NV), :])
            block_out[0, i] = (nn(put, lat[rows_of(i, NV), :]) + nn(put_side, out[rows_of(i, NM), :])).astype(BF)

        loop(images, put_image)
        write_grads()

    @pl.when(ids[0] == 1)
    def _():
        copies = Copies(sems)
        stack_rows(copies, res_reg, out, nm)
        stack_rows(copies, [piece.at[pl.ds(0, nm)] for piece in dx_in], dx, nm)
        copies.finish()

        def put_image(i):
            put = place_matrix(order, i, FIRST, NM, visible[i], PATCH)
            put_grad(i, put, dx[rows_of(i, NM), :])
            block_out[0, i] = nn(put, out[rows_of(i, NM), :]).astype(BF)

        loop(images, put_image)
        write_grads()


def place(groups, ids, visible, order, *pieces):
    images = groups * GROUP
    n = images * NV
    outs = [struct((1, images, PATCH, D)), struct((1, PATCH, images, D), F32)]
    return pl.pallas_call(
        partial(place_kernel, groups),
        in_specs=[SMEM, SMEM, VMEM] + [HBM] * (4 * groups),
        out_specs=[VMEM, HBM],
        out_shape=outs,
        scratch_shapes=[
            pltpu.VMEM((images, 1, PATCH), jnp.int32), pltpu.VMEM((n, D), F32), pltpu.VMEM((n, D), BF),
            pltpu.VMEM((images * NM, D), BF), pltpu.VMEM((images, PATCH, D), F32), pltpu.SemaphoreType.DMA((8,)),
        ],
        compiler_params=params(LIMIT),
        cost_estimate=cost(1e6, 1e5),
        name="place",
    )(ids, visible, order, *[ref for piece in pieces for ref in piece])


BITS = (2, 4, 8)


def hop(value, bit):
    return lax.ppermute(value, "dp", [(i, i ^ bit) for i in range(16)])


def combine_kernel(jobs, given, ids, *refs):
    used = sum(sum(4 if gone is None else 1 for gone in terms) for terms, *_ in jobs)
    inputs, outs, scratch = list(refs[:used]), list(refs[used : used + given]), list(refs[used + given :])
    copies = Copies(scratch.pop())
    plans = []

    def fetch(term, gone, bits, own):
        if gone is not None:
            path = tuple(bits[gone:])
            copy = copies.start(term.at[path] if path else term, own)
            return lambda: copies.wait(copy)
        wide = len(bits) == 1
        first = copies.take(2 if wide else 1)
        rest = tuple(bits[2:])

        def piece(x, low):
            ref = term[2 * x + low]
            return ref.at[rest] if rest else ref

        for x in range(2):
            for low in range(2):
                if wide:
                    pl.when(bits[0] == x)(
                        lambda x=x, low=low: copies.begin(piece(x, low), own.at[low], first + low)
                    )
                else:
                    pl.when((bits[0] == x) & (bits[1] == low))(
                        lambda x=x, low=low: copies.begin(piece(x, low), own, first)
                    )

        def wait():
            if wide:
                for low in range(2):
                    copies.wait_at(piece(0, low), own.at[low], first + low)
            else:
                copies.wait_at(piece(0, 0), own, first)

        return wait

    for kinds, first, last, targets, finals in jobs:
        terms = [inputs.pop(0) if gone is not None else [inputs.pop(0) for _ in range(4)] for gone in kinds]
        for target in targets:
            bits = []
            for bit in range(last):
                flip = bit >= first and (target >> (bit - first)) & 1
                bits.append(1 - ids[2 + bit] if flip else ids[2 + bit])
            owns = [scratch.pop(0) for _ in kinds]
            waits = [fetch(term, gone, bits, own) for term, gone, own in zip(terms, kinds, owns)]
            plans.append((waits, owns, last, finals, None if finals else outs.pop(0)))
    for waits, owns, last, finals, out in plans:
        for wait in waits:
            wait()
        spots = [()]
        for _ in range(3 - last):
            spots = [spot + (i,) for spot in spots for i in range(2)]
        for spot in spots:
            for j in range(owns[0].shape[-3]):
                value = owns[0][spot + (j,)].astype(F32)
                for more in owns[1:]:
                    value = value + more[spot + (j,)].astype(F32)
                if finals:
                    which, column = finals[j]
                    outs[which][:, column * D : (column + 1) * D] = value
                else:
                    out[spot + (j,)] = value.astype(BF)


def send_job(terms, first, last, targets=(1,)):
    return terms, first, last, targets, None


def final_job(terms, finals):
    return terms, 0, 3, (0,), finals


def combine(ids, *jobs, outs=()):
    shapes = [struct(shape, F32) for shape in outs]
    plans, inputs, scratch = [], [], []
    for terms, first, last, targets, finals in jobs:
        blocks, rows = terms[0].shape[-3:-1]
        kinds = tuple(None if isinstance(term, list) else 6 - term.ndim for term in terms)
        for term in terms:
            inputs += term if isinstance(term, list) else [term]
        plans.append((kinds, first, last, targets, finals))
        part = (2,) * (3 - last) + (blocks, rows, D)
        for _ in targets:
            scratch += [pltpu.VMEM(part, BF) for _ in terms]
            if finals is None:
                shapes.append(struct(part))
    scratch.append(pltpu.SemaphoreType.DMA((2 * len(scratch),)))
    return pl.pallas_call(
        partial(combine_kernel, tuple(plans), len(shapes)),
        in_specs=[SMEM] + [HBM] * len(inputs),
        out_specs=[VMEM] * len(shapes),
        out_shape=shapes,
        scratch_shapes=scratch,
        compiler_params=params(LIMIT),
        cost_estimate=cost(1e5, 1e4),
        name="combine",
    )(ids, *inputs)


def in_order(first, then):
    return lax.optimization_barrier((first, then))


def own_columns(rows, count):
    own = D // count
    me = lax.axis_index("dp")

    def part(block, wide):
        return lax.dynamic_slice_in_dim(block, me * wide, wide, block.ndim - 1)

    return (
        part(rows[:2], own),
        part(rows[2:6], own),
        part(rows[6:8].reshape(-1), 2 * own),
        part(rows[8:12].reshape(-1), 4 * own),
    )


def scatter_natural(block):
    shards = block.reshape(lax.axis_size("dp"), -1, D)
    return lax.psum_scatter(shards, "dp", scatter_dimension=0, tiled=True)[0].astype(F32)


def local(
    patch_rows, cotangent, patch_order, visible, qkv_weight, out_weight, up_weight, down_weight, norm_gains, biases,
    qv_bias, up_bias, target_qkv, target_out, target_up, target_down, target_gains, target_biases, target_qv_bias,
    target_up_bias,
):
    count = lax.axis_size("dp")
    tree = count == 16
    place_dp = lax.axis_index("dp")
    bits = [(place_dp // bit) % 2 for bit in (1,) + BITS]
    ids = jnp.stack([lax.axis_index("section")] + bits).astype(jnp.int32)
    groups = patch_order.shape[0] // GROUP
    weights = (qkv_weight, out_weight, up_weight, down_weight)
    targets = (target_qkv, target_out, target_up, target_down)
    vecs = (norm_gains, biases, qv_bias, up_bias)
    target_vecs = (target_gains, target_biases, target_qv_bias[None], target_up_bias[None])

    rows, cot = patch_rows.transpose(0, 2, 1, 3), cotangent.transpose(0, 2, 1, 3)
    calls = [
        encode(g, groups, ids, visible, patch_order, *vecs, rows, cot, weights) for g in range(groups)
    ]
    lat, x_e, hq_e, q_e, k_e, v_e, p_e, o_e, y1_e, h2_e, gp_e, a_e = zip(*[call[0] for call in calls])
    x_r, hq_r, q_r, dyb_r = calls[-1][1]
    sent = [lax.ppermute(piece, "section", [(0, 1)]) for piece in lat]
    vectors = (norm_gains, biases, qv_bias, up_bias)
    regressed = [regress(0, ids, visible, vectors, sent[0], x_r[0], q_r[0], dyb_r[0], weights)]
    back = [lax.ppermute(regressed[0][0], "section", [(1, 0)])]
    for g in range(1, groups):
        regressed.append(regress(g, ids, visible, vectors, sent[g], x_r[g], q_r[g], dyb_r[g], weights))
        back.append(lax.ppermute(regressed[g][0], "section", [(1, 0)]))
    _, res_r, hk_r, dq_r, dkv_r, o_r, dy1b_r, h2_r, du_r, a_r, dy1_r, sums_r = zip(*regressed)
    order_first, res_r = in_order(patch_order, res_r)
    res_e = [target(0, ids, visible, order_first, target_vecs, rows, targets)]
    res_e[0], back[0] = in_order(res_e[0], back[0])
    def mlp(g, cot):
        return mlp_grad(
            g == 0, groups, ids, visible, patch_order, norm_gains, cot, back[g], up_weight, down_weight, y1_e[g], gp_e[g]
        )

    def attention(g, dy1, sums=()):
        return attn_back(
            groups, len(sums) > 0, ids, norm_gains, sums, qkv_weight, out_weight, dy1, q_e[g], k_e[g], v_e[g], p_e[g],
            x_e[g], dq_r[g], dkv_r[g], dy1_r[g], x_r[g],
        )

    cot_e, first = mlp(0, cot)
    mlps = [first] + [mlp(g, cot_e[g])[1] for g in range(1, groups - 1)]
    attns = [attention(g, mlps[g][1]) for g in range(groups - 1)]
    last = groups - 1
    send = partial(combine, ids)
    attns, back[last] = in_order(attns, back[last])
    down, sums_down = down_grad(groups, count, ids, cot_e, back, a_e, a_r, dyb_r)
    cot_last = cot_e[last]
    down, cot_last = in_order(down, cot_last)
    mlps.append(mlp(last, cot_last)[1])
    du_e, dy1_e, dy1b_e, sums_e = (list(piece) for piece in zip(*mlps))
    if tree:
        downs = [down[0], hop(down[1], 1)]
        (down_x,), du_e[last] = in_order(send(send_job(downs, 0, 1)), du_e[last])
        downs = downs + [hop(down_x, 2)]
    up, sums_up = up_grad(groups, count, ids, du_e, h2_e, dy1b_e, o_e, du_r, h2_r, dy1b_r, o_r)
    sums_in = [piece[3] for piece in attns]
    attns.append(attention(last, dy1_e[last], (sums_down, sums_up, *sums_e, *sums_r, *sums_in)))
    dq_e, dkv_e, dx, small = (list(piece) for piece in zip(*attns))
    small = small[last]
    order_late = patch_order
    if tree:
        peers = (3, 2, 1)
        ups = [up[0], [hop(piece, 1) for piece in up[1:]]]
        (up_x,), (dq_e[last], downs) = in_order(send(send_job(ups, 0, 1)), (dq_e[last], downs))
        ups = ups + [hop(up_x, 2)]
        down_z, dq_e[last] = in_order(send(send_job(downs, 1, 3, peers)), dq_e[last])
        down_got = [hop(one, 4 * peer) for one, peer in zip(down_z, peers)]
        small = small + hop(small, 1)
        small, dq_e[last] = in_order(small, dq_e[last])
    attn = qkv_grad(groups, count, ids, dq_e, dkv_e, hq_e, hq_r, hk_r, dq_r, dkv_r)
    if tree:
        down_got, attn = in_order(down_got, attn)
        pieces = [hop(piece, 1) for piece in attn[1:]]
        pieces, small = in_order(pieces, small)
        qkvs = [attn[0], pieces]
        got = hop(small, 2)
        up_z, (qkvs, got) = in_order(send(send_job(ups, 1, 3, peers)), (qkvs, got))
        small = small + got
        up_got = [hop(one, 4 * peer) for one, peer in zip(up_z, peers)]
        (qkv_x,), got = in_order(send(send_job(qkvs, 0, 1)), hop(small, 4))
        small = small + got
        order_late, qkv_x = in_order(patch_order, qkv_x)
        qkvs = qkvs + [hop(qkv_x, 2)]
        got = hop(small, 8)
    res_e += [target(g, ids, visible, order_late, target_vecs, rows, targets) for g in range(1, groups)]
    if tree:
        qkv_z, res_e = in_order(send(send_job(qkvs, 1, 3, peers)), res_e)
        qkv_got = [hop(one, 4 * peer) for one, peer in zip(qkv_z, peers)]
    block_out, grad_rows = place(groups, ids, visible, patch_order, dx, lat, res_e, res_r)
    if tree:
        small = small + got
        down_sum, up_sum, out_sum = send(
            final_job(downs + down_got, ((0, 0),)),
            final_job(ups + up_got, tuple((1, j) for j in range(4)) + ((2, 0),)),
            outs=((D // 4, D), (D // 16, 4 * D), (D // 16, D)),
        )
        qkv_got, (down_sum, up_sum, out_sum) = in_order(qkv_got, (down_sum, up_sum, out_sum))
        (qkv_sum,) = send(final_job(qkvs + qkv_got, ((0, 1), (0, 2), (0, 0))), outs=((D // 16, 3 * D),))
    else:
        down_sum = scatter_natural(down[0])
        up_sum = jnp.concatenate([scatter_natural(one) for one in up[:4]], axis=1)
        out_sum = scatter_natural(up[4])
        qkv_sum = jnp.concatenate([scatter_natural(attn[i]) for i in (2, 0, 1)], axis=1)
        small = lax.psum(small, "dp")
    grad_rows = grad_rows.transpose(0, 2, 1, 3)
    gains, bias_rows, qv_rows, up_rows = own_columns(small, count)
    return (
        block_out,
        grad_rows,
        qkv_sum[None],
        out_sum[None],
        up_sum[None],
        down_sum[None],
        gains[None],
        bias_rows[None],
        qv_rows[None],
        up_rows[None],
    )


def solution(mesh):
    three, four = P("section", None, None), P("section", "dp", None, None)
    grad = P("section", "dp", None)
    return jax.shard_map(
        local,
        mesh=mesh,
        in_specs=(four, four, P("dp", None), P("dp"), three, three, three, three, three, three,
                  P("section", None), P("section", None), P(), P(), P(), P(), P(), P(), P(), P()),
        out_specs=(four, four, grad, grad, grad, grad, P("section", None, "dp"), P("section", None, "dp"),
                   P("section", "dp"), P("section", "dp")),
        check_vma=False,
    )
```

```python
from functools import partial

import jax
import jax.numpy as jnp
from jax import lax
from jax.experimental import pallas as pl
from jax.experimental.pallas import tpu as pltpu
from jax.sharding import PartitionSpec as P

HEADS = 12
PATCH = 196
D = 768
FF = 3072
EPS = 1e-06
NV = 144
NM = 128
FIRST = PATCH - NM
GROUP = 2
CHUNK = 32

BF = jnp.bfloat16
F32 = jnp.float32
MIB = 1024 * 1024
LIMIT = 62

HBM = pl.BlockSpec(memory_space=pl.ANY)
VMEM = pl.BlockSpec(memory_space=pltpu.VMEM)
SMEM = pl.BlockSpec(memory_space=pltpu.SMEM)


def nn(a, b):
    return jnp.dot(a, b, preferred_element_type=F32)


def nt(a, b):
    return lax.dot_general(a, b, (((1,), (1,)), ((), ())), preferred_element_type=F32)


def tn(a, b):
    return lax.dot_general(a, b, (((0,), (0,)), ((), ())), preferred_element_type=F32)


def loop(count, body, unroll=1):
    def step(i, carry):
        for u in range(unroll):
            body(i * unroll + u)
        return carry

    if count == unroll:
        step(0, 0)
    else:
        lax.fori_loop(0, count // unroll, step, 0)


def unroll_of(count):
    return next(u for u in (4, 3, 2, 1) if count % u == 0)


def rows_of(i, size):
    return pl.ds(pl.multiple_of(i * size, size), size)


def f32_row(ref, row, col=0, width=D):
    return ref[pl.ds(row, 1), pl.ds(col, width)].astype(F32)


class Copies:
    def __init__(self, sems):
        self.sems = sems
        self.used = 0
        self.open = []

    def start(self, src, dst):
        copy = pltpu.make_async_copy(src, dst, self.sems.at[self.used])
        self.used += 1
        copy.start()
        self.open.append(copy)
        return copy

    def wait(self, *copies):
        for copy in copies:
            copy.wait()
            self.open = [one for one in self.open if one is not copy]

    def finish(self):
        self.wait(*list(self.open))

    def take(self, count):
        self.used += count
        return self.used - count

    def begin(self, src, dst, at):
        pltpu.make_async_copy(src, dst, self.sems.at[at]).start()

    def wait_at(self, src, dst, at):
        pltpu.make_async_copy(src, dst, self.sems.at[at]).wait()


def gelu_pair(u):
    size = jnp.abs(u)
    base = 1.0 + (0.3275911 * 0.7071067811865476) * size
    guess = pl.reciprocal(base, approx=True)
    t = guess * (2.0 - base * guess)
    ex = jnp.exp2((u * u) * (-0.5 * 1.4426950408889634))
    poly = 0.5306027145 * t - 0.7265760135
    poly = poly * t + 0.7107068705
    poly = poly * t - 0.142248368
    poly = poly * t + 0.127414796
    tail = poly * t * ex
    phi = jnp.where(u >= 0.0, 1.0 - tail, tail)
    return u * phi, phi + u * (0.3989422804014327 * ex)


def norm_rows(src, dst, rows, gain, shift):
    def body(i):
        sel = rows_of(i, CHUNK)
        x = src[sel, :].astype(F32)
        centered = x - jnp.mean(x, axis=-1, keepdims=True)
        var = jnp.mean(centered * centered, axis=-1, keepdims=True)
        dst[sel, :] = (centered * lax.rsqrt(var + EPS) * gain + shift).astype(BF)

    loop(rows // CHUNK, body, unroll_of(rows // CHUNK))


def norm_back(src, grad, base, write, rows, gain):
    count = rows // CHUNK
    unroll = 3 if count % 3 == 0 else 2

    def step(i, carry):
        for u in range(unroll):
            carry = one(i * unroll + u, carry)
        return carry

    def one(i, carry):
        d_gain, d_shift = carry
        sel = rows_of(i, CHUNK)
        x = src[sel, :].astype(F32)
        dh = grad[sel, :]
        centered = x - jnp.mean(x, axis=-1, keepdims=True)
        var = jnp.mean(centered * centered, axis=-1, keepdims=True)
        rstd = lax.rsqrt(var + EPS)
        hat = centered * rstd
        g = dh * gain
        part = dh * hat
        dx = rstd * (
            g
            - jnp.mean(g, axis=-1, keepdims=True)
            - hat * jnp.mean(g * hat, axis=-1, keepdims=True)
        )
        if base is not None:
            dx = dx + base[sel, :].astype(F32)
        write(sel, dx)
        d_gain = d_gain + jnp.sum(part.reshape(CHUNK // 8, 8, D), axis=0)
        d_shift = d_shift + jnp.sum(dh.reshape(CHUNK // 8, 8, D), axis=0)
        return d_gain, d_shift

    zero = jnp.zeros((8, D), F32)
    d_gain, d_shift = lax.fori_loop(0, count // unroll, step, (zero, zero))
    return jnp.sum(d_gain, axis=0, keepdims=True), jnp.sum(d_shift, axis=0, keepdims=True)


def column_sum(ref, rows, col=0, width=D):
    def step(i, carry):
        x = ref[rows_of(i, CHUNK), pl.ds(col, width)].astype(F32)
        return carry + jnp.sum(x.reshape(CHUNK // 8, 8, width), axis=0)

    total = lax.fori_loop(0, rows // CHUNK, step, jnp.zeros((8, width), F32))
    return jnp.sum(total, axis=0, keepdims=True)


def as_bf16(flags):
    return jnp.where(flags, 1.0, 0.0).astype(BF)


def pick_matrix(order, image, start, count, low, high):
    row = order[image, :, pl.ds(start, count)].astype(F32)
    images = order.shape[0]
    col = jnp.broadcast_to(row, (8, count)).T[:, 0:1].astype(jnp.int32)
    rank = start + lax.broadcasted_iota(jnp.int32, (count, 1), 0)
    col = jnp.where((rank >= low) & (rank < high), col * images + image, -1)
    return as_bf16(col == lax.broadcasted_iota(jnp.int32, (count, PATCH * images), 1))


def place_matrix(order, image, start, count, low, high):
    row = order[image, :, pl.ds(start, count)]
    rank = start + lax.broadcasted_iota(jnp.int32, (1, count), 1)
    row = jnp.where((rank >= low) & (rank < high), row, -1)
    return as_bf16(row == lax.broadcasted_iota(jnp.int32, (PATCH, count), 0))


def flatten(rows, flat):
    flat[...] = rows[...].reshape(flat.shape)


def split_orders(order, split):
    for image in range(split.shape[0]):
        split[image] = order[image : image + 1, :]


def split_pair(pair):
    lane = lax.broadcasted_iota(jnp.int32, pair.shape, 1)
    zero = jnp.zeros_like(pair)
    return jnp.concatenate([jnp.where(lane < 64, pair, zero), jnp.where(lane < 64, zero, pair)], axis=0)


def join_rows(both):
    rows = both.shape[0] // 2
    lane = lax.broadcasted_iota(jnp.int32, (rows, 128), 1)
    return jnp.where(lane < 64, both[:rows], both[rows:])


def join_columns(both):
    rows = both.shape[1] // 2
    return jnp.concatenate([both[:64, :rows], both[64:, rows:]], axis=0).T


PAIRS = HEADS // 2
STEP = 6


def each_pair_group(images, body):
    def group(i):
        image = i // (PAIRS // STEP)
        first = (i % (PAIRS // STEP)) * STEP
        pairs = [first + step for step in range(STEP)]
        body(image, [image * PAIRS + pair for pair in pairs], [pl.ds(pl.multiple_of(pair * 128, 128), 128) for pair in pairs])

    loop(images * (PAIRS // STEP), group)


def softmax(scores, axis):
    ex = jnp.exp(scores - jnp.max(scores, axis=axis, keepdims=True))
    return (ex * (1.0 / jnp.sum(ex, axis=axis, keepdims=True))).astype(BF)


def score_back(probs, d_probs, axis):
    wide = probs.astype(F32)
    return (wide * (d_probs - jnp.sum(d_probs * wide, axis=axis, keepdims=True))).astype(BF)


def attention_by_rows(images, n, q, k, v, p, o, count_of):
    def body(image, slots, lanes):
        sel = rows_of(image, n)
        ok = lax.broadcasted_iota(jnp.int32, (1, n), 1) < count_of(image)
        scores = [nt(split_pair(q[sel, at]), k[sel, at]) for at in lanes]
        probs = [softmax(jnp.where(ok, one, -1000000000.0), 1) for one in scores]
        for slot, one in zip(slots, probs):
            p[slot] = one
        mixed = [nn(one, v[sel, at]) for one, at in zip(probs, lanes)]
        for at, one in zip(lanes, mixed):
            o[sel, at] = join_rows(one).astype(BF)

    each_pair_group(images, body)


def attention_by_columns(images, nk, q, k, v, p, o, key_ok):
    def body(image, slots, lanes):
        qs, ks = rows_of(image, NM), rows_of(image, nk)
        ok = key_ok(image)
        scores = [nt(k[ks, at], split_pair(q[qs, at])) for at in lanes]
        probs = [softmax(jnp.where(ok, one, -1000000000.0), 0) for one in scores]
        if p is not None:
            for slot, one in zip(slots, probs):
                p[slot] = one
        mixed = [tn(v[ks, at], one) for one, at in zip(probs, lanes)]
        for at, one in zip(lanes, mixed):
            o[qs, at] = join_columns(one).astype(BF)

    each_pair_group(images, body)


def attention_back_rows(images, n, q, k, v, p, do, dq, dkv):
    def body(image, slots, lanes):
        sel = rows_of(image, n)
        d_mixed = [split_pair(do[sel, at]) for at in lanes]
        d_probs = [nt(one, v[sel, at]) for one, at in zip(d_mixed, lanes)]
        d_scores = [score_back(p[slot], one, 1) for slot, one in zip(slots, d_probs)]
        d_values = [tn(p[slot], one) for slot, one in zip(slots, d_mixed)]
        d_query = [nn(one, k[sel, at]) for one, at in zip(d_scores, lanes)]
        d_keys = [tn(one, split_pair(q[sel, at])) for one, at in zip(d_scores, lanes)]
        for at, value, query, key in zip(lanes, d_values, d_query, d_keys):
            dq[sel, at] = (join_rows(query) * 0.125).astype(BF)
            dkv[sel, at] = key.astype(BF)
            dkv[sel, pl.ds(pl.multiple_of(D + at.start, 128), 128)] = value.astype(BF)

    each_pair_group(images, body)


def attention_back_columns(images, nk, q, k, v, p, do, dq, dkv):
    def body(image, slots, lanes):
        qs, ks = rows_of(image, NM), rows_of(image, nk)
        d_mixed = [split_pair(do[qs, at]) for at in lanes]
        d_probs = [nt(v[ks, at], one) for one, at in zip(d_mixed, lanes)]
        d_scores = [score_back(p[slot], one, 0) for slot, one in zip(slots, d_probs)]
        d_values = [nn(p[slot], one) for slot, one in zip(slots, d_mixed)]
        d_query = [tn(k[ks, at], one) for one, at in zip(d_scores, lanes)]
        d_keys = [nn(one, split_pair(q[qs, at])) for one, at in zip(d_scores, lanes)]
        for at, value, query, key in zip(lanes, d_values, d_query, d_keys):
            dq[qs, at] = (join_columns(query) * 0.125).astype(BF)
            dkv[ks, at] = key.astype(BF)
            dkv[ks, pl.ds(pl.multiple_of(D + at.start, 128), 128)] = value.astype(BF)

    each_pair_group(images, body)


HALF = 512


def mlp_forward(rows, h2, w1, w2, up_b, u, a, gp, tile, acc, out, base):
    acc[...] = base()
    steps = FF // HALF

    def multiply(t):
        u[t % 2] = nn(h2[...], w1[:, t * HALF : (t + 1) * HALF])

    def add(t):
        acc[...] += nn(tile[t % 2], w2[t * HALF : (t + 1) * HALF, :])

    multiply(0)
    for t in range(steps):
        if t + 1 < steps:
            multiply(t + 1)
        if t > 0:
            add(t - 1)
        for c in range(0, HALF, 256):
            at = slice(t * HALF + c, t * HALF + c + 256)
            shift = up_b[0:1, at].astype(F32)
            for r in range(0, rows, CHUNK):
                sel = slice(r, r + CHUNK)
                value, slope = gelu_pair(u[t % 2, sel, c : c + 256] + shift)
                low = value.astype(BF)
                tile[t % 2, sel, c : c + 256] = low
                if a is not None:
                    a[sel, at] = low
                if gp is not None:
                    gp[sel, at] = slope.astype(BF)
    add(steps - 1)
    out[...] = acc[...].astype(BF)


def mlp_back(rows, dyb, gp, w1, w2, du, u, acc, ready=lambda i, which: None):
    acc[...] = jnp.zeros_like(acc)

    def body(i):
        cols = [pl.ds(pl.multiple_of((2 * i + part) * HALF, HALF), HALF) for part in range(2)]
        ready(i, 0)
        for part in range(2):
            u[part] = nt(dyb[...], w2[cols[part], :])
        ready(i, 1)
        for part in range(2):
            for r in range(0, rows, CHUNK):
                sel = slice(r, r + CHUNK)
                du[sel, cols[part]] = (gp[sel, cols[part]].astype(F32) * u[part, sel, :]).astype(BF)
            acc[...] += nt(du[:, cols[part]], w1[:, cols[part]])

    loop(FF // (2 * HALF), body)


def project(count, rows, left, weight, first, write):
    def body(j):
        write(j, nn(left[...], weight[:, pl.ds(pl.multiple_of((first + j) * D, D), D)]))

    loop(count, body)


def set_biases(ref, bias):
    ref[0] = f32_row(bias, 0)
    ref[1] = jnp.zeros((1, D), F32)
    ref[2] = f32_row(bias, 0, D)


def cost(flops, nbytes):
    return pl.CostEstimate(flops=int(flops), bytes_accessed=int(nbytes), transcendentals=0)


def params(mib):
    return pltpu.CompilerParams(vmem_limit_bytes=mib * MIB)


def struct(shape, dtype=BF):
    return jax.ShapeDtypeStruct(shape, dtype)


def start_weights(copies, sources, scratch):
    return [copies.start(src, dst) for src, dst in zip(sources, scratch)]


def encode_kernel(group, groups, ids, visible, order_in, gains, biases, qvb, upb, rows, cot, wqkv, wo, w1, w2,
                  lat_out, x_out, hq_out, q_out, k_out, v_out, p_out, o_out, y1_out, h2_out, gp_out, a_out, *refs):
    ready, refs = refs[: 4 * groups], refs[4 * groups :]
    (order, rows_v, flat, sqkv, so, s1, s2, x, hq, qkv, p, o, y1, h2, gp, a, u, tile, acc, shifts, lat, sems) = refs
    n = GROUP * NV
    split_orders(order_in, order)

    @pl.when(ids[0] == 0)
    def _():
        copies = Copies(sems)
        got_rows = copies.start(rows.at[0], rows_v)
        got_qkv, got_o, got_1, got_2 = start_weights(
            copies, (wqkv.at[0], wo.at[0], w1.at[0], w2.at[0]), (sqkv, so, s1, s2)
        )
        gain, bias = gains.at[0], biases.at[0]
        set_biases(shifts, qvb)
        copies.wait(got_rows)
        flatten(rows_v, flat)

        def pick_rows(i):
            image = group * GROUP + i
            pick = pick_matrix(order, image, 0, NV, 0, visible[image])
            x[rows_of(i, NV), :] = nn(pick, flat[...]).astype(BF)

        loop(GROUP, pick_rows)
        copies.start(x, x_out)
        norm_rows(x, hq, n, f32_row(gain, 0), f32_row(bias, 0))
        copies.start(hq, hq_out)
        copies.wait(got_qkv)

        def keep(j, value):
            scale = jnp.where(j == 0, 0.125, 1.0)
            qkv[j] = ((value + shifts[j]).astype(BF).astype(F32) * scale).astype(BF)

        project(3, n, hq, sqkv, 0, keep)
        q, k, v = qkv.at[0], qkv.at[1], qkv.at[2]
        copies.start(q, q_out)
        copies.start(k, k_out)
        copies.start(v, v_out)
        attention_by_rows(GROUP, NV, q, k, v, p, o, lambda i: visible[group * GROUP + i])
        copies.start(p, p_out)
        copies.start(o, o_out)
        copies.wait(got_o)
        y1[...] = nn(o[...], so[...]) + f32_row(bias, 1) + x[...].astype(F32)
        copies.start(y1, y1_out)
        norm_rows(y1, h2, n, f32_row(gain, 1), f32_row(bias, 2))
        copies.start(h2, h2_out)
        copies.wait(got_1, got_2)
        mlp_forward(n, h2, s1, s2, upb, u, a, gp, tile, acc, lat, lambda: y1[...] + f32_row(bias, 3))
        copies.start(gp, gp_out)
        copies.start(a, a_out)
        copies.start(lat, lat_out)
        copies.finish()

    if group == groups - 1:

        @pl.when(ids[0] == 1)
        def _():
            copies = Copies(sems)
            m = GROUP * NM
            x_out, hq_out, q_out, dyb_out = (ready[i * groups : (i + 1) * groups] for i in range(4))
            gain, bias = gains.at[0], biases.at[0]
            got_rows = copies.start(rows.at[0], rows_v)
            got_q = copies.start(wqkv.at[0, :, pl.ds(0, D)], so)
            copies.wait(got_rows)
            flatten(rows_v, flat)
            got_cot = copies.start(cot.at[0], rows_v)
            top = pl.ds(0, m)

            def pick_group(g):
                def pick_rows(i):
                    image = g * GROUP + i
                    pick = pick_matrix(order, image, FIRST, NM, visible[image], PATCH)
                    x[rows_of(i, NM), :] = nn(pick, flat[...]).astype(BF)

                loop(GROUP, pick_rows)

            for g in range(groups):
                pick_group(g)
                norm_rows(x, hq, m, f32_row(gain, 0), f32_row(bias, 0))
                sent = [copies.start(x.at[top], x_out[g]), copies.start(hq.at[top], hq_out[g])]
                if g == 0:
                    copies.wait(got_q)
                q = qkv.at[g]
                q[top, :] = ((nn(hq[top, :], so[...]) + f32_row(qvb, 0)).astype(BF) * 0.125).astype(BF)
                copies.start(q.at[top], q_out[g])
                copies.wait(*sent)
            copies.wait(got_cot)
            flatten(rows_v, flat)
            for g in range(groups):
                pick_group(g)
                copies.wait(copies.start(x.at[top], dyb_out[g]))
            copies.finish()


def encode(group, groups, ids, visible, order, gains, biases, qvb, upb, rows, cot, weights):
    n = GROUP * NV
    images = order.shape[0]
    row, wide = struct((n, D)), struct((n, FF))
    heads = struct((GROUP * PAIRS, 2 * NV, NV))
    outs = [row] * 6 + [heads, row, struct((n, D), F32), row, wide, wide] + [struct((GROUP * NM, D))] * (4 * groups)
    vm = lambda s: pltpu.VMEM(s.shape, s.dtype)
    scratch = [
        pltpu.VMEM((images, 1, PATCH), jnp.int32),
        pltpu.VMEM((PATCH, images, D), BF), pltpu.VMEM((PATCH * images, D), BF),
        pltpu.VMEM((D, 3 * D), BF), pltpu.VMEM((D, D), BF), pltpu.VMEM((D, FF), BF), pltpu.VMEM((FF, D), BF),
        vm(row), vm(row), pltpu.VMEM((3, n, D), BF), vm(heads), vm(row), pltpu.VMEM((n, D), F32), vm(row),
        vm(wide), vm(wide), pltpu.VMEM((2, n, HALF), F32), pltpu.VMEM((2, n, HALF), BF), pltpu.VMEM((n, D), F32),
        pltpu.VMEM((3, 1, D), F32), vm(row),
        pltpu.SemaphoreType.DMA((24,)),
    ]
    got = pl.pallas_call(
        partial(encode_kernel, group, groups),
        in_specs=[SMEM, SMEM] + [VMEM] * 5 + [HBM] * 6,
        out_specs=[HBM] * len(outs),
        out_shape=outs,
        scratch_shapes=scratch,
        compiler_params=params(LIMIT),
        cost_estimate=cost(2 * n * 12 * D * D, 25e6),
        name="encode",
    )(ids, visible, order, gains, biases, qvb, upb, rows, cot, *weights)
    ready = got[12:]
    return got[:12], [ready[i * groups : (i + 1) * groups] for i in range(4)]


def block_end(copies, n, got_weights, so, s1, s2, bias, gain, up_b, x, o, y1, h2, a, gp, u, tile, acc, res):
    got_o, got_1, got_2 = got_weights
    copies.wait(got_o)
    y1[...] = nn(o[...], so[...]) + f32_row(bias, 1) + x[...].astype(F32)
    norm_rows(y1, h2, n, f32_row(gain, 1), f32_row(bias, 2))
    copies.wait(got_1, got_2)
    mlp_forward(n, h2, s1, s2, up_b, u, a, gp, tile, acc, res, lambda: y1[...] + f32_row(bias, 3))


def target_kernel(group, ids, visible, order_in, gain, bias, qvb, upb, rows, wqkv, wo, w1, w2, res_out,
                  order, rows_v, flat, sqkv, so, s1, s2, x, hq, qkv, o, y1, h2, u, tile, acc, shifts, res, sems):
    n = GROUP * NM
    q, k, v = qkv.at[0], qkv.at[1], qkv.at[2]

    @pl.when(ids[0] == 0)
    def _():
        copies = Copies(sems)
        split_orders(order_in, order)
        got_rows = copies.start(rows.at[0], rows_v)
        got_qkv = copies.start(wqkv, sqkv)
        got_weights = start_weights(copies, (wo, w1, w2), (so, s1, s2))
        set_biases(shifts, qvb)
        copies.wait(got_rows)
        flatten(rows_v, flat)

        def pick_rows(i):
            image = group * GROUP + i
            pick = pick_matrix(order, image, FIRST, NM, visible[image], PATCH)
            x[rows_of(i, NM), :] = nn(pick, flat[...]).astype(BF)

        loop(GROUP, pick_rows)
        norm_rows(x, hq, n, f32_row(gain, 0), f32_row(bias, 0))
        copies.wait(got_qkv)

        def keep(j, value):
            scale = jnp.where(j == 0, 0.125, 1.0)
            qkv[j] = ((value + shifts[j]).astype(BF).astype(F32) * scale).astype(BF)

        project(3, n, hq, sqkv, 0, keep)

        def key_ok(i):
            return lax.broadcasted_iota(jnp.int32, (NM, 1), 0) + FIRST >= visible[group * GROUP + i]

        attention_by_columns(GROUP, NM, q, k, v, None, o, key_ok)
        block_end(copies, n, got_weights, so, s1, s2, bias, gain, upb, x, o, y1, h2, None, None, u, tile, acc, res)
        copies.start(res, res_out)
        copies.finish()


def target(group, ids, visible, order, vecs, rows, weights):
    n = GROUP * NM
    images = order.shape[0]
    row, full = pltpu.VMEM((n, D), BF), pltpu.VMEM((n, D), F32)
    return pl.pallas_call(
        partial(target_kernel, group),
        in_specs=[SMEM, SMEM] + [VMEM] * 5 + [HBM] * 5,
        out_specs=HBM,
        out_shape=struct((n, D)),
        scratch_shapes=[
            pltpu.VMEM((images, 1, PATCH), jnp.int32),
            pltpu.VMEM((PATCH, images, D), BF), pltpu.VMEM((PATCH * images, D), BF),
            pltpu.VMEM((D, 3 * D), BF), pltpu.VMEM((D, D), BF), pltpu.VMEM((D, FF), BF), pltpu.VMEM((FF, D), BF),
            row, row, pltpu.VMEM((3, n, D), BF), row, full, row,
            pltpu.VMEM((2, n, HALF), F32), pltpu.VMEM((2, n, HALF), BF), full, pltpu.VMEM((3, 1, D), F32), row,
            pltpu.SemaphoreType.DMA((8,)),
        ],
        compiler_params=params(LIMIT),
        cost_estimate=cost(1e6, 1e5),
        name="target",
    )(ids, visible, order, *vecs, rows, *weights)


def regress_kernel(group, ids, visible, gains, biases, qvb, upb, lat_in, x_in, q_in, dyb_in, wqkv, wo, w1, w2,
                   dlat_out, res_out, hk_out, dq_out, dkv_out, o_out, dy1b_out, h2_out, du_out, a_out, dy1_out,
                   sums_out,
                   sqkv, so, s1, s2, x, lat, hk, q, kv, p, o, y1, h2, gp, a, u, tile, acc, shifts,
                   res, dyb, du, dy1, dy1b, do, dq, dkv, dh, dlat, sums, sems):
    n, m = GROUP * NM, GROUP * NV
    k, v = kv.at[0], kv.at[1]

    @pl.when(ids[0] == 1)
    def _():
        copies = Copies(sems)
        gain, bias = gains.at[0], biases.at[0]
        got_lat = copies.start(lat_in, lat)
        got_kv = copies.start(wqkv.at[0, :, pl.ds(D, 2 * D)], sqkv)
        got_q = copies.start(q_in, q)
        got_x = copies.start(x_in, x)
        got_weights = start_weights(copies, (wo.at[0], w1.at[0], w2.at[0]), (so, s1, s2))
        got_dyb = copies.start(dyb_in, dyb)
        set_biases(shifts, qvb)
        copies.wait(got_lat)
        norm_rows(lat, hk, m, f32_row(gain, 0), f32_row(bias, 0))
        copies.start(hk, hk_out)
        copies.wait(got_kv)

        def keep_kv(j, value):
            kv[j] = (value + shifts[j + 1]).astype(BF)

        project(2, m, hk, sqkv, 0, keep_kv)
        copies.wait(got_q, got_x)

        def key_ok(i):
            return lax.broadcasted_iota(jnp.int32, (NV, 1), 0) < visible[group * GROUP + i]

        attention_by_columns(GROUP, NV, q, k, v, p, o, key_ok)
        copies.start(o, o_out)
        block_end(copies, n, got_weights, so, s1, s2, bias, gain, upb, x, o, y1, h2, a, gp, u, tile, acc, res)
        copies.start(res, res_out)
        copies.start(h2, h2_out)
        copies.start(a, a_out)
        copies.wait(got_dyb)
        mlp_back(n, dyb, gp, s1, s2, du, u, acc)
        copies.start(du, du_out)

        def keep(sel, dx):
            dy1[sel, :] = dx
            dy1b[sel, :] = dx.astype(BF)

        g2, b2 = norm_back(y1, acc, dyb, keep, n, f32_row(gain, 1))
        copies.start(dy1, dy1_out)
        copies.start(dy1b, dy1b_out)
        do[...] = nt(dy1b[...], so[...]).astype(BF)
        attention_back_columns(GROUP, NV, q, k, v, p, do, dq, dkv)
        copies.start(dq, dq_out)
        copies.start(dkv, dkv_out)
        dh[...] = nt(dkv[:, :D], sqkv[:, :D])
        dh[...] += nt(dkv[:, D:], sqkv[:, D:])

        def keep_side(sel, dx):
            dlat[sel, :] = dx.astype(BF)

        gk, bk = norm_back(lat, dh, None, keep_side, m, f32_row(gain, 0))
        copies.start(dlat, dlat_out)
        for row, value in enumerate((gk, g2, bk, b2)):
            sums[pl.ds(row, 1), :] = value
        copies.start(sums, sums_out)
        copies.finish()


def regress(group, ids, visible, vecs, lat, x, q, dyb, weights):
    n, m = GROUP * NM, GROUP * NV
    row, side, wide = struct((n, D)), struct((m, D)), struct((n, FF))
    pair = struct((m, 2 * D))
    outs = [side, row, side, row, pair, row, row, row, wide, wide, struct((n, D), F32), struct((8, D), F32)]
    vm = lambda s: pltpu.VMEM(s.shape, s.dtype)
    full, fside = pltpu.VMEM((n, D), F32), pltpu.VMEM((m, D), F32)
    scratch = [
        pltpu.VMEM((D, 2 * D), BF), pltpu.VMEM((D, D), BF), pltpu.VMEM((D, FF), BF), pltpu.VMEM((FF, D), BF),
        vm(row), vm(side), vm(side), vm(row), pltpu.VMEM((2, m, D), BF),
        pltpu.VMEM((GROUP * PAIRS, NV, 2 * NM), BF), vm(row), full, vm(row), vm(wide), vm(wide),
        pltpu.VMEM((2, n, HALF), F32), pltpu.VMEM((2, n, HALF), BF), full, pltpu.VMEM((3, 1, D), F32),
        vm(row), vm(row), vm(wide), full, vm(row), vm(row), vm(row), vm(pair), fside, vm(side),
        pltpu.VMEM((8, D), F32),
        pltpu.SemaphoreType.DMA((24,)),
    ]
    return pl.pallas_call(
        partial(regress_kernel, group),
        in_specs=[SMEM, SMEM] + [VMEM] * 4 + [HBM] * 8,
        out_specs=[HBM] * len(outs),
        out_shape=outs,
        scratch_shapes=scratch,
        compiler_params=params(LIMIT),
        cost_estimate=cost(4 * n * 12 * D * D, 25e6),
        name="regress",
    )(ids, visible, *vecs, lat, x, q, dyb, *weights)


def stack_rows(copies, pieces, ref, size):
    return [copies.start(piece, ref.at[pl.ds(i * size, size)]) for i, piece in enumerate(pieces)]


def clear_tail(ref, used):
    ref[pl.ds(used, ref.shape[0] - used), :] = jnp.zeros((ref.shape[0] - used, ref.shape[1]), ref.dtype)


def halves(count, blocks):
    rows = D // 16
    if count == 16:
        return [struct((2, 2, 2, blocks, rows, D))] + [struct((2, blocks, rows, D))] * 4
    return [struct((D, D))] * blocks


def give_blocks(copies, core, tree, left_right, out, dest):
    size = 8 if tree else 1
    blocks = out.shape[0]
    first = copies.take(blocks * size)

    def send(j, act):
        if not tree:
            for block in range(blocks):
                pl.when(j == block)(lambda block=block: act(out.at[block], dest[block], first + block))
            return
        view = out.at[j].reshape(2, 2, 2, 2, D // 16, D)
        for x in range(2):
            for low in range(2):
                at = first + j * size + 4 * x + 2 * low
                act(view.at[:, low, x, core], dest[0].at[x, low, :, j], at)
                act(view.at[:, low, x, 1 - core], dest[1 + 2 * x + low].at[:, j], at + 1)

    def body(j):
        out[j] = left_right(j)
        send(j, copies.begin)

    loop(blocks, body)
    loop(blocks, lambda j: send(j, copies.wait_at))


def give_rows(copies, core, tree, multiply, out, dest):
    size = 4 if tree else 1
    first = copies.take(4 * size)

    def send(j, act):
        if not tree:
            act(out.at[j], dest[0].at[pl.ds(pl.multiple_of(j * D, D), D)], first + j)
            return
        view = out.at[j].reshape(2, 2, D // 4, D)
        low, high = lax.rem(j, 2), lax.div(j, 2)
        for x in range(2):
            at = first + j * size + 2 * x
            act(view.at[x, core], dest[0].at[x, low, high, 0], at)
            act(view.at[x, 1 - core], dest[1].at[x, low, high, 0], at + 1)

    def body(j):
        out[j] = multiply(j)
        send(j, copies.begin)

    loop(4, body)
    loop(4, lambda j: send(j, copies.wait_at))


def down_kernel(groups, parts, ids, *refs):
    cot, lat, a_enc, a_reg, dyb_reg = (refs[i * groups : (i + 1) * groups] for i in range(5))
    refs = refs[5 * groups :]
    dest, refs = refs[:parts], refs[parts:]
    sums_out, cot_v, dyb, a, dlat, out, sums, sems = refs
    images = groups * GROUP
    nv, nm = GROUP * NV, GROUP * NM

    @pl.when(ids[0] == 0)
    def _():
        copies = Copies(sems)
        got = stack_rows(copies, cot, cot_v, nv) + stack_rows(copies, lat, dlat, nv)
        stack_rows(copies, a_enc, a, nv)
        copies.wait(*got)
        dyb[...] = (cot_v[...].astype(F32) + dlat[...].astype(F32)).astype(BF)
        copies.finish()

    @pl.when(ids[0] == 1)
    def _():
        copies = Copies(sems)
        stack_rows(copies, a_reg, a, nm)
        stack_rows(copies, dyb_reg, dyb, nm)
        clear_tail(a, images * NM)
        clear_tail(dyb, images * NM)
        copies.finish()

    copies = Copies(sems)

    def multiply(j):
        return tn(a[:, pl.ds(pl.multiple_of(j * D, D), D)], dyb[...]).astype(BF)

    give_rows(copies, ids[1], parts == 2, multiply, out, dest)
    sums[...] = jnp.broadcast_to(column_sum(dyb, images * NV), (8, D))
    copies.start(sums, sums_out)
    copies.finish()


def down_grad(groups, count, ids, cot, dlat, a_enc, a_reg, dyb_reg):
    n = groups * GROUP * NV
    main = [struct((2, 2, 2, 1, D // 4, D))] * 2 if count == 16 else [struct((FF, D))]
    outs = main + [struct((8, D), F32)]
    row = pltpu.VMEM((n, D), BF)
    scratch = [
        row, row, pltpu.VMEM((n, FF), BF), row, pltpu.VMEM((4, D, D), BF), pltpu.VMEM((8, D), F32),
        pltpu.SemaphoreType.DMA((24,)),
    ]
    got = pl.pallas_call(
        partial(down_kernel, groups, len(main)),
        in_specs=[SMEM] + [HBM] * (5 * groups),
        out_specs=[HBM] * len(outs),
        out_shape=outs,
        scratch_shapes=scratch,
        compiler_params=params(LIMIT),
        cost_estimate=cost(1e6, 1e5),
        name="down_grad",
    )(ids, *cot, *dlat, *a_enc, *a_reg, *dyb_reg)
    return got[: len(main)], got[-1]


def mlp_kernel(first, groups, ids, visible, order_in, gains, cot, dlat_in, w1, w2, y1_in, gp_in, *refs):
    if first:
        picked, refs = refs[:groups], refs[groups:]
    du_out, dy1_out, dy1b_out, sums_out, order, rows_v, flat, refs = *refs[:7], refs[7:]
    s1, s2, cot_v, dlat, dyb, gp, y1, du, u, acc, dy1, dy1b, sums, sems = refs
    n = GROUP * NV
    third = FF // 3

    @pl.when(ids[0] == 0)
    def _():
        copies = Copies(sems)
        got = [copies.start(dlat_in, dlat)]
        if first:
            got_rows = copies.start(cot.at[0], rows_v)
        else:
            got.append(copies.start(cot, cot_v))
        start = copies.take(9)

        def parts(i):
            cols = pl.ds(pl.multiple_of(i * third, third), third)
            return (
                (w2.at[0, cols, :], s2.at[cols, :]),
                (gp_in.at[:, cols], gp.at[:, cols]),
                (w1.at[0, :, cols], s1.at[:, cols]),
            )

        for i in range(3):
            for k, (src, dst) in enumerate(parts(i)):
                copies.begin(src, dst, start + 3 * i + k)
        got_y = copies.start(y1_in, y1)

        def ready(i, which):
            for k in ((0, 1), (2,))[which]:
                copies.wait_at(*parts(i)[k], start + 3 * i + k)

        if first:
            split_orders(order_in, order)
            copies.wait(got_rows)
            flatten(rows_v, flat)
            for g in reversed(range(groups)):

                def pick_rows(i, g=g):
                    image = g * GROUP + i
                    pick = pick_matrix(order, image, 0, NV, 0, visible[image])
                    cot_v[rows_of(i, NV), :] = nn(pick, flat[...]).astype(BF)

                loop(GROUP, pick_rows)
                copies.wait(copies.start(cot_v, picked[g]))
        copies.wait(*got)
        dyb[...] = (cot_v[...].astype(F32) + dlat[...].astype(F32)).astype(BF)
        mlp_back(n, dyb, gp, s1, s2, du, u, acc, ready)
        copies.start(du, du_out)
        copies.wait(got_y)

        def keep(sel, dx):
            dy1[sel, :] = dx
            dy1b[sel, :] = dx.astype(BF)

        g2, b2 = norm_back(y1, acc, dyb, keep, n, f32_row(gains.at[0], 1))
        copies.start(dy1, dy1_out)
        copies.start(dy1b, dy1b_out)
        sums[pl.ds(0, 1), :] = g2
        sums[pl.ds(1, 1), :] = b2
        copies.start(sums, sums_out)
        copies.finish()


def mlp_grad(first, groups, ids, visible, order, gains, cot, dlat, w1, w2, y1, gp):
    n = GROUP * NV
    images = order.shape[0]
    row, wide, full = pltpu.VMEM((n, D), BF), pltpu.VMEM((n, FF), BF), pltpu.VMEM((n, D), F32)
    outs = [struct((n, D))] * (groups if first else 0) + [struct((n, FF)), struct((n, D), F32), struct((n, D)), struct((8, D), F32)]
    got = pl.pallas_call(
        partial(mlp_kernel, first, groups),
        in_specs=[SMEM, SMEM, VMEM, VMEM] + [HBM] * 6,
        out_specs=[HBM] * len(outs),
        out_shape=outs,
        scratch_shapes=[
            pltpu.VMEM((images, 1, PATCH), jnp.int32),
            pltpu.VMEM((PATCH, images, D), BF), pltpu.VMEM((PATCH * images, D), BF),
            pltpu.VMEM((D, FF), BF), pltpu.VMEM((FF, D), BF), row, row, row, wide, full, wide,
            pltpu.VMEM((2, n, HALF), F32), full, full, row, pltpu.VMEM((8, D), F32), pltpu.SemaphoreType.DMA((24,)),
        ],
        compiler_params=params(LIMIT),
        cost_estimate=cost(1e6, 1e5),
        name="mlp_grad",
    )(ids, visible, order, gains, cot, dlat, w1, w2, y1, gp)
    return got[:-4], got[-4:]


def up_kernel(groups, parts, ids, *refs):
    pieces = [refs[i * groups : (i + 1) * groups] for i in range(8)]
    refs = refs[8 * groups :]
    dest, refs = refs[:parts], refs[parts:]
    sums_out, left, right, out, sums, sems = refs
    images = groups * GROUP

    def load(du, h2, dy1b, o, size):
        copies = Copies(sems)
        stack_rows(copies, h2, left.at[0], size)
        for j in range(4):
            stack_rows(copies, [one.at[:, pl.ds(j * D, D)] for one in du], right.at[j], size)
        stack_rows(copies, o, left.at[1], size)
        stack_rows(copies, dy1b, right.at[4], size)
        return copies

    @pl.when(ids[0] == 0)
    def _():
        load(*pieces[:4], GROUP * NV).finish()

    @pl.when(ids[0] == 1)
    def _():
        copies = load(*pieces[4:], GROUP * NM)
        for ref in (left, right):
            for i in range(ref.shape[0]):
                clear_tail(ref.at[i], images * NM)
        copies.finish()

    copies = Copies(sems)

    def multiply(j):
        value = tn(left[lax.div(j, 4)], right[j]).astype(BF)
        sums[pl.ds(j, 1), :] = column_sum(right.at[j], images * NV)
        return value

    give_blocks(copies, ids[1], dest[0].ndim == 6, multiply, out, dest)
    copies.start(sums, sums_out)
    copies.finish()


def up_grad(groups, count, ids, *pieces):
    n = groups * GROUP * NV
    main = halves(count, 5)
    outs = main + [struct((8, D), F32)]
    got = pl.pallas_call(
        partial(up_kernel, groups, len(main)),
        in_specs=[SMEM] + [HBM] * (8 * groups),
        out_specs=[HBM] * len(outs),
        out_shape=outs,
        scratch_shapes=[
            pltpu.VMEM((2, n, D), BF), pltpu.VMEM((5, n, D), BF), pltpu.VMEM((5, D, D), BF), pltpu.VMEM((8, D), F32),
            pltpu.SemaphoreType.DMA((44,)),
        ],
        compiler_params=params(LIMIT),
        cost_estimate=cost(1e6, 1e5),
        name="up_grad",
    )(ids, *[ref for piece in pieces for ref in piece])
    return got[: len(main)], got[-1]


def attn_kernel(groups, last, ids, gains, *refs):
    if last:
        down_sums, up_sums, refs = refs[0], refs[1], refs[2:]
        mlp_sums, reg_sums = (refs[i * groups : (i + 1) * groups] for i in range(2))
        before, refs = refs[2 * groups : 3 * groups - 1], refs[3 * groups - 1 :]
    (wqkv, wo, dy1_enc, q_in, k_in, v_in, p_in, x_enc, dq_reg, dkv_reg, dy1_reg, x_reg,
     dq_out, dkv_out, dx_out, sums_out,
     sqkv, so, dy1, dy1b, q, k, v, p, x, do, dq, dkv, dh, sems) = refs
    m = GROUP * NM
    top = pl.ds(0, m)
    gain = f32_row(gains.at[0], 0)

    def finish(copies, rows):
        def keep(sel, dx):
            dy1[sel, :] = dx

        own = (*norm_back(x, dh, dy1, keep, rows, gain), column_sum(dq, rows), column_sum(dkv, GROUP * NV, D))
        copies.start(dy1, dx_out)
        if not last:
            for row, value in enumerate(own):
                sums_out[row : row + 1, :] = value
            copies.finish()
            return

        def total_of(sums):
            total = sums[0][...]
            for more in sums[1:]:
                total = total + more[...]
            return total

        done, mlp, reg = total_of(before), total_of(mlp_sums), total_of(reg_sums)
        g1, b1, queries, values = (one + done[row : row + 1, :] for row, one in enumerate(own))
        encoder = ids[0] == 0
        sums_out[0:1, :] = g1 + jnp.where(encoder, 0.0, reg[0:1, :])
        sums_out[1:2, :] = jnp.where(encoder, mlp[0:1, :], reg[1:2, :])
        sums_out[2:3, :] = b1 + jnp.where(encoder, 0.0, reg[2:3, :])
        sums_out[3:4, :] = up_sums[4:5, :]
        sums_out[4:5, :] = jnp.where(encoder, mlp[1:2, :], reg[3:4, :])
        sums_out[5:6, :] = down_sums[0:1, :]
        sums_out[6:7, :] = queries
        sums_out[7:8, :] = values
        sums_out[8:12, :] = up_sums[0:4, :]
        sums_out[12:16, :] = jnp.zeros((4, D), F32)
        copies.finish()

    @pl.when(ids[0] == 0)
    def _():
        copies = Copies(sems)
        got = [copies.start(dy1_enc, dy1), copies.start(wo.at[0], so)]
        later = [copies.start(src, dst) for src, dst in ((v_in, v), (p_in, p), (k_in, k), (q_in, q))]
        final = [copies.start(wqkv.at[0], sqkv), copies.start(x_enc, x)]
        copies.wait(*got)
        dy1b[...] = dy1[...].astype(BF)
        do[...] = nt(dy1b[...], so[...]).astype(BF)
        copies.wait(*later)
        attention_back_rows(GROUP, NV, q, k, v, p, do, dq, dkv)
        copies.start(dq, dq_out)
        copies.start(dkv, dkv_out)
        copies.wait(*final)
        dh[...] = nt(dq[...], sqkv[:, 0:D])
        for j in range(2):
            dh[...] += nt(dkv[:, j * D : (j + 1) * D], sqkv[:, (j + 1) * D : (j + 2) * D])
        finish(copies, GROUP * NV)

    @pl.when(ids[0] == 1)
    def _():
        copies = Copies(sems)
        for src, dst in ((dq_reg, dq), (dy1_reg, dy1), (x_reg, x)):
            copies.start(src, dst.at[top])
        copies.start(dkv_reg, dkv)
        copies.start(wqkv.at[0, :, pl.ds(0, D)], sqkv.at[:, pl.ds(0, D)])
        copies.finish()
        dh[top, :] = nt(dq[top, :], sqkv[:, 0:D])
        finish(copies, m)


def attn_back(groups, last, ids, gains, sums, *pieces):
    n = GROUP * NV
    row, full = pltpu.VMEM((n, D), BF), pltpu.VMEM((n, D), F32)
    outs = [struct((n, D)), struct((n, 2 * D)), struct((n, D), F32), struct((16, D), F32)]
    return pl.pallas_call(
        partial(attn_kernel, groups, last),
        in_specs=[SMEM, VMEM] + [VMEM] * len(sums) + [HBM] * len(pieces),
        out_specs=[HBM] * 3 + [VMEM],
        out_shape=outs,
        scratch_shapes=[
            pltpu.VMEM((D, 3 * D), BF), pltpu.VMEM((D, D), BF), full, row, row, row, row,
            pltpu.VMEM((GROUP * PAIRS, 2 * NV, NV), BF), row, row, row, pltpu.VMEM((n, 2 * D), BF), full,
            pltpu.SemaphoreType.DMA((20,)),
        ],
        compiler_params=params(LIMIT),
        cost_estimate=cost(1e6, 1e5),
        name="attn_back",
    )(ids, gains, *sums, *pieces)


def qkv_kernel(groups, parts, ids, *refs):
    pieces = [refs[i * groups : (i + 1) * groups] for i in range(7)]
    dq_enc, dkv_enc, hq_enc, hq_reg, hk_reg, dq_reg, dkv_reg = pieces
    refs = refs[7 * groups :]
    dest, refs = refs[:parts], refs[parts:]
    left, right, out, sems = refs
    images = groups * GROUP
    nv, nm = GROUP * NV, GROUP * NM
    hk, hq = left.at[0], left.at[1]
    dk, dv, dq = (right.at[i] for i in range(3))

    @pl.when(ids[0] == 0)
    def _():
        copies = Copies(sems)
        stack_rows(copies, hq_enc, hk, nv)
        stack_rows(copies, [one.at[:, pl.ds(0, D)] for one in dkv_enc], dk, nv)
        stack_rows(copies, [one.at[:, pl.ds(D, D)] for one in dkv_enc], dv, nv)
        stack_rows(copies, hq_enc, hq, nv)
        stack_rows(copies, dq_enc, dq, nv)
        copies.finish()

    @pl.when(ids[0] == 1)
    def _():
        copies = Copies(sems)
        for piece, ref in ((hq_reg, hq), (dq_reg, dq)):
            stack_rows(copies, piece, ref, nm)
            clear_tail(ref, images * NM)
        stack_rows(copies, hk_reg, hk, nv)
        stack_rows(copies, [one.at[:, pl.ds(0, D)] for one in dkv_reg], dk, nv)
        stack_rows(copies, [one.at[:, pl.ds(D, D)] for one in dkv_reg], dv, nv)
        copies.finish()

    copies = Copies(sems)

    def multiply(j):
        return tn(left[lax.div(j, 2)], right[j]).astype(BF)

    give_blocks(copies, ids[1], dest[0].ndim == 6, multiply, out, dest)


def qkv_grad(groups, count, ids, *pieces):
    n = groups * GROUP * NV
    row = pltpu.VMEM((n, D), BF)
    main = halves(count, 3)
    scratch = [
        pltpu.VMEM((2, n, D), BF), pltpu.VMEM((3, n, D), BF), pltpu.VMEM((3, D, D), BF),
        pltpu.SemaphoreType.DMA((40,)),
    ]
    return pl.pallas_call(
        partial(qkv_kernel, groups, len(main)),
        in_specs=[SMEM] + [HBM] * (7 * groups),
        out_specs=[HBM] * len(main),
        out_shape=main,
        scratch_shapes=scratch,
        compiler_params=params(LIMIT),
        cost_estimate=cost(1e6, 1e5),
        name="qkv_grad",
    )(ids, *[ref for piece in pieces for ref in piece])


def place_kernel(groups, ids, visible, order_in, *refs):
    dx_in, lat_enc, res_enc, res_reg = (refs[i * groups : (i + 1) * groups] for i in range(4))
    block_out, grad_out, order, dx, lat, out, grads, sems = refs[4 * groups :]
    images = groups * GROUP
    nv, nm = GROUP * NV, GROUP * NM
    split_orders(order_in, order)

    def put_grad(i, put, value):
        high = value.astype(BF)
        low = (value - high.astype(F32)).astype(BF)
        grads[i] = nn(put, high) + nn(put, low)

    def write_grads():
        copies = Copies(sems)
        for i in range(images):
            copies.start(grads.at[i], grad_out.at[0, :, i, :])
        copies.finish()

    @pl.when(ids[0] == 0)
    def _():
        copies = Copies(sems)
        for piece, ref, size in ((dx_in, dx, nv), (lat_enc, lat, nv), (res_enc, out, nm)):
            stack_rows(copies, piece, ref, size)
        copies.finish()

        def put_image(i):
            put = place_matrix(order, i, 0, NV, 0, visible[i])
            put_side = place_matrix(order, i, FIRST, NM, visible[i], PATCH)
            put_grad(i, put, dx[rows_of(i, NV), :])
            block_out[0, i] = (nn(put, lat[rows_of(i, NV), :]) + nn(put_side, out[rows_of(i, NM), :])).astype(BF)

        loop(images, put_image)
        write_grads()

    @pl.when(ids[0] == 1)
    def _():
        copies = Copies(sems)
        stack_rows(copies, res_reg, out, nm)
        stack_rows(copies, [piece.at[pl.ds(0, nm)] for piece in dx_in], dx, nm)
        copies.finish()

        def put_image(i):
            put = place_matrix(order, i, FIRST, NM, visible[i], PATCH)
            put_grad(i, put, dx[rows_of(i, NM), :])
            block_out[0, i] = nn(put, out[rows_of(i, NM), :]).astype(BF)

        loop(images, put_image)
        write_grads()


def place(groups, ids, visible, order, *pieces):
    images = groups * GROUP
    n = images * NV
    outs = [struct((1, images, PATCH, D)), struct((1, PATCH, images, D), F32)]
    return pl.pallas_call(
        partial(place_kernel, groups),
        in_specs=[SMEM, SMEM, VMEM] + [HBM] * (4 * groups),
        out_specs=[VMEM, HBM],
        out_shape=outs,
        scratch_shapes=[
            pltpu.VMEM((images, 1, PATCH), jnp.int32), pltpu.VMEM((n, D), F32), pltpu.VMEM((n, D), BF),
            pltpu.VMEM((images * NM, D), BF), pltpu.VMEM((images, PATCH, D), F32), pltpu.SemaphoreType.DMA((8,)),
        ],
        compiler_params=params(LIMIT),
        cost_estimate=cost(1e6, 1e5),
        name="place",
    )(ids, visible, order, *[ref for piece in pieces for ref in piece])


BITS = (2, 4, 8)


def hop(value, bit):
    return lax.ppermute(value, "dp", [(i, i ^ bit) for i in range(16)])


def combine_kernel(jobs, given, ids, *refs):
    used = sum(sum(4 if gone is None else 1 for gone in terms) for terms, *_ in jobs)
    inputs, outs, scratch = list(refs[:used]), list(refs[used : used + given]), list(refs[used + given :])
    copies = Copies(scratch.pop())
    plans = []

    def fetch(term, gone, bits, own):
        if gone is not None:
            path = tuple(bits[gone:])
            copy = copies.start(term.at[path] if path else term, own)
            return lambda: copies.wait(copy)
        wide = len(bits) == 1
        first = copies.take(2 if wide else 1)
        rest = tuple(bits[2:])

        def piece(x, low):
            ref = term[2 * x + low]
            return ref.at[rest] if rest else ref

        for x in range(2):
            for low in range(2):
                if wide:
                    pl.when(bits[0] == x)(
                        lambda x=x, low=low: copies.begin(piece(x, low), own.at[low], first + low)
                    )
                else:
                    pl.when((bits[0] == x) & (bits[1] == low))(
                        lambda x=x, low=low: copies.begin(piece(x, low), own, first)
                    )

        def wait():
            if wide:
                for low in range(2):
                    copies.wait_at(piece(0, low), own.at[low], first + low)
            else:
                copies.wait_at(piece(0, 0), own, first)

        return wait

    for kinds, first, last, targets, finals in jobs:
        terms = [inputs.pop(0) if gone is not None else [inputs.pop(0) for _ in range(4)] for gone in kinds]
        for target in targets:
            bits = []
            for bit in range(last):
                flip = bit >= first and (target >> (bit - first)) & 1
                bits.append(1 - ids[2 + bit] if flip else ids[2 + bit])
            owns = [scratch.pop(0) for _ in kinds]
            waits = [fetch(term, gone, bits, own) for term, gone, own in zip(terms, kinds, owns)]
            plans.append((waits, owns, last, finals, None if finals else outs.pop(0)))
    for waits, owns, last, finals, out in plans:
        for wait in waits:
            wait()
        spots = [()]
        for _ in range(3 - last):
            spots = [spot + (i,) for spot in spots for i in range(2)]
        for spot in spots:
            for j in range(owns[0].shape[-3]):
                value = owns[0][spot + (j,)].astype(F32)
                for more in owns[1:]:
                    value = value + more[spot + (j,)].astype(F32)
                if finals:
                    which, column = finals[j]
                    outs[which][:, column * D : (column + 1) * D] = value
                else:
                    out[spot + (j,)] = value.astype(BF)


def send_job(terms, first, last, targets=(1,)):
    return terms, first, last, targets, None


def final_job(terms, finals):
    return terms, 0, 3, (0,), finals


def combine(ids, *jobs, outs=()):
    shapes = [struct(shape, F32) for shape in outs]
    plans, inputs, scratch = [], [], []
    for terms, first, last, targets, finals in jobs:
        blocks, rows = terms[0].shape[-3:-1]
        kinds = tuple(None if isinstance(term, list) else 6 - term.ndim for term in terms)
        for term in terms:
            inputs += term if isinstance(term, list) else [term]
        plans.append((kinds, first, last, targets, finals))
        part = (2,) * (3 - last) + (blocks, rows, D)
        for _ in targets:
            scratch += [pltpu.VMEM(part, BF) for _ in terms]
            if finals is None:
                shapes.append(struct(part))
    scratch.append(pltpu.SemaphoreType.DMA((2 * len(scratch),)))
    return pl.pallas_call(
        partial(combine_kernel, tuple(plans), len(shapes)),
        in_specs=[SMEM] + [HBM] * len(inputs),
        out_specs=[VMEM] * len(shapes),
        out_shape=shapes,
        scratch_shapes=scratch,
        compiler_params=params(LIMIT),
        cost_estimate=cost(1e5, 1e4),
        name="combine",
    )(ids, *inputs)


def in_order(first, then):
    return lax.optimization_barrier((first, then))


def own_columns(rows, count):
    own = D // count
    me = lax.axis_index("dp")

    def part(block, wide):
        return lax.dynamic_slice_in_dim(block, me * wide, wide, block.ndim - 1)

    return (
        part(rows[:2], own),
        part(rows[2:6], own),
        part(rows[6:8].reshape(-1), 2 * own),
        part(rows[8:12].reshape(-1), 4 * own),
    )


def scatter_natural(block):
    shards = block.reshape(lax.axis_size("dp"), -1, D)
    return lax.psum_scatter(shards, "dp", scatter_dimension=0, tiled=True)[0].astype(F32)


def local(
    patch_rows, cotangent, patch_order, visible, qkv_weight, out_weight, up_weight, down_weight, norm_gains, biases,
    qv_bias, up_bias, target_qkv, target_out, target_up, target_down, target_gains, target_biases, target_qv_bias,
    target_up_bias,
):
    count = lax.axis_size("dp")
    tree = count == 16
    place_dp = lax.axis_index("dp")
    bits = [(place_dp // bit) % 2 for bit in (1,) + BITS]
    ids = jnp.stack([lax.axis_index("section")] + bits).astype(jnp.int32)
    groups = patch_order.shape[0] // GROUP
    weights = (qkv_weight, out_weight, up_weight, down_weight)
    targets = (target_qkv, target_out, target_up, target_down)
    vecs = (norm_gains, biases, qv_bias, up_bias)
    target_vecs = (target_gains, target_biases, target_qv_bias[None], target_up_bias[None])

    rows, cot = patch_rows.transpose(0, 2, 1, 3), cotangent.transpose(0, 2, 1, 3)
    calls = [
        encode(g, groups, ids, visible, patch_order, *vecs, rows, cot, weights) for g in range(groups)
    ]
    lat, x_e, hq_e, q_e, k_e, v_e, p_e, o_e, y1_e, h2_e, gp_e, a_e = zip(*[call[0] for call in calls])
    x_r, hq_r, q_r, dyb_r = calls[-1][1]
    sent = [lax.ppermute(piece, "section", [(0, 1)]) for piece in lat]
    vectors = (norm_gains, biases, qv_bias, up_bias)
    regressed = [regress(0, ids, visible, vectors, sent[0], x_r[0], q_r[0], dyb_r[0], weights)]
    back = [lax.ppermute(regressed[0][0], "section", [(1, 0)])]
    order_first, regressed[0] = in_order(patch_order, regressed[0])
    res_e = [target(0, ids, visible, order_first, target_vecs, rows, targets)]
    res_e[0], sent[1:] = in_order(res_e[0], sent[1:])
    for g in range(1, groups):
        regressed.append(regress(g, ids, visible, vectors, sent[g], x_r[g], q_r[g], dyb_r[g], weights))
        back.append(lax.ppermute(regressed[g][0], "section", [(1, 0)]))
    _, res_r, hk_r, dq_r, dkv_r, o_r, dy1b_r, h2_r, du_r, a_r, dy1_r, sums_r = zip(*regressed)

    def mlp(g, cot):
        return mlp_grad(
            g == 0, groups, ids, visible, patch_order, norm_gains, cot, back[g], up_weight, down_weight, y1_e[g], gp_e[g]
        )

    def attention(g, dy1, sums=()):
        return attn_back(
            groups, len(sums) > 0, ids, norm_gains, sums, qkv_weight, out_weight, dy1, q_e[g], k_e[g], v_e[g], p_e[g],
            x_e[g], dq_r[g], dkv_r[g], dy1_r[g], x_r[g],
        )

    cot_e, first = mlp(0, cot)
    mlps = [first] + [mlp(g, cot_e[g])[1] for g in range(1, groups - 1)]
    attns = [attention(g, mlps[g][1]) for g in range(groups - 1)]
    last = groups - 1
    send = partial(combine, ids)
    attns, back[last] = in_order(attns, back[last])
    down, sums_down = down_grad(groups, count, ids, cot_e, back, a_e, a_r, dyb_r)
    cot_last = cot_e[last]
    down, cot_last = in_order(down, cot_last)
    mlps.append(mlp(last, cot_last)[1])
    du_e, dy1_e, dy1b_e, sums_e = (list(piece) for piece in zip(*mlps))
    if tree:
        downs = [down[0], hop(down[1], 1)]
        (down_x,), du_e[last] = in_order(send(send_job(downs, 0, 1)), du_e[last])
        downs = downs + [hop(down_x, 2)]
    up, sums_up = up_grad(groups, count, ids, du_e, h2_e, dy1b_e, o_e, du_r, h2_r, dy1b_r, o_r)
    if tree:
        peers = (3, 2, 1)
        ups = [up[0], [hop(piece, 1) for piece in up[1:]]]
        (up_x,), downs = in_order(send(send_job(ups, 0, 1)), downs)
        ups = ups + [hop(up_x, 2)]
        down_z, dy1_e[last] = in_order(send(send_job(downs, 1, 3, peers)), dy1_e[last])
        down_got = [hop(one, 4 * peer) for one, peer in zip(down_z, peers)]
    sums_in = [piece[3] for piece in attns]
    attns.append(attention(last, dy1_e[last], (sums_down, sums_up, *sums_e, *sums_r, *sums_in)))
    dq_e, dkv_e, dx, small = (list(piece) for piece in zip(*attns))
    small = small[last]
    order_late = patch_order
    if tree:
        small = small + hop(small, 1)
        small, dq_e[last] = in_order(small, dq_e[last])
    attn = qkv_grad(groups, count, ids, dq_e, dkv_e, hq_e, hq_r, hk_r, dq_r, dkv_r)
    if tree:
        down_got, attn = in_order(down_got, attn)
        pieces = [hop(piece, 1) for piece in attn[1:]]
        pieces, small = in_order(pieces, small)
        qkvs = [attn[0], pieces]
        got = hop(small, 2)
        up_z, (qkvs, got) = in_order(send(send_job(ups, 1, 3, peers)), (qkvs, got))
        small = small + got
        up_got = [hop(one, 4 * peer) for one, peer in zip(up_z, peers)]
        (qkv_x,), got = in_order(send(send_job(qkvs, 0, 1)), hop(small, 4))
        small = small + got
        order_late, qkv_x = in_order(patch_order, qkv_x)
        qkvs = qkvs + [hop(qkv_x, 2)]
        got = hop(small, 8)
    res_e += [target(g, ids, visible, order_late, target_vecs, rows, targets) for g in range(1, groups)]
    if tree:
        qkv_z, res_e = in_order(send(send_job(qkvs, 1, 3, peers)), res_e)
        qkv_got = [hop(one, 4 * peer) for one, peer in zip(qkv_z, peers)]
    block_out, grad_rows = place(groups, ids, visible, patch_order, dx, lat, res_e, res_r)
    if tree:
        small = small + got
        (block_out, grad_rows), up_got = in_order((block_out, grad_rows), up_got)
        down_sum, up_sum, out_sum = send(
            final_job(downs + down_got, ((0, 0),)),
            final_job(ups + up_got, tuple((1, j) for j in range(4)) + ((2, 0),)),
            outs=((D // 4, D), (D // 16, 4 * D), (D // 16, D)),
        )
        qkv_got, (down_sum, up_sum, out_sum) = in_order(qkv_got, (down_sum, up_sum, out_sum))
        (qkv_sum,) = send(final_job(qkvs + qkv_got, ((0, 1), (0, 2), (0, 0))), outs=((D // 16, 3 * D),))
    else:
        down_sum = scatter_natural(down[0])
        up_sum = jnp.concatenate([scatter_natural(one) for one in up[:4]], axis=1)
        out_sum = scatter_natural(up[4])
        qkv_sum = jnp.concatenate([scatter_natural(attn[i]) for i in (2, 0, 1)], axis=1)
        small = lax.psum(small, "dp")
    grad_rows = grad_rows.transpose(0, 2, 1, 3)
    gains, bias_rows, qv_rows, up_rows = own_columns(small, count)
    return (
        block_out,
        grad_rows,
        qkv_sum[None],
        out_sum[None],
        up_sum[None],
        down_sum[None],
        gains[None],
        bias_rows[None],
        qv_rows[None],
        up_rows[None],
    )


def solution(mesh):
    three, four = P("section", None, None), P("section", "dp", None, None)
    grad = P("section", "dp", None)
    return jax.shard_map(
        local,
        mesh=mesh,
        in_specs=(four, four, P("dp", None), P("dp"), three, three, three, three, three, three,
                  P("section", None), P("section", None), P(), P(), P(), P(), P(), P(), P(), P()),
        out_specs=(four, four, grad, grad, grad, grad, P("section", None, "dp"), P("section", None, "dp"),
                   P("section", "dp"), P("section", "dp")),
        check_vma=False,
    )
```

```python
from functools import partial

import jax
import jax.numpy as jnp
from jax import lax
from jax.experimental import pallas as pl
from jax.experimental.pallas import tpu as pltpu
from jax.sharding import PartitionSpec as P

HEADS = 12
PATCH = 196
D = 768
FF = 3072
EPS = 1e-06
NV = 144
NM = 128
FIRST = PATCH - NM
GROUP = 2
CHUNK = 32

BF = jnp.bfloat16
F32 = jnp.float32
MIB = 1024 * 1024
LIMIT = 62

HBM = pl.BlockSpec(memory_space=pl.ANY)
VMEM = pl.BlockSpec(memory_space=pltpu.VMEM)
SMEM = pl.BlockSpec(memory_space=pltpu.SMEM)


def nn(a, b):
    return jnp.dot(a, b, preferred_element_type=F32)


def nt(a, b):
    return lax.dot_general(a, b, (((1,), (1,)), ((), ())), preferred_element_type=F32)


def tn(a, b):
    return lax.dot_general(a, b, (((0,), (0,)), ((), ())), preferred_element_type=F32)


def loop(count, body, unroll=1):
    def step(i, carry):
        for u in range(unroll):
            body(i * unroll + u)
        return carry

    if count == unroll:
        step(0, 0)
    else:
        lax.fori_loop(0, count // unroll, step, 0)


def unroll_of(count):
    return next(u for u in (4, 3, 2, 1) if count % u == 0)


def rows_of(i, size):
    return pl.ds(pl.multiple_of(i * size, size), size)


def f32_row(ref, row, col=0, width=D):
    return ref[pl.ds(row, 1), pl.ds(col, width)].astype(F32)


class Copies:
    def __init__(self, sems):
        self.sems = sems
        self.used = 0
        self.open = []

    def start(self, src, dst):
        copy = pltpu.make_async_copy(src, dst, self.sems.at[self.used])
        self.used += 1
        copy.start()
        self.open.append(copy)
        return copy

    def wait(self, *copies):
        for copy in copies:
            copy.wait()
            self.open = [one for one in self.open if one is not copy]

    def finish(self):
        self.wait(*list(self.open))

    def take(self, count):
        self.used += count
        return self.used - count

    def begin(self, src, dst, at):
        pltpu.make_async_copy(src, dst, self.sems.at[at]).start()

    def wait_at(self, src, dst, at):
        pltpu.make_async_copy(src, dst, self.sems.at[at]).wait()


def gelu_pair(u):
    size = jnp.abs(u)
    base = 1.0 + (0.3275911 * 0.7071067811865476) * size
    guess = pl.reciprocal(base, approx=True)
    t = guess * (2.0 - base * guess)
    ex = jnp.exp2((u * u) * (-0.5 * 1.4426950408889634))
    poly = 0.5306027145 * t - 0.7265760135
    poly = poly * t + 0.7107068705
    poly = poly * t - 0.142248368
    poly = poly * t + 0.127414796
    tail = poly * t * ex
    phi = jnp.where(u >= 0.0, 1.0 - tail, tail)
    return u * phi, phi + u * (0.3989422804014327 * ex)


def norm_rows(src, dst, rows, gain, shift):
    def body(i):
        sel = rows_of(i, CHUNK)
        x = src[sel, :].astype(F32)
        centered = x - jnp.mean(x, axis=-1, keepdims=True)
        var = jnp.mean(centered * centered, axis=-1, keepdims=True)
        dst[sel, :] = (centered * lax.rsqrt(var + EPS) * gain + shift).astype(BF)

    loop(rows // CHUNK, body, unroll_of(rows // CHUNK))


def norm_back(src, grad, base, write, rows, gain):
    count = rows // CHUNK
    unroll = 3 if count % 3 == 0 else 2

    def step(i, carry):
        for u in range(unroll):
            carry = one(i * unroll + u, carry)
        return carry

    def one(i, carry):
        d_gain, d_shift = carry
        sel = rows_of(i, CHUNK)
        x = src[sel, :].astype(F32)
        dh = grad[sel, :]
        centered = x - jnp.mean(x, axis=-1, keepdims=True)
        var = jnp.mean(centered * centered, axis=-1, keepdims=True)
        rstd = lax.rsqrt(var + EPS)
        hat = centered * rstd
        g = dh * gain
        part = dh * hat
        dx = rstd * (
            g
            - jnp.mean(g, axis=-1, keepdims=True)
            - hat * jnp.mean(g * hat, axis=-1, keepdims=True)
        )
        if base is not None:
            dx = dx + base[sel, :].astype(F32)
        write(sel, dx)
        d_gain = d_gain + jnp.sum(part.reshape(CHUNK // 8, 8, D), axis=0)
        d_shift = d_shift + jnp.sum(dh.reshape(CHUNK // 8, 8, D), axis=0)
        return d_gain, d_shift

    zero = jnp.zeros((8, D), F32)
    d_gain, d_shift = lax.fori_loop(0, count // unroll, step, (zero, zero))
    return jnp.sum(d_gain, axis=0, keepdims=True), jnp.sum(d_shift, axis=0, keepdims=True)


def column_sum(ref, rows, col=0, width=D):
    def step(i, carry):
        x = ref[rows_of(i, CHUNK), pl.ds(col, width)].astype(F32)
        return carry + jnp.sum(x.reshape(CHUNK // 8, 8, width), axis=0)

    total = lax.fori_loop(0, rows // CHUNK, step, jnp.zeros((8, width), F32))
    return jnp.sum(total, axis=0, keepdims=True)


def as_bf16(flags):
    return jnp.where(flags, 1.0, 0.0).astype(BF)


def pick_matrix(order, image, start, count, low, high):
    row = order[image, :, pl.ds(start, count)].astype(F32)
    images = order.shape[0]
    col = jnp.broadcast_to(row, (8, count)).T[:, 0:1].astype(jnp.int32)
    rank = start + lax.broadcasted_iota(jnp.int32, (count, 1), 0)
    col = jnp.where((rank >= low) & (rank < high), col * images + image, -1)
    return as_bf16(col == lax.broadcasted_iota(jnp.int32, (count, PATCH * images), 1))


def place_matrix(order, image, start, count, low, high):
    row = order[image, :, pl.ds(start, count)]
    rank = start + lax.broadcasted_iota(jnp.int32, (1, count), 1)
    row = jnp.where((rank >= low) & (rank < high), row, -1)
    return as_bf16(row == lax.broadcasted_iota(jnp.int32, (PATCH, count), 0))


def flatten(rows, flat):
    flat[...] = rows[...].reshape(flat.shape)


def split_orders(order, split):
    for image in range(split.shape[0]):
        split[image] = order[image : image + 1, :]


def split_pair(pair):
    lane = lax.broadcasted_iota(jnp.int32, pair.shape, 1)
    zero = jnp.zeros_like(pair)
    return jnp.concatenate([jnp.where(lane < 64, pair, zero), jnp.where(lane < 64, zero, pair)], axis=0)


def join_rows(both):
    rows = both.shape[0] // 2
    lane = lax.broadcasted_iota(jnp.int32, (rows, 128), 1)
    return jnp.where(lane < 64, both[:rows], both[rows:])


def join_columns(both):
    rows = both.shape[1] // 2
    return jnp.concatenate([both[:64, :rows], both[64:, rows:]], axis=0).T


PAIRS = HEADS // 2
STEP = 6


def each_pair_group(images, body):
    def group(i):
        image = i // (PAIRS // STEP)
        first = (i % (PAIRS // STEP)) * STEP
        pairs = [first + step for step in range(STEP)]
        body(image, [image * PAIRS + pair for pair in pairs], [pl.ds(pl.multiple_of(pair * 128, 128), 128) for pair in pairs])

    loop(images * (PAIRS // STEP), group)


def softmax(scores, axis):
    ex = jnp.exp(scores - jnp.max(scores, axis=axis, keepdims=True))
    return (ex * (1.0 / jnp.sum(ex, axis=axis, keepdims=True))).astype(BF)


def score_back(probs, d_probs, axis):
    wide = probs.astype(F32)
    return (wide * (d_probs - jnp.sum(d_probs * wide, axis=axis, keepdims=True))).astype(BF)


def attention_by_rows(images, n, q, k, v, p, o, count_of):
    def body(image, slots, lanes):
        sel = rows_of(image, n)
        ok = lax.broadcasted_iota(jnp.int32, (1, n), 1) < count_of(image)
        scores = [nt(split_pair(q[sel, at]), k[sel, at]) for at in lanes]
        probs = [softmax(jnp.where(ok, one, -1000000000.0), 1) for one in scores]
        for slot, one in zip(slots, probs):
            p[slot] = one
        mixed = [nn(one, v[sel, at]) for one, at in zip(probs, lanes)]
        for at, one in zip(lanes, mixed):
            o[sel, at] = join_rows(one).astype(BF)

    each_pair_group(images, body)


def attention_by_columns(images, nk, q, k, v, p, o, key_ok):
    def body(image, slots, lanes):
        qs, ks = rows_of(image, NM), rows_of(image, nk)
        ok = key_ok(image)
        scores = [nt(k[ks, at], split_pair(q[qs, at])) for at in lanes]
        probs = [softmax(jnp.where(ok, one, -1000000000.0), 0) for one in scores]
        if p is not None:
            for slot, one in zip(slots, probs):
                p[slot] = one
        mixed = [tn(v[ks, at], one) for one, at in zip(probs, lanes)]
        for at, one in zip(lanes, mixed):
            o[qs, at] = join_columns(one).astype(BF)

    each_pair_group(images, body)


def attention_back_rows(images, n, q, k, v, p, do, dq, dkv):
    def body(image, slots, lanes):
        sel = rows_of(image, n)
        d_mixed = [split_pair(do[sel, at]) for at in lanes]
        d_probs = [nt(one, v[sel, at]) for one, at in zip(d_mixed, lanes)]
        d_scores = [score_back(p[slot], one, 1) for slot, one in zip(slots, d_probs)]
        d_values = [tn(p[slot], one) for slot, one in zip(slots, d_mixed)]
        d_query = [nn(one, k[sel, at]) for one, at in zip(d_scores, lanes)]
        d_keys = [tn(one, split_pair(q[sel, at])) for one, at in zip(d_scores, lanes)]
        for at, value, query, key in zip(lanes, d_values, d_query, d_keys):
            dq[sel, at] = (join_rows(query) * 0.125).astype(BF)
            dkv[sel, at] = key.astype(BF)
            dkv[sel, pl.ds(pl.multiple_of(D + at.start, 128), 128)] = value.astype(BF)

    each_pair_group(images, body)


def attention_back_columns(images, nk, q, k, v, p, do, dq, dkv):
    def body(image, slots, lanes):
        qs, ks = rows_of(image, NM), rows_of(image, nk)
        d_mixed = [split_pair(do[qs, at]) for at in lanes]
        d_probs = [nt(v[ks, at], one) for one, at in zip(d_mixed, lanes)]
        d_scores = [score_back(p[slot], one, 0) for slot, one in zip(slots, d_probs)]
        d_values = [nn(p[slot], one) for slot, one in zip(slots, d_mixed)]
        d_query = [tn(k[ks, at], one) for one, at in zip(d_scores, lanes)]
        d_keys = [nn(one, split_pair(q[qs, at])) for one, at in zip(d_scores, lanes)]
        for at, value, query, key in zip(lanes, d_values, d_query, d_keys):
            dq[qs, at] = (join_columns(query) * 0.125).astype(BF)
            dkv[ks, at] = key.astype(BF)
            dkv[ks, pl.ds(pl.multiple_of(D + at.start, 128), 128)] = value.astype(BF)

    each_pair_group(images, body)


HALF = 512


def mlp_forward(rows, h2, w1, w2, up_b, u, a, gp, tile, acc, out, base):
    acc[...] = base()
    steps = FF // HALF

    def multiply(t):
        u[t % 2] = nn(h2[...], w1[:, t * HALF : (t + 1) * HALF])

    def add(t):
        acc[...] += nn(tile[t % 2], w2[t * HALF : (t + 1) * HALF, :])

    multiply(0)
    for t in range(steps):
        if t + 1 < steps:
            multiply(t + 1)
        if t > 0:
            add(t - 1)
        for c in range(0, HALF, 256):
            at = slice(t * HALF + c, t * HALF + c + 256)
            shift = up_b[0:1, at].astype(F32)
            for r in range(0, rows, CHUNK):
                sel = slice(r, r + CHUNK)
                value, slope = gelu_pair(u[t % 2, sel, c : c + 256] + shift)
                low = value.astype(BF)
                tile[t % 2, sel, c : c + 256] = low
                if a is not None:
                    a[sel, at] = low
                if gp is not None:
                    gp[sel, at] = slope.astype(BF)
    add(steps - 1)
    out[...] = acc[...].astype(BF)


def mlp_back(rows, dyb, gp, w1, w2, du, u, acc, ready=lambda i, which: None):
    acc[...] = jnp.zeros_like(acc)

    def body(i):
        cols = [pl.ds(pl.multiple_of((2 * i + part) * HALF, HALF), HALF) for part in range(2)]
        ready(i, 0)
        for part in range(2):
            u[part] = nt(dyb[...], w2[cols[part], :])
        ready(i, 1)
        for part in range(2):
            for r in range(0, rows, CHUNK):
                sel = slice(r, r + CHUNK)
                du[sel, cols[part]] = (gp[sel, cols[part]].astype(F32) * u[part, sel, :]).astype(BF)
            acc[...] += nt(du[:, cols[part]], w1[:, cols[part]])

    loop(FF // (2 * HALF), body)


def project(count, rows, left, weight, first, write):
    def body(j):
        write(j, nn(left[...], weight[:, pl.ds(pl.multiple_of((first + j) * D, D), D)]))

    loop(count, body)


def set_biases(ref, bias):
    ref[0] = f32_row(bias, 0)
    ref[1] = jnp.zeros((1, D), F32)
    ref[2] = f32_row(bias, 0, D)


def cost(flops, nbytes):
    return pl.CostEstimate(flops=int(flops), bytes_accessed=int(nbytes), transcendentals=0)


def params(mib):
    return pltpu.CompilerParams(vmem_limit_bytes=mib * MIB)


def struct(shape, dtype=BF):
    return jax.ShapeDtypeStruct(shape, dtype)


def start_weights(copies, sources, scratch):
    return [copies.start(src, dst) for src, dst in zip(sources, scratch)]


def encode_kernel(group, groups, ids, visible, order_in, gains, biases, qvb, upb, rows, cot, wqkv, wo, w1, w2,
                  lat_out, x_out, hq_out, q_out, k_out, v_out, p_out, o_out, y1_out, h2_out, gp_out, a_out, *refs):
    ready, refs = refs[: 4 * groups], refs[4 * groups :]
    (order, rows_v, flat, sqkv, so, s1, s2, x, hq, qkv, p, o, y1, h2, gp, a, u, tile, acc, shifts, lat, sems) = refs
    n = GROUP * NV
    split_orders(order_in, order)

    @pl.when(ids[0] == 0)
    def _():
        copies = Copies(sems)
        got_rows = copies.start(rows.at[0], rows_v)
        got_qkv, got_o, got_1, got_2 = start_weights(
            copies, (wqkv.at[0], wo.at[0], w1.at[0], w2.at[0]), (sqkv, so, s1, s2)
        )
        gain, bias = gains.at[0], biases.at[0]
        set_biases(shifts, qvb)
        copies.wait(got_rows)
        flatten(rows_v, flat)

        def pick_rows(i):
            image = group * GROUP + i
            pick = pick_matrix(order, image, 0, NV, 0, visible[image])
            x[rows_of(i, NV), :] = nn(pick, flat[...]).astype(BF)

        loop(GROUP, pick_rows)
        copies.start(x, x_out)
        norm_rows(x, hq, n, f32_row(gain, 0), f32_row(bias, 0))
        copies.start(hq, hq_out)
        copies.wait(got_qkv)

        def keep(j, value):
            scale = jnp.where(j == 0, 0.125, 1.0)
            qkv[j] = ((value + shifts[j]).astype(BF).astype(F32) * scale).astype(BF)

        project(3, n, hq, sqkv, 0, keep)
        q, k, v = qkv.at[0], qkv.at[1], qkv.at[2]
        copies.start(q, q_out)
        copies.start(k, k_out)
        copies.start(v, v_out)
        attention_by_rows(GROUP, NV, q, k, v, p, o, lambda i: visible[group * GROUP + i])
        copies.start(p, p_out)
        copies.start(o, o_out)
        copies.wait(got_o)
        y1[...] = nn(o[...], so[...]) + f32_row(bias, 1) + x[...].astype(F32)
        copies.start(y1, y1_out)
        norm_rows(y1, h2, n, f32_row(gain, 1), f32_row(bias, 2))
        copies.start(h2, h2_out)
        copies.wait(got_1, got_2)
        mlp_forward(n, h2, s1, s2, upb, u, a, gp, tile, acc, lat, lambda: y1[...] + f32_row(bias, 3))
        copies.start(gp, gp_out)
        copies.start(a, a_out)
        copies.start(lat, lat_out)
        copies.finish()

    if group == groups - 1:

        @pl.when(ids[0] == 1)
        def _():
            copies = Copies(sems)
            m = GROUP * NM
            x_out, hq_out, q_out, dyb_out = (ready[i * groups : (i + 1) * groups] for i in range(4))
            gain, bias = gains.at[0], biases.at[0]
            got_rows = copies.start(rows.at[0], rows_v)
            got_q = copies.start(wqkv.at[0, :, pl.ds(0, D)], so)
            copies.wait(got_rows)
            flatten(rows_v, flat)
            got_cot = copies.start(cot.at[0], rows_v)
            top = pl.ds(0, m)

            def pick_group(g):
                def pick_rows(i):
                    image = g * GROUP + i
                    pick = pick_matrix(order, image, FIRST, NM, visible[image], PATCH)
                    x[rows_of(i, NM), :] = nn(pick, flat[...]).astype(BF)

                loop(GROUP, pick_rows)

            for g in range(groups):
                pick_group(g)
                norm_rows(x, hq, m, f32_row(gain, 0), f32_row(bias, 0))
                sent = [copies.start(x.at[top], x_out[g]), copies.start(hq.at[top], hq_out[g])]
                if g == 0:
                    copies.wait(got_q)
                q = qkv.at[g]
                q[top, :] = ((nn(hq[top, :], so[...]) + f32_row(qvb, 0)).astype(BF) * 0.125).astype(BF)
                copies.start(q.at[top], q_out[g])
                copies.wait(*sent)
            copies.wait(got_cot)
            flatten(rows_v, flat)
            for g in range(groups):
                pick_group(g)
                copies.wait(copies.start(x.at[top], dyb_out[g]))
            copies.finish()


def encode(group, groups, ids, visible, order, gains, biases, qvb, upb, rows, cot, weights):
    n = GROUP * NV
    images = order.shape[0]
    row, wide = struct((n, D)), struct((n, FF))
    heads = struct((GROUP * PAIRS, 2 * NV, NV))
    outs = [row] * 6 + [heads, row, struct((n, D), F32), row, wide, wide] + [struct((GROUP * NM, D))] * (4 * groups)
    vm = lambda s: pltpu.VMEM(s.shape, s.dtype)
    scratch = [
        pltpu.VMEM((images, 1, PATCH), jnp.int32),
        pltpu.VMEM((PATCH, images, D), BF), pltpu.VMEM((PATCH * images, D), BF),
        pltpu.VMEM((D, 3 * D), BF), pltpu.VMEM((D, D), BF), pltpu.VMEM((D, FF), BF), pltpu.VMEM((FF, D), BF),
        vm(row), vm(row), pltpu.VMEM((3, n, D), BF), vm(heads), vm(row), pltpu.VMEM((n, D), F32), vm(row),
        vm(wide), vm(wide), pltpu.VMEM((2, n, HALF), F32), pltpu.VMEM((2, n, HALF), BF), pltpu.VMEM((n, D), F32),
        pltpu.VMEM((3, 1, D), F32), vm(row),
        pltpu.SemaphoreType.DMA((24,)),
    ]
    got = pl.pallas_call(
        partial(encode_kernel, group, groups),
        in_specs=[SMEM, SMEM] + [VMEM] * 5 + [HBM] * 6,
        out_specs=[HBM] * len(outs),
        out_shape=outs,
        scratch_shapes=scratch,
        compiler_params=params(LIMIT),
        cost_estimate=cost(2 * n * 12 * D * D, 25e6),
        name="encode",
    )(ids, visible, order, gains, biases, qvb, upb, rows, cot, *weights)
    ready = got[12:]
    return got[:12], [ready[i * groups : (i + 1) * groups] for i in range(4)]


def block_end(copies, n, got_weights, so, s1, s2, bias, gain, up_b, x, o, y1, h2, a, gp, u, tile, acc, res):
    got_o, got_1, got_2 = got_weights
    copies.wait(got_o)
    y1[...] = nn(o[...], so[...]) + f32_row(bias, 1) + x[...].astype(F32)
    norm_rows(y1, h2, n, f32_row(gain, 1), f32_row(bias, 2))
    copies.wait(got_1, got_2)
    mlp_forward(n, h2, s1, s2, up_b, u, a, gp, tile, acc, res, lambda: y1[...] + f32_row(bias, 3))


def target_kernel(group, picks, ids, visible, order_in, gain, bias, qvb, upb, rows, cot, wqkv, wo, w1, w2, res_out,
                  *refs):
    picked, refs = refs[:picks], refs[picks:]
    (order, rows_v, flat, sqkv, so, s1, s2, x, hq, qkv, o, y1, h2, u, tile, acc, shifts, res, cot_v, sems) = refs
    n = GROUP * NM
    q, k, v = qkv.at[0], qkv.at[1], qkv.at[2]

    @pl.when(ids[0] == 0)
    def _():
        copies = Copies(sems)
        split_orders(order_in, order)
        got_rows = copies.start(rows.at[0], rows_v)
        got_qkv = copies.start(wqkv, sqkv)
        got_weights = start_weights(copies, (wo, w1, w2), (so, s1, s2))
        set_biases(shifts, qvb)
        copies.wait(got_rows)
        flatten(rows_v, flat)

        def pick_rows(i):
            image = group * GROUP + i
            pick = pick_matrix(order, image, FIRST, NM, visible[image], PATCH)
            x[rows_of(i, NM), :] = nn(pick, flat[...]).astype(BF)

        loop(GROUP, pick_rows)
        norm_rows(x, hq, n, f32_row(gain, 0), f32_row(bias, 0))
        copies.wait(got_qkv)

        def keep(j, value):
            scale = jnp.where(j == 0, 0.125, 1.0)
            qkv[j] = ((value + shifts[j]).astype(BF).astype(F32) * scale).astype(BF)

        project(3, n, hq, sqkv, 0, keep)

        def key_ok(i):
            return lax.broadcasted_iota(jnp.int32, (NM, 1), 0) + FIRST >= visible[group * GROUP + i]

        attention_by_columns(GROUP, NM, q, k, v, None, o, key_ok)
        block_end(copies, n, got_weights, so, s1, s2, bias, gain, upb, x, o, y1, h2, None, None, u, tile, acc, res)
        copies.start(res, res_out)
        if picks:
            copies.wait(copies.start(cot.at[0], rows_v))
            flatten(rows_v, flat)
            for g in range(picks):

                def pick_cot(i, g=g):
                    image = g * GROUP + i
                    pick = pick_matrix(order, image, 0, NV, 0, visible[image])
                    cot_v[rows_of(i, NV), :] = nn(pick, flat[...]).astype(BF)

                loop(GROUP, pick_cot)
                copies.wait(copies.start(cot_v, picked[g]))
        copies.finish()


def target(group, picks, ids, visible, order, vecs, rows, cot, weights):
    n = GROUP * NM
    images = order.shape[0]
    row, full = pltpu.VMEM((n, D), BF), pltpu.VMEM((n, D), F32)
    got = pl.pallas_call(
        partial(target_kernel, group, picks),
        in_specs=[SMEM, SMEM] + [VMEM] * 5 + [HBM] * 6,
        out_specs=[HBM] * (1 + picks),
        out_shape=[struct((n, D))] + [struct((GROUP * NV, D))] * picks,
        scratch_shapes=[
            pltpu.VMEM((images, 1, PATCH), jnp.int32),
            pltpu.VMEM((PATCH, images, D), BF), pltpu.VMEM((PATCH * images, D), BF),
            pltpu.VMEM((D, 3 * D), BF), pltpu.VMEM((D, D), BF), pltpu.VMEM((D, FF), BF), pltpu.VMEM((FF, D), BF),
            row, row, pltpu.VMEM((3, n, D), BF), row, full, row,
            pltpu.VMEM((2, n, HALF), F32), pltpu.VMEM((2, n, HALF), BF), full, pltpu.VMEM((3, 1, D), F32), row,
            pltpu.VMEM((GROUP * NV, D), BF), pltpu.SemaphoreType.DMA((12,)),
        ],
        compiler_params=params(LIMIT),
        cost_estimate=cost(1e6, 1e5),
        name="target",
    )(ids, visible, order, *vecs, rows, cot, *weights)
    return got[0], got[1:]


def regress_kernel(group, ids, visible, gains, biases, qvb, upb, lat_in, x_in, q_in, dyb_in, wqkv, wo, w1, w2,
                   dlat_out, res_out, hk_out, dq_out, dkv_out, o_out, dy1b_out, h2_out, du_out, a_out, dy1_out,
                   sums_out,
                   sqkv, so, s1, s2, x, lat, hk, q, kv, p, o, y1, h2, gp, a, u, tile, acc, shifts,
                   res, dyb, du, dy1, dy1b, do, dq, dkv, dh, dlat, sums, sems):
    n, m = GROUP * NM, GROUP * NV
    k, v = kv.at[0], kv.at[1]

    @pl.when(ids[0] == 1)
    def _():
        copies = Copies(sems)
        gain, bias = gains.at[0], biases.at[0]
        got_lat = copies.start(lat_in, lat)
        got_kv = copies.start(wqkv.at[0, :, pl.ds(D, 2 * D)], sqkv)
        got_q = copies.start(q_in, q)
        got_x = copies.start(x_in, x)
        got_weights = start_weights(copies, (wo.at[0], w1.at[0], w2.at[0]), (so, s1, s2))
        got_dyb = copies.start(dyb_in, dyb)
        set_biases(shifts, qvb)
        copies.wait(got_lat)
        norm_rows(lat, hk, m, f32_row(gain, 0), f32_row(bias, 0))
        copies.start(hk, hk_out)
        copies.wait(got_kv)

        def keep_kv(j, value):
            kv[j] = (value + shifts[j + 1]).astype(BF)

        project(2, m, hk, sqkv, 0, keep_kv)
        copies.wait(got_q, got_x)

        def key_ok(i):
            return lax.broadcasted_iota(jnp.int32, (NV, 1), 0) < visible[group * GROUP + i]

        attention_by_columns(GROUP, NV, q, k, v, p, o, key_ok)
        copies.start(o, o_out)
        block_end(copies, n, got_weights, so, s1, s2, bias, gain, upb, x, o, y1, h2, a, gp, u, tile, acc, res)
        copies.start(res, res_out)
        copies.start(h2, h2_out)
        copies.start(a, a_out)
        copies.wait(got_dyb)
        mlp_back(n, dyb, gp, s1, s2, du, u, acc)
        copies.start(du, du_out)

        def keep(sel, dx):
            dy1[sel, :] = dx
            dy1b[sel, :] = dx.astype(BF)

        g2, b2 = norm_back(y1, acc, dyb, keep, n, f32_row(gain, 1))
        copies.start(dy1, dy1_out)
        copies.start(dy1b, dy1b_out)
        do[...] = nt(dy1b[...], so[...]).astype(BF)
        attention_back_columns(GROUP, NV, q, k, v, p, do, dq, dkv)
        copies.start(dq, dq_out)
        copies.start(dkv, dkv_out)
        dh[...] = nt(dkv[:, :D], sqkv[:, :D])
        dh[...] += nt(dkv[:, D:], sqkv[:, D:])

        def keep_side(sel, dx):
            dlat[sel, :] = dx.astype(BF)

        gk, bk = norm_back(lat, dh, None, keep_side, m, f32_row(gain, 0))
        copies.start(dlat, dlat_out)
        for row, value in enumerate((gk, g2, bk, b2)):
            sums[pl.ds(row, 1), :] = value
        copies.start(sums, sums_out)
        copies.finish()


def regress(group, ids, visible, vecs, lat, x, q, dyb, weights):
    n, m = GROUP * NM, GROUP * NV
    row, side, wide = struct((n, D)), struct((m, D)), struct((n, FF))
    pair = struct((m, 2 * D))
    outs = [side, row, side, row, pair, row, row, row, wide, wide, struct((n, D), F32), struct((8, D), F32)]
    vm = lambda s: pltpu.VMEM(s.shape, s.dtype)
    full, fside = pltpu.VMEM((n, D), F32), pltpu.VMEM((m, D), F32)
    scratch = [
        pltpu.VMEM((D, 2 * D), BF), pltpu.VMEM((D, D), BF), pltpu.VMEM((D, FF), BF), pltpu.VMEM((FF, D), BF),
        vm(row), vm(side), vm(side), vm(row), pltpu.VMEM((2, m, D), BF),
        pltpu.VMEM((GROUP * PAIRS, NV, 2 * NM), BF), vm(row), full, vm(row), vm(wide), vm(wide),
        pltpu.VMEM((2, n, HALF), F32), pltpu.VMEM((2, n, HALF), BF), full, pltpu.VMEM((3, 1, D), F32),
        vm(row), vm(row), vm(wide), full, vm(row), vm(row), vm(row), vm(pair), fside, vm(side),
        pltpu.VMEM((8, D), F32),
        pltpu.SemaphoreType.DMA((24,)),
    ]
    return pl.pallas_call(
        partial(regress_kernel, group),
        in_specs=[SMEM, SMEM] + [VMEM] * 4 + [HBM] * 8,
        out_specs=[HBM] * len(outs),
        out_shape=outs,
        scratch_shapes=scratch,
        compiler_params=params(LIMIT),
        cost_estimate=cost(4 * n * 12 * D * D, 25e6),
        name="regress",
    )(ids, visible, *vecs, lat, x, q, dyb, *weights)


def stack_rows(copies, pieces, ref, size):
    return [copies.start(piece, ref.at[pl.ds(i * size, size)]) for i, piece in enumerate(pieces)]


def clear_tail(ref, used):
    ref[pl.ds(used, ref.shape[0] - used), :] = jnp.zeros((ref.shape[0] - used, ref.shape[1]), ref.dtype)


def halves(count, blocks):
    rows = D // 16
    if count == 16:
        cut = [struct((2, blocks, rows, D))] * 4 if blocks > 4 else [struct((2, 2, 2, 1, rows, D))] * blocks
        return [struct((2, 2, 2, blocks, rows, D))] + cut
    return [struct((D, D))] * blocks


def give_blocks(copies, core, tree, left_right, out, dest):
    size = 8 if tree else 1
    blocks = out.shape[0]
    first = copies.take(blocks * size)

    def send(j, act):
        if not tree:
            for block in range(blocks):
                pl.when(j == block)(lambda block=block: act(out.at[block], dest[block], first + block))
            return
        view = out.at[j].reshape(2, 2, 2, 2, D // 16, D)
        for x in range(2):
            for low in range(2):
                at = first + j * size + 4 * x + 2 * low
                act(view.at[:, low, x, core], dest[0].at[x, low, :, j], at)
                if blocks > 4:
                    act(view.at[:, low, x, 1 - core], dest[1 + 2 * x + low].at[:, j], at + 1)
                else:
                    for block in range(blocks):
                        pl.when(j == block)(
                            lambda block=block: act(view.at[:, low, x, 1 - core], dest[1 + block].at[x, low, :, 0], at + 1)
                        )

    def body(j):
        out[j] = left_right(j)
        send(j, copies.begin)

    loop(blocks, body)
    loop(blocks, lambda j: send(j, copies.wait_at))


def give_rows(copies, core, tree, multiply, out, dest):
    size = 4 if tree else 1
    first = copies.take(4 * size)

    def send(j, act):
        if not tree:
            act(out.at[j], dest[0].at[pl.ds(pl.multiple_of(j * D, D), D)], first + j)
            return
        view = out.at[j].reshape(2, 2, D // 4, D)
        low, high = lax.rem(j, 2), lax.div(j, 2)
        for x in range(2):
            at = first + j * size + 2 * x
            act(view.at[x, core], dest[0].at[x, low, high, 0], at)
            act(view.at[x, 1 - core], dest[1].at[x, low, high, 0], at + 1)

    def body(j):
        out[j] = multiply(j)
        send(j, copies.begin)

    loop(4, body)
    loop(4, lambda j: send(j, copies.wait_at))


def down_kernel(groups, parts, ids, *refs):
    cot, lat, a_enc, a_reg, dyb_reg = (refs[i * groups : (i + 1) * groups] for i in range(5))
    refs = refs[5 * groups :]
    dest, refs = refs[:parts], refs[parts:]
    sums_out, cot_v, dyb, a, dlat, out, sums, sems = refs
    images = groups * GROUP
    nv, nm = GROUP * NV, GROUP * NM

    @pl.when(ids[0] == 0)
    def _():
        copies = Copies(sems)
        got = stack_rows(copies, cot, cot_v, nv) + stack_rows(copies, lat, dlat, nv)
        stack_rows(copies, a_enc, a, nv)
        copies.wait(*got)
        dyb[...] = (cot_v[...].astype(F32) + dlat[...].astype(F32)).astype(BF)
        copies.finish()

    @pl.when(ids[0] == 1)
    def _():
        copies = Copies(sems)
        stack_rows(copies, a_reg, a, nm)
        stack_rows(copies, dyb_reg, dyb, nm)
        clear_tail(a, images * NM)
        clear_tail(dyb, images * NM)
        copies.finish()

    copies = Copies(sems)

    def multiply(j):
        return tn(a[:, pl.ds(pl.multiple_of(j * D, D), D)], dyb[...]).astype(BF)

    give_rows(copies, ids[1], parts == 2, multiply, out, dest)
    sums[...] = jnp.broadcast_to(column_sum(dyb, images * NV), (8, D))
    copies.start(sums, sums_out)
    copies.finish()


def down_grad(groups, count, ids, cot, dlat, a_enc, a_reg, dyb_reg):
    n = groups * GROUP * NV
    main = [struct((2, 2, 2, 1, D // 4, D))] * 2 if count == 16 else [struct((FF, D))]
    outs = main + [struct((8, D), F32)]
    row = pltpu.VMEM((n, D), BF)
    scratch = [
        row, row, pltpu.VMEM((n, FF), BF), row, pltpu.VMEM((4, D, D), BF), pltpu.VMEM((8, D), F32),
        pltpu.SemaphoreType.DMA((24,)),
    ]
    got = pl.pallas_call(
        partial(down_kernel, groups, len(main)),
        in_specs=[SMEM] + [HBM] * (5 * groups),
        out_specs=[HBM] * len(outs),
        out_shape=outs,
        scratch_shapes=scratch,
        compiler_params=params(LIMIT),
        cost_estimate=cost(1e6, 1e5),
        name="down_grad",
    )(ids, *cot, *dlat, *a_enc, *a_reg, *dyb_reg)
    return got[: len(main)], got[-1]


def mlp_kernel(ids, gains, cot, dlat_in, w1, w2, y1_in, gp_in, du_out, dy1_out, dy1b_out, sums_out,
               s1, s2, cot_v, dlat, dyb, gp, y1, du, u, acc, dy1, dy1b, sums, sems):
    n = GROUP * NV
    third = FF // 3

    @pl.when(ids[0] == 0)
    def _():
        copies = Copies(sems)
        got = [copies.start(dlat_in, dlat), copies.start(cot, cot_v)]
        start = copies.take(9)

        def parts(i):
            cols = pl.ds(pl.multiple_of(i * third, third), third)
            return (
                (w2.at[0, cols, :], s2.at[cols, :]),
                (gp_in.at[:, cols], gp.at[:, cols]),
                (w1.at[0, :, cols], s1.at[:, cols]),
            )

        for i in range(3):
            for k, (src, dst) in enumerate(parts(i)):
                copies.begin(src, dst, start + 3 * i + k)
        got_y = copies.start(y1_in, y1)

        def ready(i, which):
            for k in ((0, 1), (2,))[which]:
                copies.wait_at(*parts(i)[k], start + 3 * i + k)

        copies.wait(*got)
        dyb[...] = (cot_v[...].astype(F32) + dlat[...].astype(F32)).astype(BF)
        mlp_back(n, dyb, gp, s1, s2, du, u, acc, ready)
        copies.start(du, du_out)
        copies.wait(got_y)

        def keep(sel, dx):
            dy1[sel, :] = dx
            dy1b[sel, :] = dx.astype(BF)

        g2, b2 = norm_back(y1, acc, dyb, keep, n, f32_row(gains.at[0], 1))
        copies.start(dy1, dy1_out)
        copies.start(dy1b, dy1b_out)
        sums[pl.ds(0, 1), :] = g2
        sums[pl.ds(1, 1), :] = b2
        copies.start(sums, sums_out)
        copies.finish()


def mlp_grad(ids, gains, cot, dlat, w1, w2, y1, gp):
    n = GROUP * NV
    row, wide, full = pltpu.VMEM((n, D), BF), pltpu.VMEM((n, FF), BF), pltpu.VMEM((n, D), F32)
    outs = [struct((n, FF)), struct((n, D), F32), struct((n, D)), struct((8, D), F32)]
    return pl.pallas_call(
        mlp_kernel,
        in_specs=[SMEM, VMEM] + [HBM] * 6,
        out_specs=[HBM] * len(outs),
        out_shape=outs,
        scratch_shapes=[
            pltpu.VMEM((D, FF), BF), pltpu.VMEM((FF, D), BF), row, row, row, wide, full, wide,
            pltpu.VMEM((2, n, HALF), F32), full, full, row, pltpu.VMEM((8, D), F32), pltpu.SemaphoreType.DMA((24,)),
        ],
        compiler_params=params(LIMIT),
        cost_estimate=cost(1e6, 1e5),
        name="mlp_grad",
    )(ids, gains, cot, dlat, w1, w2, y1, gp)


def up_kernel(groups, parts, ids, *refs):
    pieces = [refs[i * groups : (i + 1) * groups] for i in range(8)]
    refs = refs[8 * groups :]
    dest, refs = refs[:parts], refs[parts:]
    sums_out, left, right, out, sums, sems = refs
    images = groups * GROUP

    def load(du, h2, dy1b, o, size):
        copies = Copies(sems)
        stack_rows(copies, h2, left.at[0], size)
        for j in range(4):
            stack_rows(copies, [one.at[:, pl.ds(j * D, D)] for one in du], right.at[j], size)
        stack_rows(copies, o, left.at[1], size)
        stack_rows(copies, dy1b, right.at[4], size)
        return copies

    @pl.when(ids[0] == 0)
    def _():
        load(*pieces[:4], GROUP * NV).finish()

    @pl.when(ids[0] == 1)
    def _():
        copies = load(*pieces[4:], GROUP * NM)
        for ref in (left, right):
            for i in range(ref.shape[0]):
                clear_tail(ref.at[i], images * NM)
        copies.finish()

    copies = Copies(sems)

    def multiply(j):
        value = tn(left[lax.div(j, 4)], right[j]).astype(BF)
        sums[pl.ds(j, 1), :] = column_sum(right.at[j], images * NV)
        return value

    give_blocks(copies, ids[1], dest[0].ndim == 6, multiply, out, dest)
    copies.start(sums, sums_out)
    copies.finish()


def up_grad(groups, count, ids, *pieces):
    n = groups * GROUP * NV
    main = halves(count, 5)
    outs = main + [struct((8, D), F32)]
    got = pl.pallas_call(
        partial(up_kernel, groups, len(main)),
        in_specs=[SMEM] + [HBM] * (8 * groups),
        out_specs=[HBM] * len(outs),
        out_shape=outs,
        scratch_shapes=[
            pltpu.VMEM((2, n, D), BF), pltpu.VMEM((5, n, D), BF), pltpu.VMEM((5, D, D), BF), pltpu.VMEM((8, D), F32),
            pltpu.SemaphoreType.DMA((44,)),
        ],
        compiler_params=params(LIMIT),
        cost_estimate=cost(1e6, 1e5),
        name="up_grad",
    )(ids, *[ref for piece in pieces for ref in piece])
    return got[: len(main)], got[-1]


def attn_kernel(groups, last, ids, gains, *refs):
    if last:
        down_sums, up_sums, refs = refs[0], refs[1], refs[2:]
        mlp_sums, reg_sums = (refs[i * groups : (i + 1) * groups] for i in range(2))
        before, refs = refs[2 * groups : 3 * groups - 1], refs[3 * groups - 1 :]
    (wqkv, wo, dy1_enc, q_in, k_in, v_in, p_in, x_enc, dq_reg, dkv_reg, dy1_reg, x_reg,
     dq_out, dkv_out, dx_out, sums_out,
     sqkv, so, dy1, dy1b, q, k, v, p, x, do, dq, dkv, dh, sems) = refs
    m = GROUP * NM
    top = pl.ds(0, m)
    gain = f32_row(gains.at[0], 0)

    def finish(copies, rows):
        def keep(sel, dx):
            dy1[sel, :] = dx

        own = (*norm_back(x, dh, dy1, keep, rows, gain), column_sum(dq, rows), column_sum(dkv, GROUP * NV, D))
        copies.start(dy1, dx_out)
        if not last:
            for row, value in enumerate(own):
                sums_out[row : row + 1, :] = value
            copies.finish()
            return

        def total_of(sums):
            total = sums[0][...]
            for more in sums[1:]:
                total = total + more[...]
            return total

        done, mlp, reg = total_of(before), total_of(mlp_sums), total_of(reg_sums)
        g1, b1, queries, values = (one + done[row : row + 1, :] for row, one in enumerate(own))
        encoder = ids[0] == 0
        sums_out[0:1, :] = g1 + jnp.where(encoder, 0.0, reg[0:1, :])
        sums_out[1:2, :] = jnp.where(encoder, mlp[0:1, :], reg[1:2, :])
        sums_out[2:3, :] = b1 + jnp.where(encoder, 0.0, reg[2:3, :])
        sums_out[3:4, :] = up_sums[4:5, :]
        sums_out[4:5, :] = jnp.where(encoder, mlp[1:2, :], reg[3:4, :])
        sums_out[5:6, :] = down_sums[0:1, :]
        sums_out[6:7, :] = queries
        sums_out[7:8, :] = values
        sums_out[8:12, :] = up_sums[0:4, :]
        sums_out[12:16, :] = jnp.zeros((4, D), F32)
        copies.finish()

    @pl.when(ids[0] == 0)
    def _():
        copies = Copies(sems)
        got = [copies.start(dy1_enc, dy1), copies.start(wo.at[0], so)]
        later = [copies.start(src, dst) for src, dst in ((v_in, v), (p_in, p), (k_in, k), (q_in, q))]
        final = [copies.start(wqkv.at[0], sqkv), copies.start(x_enc, x)]
        copies.wait(*got)
        dy1b[...] = dy1[...].astype(BF)
        do[...] = nt(dy1b[...], so[...]).astype(BF)
        copies.wait(*later)
        attention_back_rows(GROUP, NV, q, k, v, p, do, dq, dkv)
        copies.start(dq, dq_out)
        copies.start(dkv, dkv_out)
        copies.wait(*final)
        dh[...] = nt(dq[...], sqkv[:, 0:D])
        for j in range(2):
            dh[...] += nt(dkv[:, j * D : (j + 1) * D], sqkv[:, (j + 1) * D : (j + 2) * D])
        finish(copies, GROUP * NV)

    @pl.when(ids[0] == 1)
    def _():
        copies = Copies(sems)
        for src, dst in ((dq_reg, dq), (dy1_reg, dy1), (x_reg, x)):
            copies.start(src, dst.at[top])
        copies.start(dkv_reg, dkv)
        copies.start(wqkv.at[0, :, pl.ds(0, D)], sqkv.at[:, pl.ds(0, D)])
        copies.finish()
        dh[top, :] = nt(dq[top, :], sqkv[:, 0:D])
        finish(copies, m)


def attn_back(groups, last, ids, gains, sums, *pieces):
    n = GROUP * NV
    row, full = pltpu.VMEM((n, D), BF), pltpu.VMEM((n, D), F32)
    outs = [struct((n, D)), struct((n, 2 * D)), struct((n, D), F32), struct((16, D), F32)]
    return pl.pallas_call(
        partial(attn_kernel, groups, last),
        in_specs=[SMEM, VMEM] + [VMEM] * len(sums) + [HBM] * len(pieces),
        out_specs=[HBM] * 3 + [VMEM],
        out_shape=outs,
        scratch_shapes=[
            pltpu.VMEM((D, 3 * D), BF), pltpu.VMEM((D, D), BF), full, row, row, row, row,
            pltpu.VMEM((GROUP * PAIRS, 2 * NV, NV), BF), row, row, row, pltpu.VMEM((n, 2 * D), BF), full,
            pltpu.SemaphoreType.DMA((20,)),
        ],
        compiler_params=params(LIMIT),
        cost_estimate=cost(1e6, 1e5),
        name="attn_back",
    )(ids, gains, *sums, *pieces)


def qkv_kernel(groups, parts, ids, *refs):
    pieces = [refs[i * groups : (i + 1) * groups] for i in range(7)]
    dq_enc, dkv_enc, hq_enc, hq_reg, hk_reg, dq_reg, dkv_reg = pieces
    refs = refs[7 * groups :]
    dest, refs = refs[:parts], refs[parts:]
    left, right, out, sems = refs
    images = groups * GROUP
    nv, nm = GROUP * NV, GROUP * NM
    hk, hq = left.at[0], left.at[1]
    dk, dv, dq = (right.at[i] for i in range(3))

    @pl.when(ids[0] == 0)
    def _():
        copies = Copies(sems)
        stack_rows(copies, hq_enc, hk, nv)
        stack_rows(copies, [one.at[:, pl.ds(0, D)] for one in dkv_enc], dk, nv)
        stack_rows(copies, [one.at[:, pl.ds(D, D)] for one in dkv_enc], dv, nv)
        stack_rows(copies, hq_enc, hq, nv)
        stack_rows(copies, dq_enc, dq, nv)
        copies.finish()

    @pl.when(ids[0] == 1)
    def _():
        copies = Copies(sems)
        for piece, ref in ((hq_reg, hq), (dq_reg, dq)):
            stack_rows(copies, piece, ref, nm)
            clear_tail(ref, images * NM)
        stack_rows(copies, hk_reg, hk, nv)
        stack_rows(copies, [one.at[:, pl.ds(0, D)] for one in dkv_reg], dk, nv)
        stack_rows(copies, [one.at[:, pl.ds(D, D)] for one in dkv_reg], dv, nv)
        copies.finish()

    copies = Copies(sems)

    def multiply(j):
        return tn(left[lax.div(j, 2)], right[j]).astype(BF)

    give_blocks(copies, ids[1], dest[0].ndim == 6, multiply, out, dest)


def qkv_grad(groups, count, ids, *pieces):
    n = groups * GROUP * NV
    row = pltpu.VMEM((n, D), BF)
    main = halves(count, 3)
    scratch = [
        pltpu.VMEM((2, n, D), BF), pltpu.VMEM((3, n, D), BF), pltpu.VMEM((3, D, D), BF),
        pltpu.SemaphoreType.DMA((40,)),
    ]
    return pl.pallas_call(
        partial(qkv_kernel, groups, len(main)),
        in_specs=[SMEM] + [HBM] * (7 * groups),
        out_specs=[HBM] * len(main),
        out_shape=main,
        scratch_shapes=scratch,
        compiler_params=params(LIMIT),
        cost_estimate=cost(1e6, 1e5),
        name="qkv_grad",
    )(ids, *[ref for piece in pieces for ref in piece])


def place_kernel(groups, ids, visible, order_in, *refs):
    dx_in, lat_enc, res_enc, res_reg = (refs[i * groups : (i + 1) * groups] for i in range(4))
    block_out, grad_out, order, dx, lat, out, grads, sems = refs[4 * groups :]
    images = groups * GROUP
    nv, nm = GROUP * NV, GROUP * NM
    split_orders(order_in, order)

    def put_grad(i, put, value):
        high = value.astype(BF)
        low = (value - high.astype(F32)).astype(BF)
        grads[i] = nn(put, high) + nn(put, low)

    def write_grads():
        copies = Copies(sems)
        for i in range(images):
            copies.start(grads.at[i], grad_out.at[0, :, i, :])
        copies.finish()

    @pl.when(ids[0] == 0)
    def _():
        copies = Copies(sems)
        for piece, ref, size in ((dx_in, dx, nv), (lat_enc, lat, nv), (res_enc, out, nm)):
            stack_rows(copies, piece, ref, size)
        copies.finish()

        def put_image(i):
            put = place_matrix(order, i, 0, NV, 0, visible[i])
            put_side = place_matrix(order, i, FIRST, NM, visible[i], PATCH)
            put_grad(i, put, dx[rows_of(i, NV), :])
            block_out[0, i] = (nn(put, lat[rows_of(i, NV), :]) + nn(put_side, out[rows_of(i, NM), :])).astype(BF)

        loop(images, put_image)
        write_grads()

    @pl.when(ids[0] == 1)
    def _():
        copies = Copies(sems)
        stack_rows(copies, res_reg, out, nm)
        stack_rows(copies, [piece.at[pl.ds(0, nm)] for piece in dx_in], dx, nm)
        copies.finish()

        def put_image(i):
            put = place_matrix(order, i, FIRST, NM, visible[i], PATCH)
            put_grad(i, put, dx[rows_of(i, NM), :])
            block_out[0, i] = nn(put, out[rows_of(i, NM), :]).astype(BF)

        loop(images, put_image)
        write_grads()


def place(groups, ids, visible, order, *pieces):
    images = groups * GROUP
    n = images * NV
    outs = [struct((1, images, PATCH, D)), struct((1, PATCH, images, D), F32)]
    return pl.pallas_call(
        partial(place_kernel, groups),
        in_specs=[SMEM, SMEM, VMEM] + [HBM] * (4 * groups),
        out_specs=[VMEM, HBM],
        out_shape=outs,
        scratch_shapes=[
            pltpu.VMEM((images, 1, PATCH), jnp.int32), pltpu.VMEM((n, D), F32), pltpu.VMEM((n, D), BF),
            pltpu.VMEM((images * NM, D), BF), pltpu.VMEM((images, PATCH, D), F32), pltpu.SemaphoreType.DMA((8,)),
        ],
        compiler_params=params(LIMIT),
        cost_estimate=cost(1e6, 1e5),
        name="place",
    )(ids, visible, order, *[ref for piece in pieces for ref in piece])


BITS = (2, 4, 8)


def hop(value, bit):
    return lax.ppermute(value, "dp", [(i, i ^ bit) for i in range(16)])


def combine_kernel(jobs, given, ids, *refs):
    def parts_of(gone):
        return 4 if gone is None else max(1, -gone)

    used = sum(sum(parts_of(gone) for gone in terms) for terms, *_ in jobs)
    inputs, outs, scratch = list(refs[:used]), list(refs[used : used + given]), list(refs[used + given :])
    copies = Copies(scratch.pop())
    plans = []

    def fetch(term, gone, bits, own):
        if gone is not None and gone < 0:
            path = tuple(bits)
            skip = (slice(None),) * (3 - len(bits))
            started = [
                copies.start(ref.at[path], own.at[skip + (pl.ds(block, 1),)]) for block, ref in enumerate(term)
            ]
            return lambda: copies.wait(*started)
        if gone is not None:
            path = tuple(bits[gone:])
            copy = copies.start(term.at[path] if path else term, own)
            return lambda: copies.wait(copy)
        wide = len(bits) == 1
        first = copies.take(2 if wide else 1)
        rest = tuple(bits[2:])

        def piece(x, low):
            ref = term[2 * x + low]
            return ref.at[rest] if rest else ref

        for x in range(2):
            for low in range(2):
                if wide:
                    pl.when(bits[0] == x)(
                        lambda x=x, low=low: copies.begin(piece(x, low), own.at[low], first + low)
                    )
                else:
                    pl.when((bits[0] == x) & (bits[1] == low))(
                        lambda x=x, low=low: copies.begin(piece(x, low), own, first)
                    )

        def wait():
            if wide:
                for low in range(2):
                    copies.wait_at(piece(0, low), own.at[low], first + low)
            else:
                copies.wait_at(piece(0, 0), own, first)

        return wait

    for kinds, first, last, targets, finals in jobs:
        terms = [
            inputs.pop(0) if gone is not None and gone >= 0 else [inputs.pop(0) for _ in range(parts_of(gone))]
            for gone in kinds
        ]
        for target in targets:
            bits = []
            for bit in range(last):
                flip = bit >= first and (target >> (bit - first)) & 1
                bits.append(1 - ids[2 + bit] if flip else ids[2 + bit])
            owns = [scratch.pop(0) for _ in kinds]
            waits = [fetch(term, gone, bits, own) for term, gone, own in zip(terms, kinds, owns)]
            plans.append((waits, owns, last, finals, None if finals else outs.pop(0)))
    for waits, owns, last, finals, out in plans:
        for wait in waits:
            wait()
        spots = [()]
        for _ in range(3 - last):
            spots = [spot + (i,) for spot in spots for i in range(2)]
        for spot in spots:
            for j in range(owns[0].shape[-3]):
                value = owns[0][spot + (j,)].astype(F32)
                for more in owns[1:]:
                    value = value + more[spot + (j,)].astype(F32)
                if finals:
                    which, column = finals[j]
                    outs[which][:, column * D : (column + 1) * D] = value
                else:
                    out[spot + (j,)] = value.astype(BF)


def send_job(terms, first, last, targets=(1,)):
    return terms, first, last, targets, None


def final_job(terms, finals):
    return terms, 0, 3, (0,), finals


def combine(ids, *jobs, outs=()):
    shapes = [struct(shape, F32) for shape in outs]
    plans, inputs, scratch, copied = [], [], [], 0
    for terms, first, last, targets, finals in jobs:
        blocks, rows = terms[0].shape[-3:-1]
        kinds = tuple(
            6 - term.ndim if not isinstance(term, list) else None if term[0].ndim == 4 else -len(term) for term in terms
        )
        for term in terms:
            inputs += term if isinstance(term, list) else [term]
        plans.append((kinds, first, last, targets, finals))
        part = (2,) * (3 - last) + (blocks, rows, D)
        for _ in targets:
            scratch += [pltpu.VMEM(part, BF) for _ in terms]
            copied += sum(len(term) if isinstance(term, list) else 1 for term in terms)
            if finals is None:
                shapes.append(struct(part))
    scratch.append(pltpu.SemaphoreType.DMA((copied,)))
    return pl.pallas_call(
        partial(combine_kernel, tuple(plans), len(shapes)),
        in_specs=[SMEM] + [HBM] * len(inputs),
        out_specs=[VMEM] * len(shapes),
        out_shape=shapes,
        scratch_shapes=scratch,
        compiler_params=params(LIMIT),
        cost_estimate=cost(1e5, 1e4),
        name="combine",
    )(ids, *inputs)


def in_order(first, then):
    return lax.optimization_barrier((first, then))


def own_columns(rows, count):
    own = D // count
    me = lax.axis_index("dp")

    def part(block, wide):
        return lax.dynamic_slice_in_dim(block, me * wide, wide, block.ndim - 1)

    return (
        part(rows[:2], own),
        part(rows[2:6], own),
        part(rows[6:8].reshape(-1), 2 * own),
        part(rows[8:12].reshape(-1), 4 * own),
    )


def scatter_natural(block):
    shards = block.reshape(lax.axis_size("dp"), -1, D)
    return lax.psum_scatter(shards, "dp", scatter_dimension=0, tiled=True)[0].astype(F32)


def local(
    patch_rows, cotangent, patch_order, visible, qkv_weight, out_weight, up_weight, down_weight, norm_gains, biases,
    qv_bias, up_bias, target_qkv, target_out, target_up, target_down, target_gains, target_biases, target_qv_bias,
    target_up_bias,
):
    count = lax.axis_size("dp")
    tree = count == 16
    place_dp = lax.axis_index("dp")
    bits = [(place_dp // bit) % 2 for bit in (1,) + BITS]
    ids = jnp.stack([lax.axis_index("section")] + bits).astype(jnp.int32)
    groups = patch_order.shape[0] // GROUP
    weights = (qkv_weight, out_weight, up_weight, down_weight)
    targets = (target_qkv, target_out, target_up, target_down)
    vecs = (norm_gains, biases, qv_bias, up_bias)
    target_vecs = (target_gains, target_biases, target_qv_bias[None], target_up_bias[None])

    rows, cot = patch_rows.transpose(0, 2, 1, 3), cotangent.transpose(0, 2, 1, 3)
    calls = [
        encode(g, groups, ids, visible, patch_order, *vecs, rows, cot, weights) for g in range(groups)
    ]
    lat, x_e, hq_e, q_e, k_e, v_e, p_e, o_e, y1_e, h2_e, gp_e, a_e = zip(*[call[0] for call in calls])
    x_r, hq_r, q_r, dyb_r = calls[-1][1]
    sent = [lax.ppermute(piece, "section", [(0, 1)]) for piece in lat]
    vectors = (norm_gains, biases, qv_bias, up_bias)
    regressed = [regress(0, ids, visible, vectors, sent[0], x_r[0], q_r[0], dyb_r[0], weights)]
    back = [lax.ppermute(regressed[0][0], "section", [(1, 0)])]
    order_first, regressed[0] = in_order(patch_order, regressed[0])
    first, cot_e = target(0, groups, ids, visible, order_first, target_vecs, rows, cot, targets)
    res_e = [first]
    res_e[0], sent[1:] = in_order(res_e[0], sent[1:])
    for g in range(1, groups):
        regressed.append(regress(g, ids, visible, vectors, sent[g], x_r[g], q_r[g], dyb_r[g], weights))
        back.append(lax.ppermute(regressed[g][0], "section", [(1, 0)]))
    _, res_r, hk_r, dq_r, dkv_r, o_r, dy1b_r, h2_r, du_r, a_r, dy1_r, sums_r = zip(*regressed)

    def mlp(g, cot):
        return mlp_grad(ids, norm_gains, cot, back[g], up_weight, down_weight, y1_e[g], gp_e[g])

    def attention(g, dy1, sums=()):
        return attn_back(
            groups, len(sums) > 0, ids, norm_gains, sums, qkv_weight, out_weight, dy1, q_e[g], k_e[g], v_e[g], p_e[g],
            x_e[g], dq_r[g], dkv_r[g], dy1_r[g], x_r[g],
        )

    mlps = [mlp(g, cot_e[g]) for g in range(groups - 1)]
    attns = [attention(g, mlps[g][1]) for g in range(groups - 1)]
    last = groups - 1
    send = partial(combine, ids)
    attns, back[last] = in_order(attns, back[last])
    down, sums_down = down_grad(groups, count, ids, cot_e, back, a_e, a_r, dyb_r)
    cot_last = cot_e[last]
    down, cot_last = in_order(down, cot_last)
    mlps.append(mlp(last, cot_last))
    du_e, dy1_e, dy1b_e, sums_e = (list(piece) for piece in zip(*mlps))
    if tree:
        downs = [down[0], hop(down[1], 1)]
        (down_x,), du_e[last] = in_order(send(send_job(downs, 0, 1)), du_e[last])
        downs = downs + [hop(down_x, 2)]
    up, sums_up = up_grad(groups, count, ids, du_e, h2_e, dy1b_e, o_e, du_r, h2_r, dy1b_r, o_r)
    if tree:
        peers = (3, 2, 1)
        ups = [up[0], [hop(piece, 1) for piece in up[1:]]]
        (up_x,), downs = in_order(send(send_job(ups, 0, 1)), downs)
        ups = ups + [hop(up_x, 2)]
        down_z, dy1_e[last] = in_order(send(send_job(downs, 1, 3, peers)), dy1_e[last])
        down_got = [hop(one, 4 * peer) for one, peer in zip(down_z, peers)]
    sums_in = [piece[3] for piece in attns]
    attns.append(attention(last, dy1_e[last], (sums_down, sums_up, *sums_e, *sums_r, *sums_in)))
    dq_e, dkv_e, dx, small = (list(piece) for piece in zip(*attns))
    small = small[last]
    order_late = patch_order
    if tree:
        small = small + hop(small, 1)
        small, dq_e[last] = in_order(small, dq_e[last])
    attn = qkv_grad(groups, count, ids, dq_e, dkv_e, hq_e, hq_r, hk_r, dq_r, dkv_r)
    if tree:
        down_got, attn = in_order(down_got, attn)
        qkvs = [attn[0], [hop(piece, 1) for piece in attn[1:]]]
        qkvs, small = in_order(qkvs, small)
        got = hop(small, 2)
        (qkv_x, up_z), got = in_order(send(send_job(qkvs, 0, 1), send_job(ups, 1, 2)), got)
        small = small + got
        order_late, qkv_x = in_order(patch_order, qkv_x)
        qkvs = qkvs + [hop(qkv_x, 2)]
        ups = ups + [hop(up_z, 4)]
        got = hop(small, 4)
    res_e += [target(g, 0, ids, visible, order_late, target_vecs, rows, cot, targets)[0] for g in range(1, groups)]
    if tree:
        (up_z,), res_e = in_order(send(send_job(ups, 2, 3)), res_e)
        ups = ups + [hop(up_z, 8)]
        (qkv_z,), (res_e, got) = in_order(send(send_job(qkvs, 1, 2)), (res_e, got))
        qkvs = qkvs + [hop(qkv_z, 4)]
        small = small + got
        got = hop(small, 8)
    block_out, grad_rows = place(groups, ids, visible, patch_order, dx, lat, res_e, res_r)
    if tree:
        (qkv_z,), (block_out, grad_rows, got, ups[-1]) = in_order(
            send(send_job(qkvs, 2, 3)), (block_out, grad_rows, got, ups[-1])
        )
        qkvs = qkvs + [hop(qkv_z, 8)]
        small = small + got
        down_sum, up_sum, out_sum = send(
            final_job(downs + down_got, ((0, 0),)),
            final_job(ups, tuple((1, j) for j in range(4)) + ((2, 0),)),
            outs=((D // 4, D), (D // 16, 4 * D), (D // 16, D)),
        )
        qkvs[-1], (down_sum, up_sum, out_sum) = in_order(qkvs[-1], (down_sum, up_sum, out_sum))
        (qkv_sum,) = send(final_job(qkvs, ((0, 1), (0, 2), (0, 0))), outs=((D // 16, 3 * D),))
    else:
        down_sum = scatter_natural(down[0])
        up_sum = jnp.concatenate([scatter_natural(one) for one in up[:4]], axis=1)
        out_sum = scatter_natural(up[4])
        qkv_sum = jnp.concatenate([scatter_natural(attn[i]) for i in (2, 0, 1)], axis=1)
        small = lax.psum(small, "dp")
    grad_rows = grad_rows.transpose(0, 2, 1, 3)
    gains, bias_rows, qv_rows, up_rows = own_columns(small, count)
    return (
        block_out,
        grad_rows,
        qkv_sum[None],
        out_sum[None],
        up_sum[None],
        down_sum[None],
        gains[None],
        bias_rows[None],
        qv_rows[None],
        up_rows[None],
    )


def solution(mesh):
    three, four = P("section", None, None), P("section", "dp", None, None)
    grad = P("section", "dp", None)
    return jax.shard_map(
        local,
        mesh=mesh,
        in_specs=(four, four, P("dp", None), P("dp"), three, three, three, three, three, three,
                  P("section", None), P("section", None), P(), P(), P(), P(), P(), P(), P(), P()),
        out_specs=(four, four, grad, grad, grad, grad, P("section", None, "dp"), P("section", None, "dp"),
                   P("section", "dp"), P("section", "dp")),
        check_vma=False,
    )
```

```python
from functools import partial

import jax
import jax.numpy as jnp
from jax import lax
from jax.experimental import pallas as pl
from jax.experimental.pallas import tpu as pltpu
from jax.sharding import PartitionSpec as P

HEADS = 12
PATCH = 196
D = 768
FF = 3072
EPS = 1e-06
NV = 144
NM = 128
FIRST = PATCH - NM
GROUP = 2
CHUNK = 32

BF = jnp.bfloat16
F32 = jnp.float32
MIB = 1024 * 1024
LIMIT = 62

HBM = pl.BlockSpec(memory_space=pl.ANY)
VMEM = pl.BlockSpec(memory_space=pltpu.VMEM)
SMEM = pl.BlockSpec(memory_space=pltpu.SMEM)


def nn(a, b):
    return jnp.dot(a, b, preferred_element_type=F32)


def nt(a, b):
    return lax.dot_general(a, b, (((1,), (1,)), ((), ())), preferred_element_type=F32)


def tn(a, b):
    return lax.dot_general(a, b, (((0,), (0,)), ((), ())), preferred_element_type=F32)


def loop(count, body, unroll=1):
    def step(i, carry):
        for u in range(unroll):
            body(i * unroll + u)
        return carry

    if count == unroll:
        step(0, 0)
    else:
        lax.fori_loop(0, count // unroll, step, 0)


def unroll_of(count):
    return next(u for u in (4, 3, 2, 1) if count % u == 0)


def rows_of(i, size):
    return pl.ds(pl.multiple_of(i * size, size), size)


def f32_row(ref, row, col=0, width=D):
    return ref[pl.ds(row, 1), pl.ds(col, width)].astype(F32)


class Copies:
    def __init__(self, sems):
        self.sems = sems
        self.used = 0
        self.open = []

    def start(self, src, dst):
        copy = pltpu.make_async_copy(src, dst, self.sems.at[self.used])
        self.used += 1
        copy.start()
        self.open.append(copy)
        return copy

    def wait(self, *copies):
        for copy in copies:
            copy.wait()
            self.open = [one for one in self.open if one is not copy]

    def finish(self):
        self.wait(*list(self.open))

    def take(self, count):
        self.used += count
        return self.used - count

    def part(self):
        other = Copies(self.sems)
        other.used = self.used
        return other

    def begin(self, src, dst, at):
        pltpu.make_async_copy(src, dst, self.sems.at[at]).start()

    def wait_at(self, src, dst, at):
        pltpu.make_async_copy(src, dst, self.sems.at[at]).wait()


def gelu_pair(u):
    size = jnp.abs(u)
    base = 1.0 + (0.3275911 * 0.7071067811865476) * size
    guess = pl.reciprocal(base, approx=True)
    t = guess * (2.0 - base * guess)
    ex = jnp.exp2((u * u) * (-0.5 * 1.4426950408889634))
    poly = 0.5306027145 * t - 0.7265760135
    poly = poly * t + 0.7107068705
    poly = poly * t - 0.142248368
    poly = poly * t + 0.127414796
    tail = poly * t * ex
    phi = jnp.where(u >= 0.0, 1.0 - tail, tail)
    return u * phi, phi + u * (0.3989422804014327 * ex)


def norm_rows(src, dst, rows, gain, shift):
    def body(i):
        sel = rows_of(i, CHUNK)
        x = src[sel, :].astype(F32)
        centered = x - jnp.mean(x, axis=-1, keepdims=True)
        var = jnp.mean(centered * centered, axis=-1, keepdims=True)
        dst[sel, :] = (centered * lax.rsqrt(var + EPS) * gain + shift).astype(BF)

    loop(rows // CHUNK, body, unroll_of(rows // CHUNK))


def norm_back(src, grad, base, write, rows, gain):
    count = rows // CHUNK
    unroll = 3 if count % 3 == 0 else 2

    def step(i, carry):
        for u in range(unroll):
            carry = one(i * unroll + u, carry)
        return carry

    def one(i, carry):
        d_gain, d_shift = carry
        sel = rows_of(i, CHUNK)
        x = src[sel, :].astype(F32)
        dh = grad[sel, :]
        centered = x - jnp.mean(x, axis=-1, keepdims=True)
        var = jnp.mean(centered * centered, axis=-1, keepdims=True)
        rstd = lax.rsqrt(var + EPS)
        hat = centered * rstd
        g = dh * gain
        part = dh * hat
        dx = rstd * (
            g
            - jnp.mean(g, axis=-1, keepdims=True)
            - hat * jnp.mean(g * hat, axis=-1, keepdims=True)
        )
        if base is not None:
            dx = dx + base[sel, :].astype(F32)
        write(sel, dx)
        d_gain = d_gain + jnp.sum(part.reshape(CHUNK // 8, 8, D), axis=0)
        d_shift = d_shift + jnp.sum(dh.reshape(CHUNK // 8, 8, D), axis=0)
        return d_gain, d_shift

    zero = jnp.zeros((8, D), F32)
    d_gain, d_shift = lax.fori_loop(0, count // unroll, step, (zero, zero))
    return jnp.sum(d_gain, axis=0, keepdims=True), jnp.sum(d_shift, axis=0, keepdims=True)


def column_sum(ref, rows, col=0, width=D):
    def step(i, carry):
        x = ref[rows_of(i, CHUNK), pl.ds(col, width)].astype(F32)
        return carry + jnp.sum(x.reshape(CHUNK // 8, 8, width), axis=0)

    total = lax.fori_loop(0, rows // CHUNK, step, jnp.zeros((8, width), F32))
    return jnp.sum(total, axis=0, keepdims=True)


def as_bf16(flags):
    return jnp.where(flags, 1.0, 0.0).astype(BF)


def pick_matrix(order, image, start, count, low, high):
    row = order[image, :, pl.ds(start, count)].astype(F32)
    images = order.shape[0]
    col = jnp.broadcast_to(row, (8, count)).T[:, 0:1].astype(jnp.int32)
    rank = start + lax.broadcasted_iota(jnp.int32, (count, 1), 0)
    col = jnp.where((rank >= low) & (rank < high), col * images + image, -1)
    return as_bf16(col == lax.broadcasted_iota(jnp.int32, (count, PATCH * images), 1))


def place_matrix(order, image, start, count, low, high):
    row = order[image, :, pl.ds(start, count)]
    rank = start + lax.broadcasted_iota(jnp.int32, (1, count), 1)
    row = jnp.where((rank >= low) & (rank < high), row, -1)
    return as_bf16(row == lax.broadcasted_iota(jnp.int32, (PATCH, count), 0))


def flatten(rows, flat):
    flat[...] = rows[...].reshape(flat.shape)


def split_orders(order, split):
    for image in range(split.shape[0]):
        split[image] = order[image : image + 1, :]


def split_pair(pair):
    lane = lax.broadcasted_iota(jnp.int32, pair.shape, 1)
    zero = jnp.zeros_like(pair)
    return jnp.concatenate([jnp.where(lane < 64, pair, zero), jnp.where(lane < 64, zero, pair)], axis=0)


def join_rows(both):
    rows = both.shape[0] // 2
    lane = lax.broadcasted_iota(jnp.int32, (rows, 128), 1)
    return jnp.where(lane < 64, both[:rows], both[rows:])


def join_columns(both):
    rows = both.shape[1] // 2
    return jnp.concatenate([both[:64, :rows], both[64:, rows:]], axis=0).T


PAIRS = HEADS // 2
STEP = 6


def each_pair_group(images, body):
    def group(i):
        image = i // (PAIRS // STEP)
        first = (i % (PAIRS // STEP)) * STEP
        pairs = [first + step for step in range(STEP)]
        body(image, [image * PAIRS + pair for pair in pairs], [pl.ds(pl.multiple_of(pair * 128, 128), 128) for pair in pairs])

    loop(images * (PAIRS // STEP), group)


def softmax(scores, axis):
    ex = jnp.exp(scores - jnp.max(scores, axis=axis, keepdims=True))
    return (ex * (1.0 / jnp.sum(ex, axis=axis, keepdims=True))).astype(BF)


def score_back(probs, d_probs, axis):
    wide = probs.astype(F32)
    return (wide * (d_probs - jnp.sum(d_probs * wide, axis=axis, keepdims=True))).astype(BF)


def attention_by_rows(images, n, q, k, v, p, o, count_of):
    def body(image, slots, lanes):
        sel = rows_of(image, n)
        ok = lax.broadcasted_iota(jnp.int32, (1, n), 1) < count_of(image)
        scores = [nt(split_pair(q[sel, at]), k[sel, at]) for at in lanes]
        probs = [softmax(jnp.where(ok, one, -1000000000.0), 1) for one in scores]
        for slot, one in zip(slots, probs):
            p[slot] = one
        mixed = [nn(one, v[sel, at]) for one, at in zip(probs, lanes)]
        for at, one in zip(lanes, mixed):
            o[sel, at] = join_rows(one).astype(BF)

    each_pair_group(images, body)


def attention_by_columns(images, nk, q, k, v, p, o, key_ok):
    def body(image, slots, lanes):
        qs, ks = rows_of(image, NM), rows_of(image, nk)
        ok = key_ok(image)
        scores = [nt(k[ks, at], split_pair(q[qs, at])) for at in lanes]
        probs = [softmax(jnp.where(ok, one, -1000000000.0), 0) for one in scores]
        if p is not None:
            for slot, one in zip(slots, probs):
                p[slot] = one
        mixed = [tn(v[ks, at], one) for one, at in zip(probs, lanes)]
        for at, one in zip(lanes, mixed):
            o[qs, at] = join_columns(one).astype(BF)

    each_pair_group(images, body)


def attention_back_rows(images, n, q, k, v, p, do, dq, dkv):
    def body(image, slots, lanes):
        sel = rows_of(image, n)
        d_mixed = [split_pair(do[sel, at]) for at in lanes]
        d_probs = [nt(one, v[sel, at]) for one, at in zip(d_mixed, lanes)]
        d_scores = [score_back(p[slot], one, 1) for slot, one in zip(slots, d_probs)]
        d_values = [tn(p[slot], one) for slot, one in zip(slots, d_mixed)]
        d_query = [nn(one, k[sel, at]) for one, at in zip(d_scores, lanes)]
        d_keys = [tn(one, split_pair(q[sel, at])) for one, at in zip(d_scores, lanes)]
        for at, value, query, key in zip(lanes, d_values, d_query, d_keys):
            dq[sel, at] = (join_rows(query) * 0.125).astype(BF)
            dkv[sel, at] = key.astype(BF)
            dkv[sel, pl.ds(pl.multiple_of(D + at.start, 128), 128)] = value.astype(BF)

    each_pair_group(images, body)


def attention_back_columns(images, nk, q, k, v, p, do, dq, dkv):
    def body(image, slots, lanes):
        qs, ks = rows_of(image, NM), rows_of(image, nk)
        d_mixed = [split_pair(do[qs, at]) for at in lanes]
        d_probs = [nt(v[ks, at], one) for one, at in zip(d_mixed, lanes)]
        d_scores = [score_back(p[slot], one, 0) for slot, one in zip(slots, d_probs)]
        d_values = [nn(p[slot], one) for slot, one in zip(slots, d_mixed)]
        d_query = [tn(k[ks, at], one) for one, at in zip(d_scores, lanes)]
        d_keys = [nn(one, split_pair(q[qs, at])) for one, at in zip(d_scores, lanes)]
        for at, value, query, key in zip(lanes, d_values, d_query, d_keys):
            dq[qs, at] = (join_columns(query) * 0.125).astype(BF)
            dkv[ks, at] = key.astype(BF)
            dkv[ks, pl.ds(pl.multiple_of(D + at.start, 128), 128)] = value.astype(BF)

    each_pair_group(images, body)


HALF = 512


def mlp_forward(rows, h2, w1, w2, up_b, u, a, gp, tile, acc, out, base):
    acc[...] = base()
    steps = FF // HALF

    def multiply(t):
        u[t % 2] = nn(h2[...], w1[:, t * HALF : (t + 1) * HALF])

    def add(t):
        acc[...] += nn(tile[t % 2], w2[t * HALF : (t + 1) * HALF, :])

    multiply(0)
    for t in range(steps):
        if t + 1 < steps:
            multiply(t + 1)
        if t > 0:
            add(t - 1)
        for c in range(0, HALF, 256):
            at = slice(t * HALF + c, t * HALF + c + 256)
            shift = up_b[0:1, at].astype(F32)
            for r in range(0, rows, CHUNK):
                sel = slice(r, r + CHUNK)
                value, slope = gelu_pair(u[t % 2, sel, c : c + 256] + shift)
                low = value.astype(BF)
                tile[t % 2, sel, c : c + 256] = low
                if a is not None:
                    a[sel, at] = low
                if gp is not None:
                    gp[sel, at] = slope.astype(BF)
    add(steps - 1)
    out[...] = acc[...].astype(BF)


def mlp_back(rows, dyb, gp, w1, w2, du, u, acc, ready=lambda i, which: None):
    acc[...] = jnp.zeros_like(acc)

    def body(i):
        cols = [pl.ds(pl.multiple_of((2 * i + part) * HALF, HALF), HALF) for part in range(2)]
        ready(i, 0)
        for part in range(2):
            u[part] = nt(dyb[...], w2[cols[part], :])
        ready(i, 1)
        for part in range(2):
            for r in range(0, rows, CHUNK):
                sel = slice(r, r + CHUNK)
                du[sel, cols[part]] = (gp[sel, cols[part]].astype(F32) * u[part, sel, :]).astype(BF)
            acc[...] += nt(du[:, cols[part]], w1[:, cols[part]])

    loop(FF // (2 * HALF), body)


def project(count, rows, left, weight, first, write):
    def body(j):
        write(j, nn(left[...], weight[:, pl.ds(pl.multiple_of((first + j) * D, D), D)]))

    loop(count, body)


def set_biases(ref, bias):
    ref[0] = f32_row(bias, 0)
    ref[1] = jnp.zeros((1, D), F32)
    ref[2] = f32_row(bias, 0, D)


def cost(flops, nbytes):
    return pl.CostEstimate(flops=int(flops), bytes_accessed=int(nbytes), transcendentals=0)


def params(mib):
    return pltpu.CompilerParams(vmem_limit_bytes=mib * MIB)


def struct(shape, dtype=BF):
    return jax.ShapeDtypeStruct(shape, dtype)


def start_weights(copies, sources, scratch):
    return [copies.start(src, dst) for src, dst in zip(sources, scratch)]


def encode_kernel(group, groups, ids, visible, order_in, gains, biases, qvb, upb, rows, cot, wqkv, wo, w1, w2,
                  lat_out, x_out, hq_out, q_out, k_out, v_out, p_out, o_out, y1_out, h2_out, gp_out, a_out, *refs):
    ready, refs = refs[: 4 * groups], refs[4 * groups :]
    (order, rows_v, flat, sqkv, so, s1, s2, x, hq, qkv, p, o, y1, h2, gp, a, u, tile, acc, shifts, lat, sems) = refs
    n = GROUP * NV
    split_orders(order_in, order)

    @pl.when(ids[0] == 0)
    def _():
        copies = Copies(sems)
        got_rows = copies.start(rows.at[0], rows_v)
        got_qkv, got_o, got_1, got_2 = start_weights(
            copies, (wqkv.at[0], wo.at[0], w1.at[0], w2.at[0]), (sqkv, so, s1, s2)
        )
        gain, bias = gains.at[0], biases.at[0]
        set_biases(shifts, qvb)
        copies.wait(got_rows)
        flatten(rows_v, flat)

        def pick_rows(i):
            image = group * GROUP + i
            pick = pick_matrix(order, image, 0, NV, 0, visible[image])
            x[rows_of(i, NV), :] = nn(pick, flat[...]).astype(BF)

        loop(GROUP, pick_rows)
        copies.start(x, x_out)
        norm_rows(x, hq, n, f32_row(gain, 0), f32_row(bias, 0))
        copies.start(hq, hq_out)
        copies.wait(got_qkv)

        def keep(j, value):
            scale = jnp.where(j == 0, 0.125, 1.0)
            qkv[j] = ((value + shifts[j]).astype(BF).astype(F32) * scale).astype(BF)

        project(3, n, hq, sqkv, 0, keep)
        q, k, v = qkv.at[0], qkv.at[1], qkv.at[2]
        copies.start(q, q_out)
        copies.start(k, k_out)
        copies.start(v, v_out)
        attention_by_rows(GROUP, NV, q, k, v, p, o, lambda i: visible[group * GROUP + i])
        copies.start(p, p_out)
        copies.start(o, o_out)
        copies.wait(got_o)
        y1[...] = nn(o[...], so[...]) + f32_row(bias, 1) + x[...].astype(F32)
        copies.start(y1, y1_out)
        norm_rows(y1, h2, n, f32_row(gain, 1), f32_row(bias, 2))
        copies.start(h2, h2_out)
        copies.wait(got_1, got_2)
        mlp_forward(n, h2, s1, s2, upb, u, a, gp, tile, acc, lat, lambda: y1[...] + f32_row(bias, 3))
        copies.start(gp, gp_out)
        copies.start(a, a_out)
        copies.start(lat, lat_out)
        copies.finish()

    if group == groups - 1:

        @pl.when(ids[0] == 1)
        def _():
            copies = Copies(sems)
            m = GROUP * NM
            x_out, hq_out, q_out, dyb_out = (ready[i * groups : (i + 1) * groups] for i in range(4))
            gain, bias = gains.at[0], biases.at[0]
            got_rows = copies.start(rows.at[0], rows_v)
            got_q = copies.start(wqkv.at[0, :, pl.ds(0, D)], so)
            copies.wait(got_rows)
            flatten(rows_v, flat)
            got_cot = copies.start(cot.at[0], rows_v)
            top = pl.ds(0, m)

            def pick_group(g):
                def pick_rows(i):
                    image = g * GROUP + i
                    pick = pick_matrix(order, image, FIRST, NM, visible[image], PATCH)
                    x[rows_of(i, NM), :] = nn(pick, flat[...]).astype(BF)

                loop(GROUP, pick_rows)

            for g in range(groups):
                pick_group(g)
                norm_rows(x, hq, m, f32_row(gain, 0), f32_row(bias, 0))
                sent = [copies.start(x.at[top], x_out[g]), copies.start(hq.at[top], hq_out[g])]
                if g == 0:
                    copies.wait(got_q)
                q = qkv.at[g]
                q[top, :] = ((nn(hq[top, :], so[...]) + f32_row(qvb, 0)).astype(BF) * 0.125).astype(BF)
                copies.start(q.at[top], q_out[g])
                copies.wait(*sent)
            copies.wait(got_cot)
            flatten(rows_v, flat)
            for g in range(groups):
                pick_group(g)
                copies.wait(copies.start(x.at[top], dyb_out[g]))
            copies.finish()


def encode(group, groups, ids, visible, order, gains, biases, qvb, upb, rows, cot, weights):
    n = GROUP * NV
    images = order.shape[0]
    row, wide = struct((n, D)), struct((n, FF))
    heads = struct((GROUP * PAIRS, 2 * NV, NV))
    outs = [row] * 6 + [heads, row, struct((n, D), F32), row, wide, wide] + [struct((GROUP * NM, D))] * (4 * groups)
    vm = lambda s: pltpu.VMEM(s.shape, s.dtype)
    scratch = [
        pltpu.VMEM((images, 1, PATCH), jnp.int32),
        pltpu.VMEM((PATCH, images, D), BF), pltpu.VMEM((PATCH * images, D), BF),
        pltpu.VMEM((D, 3 * D), BF), pltpu.VMEM((D, D), BF), pltpu.VMEM((D, FF), BF), pltpu.VMEM((FF, D), BF),
        vm(row), vm(row), pltpu.VMEM((3, n, D), BF), vm(heads), vm(row), pltpu.VMEM((n, D), F32), vm(row),
        vm(wide), vm(wide), pltpu.VMEM((2, n, HALF), F32), pltpu.VMEM((2, n, HALF), BF), pltpu.VMEM((n, D), F32),
        pltpu.VMEM((3, 1, D), F32), vm(row),
        pltpu.SemaphoreType.DMA((24,)),
    ]
    got = pl.pallas_call(
        partial(encode_kernel, group, groups),
        in_specs=[SMEM, SMEM] + [VMEM] * 5 + [HBM] * 6,
        out_specs=[HBM] * len(outs),
        out_shape=outs,
        scratch_shapes=scratch,
        compiler_params=params(LIMIT),
        cost_estimate=cost(2 * n * 12 * D * D, 25e6),
        name="encode",
    )(ids, visible, order, gains, biases, qvb, upb, rows, cot, *weights)
    ready = got[12:]
    return got[:12], [ready[i * groups : (i + 1) * groups] for i in range(4)]


def block_end(copies, n, got_weights, so, s1, s2, bias, gain, up_b, x, o, y1, h2, a, gp, u, tile, acc, res):
    got_o, got_1, got_2 = got_weights
    copies.wait(got_o)
    y1[...] = nn(o[...], so[...]) + f32_row(bias, 1) + x[...].astype(F32)
    norm_rows(y1, h2, n, f32_row(gain, 1), f32_row(bias, 2))
    copies.wait(got_1, got_2)
    mlp_forward(n, h2, s1, s2, up_b, u, a, gp, tile, acc, res, lambda: y1[...] + f32_row(bias, 3))


def target_kernel(group, ids, visible, order_in, gain, bias, qvb, upb, rows, wqkv, wo, w1, w2, res_out,
                  order, rows_v, flat, sqkv, so, s1, s2, x, hq, qkv, o, y1, h2, u, tile, acc, shifts, res, sems):
    n = GROUP * NM
    q, k, v = qkv.at[0], qkv.at[1], qkv.at[2]

    @pl.when(ids[0] == 0)
    def _():
        copies = Copies(sems)
        split_orders(order_in, order)
        got_rows = copies.start(rows.at[0], rows_v)
        got_qkv = copies.start(wqkv, sqkv)
        got_weights = start_weights(copies, (wo, w1, w2), (so, s1, s2))
        set_biases(shifts, qvb)
        copies.wait(got_rows)
        flatten(rows_v, flat)

        def pick_rows(i):
            image = group * GROUP + i
            pick = pick_matrix(order, image, FIRST, NM, visible[image], PATCH)
            x[rows_of(i, NM), :] = nn(pick, flat[...]).astype(BF)

        loop(GROUP, pick_rows)
        norm_rows(x, hq, n, f32_row(gain, 0), f32_row(bias, 0))
        copies.wait(got_qkv)

        def keep(j, value):
            scale = jnp.where(j == 0, 0.125, 1.0)
            qkv[j] = ((value + shifts[j]).astype(BF).astype(F32) * scale).astype(BF)

        project(3, n, hq, sqkv, 0, keep)

        def key_ok(i):
            return lax.broadcasted_iota(jnp.int32, (NM, 1), 0) + FIRST >= visible[group * GROUP + i]

        attention_by_columns(GROUP, NM, q, k, v, None, o, key_ok)
        block_end(copies, n, got_weights, so, s1, s2, bias, gain, upb, x, o, y1, h2, None, None, u, tile, acc, res)
        copies.start(res, res_out)
        copies.finish()


def target(group, ids, visible, order, vecs, rows, weights):
    n = GROUP * NM
    images = order.shape[0]
    row, full = pltpu.VMEM((n, D), BF), pltpu.VMEM((n, D), F32)
    return pl.pallas_call(
        partial(target_kernel, group),
        in_specs=[SMEM, SMEM] + [VMEM] * 5 + [HBM] * 5,
        out_specs=HBM,
        out_shape=struct((n, D)),
        scratch_shapes=[
            pltpu.VMEM((images, 1, PATCH), jnp.int32),
            pltpu.VMEM((PATCH, images, D), BF), pltpu.VMEM((PATCH * images, D), BF),
            pltpu.VMEM((D, 3 * D), BF), pltpu.VMEM((D, D), BF), pltpu.VMEM((D, FF), BF), pltpu.VMEM((FF, D), BF),
            row, row, pltpu.VMEM((3, n, D), BF), row, full, row,
            pltpu.VMEM((2, n, HALF), F32), pltpu.VMEM((2, n, HALF), BF), full, pltpu.VMEM((3, 1, D), F32), row,
            pltpu.SemaphoreType.DMA((8,)),
        ],
        compiler_params=params(LIMIT),
        cost_estimate=cost(1e6, 1e5),
        name="target",
    )(ids, visible, order, *vecs, rows, *weights)


def regress_kernel(group, ids, visible, gains, biases, qvb, upb, lat_in, x_in, q_in, dyb_in, wqkv, wo, w1, w2,
                   dlat_out, res_out, hk_out, dq_out, dkv_out, o_out, dy1b_out, h2_out, du_out, a_out, dy1_out,
                   sums_out,
                   sqkv, so, s1, s2, x, lat, hk, q, kv, p, o, y1, h2, gp, a, u, tile, acc, shifts,
                   res, dyb, du, dy1, dy1b, do, dq, dkv, dh, dlat, sums, sems):
    n, m = GROUP * NM, GROUP * NV
    k, v = kv.at[0], kv.at[1]

    @pl.when(ids[0] == 1)
    def _():
        copies = Copies(sems)
        gain, bias = gains.at[0], biases.at[0]
        got_lat = copies.start(lat_in, lat)
        got_kv = copies.start(wqkv.at[0, :, pl.ds(D, 2 * D)], sqkv)
        got_q = copies.start(q_in, q)
        got_x = copies.start(x_in, x)
        got_weights = start_weights(copies, (wo.at[0], w1.at[0], w2.at[0]), (so, s1, s2))
        got_dyb = copies.start(dyb_in, dyb)
        set_biases(shifts, qvb)
        copies.wait(got_lat)
        norm_rows(lat, hk, m, f32_row(gain, 0), f32_row(bias, 0))
        copies.start(hk, hk_out)
        copies.wait(got_kv)

        def keep_kv(j, value):
            kv[j] = (value + shifts[j + 1]).astype(BF)

        project(2, m, hk, sqkv, 0, keep_kv)
        copies.wait(got_q, got_x)

        def key_ok(i):
            return lax.broadcasted_iota(jnp.int32, (NV, 1), 0) < visible[group * GROUP + i]

        attention_by_columns(GROUP, NV, q, k, v, p, o, key_ok)
        copies.start(o, o_out)
        block_end(copies, n, got_weights, so, s1, s2, bias, gain, upb, x, o, y1, h2, a, gp, u, tile, acc, res)
        copies.start(res, res_out)
        copies.start(h2, h2_out)
        copies.start(a, a_out)
        copies.wait(got_dyb)
        mlp_back(n, dyb, gp, s1, s2, du, u, acc)
        copies.start(du, du_out)

        def keep(sel, dx):
            dy1[sel, :] = dx
            dy1b[sel, :] = dx.astype(BF)

        g2, b2 = norm_back(y1, acc, dyb, keep, n, f32_row(gain, 1))
        copies.start(dy1, dy1_out)
        copies.start(dy1b, dy1b_out)
        do[...] = nt(dy1b[...], so[...]).astype(BF)
        attention_back_columns(GROUP, NV, q, k, v, p, do, dq, dkv)
        copies.start(dq, dq_out)
        copies.start(dkv, dkv_out)
        dh[...] = nt(dkv[:, :D], sqkv[:, :D])
        dh[...] += nt(dkv[:, D:], sqkv[:, D:])

        def keep_side(sel, dx):
            dlat[sel, :] = dx.astype(BF)

        gk, bk = norm_back(lat, dh, None, keep_side, m, f32_row(gain, 0))
        copies.start(dlat, dlat_out)
        for row, value in enumerate((gk, g2, bk, b2)):
            sums[pl.ds(row, 1), :] = value
        copies.start(sums, sums_out)
        copies.finish()


def regress(group, ids, visible, vecs, lat, x, q, dyb, weights):
    n, m = GROUP * NM, GROUP * NV
    row, side, wide = struct((n, D)), struct((m, D)), struct((n, FF))
    pair = struct((m, 2 * D))
    outs = [side, row, side, row, pair, row, row, row, wide, wide, struct((n, D), F32), struct((8, D), F32)]
    vm = lambda s: pltpu.VMEM(s.shape, s.dtype)
    full, fside = pltpu.VMEM((n, D), F32), pltpu.VMEM((m, D), F32)
    scratch = [
        pltpu.VMEM((D, 2 * D), BF), pltpu.VMEM((D, D), BF), pltpu.VMEM((D, FF), BF), pltpu.VMEM((FF, D), BF),
        vm(row), vm(side), vm(side), vm(row), pltpu.VMEM((2, m, D), BF),
        pltpu.VMEM((GROUP * PAIRS, NV, 2 * NM), BF), vm(row), full, vm(row), vm(wide), vm(wide),
        pltpu.VMEM((2, n, HALF), F32), pltpu.VMEM((2, n, HALF), BF), full, pltpu.VMEM((3, 1, D), F32),
        vm(row), vm(row), vm(wide), full, vm(row), vm(row), vm(row), vm(pair), fside, vm(side),
        pltpu.VMEM((8, D), F32),
        pltpu.SemaphoreType.DMA((24,)),
    ]
    return pl.pallas_call(
        partial(regress_kernel, group),
        in_specs=[SMEM, SMEM] + [VMEM] * 4 + [HBM] * 8,
        out_specs=[HBM] * len(outs),
        out_shape=outs,
        scratch_shapes=scratch,
        compiler_params=params(LIMIT),
        cost_estimate=cost(4 * n * 12 * D * D, 25e6),
        name="regress",
    )(ids, visible, *vecs, lat, x, q, dyb, *weights)


def stack_rows(copies, pieces, ref, size):
    return [copies.start(piece, ref.at[pl.ds(i * size, size)]) for i, piece in enumerate(pieces)]


class BlockLoads:
    def __init__(self, copies, ids, groups, blocks, sources, dest):
        self.copies, self.ids, self.groups, self.sources, self.dest = copies, ids, groups, sources, dest
        self.first = copies.take(groups * blocks)

    def each(self, role, j, like, act):
        for g, (src, size) in enumerate(self.sources(role, like)):
            act(src, self.dest(j).at[pl.ds(g * size, size)], self.first + j * self.groups + g)

    def begin(self, role, j):
        self.each(role, j, j, self.copies.begin)

    def wait(self, j, like=0):
        for role in range(2):
            pl.when(self.ids[0] == role)(lambda role=role: self.each(role, j, like, self.copies.wait_at))


def clear_tail(ref, used):
    ref[pl.ds(used, ref.shape[0] - used), :] = jnp.zeros((ref.shape[0] - used, ref.shape[1]), ref.dtype)


def halves(count, blocks):
    rows = D // 16
    if count == 16:
        return [struct((2, 2, 2, blocks, rows, D))] + [struct((2, blocks, rows, D))] * 4
    return [struct((D, D))] * blocks


def give_blocks(copies, core, tree, left_right, out, dest):
    size = 8 if tree else 1
    blocks = out.shape[0]
    first = copies.take(blocks * size)

    def send(j, act):
        if not tree:
            for block in range(blocks):
                pl.when(j == block)(lambda block=block: act(out.at[block], dest[block], first + block))
            return
        view = out.at[j].reshape(2, 2, 2, 2, D // 16, D)
        for x in range(2):
            for low in range(2):
                at = first + j * size + 4 * x + 2 * low
                act(view.at[:, low, x, core], dest[0].at[x, low, :, j], at)
                act(view.at[:, low, x, 1 - core], dest[1 + 2 * x + low].at[:, j], at + 1)

    def body(j):
        out[j] = left_right(j)
        send(j, copies.begin)

    loop(blocks, body)
    loop(blocks, lambda j: send(j, copies.wait_at))


def give_rows(copies, core, tree, multiply, out, dest):
    size = 4 if tree else 1
    first = copies.take(4 * size)

    def send(j, act):
        if not tree:
            act(out.at[j], dest[0].at[pl.ds(pl.multiple_of(j * D, D), D)], first + j)
            return
        view = out.at[j].reshape(2, 2, D // 4, D)
        low, high = lax.rem(j, 2), lax.div(j, 2)
        for x in range(2):
            at = first + j * size + 2 * x
            act(view.at[x, core], dest[0].at[x, low, high, 0], at)
            act(view.at[x, 1 - core], dest[1].at[x, low, high, 0], at + 1)

    def body(j):
        out[j] = multiply(j)
        send(j, copies.begin)

    loop(4, body)
    loop(4, lambda j: send(j, copies.wait_at))


def down_kernel(groups, parts, ids, *refs):
    cot, lat, a_enc, a_reg, dyb_reg = (refs[i * groups : (i + 1) * groups] for i in range(5))
    refs = refs[5 * groups :]
    dest, refs = refs[:parts], refs[parts:]
    sums_out, cot_v, dyb, a, dlat, out, sums, sems = refs
    images = groups * GROUP
    nv, nm = GROUP * NV, GROUP * NM

    copies = Copies(sems)
    pieces = (a_enc, a_reg)

    def sources(role, j):
        return [(one.at[:, pl.ds(j * D, D)], (nv, nm)[role]) for one in pieces[role]]

    loads = BlockLoads(copies, ids, groups, 4, sources, lambda j: a.at[j])

    @pl.when(ids[0] == 0)
    def _():
        early = copies.part()
        got = stack_rows(early, cot, cot_v, nv) + stack_rows(early, lat, dlat, nv)
        for j in range(4):
            loads.begin(0, j)
        early.wait(*got)
        dyb[...] = (cot_v[...].astype(F32) + dlat[...].astype(F32)).astype(BF)

    @pl.when(ids[0] == 1)
    def _():
        early = copies.part()
        got = stack_rows(early, dyb_reg, dyb, nm)
        for j in range(4):
            loads.begin(1, j)
            clear_tail(a.at[j], images * NM)
        clear_tail(dyb, images * NM)
        early.wait(*got)

    copies.take(2 * groups)

    def multiply(j):
        loads.wait(j)
        return tn(a[j], dyb[...]).astype(BF)

    give_rows(copies, ids[1], parts == 2, multiply, out, dest)
    sums[...] = jnp.broadcast_to(column_sum(dyb, images * NV), (8, D))
    copies.start(sums, sums_out)
    copies.finish()


def down_grad(groups, count, ids, cot, dlat, a_enc, a_reg, dyb_reg):
    n = groups * GROUP * NV
    main = [struct((2, 2, 2, 1, D // 4, D))] * 2 if count == 16 else [struct((FF, D))]
    outs = main + [struct((8, D), F32)]
    row = pltpu.VMEM((n, D), BF)
    scratch = [
        row, row, pltpu.VMEM((4, n, D), BF), row, pltpu.VMEM((4, D, D), BF), pltpu.VMEM((8, D), F32),
        pltpu.SemaphoreType.DMA((36,)),
    ]
    got = pl.pallas_call(
        partial(down_kernel, groups, len(main)),
        in_specs=[SMEM] + [HBM] * (5 * groups),
        out_specs=[HBM] * len(outs),
        out_shape=outs,
        scratch_shapes=scratch,
        compiler_params=params(LIMIT),
        cost_estimate=cost(1e6, 1e5),
        name="down_grad",
    )(ids, *cot, *dlat, *a_enc, *a_reg, *dyb_reg)
    return got[: len(main)], got[-1]


def mlp_kernel(first, groups, ids, visible, order_in, gains, cot, dlat_in, w1, w2, y1_in, gp_in, *refs):
    if first:
        picked, refs = refs[:groups], refs[groups:]
    du_out, dy1_out, dy1b_out, sums_out, order, rows_v, flat, refs = *refs[:7], refs[7:]
    s1, s2, cot_v, dlat, dyb, gp, y1, du, u, acc, dy1, dy1b, sums, sems = refs
    n = GROUP * NV
    third = FF // 3

    @pl.when(ids[0] == 0)
    def _():
        copies = Copies(sems)
        got = [copies.start(dlat_in, dlat)]
        if first:
            got_rows = copies.start(cot.at[0], rows_v)
        else:
            got.append(copies.start(cot, cot_v))
        start = copies.take(9)

        def parts(i):
            cols = pl.ds(pl.multiple_of(i * third, third), third)
            return (
                (w2.at[0, cols, :], s2.at[cols, :]),
                (gp_in.at[:, cols], gp.at[:, cols]),
                (w1.at[0, :, cols], s1.at[:, cols]),
            )

        for i in range(3):
            for k, (src, dst) in enumerate(parts(i)):
                copies.begin(src, dst, start + 3 * i + k)
        got_y = copies.start(y1_in, y1)

        def ready(i, which):
            for k in ((0, 1), (2,))[which]:
                copies.wait_at(*parts(i)[k], start + 3 * i + k)

        if first:
            split_orders(order_in, order)
            copies.wait(got_rows)
            flatten(rows_v, flat)
            for g in reversed(range(groups)):

                def pick_rows(i, g=g):
                    image = g * GROUP + i
                    pick = pick_matrix(order, image, 0, NV, 0, visible[image])
                    cot_v[rows_of(i, NV), :] = nn(pick, flat[...]).astype(BF)

                loop(GROUP, pick_rows)
                copies.wait(copies.start(cot_v, picked[g]))
        copies.wait(*got)
        dyb[...] = (cot_v[...].astype(F32) + dlat[...].astype(F32)).astype(BF)
        mlp_back(n, dyb, gp, s1, s2, du, u, acc, ready)
        copies.start(du, du_out)
        copies.wait(got_y)

        def keep(sel, dx):
            dy1[sel, :] = dx
            dy1b[sel, :] = dx.astype(BF)

        g2, b2 = norm_back(y1, acc, dyb, keep, n, f32_row(gains.at[0], 1))
        copies.start(dy1, dy1_out)
        copies.start(dy1b, dy1b_out)
        sums[pl.ds(0, 1), :] = g2
        sums[pl.ds(1, 1), :] = b2
        copies.start(sums, sums_out)
        copies.finish()


def mlp_grad(first, groups, ids, visible, order, gains, cot, dlat, w1, w2, y1, gp):
    n = GROUP * NV
    images = order.shape[0]
    row, wide, full = pltpu.VMEM((n, D), BF), pltpu.VMEM((n, FF), BF), pltpu.VMEM((n, D), F32)
    outs = [struct((n, D))] * (groups if first else 0) + [struct((n, FF)), struct((n, D), F32), struct((n, D)), struct((8, D), F32)]
    got = pl.pallas_call(
        partial(mlp_kernel, first, groups),
        in_specs=[SMEM, SMEM, VMEM, VMEM] + [HBM] * 6,
        out_specs=[HBM] * len(outs),
        out_shape=outs,
        scratch_shapes=[
            pltpu.VMEM((images, 1, PATCH), jnp.int32),
            pltpu.VMEM((PATCH, images, D), BF), pltpu.VMEM((PATCH * images, D), BF),
            pltpu.VMEM((D, FF), BF), pltpu.VMEM((FF, D), BF), row, row, row, wide, full, wide,
            pltpu.VMEM((2, n, HALF), F32), full, full, row, pltpu.VMEM((8, D), F32), pltpu.SemaphoreType.DMA((24,)),
        ],
        compiler_params=params(LIMIT),
        cost_estimate=cost(1e6, 1e5),
        name="mlp_grad",
    )(ids, visible, order, gains, cot, dlat, w1, w2, y1, gp)
    return got[:-4], got[-4:]


def up_kernel(groups, parts, ids, *refs):
    pieces = [refs[i * groups : (i + 1) * groups] for i in range(8)]
    refs = refs[8 * groups :]
    dest, refs = refs[:parts], refs[parts:]
    sums_out, left, right, out, sums, sems = refs
    images = groups * GROUP

    nv, nm = GROUP * NV, GROUP * NM
    copies = Copies(sems)
    sides = (pieces[:4], pieces[4:])

    def sources(role, j):
        du, _, dy1b, _ = sides[role]
        ones = dy1b if j == 4 else [one.at[:, pl.ds(j * D, D)] for one in du]
        return [(one, (nv, nm)[role]) for one in ones]

    def lefts(role, i):
        _, h2, _, o = sides[role]
        return [(one, (nv, nm)[role]) for one in (h2, o)[i]]

    loads = BlockLoads(copies, ids, groups, 5, sources, lambda j: right.at[j])
    shared = BlockLoads(copies, ids, groups, 2, lefts, lambda i: left.at[i])
    for role in range(2):

        @pl.when(ids[0] == role)
        def _(role=role):
            shared.begin(role, 0)
            for j in range(5):
                loads.begin(role, j)
            shared.begin(role, 1)
            if role == 1:
                for ref in (left, right):
                    for i in range(ref.shape[0]):
                        clear_tail(ref.at[i], images * NM)

    shared.wait(0)

    def multiply(j):
        loads.wait(j)
        pl.when(j == 4)(lambda: shared.wait(1))
        value = tn(left[lax.div(j, 4)], right[j]).astype(BF)
        sums[pl.ds(j, 1), :] = column_sum(right.at[j], images * NV)
        return value

    give_blocks(copies, ids[1], dest[0].ndim == 6, multiply, out, dest)
    copies.start(sums, sums_out)
    copies.finish()


def up_grad(groups, count, ids, *pieces):
    n = groups * GROUP * NV
    main = halves(count, 5)
    outs = main + [struct((8, D), F32)]
    got = pl.pallas_call(
        partial(up_kernel, groups, len(main)),
        in_specs=[SMEM] + [HBM] * (8 * groups),
        out_specs=[HBM] * len(outs),
        out_shape=outs,
        scratch_shapes=[
            pltpu.VMEM((2, n, D), BF), pltpu.VMEM((5, n, D), BF), pltpu.VMEM((5, D, D), BF), pltpu.VMEM((8, D), F32),
            pltpu.SemaphoreType.DMA((60,)),
        ],
        compiler_params=params(LIMIT),
        cost_estimate=cost(1e6, 1e5),
        name="up_grad",
    )(ids, *[ref for piece in pieces for ref in piece])
    return got[: len(main)], got[-1]


def attn_kernel(groups, last, ids, gains, *refs):
    if last:
        down_sums, up_sums, refs = refs[0], refs[1], refs[2:]
        mlp_sums, reg_sums = (refs[i * groups : (i + 1) * groups] for i in range(2))
        before, refs = refs[2 * groups : 3 * groups - 1], refs[3 * groups - 1 :]
    (wqkv, wo, dy1_enc, q_in, k_in, v_in, p_in, x_enc, dq_reg, dkv_reg, dy1_reg, x_reg,
     dq_out, dkv_out, dx_out, sums_out,
     sqkv, so, dy1, dy1b, q, k, v, p, x, do, dq, dkv, dh, sems) = refs
    m = GROUP * NM
    top = pl.ds(0, m)
    gain = f32_row(gains.at[0], 0)

    def finish(copies, rows):
        def keep(sel, dx):
            dy1[sel, :] = dx

        own = (*norm_back(x, dh, dy1, keep, rows, gain), column_sum(dq, rows), column_sum(dkv, GROUP * NV, D))
        copies.start(dy1, dx_out)
        if not last:
            for row, value in enumerate(own):
                sums_out[row : row + 1, :] = value
            copies.finish()
            return

        def total_of(sums):
            total = sums[0][...]
            for more in sums[1:]:
                total = total + more[...]
            return total

        done, mlp, reg = total_of(before), total_of(mlp_sums), total_of(reg_sums)
        g1, b1, queries, values = (one + done[row : row + 1, :] for row, one in enumerate(own))
        encoder = ids[0] == 0
        sums_out[0:1, :] = g1 + jnp.where(encoder, 0.0, reg[0:1, :])
        sums_out[1:2, :] = jnp.where(encoder, mlp[0:1, :], reg[1:2, :])
        sums_out[2:3, :] = b1 + jnp.where(encoder, 0.0, reg[2:3, :])
        sums_out[3:4, :] = up_sums[4:5, :]
        sums_out[4:5, :] = jnp.where(encoder, mlp[1:2, :], reg[3:4, :])
        sums_out[5:6, :] = down_sums[0:1, :]
        sums_out[6:7, :] = queries
        sums_out[7:8, :] = values
        sums_out[8:12, :] = up_sums[0:4, :]
        sums_out[12:16, :] = jnp.zeros((4, D), F32)
        copies.finish()

    @pl.when(ids[0] == 0)
    def _():
        copies = Copies(sems)
        got = [copies.start(dy1_enc, dy1), copies.start(wo.at[0], so)]
        later = [copies.start(src, dst) for src, dst in ((v_in, v), (p_in, p), (k_in, k), (q_in, q))]
        final = [copies.start(wqkv.at[0], sqkv), copies.start(x_enc, x)]
        copies.wait(*got)
        dy1b[...] = dy1[...].astype(BF)
        do[...] = nt(dy1b[...], so[...]).astype(BF)
        copies.wait(*later)
        attention_back_rows(GROUP, NV, q, k, v, p, do, dq, dkv)
        copies.start(dq, dq_out)
        copies.start(dkv, dkv_out)
        copies.wait(*final)
        dh[...] = nt(dq[...], sqkv[:, 0:D])
        for j in range(2):
            dh[...] += nt(dkv[:, j * D : (j + 1) * D], sqkv[:, (j + 1) * D : (j + 2) * D])
        finish(copies, GROUP * NV)

    @pl.when(ids[0] == 1)
    def _():
        copies = Copies(sems)
        for src, dst in ((dq_reg, dq), (dy1_reg, dy1), (x_reg, x)):
            copies.start(src, dst.at[top])
        copies.start(dkv_reg, dkv)
        copies.start(wqkv.at[0, :, pl.ds(0, D)], sqkv.at[:, pl.ds(0, D)])
        copies.finish()
        dh[top, :] = nt(dq[top, :], sqkv[:, 0:D])
        finish(copies, m)


def attn_back(groups, last, ids, gains, sums, *pieces):
    n = GROUP * NV
    row, full = pltpu.VMEM((n, D), BF), pltpu.VMEM((n, D), F32)
    outs = [struct((n, D)), struct((n, 2 * D)), struct((n, D), F32), struct((16, D), F32)]
    return pl.pallas_call(
        partial(attn_kernel, groups, last),
        in_specs=[SMEM, VMEM] + [VMEM] * len(sums) + [HBM] * len(pieces),
        out_specs=[HBM] * 3 + [VMEM],
        out_shape=outs,
        scratch_shapes=[
            pltpu.VMEM((D, 3 * D), BF), pltpu.VMEM((D, D), BF), full, row, row, row, row,
            pltpu.VMEM((GROUP * PAIRS, 2 * NV, NV), BF), row, row, row, pltpu.VMEM((n, 2 * D), BF), full,
            pltpu.SemaphoreType.DMA((20,)),
        ],
        compiler_params=params(LIMIT),
        cost_estimate=cost(1e6, 1e5),
        name="attn_back",
    )(ids, gains, *sums, *pieces)


def qkv_kernel(groups, parts, ids, *refs):
    pieces = [refs[i * groups : (i + 1) * groups] for i in range(7)]
    dq_enc, dkv_enc, hq_enc, hq_reg, hk_reg, dq_reg, dkv_reg = pieces
    refs = refs[7 * groups :]
    dest, refs = refs[:parts], refs[parts:]
    left, right, out, sems = refs
    images = groups * GROUP
    nv, nm = GROUP * NV, GROUP * NM
    copies = Copies(sems)

    def sources(role, j):
        if j == 2:
            return [(one, (nv, nm)[role]) for one in (dq_enc, dq_reg)[role]]
        return [(one.at[:, pl.ds(j * D, D)], nv) for one in (dkv_enc, dkv_reg)[role]]

    def lefts(role, i):
        if role == 0:
            return [(one, nv) for one in hq_enc]
        return [(one, (nv, nm)[i]) for one in (hk_reg, hq_reg)[i]]

    loads = BlockLoads(copies, ids, groups, 3, sources, lambda j: right.at[j])
    shared = BlockLoads(copies, ids, groups, 2, lefts, lambda i: left.at[i])
    for role in range(2):

        @pl.when(ids[0] == role)
        def _(role=role):
            shared.begin(role, 0)
            for j in range(3):
                loads.begin(role, j)
            shared.begin(role, 1)
            if role == 1:
                clear_tail(left.at[1], images * NM)
                clear_tail(right.at[2], images * NM)

    shared.wait(0)

    def multiply(j):
        for block in range(3):

            @pl.when(j == block)
            def _(block=block):
                loads.wait(block, block)
                if block == 2:
                    shared.wait(1, 1)

        return tn(left[lax.div(j, 2)], right[j]).astype(BF)

    give_blocks(copies, ids[1], dest[0].ndim == 6, multiply, out, dest)


def qkv_grad(groups, count, ids, *pieces):
    n = groups * GROUP * NV
    row = pltpu.VMEM((n, D), BF)
    main = halves(count, 3)
    scratch = [
        pltpu.VMEM((2, n, D), BF), pltpu.VMEM((3, n, D), BF), pltpu.VMEM((3, D, D), BF),
        pltpu.SemaphoreType.DMA((40,)),
    ]
    return pl.pallas_call(
        partial(qkv_kernel, groups, len(main)),
        in_specs=[SMEM] + [HBM] * (7 * groups),
        out_specs=[HBM] * len(main),
        out_shape=main,
        scratch_shapes=scratch,
        compiler_params=params(LIMIT),
        cost_estimate=cost(1e6, 1e5),
        name="qkv_grad",
    )(ids, *[ref for piece in pieces for ref in piece])


def place_kernel(groups, ids, visible, order_in, *refs):
    dx_in, lat_enc, res_enc, res_reg = (refs[i * groups : (i + 1) * groups] for i in range(4))
    block_out, grad_out, order, dx, lat, out, grads, sems = refs[4 * groups :]
    images = groups * GROUP
    nv, nm = GROUP * NV, GROUP * NM
    split_orders(order_in, order)

    def put_grad(i, put, value):
        high = value.astype(BF)
        low = (value - high.astype(F32)).astype(BF)
        grads[i] = nn(put, high) + nn(put, low)

    def write_grads():
        copies = Copies(sems)
        for i in range(images):
            copies.start(grads.at[i], grad_out.at[0, :, i, :])
        copies.finish()

    @pl.when(ids[0] == 0)
    def _():
        copies = Copies(sems)
        for piece, ref, size in ((dx_in, dx, nv), (lat_enc, lat, nv), (res_enc, out, nm)):
            stack_rows(copies, piece, ref, size)
        copies.finish()

        def put_image(i):
            put = place_matrix(order, i, 0, NV, 0, visible[i])
            put_side = place_matrix(order, i, FIRST, NM, visible[i], PATCH)
            put_grad(i, put, dx[rows_of(i, NV), :])
            block_out[0, i] = (nn(put, lat[rows_of(i, NV), :]) + nn(put_side, out[rows_of(i, NM), :])).astype(BF)

        loop(images, put_image)
        write_grads()

    @pl.when(ids[0] == 1)
    def _():
        copies = Copies(sems)
        stack_rows(copies, res_reg, out, nm)
        stack_rows(copies, [piece.at[pl.ds(0, nm)] for piece in dx_in], dx, nm)
        copies.finish()

        def put_image(i):
            put = place_matrix(order, i, FIRST, NM, visible[i], PATCH)
            put_grad(i, put, dx[rows_of(i, NM), :])
            block_out[0, i] = nn(put, out[rows_of(i, NM), :]).astype(BF)

        loop(images, put_image)
        write_grads()


def place(groups, ids, visible, order, *pieces):
    images = groups * GROUP
    n = images * NV
    outs = [struct((1, images, PATCH, D)), struct((1, PATCH, images, D), F32)]
    return pl.pallas_call(
        partial(place_kernel, groups),
        in_specs=[SMEM, SMEM, VMEM] + [HBM] * (4 * groups),
        out_specs=[VMEM, HBM],
        out_shape=outs,
        scratch_shapes=[
            pltpu.VMEM((images, 1, PATCH), jnp.int32), pltpu.VMEM((n, D), F32), pltpu.VMEM((n, D), BF),
            pltpu.VMEM((images * NM, D), BF), pltpu.VMEM((images, PATCH, D), F32), pltpu.SemaphoreType.DMA((8,)),
        ],
        compiler_params=params(LIMIT),
        cost_estimate=cost(1e6, 1e5),
        name="place",
    )(ids, visible, order, *[ref for piece in pieces for ref in piece])


BITS = (2, 4, 8)


def hop(value, bit):
    return lax.ppermute(value, "dp", [(i, i ^ bit) for i in range(16)])


def combine_kernel(jobs, given, ids, *refs):
    used = sum(sum(4 if gone is None else 1 for gone in terms) for terms, *_ in jobs)
    inputs, outs, scratch = list(refs[:used]), list(refs[used : used + given]), list(refs[used + given :])
    copies = Copies(scratch.pop())
    plans = []

    def fetch(term, gone, bits, own):
        if gone is not None:
            path = tuple(bits[gone:])
            copy = copies.start(term.at[path] if path else term, own)
            return lambda: copies.wait(copy)
        wide = len(bits) == 1
        first = copies.take(2 if wide else 1)
        rest = tuple(bits[2:])

        def piece(x, low):
            ref = term[2 * x + low]
            return ref.at[rest] if rest else ref

        for x in range(2):
            for low in range(2):
                if wide:
                    pl.when(bits[0] == x)(
                        lambda x=x, low=low: copies.begin(piece(x, low), own.at[low], first + low)
                    )
                else:
                    pl.when((bits[0] == x) & (bits[1] == low))(
                        lambda x=x, low=low: copies.begin(piece(x, low), own, first)
                    )

        def wait():
            if wide:
                for low in range(2):
                    copies.wait_at(piece(0, low), own.at[low], first + low)
            else:
                copies.wait_at(piece(0, 0), own, first)

        return wait

    for kinds, first, last, targets, finals in jobs:
        terms = [inputs.pop(0) if gone is not None else [inputs.pop(0) for _ in range(4)] for gone in kinds]
        for target in targets:
            bits = []
            for bit in range(last):
                flip = bit >= first and (target >> (bit - first)) & 1
                bits.append(1 - ids[2 + bit] if flip else ids[2 + bit])
            owns = [scratch.pop(0) for _ in kinds]
            waits = [fetch(term, gone, bits, own) for term, gone, own in zip(terms, kinds, owns)]
            plans.append((waits, owns, last, finals, None if finals else outs.pop(0)))
    for waits, owns, last, finals, out in plans:
        for wait in waits:
            wait()
        spots = [()]
        for _ in range(3 - last):
            spots = [spot + (i,) for spot in spots for i in range(2)]
        for spot in spots:
            for j in range(owns[0].shape[-3]):
                value = owns[0][spot + (j,)].astype(F32)
                for more in owns[1:]:
                    value = value + more[spot + (j,)].astype(F32)
                if finals:
                    which, column = finals[j]
                    outs[which][:, column * D : (column + 1) * D] = value
                else:
                    out[spot + (j,)] = value.astype(BF)


def send_job(terms, first, last, targets=(1,)):
    return terms, first, last, targets, None


def final_job(terms, finals):
    return terms, 0, 3, (0,), finals


def combine(ids, *jobs, outs=()):
    shapes = [struct(shape, F32) for shape in outs]
    plans, inputs, scratch = [], [], []
    for terms, first, last, targets, finals in jobs:
        blocks, rows = terms[0].shape[-3:-1]
        kinds = tuple(None if isinstance(term, list) else 6 - term.ndim for term in terms)
        for term in terms:
            inputs += term if isinstance(term, list) else [term]
        plans.append((kinds, first, last, targets, finals))
        part = (2,) * (3 - last) + (blocks, rows, D)
        for _ in targets:
            scratch += [pltpu.VMEM(part, BF) for _ in terms]
            if finals is None:
                shapes.append(struct(part))
    scratch.append(pltpu.SemaphoreType.DMA((2 * len(scratch),)))
    return pl.pallas_call(
        partial(combine_kernel, tuple(plans), len(shapes)),
        in_specs=[SMEM] + [HBM] * len(inputs),
        out_specs=[VMEM] * len(shapes),
        out_shape=shapes,
        scratch_shapes=scratch,
        compiler_params=params(LIMIT),
        cost_estimate=cost(1e5, 1e4),
        name="combine",
    )(ids, *inputs)


def in_order(first, then):
    return lax.optimization_barrier((first, then))


def own_columns(rows, count):
    own = D // count
    me = lax.axis_index("dp")

    def part(block, wide):
        return lax.dynamic_slice_in_dim(block, me * wide, wide, block.ndim - 1)

    return (
        part(rows[:2], own),
        part(rows[2:6], own),
        part(rows[6:8].reshape(-1), 2 * own),
        part(rows[8:12].reshape(-1), 4 * own),
    )


def scatter_natural(block):
    shards = block.reshape(lax.axis_size("dp"), -1, D)
    return lax.psum_scatter(shards, "dp", scatter_dimension=0, tiled=True)[0].astype(F32)


def local(
    patch_rows, cotangent, patch_order, visible, qkv_weight, out_weight, up_weight, down_weight, norm_gains, biases,
    qv_bias, up_bias, target_qkv, target_out, target_up, target_down, target_gains, target_biases, target_qv_bias,
    target_up_bias,
):
    count = lax.axis_size("dp")
    tree = count == 16
    place_dp = lax.axis_index("dp")
    bits = [(place_dp // bit) % 2 for bit in (1,) + BITS]
    ids = jnp.stack([lax.axis_index("section")] + bits).astype(jnp.int32)
    groups = patch_order.shape[0] // GROUP
    weights = (qkv_weight, out_weight, up_weight, down_weight)
    targets = (target_qkv, target_out, target_up, target_down)
    vecs = (norm_gains, biases, qv_bias, up_bias)
    target_vecs = (target_gains, target_biases, target_qv_bias[None], target_up_bias[None])

    rows, cot = patch_rows.transpose(0, 2, 1, 3), cotangent.transpose(0, 2, 1, 3)
    calls = [
        encode(g, groups, ids, visible, patch_order, *vecs, rows, cot, weights) for g in range(groups)
    ]
    lat, x_e, hq_e, q_e, k_e, v_e, p_e, o_e, y1_e, h2_e, gp_e, a_e = zip(*[call[0] for call in calls])
    x_r, hq_r, q_r, dyb_r = calls[-1][1]
    sent = [lax.ppermute(piece, "section", [(0, 1)]) for piece in lat]
    vectors = (norm_gains, biases, qv_bias, up_bias)
    regressed = [regress(0, ids, visible, vectors, sent[0], x_r[0], q_r[0], dyb_r[0], weights)]
    back = [lax.ppermute(regressed[0][0], "section", [(1, 0)])]
    order_first, regressed[0] = in_order(patch_order, regressed[0])
    res_e = [target(0, ids, visible, order_first, target_vecs, rows, targets)]
    res_e[0], sent[1:] = in_order(res_e[0], sent[1:])
    for g in range(1, groups):
        regressed.append(regress(g, ids, visible, vectors, sent[g], x_r[g], q_r[g], dyb_r[g], weights))
        back.append(lax.ppermute(regressed[g][0], "section", [(1, 0)]))
    _, res_r, hk_r, dq_r, dkv_r, o_r, dy1b_r, h2_r, du_r, a_r, dy1_r, sums_r = zip(*regressed)

    def mlp(g, cot):
        return mlp_grad(
            g == 0, groups, ids, visible, patch_order, norm_gains, cot, back[g], up_weight, down_weight, y1_e[g], gp_e[g]
        )

    def attention(g, dy1, sums=()):
        return attn_back(
            groups, len(sums) > 0, ids, norm_gains, sums, qkv_weight, out_weight, dy1, q_e[g], k_e[g], v_e[g], p_e[g],
            x_e[g], dq_r[g], dkv_r[g], dy1_r[g], x_r[g],
        )

    cot_e, first = mlp(0, cot)
    mlps = [first] + [mlp(g, cot_e[g])[1] for g in range(1, groups - 1)]
    attns = [attention(g, mlps[g][1]) for g in range(groups - 1)]
    last = groups - 1
    send = partial(combine, ids)
    attns, back[last] = in_order(attns, back[last])
    down, sums_down = down_grad(groups, count, ids, cot_e, back, a_e, a_r, dyb_r)
    cot_last = cot_e[last]
    down, cot_last = in_order(down, cot_last)
    mlps.append(mlp(last, cot_last)[1])
    du_e, dy1_e, dy1b_e, sums_e = (list(piece) for piece in zip(*mlps))
    if tree:
        downs = [down[0], hop(down[1], 1)]
        (down_x,), du_e[last] = in_order(send(send_job(downs, 0, 1)), du_e[last])
        downs = downs + [hop(down_x, 2)]
    up, sums_up = up_grad(groups, count, ids, du_e, h2_e, dy1b_e, o_e, du_r, h2_r, dy1b_r, o_r)
    if tree:
        peers = (3, 2, 1)
        ups = [up[0], [hop(piece, 1) for piece in up[1:]]]
        (up_x,), downs = in_order(send(send_job(ups, 0, 1)), downs)
        ups = ups + [hop(up_x, 2)]
        down_z, dy1_e[last] = in_order(send(send_job(downs, 1, 3, peers)), dy1_e[last])
        down_got = [hop(one, 4 * peer) for one, peer in zip(down_z, peers)]
    sums_in = [piece[3] for piece in attns]
    attns.append(attention(last, dy1_e[last], (sums_down, sums_up, *sums_e, *sums_r, *sums_in)))
    dq_e, dkv_e, dx, small = (list(piece) for piece in zip(*attns))
    small = small[last]
    order_late = patch_order
    if tree:
        small = small + hop(small, 1)
        small, dq_e[last] = in_order(small, dq_e[last])
    attn = qkv_grad(groups, count, ids, dq_e, dkv_e, hq_e, hq_r, hk_r, dq_r, dkv_r)
    if tree:
        down_got, attn = in_order(down_got, attn)
        qkvs = [attn[0], [hop(piece, 1) for piece in attn[1:]]]
        small = small + hop(small, 2)
        (qkv_x, *up_z), got = in_order(send(send_job(qkvs, 0, 1), send_job(ups, 1, 3, peers)), hop(small, 4))
        small = small + got
        up_got = [hop(one, 4 * peer) for one, peer in zip(up_z, peers)]
        order_late, qkv_x = in_order(patch_order, qkv_x)
        qkvs = qkvs + [hop(qkv_x, 2)]
        got = hop(small, 8)
    res_e += [target(g, ids, visible, order_late, target_vecs, rows, targets) for g in range(1, groups)]
    if tree:
        qkv_z, res_e = in_order(send(send_job(qkvs, 1, 3, peers)), res_e)
        qkv_got = [hop(one, 4 * peer) for one, peer in zip(qkv_z, peers)]
    block_out, grad_rows = place(groups, ids, visible, patch_order, dx, lat, res_e, res_r)
    if tree:
        small = small + got
        (block_out, grad_rows), up_got = in_order((block_out, grad_rows), up_got)
        down_sum, up_sum, out_sum = send(
            final_job(downs + down_got, ((0, 0),)),
            final_job(ups + up_got, tuple((1, j) for j in range(4)) + ((2, 0),)),
            outs=((D // 4, D), (D // 16, 4 * D), (D // 16, D)),
        )
        qkv_got, (down_sum, up_sum, out_sum) = in_order(qkv_got, (down_sum, up_sum, out_sum))
        (qkv_sum,) = send(final_job(qkvs + qkv_got, ((0, 1), (0, 2), (0, 0))), outs=((D // 16, 3 * D),))
    else:
        down_sum = scatter_natural(down[0])
        up_sum = jnp.concatenate([scatter_natural(one) for one in up[:4]], axis=1)
        out_sum = scatter_natural(up[4])
        qkv_sum = jnp.concatenate([scatter_natural(attn[i]) for i in (2, 0, 1)], axis=1)
        small = lax.psum(small, "dp")
    grad_rows = grad_rows.transpose(0, 2, 1, 3)
    gains, bias_rows, qv_rows, up_rows = own_columns(small, count)
    return (
        block_out,
        grad_rows,
        qkv_sum[None],
        out_sum[None],
        up_sum[None],
        down_sum[None],
        gains[None],
        bias_rows[None],
        qv_rows[None],
        up_rows[None],
    )


def solution(mesh):
    three, four = P("section", None, None), P("section", "dp", None, None)
    grad = P("section", "dp", None)
    return jax.shard_map(
        local,
        mesh=mesh,
        in_specs=(four, four, P("dp", None), P("dp"), three, three, three, three, three, three,
                  P("section", None), P("section", None), P(), P(), P(), P(), P(), P(), P(), P()),
        out_specs=(four, four, grad, grad, grad, grad, P("section", None, "dp"), P("section", None, "dp"),
                   P("section", "dp"), P("section", "dp")),
        check_vma=False,
    )
```

```python
from functools import partial

import jax
import jax.numpy as jnp
from jax import lax
from jax.experimental import pallas as pl
from jax.experimental.pallas import tpu as pltpu
from jax.sharding import PartitionSpec as P

HEADS = 12
PATCH = 196
D = 768
FF = 3072
EPS = 1e-06
NV = 144
NM = 128
FIRST = PATCH - NM
GROUP = 2
CHUNK = 32

BF = jnp.bfloat16
F32 = jnp.float32
MIB = 1024 * 1024
LIMIT = 62

HBM = pl.BlockSpec(memory_space=pl.ANY)
VMEM = pl.BlockSpec(memory_space=pltpu.VMEM)
SMEM = pl.BlockSpec(memory_space=pltpu.SMEM)


def nn(a, b):
    return jnp.dot(a, b, preferred_element_type=F32)


def nt(a, b):
    return lax.dot_general(a, b, (((1,), (1,)), ((), ())), preferred_element_type=F32)


def tn(a, b):
    return lax.dot_general(a, b, (((0,), (0,)), ((), ())), preferred_element_type=F32)


def loop(count, body, unroll=1):
    def step(i, carry):
        for u in range(unroll):
            body(i * unroll + u)
        return carry

    if count == unroll:
        step(0, 0)
    else:
        lax.fori_loop(0, count // unroll, step, 0)


def unroll_of(count):
    return next(u for u in (4, 3, 2, 1) if count % u == 0)


def rows_of(i, size):
    return pl.ds(pl.multiple_of(i * size, size), size)


def f32_row(ref, row, col=0, width=D):
    return ref[pl.ds(row, 1), pl.ds(col, width)].astype(F32)


class Copies:
    def __init__(self, sems):
        self.sems = sems
        self.used = 0
        self.open = []

    def start(self, src, dst):
        copy = pltpu.make_async_copy(src, dst, self.sems.at[self.used])
        self.used += 1
        copy.start()
        self.open.append(copy)
        return copy

    def wait(self, *copies):
        for copy in copies:
            copy.wait()
            self.open = [one for one in self.open if one is not copy]

    def finish(self):
        self.wait(*list(self.open))

    def take(self, count):
        self.used += count
        return self.used - count

    def part(self):
        other = Copies(self.sems)
        other.used = self.used
        return other

    def begin(self, src, dst, at):
        pltpu.make_async_copy(src, dst, self.sems.at[at]).start()

    def wait_at(self, src, dst, at):
        pltpu.make_async_copy(src, dst, self.sems.at[at]).wait()


def gelu_pair(u):
    size = jnp.abs(u)
    base = 1.0 + (0.3275911 * 0.7071067811865476) * size
    guess = pl.reciprocal(base, approx=True)
    t = guess * (2.0 - base * guess)
    ex = jnp.exp2((u * u) * (-0.5 * 1.4426950408889634))
    poly = 0.5306027145 * t - 0.7265760135
    poly = poly * t + 0.7107068705
    poly = poly * t - 0.142248368
    poly = poly * t + 0.127414796
    tail = poly * t * ex
    phi = jnp.where(u >= 0.0, 1.0 - tail, tail)
    return u * phi, phi + u * (0.3989422804014327 * ex)


def norm_rows(src, dst, rows, gain, shift):
    def body(i):
        sel = rows_of(i, CHUNK)
        x = src[sel, :].astype(F32)
        centered = x - jnp.mean(x, axis=-1, keepdims=True)
        var = jnp.mean(centered * centered, axis=-1, keepdims=True)
        dst[sel, :] = (centered * lax.rsqrt(var + EPS) * gain + shift).astype(BF)

    loop(rows // CHUNK, body, unroll_of(rows // CHUNK))


def norm_back(src, grad, base, write, rows, gain):
    count = rows // CHUNK
    unroll = 3 if count % 3 == 0 else 2

    def step(i, carry):
        for u in range(unroll):
            carry = one(i * unroll + u, carry)
        return carry

    def one(i, carry):
        d_gain, d_shift = carry
        sel = rows_of(i, CHUNK)
        x = src[sel, :].astype(F32)
        dh = grad[sel, :]
        centered = x - jnp.mean(x, axis=-1, keepdims=True)
        var = jnp.mean(centered * centered, axis=-1, keepdims=True)
        rstd = lax.rsqrt(var + EPS)
        hat = centered * rstd
        g = dh * gain
        part = dh * hat
        dx = rstd * (
            g
            - jnp.mean(g, axis=-1, keepdims=True)
            - hat * jnp.mean(g * hat, axis=-1, keepdims=True)
        )
        if base is not None:
            dx = dx + base[sel, :].astype(F32)
        write(sel, dx)
        d_gain = d_gain + jnp.sum(part.reshape(CHUNK // 8, 8, D), axis=0)
        d_shift = d_shift + jnp.sum(dh.reshape(CHUNK // 8, 8, D), axis=0)
        return d_gain, d_shift

    zero = jnp.zeros((8, D), F32)
    d_gain, d_shift = lax.fori_loop(0, count // unroll, step, (zero, zero))
    return jnp.sum(d_gain, axis=0, keepdims=True), jnp.sum(d_shift, axis=0, keepdims=True)


def column_sum(ref, rows, col=0, width=D):
    def step(i, carry):
        x = ref[rows_of(i, CHUNK), pl.ds(col, width)].astype(F32)
        return carry + jnp.sum(x.reshape(CHUNK // 8, 8, width), axis=0)

    total = lax.fori_loop(0, rows // CHUNK, step, jnp.zeros((8, width), F32))
    return jnp.sum(total, axis=0, keepdims=True)


def as_bf16(flags):
    return jnp.where(flags, 1.0, 0.0).astype(BF)


def pick_matrix(order, image, start, count, low, high):
    row = order[image, :, pl.ds(start, count)].astype(F32)
    images = order.shape[0]
    col = jnp.broadcast_to(row, (8, count)).T[:, 0:1].astype(jnp.int32)
    rank = start + lax.broadcasted_iota(jnp.int32, (count, 1), 0)
    col = jnp.where((rank >= low) & (rank < high), col * images + image, -1)
    return as_bf16(col == lax.broadcasted_iota(jnp.int32, (count, PATCH * images), 1))


def place_matrix(order, image, start, count, low, high):
    row = order[image, :, pl.ds(start, count)]
    rank = start + lax.broadcasted_iota(jnp.int32, (1, count), 1)
    row = jnp.where((rank >= low) & (rank < high), row, -1)
    return as_bf16(row == lax.broadcasted_iota(jnp.int32, (PATCH, count), 0))


def flatten(rows, flat):
    flat[...] = rows[...].reshape(flat.shape)


def split_orders(order, split):
    for image in range(split.shape[0]):
        split[image] = order[image : image + 1, :]


def split_pair(pair):
    lane = lax.broadcasted_iota(jnp.int32, pair.shape, 1)
    zero = jnp.zeros_like(pair)
    return jnp.concatenate([jnp.where(lane < 64, pair, zero), jnp.where(lane < 64, zero, pair)], axis=0)


def join_rows(both):
    rows = both.shape[0] // 2
    lane = lax.broadcasted_iota(jnp.int32, (rows, 128), 1)
    return jnp.where(lane < 64, both[:rows], both[rows:])


def join_columns(both):
    rows = both.shape[1] // 2
    return jnp.concatenate([both[:64, :rows], both[64:, rows:]], axis=0).T


PAIRS = HEADS // 2
STEP = 6


def each_pair_group(images, body):
    def group(i):
        image = i // (PAIRS // STEP)
        first = (i % (PAIRS // STEP)) * STEP
        pairs = [first + step for step in range(STEP)]
        body(image, [image * PAIRS + pair for pair in pairs], [pl.ds(pl.multiple_of(pair * 128, 128), 128) for pair in pairs])

    loop(images * (PAIRS // STEP), group)


def softmax(scores, axis):
    ex = jnp.exp(scores - jnp.max(scores, axis=axis, keepdims=True))
    return (ex * (1.0 / jnp.sum(ex, axis=axis, keepdims=True))).astype(BF)


def score_back(probs, d_probs, axis):
    wide = probs.astype(F32)
    return (wide * (d_probs - jnp.sum(d_probs * wide, axis=axis, keepdims=True))).astype(BF)


def attention_by_rows(images, n, q, k, v, p, o, count_of):
    def body(image, slots, lanes):
        sel = rows_of(image, n)
        ok = lax.broadcasted_iota(jnp.int32, (1, n), 1) < count_of(image)
        scores = [nt(split_pair(q[sel, at]), k[sel, at]) for at in lanes]
        probs = [softmax(jnp.where(ok, one, -1000000000.0), 1) for one in scores]
        for slot, one in zip(slots, probs):
            p[slot] = one
        mixed = [nn(one, v[sel, at]) for one, at in zip(probs, lanes)]
        for at, one in zip(lanes, mixed):
            o[sel, at] = join_rows(one).astype(BF)

    each_pair_group(images, body)


def attention_by_columns(images, nk, q, k, v, p, o, key_ok):
    def body(image, slots, lanes):
        qs, ks = rows_of(image, NM), rows_of(image, nk)
        ok = key_ok(image)
        scores = [nt(k[ks, at], split_pair(q[qs, at])) for at in lanes]
        probs = [softmax(jnp.where(ok, one, -1000000000.0), 0) for one in scores]
        if p is not None:
            for slot, one in zip(slots, probs):
                p[slot] = one
        mixed = [tn(v[ks, at], one) for one, at in zip(probs, lanes)]
        for at, one in zip(lanes, mixed):
            o[qs, at] = join_columns(one).astype(BF)

    each_pair_group(images, body)


def attention_back_rows(images, n, q, k, v, p, do, dq, dkv):
    def body(image, slots, lanes):
        sel = rows_of(image, n)
        d_mixed = [split_pair(do[sel, at]) for at in lanes]
        d_probs = [nt(one, v[sel, at]) for one, at in zip(d_mixed, lanes)]
        d_scores = [score_back(p[slot], one, 1) for slot, one in zip(slots, d_probs)]
        d_values = [tn(p[slot], one) for slot, one in zip(slots, d_mixed)]
        d_query = [nn(one, k[sel, at]) for one, at in zip(d_scores, lanes)]
        d_keys = [tn(one, split_pair(q[sel, at])) for one, at in zip(d_scores, lanes)]
        for at, value, query, key in zip(lanes, d_values, d_query, d_keys):
            dq[sel, at] = (join_rows(query) * 0.125).astype(BF)
            dkv[sel, at] = key.astype(BF)
            dkv[sel, pl.ds(pl.multiple_of(D + at.start, 128), 128)] = value.astype(BF)

    each_pair_group(images, body)


def attention_back_columns(images, nk, q, k, v, p, do, dq, dkv):
    def body(image, slots, lanes):
        qs, ks = rows_of(image, NM), rows_of(image, nk)
        d_mixed = [split_pair(do[qs, at]) for at in lanes]
        d_probs = [nt(v[ks, at], one) for one, at in zip(d_mixed, lanes)]
        d_scores = [score_back(p[slot], one, 0) for slot, one in zip(slots, d_probs)]
        d_values = [nn(p[slot], one) for slot, one in zip(slots, d_mixed)]
        d_query = [tn(k[ks, at], one) for one, at in zip(d_scores, lanes)]
        d_keys = [nn(one, split_pair(q[qs, at])) for one, at in zip(d_scores, lanes)]
        for at, value, query, key in zip(lanes, d_values, d_query, d_keys):
            dq[qs, at] = (join_columns(query) * 0.125).astype(BF)
            dkv[ks, at] = key.astype(BF)
            dkv[ks, pl.ds(pl.multiple_of(D + at.start, 128), 128)] = value.astype(BF)

    each_pair_group(images, body)


HALF = 512


def mlp_forward(rows, h2, w1, w2, up_b, u, a, gp, tile, acc, out, base):
    acc[...] = base()
    steps = FF // HALF

    def multiply(t):
        u[t % 2] = nn(h2[...], w1[:, t * HALF : (t + 1) * HALF])

    def add(t):
        acc[...] += nn(tile[t % 2], w2[t * HALF : (t + 1) * HALF, :])

    multiply(0)
    for t in range(steps):
        if t + 1 < steps:
            multiply(t + 1)
        if t > 0:
            add(t - 1)
        for c in range(0, HALF, 256):
            at = slice(t * HALF + c, t * HALF + c + 256)
            shift = up_b[0:1, at].astype(F32)
            for r in range(0, rows, CHUNK):
                sel = slice(r, r + CHUNK)
                value, slope = gelu_pair(u[t % 2, sel, c : c + 256] + shift)
                low = value.astype(BF)
                tile[t % 2, sel, c : c + 256] = low
                if a is not None:
                    a[sel, at] = low
                if gp is not None:
                    gp[sel, at] = slope.astype(BF)
    add(steps - 1)
    out[...] = acc[...].astype(BF)


def mlp_back(rows, dyb, gp, w1, w2, du, u, acc, ready=lambda i, which: None):
    acc[...] = jnp.zeros_like(acc)

    def body(i):
        cols = [pl.ds(pl.multiple_of((2 * i + part) * HALF, HALF), HALF) for part in range(2)]
        ready(i, 0)
        for part in range(2):
            u[part] = nt(dyb[...], w2[cols[part], :])
        ready(i, 1)
        for part in range(2):
            for r in range(0, rows, CHUNK):
                sel = slice(r, r + CHUNK)
                du[sel, cols[part]] = (gp[sel, cols[part]].astype(F32) * u[part, sel, :]).astype(BF)
            acc[...] += nt(du[:, cols[part]], w1[:, cols[part]])

    loop(FF // (2 * HALF), body)


def project(count, rows, left, weight, first, write):
    def body(j):
        write(j, nn(left[...], weight[:, pl.ds(pl.multiple_of((first + j) * D, D), D)]))

    loop(count, body)


def set_biases(ref, bias):
    ref[0] = f32_row(bias, 0)
    ref[1] = jnp.zeros((1, D), F32)
    ref[2] = f32_row(bias, 0, D)


def cost(flops, nbytes):
    return pl.CostEstimate(flops=int(flops), bytes_accessed=int(nbytes), transcendentals=0)


def params(mib):
    return pltpu.CompilerParams(vmem_limit_bytes=mib * MIB)


def struct(shape, dtype=BF):
    return jax.ShapeDtypeStruct(shape, dtype)


def start_weights(copies, sources, scratch):
    return [copies.start(src, dst) for src, dst in zip(sources, scratch)]


def encode_kernel(group, groups, ids, visible, order_in, gains, biases, qvb, upb, rows, cot, wqkv, wo, w1, w2,
                  lat_out, x_out, hq_out, q_out, k_out, v_out, p_out, o_out, y1_out, h2_out, gp_out, a_out, *refs):
    ready, refs = refs[: 4 * groups], refs[4 * groups :]
    (order, rows_v, flat, sqkv, so, s1, s2, x, hq, qkv, p, o, y1, h2, gp, a, u, tile, acc, shifts, lat, sems) = refs
    n = GROUP * NV
    split_orders(order_in, order)

    @pl.when(ids[0] == 0)
    def _():
        copies = Copies(sems)
        got_rows = copies.start(rows.at[0], rows_v)
        got_qkv, got_o, got_1, got_2 = start_weights(
            copies, (wqkv.at[0], wo.at[0], w1.at[0], w2.at[0]), (sqkv, so, s1, s2)
        )
        gain, bias = gains.at[0], biases.at[0]
        set_biases(shifts, qvb)
        copies.wait(got_rows)
        flatten(rows_v, flat)

        def pick_rows(i):
            image = group * GROUP + i
            pick = pick_matrix(order, image, 0, NV, 0, visible[image])
            x[rows_of(i, NV), :] = nn(pick, flat[...]).astype(BF)

        loop(GROUP, pick_rows)
        copies.start(x, x_out)
        norm_rows(x, hq, n, f32_row(gain, 0), f32_row(bias, 0))
        copies.start(hq, hq_out)
        copies.wait(got_qkv)

        def keep(j, value):
            scale = jnp.where(j == 0, 0.125, 1.0)
            qkv[j] = ((value + shifts[j]).astype(BF).astype(F32) * scale).astype(BF)

        project(3, n, hq, sqkv, 0, keep)
        q, k, v = qkv.at[0], qkv.at[1], qkv.at[2]
        copies.start(q, q_out)
        copies.start(k, k_out)
        copies.start(v, v_out)
        attention_by_rows(GROUP, NV, q, k, v, p, o, lambda i: visible[group * GROUP + i])
        copies.start(p, p_out)
        copies.start(o, o_out)
        copies.wait(got_o)
        y1[...] = nn(o[...], so[...]) + f32_row(bias, 1) + x[...].astype(F32)
        copies.start(y1, y1_out)
        norm_rows(y1, h2, n, f32_row(gain, 1), f32_row(bias, 2))
        copies.start(h2, h2_out)
        copies.wait(got_1, got_2)
        mlp_forward(n, h2, s1, s2, upb, u, a, gp, tile, acc, lat, lambda: y1[...] + f32_row(bias, 3))
        copies.start(gp, gp_out)
        copies.start(a, a_out)
        copies.start(lat, lat_out)
        copies.finish()

    if group == groups - 1:

        @pl.when(ids[0] == 1)
        def _():
            copies = Copies(sems)
            m = GROUP * NM
            x_out, hq_out, q_out, dyb_out = (ready[i * groups : (i + 1) * groups] for i in range(4))
            gain, bias = gains.at[0], biases.at[0]
            got_rows = copies.start(rows.at[0], rows_v)
            got_q = copies.start(wqkv.at[0, :, pl.ds(0, D)], so)
            copies.wait(got_rows)
            flatten(rows_v, flat)
            got_cot = copies.start(cot.at[0], rows_v)
            top = pl.ds(0, m)

            def pick_group(g):
                def pick_rows(i):
                    image = g * GROUP + i
                    pick = pick_matrix(order, image, FIRST, NM, visible[image], PATCH)
                    x[rows_of(i, NM), :] = nn(pick, flat[...]).astype(BF)

                loop(GROUP, pick_rows)

            for g in range(groups):
                pick_group(g)
                norm_rows(x, hq, m, f32_row(gain, 0), f32_row(bias, 0))
                sent = [copies.start(x.at[top], x_out[g]), copies.start(hq.at[top], hq_out[g])]
                if g == 0:
                    copies.wait(got_q)
                q = qkv.at[g]
                q[top, :] = ((nn(hq[top, :], so[...]) + f32_row(qvb, 0)).astype(BF) * 0.125).astype(BF)
                copies.start(q.at[top], q_out[g])
                copies.wait(*sent)
            copies.wait(got_cot)
            flatten(rows_v, flat)
            for g in range(groups):
                pick_group(g)
                copies.wait(copies.start(x.at[top], dyb_out[g]))
            copies.finish()


def encode(group, groups, ids, visible, order, gains, biases, qvb, upb, rows, cot, weights):
    n = GROUP * NV
    images = order.shape[0]
    row, wide = struct((n, D)), struct((n, FF))
    heads = struct((GROUP * PAIRS, 2 * NV, NV))
    outs = [row] * 6 + [heads, row, struct((n, D), F32), row, wide, wide] + [struct((GROUP * NM, D))] * (4 * groups)
    vm = lambda s: pltpu.VMEM(s.shape, s.dtype)
    scratch = [
        pltpu.VMEM((images, 1, PATCH), jnp.int32),
        pltpu.VMEM((PATCH, images, D), BF), pltpu.VMEM((PATCH * images, D), BF),
        pltpu.VMEM((D, 3 * D), BF), pltpu.VMEM((D, D), BF), pltpu.VMEM((D, FF), BF), pltpu.VMEM((FF, D), BF),
        vm(row), vm(row), pltpu.VMEM((3, n, D), BF), vm(heads), vm(row), pltpu.VMEM((n, D), F32), vm(row),
        vm(wide), vm(wide), pltpu.VMEM((2, n, HALF), F32), pltpu.VMEM((2, n, HALF), BF), pltpu.VMEM((n, D), F32),
        pltpu.VMEM((3, 1, D), F32), vm(row),
        pltpu.SemaphoreType.DMA((24,)),
    ]
    got = pl.pallas_call(
        partial(encode_kernel, group, groups),
        in_specs=[SMEM, SMEM] + [VMEM] * 5 + [HBM] * 6,
        out_specs=[HBM] * len(outs),
        out_shape=outs,
        scratch_shapes=scratch,
        compiler_params=params(LIMIT),
        cost_estimate=cost(2 * n * 12 * D * D, 25e6),
        name="encode",
    )(ids, visible, order, gains, biases, qvb, upb, rows, cot, *weights)
    ready = got[12:]
    return got[:12], [ready[i * groups : (i + 1) * groups] for i in range(4)]


def block_end(copies, n, got_weights, so, s1, s2, bias, gain, up_b, x, o, y1, h2, a, gp, u, tile, acc, res):
    got_o, got_1, got_2 = got_weights
    copies.wait(got_o)
    y1[...] = nn(o[...], so[...]) + f32_row(bias, 1) + x[...].astype(F32)
    norm_rows(y1, h2, n, f32_row(gain, 1), f32_row(bias, 2))
    copies.wait(got_1, got_2)
    mlp_forward(n, h2, s1, s2, up_b, u, a, gp, tile, acc, res, lambda: y1[...] + f32_row(bias, 3))


def target_kernel(group, ids, visible, order_in, gain, bias, qvb, upb, rows, wqkv, wo, w1, w2, res_out,
                  order, rows_v, flat, sqkv, so, s1, s2, x, hq, qkv, o, y1, h2, u, tile, acc, shifts, res, sems):
    n = GROUP * NM
    q, k, v = qkv.at[0], qkv.at[1], qkv.at[2]

    @pl.when(ids[0] == 0)
    def _():
        copies = Copies(sems)
        split_orders(order_in, order)
        got_rows = copies.start(rows.at[0], rows_v)
        got_qkv = copies.start(wqkv, sqkv)
        got_weights = start_weights(copies, (wo, w1, w2), (so, s1, s2))
        set_biases(shifts, qvb)
        copies.wait(got_rows)
        flatten(rows_v, flat)

        def pick_rows(i):
            image = group * GROUP + i
            pick = pick_matrix(order, image, FIRST, NM, visible[image], PATCH)
            x[rows_of(i, NM), :] = nn(pick, flat[...]).astype(BF)

        loop(GROUP, pick_rows)
        norm_rows(x, hq, n, f32_row(gain, 0), f32_row(bias, 0))
        copies.wait(got_qkv)

        def keep(j, value):
            scale = jnp.where(j == 0, 0.125, 1.0)
            qkv[j] = ((value + shifts[j]).astype(BF).astype(F32) * scale).astype(BF)

        project(3, n, hq, sqkv, 0, keep)

        def key_ok(i):
            return lax.broadcasted_iota(jnp.int32, (NM, 1), 0) + FIRST >= visible[group * GROUP + i]

        attention_by_columns(GROUP, NM, q, k, v, None, o, key_ok)
        block_end(copies, n, got_weights, so, s1, s2, bias, gain, upb, x, o, y1, h2, None, None, u, tile, acc, res)
        copies.start(res, res_out)
        copies.finish()


def target(group, ids, visible, order, vecs, rows, weights):
    n = GROUP * NM
    images = order.shape[0]
    row, full = pltpu.VMEM((n, D), BF), pltpu.VMEM((n, D), F32)
    return pl.pallas_call(
        partial(target_kernel, group),
        in_specs=[SMEM, SMEM] + [VMEM] * 5 + [HBM] * 5,
        out_specs=HBM,
        out_shape=struct((n, D)),
        scratch_shapes=[
            pltpu.VMEM((images, 1, PATCH), jnp.int32),
            pltpu.VMEM((PATCH, images, D), BF), pltpu.VMEM((PATCH * images, D), BF),
            pltpu.VMEM((D, 3 * D), BF), pltpu.VMEM((D, D), BF), pltpu.VMEM((D, FF), BF), pltpu.VMEM((FF, D), BF),
            row, row, pltpu.VMEM((3, n, D), BF), row, full, row,
            pltpu.VMEM((2, n, HALF), F32), pltpu.VMEM((2, n, HALF), BF), full, pltpu.VMEM((3, 1, D), F32), row,
            pltpu.SemaphoreType.DMA((8,)),
        ],
        compiler_params=params(LIMIT),
        cost_estimate=cost(2e+10, 1e5),
        name="target",
    )(ids, visible, order, *vecs, rows, *weights)


def regress_kernel(group, ids, visible, gains, biases, qvb, upb, lat_in, x_in, q_in, dyb_in, wqkv, wo, w1, w2,
                   dlat_out, res_out, hk_out, dq_out, dkv_out, o_out, dy1b_out, h2_out, du_out, a_out, dy1_out,
                   sums_out,
                   sqkv, so, s1, s2, x, lat, hk, q, kv, p, o, y1, h2, gp, a, u, tile, acc, shifts,
                   res, dyb, du, dy1, dy1b, do, dq, dkv, dh, dlat, sums, sems):
    n, m = GROUP * NM, GROUP * NV
    k, v = kv.at[0], kv.at[1]

    @pl.when(ids[0] == 1)
    def _():
        copies = Copies(sems)
        gain, bias = gains.at[0], biases.at[0]
        got_lat = copies.start(lat_in, lat)
        got_kv = copies.start(wqkv.at[0, :, pl.ds(D, 2 * D)], sqkv)
        got_q = copies.start(q_in, q)
        got_x = copies.start(x_in, x)
        got_weights = start_weights(copies, (wo.at[0], w1.at[0], w2.at[0]), (so, s1, s2))
        got_dyb = copies.start(dyb_in, dyb)
        set_biases(shifts, qvb)
        copies.wait(got_lat)
        norm_rows(lat, hk, m, f32_row(gain, 0), f32_row(bias, 0))
        copies.start(hk, hk_out)
        copies.wait(got_kv)

        def keep_kv(j, value):
            kv[j] = (value + shifts[j + 1]).astype(BF)

        project(2, m, hk, sqkv, 0, keep_kv)
        copies.wait(got_q, got_x)

        def key_ok(i):
            return lax.broadcasted_iota(jnp.int32, (NV, 1), 0) < visible[group * GROUP + i]

        attention_by_columns(GROUP, NV, q, k, v, p, o, key_ok)
        copies.start(o, o_out)
        block_end(copies, n, got_weights, so, s1, s2, bias, gain, upb, x, o, y1, h2, a, gp, u, tile, acc, res)
        copies.start(res, res_out)
        copies.start(h2, h2_out)
        copies.start(a, a_out)
        copies.wait(got_dyb)
        mlp_back(n, dyb, gp, s1, s2, du, u, acc)
        copies.start(du, du_out)

        def keep(sel, dx):
            dy1[sel, :] = dx
            dy1b[sel, :] = dx.astype(BF)

        g2, b2 = norm_back(y1, acc, dyb, keep, n, f32_row(gain, 1))
        copies.start(dy1, dy1_out)
        copies.start(dy1b, dy1b_out)
        do[...] = nt(dy1b[...], so[...]).astype(BF)
        attention_back_columns(GROUP, NV, q, k, v, p, do, dq, dkv)
        copies.start(dq, dq_out)
        copies.start(dkv, dkv_out)
        dh[...] = nt(dkv[:, :D], sqkv[:, :D])
        dh[...] += nt(dkv[:, D:], sqkv[:, D:])

        def keep_side(sel, dx):
            dlat[sel, :] = dx.astype(BF)

        gk, bk = norm_back(lat, dh, None, keep_side, m, f32_row(gain, 0))
        copies.start(dlat, dlat_out)
        for row, value in enumerate((gk, g2, bk, b2)):
            sums[pl.ds(row, 1), :] = value
        copies.start(sums, sums_out)
        copies.finish()


def regress(group, ids, visible, vecs, lat, x, q, dyb, weights):
    n, m = GROUP * NM, GROUP * NV
    row, side, wide = struct((n, D)), struct((m, D)), struct((n, FF))
    pair = struct((m, 2 * D))
    outs = [side, row, side, row, pair, row, row, row, wide, wide, struct((n, D), F32), struct((8, D), F32)]
    vm = lambda s: pltpu.VMEM(s.shape, s.dtype)
    full, fside = pltpu.VMEM((n, D), F32), pltpu.VMEM((m, D), F32)
    scratch = [
        pltpu.VMEM((D, 2 * D), BF), pltpu.VMEM((D, D), BF), pltpu.VMEM((D, FF), BF), pltpu.VMEM((FF, D), BF),
        vm(row), vm(side), vm(side), vm(row), pltpu.VMEM((2, m, D), BF),
        pltpu.VMEM((GROUP * PAIRS, NV, 2 * NM), BF), vm(row), full, vm(row), vm(wide), vm(wide),
        pltpu.VMEM((2, n, HALF), F32), pltpu.VMEM((2, n, HALF), BF), full, pltpu.VMEM((3, 1, D), F32),
        vm(row), vm(row), vm(wide), full, vm(row), vm(row), vm(row), vm(pair), fside, vm(side),
        pltpu.VMEM((8, D), F32),
        pltpu.SemaphoreType.DMA((24,)),
    ]
    return pl.pallas_call(
        partial(regress_kernel, group),
        in_specs=[SMEM, SMEM] + [VMEM] * 4 + [HBM] * 8,
        out_specs=[HBM] * len(outs),
        out_shape=outs,
        scratch_shapes=scratch,
        compiler_params=params(LIMIT),
        cost_estimate=cost(4 * n * 12 * D * D, 25e6),
        name="regress",
    )(ids, visible, *vecs, lat, x, q, dyb, *weights)


def stack_rows(copies, pieces, ref, size):
    return [copies.start(piece, ref.at[pl.ds(i * size, size)]) for i, piece in enumerate(pieces)]


class BlockLoads:
    def __init__(self, copies, ids, groups, blocks, sources, dest):
        self.copies, self.ids, self.groups, self.sources, self.dest = copies, ids, groups, sources, dest
        self.first = copies.take(groups * blocks)

    def each(self, role, j, like, act):
        for g, (src, size) in enumerate(self.sources(role, like)):
            act(src, self.dest(j).at[pl.ds(g * size, size)], self.first + j * self.groups + g)

    def begin(self, role, j):
        self.each(role, j, j, self.copies.begin)

    def wait(self, j, like=0):
        for role in range(2):
            pl.when(self.ids[0] == role)(lambda role=role: self.each(role, j, like, self.copies.wait_at))


def clear_tail(ref, used):
    ref[pl.ds(used, ref.shape[0] - used), :] = jnp.zeros((ref.shape[0] - used, ref.shape[1]), ref.dtype)


def halves(count, blocks):
    rows = D // 16
    if count == 16:
        return [struct((2, 2, 2, blocks, rows, D))] + [struct((2, blocks, rows, D))] * 4
    return [struct((D, D))] * blocks


def give_blocks(copies, core, tree, left_right, out, dest):
    size = 8 if tree else 1
    blocks = out.shape[0]
    first = copies.take(blocks * size)

    def send(j, act):
        if not tree:
            for block in range(blocks):
                pl.when(j == block)(lambda block=block: act(out.at[block], dest[block], first + block))
            return
        view = out.at[j].reshape(2, 2, 2, 2, D // 16, D)
        for x in range(2):
            for low in range(2):
                at = first + j * size + 4 * x + 2 * low
                act(view.at[:, low, x, core], dest[0].at[x, low, :, j], at)
                act(view.at[:, low, x, 1 - core], dest[1 + 2 * x + low].at[:, j], at + 1)

    def body(j):
        out[j] = left_right(j)
        send(j, copies.begin)

    loop(blocks, body)
    loop(blocks, lambda j: send(j, copies.wait_at))


def give_rows(copies, core, tree, multiply, out, dest):
    size = 4 if tree else 1
    first = copies.take(4 * size)

    def send(j, act):
        if not tree:
            act(out.at[j], dest[0].at[pl.ds(pl.multiple_of(j * D, D), D)], first + j)
            return
        view = out.at[j].reshape(2, 2, D // 4, D)
        low, high = lax.rem(j, 2), lax.div(j, 2)
        for x in range(2):
            at = first + j * size + 2 * x
            act(view.at[x, core], dest[0].at[x, low, high, 0], at)
            act(view.at[x, 1 - core], dest[1].at[x, low, high, 0], at + 1)

    def body(j):
        out[j] = multiply(j)
        send(j, copies.begin)

    loop(4, body)
    loop(4, lambda j: send(j, copies.wait_at))


def down_kernel(groups, parts, ids, *refs):
    cot, lat, a_enc, a_reg, dyb_reg = (refs[i * groups : (i + 1) * groups] for i in range(5))
    refs = refs[5 * groups :]
    dest, refs = refs[:parts], refs[parts:]
    sums_out, cot_v, dyb, a, dlat, out, sums, sems = refs
    images = groups * GROUP
    nv, nm = GROUP * NV, GROUP * NM

    copies = Copies(sems)
    pieces = (a_enc, a_reg)

    def sources(role, j):
        return [(one.at[:, pl.ds(j * D, D)], (nv, nm)[role]) for one in pieces[role]]

    loads = BlockLoads(copies, ids, groups, 4, sources, lambda j: a.at[j])

    @pl.when(ids[0] == 0)
    def _():
        early = copies.part()
        got = stack_rows(early, cot, cot_v, nv) + stack_rows(early, lat, dlat, nv)
        for j in range(4):
            loads.begin(0, j)
        early.wait(*got)
        dyb[...] = (cot_v[...].astype(F32) + dlat[...].astype(F32)).astype(BF)

    @pl.when(ids[0] == 1)
    def _():
        early = copies.part()
        got = stack_rows(early, dyb_reg, dyb, nm)
        for j in range(4):
            loads.begin(1, j)
            clear_tail(a.at[j], images * NM)
        clear_tail(dyb, images * NM)
        early.wait(*got)

    copies.take(2 * groups)

    def multiply(j):
        loads.wait(j)
        return tn(a[j], dyb[...]).astype(BF)

    give_rows(copies, ids[1], parts == 2, multiply, out, dest)
    sums[...] = jnp.broadcast_to(column_sum(dyb, images * NV), (8, D))
    copies.start(sums, sums_out)
    copies.finish()


def down_grad(groups, count, ids, cot, dlat, a_enc, a_reg, dyb_reg):
    n = groups * GROUP * NV
    main = [struct((2, 2, 2, 1, D // 4, D))] * 2 if count == 16 else [struct((FF, D))]
    outs = main + [struct((8, D), F32)]
    row = pltpu.VMEM((n, D), BF)
    scratch = [
        row, row, pltpu.VMEM((4, n, D), BF), row, pltpu.VMEM((4, D, D), BF), pltpu.VMEM((8, D), F32),
        pltpu.SemaphoreType.DMA((36,)),
    ]
    got = pl.pallas_call(
        partial(down_kernel, groups, len(main)),
        in_specs=[SMEM] + [HBM] * (5 * groups),
        out_specs=[HBM] * len(outs),
        out_shape=outs,
        scratch_shapes=scratch,
        compiler_params=params(LIMIT),
        cost_estimate=cost(1e6, 1e5),
        name="down_grad",
    )(ids, *cot, *dlat, *a_enc, *a_reg, *dyb_reg)
    return got[: len(main)], got[-1]


def pick_kernel(groups, ids, visible, order_in, cot, *refs):
    picked = refs[:groups]
    order, rows_v, flat, cot_v, sems = refs[groups:]

    @pl.when(ids[0] == 0)
    def _():
        copies = Copies(sems)
        got = copies.start(cot.at[0], rows_v)
        split_orders(order_in, order)
        copies.wait(got)
        flatten(rows_v, flat)

        def pick_rows(image):
            pick = pick_matrix(order, image, 0, NV, 0, visible[image])
            cot_v[rows_of(image, NV), :] = nn(pick, flat[...]).astype(BF)

        loop(groups * GROUP, pick_rows)
        for g in range(groups):
            copies.start(cot_v.at[pl.ds(g * GROUP * NV, GROUP * NV)], picked[g])
        copies.finish()


def pick_cot(groups, ids, visible, order, cot):
    images = order.shape[0]
    outs = [struct((GROUP * NV, D))] * groups
    return list(pl.pallas_call(
        partial(pick_kernel, groups),
        in_specs=[SMEM, SMEM, VMEM, HBM],
        out_specs=[HBM] * groups,
        out_shape=outs,
        scratch_shapes=[
            pltpu.VMEM((images, 1, PATCH), jnp.int32),
            pltpu.VMEM((PATCH, images, D), BF), pltpu.VMEM((PATCH * images, D), BF),
            pltpu.VMEM((images * NV, D), BF), pltpu.SemaphoreType.DMA((8,)),
        ],
        compiler_params=params(LIMIT),
        cost_estimate=cost(1e6, 1e5),
        name="pick_cot",
    )(ids, visible, order, cot))


def mlp_kernel(ids, gains, cot, dlat_in, w1, w2, y1_in, gp_in, du_out, dy1_out, dy1b_out, sums_out,
               s1, s2, cot_v, dlat, dyb, gp, y1, du, u, acc, dy1, dy1b, sums, sems):
    n = GROUP * NV
    third = FF // 3

    @pl.when(ids[0] == 0)
    def _():
        copies = Copies(sems)
        got = [copies.start(dlat_in, dlat), copies.start(cot, cot_v)]
        start = copies.take(9)

        def parts(i):
            cols = pl.ds(pl.multiple_of(i * third, third), third)
            return (
                (w2.at[0, cols, :], s2.at[cols, :]),
                (gp_in.at[:, cols], gp.at[:, cols]),
                (w1.at[0, :, cols], s1.at[:, cols]),
            )

        for i in range(3):
            for k, (src, dst) in enumerate(parts(i)):
                copies.begin(src, dst, start + 3 * i + k)
        got_y = copies.start(y1_in, y1)

        def ready(i, which):
            for k in ((0, 1), (2,))[which]:
                copies.wait_at(*parts(i)[k], start + 3 * i + k)

        copies.wait(*got)
        dyb[...] = (cot_v[...].astype(F32) + dlat[...].astype(F32)).astype(BF)
        mlp_back(n, dyb, gp, s1, s2, du, u, acc, ready)
        copies.start(du, du_out)
        copies.wait(got_y)

        def keep(sel, dx):
            dy1[sel, :] = dx
            dy1b[sel, :] = dx.astype(BF)

        g2, b2 = norm_back(y1, acc, dyb, keep, n, f32_row(gains.at[0], 1))
        copies.start(dy1, dy1_out)
        copies.start(dy1b, dy1b_out)
        sums[pl.ds(0, 1), :] = g2
        sums[pl.ds(1, 1), :] = b2
        copies.start(sums, sums_out)
        copies.finish()


def mlp_grad(ids, gains, cot, dlat, w1, w2, y1, gp):
    n = GROUP * NV
    row, wide, full = pltpu.VMEM((n, D), BF), pltpu.VMEM((n, FF), BF), pltpu.VMEM((n, D), F32)
    outs = [struct((n, FF)), struct((n, D), F32), struct((n, D)), struct((8, D), F32)]
    return pl.pallas_call(
        mlp_kernel,
        in_specs=[SMEM, VMEM] + [HBM] * 6,
        out_specs=[HBM] * len(outs),
        out_shape=outs,
        scratch_shapes=[
            pltpu.VMEM((D, FF), BF), pltpu.VMEM((FF, D), BF), row, row, row, wide, full, wide,
            pltpu.VMEM((2, n, HALF), F32), full, full, row, pltpu.VMEM((8, D), F32), pltpu.SemaphoreType.DMA((24,)),
        ],
        compiler_params=params(LIMIT),
        cost_estimate=cost(1e6, 1e5),
        name="mlp_grad",
    )(ids, gains, cot, dlat, w1, w2, y1, gp)


def up_kernel(groups, parts, ids, *refs):
    pieces = [refs[i * groups : (i + 1) * groups] for i in range(8)]
    refs = refs[8 * groups :]
    dest, refs = refs[:parts], refs[parts:]
    sums_out, left, right, out, sums, sems = refs
    images = groups * GROUP

    nv, nm = GROUP * NV, GROUP * NM
    copies = Copies(sems)
    sides = (pieces[:4], pieces[4:])

    def sources(role, j):
        du, _, dy1b, _ = sides[role]
        ones = dy1b if j == 4 else [one.at[:, pl.ds(j * D, D)] for one in du]
        return [(one, (nv, nm)[role]) for one in ones]

    def lefts(role, i):
        _, h2, _, o = sides[role]
        return [(one, (nv, nm)[role]) for one in (h2, o)[i]]

    loads = BlockLoads(copies, ids, groups, 5, sources, lambda j: right.at[j])
    shared = BlockLoads(copies, ids, groups, 2, lefts, lambda i: left.at[i])
    for role in range(2):

        @pl.when(ids[0] == role)
        def _(role=role):
            shared.begin(role, 0)
            for j in range(5):
                loads.begin(role, j)
            shared.begin(role, 1)
            if role == 1:
                for ref in (left, right):
                    for i in range(ref.shape[0]):
                        clear_tail(ref.at[i], images * NM)

    shared.wait(0)

    def multiply(j):
        loads.wait(j)
        pl.when(j == 4)(lambda: shared.wait(1))
        value = tn(left[lax.div(j, 4)], right[j]).astype(BF)
        sums[pl.ds(j, 1), :] = column_sum(right.at[j], images * NV)
        return value

    give_blocks(copies, ids[1], dest[0].ndim == 6, multiply, out, dest)
    copies.start(sums, sums_out)
    copies.finish()


def up_grad(groups, count, ids, *pieces):
    n = groups * GROUP * NV
    main = halves(count, 5)
    outs = main + [struct((8, D), F32)]
    got = pl.pallas_call(
        partial(up_kernel, groups, len(main)),
        in_specs=[SMEM] + [HBM] * (8 * groups),
        out_specs=[HBM] * len(outs),
        out_shape=outs,
        scratch_shapes=[
            pltpu.VMEM((2, n, D), BF), pltpu.VMEM((5, n, D), BF), pltpu.VMEM((5, D, D), BF), pltpu.VMEM((8, D), F32),
            pltpu.SemaphoreType.DMA((60,)),
        ],
        compiler_params=params(LIMIT),
        cost_estimate=cost(1e6, 1e5),
        name="up_grad",
    )(ids, *[ref for piece in pieces for ref in piece])
    return got[: len(main)], got[-1]


def attn_kernel(groups, last, ids, gains, *refs):
    if last:
        down_sums, up_sums, refs = refs[0], refs[1], refs[2:]
        mlp_sums, reg_sums = (refs[i * groups : (i + 1) * groups] for i in range(2))
        before, refs = refs[2 * groups : 3 * groups - 1], refs[3 * groups - 1 :]
    (wqkv, wo, dy1_enc, q_in, k_in, v_in, p_in, x_enc, dq_reg, dkv_reg, dy1_reg, x_reg,
     dq_out, dkv_out, dx_out, sums_out,
     sqkv, so, dy1, dy1b, q, k, v, p, x, do, dq, dkv, dh, sems) = refs
    m = GROUP * NM
    top = pl.ds(0, m)
    gain = f32_row(gains.at[0], 0)

    def finish(copies, rows):
        def keep(sel, dx):
            dy1[sel, :] = dx

        own = (*norm_back(x, dh, dy1, keep, rows, gain), column_sum(dq, rows), column_sum(dkv, GROUP * NV, D))
        copies.start(dy1, dx_out)
        if not last:
            for row, value in enumerate(own):
                sums_out[row : row + 1, :] = value
            copies.finish()
            return

        def total_of(sums):
            total = sums[0][...]
            for more in sums[1:]:
                total = total + more[...]
            return total

        done, mlp, reg = total_of(before), total_of(mlp_sums), total_of(reg_sums)
        g1, b1, queries, values = (one + done[row : row + 1, :] for row, one in enumerate(own))
        encoder = ids[0] == 0
        sums_out[0:1, :] = g1 + jnp.where(encoder, 0.0, reg[0:1, :])
        sums_out[1:2, :] = jnp.where(encoder, mlp[0:1, :], reg[1:2, :])
        sums_out[2:3, :] = b1 + jnp.where(encoder, 0.0, reg[2:3, :])
        sums_out[3:4, :] = up_sums[4:5, :]
        sums_out[4:5, :] = jnp.where(encoder, mlp[1:2, :], reg[3:4, :])
        sums_out[5:6, :] = down_sums[0:1, :]
        sums_out[6:7, :] = queries
        sums_out[7:8, :] = values
        sums_out[8:12, :] = up_sums[0:4, :]
        sums_out[12:16, :] = jnp.zeros((4, D), F32)
        copies.finish()

    @pl.when(ids[0] == 0)
    def _():
        copies = Copies(sems)
        got = [copies.start(dy1_enc, dy1), copies.start(wo.at[0], so)]
        later = [copies.start(src, dst) for src, dst in ((v_in, v), (p_in, p), (k_in, k), (q_in, q))]
        final = [copies.start(wqkv.at[0], sqkv), copies.start(x_enc, x)]
        copies.wait(*got)
        dy1b[...] = dy1[...].astype(BF)
        do[...] = nt(dy1b[...], so[...]).astype(BF)
        copies.wait(*later)
        attention_back_rows(GROUP, NV, q, k, v, p, do, dq, dkv)
        copies.start(dq, dq_out)
        copies.start(dkv, dkv_out)
        copies.wait(*final)
        dh[...] = nt(dq[...], sqkv[:, 0:D])
        for j in range(2):
            dh[...] += nt(dkv[:, j * D : (j + 1) * D], sqkv[:, (j + 1) * D : (j + 2) * D])
        finish(copies, GROUP * NV)

    @pl.when(ids[0] == 1)
    def _():
        copies = Copies(sems)
        for src, dst in ((dq_reg, dq), (dy1_reg, dy1), (x_reg, x)):
            copies.start(src, dst.at[top])
        copies.start(dkv_reg, dkv)
        copies.start(wqkv.at[0, :, pl.ds(0, D)], sqkv.at[:, pl.ds(0, D)])
        copies.finish()
        dh[top, :] = nt(dq[top, :], sqkv[:, 0:D])
        finish(copies, m)


def attn_back(groups, last, ids, gains, sums, *pieces):
    n = GROUP * NV
    row, full = pltpu.VMEM((n, D), BF), pltpu.VMEM((n, D), F32)
    outs = [struct((n, D)), struct((n, 2 * D)), struct((n, D), F32), struct((16, D), F32)]
    return pl.pallas_call(
        partial(attn_kernel, groups, last),
        in_specs=[SMEM, VMEM] + [VMEM] * len(sums) + [HBM] * len(pieces),
        out_specs=[HBM] * 3 + [VMEM],
        out_shape=outs,
        scratch_shapes=[
            pltpu.VMEM((D, 3 * D), BF), pltpu.VMEM((D, D), BF), full, row, row, row, row,
            pltpu.VMEM((GROUP * PAIRS, 2 * NV, NV), BF), row, row, row, pltpu.VMEM((n, 2 * D), BF), full,
            pltpu.SemaphoreType.DMA((20,)),
        ],
        compiler_params=params(LIMIT),
        cost_estimate=cost(1e6, 1e5),
        name="attn_back",
    )(ids, gains, *sums, *pieces)


def qkv_kernel(groups, parts, ids, *refs):
    pieces = [refs[i * groups : (i + 1) * groups] for i in range(7)]
    dq_enc, dkv_enc, hq_enc, hq_reg, hk_reg, dq_reg, dkv_reg = pieces
    refs = refs[7 * groups :]
    dest, refs = refs[:parts], refs[parts:]
    left, right, out, sems = refs
    images = groups * GROUP
    nv, nm = GROUP * NV, GROUP * NM
    copies = Copies(sems)

    def sources(role, j):
        if j == 2:
            return [(one, (nv, nm)[role]) for one in (dq_enc, dq_reg)[role]]
        return [(one.at[:, pl.ds(j * D, D)], nv) for one in (dkv_enc, dkv_reg)[role]]

    def lefts(role, i):
        if role == 0:
            return [(one, nv) for one in hq_enc]
        return [(one, (nv, nm)[i]) for one in (hk_reg, hq_reg)[i]]

    loads = BlockLoads(copies, ids, groups, 3, sources, lambda j: right.at[j])
    shared = BlockLoads(copies, ids, groups, 2, lefts, lambda i: left.at[i])
    for role in range(2):

        @pl.when(ids[0] == role)
        def _(role=role):
            shared.begin(role, 0)
            for j in range(3):
                loads.begin(role, j)
            shared.begin(role, 1)
            if role == 1:
                clear_tail(left.at[1], images * NM)
                clear_tail(right.at[2], images * NM)

    shared.wait(0)

    def multiply(j):
        for block in range(3):

            @pl.when(j == block)
            def _(block=block):
                loads.wait(block, block)
                if block == 2:
                    shared.wait(1, 1)

        return tn(left[lax.div(j, 2)], right[j]).astype(BF)

    give_blocks(copies, ids[1], dest[0].ndim == 6, multiply, out, dest)


def qkv_grad(groups, count, ids, *pieces):
    n = groups * GROUP * NV
    row = pltpu.VMEM((n, D), BF)
    main = halves(count, 3)
    scratch = [
        pltpu.VMEM((2, n, D), BF), pltpu.VMEM((3, n, D), BF), pltpu.VMEM((3, D, D), BF),
        pltpu.SemaphoreType.DMA((40,)),
    ]
    return pl.pallas_call(
        partial(qkv_kernel, groups, len(main)),
        in_specs=[SMEM] + [HBM] * (7 * groups),
        out_specs=[HBM] * len(main),
        out_shape=main,
        scratch_shapes=scratch,
        compiler_params=params(LIMIT),
        cost_estimate=cost(1e6, 1e5),
        name="qkv_grad",
    )(ids, *[ref for piece in pieces for ref in piece])


def place_kernel(groups, ids, visible, order_in, *refs):
    dx_in, lat_enc, res_enc, res_reg = (refs[i * groups : (i + 1) * groups] for i in range(4))
    block_out, grad_out, order, dx, lat, out, grads, sems = refs[4 * groups :]
    images = groups * GROUP
    nv, nm = GROUP * NV, GROUP * NM
    split_orders(order_in, order)

    def put_grad(i, put, value):
        high = value.astype(BF)
        low = (value - high.astype(F32)).astype(BF)
        grads[i] = nn(put, high) + nn(put, low)

    def write_grads():
        copies = Copies(sems)
        for i in range(images):
            copies.start(grads.at[i], grad_out.at[0, :, i, :])
        copies.finish()

    @pl.when(ids[0] == 0)
    def _():
        copies = Copies(sems)
        for piece, ref, size in ((dx_in, dx, nv), (lat_enc, lat, nv), (res_enc, out, nm)):
            stack_rows(copies, piece, ref, size)
        copies.finish()

        def put_image(i):
            put = place_matrix(order, i, 0, NV, 0, visible[i])
            put_side = place_matrix(order, i, FIRST, NM, visible[i], PATCH)
            put_grad(i, put, dx[rows_of(i, NV), :])
            block_out[0, i] = (nn(put, lat[rows_of(i, NV), :]) + nn(put_side, out[rows_of(i, NM), :])).astype(BF)

        loop(images, put_image)
        write_grads()

    @pl.when(ids[0] == 1)
    def _():
        copies = Copies(sems)
        stack_rows(copies, res_reg, out, nm)
        stack_rows(copies, [piece.at[pl.ds(0, nm)] for piece in dx_in], dx, nm)
        copies.finish()

        def put_image(i):
            put = place_matrix(order, i, FIRST, NM, visible[i], PATCH)
            put_grad(i, put, dx[rows_of(i, NM), :])
            block_out[0, i] = nn(put, out[rows_of(i, NM), :]).astype(BF)

        loop(images, put_image)
        write_grads()


def place(groups, ids, visible, order, *pieces):
    images = groups * GROUP
    n = images * NV
    outs = [struct((1, images, PATCH, D)), struct((1, PATCH, images, D), F32)]
    return pl.pallas_call(
        partial(place_kernel, groups),
        in_specs=[SMEM, SMEM, VMEM] + [HBM] * (4 * groups),
        out_specs=[VMEM, HBM],
        out_shape=outs,
        scratch_shapes=[
            pltpu.VMEM((images, 1, PATCH), jnp.int32), pltpu.VMEM((n, D), F32), pltpu.VMEM((n, D), BF),
            pltpu.VMEM((images * NM, D), BF), pltpu.VMEM((images, PATCH, D), F32), pltpu.SemaphoreType.DMA((8,)),
        ],
        compiler_params=params(LIMIT),
        cost_estimate=cost(1e+06, 1e5),
        name="place",
    )(ids, visible, order, *[ref for piece in pieces for ref in piece])


BITS = (2, 4, 8)


def hop(value, bit):
    return lax.ppermute(value, "dp", [(i, i ^ bit) for i in range(16)])


def combine_kernel(jobs, given, ids, *refs):
    used = sum(sum(4 if gone is None else 1 for gone in terms) for terms, *_ in jobs)
    inputs, outs, scratch = list(refs[:used]), list(refs[used : used + given]), list(refs[used + given :])
    copies = Copies(scratch.pop())
    plans = []

    def fetch(term, gone, bits, own):
        if gone is not None:
            path = tuple(bits[gone:])
            copy = copies.start(term.at[path] if path else term, own)
            return lambda: copies.wait(copy)
        wide = len(bits) == 1
        first = copies.take(2 if wide else 1)
        rest = tuple(bits[2:])

        def piece(x, low):
            ref = term[2 * x + low]
            return ref.at[rest] if rest else ref

        for x in range(2):
            for low in range(2):
                if wide:
                    pl.when(bits[0] == x)(
                        lambda x=x, low=low: copies.begin(piece(x, low), own.at[low], first + low)
                    )
                else:
                    pl.when((bits[0] == x) & (bits[1] == low))(
                        lambda x=x, low=low: copies.begin(piece(x, low), own, first)
                    )

        def wait():
            if wide:
                for low in range(2):
                    copies.wait_at(piece(0, low), own.at[low], first + low)
            else:
                copies.wait_at(piece(0, 0), own, first)

        return wait

    for kinds, first, last, targets, finals in jobs:
        terms = [inputs.pop(0) if gone is not None else [inputs.pop(0) for _ in range(4)] for gone in kinds]
        for target in targets:
            bits = []
            for bit in range(last):
                flip = bit >= first and (target >> (bit - first)) & 1
                bits.append(1 - ids[2 + bit] if flip else ids[2 + bit])
            owns = [scratch.pop(0) for _ in kinds]
            waits = [fetch(term, gone, bits, own) for term, gone, own in zip(terms, kinds, owns)]
            plans.append((waits, owns, last, finals, None if finals else outs.pop(0)))
    for waits, owns, last, finals, out in plans:
        for wait in waits:
            wait()
        spots = [()]
        for _ in range(3 - last):
            spots = [spot + (i,) for spot in spots for i in range(2)]
        for spot in spots:
            for j in range(owns[0].shape[-3]):
                value = owns[0][spot + (j,)].astype(F32)
                for more in owns[1:]:
                    value = value + more[spot + (j,)].astype(F32)
                if finals:
                    which, column = finals[j]
                    outs[which][:, column * D : (column + 1) * D] = value
                else:
                    out[spot + (j,)] = value.astype(BF)


def send_job(terms, first, last, targets=(1,)):
    return terms, first, last, targets, None


def final_job(terms, finals):
    return terms, 0, 3, (0,), finals


def combine(ids, *jobs, outs=()):
    shapes = [struct(shape, F32) for shape in outs]
    plans, inputs, scratch = [], [], []
    for terms, first, last, targets, finals in jobs:
        blocks, rows = terms[0].shape[-3:-1]
        kinds = tuple(None if isinstance(term, list) else 6 - term.ndim for term in terms)
        for term in terms:
            inputs += term if isinstance(term, list) else [term]
        plans.append((kinds, first, last, targets, finals))
        part = (2,) * (3 - last) + (blocks, rows, D)
        for _ in targets:
            scratch += [pltpu.VMEM(part, BF) for _ in terms]
            if finals is None:
                shapes.append(struct(part))
    scratch.append(pltpu.SemaphoreType.DMA((2 * len(scratch),)))
    return pl.pallas_call(
        partial(combine_kernel, tuple(plans), len(shapes)),
        in_specs=[SMEM] + [HBM] * len(inputs),
        out_specs=[VMEM] * len(shapes),
        out_shape=shapes,
        scratch_shapes=scratch,
        compiler_params=params(LIMIT),
        cost_estimate=cost(1e5, 1e4),
        name="combine",
    )(ids, *inputs)


def in_order(first, then):
    return lax.optimization_barrier((first, then))


def own_columns(rows, count):
    own = D // count
    me = lax.axis_index("dp")

    def part(block, wide):
        return lax.dynamic_slice_in_dim(block, me * wide, wide, block.ndim - 1)

    return (
        part(rows[:2], own),
        part(rows[2:6], own),
        part(rows[6:8].reshape(-1), 2 * own),
        part(rows[8:12].reshape(-1), 4 * own),
    )


def scatter_natural(block):
    shards = block.reshape(lax.axis_size("dp"), -1, D)
    return lax.psum_scatter(shards, "dp", scatter_dimension=0, tiled=True)[0].astype(F32)


def local(
    patch_rows, cotangent, patch_order, visible, qkv_weight, out_weight, up_weight, down_weight, norm_gains, biases,
    qv_bias, up_bias, target_qkv, target_out, target_up, target_down, target_gains, target_biases, target_qv_bias,
    target_up_bias,
):
    count = lax.axis_size("dp")
    tree = count == 16
    place_dp = lax.axis_index("dp")
    bits = [(place_dp // bit) % 2 for bit in (1,) + BITS]
    ids = jnp.stack([lax.axis_index("section")] + bits).astype(jnp.int32)
    groups = patch_order.shape[0] // GROUP
    weights = (qkv_weight, out_weight, up_weight, down_weight)
    targets = (target_qkv, target_out, target_up, target_down)
    vecs = (norm_gains, biases, qv_bias, up_bias)
    target_vecs = (target_gains, target_biases, target_qv_bias[None], target_up_bias[None])

    rows, cot = patch_rows.transpose(0, 2, 1, 3), cotangent.transpose(0, 2, 1, 3)
    calls = [
        encode(g, groups, ids, visible, patch_order, *vecs, rows, cot, weights) for g in range(groups)
    ]
    lat, x_e, hq_e, q_e, k_e, v_e, p_e, o_e, y1_e, h2_e, gp_e, a_e = zip(*[call[0] for call in calls])
    x_r, hq_r, q_r, dyb_r = calls[-1][1]
    sent = [lax.ppermute(piece, "section", [(0, 1)]) for piece in lat]
    vectors = (norm_gains, biases, qv_bias, up_bias)
    regressed = [regress(0, ids, visible, vectors, sent[0], x_r[0], q_r[0], dyb_r[0], weights)]
    back = [lax.ppermute(regressed[0][0], "section", [(1, 0)])]
    order_first, regressed[0] = in_order(patch_order, regressed[0])
    res_e = [target(0, ids, visible, order_first, target_vecs, rows, targets)]
    res_e[0], sent[1:] = in_order(res_e[0], sent[1:])
    for g in range(1, groups):
        regressed.append(regress(g, ids, visible, vectors, sent[g], x_r[g], q_r[g], dyb_r[g], weights))
        back.append(lax.ppermute(regressed[g][0], "section", [(1, 0)]))
    _, res_r, hk_r, dq_r, dkv_r, o_r, dy1b_r, h2_r, du_r, a_r, dy1_r, sums_r = zip(*regressed)

    order_next, res_r = in_order(patch_order, res_r)
    cot_e = pick_cot(groups, ids, visible, order_next, cot)
    cot_e, back[0] = in_order(cot_e, back[0])

    def mlp(g, cot):
        return mlp_grad(ids, norm_gains, cot, back[g], up_weight, down_weight, y1_e[g], gp_e[g])

    def attention(g, dy1, sums=()):
        return attn_back(
            groups, len(sums) > 0, ids, norm_gains, sums, qkv_weight, out_weight, dy1, q_e[g], k_e[g], v_e[g], p_e[g],
            x_e[g], dq_r[g], dkv_r[g], dy1_r[g], x_r[g],
        )

    mlps = [mlp(g, cot_e[g]) for g in range(groups - 1)]
    attns = [attention(g, mlps[g][1]) for g in range(groups - 1)]
    last = groups - 1
    send = partial(combine, ids)
    attns, back[last] = in_order(attns, back[last])
    down, sums_down = down_grad(groups, count, ids, cot_e, back, a_e, a_r, dyb_r)
    cot_last = cot_e[last]
    down, cot_last = in_order(down, cot_last)
    mlps.append(mlp(last, cot_last))
    du_e, dy1_e, dy1b_e, sums_e = (list(piece) for piece in zip(*mlps))
    if tree:
        downs = [down[0], hop(down[1], 1)]
        (down_x,), du_e[last] = in_order(send(send_job(downs, 0, 1)), du_e[last])
        downs = downs + [hop(down_x, 2)]
    up, sums_up = up_grad(groups, count, ids, du_e, h2_e, dy1b_e, o_e, du_r, h2_r, dy1b_r, o_r)
    if tree:
        peers = (3, 2, 1)
        ups = [up[0], [hop(piece, 1) for piece in up[1:]]]
        (up_x,), downs[:2] = in_order(send(send_job(ups, 0, 1)), downs[:2])
        ups = ups + [hop(up_x, 2)]
        down_z, dy1_e[last] = in_order(send(send_job(downs, 1, 3, peers)), dy1_e[last])
        down_got = [hop(one, 4 * peer) for one, peer in zip(down_z, peers)]
    sums_in = [piece[3] for piece in attns]
    attns.append(attention(last, dy1_e[last], (sums_down, sums_up, *sums_e, *sums_r, *sums_in)))
    dq_e, dkv_e, dx, small = (list(piece) for piece in zip(*attns))
    small = small[last]
    order_late = patch_order
    if tree:
        small = small + hop(small, 1)
        small, dq_e[last] = in_order(small, dq_e[last])
    attn = qkv_grad(groups, count, ids, dq_e, dkv_e, hq_e, hq_r, hk_r, dq_r, dkv_r)
    if tree:
        (down_got, got), attn = in_order((down_got, hop(small, 2)), attn)
        small = small + got
        up_z, attn = in_order(send(send_job(ups, 1, 3, peers)), attn)
        up_got = [hop(one, 4 * peer) for one, peer in zip(up_z, peers)]
        qkvs = [attn[0], [hop(piece, 1) for piece in attn[1:]]]
        (qkv_x,), got = in_order(send(send_job(qkvs, 0, 1)), hop(small, 4))
        small = small + got
        order_late, qkv_x = in_order(patch_order, qkv_x)
        qkvs = qkvs + [hop(qkv_x, 2)]
        got = hop(small, 8)
    res_e += [target(g, ids, visible, order_late, target_vecs, rows, targets) for g in range(1, groups)]
    if tree:
        qkv_z, res_e = in_order(send(send_job(qkvs, 1, 3, peers)), res_e)
        qkv_got = [hop(one, 4 * peer) for one, peer in zip(qkv_z, peers)]
    block_out, grad_rows = place(groups, ids, visible, patch_order, dx, lat, res_e, res_r)
    if tree:
        small = small + got
        (block_out, grad_rows), up_got = in_order((block_out, grad_rows), up_got)
        down_sum, up_sum, out_sum = send(
            final_job(downs + down_got, ((0, 0),)),
            final_job(ups + up_got, tuple((1, j) for j in range(4)) + ((2, 0),)),
            outs=((D // 4, D), (D // 16, 4 * D), (D // 16, D)),
        )
        qkv_got, (down_sum, up_sum, out_sum) = in_order(qkv_got, (down_sum, up_sum, out_sum))
        (qkv_sum,) = send(final_job(qkvs + qkv_got, ((0, 1), (0, 2), (0, 0))), outs=((D // 16, 3 * D),))
    else:
        down_sum = scatter_natural(down[0])
        up_sum = jnp.concatenate([scatter_natural(one) for one in up[:4]], axis=1)
        out_sum = scatter_natural(up[4])
        qkv_sum = jnp.concatenate([scatter_natural(attn[i]) for i in (2, 0, 1)], axis=1)
        small = lax.psum(small, "dp")
    grad_rows = grad_rows.transpose(0, 2, 1, 3)
    gains, bias_rows, qv_rows, up_rows = own_columns(small, count)
    return (
        block_out,
        grad_rows,
        qkv_sum[None],
        out_sum[None],
        up_sum[None],
        down_sum[None],
        gains[None],
        bias_rows[None],
        qv_rows[None],
        up_rows[None],
    )


def solution(mesh):
    three, four = P("section", None, None), P("section", "dp", None, None)
    grad = P("section", "dp", None)
    return jax.shard_map(
        local,
        mesh=mesh,
        in_specs=(four, four, P("dp", None), P("dp"), three, three, three, three, three, three,
                  P("section", None), P("section", None), P(), P(), P(), P(), P(), P(), P(), P()),
        out_specs=(four, four, grad, grad, grad, grad, P("section", None, "dp"), P("section", None, "dp"),
                   P("section", "dp"), P("section", "dp")),
        check_vma=False,
    )
```

```python
from functools import partial

import jax
import jax.numpy as jnp
from jax import lax
from jax.experimental import pallas as pl
from jax.experimental.pallas import tpu as pltpu
from jax.sharding import PartitionSpec as P

HEADS = 12
PATCH = 196
D = 768
FF = 3072
EPS = 1e-06
NV = 144
NM = 128
FIRST = PATCH - NM
GROUP = 2
CHUNK = 32

BF = jnp.bfloat16
F32 = jnp.float32
MIB = 1024 * 1024
LIMIT = 62

HBM = pl.BlockSpec(memory_space=pl.ANY)
VMEM = pl.BlockSpec(memory_space=pltpu.VMEM)
SMEM = pl.BlockSpec(memory_space=pltpu.SMEM)


def nn(a, b):
    return jnp.dot(a, b, preferred_element_type=F32)


def nt(a, b):
    return lax.dot_general(a, b, (((1,), (1,)), ((), ())), preferred_element_type=F32)


def tn(a, b):
    return lax.dot_general(a, b, (((0,), (0,)), ((), ())), preferred_element_type=F32)


def loop(count, body, unroll=1):
    def step(i, carry):
        for u in range(unroll):
            body(i * unroll + u)
        return carry

    if count == unroll:
        step(0, 0)
    else:
        lax.fori_loop(0, count // unroll, step, 0)


def unroll_of(count):
    return next(u for u in (4, 3, 2, 1) if count % u == 0)


def rows_of(i, size):
    return pl.ds(pl.multiple_of(i * size, size), size)


def f32_row(ref, row, col=0, width=D):
    return ref[pl.ds(row, 1), pl.ds(col, width)].astype(F32)


class Copies:
    def __init__(self, sems):
        self.sems = sems
        self.used = 0
        self.open = []

    def start(self, src, dst):
        copy = pltpu.make_async_copy(src, dst, self.sems.at[self.used])
        self.used += 1
        copy.start()
        self.open.append(copy)
        return copy

    def wait(self, *copies):
        for copy in copies:
            copy.wait()
            self.open = [one for one in self.open if one is not copy]

    def finish(self):
        self.wait(*list(self.open))

    def take(self, count):
        self.used += count
        return self.used - count

    def part(self):
        other = Copies(self.sems)
        other.used = self.used
        return other

    def begin(self, src, dst, at):
        pltpu.make_async_copy(src, dst, self.sems.at[at]).start()

    def wait_at(self, src, dst, at):
        pltpu.make_async_copy(src, dst, self.sems.at[at]).wait()


def gelu_pair(u):
    size = jnp.abs(u)
    base = 1.0 + (0.3275911 * 0.7071067811865476) * size
    guess = pl.reciprocal(base, approx=True)
    t = guess * (2.0 - base * guess)
    ex = jnp.exp2((u * u) * (-0.5 * 1.4426950408889634))
    poly = 0.5306027145 * t - 0.7265760135
    poly = poly * t + 0.7107068705
    poly = poly * t - 0.142248368
    poly = poly * t + 0.127414796
    tail = poly * t * ex
    phi = jnp.where(u >= 0.0, 1.0 - tail, tail)
    return u * phi, phi + u * (0.3989422804014327 * ex)


def norm_rows(src, dst, rows, gain, shift):
    def body(i):
        sel = rows_of(i, CHUNK)
        x = src[sel, :].astype(F32)
        centered = x - jnp.mean(x, axis=-1, keepdims=True)
        var = jnp.mean(centered * centered, axis=-1, keepdims=True)
        dst[sel, :] = (centered * lax.rsqrt(var + EPS) * gain + shift).astype(BF)

    loop(rows // CHUNK, body, unroll_of(rows // CHUNK))


def norm_back(src, grad, base, write, rows, gain):
    count = rows // CHUNK
    unroll = 3 if count % 3 == 0 else 2

    def step(i, carry):
        for u in range(unroll):
            carry = one(i * unroll + u, carry)
        return carry

    def one(i, carry):
        d_gain, d_shift = carry
        sel = rows_of(i, CHUNK)
        x = src[sel, :].astype(F32)
        dh = grad[sel, :]
        centered = x - jnp.mean(x, axis=-1, keepdims=True)
        var = jnp.mean(centered * centered, axis=-1, keepdims=True)
        rstd = lax.rsqrt(var + EPS)
        hat = centered * rstd
        g = dh * gain
        part = dh * hat
        dx = rstd * (
            g
            - jnp.mean(g, axis=-1, keepdims=True)
            - hat * jnp.mean(g * hat, axis=-1, keepdims=True)
        )
        if base is not None:
            dx = dx + base[sel, :].astype(F32)
        write(sel, dx)
        d_gain = d_gain + jnp.sum(part.reshape(CHUNK // 8, 8, D), axis=0)
        d_shift = d_shift + jnp.sum(dh.reshape(CHUNK // 8, 8, D), axis=0)
        return d_gain, d_shift

    zero = jnp.zeros((8, D), F32)
    d_gain, d_shift = lax.fori_loop(0, count // unroll, step, (zero, zero))
    return jnp.sum(d_gain, axis=0, keepdims=True), jnp.sum(d_shift, axis=0, keepdims=True)


def column_sum(ref, rows, col=0, width=D):
    def step(i, carry):
        x = ref[rows_of(i, CHUNK), pl.ds(col, width)].astype(F32)
        return carry + jnp.sum(x.reshape(CHUNK // 8, 8, width), axis=0)

    total = lax.fori_loop(0, rows // CHUNK, step, jnp.zeros((8, width), F32))
    return jnp.sum(total, axis=0, keepdims=True)


def as_bf16(flags):
    return jnp.where(flags, 1.0, 0.0).astype(BF)


def pick_matrix(order, image, start, count, low, high):
    row = order[image, :, pl.ds(start, count)].astype(F32)
    images = order.shape[0]
    col = jnp.broadcast_to(row, (8, count)).T[:, 0:1].astype(jnp.int32)
    rank = start + lax.broadcasted_iota(jnp.int32, (count, 1), 0)
    col = jnp.where((rank >= low) & (rank < high), col * images + image, -1)
    return as_bf16(col == lax.broadcasted_iota(jnp.int32, (count, PATCH * images), 1))


def place_matrix(order, image, start, count, low, high):
    row = order[image, :, pl.ds(start, count)]
    rank = start + lax.broadcasted_iota(jnp.int32, (1, count), 1)
    row = jnp.where((rank >= low) & (rank < high), row, -1)
    return as_bf16(row == lax.broadcasted_iota(jnp.int32, (PATCH, count), 0))


def flatten(rows, flat):
    flat[...] = rows[...].reshape(flat.shape)


def split_orders(order, split):
    for image in range(split.shape[0]):
        split[image] = order[image : image + 1, :]


def split_pair(pair):
    lane = lax.broadcasted_iota(jnp.int32, pair.shape, 1)
    zero = jnp.zeros_like(pair)
    return jnp.concatenate([jnp.where(lane < 64, pair, zero), jnp.where(lane < 64, zero, pair)], axis=0)


def join_rows(both):
    rows = both.shape[0] // 2
    lane = lax.broadcasted_iota(jnp.int32, (rows, 128), 1)
    return jnp.where(lane < 64, both[:rows], both[rows:])


def join_columns(both):
    rows = both.shape[1] // 2
    return jnp.concatenate([both[:64, :rows], both[64:, rows:]], axis=0).T


PAIRS = HEADS // 2
STEP = 6


def each_pair_group(images, body):
    def group(i):
        image = i // (PAIRS // STEP)
        first = (i % (PAIRS // STEP)) * STEP
        pairs = [first + step for step in range(STEP)]
        body(image, [image * PAIRS + pair for pair in pairs], [pl.ds(pl.multiple_of(pair * 128, 128), 128) for pair in pairs])

    loop(images * (PAIRS // STEP), group)


def softmax(scores, axis):
    ex = jnp.exp(scores - jnp.max(scores, axis=axis, keepdims=True))
    return (ex * (1.0 / jnp.sum(ex, axis=axis, keepdims=True))).astype(BF)


def score_back(probs, d_probs, axis):
    wide = probs.astype(F32)
    return (wide * (d_probs - jnp.sum(d_probs * wide, axis=axis, keepdims=True))).astype(BF)


def attention_by_rows(images, n, q, k, v, p, o, count_of):
    def body(image, slots, lanes):
        sel = rows_of(image, n)
        ok = lax.broadcasted_iota(jnp.int32, (1, n), 1) < count_of(image)
        scores = [nt(split_pair(q[sel, at]), k[sel, at]) for at in lanes]
        probs = [softmax(jnp.where(ok, one, -1000000000.0), 1) for one in scores]
        for slot, one in zip(slots, probs):
            p[slot] = one
        mixed = [nn(one, v[sel, at]) for one, at in zip(probs, lanes)]
        for at, one in zip(lanes, mixed):
            o[sel, at] = join_rows(one).astype(BF)

    each_pair_group(images, body)


def attention_by_columns(images, nk, q, k, v, p, o, key_ok):
    def body(image, slots, lanes):
        qs, ks = rows_of(image, NM), rows_of(image, nk)
        ok = key_ok(image)
        scores = [nt(k[ks, at], split_pair(q[qs, at])) for at in lanes]
        probs = [softmax(jnp.where(ok, one, -1000000000.0), 0) for one in scores]
        if p is not None:
            for slot, one in zip(slots, probs):
                p[slot] = one
        mixed = [tn(v[ks, at], one) for one, at in zip(probs, lanes)]
        for at, one in zip(lanes, mixed):
            o[qs, at] = join_columns(one).astype(BF)

    each_pair_group(images, body)


def attention_back_rows(images, n, q, k, v, p, do, dq, dkv):
    def body(image, slots, lanes):
        sel = rows_of(image, n)
        d_mixed = [split_pair(do[sel, at]) for at in lanes]
        d_probs = [nt(one, v[sel, at]) for one, at in zip(d_mixed, lanes)]
        d_scores = [score_back(p[slot], one, 1) for slot, one in zip(slots, d_probs)]
        d_values = [tn(p[slot], one) for slot, one in zip(slots, d_mixed)]
        d_query = [nn(one, k[sel, at]) for one, at in zip(d_scores, lanes)]
        d_keys = [tn(one, split_pair(q[sel, at])) for one, at in zip(d_scores, lanes)]
        for at, value, query, key in zip(lanes, d_values, d_query, d_keys):
            dq[sel, at] = (join_rows(query) * 0.125).astype(BF)
            dkv[sel, at] = key.astype(BF)
            dkv[sel, pl.ds(pl.multiple_of(D + at.start, 128), 128)] = value.astype(BF)

    each_pair_group(images, body)


def attention_back_columns(images, nk, q, k, v, p, do, dq, dkv):
    def body(image, slots, lanes):
        qs, ks = rows_of(image, NM), rows_of(image, nk)
        d_mixed = [split_pair(do[qs, at]) for at in lanes]
        d_probs = [nt(v[ks, at], one) for one, at in zip(d_mixed, lanes)]
        d_scores = [score_back(p[slot], one, 0) for slot, one in zip(slots, d_probs)]
        d_values = [nn(p[slot], one) for slot, one in zip(slots, d_mixed)]
        d_query = [tn(k[ks, at], one) for one, at in zip(d_scores, lanes)]
        d_keys = [nn(one, split_pair(q[qs, at])) for one, at in zip(d_scores, lanes)]
        for at, value, query, key in zip(lanes, d_values, d_query, d_keys):
            dq[qs, at] = (join_columns(query) * 0.125).astype(BF)
            dkv[ks, at] = key.astype(BF)
            dkv[ks, pl.ds(pl.multiple_of(D + at.start, 128), 128)] = value.astype(BF)

    each_pair_group(images, body)


HALF = 512


def mlp_forward(rows, h2, w1, w2, up_b, u, a, gp, tile, acc, out, base):
    acc[...] = base()
    steps = FF // HALF

    def multiply(t):
        u[t % 2] = nn(h2[...], w1[:, t * HALF : (t + 1) * HALF])

    def add(t):
        acc[...] += nn(tile[t % 2], w2[t * HALF : (t + 1) * HALF, :])

    multiply(0)
    for t in range(steps):
        if t + 1 < steps:
            multiply(t + 1)
        if t > 0:
            add(t - 1)
        for c in range(0, HALF, 256):
            at = slice(t * HALF + c, t * HALF + c + 256)
            shift = up_b[0:1, at].astype(F32)
            for r in range(0, rows, CHUNK):
                sel = slice(r, r + CHUNK)
                value, slope = gelu_pair(u[t % 2, sel, c : c + 256] + shift)
                low = value.astype(BF)
                tile[t % 2, sel, c : c + 256] = low
                if a is not None:
                    a[sel, at] = low
                if gp is not None:
                    gp[sel, at] = slope.astype(BF)
    add(steps - 1)
    out[...] = acc[...].astype(BF)


def mlp_back(rows, dyb, gp, w1, w2, du, u, acc, ready=lambda i, which: None):
    acc[...] = jnp.zeros_like(acc)

    def body(i):
        cols = [pl.ds(pl.multiple_of((2 * i + part) * HALF, HALF), HALF) for part in range(2)]
        ready(i, 0)
        for part in range(2):
            u[part] = nt(dyb[...], w2[cols[part], :])
        ready(i, 1)
        for part in range(2):
            for r in range(0, rows, CHUNK):
                sel = slice(r, r + CHUNK)
                du[sel, cols[part]] = (gp[sel, cols[part]].astype(F32) * u[part, sel, :]).astype(BF)
            acc[...] += nt(du[:, cols[part]], w1[:, cols[part]])

    loop(FF // (2 * HALF), body)


def project(count, rows, left, weight, first, write):
    def body(j):
        write(j, nn(left[...], weight[:, pl.ds(pl.multiple_of((first + j) * D, D), D)]))

    loop(count, body)


def set_biases(ref, bias):
    ref[0] = f32_row(bias, 0)
    ref[1] = jnp.zeros((1, D), F32)
    ref[2] = f32_row(bias, 0, D)


def cost(flops, nbytes):
    return pl.CostEstimate(flops=int(flops), bytes_accessed=int(nbytes), transcendentals=0)


def params(mib):
    return pltpu.CompilerParams(vmem_limit_bytes=mib * MIB)


def struct(shape, dtype=BF):
    return jax.ShapeDtypeStruct(shape, dtype)


def start_weights(copies, sources, scratch):
    return [copies.start(src, dst) for src, dst in zip(sources, scratch)]


def encode_kernel(group, groups, ids, visible, order_in, gains, biases, qvb, upb, rows, cot, wqkv, wo, w1, w2,
                  lat_out, x_out, hq_out, q_out, k_out, v_out, p_out, o_out, y1_out, h2_out, gp_out, a_out, *refs):
    ready, refs = refs[: 4 * groups], refs[4 * groups :]
    (order, rows_v, flat, sqkv, so, s1, s2, x, hq, qkv, p, o, y1, h2, gp, a, u, tile, acc, shifts, lat, sems) = refs
    n = GROUP * NV
    split_orders(order_in, order)

    @pl.when(ids[0] == 0)
    def _():
        copies = Copies(sems)
        got_rows = copies.start(rows.at[0], rows_v)
        got_qkv, got_o, got_1, got_2 = start_weights(
            copies, (wqkv.at[0], wo.at[0], w1.at[0], w2.at[0]), (sqkv, so, s1, s2)
        )
        gain, bias = gains.at[0], biases.at[0]
        set_biases(shifts, qvb)
        copies.wait(got_rows)
        flatten(rows_v, flat)

        def pick_rows(i):
            image = group * GROUP + i
            pick = pick_matrix(order, image, 0, NV, 0, visible[image])
            x[rows_of(i, NV), :] = nn(pick, flat[...]).astype(BF)

        loop(GROUP, pick_rows)
        copies.start(x, x_out)
        norm_rows(x, hq, n, f32_row(gain, 0), f32_row(bias, 0))
        copies.start(hq, hq_out)
        copies.wait(got_qkv)

        def keep(j, value):
            scale = jnp.where(j == 0, 0.125, 1.0)
            qkv[j] = ((value + shifts[j]).astype(BF).astype(F32) * scale).astype(BF)

        project(3, n, hq, sqkv, 0, keep)
        q, k, v = qkv.at[0], qkv.at[1], qkv.at[2]
        copies.start(q, q_out)
        copies.start(k, k_out)
        copies.start(v, v_out)
        attention_by_rows(GROUP, NV, q, k, v, p, o, lambda i: visible[group * GROUP + i])
        copies.start(p, p_out)
        copies.start(o, o_out)
        copies.wait(got_o)
        y1[...] = nn(o[...], so[...]) + f32_row(bias, 1) + x[...].astype(F32)
        copies.start(y1, y1_out)
        norm_rows(y1, h2, n, f32_row(gain, 1), f32_row(bias, 2))
        copies.start(h2, h2_out)
        copies.wait(got_1, got_2)
        mlp_forward(n, h2, s1, s2, upb, u, a, gp, tile, acc, lat, lambda: y1[...] + f32_row(bias, 3))
        copies.start(gp, gp_out)
        copies.start(a, a_out)
        copies.start(lat, lat_out)
        copies.finish()

    if group == groups - 1:

        @pl.when(ids[0] == 1)
        def _():
            copies = Copies(sems)
            m = GROUP * NM
            x_out, hq_out, q_out, dyb_out = (ready[i * groups : (i + 1) * groups] for i in range(4))
            gain, bias = gains.at[0], biases.at[0]
            got_rows = copies.start(rows.at[0], rows_v)
            got_q = copies.start(wqkv.at[0, :, pl.ds(0, D)], so)
            copies.wait(got_rows)
            flatten(rows_v, flat)
            got_cot = copies.start(cot.at[0], rows_v)
            top = pl.ds(0, m)

            def pick_group(g):
                def pick_rows(i):
                    image = g * GROUP + i
                    pick = pick_matrix(order, image, FIRST, NM, visible[image], PATCH)
                    x[rows_of(i, NM), :] = nn(pick, flat[...]).astype(BF)

                loop(GROUP, pick_rows)

            for g in range(groups):
                pick_group(g)
                norm_rows(x, hq, m, f32_row(gain, 0), f32_row(bias, 0))
                sent = [copies.start(x.at[top], x_out[g]), copies.start(hq.at[top], hq_out[g])]
                if g == 0:
                    copies.wait(got_q)
                q = qkv.at[g]
                q[top, :] = ((nn(hq[top, :], so[...]) + f32_row(qvb, 0)).astype(BF) * 0.125).astype(BF)
                copies.start(q.at[top], q_out[g])
                copies.wait(*sent)
            copies.wait(got_cot)
            flatten(rows_v, flat)
            for g in range(groups):
                pick_group(g)
                copies.wait(copies.start(x.at[top], dyb_out[g]))
            copies.finish()


def encode(group, groups, ids, visible, order, gains, biases, qvb, upb, rows, cot, weights):
    n = GROUP * NV
    images = order.shape[0]
    row, wide = struct((n, D)), struct((n, FF))
    heads = struct((GROUP * PAIRS, 2 * NV, NV))
    outs = [row] * 6 + [heads, row, struct((n, D), F32), row, wide, wide] + [struct((GROUP * NM, D))] * (4 * groups)
    vm = lambda s: pltpu.VMEM(s.shape, s.dtype)
    scratch = [
        pltpu.VMEM((images, 1, PATCH), jnp.int32),
        pltpu.VMEM((PATCH, images, D), BF), pltpu.VMEM((PATCH * images, D), BF),
        pltpu.VMEM((D, 3 * D), BF), pltpu.VMEM((D, D), BF), pltpu.VMEM((D, FF), BF), pltpu.VMEM((FF, D), BF),
        vm(row), vm(row), pltpu.VMEM((3, n, D), BF), vm(heads), vm(row), pltpu.VMEM((n, D), F32), vm(row),
        vm(wide), vm(wide), pltpu.VMEM((2, n, HALF), F32), pltpu.VMEM((2, n, HALF), BF), pltpu.VMEM((n, D), F32),
        pltpu.VMEM((3, 1, D), F32), vm(row),
        pltpu.SemaphoreType.DMA((24,)),
    ]
    got = pl.pallas_call(
        partial(encode_kernel, group, groups),
        in_specs=[SMEM, SMEM] + [VMEM] * 5 + [HBM] * 6,
        out_specs=[HBM] * len(outs),
        out_shape=outs,
        scratch_shapes=scratch,
        compiler_params=params(LIMIT),
        cost_estimate=cost(2 * n * 12 * D * D, 25e6),
        name="encode",
    )(ids, visible, order, gains, biases, qvb, upb, rows, cot, *weights)
    ready = got[12:]
    return got[:12], [ready[i * groups : (i + 1) * groups] for i in range(4)]


def block_end(copies, n, got_weights, so, s1, s2, bias, gain, up_b, x, o, y1, h2, a, gp, u, tile, acc, res):
    got_o, got_1, got_2 = got_weights
    copies.wait(got_o)
    y1[...] = nn(o[...], so[...]) + f32_row(bias, 1) + x[...].astype(F32)
    norm_rows(y1, h2, n, f32_row(gain, 1), f32_row(bias, 2))
    copies.wait(got_1, got_2)
    mlp_forward(n, h2, s1, s2, up_b, u, a, gp, tile, acc, res, lambda: y1[...] + f32_row(bias, 3))


def target_kernel(group, ids, visible, order_in, gain, bias, qvb, upb, rows, wqkv, wo, w1, w2, res_out,
                  order, rows_v, flat, sqkv, so, s1, s2, x, hq, qkv, o, y1, h2, u, tile, acc, shifts, res, sems):
    n = GROUP * NM
    q, k, v = qkv.at[0], qkv.at[1], qkv.at[2]

    @pl.when(ids[0] == 0)
    def _():
        copies = Copies(sems)
        split_orders(order_in, order)
        got_rows = copies.start(rows.at[0], rows_v)
        got_qkv = copies.start(wqkv, sqkv)
        got_weights = start_weights(copies, (wo, w1, w2), (so, s1, s2))
        set_biases(shifts, qvb)
        copies.wait(got_rows)
        flatten(rows_v, flat)

        def pick_rows(i):
            image = group * GROUP + i
            pick = pick_matrix(order, image, FIRST, NM, visible[image], PATCH)
            x[rows_of(i, NM), :] = nn(pick, flat[...]).astype(BF)

        loop(GROUP, pick_rows)
        norm_rows(x, hq, n, f32_row(gain, 0), f32_row(bias, 0))
        copies.wait(got_qkv)

        def keep(j, value):
            scale = jnp.where(j == 0, 0.125, 1.0)
            qkv[j] = ((value + shifts[j]).astype(BF).astype(F32) * scale).astype(BF)

        project(3, n, hq, sqkv, 0, keep)

        def key_ok(i):
            return lax.broadcasted_iota(jnp.int32, (NM, 1), 0) + FIRST >= visible[group * GROUP + i]

        attention_by_columns(GROUP, NM, q, k, v, None, o, key_ok)
        block_end(copies, n, got_weights, so, s1, s2, bias, gain, upb, x, o, y1, h2, None, None, u, tile, acc, res)
        copies.start(res, res_out)
        copies.finish()


def target(group, ids, visible, order, vecs, rows, weights):
    n = GROUP * NM
    images = order.shape[0]
    row, full = pltpu.VMEM((n, D), BF), pltpu.VMEM((n, D), F32)
    return pl.pallas_call(
        partial(target_kernel, group),
        in_specs=[SMEM, SMEM] + [VMEM] * 5 + [HBM] * 5,
        out_specs=HBM,
        out_shape=struct((n, D)),
        scratch_shapes=[
            pltpu.VMEM((images, 1, PATCH), jnp.int32),
            pltpu.VMEM((PATCH, images, D), BF), pltpu.VMEM((PATCH * images, D), BF),
            pltpu.VMEM((D, 3 * D), BF), pltpu.VMEM((D, D), BF), pltpu.VMEM((D, FF), BF), pltpu.VMEM((FF, D), BF),
            row, row, pltpu.VMEM((3, n, D), BF), row, full, row,
            pltpu.VMEM((2, n, HALF), F32), pltpu.VMEM((2, n, HALF), BF), full, pltpu.VMEM((3, 1, D), F32), row,
            pltpu.SemaphoreType.DMA((8,)),
        ],
        compiler_params=params(LIMIT),
        cost_estimate=cost(2e+10, 1e5),
        name="target",
    )(ids, visible, order, *vecs, rows, *weights)


def regress_kernel(group, ids, visible, gains, biases, qvb, upb, lat_in, x_in, q_in, dyb_in, wqkv, wo, w1, w2,
                   dlat_out, res_out, hk_out, dq_out, dkv_out, o_out, dy1b_out, h2_out, du_out, a_out, dy1_out,
                   sums_out,
                   sqkv, so, s1, s2, x, lat, hk, q, kv, p, o, y1, h2, gp, a, u, tile, acc, shifts,
                   res, dyb, du, dy1, dy1b, do, dq, dkv, dh, dlat, sums, sems):
    n, m = GROUP * NM, GROUP * NV
    k, v = kv.at[0], kv.at[1]

    @pl.when(ids[0] == 1)
    def _():
        copies = Copies(sems)
        gain, bias = gains.at[0], biases.at[0]
        got_lat = copies.start(lat_in, lat)
        got_kv = copies.start(wqkv.at[0, :, pl.ds(D, 2 * D)], sqkv)
        got_q = copies.start(q_in, q)
        got_x = copies.start(x_in, x)
        got_weights = start_weights(copies, (wo.at[0], w1.at[0], w2.at[0]), (so, s1, s2))
        got_dyb = copies.start(dyb_in, dyb)
        set_biases(shifts, qvb)
        copies.wait(got_lat)
        norm_rows(lat, hk, m, f32_row(gain, 0), f32_row(bias, 0))
        copies.start(hk, hk_out)
        copies.wait(got_kv)

        def keep_kv(j, value):
            kv[j] = (value + shifts[j + 1]).astype(BF)

        project(2, m, hk, sqkv, 0, keep_kv)
        copies.wait(got_q, got_x)

        def key_ok(i):
            return lax.broadcasted_iota(jnp.int32, (NV, 1), 0) < visible[group * GROUP + i]

        attention_by_columns(GROUP, NV, q, k, v, p, o, key_ok)
        copies.start(o, o_out)
        block_end(copies, n, got_weights, so, s1, s2, bias, gain, upb, x, o, y1, h2, a, gp, u, tile, acc, res)
        copies.start(res, res_out)
        copies.start(h2, h2_out)
        copies.start(a, a_out)
        copies.wait(got_dyb)
        mlp_back(n, dyb, gp, s1, s2, du, u, acc)
        copies.start(du, du_out)

        def keep(sel, dx):
            dy1[sel, :] = dx
            dy1b[sel, :] = dx.astype(BF)

        g2, b2 = norm_back(y1, acc, dyb, keep, n, f32_row(gain, 1))
        copies.start(dy1, dy1_out)
        copies.start(dy1b, dy1b_out)
        do[...] = nt(dy1b[...], so[...]).astype(BF)
        attention_back_columns(GROUP, NV, q, k, v, p, do, dq, dkv)
        copies.start(dq, dq_out)
        copies.start(dkv, dkv_out)
        dh[...] = nt(dkv[:, :D], sqkv[:, :D])
        dh[...] += nt(dkv[:, D:], sqkv[:, D:])

        def keep_side(sel, dx):
            dlat[sel, :] = dx.astype(BF)

        gk, bk = norm_back(lat, dh, None, keep_side, m, f32_row(gain, 0))
        copies.start(dlat, dlat_out)
        for row, value in enumerate((gk, g2, bk, b2)):
            sums[pl.ds(row, 1), :] = value
        copies.start(sums, sums_out)
        copies.finish()


def regress(group, ids, visible, vecs, lat, x, q, dyb, weights):
    n, m = GROUP * NM, GROUP * NV
    row, side, wide = struct((n, D)), struct((m, D)), struct((n, FF))
    pair = struct((m, 2 * D))
    outs = [side, row, side, row, pair, row, row, row, wide, wide, struct((n, D), F32), struct((8, D), F32)]
    vm = lambda s: pltpu.VMEM(s.shape, s.dtype)
    full, fside = pltpu.VMEM((n, D), F32), pltpu.VMEM((m, D), F32)
    scratch = [
        pltpu.VMEM((D, 2 * D), BF), pltpu.VMEM((D, D), BF), pltpu.VMEM((D, FF), BF), pltpu.VMEM((FF, D), BF),
        vm(row), vm(side), vm(side), vm(row), pltpu.VMEM((2, m, D), BF),
        pltpu.VMEM((GROUP * PAIRS, NV, 2 * NM), BF), vm(row), full, vm(row), vm(wide), vm(wide),
        pltpu.VMEM((2, n, HALF), F32), pltpu.VMEM((2, n, HALF), BF), full, pltpu.VMEM((3, 1, D), F32),
        vm(row), vm(row), vm(wide), full, vm(row), vm(row), vm(row), vm(pair), fside, vm(side),
        pltpu.VMEM((8, D), F32),
        pltpu.SemaphoreType.DMA((24,)),
    ]
    return pl.pallas_call(
        partial(regress_kernel, group),
        in_specs=[SMEM, SMEM] + [VMEM] * 4 + [HBM] * 8,
        out_specs=[HBM] * len(outs),
        out_shape=outs,
        scratch_shapes=scratch,
        compiler_params=params(LIMIT),
        cost_estimate=cost(4 * n * 12 * D * D, 25e6),
        name="regress",
    )(ids, visible, *vecs, lat, x, q, dyb, *weights)


def stack_rows(copies, pieces, ref, size):
    return [copies.start(piece, ref.at[pl.ds(i * size, size)]) for i, piece in enumerate(pieces)]


class BlockLoads:
    def __init__(self, copies, ids, groups, blocks, sources, dest):
        self.copies, self.ids, self.groups, self.sources, self.dest = copies, ids, groups, sources, dest
        self.first = copies.take(groups * blocks)

    def each(self, role, j, like, act):
        for g, (src, size) in enumerate(self.sources(role, like)):
            act(src, self.dest(j).at[pl.ds(g * size, size)], self.first + j * self.groups + g)

    def begin(self, role, j):
        self.each(role, j, j, self.copies.begin)

    def wait(self, j, like=0):
        for role in range(2):
            pl.when(self.ids[0] == role)(lambda role=role: self.each(role, j, like, self.copies.wait_at))


def clear_tail(ref, used):
    ref[pl.ds(used, ref.shape[0] - used), :] = jnp.zeros((ref.shape[0] - used, ref.shape[1]), ref.dtype)


def halves(count, blocks):
    rows = D // 16
    if count == 16:
        return [struct((2, 2, 2, blocks, rows, D))] + [struct((2, blocks, rows, D))] * 4
    return [struct((D, D))] * blocks


def give_blocks(copies, core, tree, left_right, out, dest):
    size = 8 if tree else 1
    blocks = out.shape[0]
    first = copies.take(blocks * size)

    def send(j, act):
        if not tree:
            for block in range(blocks):
                pl.when(j == block)(lambda block=block: act(out.at[block], dest[block], first + block))
            return
        view = out.at[j].reshape(2, 2, 2, 2, D // 16, D)
        for x in range(2):
            for low in range(2):
                at = first + j * size + 4 * x + 2 * low
                act(view.at[:, low, x, core], dest[0].at[x, low, :, j], at)
                act(view.at[:, low, x, 1 - core], dest[1 + 2 * x + low].at[:, j], at + 1)

    def body(j):
        out[j] = left_right(j)
        send(j, copies.begin)

    loop(blocks, body)
    loop(blocks, lambda j: send(j, copies.wait_at))


def give_rows(copies, core, tree, multiply, out, dest):
    size = 4 if tree else 1
    first = copies.take(4 * size)

    def send(j, act):
        if not tree:
            act(out.at[j], dest[0].at[pl.ds(pl.multiple_of(j * D, D), D)], first + j)
            return
        view = out.at[j].reshape(2, 2, D // 4, D)
        low, high = lax.rem(j, 2), lax.div(j, 2)
        for x in range(2):
            at = first + j * size + 2 * x
            act(view.at[x, core], dest[0].at[x, low, high, 0], at)
            act(view.at[x, 1 - core], dest[1].at[x, low, high, 0], at + 1)

    def body(j):
        out[j] = multiply(j)
        send(j, copies.begin)

    loop(4, body)
    loop(4, lambda j: send(j, copies.wait_at))


def down_kernel(groups, parts, ids, *refs):
    cot, lat, a_enc, a_reg, dyb_reg = (refs[i * groups : (i + 1) * groups] for i in range(5))
    refs = refs[5 * groups :]
    dest, refs = refs[:parts], refs[parts:]
    sums_out, cot_v, dyb, a, dlat, out, sums, sems = refs
    images = groups * GROUP
    nv, nm = GROUP * NV, GROUP * NM

    copies = Copies(sems)
    pieces = (a_enc, a_reg)

    def sources(role, j):
        return [(one.at[:, pl.ds(j * D, D)], (nv, nm)[role]) for one in pieces[role]]

    loads = BlockLoads(copies, ids, groups, 4, sources, lambda j: a.at[j])

    @pl.when(ids[0] == 0)
    def _():
        early = copies.part()
        got = stack_rows(early, cot, cot_v, nv) + stack_rows(early, lat, dlat, nv)
        for j in range(4):
            loads.begin(0, j)
        early.wait(*got)
        dyb[...] = (cot_v[...].astype(F32) + dlat[...].astype(F32)).astype(BF)

    @pl.when(ids[0] == 1)
    def _():
        early = copies.part()
        got = stack_rows(early, dyb_reg, dyb, nm)
        for j in range(4):
            loads.begin(1, j)
            clear_tail(a.at[j], images * NM)
        clear_tail(dyb, images * NM)
        early.wait(*got)

    copies.take(2 * groups)

    def multiply(j):
        loads.wait(j)
        return tn(a[j], dyb[...]).astype(BF)

    give_rows(copies, ids[1], parts == 2, multiply, out, dest)
    sums[...] = jnp.broadcast_to(column_sum(dyb, images * NV), (8, D))
    copies.start(sums, sums_out)
    copies.finish()


def down_grad(groups, count, ids, cot, dlat, a_enc, a_reg, dyb_reg):
    n = groups * GROUP * NV
    main = [struct((2, 2, 2, 1, D // 4, D))] * 2 if count == 16 else [struct((FF, D))]
    outs = main + [struct((8, D), F32)]
    row = pltpu.VMEM((n, D), BF)
    scratch = [
        row, row, pltpu.VMEM((4, n, D), BF), row, pltpu.VMEM((4, D, D), BF), pltpu.VMEM((8, D), F32),
        pltpu.SemaphoreType.DMA((36,)),
    ]
    got = pl.pallas_call(
        partial(down_kernel, groups, len(main)),
        in_specs=[SMEM] + [HBM] * (5 * groups),
        out_specs=[HBM] * len(outs),
        out_shape=outs,
        scratch_shapes=scratch,
        compiler_params=params(LIMIT),
        cost_estimate=cost(1e6, 1e5),
        name="down_grad",
    )(ids, *cot, *dlat, *a_enc, *a_reg, *dyb_reg)
    return got[: len(main)], got[-1]


def pick_kernel(groups, ids, visible, order_in, cot, *refs):
    picked = refs[:groups]
    order, rows_v, flat, cot_v, sems = refs[groups:]

    @pl.when(ids[0] == 0)
    def _():
        copies = Copies(sems)
        got = copies.start(cot.at[0], rows_v)
        split_orders(order_in, order)
        copies.wait(got)
        flatten(rows_v, flat)

        def pick_rows(image):
            pick = pick_matrix(order, image, 0, NV, 0, visible[image])
            cot_v[rows_of(image, NV), :] = nn(pick, flat[...]).astype(BF)

        loop(groups * GROUP, pick_rows)
        for g in range(groups):
            copies.start(cot_v.at[pl.ds(g * GROUP * NV, GROUP * NV)], picked[g])
        copies.finish()


def pick_cot(groups, ids, visible, order, cot):
    images = order.shape[0]
    outs = [struct((GROUP * NV, D))] * groups
    return list(pl.pallas_call(
        partial(pick_kernel, groups),
        in_specs=[SMEM, SMEM, VMEM, HBM],
        out_specs=[HBM] * groups,
        out_shape=outs,
        scratch_shapes=[
            pltpu.VMEM((images, 1, PATCH), jnp.int32),
            pltpu.VMEM((PATCH, images, D), BF), pltpu.VMEM((PATCH * images, D), BF),
            pltpu.VMEM((images * NV, D), BF), pltpu.SemaphoreType.DMA((8,)),
        ],
        compiler_params=params(LIMIT),
        cost_estimate=cost(1e6, 1e5),
        name="pick_cot",
    )(ids, visible, order, cot))


def mlp_kernel(ids, gains, cot, dlat_in, w1, w2, y1_in, gp_in, du_out, dy1_out, dy1b_out, sums_out,
               s1, s2, cot_v, dlat, dyb, gp, y1, du, u, acc, dy1, dy1b, sums, sems):
    n = GROUP * NV
    third = FF // 3

    @pl.when(ids[0] == 0)
    def _():
        copies = Copies(sems)
        got = [copies.start(dlat_in, dlat), copies.start(cot, cot_v)]
        start = copies.take(9)

        def parts(i):
            cols = pl.ds(pl.multiple_of(i * third, third), third)
            return (
                (w2.at[0, cols, :], s2.at[cols, :]),
                (gp_in.at[:, cols], gp.at[:, cols]),
                (w1.at[0, :, cols], s1.at[:, cols]),
            )

        for i in range(3):
            for k, (src, dst) in enumerate(parts(i)):
                copies.begin(src, dst, start + 3 * i + k)
        got_y = copies.start(y1_in, y1)

        def ready(i, which):
            for k in ((0, 1), (2,))[which]:
                copies.wait_at(*parts(i)[k], start + 3 * i + k)

        copies.wait(*got)
        dyb[...] = (cot_v[...].astype(F32) + dlat[...].astype(F32)).astype(BF)
        mlp_back(n, dyb, gp, s1, s2, du, u, acc, ready)
        copies.start(du, du_out)
        copies.wait(got_y)

        def keep(sel, dx):
            dy1[sel, :] = dx
            dy1b[sel, :] = dx.astype(BF)

        g2, b2 = norm_back(y1, acc, dyb, keep, n, f32_row(gains.at[0], 1))
        copies.start(dy1, dy1_out)
        copies.start(dy1b, dy1b_out)
        sums[pl.ds(0, 1), :] = g2
        sums[pl.ds(1, 1), :] = b2
        copies.start(sums, sums_out)
        copies.finish()


def mlp_grad(ids, gains, cot, dlat, w1, w2, y1, gp):
    n = GROUP * NV
    row, wide, full = pltpu.VMEM((n, D), BF), pltpu.VMEM((n, FF), BF), pltpu.VMEM((n, D), F32)
    outs = [struct((n, FF)), struct((n, D), F32), struct((n, D)), struct((8, D), F32)]
    return pl.pallas_call(
        mlp_kernel,
        in_specs=[SMEM, VMEM] + [HBM] * 6,
        out_specs=[HBM] * len(outs),
        out_shape=outs,
        scratch_shapes=[
            pltpu.VMEM((D, FF), BF), pltpu.VMEM((FF, D), BF), row, row, row, wide, full, wide,
            pltpu.VMEM((2, n, HALF), F32), full, full, row, pltpu.VMEM((8, D), F32), pltpu.SemaphoreType.DMA((24,)),
        ],
        compiler_params=params(LIMIT),
        cost_estimate=cost(1e6, 1e5),
        name="mlp_grad",
    )(ids, gains, cot, dlat, w1, w2, y1, gp)


def up_kernel(groups, parts, ids, *refs):
    pieces = [refs[i * groups : (i + 1) * groups] for i in range(8)]
    refs = refs[8 * groups :]
    dest, refs = refs[:parts], refs[parts:]
    sums_out, left, right, out, sums, sems = refs
    images = groups * GROUP

    nv, nm = GROUP * NV, GROUP * NM
    copies = Copies(sems)
    sides = (pieces[:4], pieces[4:])

    def sources(role, j):
        du, _, dy1b, _ = sides[role]
        ones = dy1b if j == 4 else [one.at[:, pl.ds(j * D, D)] for one in du]
        return [(one, (nv, nm)[role]) for one in ones]

    def lefts(role, i):
        _, h2, _, o = sides[role]
        return [(one, (nv, nm)[role]) for one in (h2, o)[i]]

    loads = BlockLoads(copies, ids, groups, 5, sources, lambda j: right.at[j])
    shared = BlockLoads(copies, ids, groups, 2, lefts, lambda i: left.at[i])
    for role in range(2):

        @pl.when(ids[0] == role)
        def _(role=role):
            shared.begin(role, 0)
            for j in range(5):
                loads.begin(role, j)
            shared.begin(role, 1)
            if role == 1:
                for ref in (left, right):
                    for i in range(ref.shape[0]):
                        clear_tail(ref.at[i], images * NM)

    shared.wait(0)

    def multiply(j):
        loads.wait(j)
        pl.when(j == 4)(lambda: shared.wait(1))
        value = tn(left[lax.div(j, 4)], right[j]).astype(BF)
        sums[pl.ds(j, 1), :] = column_sum(right.at[j], images * NV)
        return value

    give_blocks(copies, ids[1], dest[0].ndim == 6, multiply, out, dest)
    copies.start(sums, sums_out)
    copies.finish()


def up_grad(groups, count, ids, *pieces):
    n = groups * GROUP * NV
    main = halves(count, 5)
    outs = main + [struct((8, D), F32)]
    got = pl.pallas_call(
        partial(up_kernel, groups, len(main)),
        in_specs=[SMEM] + [HBM] * (8 * groups),
        out_specs=[HBM] * len(outs),
        out_shape=outs,
        scratch_shapes=[
            pltpu.VMEM((2, n, D), BF), pltpu.VMEM((5, n, D), BF), pltpu.VMEM((5, D, D), BF), pltpu.VMEM((8, D), F32),
            pltpu.SemaphoreType.DMA((60,)),
        ],
        compiler_params=params(LIMIT),
        cost_estimate=cost(1e6, 1e5),
        name="up_grad",
    )(ids, *[ref for piece in pieces for ref in piece])
    return got[: len(main)], got[-1]


def attn_kernel(groups, last, ids, gains, *refs):
    if last:
        down_sums, up_sums, refs = refs[0], refs[1], refs[2:]
        mlp_sums, reg_sums = (refs[i * groups : (i + 1) * groups] for i in range(2))
        before, refs = refs[2 * groups : 3 * groups - 1], refs[3 * groups - 1 :]
    (wqkv, wo, dy1_enc, q_in, k_in, v_in, p_in, x_enc, dq_reg, dkv_reg, dy1_reg, x_reg,
     dq_out, dkv_out, dx_out, sums_out,
     sqkv, so, dy1, dy1b, q, k, v, p, x, do, dq, dkv, dh, sems) = refs
    m = GROUP * NM
    top = pl.ds(0, m)
    gain = f32_row(gains.at[0], 0)

    def finish(copies, rows):
        def keep(sel, dx):
            dy1[sel, :] = dx

        own = (*norm_back(x, dh, dy1, keep, rows, gain), column_sum(dq, rows), column_sum(dkv, GROUP * NV, D))
        copies.start(dy1, dx_out)
        if not last:
            for row, value in enumerate(own):
                sums_out[row : row + 1, :] = value
            copies.finish()
            return

        def total_of(sums):
            total = sums[0][...]
            for more in sums[1:]:
                total = total + more[...]
            return total

        done, mlp, reg = total_of(before), total_of(mlp_sums), total_of(reg_sums)
        g1, b1, queries, values = (one + done[row : row + 1, :] for row, one in enumerate(own))
        encoder = ids[0] == 0
        sums_out[0:1, :] = g1 + jnp.where(encoder, 0.0, reg[0:1, :])
        sums_out[1:2, :] = jnp.where(encoder, mlp[0:1, :], reg[1:2, :])
        sums_out[2:3, :] = b1 + jnp.where(encoder, 0.0, reg[2:3, :])
        sums_out[3:4, :] = up_sums[4:5, :]
        sums_out[4:5, :] = jnp.where(encoder, mlp[1:2, :], reg[3:4, :])
        sums_out[5:6, :] = down_sums[0:1, :]
        sums_out[6:7, :] = queries
        sums_out[7:8, :] = values
        sums_out[8:12, :] = up_sums[0:4, :]
        sums_out[12:16, :] = jnp.zeros((4, D), F32)
        copies.finish()

    @pl.when(ids[0] == 0)
    def _():
        copies = Copies(sems)
        got = [copies.start(dy1_enc, dy1), copies.start(wo.at[0], so)]
        later = [copies.start(src, dst) for src, dst in ((v_in, v), (p_in, p), (k_in, k), (q_in, q))]
        final = [copies.start(wqkv.at[0], sqkv), copies.start(x_enc, x)]
        copies.wait(*got)
        dy1b[...] = dy1[...].astype(BF)
        do[...] = nt(dy1b[...], so[...]).astype(BF)
        copies.wait(*later)
        attention_back_rows(GROUP, NV, q, k, v, p, do, dq, dkv)
        copies.start(dq, dq_out)
        copies.start(dkv, dkv_out)
        copies.wait(*final)
        dh[...] = nt(dq[...], sqkv[:, 0:D])
        for j in range(2):
            dh[...] += nt(dkv[:, j * D : (j + 1) * D], sqkv[:, (j + 1) * D : (j + 2) * D])
        finish(copies, GROUP * NV)

    @pl.when(ids[0] == 1)
    def _():
        copies = Copies(sems)
        for src, dst in ((dq_reg, dq), (dy1_reg, dy1), (x_reg, x)):
            copies.start(src, dst.at[top])
        copies.start(dkv_reg, dkv)
        copies.start(wqkv.at[0, :, pl.ds(0, D)], sqkv.at[:, pl.ds(0, D)])
        copies.finish()
        dh[top, :] = nt(dq[top, :], sqkv[:, 0:D])
        finish(copies, m)


def attn_back(groups, last, ids, gains, sums, *pieces):
    n = GROUP * NV
    row, full = pltpu.VMEM((n, D), BF), pltpu.VMEM((n, D), F32)
    outs = [struct((n, D)), struct((n, 2 * D)), struct((n, D), F32), struct((16, D), F32)]
    return pl.pallas_call(
        partial(attn_kernel, groups, last),
        in_specs=[SMEM, VMEM] + [VMEM] * len(sums) + [HBM] * len(pieces),
        out_specs=[HBM] * 3 + [VMEM],
        out_shape=outs,
        scratch_shapes=[
            pltpu.VMEM((D, 3 * D), BF), pltpu.VMEM((D, D), BF), full, row, row, row, row,
            pltpu.VMEM((GROUP * PAIRS, 2 * NV, NV), BF), row, row, row, pltpu.VMEM((n, 2 * D), BF), full,
            pltpu.SemaphoreType.DMA((20,)),
        ],
        compiler_params=params(LIMIT),
        cost_estimate=cost(1e6, 1e5),
        name="attn_back",
    )(ids, gains, *sums, *pieces)


def qkv_kernel(groups, parts, ids, *refs):
    pieces = [refs[i * groups : (i + 1) * groups] for i in range(7)]
    dq_enc, dkv_enc, hq_enc, hq_reg, hk_reg, dq_reg, dkv_reg = pieces
    refs = refs[7 * groups :]
    dest, refs = refs[:parts], refs[parts:]
    left, right, out, sems = refs
    images = groups * GROUP
    nv, nm = GROUP * NV, GROUP * NM
    copies = Copies(sems)

    def sources(role, j):
        if j == 2:
            return [(one, (nv, nm)[role]) for one in (dq_enc, dq_reg)[role]]
        return [(one.at[:, pl.ds(j * D, D)], nv) for one in (dkv_enc, dkv_reg)[role]]

    def lefts(role, i):
        if role == 0:
            return [(one, nv) for one in hq_enc]
        return [(one, (nv, nm)[i]) for one in (hk_reg, hq_reg)[i]]

    loads = BlockLoads(copies, ids, groups, 3, sources, lambda j: right.at[j])
    shared = BlockLoads(copies, ids, groups, 2, lefts, lambda i: left.at[i])
    for role in range(2):

        @pl.when(ids[0] == role)
        def _(role=role):
            shared.begin(role, 0)
            for j in range(3):
                loads.begin(role, j)
            shared.begin(role, 1)
            if role == 1:
                clear_tail(left.at[1], images * NM)
                clear_tail(right.at[2], images * NM)

    shared.wait(0)

    def multiply(j):
        for block in range(3):

            @pl.when(j == block)
            def _(block=block):
                loads.wait(block, block)
                if block == 2:
                    shared.wait(1, 1)

        return tn(left[lax.div(j, 2)], right[j]).astype(BF)

    give_blocks(copies, ids[1], dest[0].ndim == 6, multiply, out, dest)


def qkv_grad(groups, count, ids, *pieces):
    n = groups * GROUP * NV
    row = pltpu.VMEM((n, D), BF)
    main = halves(count, 3)
    scratch = [
        pltpu.VMEM((2, n, D), BF), pltpu.VMEM((3, n, D), BF), pltpu.VMEM((3, D, D), BF),
        pltpu.SemaphoreType.DMA((40,)),
    ]
    return pl.pallas_call(
        partial(qkv_kernel, groups, len(main)),
        in_specs=[SMEM] + [HBM] * (7 * groups),
        out_specs=[HBM] * len(main),
        out_shape=main,
        scratch_shapes=scratch,
        compiler_params=params(LIMIT),
        cost_estimate=cost(1e6, 1e5),
        name="qkv_grad",
    )(ids, *[ref for piece in pieces for ref in piece])


def place_kernel(groups, ids, visible, order_in, *refs):
    dx_in, lat_enc, res_enc, res_reg = (refs[i * groups : (i + 1) * groups] for i in range(4))
    block_out, grad_out, order, dx, lat, out, grads, sems = refs[4 * groups :]
    images = groups * GROUP
    nv, nm = GROUP * NV, GROUP * NM
    split_orders(order_in, order)

    def put_grad(i, put, value):
        high = value.astype(BF)
        low = (value - high.astype(F32)).astype(BF)
        grads[i] = nn(put, high) + nn(put, low)

    def write_grads():
        copies = Copies(sems)
        for i in range(images):
            copies.start(grads.at[i], grad_out.at[0, :, i, :])
        copies.finish()

    @pl.when(ids[0] == 0)
    def _():
        copies = Copies(sems)
        for piece, ref, size in ((dx_in, dx, nv), (lat_enc, lat, nv), (res_enc, out, nm)):
            stack_rows(copies, piece, ref, size)
        copies.finish()

        def put_image(i):
            put = place_matrix(order, i, 0, NV, 0, visible[i])
            put_side = place_matrix(order, i, FIRST, NM, visible[i], PATCH)
            put_grad(i, put, dx[rows_of(i, NV), :])
            block_out[0, i] = (nn(put, lat[rows_of(i, NV), :]) + nn(put_side, out[rows_of(i, NM), :])).astype(BF)

        loop(images, put_image)
        write_grads()

    @pl.when(ids[0] == 1)
    def _():
        copies = Copies(sems)
        stack_rows(copies, res_reg, out, nm)
        stack_rows(copies, [piece.at[pl.ds(0, nm)] for piece in dx_in], dx, nm)
        copies.finish()

        def put_image(i):
            put = place_matrix(order, i, FIRST, NM, visible[i], PATCH)
            put_grad(i, put, dx[rows_of(i, NM), :])
            block_out[0, i] = nn(put, out[rows_of(i, NM), :]).astype(BF)

        loop(images, put_image)
        write_grads()


def place(groups, ids, visible, order, *pieces):
    images = groups * GROUP
    n = images * NV
    outs = [struct((1, images, PATCH, D)), struct((1, PATCH, images, D), F32)]
    return pl.pallas_call(
        partial(place_kernel, groups),
        in_specs=[SMEM, SMEM, VMEM] + [HBM] * (4 * groups),
        out_specs=[VMEM, HBM],
        out_shape=outs,
        scratch_shapes=[
            pltpu.VMEM((images, 1, PATCH), jnp.int32), pltpu.VMEM((n, D), F32), pltpu.VMEM((n, D), BF),
            pltpu.VMEM((images * NM, D), BF), pltpu.VMEM((images, PATCH, D), F32), pltpu.SemaphoreType.DMA((8,)),
        ],
        compiler_params=params(LIMIT),
        cost_estimate=cost(1e6, 1e5),
        name="place",
    )(ids, visible, order, *[ref for piece in pieces for ref in piece])


BITS = (2, 4, 8)


def hop(value, bit):
    return lax.ppermute(value, "dp", [(i, i ^ bit) for i in range(16)])


def combine_kernel(jobs, given, ids, *refs):
    used = sum(sum(4 if gone is None else 1 for gone in terms) for terms, *_ in jobs)
    inputs, outs, scratch = list(refs[:used]), list(refs[used : used + given]), list(refs[used + given :])
    copies = Copies(scratch.pop())
    plans = []

    def fetch(term, gone, bits, own):
        if gone is not None:
            path = tuple(bits[gone:])
            copy = copies.start(term.at[path] if path else term, own)
            return lambda: copies.wait(copy)
        wide = len(bits) == 1
        first = copies.take(2 if wide else 1)
        rest = tuple(bits[2:])

        def piece(x, low):
            ref = term[2 * x + low]
            return ref.at[rest] if rest else ref

        for x in range(2):
            for low in range(2):
                if wide:
                    pl.when(bits[0] == x)(
                        lambda x=x, low=low: copies.begin(piece(x, low), own.at[low], first + low)
                    )
                else:
                    pl.when((bits[0] == x) & (bits[1] == low))(
                        lambda x=x, low=low: copies.begin(piece(x, low), own, first)
                    )

        def wait():
            if wide:
                for low in range(2):
                    copies.wait_at(piece(0, low), own.at[low], first + low)
            else:
                copies.wait_at(piece(0, 0), own, first)

        return wait

    for kinds, first, last, targets, finals in jobs:
        terms = [inputs.pop(0) if gone is not None else [inputs.pop(0) for _ in range(4)] for gone in kinds]
        for target in targets:
            bits = []
            for bit in range(last):
                flip = bit >= first and (target >> (bit - first)) & 1
                bits.append(1 - ids[2 + bit] if flip else ids[2 + bit])
            owns = [scratch.pop(0) for _ in kinds]
            waits = [fetch(term, gone, bits, own) for term, gone, own in zip(terms, kinds, owns)]
            plans.append((waits, owns, last, finals, None if finals else outs.pop(0)))
    for waits, owns, last, finals, out in plans:
        for wait in waits:
            wait()
        spots = [()]
        for _ in range(3 - last):
            spots = [spot + (i,) for spot in spots for i in range(2)]
        for spot in spots:
            for j in range(owns[0].shape[-3]):
                value = owns[0][spot + (j,)].astype(F32)
                for more in owns[1:]:
                    value = value + more[spot + (j,)].astype(F32)
                if finals:
                    which, column = finals[j]
                    outs[which][:, column * D : (column + 1) * D] = value
                else:
                    out[spot + (j,)] = value.astype(BF)


def send_job(terms, first, last, targets=(1,)):
    return terms, first, last, targets, None


def final_job(terms, finals):
    return terms, 0, 3, (0,), finals


def combine(ids, *jobs, outs=()):
    shapes = [struct(shape, F32) for shape in outs]
    plans, inputs, scratch = [], [], []
    for terms, first, last, targets, finals in jobs:
        blocks, rows = terms[0].shape[-3:-1]
        kinds = tuple(None if isinstance(term, list) else 6 - term.ndim for term in terms)
        for term in terms:
            inputs += term if isinstance(term, list) else [term]
        plans.append((kinds, first, last, targets, finals))
        part = (2,) * (3 - last) + (blocks, rows, D)
        for _ in targets:
            scratch += [pltpu.VMEM(part, BF) for _ in terms]
            if finals is None:
                shapes.append(struct(part))
    scratch.append(pltpu.SemaphoreType.DMA((2 * len(scratch),)))
    return pl.pallas_call(
        partial(combine_kernel, tuple(plans), len(shapes)),
        in_specs=[SMEM] + [HBM] * len(inputs),
        out_specs=[VMEM] * len(shapes),
        out_shape=shapes,
        scratch_shapes=scratch,
        compiler_params=params(LIMIT),
        cost_estimate=cost(1e5, 1e4),
        name="combine",
    )(ids, *inputs)


def in_order(first, then):
    return lax.optimization_barrier((first, then))


def own_columns(rows, count):
    own = D // count
    me = lax.axis_index("dp")

    def part(block, wide):
        return lax.dynamic_slice_in_dim(block, me * wide, wide, block.ndim - 1)

    return (
        part(rows[:2], own),
        part(rows[2:6], own),
        part(rows[6:8].reshape(-1), 2 * own),
        part(rows[8:12].reshape(-1), 4 * own),
    )


def scatter_natural(block):
    shards = block.reshape(lax.axis_size("dp"), -1, D)
    return lax.psum_scatter(shards, "dp", scatter_dimension=0, tiled=True)[0].astype(F32)


def local(
    patch_rows, cotangent, patch_order, visible, qkv_weight, out_weight, up_weight, down_weight, norm_gains, biases,
    qv_bias, up_bias, target_qkv, target_out, target_up, target_down, target_gains, target_biases, target_qv_bias,
    target_up_bias,
):
    count = lax.axis_size("dp")
    tree = count == 16
    place_dp = lax.axis_index("dp")
    bits = [(place_dp // bit) % 2 for bit in (1,) + BITS]
    ids = jnp.stack([lax.axis_index("section")] + bits).astype(jnp.int32)
    groups = patch_order.shape[0] // GROUP
    weights = (qkv_weight, out_weight, up_weight, down_weight)
    targets = (target_qkv, target_out, target_up, target_down)
    vecs = (norm_gains, biases, qv_bias, up_bias)
    target_vecs = (target_gains, target_biases, target_qv_bias[None], target_up_bias[None])

    rows, cot = patch_rows.transpose(0, 2, 1, 3), cotangent.transpose(0, 2, 1, 3)
    calls = [
        encode(g, groups, ids, visible, patch_order, *vecs, rows, cot, weights) for g in range(groups)
    ]
    lat, x_e, hq_e, q_e, k_e, v_e, p_e, o_e, y1_e, h2_e, gp_e, a_e = zip(*[call[0] for call in calls])
    x_r, hq_r, q_r, dyb_r = calls[-1][1]
    sent = [lax.ppermute(piece, "section", [(0, 1)]) for piece in lat]
    vectors = (norm_gains, biases, qv_bias, up_bias)
    regressed = [regress(0, ids, visible, vectors, sent[0], x_r[0], q_r[0], dyb_r[0], weights)]
    back = [lax.ppermute(regressed[0][0], "section", [(1, 0)])]
    order_first, regressed[0] = in_order(patch_order, regressed[0])
    res_e = [target(0, ids, visible, order_first, target_vecs, rows, targets)]
    res_e[0], sent[1:] = in_order(res_e[0], sent[1:])
    for g in range(1, groups):
        regressed.append(regress(g, ids, visible, vectors, sent[g], x_r[g], q_r[g], dyb_r[g], weights))
        back.append(lax.ppermute(regressed[g][0], "section", [(1, 0)]))
    _, res_r, hk_r, dq_r, dkv_r, o_r, dy1b_r, h2_r, du_r, a_r, dy1_r, sums_r = zip(*regressed)

    order_next, res_r = in_order(patch_order, res_r)
    cot_e = pick_cot(groups, ids, visible, order_next, cot)
    cot_e, back[0] = in_order(cot_e, back[0])

    def mlp(g, cot):
        return mlp_grad(ids, norm_gains, cot, back[g], up_weight, down_weight, y1_e[g], gp_e[g])

    def attention(g, dy1, sums=()):
        return attn_back(
            groups, len(sums) > 0, ids, norm_gains, sums, qkv_weight, out_weight, dy1, q_e[g], k_e[g], v_e[g], p_e[g],
            x_e[g], dq_r[g], dkv_r[g], dy1_r[g], x_r[g],
        )

    mlps = [mlp(g, cot_e[g]) for g in range(groups - 1)]
    attns = [attention(g, mlps[g][1]) for g in range(groups - 1)]
    last = groups - 1
    send = partial(combine, ids)
    attns, back[last] = in_order(attns, back[last])
    down, sums_down = down_grad(groups, count, ids, cot_e, back, a_e, a_r, dyb_r)
    cot_last = cot_e[last]
    down, cot_last = in_order(down, cot_last)
    mlps.append(mlp(last, cot_last))
    du_e, dy1_e, dy1b_e, sums_e = (list(piece) for piece in zip(*mlps))
    if tree:
        downs = [down[0], hop(down[1], 1)]
        (down_x,), du_e[last] = in_order(send(send_job(downs, 0, 1)), du_e[last])
        downs = downs + [hop(down_x, 2)]
    up, sums_up = up_grad(groups, count, ids, du_e, h2_e, dy1b_e, o_e, du_r, h2_r, dy1b_r, o_r)
    if tree:
        peers = (3, 2, 1)
        ups = [up[0], [hop(piece, 1) for piece in up[1:]]]
        (up_x,), downs = in_order(send(send_job(ups, 0, 1)), downs)
        ups = ups + [hop(up_x, 2)]
        down_z, dy1_e[last] = in_order(send(send_job(downs, 1, 3, peers)), dy1_e[last])
        down_got = [hop(one, 4 * peer) for one, peer in zip(down_z, peers)]
    sums_in = [piece[3] for piece in attns]
    attns.append(attention(last, dy1_e[last], (sums_down, sums_up, *sums_e, *sums_r, *sums_in)))
    dq_e, dkv_e, dx, small = (list(piece) for piece in zip(*attns))
    small = small[last]
    order_late = patch_order
    if tree:
        small = small + hop(small, 1)
        small, dq_e[last] = in_order(small, dq_e[last])
    attn = qkv_grad(groups, count, ids, dq_e, dkv_e, hq_e, hq_r, hk_r, dq_r, dkv_r)
    if tree:
        (down_got, got), attn = in_order((down_got, hop(small, 2)), attn)
        small = small + got
        up_z, (attn, got) = in_order(send(send_job(ups, 1, 3, peers)), (attn, hop(small, 4)))
        small = small + got
        up_got = [hop(one, 4 * peer) for one, peer in zip(up_z, peers)]
        qkvs = [attn[0], [hop(piece, 1) for piece in attn[1:]]]
        (qkv_x,), got = in_order(send(send_job(qkvs, 0, 1)), hop(small, 8))
        small = small + got
        order_late, qkv_x = in_order(patch_order, qkv_x)
        qkvs = qkvs + [hop(qkv_x, 2)]
    res_e += [target(g, ids, visible, order_late, target_vecs, rows, targets) for g in range(1, groups)]
    if tree:
        qkv_z, res_e = in_order(send(send_job(qkvs, 1, 3, peers)), res_e)
        qkv_got = [hop(one, 4 * peer) for one, peer in zip(qkv_z, peers)]
    block_out, grad_rows = place(groups, ids, visible, patch_order, dx, lat, res_e, res_r)
    if tree:
        (block_out, grad_rows), up_got = in_order((block_out, grad_rows), up_got)
        down_sum, up_sum, out_sum = send(
            final_job(downs + down_got, ((0, 0),)),
            final_job(ups + up_got, tuple((1, j) for j in range(4)) + ((2, 0),)),
            outs=((D // 4, D), (D // 16, 4 * D), (D // 16, D)),
        )
        qkv_got, (down_sum, up_sum, out_sum) = in_order(qkv_got, (down_sum, up_sum, out_sum))
        (qkv_sum,) = send(final_job(qkvs + qkv_got, ((0, 1), (0, 2), (0, 0))), outs=((D // 16, 3 * D),))
    else:
        down_sum = scatter_natural(down[0])
        up_sum = jnp.concatenate([scatter_natural(one) for one in up[:4]], axis=1)
        out_sum = scatter_natural(up[4])
        qkv_sum = jnp.concatenate([scatter_natural(attn[i]) for i in (2, 0, 1)], axis=1)
        small = lax.psum(small, "dp")
    grad_rows = grad_rows.transpose(0, 2, 1, 3)
    gains, bias_rows, qv_rows, up_rows = own_columns(small, count)
    return (
        block_out,
        grad_rows,
        qkv_sum[None],
        out_sum[None],
        up_sum[None],
        down_sum[None],
        gains[None],
        bias_rows[None],
        qv_rows[None],
        up_rows[None],
    )


def solution(mesh):
    three, four = P("section", None, None), P("section", "dp", None, None)
    grad = P("section", "dp", None)
    return jax.shard_map(
        local,
        mesh=mesh,
        in_specs=(four, four, P("dp", None), P("dp"), three, three, three, three, three, three,
                  P("section", None), P("section", None), P(), P(), P(), P(), P(), P(), P(), P()),
        out_specs=(four, four, grad, grad, grad, grad, P("section", None, "dp"), P("section", None, "dp"),
                   P("section", "dp"), P("section", "dp")),
        check_vma=False,
    )
```

```python
from functools import partial

import jax
import jax.numpy as jnp
from jax import lax
from jax.experimental import pallas as pl
from jax.experimental.pallas import tpu as pltpu
from jax.sharding import PartitionSpec as P

HEADS = 12
PATCH = 196
D = 768
FF = 3072
EPS = 1e-06
NV = 144
NM = 128
FIRST = PATCH - NM
GROUP = 2
CHUNK = 32

BF = jnp.bfloat16
F32 = jnp.float32
MIB = 1024 * 1024
LIMIT = 62

HBM = pl.BlockSpec(memory_space=pl.ANY)
VMEM = pl.BlockSpec(memory_space=pltpu.VMEM)
SMEM = pl.BlockSpec(memory_space=pltpu.SMEM)


def nn(a, b):
    return jnp.dot(a, b, preferred_element_type=F32)


def nt(a, b):
    return lax.dot_general(a, b, (((1,), (1,)), ((), ())), preferred_element_type=F32)


def tn(a, b):
    return lax.dot_general(a, b, (((0,), (0,)), ((), ())), preferred_element_type=F32)


def loop(count, body, unroll=1):
    def step(i, carry):
        for u in range(unroll):
            body(i * unroll + u)
        return carry

    if count == unroll:
        step(0, 0)
    else:
        lax.fori_loop(0, count // unroll, step, 0)


def unroll_of(count):
    return next(u for u in (4, 3, 2, 1) if count % u == 0)


def rows_of(i, size):
    return pl.ds(pl.multiple_of(i * size, size), size)


def f32_row(ref, row, col=0, width=D):
    return ref[pl.ds(row, 1), pl.ds(col, width)].astype(F32)


class Copies:
    def __init__(self, sems):
        self.sems = sems
        self.used = 0
        self.open = []

    def start(self, src, dst):
        copy = pltpu.make_async_copy(src, dst, self.sems.at[self.used])
        self.used += 1
        copy.start()
        self.open.append(copy)
        return copy

    def wait(self, *copies):
        for copy in copies:
            copy.wait()
            self.open = [one for one in self.open if one is not copy]

    def finish(self):
        self.wait(*list(self.open))

    def take(self, count):
        self.used += count
        return self.used - count

    def part(self):
        other = Copies(self.sems)
        other.used = self.used
        return other

    def begin(self, src, dst, at):
        pltpu.make_async_copy(src, dst, self.sems.at[at]).start()

    def wait_at(self, src, dst, at):
        pltpu.make_async_copy(src, dst, self.sems.at[at]).wait()


def gelu_pair(u):
    size = jnp.abs(u)
    base = 1.0 + (0.3275911 * 0.7071067811865476) * size
    guess = pl.reciprocal(base, approx=True)
    t = guess * (2.0 - base * guess)
    ex = jnp.exp2((u * u) * (-0.5 * 1.4426950408889634))
    poly = 0.5306027145 * t - 0.7265760135
    poly = poly * t + 0.7107068705
    poly = poly * t - 0.142248368
    poly = poly * t + 0.127414796
    tail = poly * t * ex
    phi = jnp.where(u >= 0.0, 1.0 - tail, tail)
    return u * phi, phi + u * (0.3989422804014327 * ex)


def norm_rows(src, dst, rows, gain, shift):
    def body(i):
        sel = rows_of(i, CHUNK)
        x = src[sel, :].astype(F32)
        centered = x - jnp.mean(x, axis=-1, keepdims=True)
        var = jnp.mean(centered * centered, axis=-1, keepdims=True)
        dst[sel, :] = (centered * lax.rsqrt(var + EPS) * gain + shift).astype(BF)

    loop(rows // CHUNK, body, unroll_of(rows // CHUNK))


def norm_back(src, grad, base, write, rows, gain):
    count = rows // CHUNK
    unroll = 3 if count % 3 == 0 else 2

    def step(i, carry):
        for u in range(unroll):
            carry = one(i * unroll + u, carry)
        return carry

    def one(i, carry):
        d_gain, d_shift = carry
        sel = rows_of(i, CHUNK)
        x = src[sel, :].astype(F32)
        dh = grad[sel, :]
        centered = x - jnp.mean(x, axis=-1, keepdims=True)
        var = jnp.mean(centered * centered, axis=-1, keepdims=True)
        rstd = lax.rsqrt(var + EPS)
        hat = centered * rstd
        g = dh * gain
        part = dh * hat
        dx = rstd * (
            g
            - jnp.mean(g, axis=-1, keepdims=True)
            - hat * jnp.mean(g * hat, axis=-1, keepdims=True)
        )
        if base is not None:
            dx = dx + base[sel, :].astype(F32)
        write(sel, dx)
        d_gain = d_gain + jnp.sum(part.reshape(CHUNK // 8, 8, D), axis=0)
        d_shift = d_shift + jnp.sum(dh.reshape(CHUNK // 8, 8, D), axis=0)
        return d_gain, d_shift

    zero = jnp.zeros((8, D), F32)
    d_gain, d_shift = lax.fori_loop(0, count // unroll, step, (zero, zero))
    return jnp.sum(d_gain, axis=0, keepdims=True), jnp.sum(d_shift, axis=0, keepdims=True)


def column_sum(ref, rows, col=0, width=D):
    def step(i, carry):
        x = ref[rows_of(i, CHUNK), pl.ds(col, width)].astype(F32)
        return carry + jnp.sum(x.reshape(CHUNK // 8, 8, width), axis=0)

    total = lax.fori_loop(0, rows // CHUNK, step, jnp.zeros((8, width), F32))
    return jnp.sum(total, axis=0, keepdims=True)


def as_bf16(flags):
    return jnp.where(flags, 1.0, 0.0).astype(BF)


def pick_matrix(order, image, start, count, low, high):
    row = order[image, :, pl.ds(start, count)].astype(F32)
    images = order.shape[0]
    col = jnp.broadcast_to(row, (8, count)).T[:, 0:1].astype(jnp.int32)
    rank = start + lax.broadcasted_iota(jnp.int32, (count, 1), 0)
    col = jnp.where((rank >= low) & (rank < high), col * images + image, -1)
    return as_bf16(col == lax.broadcasted_iota(jnp.int32, (count, PATCH * images), 1))


def place_matrix(order, image, start, count, low, high):
    row = order[image, :, pl.ds(start, count)]
    rank = start + lax.broadcasted_iota(jnp.int32, (1, count), 1)
    row = jnp.where((rank >= low) & (rank < high), row, -1)
    return as_bf16(row == lax.broadcasted_iota(jnp.int32, (PATCH, count), 0))


def flatten(rows, flat):
    flat[...] = rows[...].reshape(flat.shape)


def split_orders(order, split):
    for image in range(split.shape[0]):
        split[image] = order[image : image + 1, :]


def split_pair(pair):
    lane = lax.broadcasted_iota(jnp.int32, pair.shape, 1)
    zero = jnp.zeros_like(pair)
    return jnp.concatenate([jnp.where(lane < 64, pair, zero), jnp.where(lane < 64, zero, pair)], axis=0)


def join_rows(both):
    rows = both.shape[0] // 2
    lane = lax.broadcasted_iota(jnp.int32, (rows, 128), 1)
    return jnp.where(lane < 64, both[:rows], both[rows:])


def join_columns(both):
    rows = both.shape[1] // 2
    return jnp.concatenate([both[:64, :rows], both[64:, rows:]], axis=0).T


PAIRS = HEADS // 2
STEP = 6


def each_pair_group(images, body):
    def group(i):
        image = i // (PAIRS // STEP)
        first = (i % (PAIRS // STEP)) * STEP
        pairs = [first + step for step in range(STEP)]
        body(image, [image * PAIRS + pair for pair in pairs], [pl.ds(pl.multiple_of(pair * 128, 128), 128) for pair in pairs])

    loop(images * (PAIRS // STEP), group)


def softmax(scores, axis):
    ex = jnp.exp(scores - jnp.max(scores, axis=axis, keepdims=True))
    return (ex * (1.0 / jnp.sum(ex, axis=axis, keepdims=True))).astype(BF)


def score_back(probs, d_probs, axis):
    wide = probs.astype(F32)
    return (wide * (d_probs - jnp.sum(d_probs * wide, axis=axis, keepdims=True))).astype(BF)


def attention_by_rows(images, n, q, k, v, p, o, count_of):
    def body(image, slots, lanes):
        sel = rows_of(image, n)
        ok = lax.broadcasted_iota(jnp.int32, (1, n), 1) < count_of(image)
        scores = [nt(split_pair(q[sel, at]), k[sel, at]) for at in lanes]
        probs = [softmax(jnp.where(ok, one, -1000000000.0), 1) for one in scores]
        for slot, one in zip(slots, probs):
            p[slot] = one
        mixed = [nn(one, v[sel, at]) for one, at in zip(probs, lanes)]
        for at, one in zip(lanes, mixed):
            o[sel, at] = join_rows(one).astype(BF)

    each_pair_group(images, body)


def attention_by_columns(images, nk, q, k, v, p, o, key_ok):
    def body(image, slots, lanes):
        qs, ks = rows_of(image, NM), rows_of(image, nk)
        ok = key_ok(image)
        scores = [nt(k[ks, at], split_pair(q[qs, at])) for at in lanes]
        probs = [softmax(jnp.where(ok, one, -1000000000.0), 0) for one in scores]
        if p is not None:
            for slot, one in zip(slots, probs):
                p[slot] = one
        mixed = [tn(v[ks, at], one) for one, at in zip(probs, lanes)]
        for at, one in zip(lanes, mixed):
            o[qs, at] = join_columns(one).astype(BF)

    each_pair_group(images, body)


def attention_back_rows(images, n, q, k, v, p, do, dq, dkv):
    def body(image, slots, lanes):
        sel = rows_of(image, n)
        d_mixed = [split_pair(do[sel, at]) for at in lanes]
        d_probs = [nt(one, v[sel, at]) for one, at in zip(d_mixed, lanes)]
        d_scores = [score_back(p[slot], one, 1) for slot, one in zip(slots, d_probs)]
        d_values = [tn(p[slot], one) for slot, one in zip(slots, d_mixed)]
        d_query = [nn(one, k[sel, at]) for one, at in zip(d_scores, lanes)]
        d_keys = [tn(one, split_pair(q[sel, at])) for one, at in zip(d_scores, lanes)]
        for at, value, query, key in zip(lanes, d_values, d_query, d_keys):
            dq[sel, at] = (join_rows(query) * 0.125).astype(BF)
            dkv[sel, at] = key.astype(BF)
            dkv[sel, pl.ds(pl.multiple_of(D + at.start, 128), 128)] = value.astype(BF)

    each_pair_group(images, body)


def attention_back_columns(images, nk, q, k, v, p, do, dq, dkv):
    def body(image, slots, lanes):
        qs, ks = rows_of(image, NM), rows_of(image, nk)
        d_mixed = [split_pair(do[qs, at]) for at in lanes]
        d_probs = [nt(v[ks, at], one) for one, at in zip(d_mixed, lanes)]
        d_scores = [score_back(p[slot], one, 0) for slot, one in zip(slots, d_probs)]
        d_values = [nn(p[slot], one) for slot, one in zip(slots, d_mixed)]
        d_query = [tn(k[ks, at], one) for one, at in zip(d_scores, lanes)]
        d_keys = [nn(one, split_pair(q[qs, at])) for one, at in zip(d_scores, lanes)]
        for at, value, query, key in zip(lanes, d_values, d_query, d_keys):
            dq[qs, at] = (join_columns(query) * 0.125).astype(BF)
            dkv[ks, at] = key.astype(BF)
            dkv[ks, pl.ds(pl.multiple_of(D + at.start, 128), 128)] = value.astype(BF)

    each_pair_group(images, body)


HALF = 512


def mlp_forward(rows, h2, w1, w2, up_b, u, a, gp, tile, acc, out, base):
    acc[...] = base()
    steps = FF // HALF

    def multiply(t):
        u[t % 2] = nn(h2[...], w1[:, t * HALF : (t + 1) * HALF])

    def add(t):
        acc[...] += nn(tile[t % 2], w2[t * HALF : (t + 1) * HALF, :])

    multiply(0)
    for t in range(steps):
        if t + 1 < steps:
            multiply(t + 1)
        if t > 0:
            add(t - 1)
        for c in range(0, HALF, 256):
            at = slice(t * HALF + c, t * HALF + c + 256)
            shift = up_b[0:1, at].astype(F32)
            for r in range(0, rows, CHUNK):
                sel = slice(r, r + CHUNK)
                value, slope = gelu_pair(u[t % 2, sel, c : c + 256] + shift)
                low = value.astype(BF)
                tile[t % 2, sel, c : c + 256] = low
                if a is not None:
                    a[sel, at] = low
                if gp is not None:
                    gp[sel, at] = slope.astype(BF)
    add(steps - 1)
    out[...] = acc[...].astype(BF)


def mlp_back(rows, dyb, gp, w1, w2, du, u, acc, ready=lambda i, which: None):
    acc[...] = jnp.zeros_like(acc)

    def body(i):
        cols = [pl.ds(pl.multiple_of((2 * i + part) * HALF, HALF), HALF) for part in range(2)]
        ready(i, 0)
        for part in range(2):
            u[part] = nt(dyb[...], w2[cols[part], :])
        ready(i, 1)
        for part in range(2):
            for r in range(0, rows, CHUNK):
                sel = slice(r, r + CHUNK)
                du[sel, cols[part]] = (gp[sel, cols[part]].astype(F32) * u[part, sel, :]).astype(BF)
            acc[...] += nt(du[:, cols[part]], w1[:, cols[part]])

    loop(FF // (2 * HALF), body)


def project(count, rows, left, weight, first, write):
    def body(j):
        write(j, nn(left[...], weight[:, pl.ds(pl.multiple_of((first + j) * D, D), D)]))

    loop(count, body)


def set_biases(ref, bias):
    ref[0] = f32_row(bias, 0)
    ref[1] = jnp.zeros((1, D), F32)
    ref[2] = f32_row(bias, 0, D)


def cost(flops, nbytes):
    return pl.CostEstimate(flops=int(flops), bytes_accessed=int(nbytes), transcendentals=0)


def params(mib):
    return pltpu.CompilerParams(vmem_limit_bytes=mib * MIB)


def struct(shape, dtype=BF):
    return jax.ShapeDtypeStruct(shape, dtype)


def start_weights(copies, sources, scratch):
    return [copies.start(src, dst) for src, dst in zip(sources, scratch)]


def encode_kernel(group, groups, ids, visible, order_in, gains, biases, qvb, upb, rows, cot, wqkv, wo, w1, w2,
                  lat_out, x_out, hq_out, q_out, k_out, v_out, p_out, o_out, y1_out, h2_out, gp_out, a_out, *refs):
    ready, refs = refs[: 4 * groups], refs[4 * groups :]
    (order, rows_v, flat, sqkv, so, s1, s2, x, hq, qkv, p, o, y1, h2, gp, a, u, tile, acc, shifts, lat, sems) = refs
    n = GROUP * NV
    split_orders(order_in, order)

    @pl.when(ids[0] == 0)
    def _():
        copies = Copies(sems)
        got_rows = copies.start(rows.at[0], rows_v)
        got_qkv, got_o, got_1, got_2 = start_weights(
            copies, (wqkv.at[0], wo.at[0], w1.at[0], w2.at[0]), (sqkv, so, s1, s2)
        )
        gain, bias = gains.at[0], biases.at[0]
        set_biases(shifts, qvb)
        copies.wait(got_rows)
        flatten(rows_v, flat)

        def pick_rows(i):
            image = group * GROUP + i
            pick = pick_matrix(order, image, 0, NV, 0, visible[image])
            x[rows_of(i, NV), :] = nn(pick, flat[...]).astype(BF)

        loop(GROUP, pick_rows)
        copies.start(x, x_out)
        norm_rows(x, hq, n, f32_row(gain, 0), f32_row(bias, 0))
        copies.start(hq, hq_out)
        copies.wait(got_qkv)

        def keep(j, value):
            scale = jnp.where(j == 0, 0.125, 1.0)
            qkv[j] = ((value + shifts[j]).astype(BF).astype(F32) * scale).astype(BF)

        project(3, n, hq, sqkv, 0, keep)
        q, k, v = qkv.at[0], qkv.at[1], qkv.at[2]
        copies.start(q, q_out)
        copies.start(k, k_out)
        copies.start(v, v_out)
        attention_by_rows(GROUP, NV, q, k, v, p, o, lambda i: visible[group * GROUP + i])
        copies.start(p, p_out)
        copies.start(o, o_out)
        copies.wait(got_o)
        y1[...] = nn(o[...], so[...]) + f32_row(bias, 1) + x[...].astype(F32)
        copies.start(y1, y1_out)
        norm_rows(y1, h2, n, f32_row(gain, 1), f32_row(bias, 2))
        copies.start(h2, h2_out)
        copies.wait(got_1, got_2)
        mlp_forward(n, h2, s1, s2, upb, u, a, gp, tile, acc, lat, lambda: y1[...] + f32_row(bias, 3))
        copies.start(gp, gp_out)
        copies.start(a, a_out)
        copies.start(lat, lat_out)
        copies.finish()

    if group == groups - 1:

        @pl.when(ids[0] == 1)
        def _():
            copies = Copies(sems)
            m = GROUP * NM
            x_out, hq_out, q_out, dyb_out = (ready[i * groups : (i + 1) * groups] for i in range(4))
            gain, bias = gains.at[0], biases.at[0]
            got_rows = copies.start(rows.at[0], rows_v)
            got_q = copies.start(wqkv.at[0, :, pl.ds(0, D)], so)
            copies.wait(got_rows)
            flatten(rows_v, flat)
            got_cot = copies.start(cot.at[0], rows_v)
            top = pl.ds(0, m)

            def pick_group(g):
                def pick_rows(i):
                    image = g * GROUP + i
                    pick = pick_matrix(order, image, FIRST, NM, visible[image], PATCH)
                    x[rows_of(i, NM), :] = nn(pick, flat[...]).astype(BF)

                loop(GROUP, pick_rows)

            for g in range(groups):
                pick_group(g)
                norm_rows(x, hq, m, f32_row(gain, 0), f32_row(bias, 0))
                sent = [copies.start(x.at[top], x_out[g]), copies.start(hq.at[top], hq_out[g])]
                if g == 0:
                    copies.wait(got_q)
                q = qkv.at[g]
                q[top, :] = ((nn(hq[top, :], so[...]) + f32_row(qvb, 0)).astype(BF) * 0.125).astype(BF)
                copies.start(q.at[top], q_out[g])
                copies.wait(*sent)
            copies.wait(got_cot)
            flatten(rows_v, flat)
            for g in range(groups):
                pick_group(g)
                copies.wait(copies.start(x.at[top], dyb_out[g]))
            copies.finish()


def encode(group, groups, ids, visible, order, gains, biases, qvb, upb, rows, cot, weights):
    n = GROUP * NV
    images = order.shape[0]
    row, wide = struct((n, D)), struct((n, FF))
    heads = struct((GROUP * PAIRS, 2 * NV, NV))
    outs = [row] * 6 + [heads, row, struct((n, D), F32), row, wide, wide] + [struct((GROUP * NM, D))] * (4 * groups)
    vm = lambda s: pltpu.VMEM(s.shape, s.dtype)
    scratch = [
        pltpu.VMEM((images, 1, PATCH), jnp.int32),
        pltpu.VMEM((PATCH, images, D), BF), pltpu.VMEM((PATCH * images, D), BF),
        pltpu.VMEM((D, 3 * D), BF), pltpu.VMEM((D, D), BF), pltpu.VMEM((D, FF), BF), pltpu.VMEM((FF, D), BF),
        vm(row), vm(row), pltpu.VMEM((3, n, D), BF), vm(heads), vm(row), pltpu.VMEM((n, D), F32), vm(row),
        vm(wide), vm(wide), pltpu.VMEM((2, n, HALF), F32), pltpu.VMEM((2, n, HALF), BF), pltpu.VMEM((n, D), F32),
        pltpu.VMEM((3, 1, D), F32), vm(row),
        pltpu.SemaphoreType.DMA((24,)),
    ]
    got = pl.pallas_call(
        partial(encode_kernel, group, groups),
        in_specs=[SMEM, SMEM] + [VMEM] * 5 + [HBM] * 6,
        out_specs=[HBM] * len(outs),
        out_shape=outs,
        scratch_shapes=scratch,
        compiler_params=params(LIMIT),
        cost_estimate=cost(2 * n * 12 * D * D, 25e6),
        name="encode",
    )(ids, visible, order, gains, biases, qvb, upb, rows, cot, *weights)
    ready = got[12:]
    return got[:12], [ready[i * groups : (i + 1) * groups] for i in range(4)]


def block_end(copies, n, got_weights, so, s1, s2, bias, gain, up_b, x, o, y1, h2, a, gp, u, tile, acc, res):
    got_o, got_1, got_2 = got_weights
    copies.wait(got_o)
    y1[...] = nn(o[...], so[...]) + f32_row(bias, 1) + x[...].astype(F32)
    norm_rows(y1, h2, n, f32_row(gain, 1), f32_row(bias, 2))
    copies.wait(got_1, got_2)
    mlp_forward(n, h2, s1, s2, up_b, u, a, gp, tile, acc, res, lambda: y1[...] + f32_row(bias, 3))


def target_kernel(group, ids, visible, order_in, gain, bias, qvb, upb, rows, wqkv, wo, w1, w2, res_out,
                  order, rows_v, flat, sqkv, so, s1, s2, x, hq, qkv, o, y1, h2, u, tile, acc, shifts, res, sems):
    n = GROUP * NM
    q, k, v = qkv.at[0], qkv.at[1], qkv.at[2]

    @pl.when(ids[0] == 0)
    def _():
        copies = Copies(sems)
        split_orders(order_in, order)
        got_rows = copies.start(rows.at[0], rows_v)
        got_qkv = copies.start(wqkv, sqkv)
        got_weights = start_weights(copies, (wo, w1, w2), (so, s1, s2))
        set_biases(shifts, qvb)
        copies.wait(got_rows)
        flatten(rows_v, flat)

        def pick_rows(i):
            image = group * GROUP + i
            pick = pick_matrix(order, image, FIRST, NM, visible[image], PATCH)
            x[rows_of(i, NM), :] = nn(pick, flat[...]).astype(BF)

        loop(GROUP, pick_rows)
        norm_rows(x, hq, n, f32_row(gain, 0), f32_row(bias, 0))
        copies.wait(got_qkv)

        def keep(j, value):
            scale = jnp.where(j == 0, 0.125, 1.0)
            qkv[j] = ((value + shifts[j]).astype(BF).astype(F32) * scale).astype(BF)

        project(3, n, hq, sqkv, 0, keep)

        def key_ok(i):
            return lax.broadcasted_iota(jnp.int32, (NM, 1), 0) + FIRST >= visible[group * GROUP + i]

        attention_by_columns(GROUP, NM, q, k, v, None, o, key_ok)
        block_end(copies, n, got_weights, so, s1, s2, bias, gain, upb, x, o, y1, h2, None, None, u, tile, acc, res)
        copies.start(res, res_out)
        copies.finish()


def target(group, ids, visible, order, vecs, rows, weights):
    n = GROUP * NM
    images = order.shape[0]
    row, full = pltpu.VMEM((n, D), BF), pltpu.VMEM((n, D), F32)
    return pl.pallas_call(
        partial(target_kernel, group),
        in_specs=[SMEM, SMEM] + [VMEM] * 5 + [HBM] * 5,
        out_specs=HBM,
        out_shape=struct((n, D)),
        scratch_shapes=[
            pltpu.VMEM((images, 1, PATCH), jnp.int32),
            pltpu.VMEM((PATCH, images, D), BF), pltpu.VMEM((PATCH * images, D), BF),
            pltpu.VMEM((D, 3 * D), BF), pltpu.VMEM((D, D), BF), pltpu.VMEM((D, FF), BF), pltpu.VMEM((FF, D), BF),
            row, row, pltpu.VMEM((3, n, D), BF), row, full, row,
            pltpu.VMEM((2, n, HALF), F32), pltpu.VMEM((2, n, HALF), BF), full, pltpu.VMEM((3, 1, D), F32), row,
            pltpu.SemaphoreType.DMA((8,)),
        ],
        compiler_params=params(LIMIT),
        cost_estimate=cost(2e+10, 1e5),
        name="target",
    )(ids, visible, order, *vecs, rows, *weights)


def regress_kernel(group, ids, visible, gains, biases, qvb, upb, lat_in, x_in, q_in, dyb_in, wqkv, wo, w1, w2,
                   dlat_out, res_out, hk_out, dq_out, dkv_out, o_out, dy1b_out, h2_out, du_out, a_out, dy1_out,
                   sums_out,
                   sqkv, so, s1, s2, x, lat, hk, q, kv, p, o, y1, h2, gp, a, u, tile, acc, shifts,
                   res, dyb, du, dy1, dy1b, do, dq, dkv, dh, dlat, sums, sems):
    n, m = GROUP * NM, GROUP * NV
    k, v = kv.at[0], kv.at[1]

    @pl.when(ids[0] == 1)
    def _():
        copies = Copies(sems)
        gain, bias = gains.at[0], biases.at[0]
        got_lat = copies.start(lat_in, lat)
        got_kv = copies.start(wqkv.at[0, :, pl.ds(D, 2 * D)], sqkv)
        got_q = copies.start(q_in, q)
        got_x = copies.start(x_in, x)
        got_weights = start_weights(copies, (wo.at[0], w1.at[0], w2.at[0]), (so, s1, s2))
        got_dyb = copies.start(dyb_in, dyb)
        set_biases(shifts, qvb)
        copies.wait(got_lat)
        norm_rows(lat, hk, m, f32_row(gain, 0), f32_row(bias, 0))
        copies.start(hk, hk_out)
        copies.wait(got_kv)

        def keep_kv(j, value):
            kv[j] = (value + shifts[j + 1]).astype(BF)

        project(2, m, hk, sqkv, 0, keep_kv)
        copies.wait(got_q, got_x)

        def key_ok(i):
            return lax.broadcasted_iota(jnp.int32, (NV, 1), 0) < visible[group * GROUP + i]

        attention_by_columns(GROUP, NV, q, k, v, p, o, key_ok)
        copies.start(o, o_out)
        block_end(copies, n, got_weights, so, s1, s2, bias, gain, upb, x, o, y1, h2, a, gp, u, tile, acc, res)
        copies.start(res, res_out)
        copies.start(h2, h2_out)
        copies.start(a, a_out)
        copies.wait(got_dyb)
        mlp_back(n, dyb, gp, s1, s2, du, u, acc)
        copies.start(du, du_out)

        def keep(sel, dx):
            dy1[sel, :] = dx
            dy1b[sel, :] = dx.astype(BF)

        g2, b2 = norm_back(y1, acc, dyb, keep, n, f32_row(gain, 1))
        copies.start(dy1, dy1_out)
        copies.start(dy1b, dy1b_out)
        do[...] = nt(dy1b[...], so[...]).astype(BF)
        attention_back_columns(GROUP, NV, q, k, v, p, do, dq, dkv)
        copies.start(dq, dq_out)
        copies.start(dkv, dkv_out)
        dh[...] = nt(dkv[:, :D], sqkv[:, :D])
        dh[...] += nt(dkv[:, D:], sqkv[:, D:])

        def keep_side(sel, dx):
            dlat[sel, :] = dx.astype(BF)

        gk, bk = norm_back(lat, dh, None, keep_side, m, f32_row(gain, 0))
        copies.start(dlat, dlat_out)
        for row, value in enumerate((gk, g2, bk, b2)):
            sums[pl.ds(row, 1), :] = value
        copies.start(sums, sums_out)
        copies.finish()


def regress(group, ids, visible, vecs, lat, x, q, dyb, weights):
    n, m = GROUP * NM, GROUP * NV
    row, side, wide = struct((n, D)), struct((m, D)), struct((n, FF))
    pair = struct((m, 2 * D))
    outs = [side, row, side, row, pair, row, row, row, wide, wide, struct((n, D), F32), struct((8, D), F32)]
    vm = lambda s: pltpu.VMEM(s.shape, s.dtype)
    full, fside = pltpu.VMEM((n, D), F32), pltpu.VMEM((m, D), F32)
    scratch = [
        pltpu.VMEM((D, 2 * D), BF), pltpu.VMEM((D, D), BF), pltpu.VMEM((D, FF), BF), pltpu.VMEM((FF, D), BF),
        vm(row), vm(side), vm(side), vm(row), pltpu.VMEM((2, m, D), BF),
        pltpu.VMEM((GROUP * PAIRS, NV, 2 * NM), BF), vm(row), full, vm(row), vm(wide), vm(wide),
        pltpu.VMEM((2, n, HALF), F32), pltpu.VMEM((2, n, HALF), BF), full, pltpu.VMEM((3, 1, D), F32),
        vm(row), vm(row), vm(wide), full, vm(row), vm(row), vm(row), vm(pair), fside, vm(side),
        pltpu.VMEM((8, D), F32),
        pltpu.SemaphoreType.DMA((24,)),
    ]
    return pl.pallas_call(
        partial(regress_kernel, group),
        in_specs=[SMEM, SMEM] + [VMEM] * 4 + [HBM] * 8,
        out_specs=[HBM] * len(outs),
        out_shape=outs,
        scratch_shapes=scratch,
        compiler_params=params(LIMIT),
        cost_estimate=cost(4 * n * 12 * D * D, 25e6),
        name="regress",
    )(ids, visible, *vecs, lat, x, q, dyb, *weights)


def stack_rows(copies, pieces, ref, size):
    return [copies.start(piece, ref.at[pl.ds(i * size, size)]) for i, piece in enumerate(pieces)]


class BlockLoads:
    def __init__(self, copies, ids, groups, blocks, sources, dest):
        self.copies, self.ids, self.groups, self.sources, self.dest = copies, ids, groups, sources, dest
        self.first = copies.take(groups * blocks)

    def each(self, role, j, like, act):
        for g, (src, size) in enumerate(self.sources(role, like)):
            act(src, self.dest(j).at[pl.ds(g * size, size)], self.first + j * self.groups + g)

    def begin(self, role, j):
        self.each(role, j, j, self.copies.begin)

    def wait(self, j, like=0):
        for role in range(2):
            pl.when(self.ids[0] == role)(lambda role=role: self.each(role, j, like, self.copies.wait_at))


def clear_tail(ref, used):
    ref[pl.ds(used, ref.shape[0] - used), :] = jnp.zeros((ref.shape[0] - used, ref.shape[1]), ref.dtype)


def halves(count, blocks):
    rows = D // 16
    if count == 16:
        return [struct((2, 2, 2, blocks, rows, D))] + [struct((2, blocks, rows, D))] * 4
    return [struct((D, D))] * blocks


def give_blocks(copies, core, tree, left_right, out, dest):
    size = 8 if tree else 1
    blocks = out.shape[0]
    first = copies.take(blocks * size)

    def send(j, act):
        if not tree:
            for block in range(blocks):
                pl.when(j == block)(lambda block=block: act(out.at[block], dest[block], first + block))
            return
        view = out.at[j].reshape(2, 2, 2, 2, D // 16, D)
        for x in range(2):
            for low in range(2):
                at = first + j * size + 4 * x + 2 * low
                act(view.at[:, low, x, core], dest[0].at[x, low, :, j], at)
                act(view.at[:, low, x, 1 - core], dest[1 + 2 * x + low].at[:, j], at + 1)

    def body(j):
        out[j] = left_right(j)
        send(j, copies.begin)

    loop(blocks, body)
    loop(blocks, lambda j: send(j, copies.wait_at))


def give_rows(copies, core, tree, multiply, out, dest):
    size = 4 if tree else 1
    first = copies.take(4 * size)

    def send(j, act):
        if not tree:
            act(out.at[j], dest[0].at[pl.ds(pl.multiple_of(j * D, D), D)], first + j)
            return
        view = out.at[j].reshape(2, 2, D // 4, D)
        low, high = lax.rem(j, 2), lax.div(j, 2)
        for x in range(2):
            at = first + j * size + 2 * x
            act(view.at[x, core], dest[0].at[x, low, high, 0], at)
            act(view.at[x, 1 - core], dest[1].at[x, low, high, 0], at + 1)

    def body(j):
        out[j] = multiply(j)
        send(j, copies.begin)

    loop(4, body)
    loop(4, lambda j: send(j, copies.wait_at))


def down_kernel(groups, parts, ids, *refs):
    cot, lat, a_enc, a_reg, dyb_reg = (refs[i * groups : (i + 1) * groups] for i in range(5))
    refs = refs[5 * groups :]
    dest, refs = refs[:parts], refs[parts:]
    sums_out, cot_v, dyb, a, dlat, out, sums, sems = refs
    images = groups * GROUP
    nv, nm = GROUP * NV, GROUP * NM

    copies = Copies(sems)
    pieces = (a_enc, a_reg)

    def sources(role, j):
        return [(one.at[:, pl.ds(j * D, D)], (nv, nm)[role]) for one in pieces[role]]

    loads = BlockLoads(copies, ids, groups, 4, sources, lambda j: a.at[j])

    @pl.when(ids[0] == 0)
    def _():
        early = copies.part()
        got = stack_rows(early, cot, cot_v, nv) + stack_rows(early, lat, dlat, nv)
        for j in range(4):
            loads.begin(0, j)
        early.wait(*got)
        dyb[...] = (cot_v[...].astype(F32) + dlat[...].astype(F32)).astype(BF)

    @pl.when(ids[0] == 1)
    def _():
        early = copies.part()
        got = stack_rows(early, dyb_reg, dyb, nm)
        for j in range(4):
            loads.begin(1, j)
            clear_tail(a.at[j], images * NM)
        clear_tail(dyb, images * NM)
        early.wait(*got)

    copies.take(2 * groups)

    def multiply(j):
        loads.wait(j)
        return tn(a[j], dyb[...]).astype(BF)

    give_rows(copies, ids[1], parts == 2, multiply, out, dest)
    sums[...] = jnp.broadcast_to(column_sum(dyb, images * NV), (8, D))
    copies.start(sums, sums_out)
    copies.finish()


def down_grad(groups, count, ids, cot, dlat, a_enc, a_reg, dyb_reg):
    n = groups * GROUP * NV
    main = [struct((2, 2, 2, 1, D // 4, D))] * 2 if count == 16 else [struct((FF, D))]
    outs = main + [struct((8, D), F32)]
    row = pltpu.VMEM((n, D), BF)
    scratch = [
        row, row, pltpu.VMEM((4, n, D), BF), row, pltpu.VMEM((4, D, D), BF), pltpu.VMEM((8, D), F32),
        pltpu.SemaphoreType.DMA((36,)),
    ]
    got = pl.pallas_call(
        partial(down_kernel, groups, len(main)),
        in_specs=[SMEM] + [HBM] * (5 * groups),
        out_specs=[HBM] * len(outs),
        out_shape=outs,
        scratch_shapes=scratch,
        compiler_params=params(LIMIT),
        cost_estimate=cost(1e6, 1e5),
        name="down_grad",
    )(ids, *cot, *dlat, *a_enc, *a_reg, *dyb_reg)
    return got[: len(main)], got[-1]


def pick_kernel(groups, ids, visible, order_in, cot, *refs):
    picked = refs[:groups]
    order, rows_v, flat, cot_v, sems = refs[groups:]

    @pl.when(ids[0] == 0)
    def _():
        copies = Copies(sems)
        got = copies.start(cot.at[0], rows_v)
        split_orders(order_in, order)
        copies.wait(got)
        flatten(rows_v, flat)

        def pick_rows(image):
            pick = pick_matrix(order, image, 0, NV, 0, visible[image])
            cot_v[rows_of(image, NV), :] = nn(pick, flat[...]).astype(BF)

        loop(groups * GROUP, pick_rows)
        for g in range(groups):
            copies.start(cot_v.at[pl.ds(g * GROUP * NV, GROUP * NV)], picked[g])
        copies.finish()


def pick_cot(groups, ids, visible, order, cot):
    images = order.shape[0]
    outs = [struct((GROUP * NV, D))] * groups
    return list(pl.pallas_call(
        partial(pick_kernel, groups),
        in_specs=[SMEM, SMEM, VMEM, HBM],
        out_specs=[HBM] * groups,
        out_shape=outs,
        scratch_shapes=[
            pltpu.VMEM((images, 1, PATCH), jnp.int32),
            pltpu.VMEM((PATCH, images, D), BF), pltpu.VMEM((PATCH * images, D), BF),
            pltpu.VMEM((images * NV, D), BF), pltpu.SemaphoreType.DMA((8,)),
        ],
        compiler_params=params(LIMIT),
        cost_estimate=cost(1e6, 1e5),
        name="pick_cot",
    )(ids, visible, order, cot))


def mlp_kernel(ids, gains, cot, dlat_in, w1, w2, y1_in, gp_in, du_out, dy1_out, dy1b_out, sums_out,
               s1, s2, cot_v, dlat, dyb, gp, y1, du, u, acc, dy1, dy1b, sums, sems):
    n = GROUP * NV
    third = FF // 3

    @pl.when(ids[0] == 0)
    def _():
        copies = Copies(sems)
        got = [copies.start(dlat_in, dlat), copies.start(cot, cot_v)]
        start = copies.take(9)

        def parts(i):
            cols = pl.ds(pl.multiple_of(i * third, third), third)
            return (
                (w2.at[0, cols, :], s2.at[cols, :]),
                (gp_in.at[:, cols], gp.at[:, cols]),
                (w1.at[0, :, cols], s1.at[:, cols]),
            )

        for i in range(3):
            for k, (src, dst) in enumerate(parts(i)):
                copies.begin(src, dst, start + 3 * i + k)
        got_y = copies.start(y1_in, y1)

        def ready(i, which):
            for k in ((0, 1), (2,))[which]:
                copies.wait_at(*parts(i)[k], start + 3 * i + k)

        copies.wait(*got)
        dyb[...] = (cot_v[...].astype(F32) + dlat[...].astype(F32)).astype(BF)
        mlp_back(n, dyb, gp, s1, s2, du, u, acc, ready)
        copies.start(du, du_out)
        copies.wait(got_y)

        def keep(sel, dx):
            dy1[sel, :] = dx
            dy1b[sel, :] = dx.astype(BF)

        g2, b2 = norm_back(y1, acc, dyb, keep, n, f32_row(gains.at[0], 1))
        copies.start(dy1, dy1_out)
        copies.start(dy1b, dy1b_out)
        sums[pl.ds(0, 1), :] = g2
        sums[pl.ds(1, 1), :] = b2
        copies.start(sums, sums_out)
        copies.finish()


def mlp_grad(ids, gains, cot, dlat, w1, w2, y1, gp):
    n = GROUP * NV
    row, wide, full = pltpu.VMEM((n, D), BF), pltpu.VMEM((n, FF), BF), pltpu.VMEM((n, D), F32)
    outs = [struct((n, FF)), struct((n, D), F32), struct((n, D)), struct((8, D), F32)]
    return pl.pallas_call(
        mlp_kernel,
        in_specs=[SMEM, VMEM] + [HBM] * 6,
        out_specs=[HBM] * len(outs),
        out_shape=outs,
        scratch_shapes=[
            pltpu.VMEM((D, FF), BF), pltpu.VMEM((FF, D), BF), row, row, row, wide, full, wide,
            pltpu.VMEM((2, n, HALF), F32), full, full, row, pltpu.VMEM((8, D), F32), pltpu.SemaphoreType.DMA((24,)),
        ],
        compiler_params=params(LIMIT),
        cost_estimate=cost(1e6, 1e5),
        name="mlp_grad",
    )(ids, gains, cot, dlat, w1, w2, y1, gp)


def up_kernel(groups, parts, ids, *refs):
    pieces = [refs[i * groups : (i + 1) * groups] for i in range(8)]
    refs = refs[8 * groups :]
    dest, refs = refs[:parts], refs[parts:]
    sums_out, left, right, out, sums, sems = refs
    images = groups * GROUP

    nv, nm = GROUP * NV, GROUP * NM
    copies = Copies(sems)
    sides = (pieces[:4], pieces[4:])

    def sources(role, j):
        du, _, dy1b, _ = sides[role]
        ones = dy1b if j == 4 else [one.at[:, pl.ds(j * D, D)] for one in du]
        return [(one, (nv, nm)[role]) for one in ones]

    def lefts(role, i):
        _, h2, _, o = sides[role]
        return [(one, (nv, nm)[role]) for one in (h2, o)[i]]

    loads = BlockLoads(copies, ids, groups, 5, sources, lambda j: right.at[j])
    shared = BlockLoads(copies, ids, groups, 2, lefts, lambda i: left.at[i])
    for role in range(2):

        @pl.when(ids[0] == role)
        def _(role=role):
            shared.begin(role, 0)
            for j in range(5):
                loads.begin(role, j)
            shared.begin(role, 1)
            if role == 1:
                for ref in (left, right):
                    for i in range(ref.shape[0]):
                        clear_tail(ref.at[i], images * NM)

    shared.wait(0)

    def multiply(j):
        loads.wait(j)
        pl.when(j == 4)(lambda: shared.wait(1))
        value = tn(left[lax.div(j, 4)], right[j]).astype(BF)
        sums[pl.ds(j, 1), :] = column_sum(right.at[j], images * NV)
        return value

    give_blocks(copies, ids[1], dest[0].ndim == 6, multiply, out, dest)
    copies.start(sums, sums_out)
    copies.finish()


def up_grad(groups, count, ids, *pieces):
    n = groups * GROUP * NV
    main = halves(count, 5)
    outs = main + [struct((8, D), F32)]
    got = pl.pallas_call(
        partial(up_kernel, groups, len(main)),
        in_specs=[SMEM] + [HBM] * (8 * groups),
        out_specs=[HBM] * len(outs),
        out_shape=outs,
        scratch_shapes=[
            pltpu.VMEM((2, n, D), BF), pltpu.VMEM((5, n, D), BF), pltpu.VMEM((5, D, D), BF), pltpu.VMEM((8, D), F32),
            pltpu.SemaphoreType.DMA((60,)),
        ],
        compiler_params=params(LIMIT),
        cost_estimate=cost(1e6, 1e5),
        name="up_grad",
    )(ids, *[ref for piece in pieces for ref in piece])
    return got[: len(main)], got[-1]


def attn_kernel(groups, last, ids, gains, *refs):
    if last:
        down_sums, up_sums, refs = refs[0], refs[1], refs[2:]
        mlp_sums, reg_sums = (refs[i * groups : (i + 1) * groups] for i in range(2))
        before, refs = refs[2 * groups : 3 * groups - 1], refs[3 * groups - 1 :]
    (wqkv, wo, dy1_enc, q_in, k_in, v_in, p_in, x_enc, dq_reg, dkv_reg, dy1_reg, x_reg,
     dq_out, dkv_out, dx_out, sums_out,
     sqkv, so, dy1, dy1b, q, k, v, p, x, do, dq, dkv, dh, sems) = refs
    m = GROUP * NM
    top = pl.ds(0, m)
    gain = f32_row(gains.at[0], 0)

    def finish(copies, rows):
        def keep(sel, dx):
            dy1[sel, :] = dx

        own = (*norm_back(x, dh, dy1, keep, rows, gain), column_sum(dq, rows), column_sum(dkv, GROUP * NV, D))
        copies.start(dy1, dx_out)
        if not last:
            for row, value in enumerate(own):
                sums_out[row : row + 1, :] = value
            copies.finish()
            return

        def total_of(sums):
            total = sums[0][...]
            for more in sums[1:]:
                total = total + more[...]
            return total

        done, mlp, reg = total_of(before), total_of(mlp_sums), total_of(reg_sums)
        g1, b1, queries, values = (one + done[row : row + 1, :] for row, one in enumerate(own))
        encoder = ids[0] == 0
        sums_out[0:1, :] = g1 + jnp.where(encoder, 0.0, reg[0:1, :])
        sums_out[1:2, :] = jnp.where(encoder, mlp[0:1, :], reg[1:2, :])
        sums_out[2:3, :] = b1 + jnp.where(encoder, 0.0, reg[2:3, :])
        sums_out[3:4, :] = up_sums[4:5, :]
        sums_out[4:5, :] = jnp.where(encoder, mlp[1:2, :], reg[3:4, :])
        sums_out[5:6, :] = down_sums[0:1, :]
        sums_out[6:7, :] = queries
        sums_out[7:8, :] = values
        sums_out[8:12, :] = up_sums[0:4, :]
        sums_out[12:16, :] = jnp.zeros((4, D), F32)
        copies.finish()

    @pl.when(ids[0] == 0)
    def _():
        copies = Copies(sems)
        got = [copies.start(dy1_enc, dy1), copies.start(wo.at[0], so)]
        later = [copies.start(src, dst) for src, dst in ((v_in, v), (p_in, p), (k_in, k), (q_in, q))]
        final = [copies.start(wqkv.at[0], sqkv), copies.start(x_enc, x)]
        copies.wait(*got)
        dy1b[...] = dy1[...].astype(BF)
        do[...] = nt(dy1b[...], so[...]).astype(BF)
        copies.wait(*later)
        attention_back_rows(GROUP, NV, q, k, v, p, do, dq, dkv)
        copies.start(dq, dq_out)
        copies.start(dkv, dkv_out)
        copies.wait(*final)
        dh[...] = nt(dq[...], sqkv[:, 0:D])
        for j in range(2):
            dh[...] += nt(dkv[:, j * D : (j + 1) * D], sqkv[:, (j + 1) * D : (j + 2) * D])
        finish(copies, GROUP * NV)

    @pl.when(ids[0] == 1)
    def _():
        copies = Copies(sems)
        for src, dst in ((dq_reg, dq), (dy1_reg, dy1), (x_reg, x)):
            copies.start(src, dst.at[top])
        copies.start(dkv_reg, dkv)
        copies.start(wqkv.at[0, :, pl.ds(0, D)], sqkv.at[:, pl.ds(0, D)])
        copies.finish()
        dh[top, :] = nt(dq[top, :], sqkv[:, 0:D])
        finish(copies, m)


def attn_back(groups, last, ids, gains, sums, *pieces):
    n = GROUP * NV
    row, full = pltpu.VMEM((n, D), BF), pltpu.VMEM((n, D), F32)
    outs = [struct((n, D)), struct((n, 2 * D)), struct((n, D), F32), struct((16, D), F32)]
    return pl.pallas_call(
        partial(attn_kernel, groups, last),
        in_specs=[SMEM, VMEM] + [VMEM] * len(sums) + [HBM] * len(pieces),
        out_specs=[HBM] * 3 + [VMEM],
        out_shape=outs,
        scratch_shapes=[
            pltpu.VMEM((D, 3 * D), BF), pltpu.VMEM((D, D), BF), full, row, row, row, row,
            pltpu.VMEM((GROUP * PAIRS, 2 * NV, NV), BF), row, row, row, pltpu.VMEM((n, 2 * D), BF), full,
            pltpu.SemaphoreType.DMA((20,)),
        ],
        compiler_params=params(LIMIT),
        cost_estimate=cost(1e6, 1e5),
        name="attn_back",
    )(ids, gains, *sums, *pieces)


def qkv_kernel(groups, parts, ids, *refs):
    pieces = [refs[i * groups : (i + 1) * groups] for i in range(7)]
    dq_enc, dkv_enc, hq_enc, hq_reg, hk_reg, dq_reg, dkv_reg = pieces
    refs = refs[7 * groups :]
    dest, refs = refs[:parts], refs[parts:]
    left, right, out, sems = refs
    images = groups * GROUP
    nv, nm = GROUP * NV, GROUP * NM
    copies = Copies(sems)

    def sources(role, j):
        if j == 2:
            return [(one, (nv, nm)[role]) for one in (dq_enc, dq_reg)[role]]
        return [(one.at[:, pl.ds(j * D, D)], nv) for one in (dkv_enc, dkv_reg)[role]]

    def lefts(role, i):
        if role == 0:
            return [(one, nv) for one in hq_enc]
        return [(one, (nv, nm)[i]) for one in (hk_reg, hq_reg)[i]]

    loads = BlockLoads(copies, ids, groups, 3, sources, lambda j: right.at[j])
    shared = BlockLoads(copies, ids, groups, 2, lefts, lambda i: left.at[i])
    for role in range(2):

        @pl.when(ids[0] == role)
        def _(role=role):
            shared.begin(role, 0)
            for j in range(3):
                loads.begin(role, j)
            shared.begin(role, 1)
            if role == 1:
                clear_tail(left.at[1], images * NM)
                clear_tail(right.at[2], images * NM)

    shared.wait(0)

    def multiply(j):
        for block in range(3):

            @pl.when(j == block)
            def _(block=block):
                loads.wait(block, block)
                if block == 2:
                    shared.wait(1, 1)

        return tn(left[lax.div(j, 2)], right[j]).astype(BF)

    give_blocks(copies, ids[1], dest[0].ndim == 6, multiply, out, dest)


def qkv_grad(groups, count, ids, *pieces):
    n = groups * GROUP * NV
    row = pltpu.VMEM((n, D), BF)
    main = halves(count, 3)
    scratch = [
        pltpu.VMEM((2, n, D), BF), pltpu.VMEM((3, n, D), BF), pltpu.VMEM((3, D, D), BF),
        pltpu.SemaphoreType.DMA((40,)),
    ]
    return pl.pallas_call(
        partial(qkv_kernel, groups, len(main)),
        in_specs=[SMEM] + [HBM] * (7 * groups),
        out_specs=[HBM] * len(main),
        out_shape=main,
        scratch_shapes=scratch,
        compiler_params=params(LIMIT),
        cost_estimate=cost(1e6, 1e5),
        name="qkv_grad",
    )(ids, *[ref for piece in pieces for ref in piece])


def place_kernel(groups, ids, visible, order_in, *refs):
    dx_in, lat_enc, res_enc, res_reg = (refs[i * groups : (i + 1) * groups] for i in range(4))
    block_out, grad_out, order, dx, lat, out, grads, sems = refs[4 * groups :]
    images = groups * GROUP
    nv, nm = GROUP * NV, GROUP * NM
    split_orders(order_in, order)

    def put_grad(i, put, value):
        high = value.astype(BF)
        low = (value - high.astype(F32)).astype(BF)
        grads[i] = nn(put, high) + nn(put, low)

    def write_grads():
        copies = Copies(sems)
        for i in range(images):
            copies.start(grads.at[i], grad_out.at[0, :, i, :])
        copies.finish()

    @pl.when(ids[0] == 0)
    def _():
        copies = Copies(sems)
        for piece, ref, size in ((dx_in, dx, nv), (lat_enc, lat, nv), (res_enc, out, nm)):
            stack_rows(copies, piece, ref, size)
        copies.finish()

        def put_image(i):
            put = place_matrix(order, i, 0, NV, 0, visible[i])
            put_side = place_matrix(order, i, FIRST, NM, visible[i], PATCH)
            put_grad(i, put, dx[rows_of(i, NV), :])
            block_out[0, i] = (nn(put, lat[rows_of(i, NV), :]) + nn(put_side, out[rows_of(i, NM), :])).astype(BF)

        loop(images, put_image)
        write_grads()

    @pl.when(ids[0] == 1)
    def _():
        copies = Copies(sems)
        stack_rows(copies, res_reg, out, nm)
        stack_rows(copies, [piece.at[pl.ds(0, nm)] for piece in dx_in], dx, nm)
        copies.finish()

        def put_image(i):
            put = place_matrix(order, i, FIRST, NM, visible[i], PATCH)
            put_grad(i, put, dx[rows_of(i, NM), :])
            block_out[0, i] = nn(put, out[rows_of(i, NM), :]).astype(BF)

        loop(images, put_image)
        write_grads()


def place(groups, ids, visible, order, *pieces):
    images = groups * GROUP
    n = images * NV
    outs = [struct((1, images, PATCH, D)), struct((1, PATCH, images, D), F32)]
    return pl.pallas_call(
        partial(place_kernel, groups),
        in_specs=[SMEM, SMEM, VMEM] + [HBM] * (4 * groups),
        out_specs=[VMEM, HBM],
        out_shape=outs,
        scratch_shapes=[
            pltpu.VMEM((images, 1, PATCH), jnp.int32), pltpu.VMEM((n, D), F32), pltpu.VMEM((n, D), BF),
            pltpu.VMEM((images * NM, D), BF), pltpu.VMEM((images, PATCH, D), F32), pltpu.SemaphoreType.DMA((8,)),
        ],
        compiler_params=params(LIMIT),
        cost_estimate=cost(1e6, 1e5),
        name="place",
    )(ids, visible, order, *[ref for piece in pieces for ref in piece])


BITS = (2, 4, 8)


def hop(value, bit):
    return lax.ppermute(value, "dp", [(i, i ^ bit) for i in range(16)])


def combine_kernel(jobs, given, ids, *refs):
    used = sum(sum(4 if gone is None else 1 for gone in terms) for terms, *_ in jobs)
    inputs, outs, scratch = list(refs[:used]), list(refs[used : used + given]), list(refs[used + given :])
    copies = Copies(scratch.pop())
    plans = []

    def fetch(term, gone, bits, own):
        if gone is not None:
            path = tuple(bits[gone:])
            copy = copies.start(term.at[path] if path else term, own)
            return lambda: copies.wait(copy)
        wide = len(bits) == 1
        first = copies.take(2 if wide else 1)
        rest = tuple(bits[2:])

        def piece(x, low):
            ref = term[2 * x + low]
            return ref.at[rest] if rest else ref

        for x in range(2):
            for low in range(2):
                if wide:
                    pl.when(bits[0] == x)(
                        lambda x=x, low=low: copies.begin(piece(x, low), own.at[low], first + low)
                    )
                else:
                    pl.when((bits[0] == x) & (bits[1] == low))(
                        lambda x=x, low=low: copies.begin(piece(x, low), own, first)
                    )

        def wait():
            if wide:
                for low in range(2):
                    copies.wait_at(piece(0, low), own.at[low], first + low)
            else:
                copies.wait_at(piece(0, 0), own, first)

        return wait

    for kinds, first, last, targets, finals in jobs:
        terms = [inputs.pop(0) if gone is not None else [inputs.pop(0) for _ in range(4)] for gone in kinds]
        for target in targets:
            bits = []
            for bit in range(last):
                flip = bit >= first and (target >> (bit - first)) & 1
                bits.append(1 - ids[2 + bit] if flip else ids[2 + bit])
            owns = [scratch.pop(0) for _ in kinds]
            waits = [fetch(term, gone, bits, own) for term, gone, own in zip(terms, kinds, owns)]
            plans.append((waits, owns, last, finals, None if finals else outs.pop(0)))
    for waits, owns, last, finals, out in plans:
        for wait in waits:
            wait()
        spots = [()]
        for _ in range(3 - last):
            spots = [spot + (i,) for spot in spots for i in range(2)]
        for spot in spots:
            for j in range(owns[0].shape[-3]):
                value = owns[0][spot + (j,)].astype(F32)
                for more in owns[1:]:
                    value = value + more[spot + (j,)].astype(F32)
                if finals:
                    which, column = finals[j]
                    outs[which][:, column * D : (column + 1) * D] = value
                else:
                    out[spot + (j,)] = value.astype(BF)


def send_job(terms, first, last, targets=(1,)):
    return terms, first, last, targets, None


def final_job(terms, finals):
    return terms, 0, 3, (0,), finals


def combine(ids, *jobs, outs=()):
    shapes = [struct(shape, F32) for shape in outs]
    plans, inputs, scratch = [], [], []
    for terms, first, last, targets, finals in jobs:
        blocks, rows = terms[0].shape[-3:-1]
        kinds = tuple(None if isinstance(term, list) else 6 - term.ndim for term in terms)
        for term in terms:
            inputs += term if isinstance(term, list) else [term]
        plans.append((kinds, first, last, targets, finals))
        part = (2,) * (3 - last) + (blocks, rows, D)
        for _ in targets:
            scratch += [pltpu.VMEM(part, BF) for _ in terms]
            if finals is None:
                shapes.append(struct(part))
    scratch.append(pltpu.SemaphoreType.DMA((2 * len(scratch),)))
    return pl.pallas_call(
        partial(combine_kernel, tuple(plans), len(shapes)),
        in_specs=[SMEM] + [HBM] * len(inputs),
        out_specs=[VMEM] * len(shapes),
        out_shape=shapes,
        scratch_shapes=scratch,
        compiler_params=params(LIMIT),
        cost_estimate=cost(1e5, 1e4),
        name="combine",
    )(ids, *inputs)


def in_order(first, then):
    return lax.optimization_barrier((first, then))


def own_columns(rows, count):
    own = D // count
    me = lax.axis_index("dp")

    def part(block, wide):
        return lax.dynamic_slice_in_dim(block, me * wide, wide, block.ndim - 1)

    return (
        part(rows[:2], own),
        part(rows[2:6], own),
        part(rows[6:8].reshape(-1), 2 * own),
        part(rows[8:12].reshape(-1), 4 * own),
    )


def scatter_natural(block):
    shards = block.reshape(lax.axis_size("dp"), -1, D)
    return lax.psum_scatter(shards, "dp", scatter_dimension=0, tiled=True)[0].astype(F32)


def local(
    patch_rows, cotangent, patch_order, visible, qkv_weight, out_weight, up_weight, down_weight, norm_gains, biases,
    qv_bias, up_bias, target_qkv, target_out, target_up, target_down, target_gains, target_biases, target_qv_bias,
    target_up_bias,
):
    count = lax.axis_size("dp")
    tree = count == 16
    place_dp = lax.axis_index("dp")
    bits = [(place_dp // bit) % 2 for bit in (1,) + BITS]
    ids = jnp.stack([lax.axis_index("section")] + bits).astype(jnp.int32)
    groups = patch_order.shape[0] // GROUP
    weights = (qkv_weight, out_weight, up_weight, down_weight)
    targets = (target_qkv, target_out, target_up, target_down)
    vecs = (norm_gains, biases, qv_bias, up_bias)
    target_vecs = (target_gains, target_biases, target_qv_bias[None], target_up_bias[None])

    rows, cot = patch_rows.transpose(0, 2, 1, 3), cotangent.transpose(0, 2, 1, 3)
    calls = [
        encode(g, groups, ids, visible, patch_order, *vecs, rows, cot, weights) for g in range(groups)
    ]
    lat, x_e, hq_e, q_e, k_e, v_e, p_e, o_e, y1_e, h2_e, gp_e, a_e = zip(*[call[0] for call in calls])
    x_r, hq_r, q_r, dyb_r = calls[-1][1]
    sent = [lax.ppermute(piece, "section", [(0, 1)]) for piece in lat]
    vectors = (norm_gains, biases, qv_bias, up_bias)
    regressed = [regress(0, ids, visible, vectors, sent[0], x_r[0], q_r[0], dyb_r[0], weights)]
    back = [lax.ppermute(regressed[0][0], "section", [(1, 0)])]
    order_first, regressed[0] = in_order(patch_order, regressed[0])
    res_e = [target(0, ids, visible, order_first, target_vecs, rows, targets)]
    res_e[0], sent[1:] = in_order(res_e[0], sent[1:])
    for g in range(1, groups):
        regressed.append(regress(g, ids, visible, vectors, sent[g], x_r[g], q_r[g], dyb_r[g], weights))
        back.append(lax.ppermute(regressed[g][0], "section", [(1, 0)]))
    _, res_r, hk_r, dq_r, dkv_r, o_r, dy1b_r, h2_r, du_r, a_r, dy1_r, sums_r = zip(*regressed)

    order_next, res_r = in_order(patch_order, res_r)
    cot_e = pick_cot(groups, ids, visible, order_next, cot)
    cot_e, back[0] = in_order(cot_e, back[0])

    def mlp(g, cot):
        return mlp_grad(ids, norm_gains, cot, back[g], up_weight, down_weight, y1_e[g], gp_e[g])

    def attention(g, dy1, sums=()):
        return attn_back(
            groups, len(sums) > 0, ids, norm_gains, sums, qkv_weight, out_weight, dy1, q_e[g], k_e[g], v_e[g], p_e[g],
            x_e[g], dq_r[g], dkv_r[g], dy1_r[g], x_r[g],
        )

    mlps = [mlp(g, cot_e[g]) for g in range(groups - 1)]
    attns = [attention(g, mlps[g][1]) for g in range(groups - 1)]
    last = groups - 1
    send = partial(combine, ids)
    attns, back[last] = in_order(attns, back[last])
    down, sums_down = down_grad(groups, count, ids, cot_e, back, a_e, a_r, dyb_r)
    cot_last = cot_e[last]
    down, cot_last = in_order(down, cot_last)
    mlps.append(mlp(last, cot_last))
    du_e, dy1_e, dy1b_e, sums_e = (list(piece) for piece in zip(*mlps))
    if tree:
        downs = [down[0], hop(down[1], 1)]
        (down_x,), du_e[last] = in_order(send(send_job(downs, 0, 1)), du_e[last])
        downs = downs + [hop(down_x, 2)]
    up, sums_up = up_grad(groups, count, ids, du_e, h2_e, dy1b_e, o_e, du_r, h2_r, dy1b_r, o_r)
    if tree:
        peers = (3, 2, 1)
        ups = [up[0], [hop(piece, 1) for piece in up[1:]]]
        (up_x,), downs = in_order(send(send_job(ups, 0, 1)), downs)
        ups = ups + [hop(up_x, 2)]
        down_z, dy1_e[last] = in_order(send(send_job(downs, 1, 3, peers)), dy1_e[last])
        down_got = [hop(one, 4 * peer) for one, peer in zip(down_z, peers)]
    sums_in = [piece[3] for piece in attns]
    attns.append(attention(last, dy1_e[last], (sums_down, sums_up, *sums_e, *sums_r, *sums_in)))
    dq_e, dkv_e, dx, small = (list(piece) for piece in zip(*attns))
    small = small[last]
    order_late = patch_order
    if tree:
        small = small + hop(small, 1)
        small, dq_e[last] = in_order(small, dq_e[last])
    attn = qkv_grad(groups, count, ids, dq_e, dkv_e, hq_e, hq_r, hk_r, dq_r, dkv_r)
    if tree:
        (down_got, got), attn = in_order((down_got, hop(small, 2)), attn)
        small = small + got
        up_z, (attn, got) = in_order(send(send_job(ups, 1, 3, peers)), (attn, hop(small, 4)))
        small = small + got
        up_got = [hop(one, 4 * peer) for one, peer in zip(up_z, peers)]
        qkvs = [attn[0], [hop(piece, 1) for piece in attn[1:]]]
        (qkv_x,), got = in_order(send(send_job(qkvs, 0, 1)), hop(small, 8))
        small = small + got
        order_late, qkv_x = in_order(patch_order, qkv_x)
        qkvs = qkvs + [hop(qkv_x, 2)]
    res_e += [target(g, ids, visible, order_late, target_vecs, rows, targets) for g in range(1, groups)]
    block_out, grad_rows = place(groups, ids, visible, patch_order, dx, lat, res_e, res_r)
    if tree:
        qkvs[-1], (block_out, grad_rows) = in_order(qkvs[-1], (block_out, grad_rows))
        qkv_z, up_got = in_order(send(send_job(qkvs, 1, 3, peers)), up_got)
        qkv_got = [hop(one, 4 * peer) for one, peer in zip(qkv_z, peers)]
        down_sum, up_sum, out_sum = send(
            final_job(downs + down_got, ((0, 0),)),
            final_job(ups + up_got, tuple((1, j) for j in range(4)) + ((2, 0),)),
            outs=((D // 4, D), (D // 16, 4 * D), (D // 16, D)),
        )
        qkv_got, (down_sum, up_sum, out_sum) = in_order(qkv_got, (down_sum, up_sum, out_sum))
        (qkv_sum,) = send(final_job(qkvs + qkv_got, ((0, 1), (0, 2), (0, 0))), outs=((D // 16, 3 * D),))
    else:
        down_sum = scatter_natural(down[0])
        up_sum = jnp.concatenate([scatter_natural(one) for one in up[:4]], axis=1)
        out_sum = scatter_natural(up[4])
        qkv_sum = jnp.concatenate([scatter_natural(attn[i]) for i in (2, 0, 1)], axis=1)
        small = lax.psum(small, "dp")
    grad_rows = grad_rows.transpose(0, 2, 1, 3)
    gains, bias_rows, qv_rows, up_rows = own_columns(small, count)
    return (
        block_out,
        grad_rows,
        qkv_sum[None],
        out_sum[None],
        up_sum[None],
        down_sum[None],
        gains[None],
        bias_rows[None],
        qv_rows[None],
        up_rows[None],
    )


def solution(mesh):
    three, four = P("section", None, None), P("section", "dp", None, None)
    grad = P("section", "dp", None)
    return jax.shard_map(
        local,
        mesh=mesh,
        in_specs=(four, four, P("dp", None), P("dp"), three, three, three, three, three, three,
                  P("section", None), P("section", None), P(), P(), P(), P(), P(), P(), P(), P()),
        out_specs=(four, four, grad, grad, grad, grad, P("section", None, "dp"), P("section", None, "dp"),
                   P("section", "dp"), P("section", "dp")),
        check_vma=False,
    )
```
